32 devices in a mesh: dp: 8 (over z, x), tensor: 4 (over y, core).
Axes of the slice: x: 2, y: 2, z: 4, core: 2. Of those that a mesh axis runs over, the one named last changes fastest.
Arguments:
- tokens: bfloat16 [16384, 768], P('dp'), may hold values from -6 to 6
- pass_ids: int32 [16384], P('dp'), may hold values from 0 to 4
- doc_lengths: int32 [8, 8], P('dp'), may hold values from 1 to 1024, 2048 in all within a row
- cotangent: bfloat16 [16384, 768], P('dp'), may hold values from -6 to 6
- block_weights: float32 [4, 48, 192, 192], P('tensor', 'dp'), may hold values from -2 to 2
- vector_params: float32 [9, 768], P(None, 'dp'), may hold values from -2 to 2
- vector_moment: float32 [9, 768], P(None, 'dp'), may hold values from 4096 to 16384
- block_left: float32 [4, 48, 192, 192], P('tensor', 'dp'), may hold values from -6291456 to 6291456
- block_right: float32 [4, 48, 192, 192], P('tensor', 'dp'), may hold values from -6291456 to 6291456
- block_left_root: float32 [4, 48, 192, 192], P('tensor', 'dp'), may hold values from -2 to 2
- block_right_root: float32 [4, 48, 192, 192], P('tensor', 'dp'), may hold values from -2 to 2
Outputs:
- output: bfloat16 [16384, 768], P('dp')
- input_grad: bfloat16 [16384, 768], P('dp')
- block_left_new: float32 [4, 48, 192, 192], P('tensor', 'dp')
- block_right_new: float32 [4, 48, 192, 192], P('tensor', 'dp')
- block_step: float32 [4, 48, 192, 192], P('tensor', 'dp')
- block_new: float32 [4, 48, 192, 192], P('tensor', 'dp')
- vector_grad: float32 [9, 768], P(None, 'dp')
- vector_moment_new: float32 [9, 768], P(None, 'dp')
- vector_new: float32 [9, 768], P(None, 'dp')
The draws below stay inside these ranges and needn't reach their ends.
All inputs are finite; a program needn't handle non-finite values.
Results may differ from the reference program's by a relative error of at most 0.014.
Values may be sent and summed in bfloat16 or wider, within the bound.
A program may use at most 192 MiB of HBM per device.

```python
import math
import jax
import jax.numpy as jnp
import numpy as np
from jax import lax

D = 768
HEADS = 12
HD = 64
FF = 3072
PASSES = 5
SEQ = 2048
NDOC = 8
DOC_MAX = 1024
TOKENS = 16384
BLOCK = 192
NBLK = 48
SLOTS = 48
N_DP = 8
N_TENSOR = 4


def slot_index():
    return jnp.arange(SLOTS, dtype=jnp.int32)


def kind_factor(stat_side):
    slots = slot_index()
    count = N_TENSOR
    ratio = FF // D
    lower_start = 4 * count + count * ratio
    if stat_side:
        factor = jnp.where((slots >= lower_start) & (slots < NBLK), 0.4, 0.1)
    else:
        factor = jnp.where(slots < 3 * count, 0.3, jnp.where(slots < lower_start, 0.1, jnp.where(slots < NBLK, 0.4, 0.1)))
    return factor.astype(jnp.float32)[None, :, None, None]


def state_matrix(key, scale, low_end, high_end, off):
    diag_key, off_key = jax.random.split(key)
    lead = (N_TENSOR, SLOTS)
    side = BLOCK
    diag = jnp.exp(jax.random.uniform(diag_key, lead + (side,), jnp.float32, math.log(low_end), math.log(high_end)))
    noise = jnp.clip(jax.random.normal(off_key, lead + (side, side), jnp.float32), -3.0, 3.0)
    noise = (noise + jnp.swapaxes(noise, -1, -2)) * (0.5 * off / math.sqrt(side))
    eye = jnp.eye(side, dtype=jnp.float32)
    return scale * (diag[..., :, None] * eye + noise * (1.0 - eye))


def stat_draw(key, salt):
    scale = kind_factor(True) * (TOKENS * BLOCK)
    return state_matrix(jax.random.fold_in(key, salt), scale, 1.0, 4.0, 0.1)


def root_draw(key, salt):
    scale = (kind_factor(False) * TOKENS) ** (-0.25)
    return state_matrix(jax.random.fold_in(key, salt), scale, 0.5, 2.0, 0.5)


def draw_block_weights(key, part):
    slots = slot_index()
    count = N_TENSOR
    ratio = FF // D
    scale = jnp.where(slots < 3 * count, D ** (-0.5), jnp.where(slots < 4 * count, (D // 8) ** (-0.5), jnp.where(slots < 4 * count + count * ratio, D ** (-0.5), FF ** (-0.5))))
    noise = jnp.clip(jax.random.normal(jax.random.fold_in(key, 31), (N_TENSOR, SLOTS, BLOCK, BLOCK), jnp.float32), -4.0, 4.0)
    return noise * scale.astype(jnp.float32)[None, :, None, None]


def draw_vector_params(key, part):
    rows_key, gain_key, shift_key = jax.random.split(jax.random.fold_in(key, 37), 3)
    embed = 0.5 * jnp.clip(jax.random.normal(rows_key, (PASSES, D), jnp.float32), -4.0, 4.0)
    gains = jax.random.uniform(gain_key, (2, D), jnp.float32, 0.5, 1.5)
    shifts = 0.3 * jnp.clip(jax.random.normal(shift_key, (2, D), jnp.float32), -4.0, 4.0)
    return jnp.concatenate([embed, gains[0:1], shifts[0:1], gains[1:2], shifts[1:2]], axis=0)


def draw_block_left(key, part):
    return stat_draw(key, 11)


def draw_block_right(key, part):
    return stat_draw(key, 13)


def draw_block_left_root(key, part):
    return root_draw(key, 23)


def draw_block_right_root(key, part):
    return root_draw(key, 29)


def touch_ends(array, own_key, least, high):
    longest = array.shape.index(max(array.shape))
    spots = []
    for shift in (0, 1):
        where = [jax.random.randint(jax.random.fold_in(own_key, axis), (), 0, length) for axis, length in enumerate(array.shape)]
        where[longest] = (where[longest] + shift) % array.shape[longest]
        spots.append(tuple(where))
    return array.at[spots[0]].set(least).at[spots[1]].set(high)


def level_of(stream_key, extent, pieces, least, top_value):
    def one(position, blocks):
        steps = jax.random.uniform(jax.random.fold_in(jax.random.fold_in(stream_key, 6), position), (blocks,), jnp.float32, least / len(pieces), top_value / len(pieces))
        return jnp.repeat(jnp.exp(steps), extent[position] // blocks).reshape((-1,) + (1,) * (len(extent) - position - 1))

    level = one(*pieces[0])
    for cut in pieces[1:]:
        level = level * one(*cut)
    return level


def length_profile(number_of, total, reach, lean):
    weights = [(1 << 20) // math.isqrt(standing ** lean) + 1 for standing in range(2, number_of + 1)]
    surplus, counts = total - reach - (number_of - 1), [1] * (number_of - 1)
    while surplus > 0:
        candidates = [i for i in range(number_of - 1) if counts[i] < reach]
        pool, left = sum([weights[i] for i in candidates]), surplus
        for i in candidates:
            extra = min(reach - counts[i], max(1, left * weights[i] // pool), surplus)
            counts[i] = counts[i] + extra
            surplus = surplus - extra
    return np.array([reach] + counts)


def ragged_sizes(stream_key, number_of, total, most, slope):
    if number_of == 2:
        one = jax.random.randint(stream_key, (), max(1, total - most), min(most, total - 1) + 1)
        return jnp.stack([one, total - one])
    sizes = jnp.asarray(length_profile(number_of, total, most, slope), jnp.int32)
    couples = (number_of - 1) // 2
    donor, receiver = sizes[1:1 + 2 * couples:2], sizes[2:2 + 2 * couples:2]
    slack = jnp.minimum(donor - 1, most - receiver)
    moved = jax.random.randint(jax.random.fold_in(stream_key, 1), (couples,), 0, 1 << 20) % (slack + 1)
    sizes = sizes.at[1:1 + 2 * couples:2].set(donor - moved).at[2:2 + 2 * couples:2].set(receiver + moved)
    return sizes[jax.random.permutation(jax.random.fold_in(stream_key, 2), number_of)]


def bell_draw(rng, dims, deviation, most, cuts=(), kind=jnp.bfloat16):
    level = level_of(rng, dims, cuts, -0.22, 0.18) if cuts else 1.0
    array = jax.random.normal(rng, dims, jnp.float32) * deviation * level
    return jnp.minimum(jnp.maximum(array, -most), most).astype(kind)


def setup_inputs(seed: int = 0) -> dict:
    key_of = jax.random.split(jax.random.key(seed), 12)
    return {
        "tokens": bell_draw(key_of[0], (TOKENS, D), 1.0, 6.0, ((0, 8),)),
        "pass_ids": touch_ends(jax.random.randint(key_of[1], (TOKENS,), 0, PASSES), jax.random.fold_in(key_of[1], 1), 0, PASSES - 1).astype(jnp.int32),
        "doc_lengths": jax.vmap(lambda own: ragged_sizes(own, NDOC, SEQ, DOC_MAX, 2))(jax.random.split(key_of[2], N_DP)).reshape((N_DP, NDOC)).astype(jnp.int32),
        "cotangent": bell_draw(key_of[3], (TOKENS, D), 1.0, 6.0, ((0, 8),)),
        "block_weights": draw_block_weights(jax.random.fold_in(key_of[11], 71), 0),
        "vector_params": draw_vector_params(jax.random.fold_in(key_of[11], 71), 0),
        "vector_moment": jnp.clip(jnp.exp(math.log(16384.0) - 1.3862944 * jax.random.uniform(key_of[6], (PASSES + 4, D), jnp.float32) ** level_of(key_of[6], (PASSES + 4, D), ((1, 8),), -0.2, 0.2)), 4096.0, 16384.0),
        "block_left": draw_block_left(jax.random.fold_in(key_of[11], 71), 0),
        "block_right": draw_block_right(jax.random.fold_in(key_of[11], 71), 0),
        "block_left_root": draw_block_left_root(jax.random.fold_in(key_of[11], 71), 0),
        "block_right_root": draw_block_right_root(jax.random.fold_in(key_of[11], 71), 0),
    }


@jax.custom_vjp
def low(v):
    return lax.optimization_barrier(v.astype(jnp.bfloat16)).astype(jnp.float32)

@jax.custom_vjp
def low_back(v):
    return v

def low_keep(v):
    return (low(v), None)

def low_pass(kept, grad):
    return (grad,)

def back_keep(v):
    return (v, None)

def back_low(kept, grad):
    return (low(grad),)
low.defvjp(low_keep, low_pass)
low_back.defvjp(back_keep, back_low)
norm_eps = 1e-05
moment_eps = 1e-08
rate_matrix = 0.03
rate_vector = 0.2
decay = 0.5
gelu_coef = 0.7978845608028654
masked_score = -1e+30
highest = lax.Precision.HIGHEST

def layer_norm(hidden, gain, shift):
    mean = lax.optimization_barrier(jnp.mean(hidden, axis=-1, keepdims=True))
    center = hidden - mean
    spread = lax.optimization_barrier(jnp.mean(center * center, axis=-1, keepdims=True))
    return center * lax.rsqrt(spread + norm_eps) * gain + shift

def gelu_tanh(value):
    return 0.5 * value * (1.0 + jnp.tanh(gelu_coef * (value + 0.044715 * value * value * value)))

def doc_numbers(lengths, count):
    ends = jnp.cumsum(lengths)
    places = jnp.arange(count, dtype=jnp.int32)
    return lax.optimization_barrier(jnp.sum((ends[None, :] <= places[:, None]).astype(jnp.int32), axis=1)).astype(jnp.int32)

def precondition(grad, weight, left, right, left_root, right_root):
    left_new = decay * left + (1.0 - decay) * jnp.einsum('...ij,...kj->...ik', grad, grad, precision=highest)
    right_new = decay * right + (1.0 - decay) * jnp.einsum('...ji,...jk->...ik', grad, grad, precision=highest)
    half = jnp.einsum('...ij,...jk->...ik', left_root, grad, precision=highest)
    step = jnp.einsum('...ij,...jk->...ik', half, right_root, precision=highest)
    return (left_new, right_new, step, weight - rate_matrix * step)

def assemble_all(blocks):
    count = N_TENSOR
    ratio = FF // D
    side = BLOCK
    qkv = blocks[:, 0:3 * count].reshape(count, 3, count, side, side).transpose(1, 2, 3, 0, 4).reshape(3, D, D)
    out = blocks[:, 3 * count:4 * count].transpose(0, 2, 1, 3).reshape(D, D)
    upper = blocks[:, 4 * count:4 * count + count * ratio].reshape(count, count, ratio, side, side).transpose(1, 3, 0, 2, 4).reshape(D, FF)
    lower = blocks[:, 4 * count + count * ratio:NBLK].reshape(count, ratio, count, side, side).transpose(0, 1, 3, 2, 4).reshape(FF, D)
    return (qkv, out, upper, lower)

def split_all(grad_qkv, grad_out, grad_up, grad_down):
    count = N_TENSOR
    ratio = FF // D
    side = BLOCK
    qkv = grad_qkv.reshape(3, count, side, count, side).transpose(3, 0, 1, 2, 4).reshape(count, 3 * count, side, side)
    out = grad_out.reshape(count, side, count, side).transpose(0, 2, 1, 3)
    upper = grad_up.reshape(count, side, count, ratio, side).transpose(2, 0, 3, 1, 4).reshape(count, count * ratio, side, side)
    lower = grad_down.reshape(count, ratio, side, count, side).transpose(0, 1, 3, 2, 4).reshape(count, ratio * count, side, side)
    spare = jnp.zeros((count, SLOTS - NBLK, side, side), jnp.float32)
    return jnp.concatenate([qkv, out, upper, lower, spare], axis=1)

def forward_seq(params, hidden, pass_row, length_row):
    qkv_w, out_w, up_w, down_w, vector = params
    seq = hidden.shape[0]
    scale = HD ** (-0.5)
    width = min(512, seq)
    first = hidden + vector[:PASSES][pass_row]
    normed_one = low(layer_norm(first, vector[PASSES], vector[PASSES + 1]))
    project = low_back(low(jnp.einsum('sd,kde->kse', normed_one, low(qkv_w), precision=highest)))
    queries = project[0].reshape(seq, HEADS, HD)
    keys = project[1].reshape(seq, HEADS, HD)
    values = project[2].reshape(seq, HEADS, HD)
    docs = doc_numbers(length_row, seq)

    def one_block(start):
        query_rows = lax.dynamic_slice_in_dim(queries, start, width, 0)
        query_docs = lax.dynamic_slice_in_dim(docs, start, width, 0)
        raw = jnp.einsum('qhd,khd->hqk', query_rows, keys, precision=highest)
        scores = low_back(raw * scale)
        rows = start + jnp.arange(width, dtype=jnp.int32)
        cols = jnp.arange(seq, dtype=jnp.int32)
        allowed = (query_docs[:, None] == docs[None, :]) & (cols[None, :] <= rows[:, None])
        masked = jnp.where(allowed[None], scores, masked_score)
        top = lax.optimization_barrier(jnp.max(masked, axis=-1, keepdims=True))
        total = lax.optimization_barrier(jnp.sum(jnp.exp(masked - top), axis=-1, keepdims=True))
        probs = low(jnp.exp(masked - (top + jnp.log(total))))
        return jnp.einsum('hqk,khd->qhd', probs, values, precision=highest)
    starts = jnp.arange(seq // width, dtype=jnp.int32) * width
    mixed = lax.map(jax.checkpoint(one_block), starts).reshape(seq, D)
    mixed = low_back(low(mixed))
    second = first + low_back(jnp.dot(mixed, low(out_w), precision=highest))
    normed_two = low(layer_norm(second, vector[PASSES + 2], vector[PASSES + 3]))
    upper = low_back(jnp.dot(normed_two, low(up_w), precision=highest))
    act = low(gelu_tanh(upper))
    return second + low_back(jnp.dot(act, low(down_w), precision=highest))

def reference(tokens, pass_ids, doc_lengths, cotangent, block_weights, vector_params, vector_moment, block_left, block_right, block_left_root, block_right_root):
    qkv_weight, out_weight, up_weight, down_weight = assemble_all(block_weights[:, :NBLK])
    params = (qkv_weight, out_weight, up_weight, down_weight, vector_params)
    hidden_all = tokens.astype(jnp.float32).reshape(N_DP, SEQ, D)
    grad_all = cotangent.astype(jnp.float32).reshape(N_DP, SEQ, D)
    pass_all = pass_ids.reshape(N_DP, SEQ)

    def one_sequence(carry, item):
        hidden, pass_row, length_row, grad_row = item
        result, back = jax.vjp(lambda p, h: forward_seq(p, h, pass_row, length_row), params, hidden)
        grad_params, grad_hidden = back(grad_row)
        carry = jax.tree.map(lambda a, b: a + b, carry, grad_params)
        return (carry, (result.astype(jnp.bfloat16), grad_hidden.astype(jnp.bfloat16)))
    zeros = jax.tree.map(jnp.zeros_like, params)
    grads, (outputs, input_grads) = lax.scan(one_sequence, zeros, (hidden_all, pass_all, doc_lengths, grad_all))
    grad_qkv, grad_out, grad_up, grad_down, grad_vector = grads
    grad_blocks = split_all(grad_qkv, grad_out, grad_up, grad_down)
    left_new, right_new, step, weight_new = precondition(grad_blocks, block_weights, block_left, block_right, block_left_root, block_right_root)
    moment_new = decay * vector_moment + (1.0 - decay) * grad_vector * grad_vector
    vector_new = vector_params - rate_vector * grad_vector / (jnp.sqrt(moment_new) + moment_eps)
    return (outputs.reshape(TOKENS, D), input_grads.reshape(TOKENS, D), left_new, right_new, step, weight_new, grad_vector, moment_new, vector_new)
```

```python
import functools

import jax
import jax.numpy as jnp
from jax import lax
from jax.experimental import pallas as pl
from jax.experimental.pallas import tpu as pltpu
from jax.sharding import PartitionSpec as P

D = 768
HD = 64
FF = 3072
PASSES = 5
SIDE = 192
PAIR = 2 * SIDE
ROWS = 256
DOCS = 8
NT = 4

norm_eps = 1e-05
moment_eps = 1e-08
rate_matrix = 0.03
rate_vector = 0.2
decay = 0.5
gelu_coef = 0.7978845608028654
masked_score = -1e30
f32 = jnp.float32
bf16 = jnp.bfloat16
VMEM_LIMIT = 56 * 1024 * 1024


def nn(a, b):
    return lax.dot_general(a, b, (((1,), (0,)), ((), ())), preferred_element_type=f32)


def nt(a, b):
    return lax.dot_general(a, b, (((1,), (1,)), ((), ())), preferred_element_type=f32)


def tn(a, b):
    return lax.dot_general(a, b, (((0,), (0,)), ((), ())), preferred_element_type=f32)


def split_three(value):
    high = value.astype(bf16)
    rest = value - high.astype(f32)
    mid = rest.astype(bf16)
    return high, mid, (rest - mid.astype(f32)).astype(bf16)


def one_hot(pass_row):
    kinds = lax.broadcasted_iota(jnp.int32, (16, pass_row.shape[1]), 0)
    return (kinds == pass_row).astype(f32).astype(bf16)


def embedded(tokens, pass_row, vec):
    chosen = one_hot(pass_row)
    high, mid, low = split_three(vec)
    return tokens.astype(f32) + (tn(chosen, high) + tn(chosen, mid) + tn(chosen, low))


def hat_of(hidden):
    mean = jnp.mean(hidden, axis=-1, keepdims=True)
    center = hidden - mean
    spread = jnp.mean(center * center, axis=-1, keepdims=True)
    root = lax.rsqrt(spread + norm_eps)
    return center * root, root


def norm_back(hat, root, grad, gain):
    scaled = grad * gain
    first = jnp.mean(scaled, axis=-1, keepdims=True)
    second = jnp.mean(scaled * hat, axis=-1, keepdims=True)
    return root * (scaled - first - hat * second)


def params(**kw):
    return pltpu.CompilerParams(vmem_limit_bytes=VMEM_LIMIT, **kw)


def full(shape):
    return pl.BlockSpec(shape, lambda *_: (0,) * len(shape))


def project_kernel(tok, pas, vec, wq, norm, q, k, v, cat):
    @pl.when(pl.program_id(0) == 0)
    def _():
        for x in range(3):
            for i in range(4):
                at = (i % 2) * SIDE
                parts = [wq[h, 2 * x + i // 2][:, at : at + SIDE] for h in range(2)]
                cat[x, i * SIDE : (i + 1) * SIDE, :] = jnp.concatenate(parts, axis=1)

    first = embedded(tok[...], pas[...], vec[...])
    hat, _ = hat_of(first)
    low = (hat * vec[PASSES : PASSES + 1] + vec[PASSES + 1 : PASSES + 2]).astype(bf16)
    norm[...] = low
    for x, out in enumerate((q, k, v)):
        out[...] = nn(low, cat[x]).astype(bf16)


def project(tokens, passes, vec, wq):
    seq = tokens.shape[0]
    row = lambda n: pl.BlockSpec((ROWS, n), lambda i: (i, 0))
    wide = jax.ShapeDtypeStruct((seq, PAIR), bf16)
    return pl.pallas_call(
        project_kernel,
        grid=(seq // ROWS,),
        in_specs=[row(D), pl.BlockSpec((1, ROWS), lambda i: (0, i)), full((16, D)), full(wq.shape)],
        out_specs=[row(D), row(PAIR), row(PAIR), row(PAIR), full((3, D, PAIR))],
        out_shape=[
            jax.ShapeDtypeStruct((seq, D), bf16),
            wide,
            wide,
            wide,
            jax.ShapeDtypeStruct((3, D, PAIR), bf16),
        ],
        compiler_params=params(),
        name="project",
    )(tokens, passes, vec, wq)


def doc_state(lens, base):
    rows = base + lax.broadcasted_iota(jnp.int32, (1, ROWS), 1)
    rows = jnp.concatenate([rows, rows], axis=1)
    begin = jnp.int32(0)
    first = jnp.int32(0)
    starts = jnp.zeros((1, 2 * ROWS), jnp.int32)
    for c in range(DOCS):
        starts = jnp.where(rows >= begin, begin, starts)
        first = jnp.where(base >= begin, begin, first)
        begin = begin + lens[c]
    return rows, starts, first


def two_heads(block):
    left = lax.broadcasted_iota(jnp.int32, block.shape, 1) < HD
    none = jnp.zeros_like(block)
    return jnp.concatenate([jnp.where(left, block, none), jnp.where(left, none, block)], axis=0)


def one_above(both):
    return jnp.concatenate([both[:HD, :ROWS], both[HD:, ROWS:]], axis=0).T


def attend_kernel(lens, q, k, v, out, lse, top, total, acc):
    i = pl.program_id(0)
    base = i * ROWS
    rows, starts, first = doc_state(lens, base)
    pairs = [two_heads(q[:, p * 128 : (p + 1) * 128] * bf16(0.125)) for p in range(3)]
    for p in range(3):
        top[p] = jnp.full((1, 2 * ROWS), masked_score, f32)
        total[p] = jnp.zeros((1, 2 * ROWS), f32)
        acc[p] = jnp.zeros((128, 2 * ROWS), f32)

    def step(j, carry):
        at = pl.multiple_of(j * ROWS, ROWS)
        keys = at + lax.broadcasted_iota(jnp.int32, (ROWS, 2 * ROWS), 0)
        seen = (keys >= starts) & (keys <= rows)
        for p in range(3):
            cols = slice(p * 128, (p + 1) * 128)
            scores = jnp.where(seen, nt(k[pl.ds(at, ROWS), cols], pairs[p]), masked_score)
            before = top[p]
            now = jnp.maximum(before, jnp.max(scores, axis=0, keepdims=True))
            probs = jnp.exp(scores - now)
            fade = jnp.exp(before - now)
            top[p] = now
            total[p] = total[p] * fade + jnp.sum(probs, axis=0, keepdims=True)
            acc[p] = acc[p] * fade + tn(v[pl.ds(at, ROWS), cols], probs.astype(bf16))
        return carry

    lax.fori_loop(first // ROWS, i + 1, step, 0)
    lines = []
    for p in range(3):
        out[:, p * 128 : (p + 1) * 128] = one_above(acc[p] / total[p]).astype(bf16)
        line = top[p] + jnp.log(total[p])
        lines += [line[:, :ROWS], line[:, ROWS:]]
    lse[...] = jnp.concatenate(lines + lines[:2], axis=0)


def attend(lens, q, k, v):
    seq = q.shape[0]
    row = pl.BlockSpec((ROWS, PAIR), lambda i, s: (i, 0))
    return pl.pallas_call(
        attend_kernel,
        grid_spec=pltpu.PrefetchScalarGridSpec(
            num_scalar_prefetch=1,
            grid=(seq // ROWS,),
            in_specs=[row, full((seq, PAIR)), full((seq, PAIR))],
            out_specs=[row, pl.BlockSpec((8, ROWS), lambda i, s: (0, i))],
            scratch_shapes=[
                pltpu.VMEM((3, 1, 2 * ROWS), f32),
                pltpu.VMEM((3, 1, 2 * ROWS), f32),
                pltpu.VMEM((3, 128, 2 * ROWS), f32),
            ],
        ),
        out_shape=[
            jax.ShapeDtypeStruct((seq, PAIR), bf16),
            jax.ShapeDtypeStruct((8, seq), f32),
        ],
        compiler_params=params(),
        name="attend",
    )(lens, q, k, v)


def attend_back_kernel(
    lens, place, q, k, v, mixed, lse, mine, other, wo, dq, dk, dv, gwo, dk_acc, dv_acc, dq_acc, gwo_acc
):
    i = pl.program_id(0)
    count = pl.num_programs(0)
    base = i * ROWS

    @pl.when(i == 0)
    def _():
        dk_acc[...] = jnp.zeros_like(dk_acc)
        dv_acc[...] = jnp.zeros_like(dv_acc)
        gwo_acc[...] = jnp.zeros_like(gwo_acc)

    half = (i >= count // 2).astype(jnp.int32)
    grad = jnp.where(half == place[0], mine[...], other[...])
    weight = jnp.concatenate(
        [jnp.concatenate([wo[h, 0], wo[h, 1]], axis=1) for h in range(2)], axis=0
    )
    grad_mixed = nt(grad, weight).astype(bf16)
    gwo_acc[...] += tn(mixed[...], grad)

    rows, starts, first = doc_state(lens, base)
    heads = lax.broadcasted_iota(jnp.int32, (8, 128), 0)
    lanes = lax.broadcasted_iota(jnp.int32, (8, 128), 1)
    pick = (lanes // HD == heads).astype(f32)
    queries, grads, inner, lines = [], [], [], []
    for p in range(3):
        cols = slice(p * 128, (p + 1) * 128)
        queries.append(two_heads(q[:, cols] * bf16(0.125)))
        grads.append(two_heads(grad_mixed[:, cols]))
        product = grad_mixed[:, cols].astype(f32) * mixed[:, cols].astype(f32)
        sums = lax.dot_general(
            pick,
            product,
            (((1,), (1,)), ((), ())),
            precision=lax.Precision.HIGHEST,
            preferred_element_type=f32,
        )
        inner.append(jnp.concatenate([sums[0:1], sums[1:2]], axis=1))
        lines.append(jnp.concatenate([lse[2 * p : 2 * p + 1], lse[2 * p + 1 : 2 * p + 2]], axis=1))
        dq_acc[p] = jnp.zeros((128, 2 * ROWS), f32)

    def step(j, carry):
        at = pl.multiple_of(j * ROWS, ROWS)
        keys = at + lax.broadcasted_iota(jnp.int32, (ROWS, 2 * ROWS), 0)
        seen = (keys >= starts) & (keys <= rows)
        here = pl.ds(at, ROWS)
        for p in range(3):
            cols = slice(p * 128, (p + 1) * 128)
            kb = k[here, cols]
            scores = jnp.where(seen, nt(kb, queries[p]) - lines[p], masked_score)
            probs = jnp.exp(scores)
            grad_probs = nt(v[here, cols], grads[p])
            grad_scores = (probs * (grad_probs - inner[p])).astype(bf16)
            dv_acc[here, cols] += nn(probs.astype(bf16), grads[p])
            dk_acc[here, cols] += nn(grad_scores, queries[p])
            dq_acc[p] += tn(kb, grad_scores)
        return carry

    lax.fori_loop(first // ROWS, i + 1, step, 0)
    for p in range(3):
        dq[:, p * 128 : (p + 1) * 128] = (one_above(dq_acc[p]) * 0.125).astype(bf16)

    @pl.when(i == count - 1)
    def _():
        dk[...] = dk_acc[...].astype(bf16)
        dv[...] = dv_acc[...].astype(bf16)
        at = pl.multiple_of(place[1] * SIDE, SIDE)
        for m in range(2):
            gwo[m] = gwo_acc[pl.ds(at, SIDE), m * PAIR : (m + 1) * PAIR].astype(bf16)


def attend_back(lens, place, q, k, v, mixed, lse, mine, other, wo):
    seq = q.shape[0]
    count = seq // ROWS
    row = pl.BlockSpec((ROWS, PAIR), lambda i, s, t: (i, 0))
    half = pl.BlockSpec((ROWS, D), lambda i, s, t: (lax.rem(i, count // 2), 0))
    wide = jax.ShapeDtypeStruct((seq, PAIR), bf16)
    return pl.pallas_call(
        attend_back_kernel,
        grid_spec=pltpu.PrefetchScalarGridSpec(
            num_scalar_prefetch=2,
            grid=(count,),
            in_specs=[
                row,
                full((seq, PAIR)),
                full((seq, PAIR)),
                row,
                pl.BlockSpec((8, ROWS), lambda i, s, t: (0, i)),
                half,
                half,
                full(wo.shape),
            ],
            out_specs=[row, full((seq, PAIR)), full((seq, PAIR)), full((2, SIDE, PAIR))],
            scratch_shapes=[
                pltpu.VMEM((seq, PAIR), f32),
                pltpu.VMEM((seq, PAIR), f32),
                pltpu.VMEM((3, 128, 2 * ROWS), f32),
                pltpu.VMEM((PAIR, D), f32),
            ],
        ),
        out_shape=[wide, wide, wide, jax.ShapeDtypeStruct((2, SIDE, PAIR), bf16)],
        compiler_params=params(),
        name="attend_back",
    )(lens, place, q, k, v, mixed, lse, mine, other, wo)


def mlp_kernel(
    place, tok, pas, vec, mine, other, cot, wo_mine, wo_other, w12,
    out_send, out_keep, gn_send, gn_keep, second_keep, grads,
    wom, woo, up, down, gup, gdown,
):
    i = pl.program_id(0)
    count = pl.num_programs(0)

    @pl.when(i == 0)
    def _():
        for h in range(2):
            for m in range(2):
                rows, cols = slice(h * SIDE, (h + 1) * SIDE), slice(m * PAIR, (m + 1) * PAIR)
                wom[rows, cols] = wo_mine[h, m]
                woo[rows, cols] = wo_other[h, m]
        for r in range(4):
            for m in range(2):
                rows, cols = slice(r * SIDE, (r + 1) * SIDE), slice(m * PAIR, (m + 1) * PAIR)
                up[rows, cols] = w12[2 * r + m]
                down[rows, cols] = w12[8 + 2 * r + m]
        gup[...] = jnp.zeros_like(gup)
        gdown[...] = jnp.zeros_like(gdown)

    first = embedded(tok[...], pas[...], vec[...])
    second = first + (nn(mine[...], wom[...]) + nn(other[...], woo[...]))
    hat, _ = hat_of(second)
    low = (hat * vec[PASSES + 2 : PASSES + 3] + vec[PASSES + 3 : PASSES + 4]).astype(bf16)
    upper = nn(low, up[...])
    square = upper * upper
    bent = jnp.tanh(gelu_coef * upper * (1.0 + 0.044715 * square))
    act = (0.5 * upper * (1.0 + bent)).astype(bf16)
    slope = 0.5 * (1.0 + bent) + (0.5 * gelu_coef) * upper * (1.0 - bent * bent) * (
        1.0 + (3 * 0.044715) * square
    )
    out_part = nn(act, down[...])
    grad_act = nt(cot[...], down[...])
    gdown[...] += tn(act, cot[...])
    grad_upper = (grad_act * slope).astype(bf16)
    gn_part = nt(grad_upper, up[...])
    gup[...] += tn(low, grad_upper)

    @pl.when(i < count // 2)
    def _():
        out_send[...] = out_part.astype(bf16)
        gn_send[...] = gn_part.astype(bf16)

    @pl.when(i >= count // 2)
    def _():
        out_keep[...] = out_part.astype(bf16)
        gn_keep[...] = gn_part
        second_keep[...] = second

    @pl.when(i == count - 1)
    def _():
        for r in range(4):
            for m in range(2):
                rows, cols = slice(r * SIDE, (r + 1) * SIDE), slice(m * PAIR, (m + 1) * PAIR)
                grads[2 * r + m] = gup[rows, cols].astype(bf16)
                grads[8 + 2 * r + m] = gdown[rows, cols].astype(bf16)


def mlp(place, tokens, passes, vec, mine, other, cotangent, wo_mine, wo_other, w12):
    seq = tokens.shape[0]
    count = seq // ROWS
    where = lambda i, s: lax.rem(i + (1 - s[0]) * (count // 2), count)
    row = lambda n: pl.BlockSpec((ROWS, n), lambda i, s: (where(i, s), 0))
    send = pl.BlockSpec((ROWS, D), lambda i, s: (jnp.minimum(i, count // 2 - 1), 0))
    keep = pl.BlockSpec((ROWS, D), lambda i, s: (jnp.maximum(i - count // 2, 0), 0))
    half = lambda kind: jax.ShapeDtypeStruct((seq // 2, D), kind)
    return pl.pallas_call(
        mlp_kernel,
        grid_spec=pltpu.PrefetchScalarGridSpec(
            num_scalar_prefetch=1,
            grid=(count,),
            in_specs=[
                row(D),
                pl.BlockSpec((1, ROWS), lambda i, s: (0, where(i, s))),
                full((16, D)),
                row(PAIR),
                row(PAIR),
                row(D),
                full(wo_mine.shape),
                full(wo_other.shape),
                full(w12.shape),
            ],
            out_specs=[send, keep, send, keep, keep, full((16, SIDE, PAIR))],
            scratch_shapes=[
                pltpu.VMEM((PAIR, D), bf16),
                pltpu.VMEM((PAIR, D), bf16),
                pltpu.VMEM((D, D), bf16),
                pltpu.VMEM((D, D), bf16),
                pltpu.VMEM((D, D), f32),
                pltpu.VMEM((D, D), f32),
            ],
        ),
        out_shape=[
            half(bf16),
            half(bf16),
            half(bf16),
            half(f32),
            half(f32),
            jax.ShapeDtypeStruct((16, SIDE, PAIR), bf16),
        ],
        compiler_params=params(),
        name="feed_forward",
    )(place, tokens, passes, vec, mine, other, cotangent, wo_mine, wo_other, w12)


def second_back_kernel(place, one, two, second, cot, vec, out, low, sums):
    @pl.when(pl.program_id(0) == 0)
    def _():
        sums[...] = jnp.zeros_like(sums)

    grad = one[...].astype(f32) + two[...].astype(f32)
    hat, root = hat_of(second[...])
    result = cot[...].astype(f32) + norm_back(hat, root, grad, vec[PASSES + 2 : PASSES + 3])
    out[...] = result
    low[...] = result.astype(bf16)
    sums[0:1] += jnp.sum(grad * hat, axis=0, keepdims=True)
    sums[1:2] += jnp.sum(grad, axis=0, keepdims=True)


def second_back(place, one, two, second, cotangent, vec):
    rows = one.shape[0]
    count = rows // ROWS
    row = pl.BlockSpec((ROWS, D), lambda i, s: (i, 0))
    mine = pl.BlockSpec((ROWS, D), lambda i, s: (i + s[0] * count, 0))
    return pl.pallas_call(
        second_back_kernel,
        grid_spec=pltpu.PrefetchScalarGridSpec(
            num_scalar_prefetch=1,
            grid=(count,),
            in_specs=[row, row, row, mine, full((16, D))],
            out_specs=[row, row, full((8, D))],
        ),
        out_shape=[
            jax.ShapeDtypeStruct((rows, D), f32),
            jax.ShapeDtypeStruct((rows, D), bf16),
            jax.ShapeDtypeStruct((8, D), f32),
        ],
        compiler_params=params(),
        name="second_back",
    )(place, one, two, second, cotangent, vec)


def project_back_kernel(place, norm, dq, dk, dv, cat, send, keep, grads, acc):
    i = pl.program_id(0)
    count = pl.num_programs(0)

    @pl.when(i == 0)
    def _():
        acc[...] = jnp.zeros_like(acc)

    total = nt(dq[...], cat[0]) + nt(dk[...], cat[1]) + nt(dv[...], cat[2])
    for x, grad in enumerate((dq, dk, dv)):
        mine = jnp.where(place[1] == 0, grad[:, :SIDE].astype(f32), grad[:, SIDE:].astype(f32))
        acc[x] += tn(norm[...], mine.astype(bf16))

    @pl.when(i < count // 2)
    def _():
        send[...] = total.astype(bf16)

    @pl.when(i >= count // 2)
    def _():
        keep[...] = total.astype(bf16)

    @pl.when(i == count - 1)
    def _():
        for x in range(3):
            for m in range(2):
                at = 2 * m * SIDE
                grads[2 * x + m] = jnp.concatenate(
                    [acc[x, at : at + SIDE], acc[x, at + SIDE : at + 2 * SIDE]], axis=1
                ).astype(bf16)


def project_back(place, norm, dq, dk, dv, cat):
    seq = norm.shape[0]
    count = seq // ROWS
    where = lambda i, s: lax.rem(i + (1 - s[0]) * (count // 2), count)
    row = lambda n: pl.BlockSpec((ROWS, n), lambda i, s: (where(i, s), 0))
    send = pl.BlockSpec((ROWS, D), lambda i, s: (jnp.minimum(i, count // 2 - 1), 0))
    keep = pl.BlockSpec((ROWS, D), lambda i, s: (jnp.maximum(i - count // 2, 0), 0))
    half = jax.ShapeDtypeStruct((seq // 2, D), bf16)
    return pl.pallas_call(
        project_back_kernel,
        grid_spec=pltpu.PrefetchScalarGridSpec(
            num_scalar_prefetch=1,
            grid=(count,),
            in_specs=[row(D), row(PAIR), row(PAIR), row(PAIR), full(cat.shape)],
            out_specs=[send, keep, full((6, SIDE, PAIR))],
            scratch_shapes=[pltpu.VMEM((3, D, SIDE), f32)],
        ),
        out_shape=[half, half, jax.ShapeDtypeStruct((6, SIDE, PAIR), bf16)],
        compiler_params=params(),
        name="project_back",
    )(place, norm, dq, dk, dv, cat)


def first_back_kernel(place, tok, pas, vec, one, two, grad_second, low, sums):
    @pl.when(pl.program_id(0) == 0)
    def _():
        sums[...] = jnp.zeros_like(sums)

    grad = one[...].astype(f32) + two[...].astype(f32)
    hat, root = hat_of(embedded(tok[...], pas[...], vec[...]))
    result = grad_second[...] + norm_back(hat, root, grad, vec[PASSES : PASSES + 1])
    low[...] = result.astype(bf16)
    chosen = one_hot(pas[...])
    high, mid, rest = split_three(result)
    sums[...] += nn(chosen, high) + nn(chosen, mid) + nn(chosen, rest)
    sums[PASSES : PASSES + 1] += jnp.sum(grad * hat, axis=0, keepdims=True)
    sums[PASSES + 1 : PASSES + 2] += jnp.sum(grad, axis=0, keepdims=True)


def first_back(place, tokens, passes, vec, one, two, grad_second):
    rows = one.shape[0]
    count = rows // ROWS
    row = pl.BlockSpec((ROWS, D), lambda i, s: (i, 0))
    mine = pl.BlockSpec((ROWS, D), lambda i, s: (i + s[0] * count, 0))
    return pl.pallas_call(
        first_back_kernel,
        grid_spec=pltpu.PrefetchScalarGridSpec(
            num_scalar_prefetch=1,
            grid=(count,),
            in_specs=[
                mine,
                pl.BlockSpec((1, ROWS), lambda i, s: (0, i + s[0] * count)),
                full((16, D)),
                row,
                row,
                row,
            ],
            out_specs=[row, full((16, D))],
        ),
        out_shape=[
            jax.ShapeDtypeStruct((rows, D), bf16),
            jax.ShapeDtypeStruct((16, D), f32),
        ],
        compiler_params=params(),
        name="first_back",
    )(place, tokens, passes, vec, one, two, grad_second)


def precondition(grad, weight, left, right, left_root, right_root):
    high = lax.Precision.HIGHEST
    left_new = decay * left + (1.0 - decay) * jnp.einsum(
        "...ij,...kj->...ik", grad, grad, precision=high
    )
    right_new = decay * right + (1.0 - decay) * jnp.einsum(
        "...ji,...jk->...ik", grad, grad, precision=high
    )
    half = jnp.einsum("...ij,...jk->...ik", left_root, grad, precision=high)
    step = jnp.einsum("...ij,...jk->...ik", half, right_root, precision=high)
    return (left_new, right_new, step, weight - rate_matrix * step)


def to_pairs(blocks):
    n = blocks.shape[0] // 2
    return blocks.reshape(n, 2, SIDE, SIDE).transpose(0, 2, 1, 3).reshape(n, SIDE, PAIR)


def from_pairs(pairs):
    n = pairs.shape[0]
    return pairs.reshape(n, SIDE, 2, SIDE).transpose(0, 2, 1, 3).reshape(2 * n, SIDE, SIDE)


def swap(value, bit):
    return lax.ppermute(value, "tensor", [(t, t ^ bit) for t in range(NT)])


def on_device(
    tokens,
    pass_ids,
    doc_lengths,
    cotangent,
    block_weights,
    vector_params,
    vector_moment,
    block_left,
    block_right,
    block_left_root,
    block_right_root,
):
    t = lax.axis_index("tensor")
    core, side = t % 2, t // 2
    place = jnp.stack([core, side]).astype(jnp.int32)
    lens = doc_lengths[0]
    seq = tokens.shape[0]
    passes = pass_ids.reshape(1, seq)
    total_blocks = (D // SIDE) * (4 + 2 * (FF // D))
    n_dp = lax.axis_size("dp")

    every = lax.all_gather(block_weights.astype(bf16), "dp", axis=1, tiled=True)[0]
    slots = every.shape[0]
    pairs = to_pairs(every[:total_blocks])
    vec = lax.all_gather(vector_params, "dp", axis=1, tiled=True)
    vec = jnp.pad(vec, ((0, 16 - vec.shape[0]), (0, 0)))
    shared = pairs[:8]
    shared_far = swap(shared, 2)
    both = jnp.where(side == 0, jnp.stack([shared, shared_far]), jnp.stack([shared_far, shared]))
    wq, wo_mine = both[:, :6], both[:, 6:]
    wo_other = swap(wo_mine, 1)
    w12 = pairs[8:]

    norm, q, k, v, cat = project(tokens, passes, vec, wq)
    mine, lse = attend(lens, q, k, v)
    other = swap(mine, 1)
    out_send, out_keep, gn_send, gn_keep, second, grads_12 = mlp(
        place, tokens, passes, vec, mine, other, cotangent, wo_mine, wo_other, w12
    )
    gn_chip = (gn_keep + swap(gn_send, 1).astype(f32)).astype(bf16)
    gn_far = swap(gn_chip, 2)
    grad_second, grad_attn, sums_two = second_back(place, gn_chip, gn_far, second, cotangent, vec)
    grad_attn_other = swap(grad_attn, 1)
    dq, dk, dv, grads_o = attend_back(
        lens, place, q, k, v, mine, lse, grad_attn, grad_attn_other, wo_mine
    )
    g1_send, g1_keep, grads_qkv = project_back(place, norm, dq, dk, dv, cat)
    low_half, sums_one = first_back(
        place, tokens, passes, vec, g1_keep, swap(g1_send, 1), grad_second
    )
    out_chip = (out_keep.astype(f32) + swap(out_send, 1).astype(f32)).astype(bf16)
    out_half = (second + (out_chip.astype(f32) + swap(out_chip, 2).astype(f32))).astype(bf16)

    def join(half):
        far = swap(half, 1)
        low = jnp.where(core == 0, half, far)
        high = jnp.where(core == 0, far, half)
        return jnp.concatenate([low, high], axis=0)

    output, input_grad = join(out_half), join(low_half)
    vector_part = jnp.concatenate([sums_one[: PASSES + 2], sums_two[:2]], axis=0)
    vector_part = vector_part + swap(vector_part, 1)
    grad_blocks = from_pairs(jnp.concatenate([grads_qkv, grads_o, grads_12], axis=0)).astype(f32)
    spare = jnp.zeros((slots - total_blocks, SIDE, SIDE), f32)
    grad_blocks = jnp.concatenate([grad_blocks, spare], axis=0)[None]
    owned = lax.psum_scatter(grad_blocks, "dp", scatter_dimension=1, tiled=True)
    vector_grad = lax.psum_scatter(vector_part, "dp", scatter_dimension=1, tiled=True)
    left_new, right_new, step, weight_new = precondition(
        owned, block_weights, block_left, block_right, block_left_root, block_right_root
    )
    moment_new = decay * vector_moment + (1.0 - decay) * vector_grad * vector_grad
    vector_new = vector_params - rate_vector * vector_grad / (jnp.sqrt(moment_new) + moment_eps)
    return (
        output,
        input_grad,
        left_new,
        right_new,
        step,
        weight_new,
        vector_grad,
        moment_new,
        vector_new,
    )


def solution(mesh):
    rows, line = P("dp", None), P(None, "dp")
    block = P("tensor", "dp", None, None)
    return jax.shard_map(
        on_device,
        mesh=mesh,
        in_specs=(rows, P("dp"), rows, rows, block, line, line, block, block, block, block),
        out_specs=(rows, rows, block, block, block, block, line, line, line),
        check_vma=False,
    )
```

```python
import functools

import jax
import jax.numpy as jnp
from jax import lax
from jax.experimental import pallas as pl
from jax.experimental.pallas import tpu as pltpu
from jax.sharding import PartitionSpec as P

D = 768
HD = 64
FF = 3072
PASSES = 5
SIDE = 192
PAIR = 2 * SIDE
ROWS = 256
DOCS = 8
NT = 4

norm_eps = 1e-05
moment_eps = 1e-08
rate_matrix = 0.03
rate_vector = 0.2
decay = 0.5
gelu_coef = 0.7978845608028654
masked_score = -1e30
f32 = jnp.float32
bf16 = jnp.bfloat16
MESH = pl.DeviceIdType.MESH
VMEM_LIMIT = 56 * 1024 * 1024


def nn(a, b):
    return lax.dot_general(a, b, (((1,), (0,)), ((), ())), preferred_element_type=f32)


def nt(a, b):
    return lax.dot_general(a, b, (((1,), (1,)), ((), ())), preferred_element_type=f32)


def tn(a, b):
    return lax.dot_general(a, b, (((0,), (0,)), ((), ())), preferred_element_type=f32)


def split_three(value):
    high = value.astype(bf16)
    rest = value - high.astype(f32)
    mid = rest.astype(bf16)
    return high, mid, (rest - mid.astype(f32)).astype(bf16)


def one_hot(pass_row):
    kinds = lax.broadcasted_iota(jnp.int32, (16, pass_row.shape[1]), 0)
    return (kinds == pass_row).astype(f32).astype(bf16)


def embedded(tokens, pass_row, vec):
    chosen = one_hot(pass_row)
    high, mid, low = split_three(vec)
    return tokens.astype(f32) + (tn(chosen, high) + tn(chosen, mid) + tn(chosen, low))


def hat_of(hidden):
    mean = jnp.mean(hidden, axis=-1, keepdims=True)
    center = hidden - mean
    spread = jnp.mean(center * center, axis=-1, keepdims=True)
    root = lax.rsqrt(spread + norm_eps)
    return center * root, root


def norm_back(hat, root, grad, gain):
    scaled = grad * gain
    first = jnp.mean(scaled, axis=-1, keepdims=True)
    second = jnp.mean(scaled * hat, axis=-1, keepdims=True)
    return root * (scaled - first - hat * second)


def params(**kw):
    return pltpu.CompilerParams(vmem_limit_bytes=VMEM_LIMIT, **kw)


def full(shape):
    return pl.BlockSpec(shape, lambda *_: (0,) * len(shape))


def gather_kernel(own, vec_own, all_pairs, vec_out, pack, vec_pack, vec_land, *sems):
    (s_z1, r_z1, s_x1, r_x1, s_y1, r_y1, s_d1, r_d1, s_l, r_l, s_r, r_r, s_x2, r_x2, s_y2, r_y2, s_v, r_v, loc) = sems
    dp, t = lax.axis_index("dp"), lax.axis_index("tensor")
    z, x = dp // 2, dp % 2
    y, core = t // 2, t % 2
    far_x, far_y = z * 2 + (1 - x), (1 - y) * 2 + core

    barrier = pltpu.get_barrier_semaphore()
    peers = [lax.rem(dp + k, 8) for k in range(1, 8)]
    for peer in peers:
        pl.semaphore_signal(barrier, inc=1, device_id={"dp": peer, "tensor": t}, device_id_type=MESH)
    pl.semaphore_signal(barrier, inc=1, device_id={"dp": dp, "tensor": far_y}, device_id_type=MESH)

    for m in range(3):
        pack[m] = jnp.concatenate([own[0, 2 * m], own[0, 2 * m + 1]], axis=1).astype(bf16)
    vec_pack[...] = jnp.zeros_like(vec_pack)
    vec_pack[0 : PASSES + 4, 0 : D // 8] = vec_own[...]
    pl.semaphore_wait(barrier, 8)

    started = []

    def send(src, dst, s_sem, r_sem, dp_to, t_to, cond=None):
        copy = pltpu.make_async_remote_copy(
            src_ref=src,
            dst_ref=dst,
            send_sem=s_sem,
            recv_sem=r_sem,
            device_id={"dp": dp_to, "tensor": t_to},
            device_id_type=MESH,
        )
        started.append((cond, copy))
        if cond is None:
            copy.start()
        else:
            pl.when(cond)(copy.start)

    def arrived(dst, r_sem, cond=None):
        copy = pltpu.make_async_remote_copy(
            src_ref=dst,
            dst_ref=dst,
            send_sem=loc,
            recv_sem=r_sem,
            device_id={"dp": far_x, "tensor": t},
            device_id_type=MESH,
        )
        if cond is None:
            copy.wait_recv()
        else:
            pl.when(cond)(copy.wait_recv)

    own_copy = pltpu.make_async_copy(pack, all_pairs.at[y, pl.ds(3 * dp, 3)], loc)
    own_copy.start()

    for m in range(3):
        send(pack.at[m], all_pairs.at[y, 3 * dp + m], s_l.at[0, m], r_l.at[0, m], dp - 2, t, z > 0)
    for k, peer in enumerate(peers):
        send(vec_pack, vec_land.at[dp], s_v.at[k], r_v.at[dp], peer, t)
    for m in range(3):
        send(pack.at[m], all_pairs.at[y, 3 * dp + m], s_x2.at[z, m], r_x2.at[z, m], far_x, t, z > m)
    own_copy.wait()

    half = SIDE // 2

    def piece(side, column, k):
        return all_pairs.at[side, 3 * column + k // 2, pl.ds((k % 2) * half, half)]

    def diagonal(k):
        arrived(piece(y, 1 - x, k), r_x1.at[k])
        send(piece(y, 1 - x, k), piece(y, 1 - x, k), s_d1.at[k], r_d1.at[k], dp, far_y)

    def from_right(d, m):
        arrived(all_pairs.at[y, 3 * dp + 6 * d + m], r_l.at[d - 1, m], z + d < 4)
        if d < 3:
            ref = all_pairs.at[y, 3 * dp + 6 * d + m]
            send(ref, ref, s_l.at[d, m], r_l.at[d, m], dp - 2, t, (z + d < 4) & (z > 0))

    def right_along_x(d, m):
        ref = all_pairs.at[y, 3 * dp + 6 * d + m]
        send(ref, ref, s_x2.at[z + d, m], r_x2.at[z + d, m], far_x, t, z + d < 4)

    for k in range(6):
        arrived(piece(y, x, k), r_z1.at[k], z > 0)
        send(piece(y, x, k), piece(y, x, k), s_z1.at[k], r_z1.at[k], dp + 2, t, z < 3)
        send(piece(y, x, k), piece(y, x, k), s_x1.at[k], r_x1.at[k], far_x, t)
        send(piece(y, x, k), piece(y, x, k), s_y1.at[k], r_y1.at[k], dp, far_y)
        if k >= 1:
            diagonal(k - 1)
        if k % 2 == 1:
            from_right(1, k // 2)
    diagonal(5)

    for m in range(3):
        send(pack.at[m], all_pairs.at[y, 3 * dp + m], s_x2.at[z, m], r_x2.at[z, m], far_x, t, (z > 0) & (z <= m))
    for m in range(3):
        send(pack.at[m], all_pairs.at[y, 3 * dp + m], s_r.at[0, m], r_r.at[0, m], dp + 2, t, (z > 0) & (z < 3))
    for m in range(3):
        right_along_x(1, m)
    for d in (2, 3):
        for m in range(3):
            from_right(d, m)
            right_along_x(d, m)
    for d in (1, 2):
        for m in range(3):
            ref = all_pairs.at[y, 3 * dp - 6 * d + m]
            arrived(ref, r_r.at[d - 1, m], z - d > 0)
            if d == 1:
                send(ref, ref, s_r.at[1, m], r_r.at[1, m], dp + 2, t, (z - d > 0) & (z < 3))
            send(ref, ref, s_x2.at[z - d, m], r_x2.at[z - d, m], far_x, t, z - d > 0)
    for m in range(2):
        ref = all_pairs.at[y, 6 + m]
        arrived(ref, r_x2.at[1, m], x == 1)
        send(ref, ref, s_y2.at[m], r_y2.at[m], dp, far_y)

    for k in range(6):
        arrived(piece(1 - y, x, k), r_y1.at[k])
        arrived(piece(1 - y, 1 - x, k), r_d1.at[k])
    for w in range(1, 4):
        for m in range(3):
            ref = all_pairs.at[y, 6 * w + 3 * (1 - x) + m]
            if w == 1 and m < 2:
                arrived(ref, r_x2.at[w, m], x == 0)
            else:
                arrived(ref, r_x2.at[w, m])
    for m in range(2):
        arrived(all_pairs.at[1 - y, 6 + m], r_y2.at[m])
    for peer in peers:
        arrived(vec_land.at[peer], r_v.at[peer])
    vec_land[dp] = vec_pack[...]
    vec_out[...] = jnp.concatenate([vec_land[d][:, : D // 8] for d in range(8)], axis=1)
    for cond, copy in started:
        if cond is None:
            copy.wait_send()
        else:
            pl.when(cond)(copy.wait_send)


def gather(block_weights, vector_params):
    dma = pltpu.SemaphoreType.DMA
    sizes = [(6,)] * 8 + [(3, 3)] * 2 + [(2, 3)] * 2 + [(4, 3)] * 2 + [(2,)] * 2 + [(7,), (8,)]
    return pl.pallas_call(
        gather_kernel,
        in_specs=[pl.BlockSpec(memory_space=pltpu.VMEM)] * 2,
        out_specs=[pl.BlockSpec(memory_space=pl.ANY), pl.BlockSpec(memory_space=pltpu.VMEM)],
        out_shape=[
            jax.ShapeDtypeStruct((2, 24, SIDE, PAIR), bf16),
            jax.ShapeDtypeStruct((16, D), f32),
        ],
        scratch_shapes=[
            pltpu.VMEM((3, SIDE, PAIR), bf16),
            pltpu.VMEM((16, 128), f32),
            pltpu.VMEM((8, 16, 128), f32),
        ]
        + [dma(size) for size in sizes]
        + [dma],
        compiler_params=params(collective_id=0, has_side_effects=True),
        name="gather",
    )(block_weights, vector_params)


def project_kernel(tok, pas, vec, wq, norm, q, k, v, cat):
    @pl.when(pl.program_id(0) == 0)
    def _():
        for x in range(3):
            for i in range(4):
                at = (i % 2) * SIDE
                parts = [wq[h, 2 * x + i // 2][:, at : at + SIDE] for h in range(2)]
                cat[x, i * SIDE : (i + 1) * SIDE, :] = jnp.concatenate(parts, axis=1)

    first = embedded(tok[...], pas[...], vec[...])
    hat, _ = hat_of(first)
    low = (hat * vec[PASSES : PASSES + 1] + vec[PASSES + 1 : PASSES + 2]).astype(bf16)
    norm[...] = low
    for x, out in enumerate((q, k, v)):
        out[...] = nn(low, cat[x]).astype(bf16)


def project(tokens, passes, vec, wq):
    seq = tokens.shape[0]
    row = lambda n: pl.BlockSpec((ROWS, n), lambda i: (i, 0))
    wide = jax.ShapeDtypeStruct((seq, PAIR), bf16)
    return pl.pallas_call(
        project_kernel,
        grid=(seq // ROWS,),
        in_specs=[
            row(D),
            pl.BlockSpec((1, ROWS), lambda i: (0, i)),
            full((16, D)),
            full((2, 6, SIDE, PAIR)),
        ],
        out_specs=[row(D), row(PAIR), row(PAIR), row(PAIR), full((3, D, PAIR))],
        out_shape=[
            jax.ShapeDtypeStruct((seq, D), bf16),
            wide,
            wide,
            wide,
            jax.ShapeDtypeStruct((3, D, PAIR), bf16),
        ],
        compiler_params=params(),
        name="project",
    )(tokens, passes, vec, wq)


def doc_state(lens, base):
    rows = base + lax.broadcasted_iota(jnp.int32, (1, ROWS), 1)
    rows = jnp.concatenate([rows, rows], axis=1)
    begin = jnp.int32(0)
    first = jnp.int32(0)
    starts = jnp.zeros((1, 2 * ROWS), jnp.int32)
    for c in range(DOCS):
        starts = jnp.where(rows >= begin, begin, starts)
        first = jnp.where(base >= begin, begin, first)
        begin = begin + lens[c]
    return rows, starts, first


def two_heads(block):
    left = lax.broadcasted_iota(jnp.int32, block.shape, 1) < HD
    none = jnp.zeros_like(block)
    return jnp.concatenate([jnp.where(left, block, none), jnp.where(left, none, block)], axis=0)


def one_above(both):
    return jnp.concatenate([both[:HD, :ROWS], both[HD:, ROWS:]], axis=0).T


def attend_kernel(lens, q, k, v, out, lse, top, total, acc):
    i = pl.program_id(0)
    base = i * ROWS
    rows, starts, first = doc_state(lens, base)
    pairs = [two_heads(q[:, p * 128 : (p + 1) * 128] * bf16(0.125)) for p in range(3)]
    for p in range(3):
        top[p] = jnp.full((1, 2 * ROWS), masked_score, f32)
        total[p] = jnp.zeros((1, 2 * ROWS), f32)
        acc[p] = jnp.zeros((128, 2 * ROWS), f32)

    def step(j, carry):
        at = pl.multiple_of(j * ROWS, ROWS)
        keys = at + lax.broadcasted_iota(jnp.int32, (ROWS, 2 * ROWS), 0)
        seen = (keys >= starts) & (keys <= rows)
        for p in range(3):
            cols = slice(p * 128, (p + 1) * 128)
            scores = jnp.where(seen, nt(k[pl.ds(at, ROWS), cols], pairs[p]), masked_score)
            before = top[p]
            now = jnp.maximum(before, jnp.max(scores, axis=0, keepdims=True))
            probs = jnp.exp(scores - now)
            fade = jnp.exp(before - now)
            top[p] = now
            total[p] = total[p] * fade + jnp.sum(probs, axis=0, keepdims=True)
            acc[p] = acc[p] * fade + tn(v[pl.ds(at, ROWS), cols], probs.astype(bf16))
        return carry

    lax.fori_loop(first // ROWS, i + 1, step, 0)
    lines = []
    for p in range(3):
        out[:, p * 128 : (p + 1) * 128] = one_above(acc[p] / total[p]).astype(bf16)
        line = top[p] + jnp.log(total[p])
        lines += [line[:, :ROWS], line[:, ROWS:]]
    lse[...] = jnp.concatenate(lines + lines[:2], axis=0)


def attend(lens, q, k, v):
    seq = q.shape[0]
    row = pl.BlockSpec((ROWS, PAIR), lambda i, s: (i, 0))
    return pl.pallas_call(
        attend_kernel,
        grid_spec=pltpu.PrefetchScalarGridSpec(
            num_scalar_prefetch=1,
            grid=(seq // ROWS,),
            in_specs=[row, full((seq, PAIR)), full((seq, PAIR))],
            out_specs=[row, pl.BlockSpec((8, ROWS), lambda i, s: (0, i))],
            scratch_shapes=[
                pltpu.VMEM((3, 1, 2 * ROWS), f32),
                pltpu.VMEM((3, 1, 2 * ROWS), f32),
                pltpu.VMEM((3, 128, 2 * ROWS), f32),
            ],
        ),
        out_shape=[
            jax.ShapeDtypeStruct((seq, PAIR), bf16),
            jax.ShapeDtypeStruct((8, seq), f32),
        ],
        compiler_params=params(),
        name="attend",
    )(lens, q, k, v)


def attend_back_kernel(
    lens, place, q, k, v, mixed, lse, mine, other, wo, dq, dk, dv, gwo, dk_acc, dv_acc, dq_acc, gwo_acc
):
    i = pl.program_id(0)
    count = pl.num_programs(0)
    base = i * ROWS

    @pl.when(i == 0)
    def _():
        dk_acc[...] = jnp.zeros_like(dk_acc)
        dv_acc[...] = jnp.zeros_like(dv_acc)
        gwo_acc[...] = jnp.zeros_like(gwo_acc)

    half = (i >= count // 2).astype(jnp.int32)
    grad = jnp.where(half == place[0], mine[...], other[...])
    weight = jnp.concatenate(
        [jnp.concatenate([wo[h, 0], wo[h, 1]], axis=1) for h in range(2)], axis=0
    )
    grad_mixed = nt(grad, weight).astype(bf16)
    gwo_acc[...] += tn(mixed[...], grad)

    rows, starts, first = doc_state(lens, base)
    heads = lax.broadcasted_iota(jnp.int32, (8, 128), 0)
    lanes = lax.broadcasted_iota(jnp.int32, (8, 128), 1)
    pick = (lanes // HD == heads).astype(f32)
    queries, grads, inner, lines = [], [], [], []
    for p in range(3):
        cols = slice(p * 128, (p + 1) * 128)
        queries.append(two_heads(q[:, cols] * bf16(0.125)))
        grads.append(two_heads(grad_mixed[:, cols]))
        product = grad_mixed[:, cols].astype(f32) * mixed[:, cols].astype(f32)
        sums = lax.dot_general(
            pick,
            product,
            (((1,), (1,)), ((), ())),
            precision=lax.Precision.HIGHEST,
            preferred_element_type=f32,
        )
        inner.append(jnp.concatenate([sums[0:1], sums[1:2]], axis=1))
        lines.append(jnp.concatenate([lse[2 * p : 2 * p + 1], lse[2 * p + 1 : 2 * p + 2]], axis=1))
        dq_acc[p] = jnp.zeros((128, 2 * ROWS), f32)

    def step(j, carry):
        at = pl.multiple_of(j * ROWS, ROWS)
        keys = at + lax.broadcasted_iota(jnp.int32, (ROWS, 2 * ROWS), 0)
        seen = (keys >= starts) & (keys <= rows)
        here = pl.ds(at, ROWS)
        for p in range(3):
            cols = slice(p * 128, (p + 1) * 128)
            kb = k[here, cols]
            scores = jnp.where(seen, nt(kb, queries[p]) - lines[p], masked_score)
            probs = jnp.exp(scores)
            grad_probs = nt(v[here, cols], grads[p])
            grad_scores = (probs * (grad_probs - inner[p])).astype(bf16)
            dv_acc[here, cols] += nn(probs.astype(bf16), grads[p])
            dk_acc[here, cols] += nn(grad_scores, queries[p])
            dq_acc[p] += tn(kb, grad_scores)
        return carry

    lax.fori_loop(first // ROWS, i + 1, step, 0)
    for p in range(3):
        dq[:, p * 128 : (p + 1) * 128] = (one_above(dq_acc[p]) * 0.125).astype(bf16)

    @pl.when(i == count - 1)
    def _():
        dk[...] = dk_acc[...].astype(bf16)
        dv[...] = dv_acc[...].astype(bf16)
        at = pl.multiple_of(place[1] * SIDE, SIDE)
        for m in range(2):
            gwo[m] = gwo_acc[pl.ds(at, SIDE), m * PAIR : (m + 1) * PAIR].astype(bf16)


def attend_back(lens, place, q, k, v, mixed, lse, mine, other, wo):
    seq = q.shape[0]
    count = seq // ROWS
    row = pl.BlockSpec((ROWS, PAIR), lambda i, s, t: (i, 0))
    half = pl.BlockSpec((ROWS, D), lambda i, s, t: (lax.rem(i, count // 2), 0))
    wide = jax.ShapeDtypeStruct((seq, PAIR), bf16)
    return pl.pallas_call(
        attend_back_kernel,
        grid_spec=pltpu.PrefetchScalarGridSpec(
            num_scalar_prefetch=2,
            grid=(count,),
            in_specs=[
                row,
                full((seq, PAIR)),
                full((seq, PAIR)),
                row,
                pl.BlockSpec((8, ROWS), lambda i, s, t: (0, i)),
                half,
                half,
                pl.BlockSpec((2, 2, SIDE, PAIR), lambda i, s, t: (0, 3, 0, 0)),
            ],
            out_specs=[row, full((seq, PAIR)), full((seq, PAIR)), full((2, SIDE, PAIR))],
            scratch_shapes=[
                pltpu.VMEM((seq, PAIR), f32),
                pltpu.VMEM((seq, PAIR), f32),
                pltpu.VMEM((3, 128, 2 * ROWS), f32),
                pltpu.VMEM((PAIR, D), f32),
            ],
        ),
        out_shape=[wide, wide, wide, jax.ShapeDtypeStruct((2, SIDE, PAIR), bf16)],
        compiler_params=params(),
        name="attend_back",
    )(lens, place, q, k, v, mixed, lse, mine, other, wo)


def mlp_kernel(
    place, tok, pas, vec, mine, other, cot, wo_mine, wo_other, w1, w2,
    out_send, out_keep, gn_send, gn_keep, second_keep, g_send, g_keep,
    wom, woo, up, down, gup, gdown,
):
    i = pl.program_id(0)
    count = pl.num_programs(0)

    @pl.when(i == 0)
    def _():
        for h in range(2):
            for m in range(2):
                rows, cols = slice(h * SIDE, (h + 1) * SIDE), slice(m * PAIR, (m + 1) * PAIR)
                wom[rows, cols] = wo_mine[h, m]
                woo[rows, cols] = wo_other[h, m]
        for r in range(4):
            for m in range(2):
                rows, cols = slice(r * SIDE, (r + 1) * SIDE), slice(m * PAIR, (m + 1) * PAIR)
                up[rows, cols] = w1[0, 2 * r + m]
                down[rows, cols] = w2[0, 2 * r + m]
        gup[...] = jnp.zeros_like(gup)
        gdown[...] = jnp.zeros_like(gdown)

    first = embedded(tok[...], pas[...], vec[...])
    second = first + (nn(mine[...], wom[...]) + nn(other[...], woo[...]))
    hat, _ = hat_of(second)
    low = (hat * vec[PASSES + 2 : PASSES + 3] + vec[PASSES + 3 : PASSES + 4]).astype(bf16)
    upper = nn(low, up[...])
    square = upper * upper
    bent = jnp.tanh(gelu_coef * upper * (1.0 + 0.044715 * square))
    act = (0.5 * upper * (1.0 + bent)).astype(bf16)
    slope = 0.5 * (1.0 + bent) + (0.5 * gelu_coef) * upper * (1.0 - bent * bent) * (
        1.0 + (3 * 0.044715) * square
    )
    out_part = nn(act, down[...])
    grad_act = nt(cot[...], down[...])
    gdown[...] += tn(act, cot[...])
    grad_upper = (grad_act * slope).astype(bf16)
    gn_part = nt(grad_upper, up[...])
    gup[...] += tn(low, grad_upper)

    @pl.when(i < count // 2)
    def _():
        out_send[...] = out_part.astype(bf16)
        gn_send[...] = gn_part.astype(bf16)

    @pl.when(i >= count // 2)
    def _():
        out_keep[...] = out_part.astype(bf16)
        gn_keep[...] = gn_part
        second_keep[...] = second

    @pl.when(i == count - 1)
    def _():
        for r in range(4):
            for m in range(2):
                rows, cols = slice(r * SIDE, (r + 1) * SIDE), slice(m * PAIR, (m + 1) * PAIR)
                for at, total in ((8, gup), (16, gdown)):
                    pair = at + 2 * r + m
                    slot, column = (pair // 6 - 1) * 3 + pair % 3, pair // 3 % 2
                    value = total[rows, cols].astype(bf16)

                    @pl.when(place[2] == column)
                    def _():
                        g_keep[slot] = value

                    @pl.when(place[2] != column)
                    def _():
                        g_send[slot] = value
        for slot in range(2):

            @pl.when(place[2] == 0)
            def _():
                g_keep[slot] = jnp.zeros((SIDE, PAIR), bf16)

            @pl.when(place[2] != 0)
            def _():
                g_send[slot] = jnp.zeros((SIDE, PAIR), bf16)


def mlp(place, tokens, passes, vec, mine, other, cotangent, pairs, wo_other):
    seq = tokens.shape[0]
    count = seq // ROWS
    where = lambda i, s: lax.rem(i + (1 - s[0]) * (count // 2), count)
    row = lambda n: pl.BlockSpec((ROWS, n), lambda i, s: (where(i, s), 0))
    send = pl.BlockSpec((ROWS, D), lambda i, s: (jnp.minimum(i, count // 2 - 1), 0))
    keep = pl.BlockSpec((ROWS, D), lambda i, s: (jnp.maximum(i - count // 2, 0), 0))
    half = lambda kind: jax.ShapeDtypeStruct((seq // 2, D), kind)
    return pl.pallas_call(
        mlp_kernel,
        grid_spec=pltpu.PrefetchScalarGridSpec(
            num_scalar_prefetch=1,
            grid=(count,),
            in_specs=[
                row(D),
                pl.BlockSpec((1, ROWS), lambda i, s: (0, where(i, s))),
                full((16, D)),
                row(PAIR),
                row(PAIR),
                row(D),
                pl.BlockSpec((2, 2, SIDE, PAIR), lambda i, s: (0, 3, 0, 0)),
                full(wo_other.shape),
                pl.BlockSpec((1, 8, SIDE, PAIR), lambda i, s: (s[1], 1, 0, 0)),
                pl.BlockSpec((1, 8, SIDE, PAIR), lambda i, s: (s[1], 2, 0, 0)),
            ],
            out_specs=[send, keep, send, keep, keep, full((9, SIDE, PAIR)), full((9, SIDE, PAIR))],
            scratch_shapes=[
                pltpu.VMEM((PAIR, D), bf16),
                pltpu.VMEM((PAIR, D), bf16),
                pltpu.VMEM((D, D), bf16),
                pltpu.VMEM((D, D), bf16),
                pltpu.VMEM((D, D), f32),
                pltpu.VMEM((D, D), f32),
            ],
        ),
        out_shape=[
            half(bf16),
            half(bf16),
            half(bf16),
            half(f32),
            half(f32),
            jax.ShapeDtypeStruct((9, SIDE, PAIR), bf16),
            jax.ShapeDtypeStruct((9, SIDE, PAIR), bf16),
        ],
        compiler_params=params(),
        name="feed_forward",
    )(place, tokens, passes, vec, mine, other, cotangent, pairs, wo_other, pairs, pairs)


def second_back_kernel(place, one, two, second, cot, vec, out, low, sums):
    @pl.when(pl.program_id(0) == 0)
    def _():
        sums[...] = jnp.zeros_like(sums)

    grad = one[...].astype(f32) + two[...].astype(f32)
    hat, root = hat_of(second[...])
    result = cot[...].astype(f32) + norm_back(hat, root, grad, vec[PASSES + 2 : PASSES + 3])
    out[...] = result
    low[...] = result.astype(bf16)
    sums[0:1] += jnp.sum(grad * hat, axis=0, keepdims=True)
    sums[1:2] += jnp.sum(grad, axis=0, keepdims=True)


def second_back(place, one, two, second, cotangent, vec):
    rows = one.shape[0]
    count = rows // ROWS
    row = pl.BlockSpec((ROWS, D), lambda i, s: (i, 0))
    mine = pl.BlockSpec((ROWS, D), lambda i, s: (i + s[0] * count, 0))
    return pl.pallas_call(
        second_back_kernel,
        grid_spec=pltpu.PrefetchScalarGridSpec(
            num_scalar_prefetch=1,
            grid=(count,),
            in_specs=[row, row, row, mine, full((16, D))],
            out_specs=[row, row, full((8, D))],
        ),
        out_shape=[
            jax.ShapeDtypeStruct((rows, D), f32),
            jax.ShapeDtypeStruct((rows, D), bf16),
            jax.ShapeDtypeStruct((8, D), f32),
        ],
        compiler_params=params(),
        name="second_back",
    )(place, one, two, second, cotangent, vec)


def project_back_kernel(place, norm, dq, dk, dv, cat, send, keep, g_send, g_keep, acc):
    i = pl.program_id(0)
    count = pl.num_programs(0)

    @pl.when(i == 0)
    def _():
        acc[...] = jnp.zeros_like(acc)

    total = nt(dq[...], cat[0]) + nt(dk[...], cat[1]) + nt(dv[...], cat[2])
    for x, grad in enumerate((dq, dk, dv)):
        mine = jnp.where(place[1] == 0, grad[:, :SIDE].astype(f32), grad[:, SIDE:].astype(f32))
        acc[x] += tn(norm[...], mine.astype(bf16))

    @pl.when(i < count // 2)
    def _():
        send[...] = total.astype(bf16)

    @pl.when(i >= count // 2)
    def _():
        keep[...] = total.astype(bf16)

    @pl.when(i == count - 1)
    def _():
        for x in range(3):
            for m in range(2):
                at = 2 * m * SIDE
                value = jnp.concatenate(
                    [acc[x, at : at + SIDE], acc[x, at + SIDE : at + 2 * SIDE]], axis=1
                ).astype(bf16)
                slot, column = (2 * x + m) % 3, (2 * x + m) // 3

                @pl.when(place[2] == column)
                def _():
                    g_keep[slot] = value

                @pl.when(place[2] != column)
                def _():
                    g_send[slot] = value


def project_back(place, norm, dq, dk, dv, cat):
    seq = norm.shape[0]
    count = seq // ROWS
    where = lambda i, s: lax.rem(i + (1 - s[0]) * (count // 2), count)
    row = lambda n: pl.BlockSpec((ROWS, n), lambda i, s: (where(i, s), 0))
    send = pl.BlockSpec((ROWS, D), lambda i, s: (jnp.minimum(i, count // 2 - 1), 0))
    keep = pl.BlockSpec((ROWS, D), lambda i, s: (jnp.maximum(i - count // 2, 0), 0))
    half = jax.ShapeDtypeStruct((seq // 2, D), bf16)
    return pl.pallas_call(
        project_back_kernel,
        grid_spec=pltpu.PrefetchScalarGridSpec(
            num_scalar_prefetch=1,
            grid=(count,),
            in_specs=[row(D), row(PAIR), row(PAIR), row(PAIR), full(cat.shape)],
            out_specs=[send, keep, full((3, SIDE, PAIR)), full((3, SIDE, PAIR))],
            scratch_shapes=[pltpu.VMEM((3, D, SIDE), f32)],
        ),
        out_shape=[half, half] + [jax.ShapeDtypeStruct((3, SIDE, PAIR), bf16)] * 2,
        compiler_params=params(),
        name="project_back",
    )(place, norm, dq, dk, dv, cat)


def first_back_kernel(place, tok, pas, vec, one, two, grad_second, low, sums):
    @pl.when(pl.program_id(0) == 0)
    def _():
        sums[...] = jnp.zeros_like(sums)

    grad = one[...].astype(f32) + two[...].astype(f32)
    hat, root = hat_of(embedded(tok[...], pas[...], vec[...]))
    result = grad_second[...] + norm_back(hat, root, grad, vec[PASSES : PASSES + 1])
    low[...] = result.astype(bf16)
    chosen = one_hot(pas[...])
    high, mid, rest = split_three(result)
    sums[...] += nn(chosen, high) + nn(chosen, mid) + nn(chosen, rest)
    sums[PASSES : PASSES + 1] += jnp.sum(grad * hat, axis=0, keepdims=True)
    sums[PASSES + 1 : PASSES + 2] += jnp.sum(grad, axis=0, keepdims=True)


def first_back(place, tokens, passes, vec, one, two, grad_second):
    rows = one.shape[0]
    count = rows // ROWS
    row = pl.BlockSpec((ROWS, D), lambda i, s: (i, 0))
    mine = pl.BlockSpec((ROWS, D), lambda i, s: (i + s[0] * count, 0))
    return pl.pallas_call(
        first_back_kernel,
        grid_spec=pltpu.PrefetchScalarGridSpec(
            num_scalar_prefetch=1,
            grid=(count,),
            in_specs=[
                mine,
                pl.BlockSpec((1, ROWS), lambda i, s: (0, i + s[0] * count)),
                full((16, D)),
                row,
                row,
                row,
            ],
            out_specs=[row, full((16, D))],
        ),
        out_shape=[
            jax.ShapeDtypeStruct((rows, D), bf16),
            jax.ShapeDtypeStruct((16, D), f32),
        ],
        compiler_params=params(),
        name="first_back",
    )(place, tokens, passes, vec, one, two, grad_second)


def precondition(grad, weight, left, right, left_root, right_root):
    high = lax.Precision.HIGHEST
    left_new = decay * left + (1.0 - decay) * jnp.einsum(
        "...ij,...kj->...ik", grad, grad, precision=high
    )
    right_new = decay * right + (1.0 - decay) * jnp.einsum(
        "...ji,...jk->...ik", grad, grad, precision=high
    )
    half = jnp.einsum("...ij,...jk->...ik", left_root, grad, precision=high)
    step = jnp.einsum("...ij,...jk->...ik", half, right_root, precision=high)
    return (left_new, right_new, step, weight - rate_matrix * step)


def to_pairs(blocks):
    n = blocks.shape[0] // 2
    return blocks.reshape(n, 2, SIDE, SIDE).transpose(0, 2, 1, 3).reshape(n, SIDE, PAIR)


def from_pairs(pairs):
    n = pairs.shape[0]
    return pairs.reshape(n, SIDE, 2, SIDE).transpose(0, 2, 1, 3).reshape(2 * n, SIDE, SIDE)


def swap(value, bit):
    return lax.ppermute(value, "tensor", [(t, t ^ bit) for t in range(NT)])


def hop_x(value):
    return lax.ppermute(value, "dp", [(d, d ^ 1) for d in range(8)])


def hop_z(value, turn, ends):
    pairs = [(d, (d + 2 * turn) % 8) for d in range(8) if (d // 2 + turn) % 4 in ends]
    return lax.ppermute(value, "dp", pairs)


def owners_sum(keep, send, z, ends):
    both = (keep.astype(f32) + hop_x(send).astype(f32)).astype(bf16)

    def term(turn):
        at = jnp.clip((z + turn) % 4 - ends[0], 0, len(ends) - 1)
        return lax.dynamic_index_in_dim(both, at, 0, keepdims=False)

    total = term(0).astype(f32)
    for turn in (1, 2, 3):
        total = total + hop_z(term(turn), turn, ends).astype(f32)
    return total


def on_device(
    tokens,
    pass_ids,
    doc_lengths,
    cotangent,
    block_weights,
    vector_params,
    vector_moment,
    block_left,
    block_right,
    block_left_root,
    block_right_root,
):
    t, dp = lax.axis_index("tensor"), lax.axis_index("dp")
    core, side = t % 2, t // 2
    n_dp = lax.axis_size("dp")
    small = n_dp == 8
    z, column = (dp // 2, dp % 2) if small else (0, 0)
    place = jnp.stack([core, side, jnp.asarray(column, jnp.int32)]).astype(jnp.int32)
    lens = doc_lengths[0]
    seq = tokens.shape[0]
    passes = pass_ids.reshape(1, seq)
    total_blocks = (D // SIDE) * (4 + 2 * (FF // D))
    slots = block_weights.shape[1] * n_dp

    if small:
        pairs, vec = gather(block_weights, vector_params)
    else:
        every = lax.all_gather(block_weights.astype(bf16), "dp", axis=1, tiled=True)[0]
        near = to_pairs(every[:total_blocks])
        far = swap(near, 2)
        pairs = jnp.where(side == 0, jnp.stack([near, far]), jnp.stack([far, near]))
        vec = lax.all_gather(vector_params, "dp", axis=1, tiled=True)
        vec = jnp.pad(vec, ((0, 16 - vec.shape[0]), (0, 0)))
    wo_other = swap(pairs[:, 6:8], 1)

    norm, q, k, v, cat = project(tokens, passes, vec, pairs)
    mine, lse = attend(lens, q, k, v)
    other = swap(mine, 1)
    out_send, out_keep, gn_send, gn_keep, second, w12_send, w12_keep = mlp(
        place, tokens, passes, vec, mine, other, cotangent, pairs, wo_other
    )
    gn_chip = (gn_keep + swap(gn_send, 1).astype(f32)).astype(bf16)
    gn_far = swap(gn_chip, 2)
    grad_second, grad_attn, sums_two = second_back(place, gn_chip, gn_far, second, cotangent, vec)
    grad_attn_other = swap(grad_attn, 1)
    dq, dk, dv, grads_o = attend_back(
        lens, place, q, k, v, mine, lse, grad_attn, grad_attn_other, pairs
    )
    g1_send, g1_keep, qkv_send, qkv_keep = project_back(place, norm, dq, dk, dv, cat)
    low_half, sums_one = first_back(
        place, tokens, passes, vec, g1_keep, swap(g1_send, 1), grad_second
    )
    out_chip = (out_keep.astype(f32) + swap(out_send, 1).astype(f32)).astype(bf16)
    out_half = (second + (out_chip.astype(f32) + swap(out_chip, 2).astype(f32))).astype(bf16)

    def join(half):
        far = swap(half, 1)
        low = jnp.where(core == 0, half, far)
        high = jnp.where(core == 0, far, half)
        return jnp.concatenate([low, high], axis=0)

    output, input_grad = join(out_half), join(low_half)
    vector_part = jnp.concatenate([sums_one[: PASSES + 2], sums_two[:2]], axis=0)
    vector_part = vector_part + swap(vector_part, 1)
    if small:
        by_z = lambda value: value.reshape(-1, 3, SIDE, PAIR)
        owned = owners_sum(by_z(w12_keep), by_z(w12_send), z, (1, 2, 3))
        late = owners_sum(by_z(qkv_keep), by_z(qkv_send), z, (0,))
        nothing = jnp.zeros_like(grads_o)
        o_keep = jnp.where(column == 0, grads_o, nothing)
        o_send = jnp.where(column == 0, nothing, grads_o)
        o_sum = owners_sum(o_keep[None], o_send[None], z, (1,))
        o_sum = jnp.concatenate([o_sum, jnp.zeros((1, SIDE, PAIR), f32)], axis=0)
        owned = jnp.where(z == 0, late, owned + jnp.where(dp == 2, o_sum, 0.0))
        owned = from_pairs(owned)[None]
        vector_part = vector_part + hop_x(vector_part)
        vector_sum = vector_part
        for turn in (1, 2, 3):
            vector_sum = vector_sum + hop_z(vector_part, turn, (0, 1, 2, 3))
        wide = vector_params.shape[1]
        vector_grad = lax.dynamic_slice_in_dim(vector_sum, dp * wide, wide, 1)
    else:
        up_down = jnp.stack([w12_keep.reshape(3, 3, SIDE, PAIR), w12_send.reshape(3, 3, SIDE, PAIR)], axis=1)
        up_down = up_down.reshape(18, SIDE, PAIR)[2:]
        grad_blocks = from_pairs(
            jnp.concatenate([qkv_keep, qkv_send, grads_o, up_down], axis=0)
        ).astype(f32)
        spare = jnp.zeros((slots - total_blocks, SIDE, SIDE), f32)
        grad_blocks = jnp.concatenate([grad_blocks, spare], axis=0)[None]
        owned = lax.psum_scatter(grad_blocks, "dp", scatter_dimension=1, tiled=True)
        vector_grad = lax.psum_scatter(vector_part, "dp", scatter_dimension=1, tiled=True)
    left_new, right_new, step, weight_new = precondition(
        owned, block_weights, block_left, block_right, block_left_root, block_right_root
    )
    moment_new = decay * vector_moment + (1.0 - decay) * vector_grad * vector_grad
    vector_new = vector_params - rate_vector * vector_grad / (jnp.sqrt(moment_new) + moment_eps)
    return (
        output,
        input_grad,
        left_new,
        right_new,
        step,
        weight_new,
        vector_grad,
        moment_new,
        vector_new,
    )


def solution(mesh):
    rows, line = P("dp", None), P(None, "dp")
    block = P("tensor", "dp", None, None)
    return jax.shard_map(
        on_device,
        mesh=mesh,
        in_specs=(rows, P("dp"), rows, rows, block, line, line, block, block, block, block),
        out_specs=(rows, rows, block, block, block, block, line, line, line),
        check_vma=False,
    )
```

```python
import functools

import jax
import jax.numpy as jnp
from jax import lax
from jax.experimental import pallas as pl
from jax.experimental.pallas import tpu as pltpu
from jax.sharding import PartitionSpec as P

D = 768
HD = 64
FF = 3072
PASSES = 5
SIDE = 192
PAIR = 2 * SIDE
ROWS = 256
DOCS = 8
NT = 4

norm_eps = 1e-05
moment_eps = 1e-08
rate_matrix = 0.03
rate_vector = 0.2
decay = 0.5
gelu_coef = 0.7978845608028654
masked_score = -1e30
f32 = jnp.float32
bf16 = jnp.bfloat16
MESH = pl.DeviceIdType.MESH
VMEM_LIMIT = 56 * 1024 * 1024


def nn(a, b):
    return lax.dot_general(a, b, (((1,), (0,)), ((), ())), preferred_element_type=f32)


def nt(a, b):
    return lax.dot_general(a, b, (((1,), (1,)), ((), ())), preferred_element_type=f32)


def tn(a, b):
    return lax.dot_general(a, b, (((0,), (0,)), ((), ())), preferred_element_type=f32)


def split_three(value):
    high = value.astype(bf16)
    rest = value - high.astype(f32)
    mid = rest.astype(bf16)
    return high, mid, (rest - mid.astype(f32)).astype(bf16)


def one_hot(pass_row):
    kinds = lax.broadcasted_iota(jnp.int32, (16, pass_row.shape[1]), 0)
    return (kinds == pass_row).astype(f32).astype(bf16)


def embedded(tokens, pass_row, vec):
    chosen = one_hot(pass_row)
    high, mid, low = split_three(vec)
    return tokens.astype(f32) + (tn(chosen, high) + tn(chosen, mid) + tn(chosen, low))


def hat_of(hidden):
    mean = jnp.mean(hidden, axis=-1, keepdims=True)
    center = hidden - mean
    spread = jnp.mean(center * center, axis=-1, keepdims=True)
    root = lax.rsqrt(spread + norm_eps)
    return center * root, root


def norm_back(hat, root, grad, gain):
    scaled = grad * gain
    first = jnp.mean(scaled, axis=-1, keepdims=True)
    second = jnp.mean(scaled * hat, axis=-1, keepdims=True)
    return root * (scaled - first - hat * second)


def params(**kw):
    return pltpu.CompilerParams(vmem_limit_bytes=VMEM_LIMIT, **kw)


def cost(micros):
    return pl.CostEstimate(flops=int(micros * 1.1e9), bytes_accessed=int(micros * 1e6), transcendentals=0)


def full(shape):
    return pl.BlockSpec(shape, lambda *_: (0,) * len(shape))


def gather_kernel(own, vec_own, all_pairs, vec_out, pack, vec_pack, vec_land, *sems):
    (s_z1, r_z1, s_x1, r_x1, s_y1, r_y1, s_d1, r_d1, s_l, r_l, s_r, r_r, s_x2, r_x2, s_y2, r_y2, s_v, r_v, loc) = sems
    dp, t = lax.axis_index("dp"), lax.axis_index("tensor")
    z, x = dp // 2, dp % 2
    y, core = t // 2, t % 2
    far_x, far_y = z * 2 + (1 - x), (1 - y) * 2 + core

    barrier = pltpu.get_barrier_semaphore()
    peers = [lax.rem(dp + k, 8) for k in range(1, 8)]
    for peer in peers:
        pl.semaphore_signal(barrier, inc=1, device_id={"dp": peer, "tensor": t}, device_id_type=MESH)
    pl.semaphore_signal(barrier, inc=1, device_id={"dp": dp, "tensor": far_y}, device_id_type=MESH)

    for m in range(3):
        pack[m] = jnp.concatenate([own[0, 2 * m], own[0, 2 * m + 1]], axis=1).astype(bf16)
    vec_pack[...] = jnp.zeros_like(vec_pack)
    vec_pack[0 : PASSES + 4, 0 : D // 8] = vec_own[...]
    pl.semaphore_wait(barrier, 8)

    started = []

    def send(src, dst, s_sem, r_sem, dp_to, t_to, cond=None):
        copy = pltpu.make_async_remote_copy(
            src_ref=src,
            dst_ref=dst,
            send_sem=s_sem,
            recv_sem=r_sem,
            device_id={"dp": dp_to, "tensor": t_to},
            device_id_type=MESH,
        )
        started.append((cond, copy))
        if cond is None:
            copy.start()
        else:
            pl.when(cond)(copy.start)

    def arrived(dst, r_sem, cond=None):
        copy = pltpu.make_async_remote_copy(
            src_ref=dst,
            dst_ref=dst,
            send_sem=loc,
            recv_sem=r_sem,
            device_id={"dp": far_x, "tensor": t},
            device_id_type=MESH,
        )
        if cond is None:
            copy.wait_recv()
        else:
            pl.when(cond)(copy.wait_recv)

    own_copy = pltpu.make_async_copy(pack, all_pairs.at[y, pl.ds(3 * dp, 3)], loc)
    own_copy.start()

    for m in range(3):
        send(pack.at[m], all_pairs.at[y, 3 * dp + m], s_l.at[0, m], r_l.at[0, m], dp - 2, t, z > 0)
    for k, peer in enumerate(peers):
        send(vec_pack, vec_land.at[dp], s_v.at[k], r_v.at[dp], peer, t)
    for m in range(3):
        send(pack.at[m], all_pairs.at[y, 3 * dp + m], s_x2.at[z, m], r_x2.at[z, m], far_x, t, z > m)
    own_copy.wait()

    half = SIDE // 2

    def piece(side, column, k):
        return all_pairs.at[side, 3 * column + k // 2, pl.ds((k % 2) * half, half)]

    def diagonal(k):
        arrived(piece(y, 1 - x, k), r_x1.at[k])
        send(piece(y, 1 - x, k), piece(y, 1 - x, k), s_d1.at[k], r_d1.at[k], dp, far_y)

    def from_right(d, m):
        arrived(all_pairs.at[y, 3 * dp + 6 * d + m], r_l.at[d - 1, m], z + d < 4)
        if d < 3:
            ref = all_pairs.at[y, 3 * dp + 6 * d + m]
            send(ref, ref, s_l.at[d, m], r_l.at[d, m], dp - 2, t, (z + d < 4) & (z > 0))

    def right_along_x(d, m):
        ref = all_pairs.at[y, 3 * dp + 6 * d + m]
        send(ref, ref, s_x2.at[z + d, m], r_x2.at[z + d, m], far_x, t, z + d < 4)

    for k in range(6):
        arrived(piece(y, x, k), r_z1.at[k], z > 0)
        send(piece(y, x, k), piece(y, x, k), s_z1.at[k], r_z1.at[k], dp + 2, t, z < 3)
        send(piece(y, x, k), piece(y, x, k), s_x1.at[k], r_x1.at[k], far_x, t)
        send(piece(y, x, k), piece(y, x, k), s_y1.at[k], r_y1.at[k], dp, far_y)
        if k >= 1:
            diagonal(k - 1)
        if k % 2 == 1:
            from_right(1, k // 2)
    diagonal(5)

    for m in range(3):
        send(pack.at[m], all_pairs.at[y, 3 * dp + m], s_x2.at[z, m], r_x2.at[z, m], far_x, t, (z > 0) & (z <= m))
    for m in range(3):
        send(pack.at[m], all_pairs.at[y, 3 * dp + m], s_r.at[0, m], r_r.at[0, m], dp + 2, t, (z > 0) & (z < 3))
    for m in range(3):
        right_along_x(1, m)
    for d in (2, 3):
        for m in range(3):
            from_right(d, m)
            right_along_x(d, m)
    for d in (1, 2):
        for m in range(3):
            ref = all_pairs.at[y, 3 * dp - 6 * d + m]
            arrived(ref, r_r.at[d - 1, m], z - d > 0)
            if d == 1:
                send(ref, ref, s_r.at[1, m], r_r.at[1, m], dp + 2, t, (z - d > 0) & (z < 3))
            send(ref, ref, s_x2.at[z - d, m], r_x2.at[z - d, m], far_x, t, z - d > 0)
    for m in range(2):
        ref = all_pairs.at[y, 6 + m]
        arrived(ref, r_x2.at[1, m], x == 1)
        send(ref, ref, s_y2.at[m], r_y2.at[m], dp, far_y)

    for k in range(6):
        arrived(piece(1 - y, x, k), r_y1.at[k])
        arrived(piece(1 - y, 1 - x, k), r_d1.at[k])
    for w in range(1, 4):
        for m in range(3):
            ref = all_pairs.at[y, 6 * w + 3 * (1 - x) + m]
            if w == 1 and m < 2:
                arrived(ref, r_x2.at[w, m], x == 0)
            else:
                arrived(ref, r_x2.at[w, m])
    for m in range(2):
        arrived(all_pairs.at[1 - y, 6 + m], r_y2.at[m])
    for peer in peers:
        arrived(vec_land.at[peer], r_v.at[peer])
    vec_land[dp] = vec_pack[...]
    vec_out[...] = jnp.concatenate([vec_land[d][:, : D // 8] for d in range(8)], axis=1)
    for cond, copy in started:
        if cond is None:
            copy.wait_send()
        else:
            pl.when(cond)(copy.wait_send)


def gather(block_weights, vector_params):
    dma = pltpu.SemaphoreType.DMA
    sizes = [(6,)] * 8 + [(3, 3)] * 2 + [(2, 3)] * 2 + [(4, 3)] * 2 + [(2,)] * 2 + [(7,), (8,)]
    return pl.pallas_call(
        gather_kernel,
        in_specs=[pl.BlockSpec(memory_space=pltpu.VMEM)] * 2,
        out_specs=[pl.BlockSpec(memory_space=pl.ANY), pl.BlockSpec(memory_space=pltpu.VMEM)],
        out_shape=[
            jax.ShapeDtypeStruct((2, 24, SIDE, PAIR), bf16),
            jax.ShapeDtypeStruct((16, D), f32),
        ],
        scratch_shapes=[
            pltpu.VMEM((3, SIDE, PAIR), bf16),
            pltpu.VMEM((16, 128), f32),
            pltpu.VMEM((8, 16, 128), f32),
        ]
        + [dma(size) for size in sizes]
        + [dma],
        compiler_params=params(collective_id=0, has_side_effects=True),
        name="gather",
    )(block_weights, vector_params)


def project_kernel(tok, pas, vec, wq, norm, q, k, v, cat):
    @pl.when(pl.program_id(0) == 0)
    def _():
        for x in range(3):
            for i in range(4):
                at = (i % 2) * SIDE
                parts = [wq[h, 2 * x + i // 2][:, at : at + SIDE] for h in range(2)]
                cat[x, i * SIDE : (i + 1) * SIDE, :] = jnp.concatenate(parts, axis=1)

    first = embedded(tok[...], pas[...], vec[...])
    hat, _ = hat_of(first)
    low = (hat * vec[PASSES : PASSES + 1] + vec[PASSES + 1 : PASSES + 2]).astype(bf16)
    norm[...] = low
    for x, out in enumerate((q, k, v)):
        out[...] = nn(low, cat[x]).astype(bf16)


def project(tokens, passes, vec, wq):
    seq = tokens.shape[0]
    row = lambda n: pl.BlockSpec((ROWS, n), lambda i: (i, 0))
    wide = jax.ShapeDtypeStruct((seq, PAIR), bf16)
    return pl.pallas_call(
        project_kernel,
        grid=(seq // ROWS,),
        in_specs=[
            row(D),
            pl.BlockSpec((1, ROWS), lambda i: (0, i)),
            full((16, D)),
            full((2, 6, SIDE, PAIR)),
        ],
        out_specs=[row(D), row(PAIR), row(PAIR), row(PAIR), full((3, D, PAIR))],
        out_shape=[
            jax.ShapeDtypeStruct((seq, D), bf16),
            wide,
            wide,
            wide,
            jax.ShapeDtypeStruct((3, D, PAIR), bf16),
        ],
        compiler_params=params(),
        cost_estimate=cost(16),
        name="project",
    )(tokens, passes, vec, wq)


def doc_state(lens, base):
    rows = base + lax.broadcasted_iota(jnp.int32, (1, ROWS), 1)
    rows = jnp.concatenate([rows, rows], axis=1)
    begin = jnp.int32(0)
    first = jnp.int32(0)
    starts = jnp.zeros((1, 2 * ROWS), jnp.int32)
    for c in range(DOCS):
        starts = jnp.where(rows >= begin, begin, starts)
        first = jnp.where(base >= begin, begin, first)
        begin = begin + lens[c]
    return rows, starts, first


def two_heads(block):
    left = lax.broadcasted_iota(jnp.int32, block.shape, 1) < HD
    none = jnp.zeros_like(block)
    return jnp.concatenate([jnp.where(left, block, none), jnp.where(left, none, block)], axis=0)


def one_above(both):
    return jnp.concatenate([both[:HD, :ROWS], both[HD:, ROWS:]], axis=0).T


def attend_kernel(lens, q, k, v, out, lse, top, total, acc):
    i = pl.program_id(0)
    base = i * ROWS
    rows, starts, first = doc_state(lens, base)
    pairs = [two_heads(q[:, p * 128 : (p + 1) * 128] * bf16(0.125)) for p in range(3)]
    for p in range(3):
        top[p] = jnp.full((1, 2 * ROWS), masked_score, f32)
        total[p] = jnp.zeros((1, 2 * ROWS), f32)
        acc[p] = jnp.zeros((128, 2 * ROWS), f32)

    def step(j, carry):
        at = pl.multiple_of(j * ROWS, ROWS)
        keys = at + lax.broadcasted_iota(jnp.int32, (ROWS, 2 * ROWS), 0)
        seen = (keys >= starts) & (keys <= rows)
        for p in range(3):
            cols = slice(p * 128, (p + 1) * 128)
            scores = jnp.where(seen, nt(k[pl.ds(at, ROWS), cols], pairs[p]), masked_score)
            before = top[p]
            now = jnp.maximum(before, jnp.max(scores, axis=0, keepdims=True))
            probs = jnp.exp(scores - now)
            fade = jnp.exp(before - now)
            top[p] = now
            total[p] = total[p] * fade + jnp.sum(probs, axis=0, keepdims=True)
            acc[p] = acc[p] * fade + tn(v[pl.ds(at, ROWS), cols], probs.astype(bf16))
        return carry

    lax.fori_loop(first // ROWS, i + 1, step, 0)
    lines = []
    for p in range(3):
        out[:, p * 128 : (p + 1) * 128] = one_above(acc[p] / total[p]).astype(bf16)
        line = top[p] + jnp.log(total[p])
        lines += [line[:, :ROWS], line[:, ROWS:]]
    lse[...] = jnp.concatenate(lines + lines[:2], axis=0)


def attend(lens, q, k, v):
    seq = q.shape[0]
    row = pl.BlockSpec((ROWS, PAIR), lambda i, s: (i, 0))
    return pl.pallas_call(
        attend_kernel,
        grid_spec=pltpu.PrefetchScalarGridSpec(
            num_scalar_prefetch=1,
            grid=(seq // ROWS,),
            in_specs=[row, full((seq, PAIR)), full((seq, PAIR))],
            out_specs=[row, pl.BlockSpec((8, ROWS), lambda i, s: (0, i))],
            scratch_shapes=[
                pltpu.VMEM((3, 1, 2 * ROWS), f32),
                pltpu.VMEM((3, 1, 2 * ROWS), f32),
                pltpu.VMEM((3, 128, 2 * ROWS), f32),
            ],
        ),
        out_shape=[
            jax.ShapeDtypeStruct((seq, PAIR), bf16),
            jax.ShapeDtypeStruct((8, seq), f32),
        ],
        compiler_params=params(),
        cost_estimate=cost(30),
        name="attend",
    )(lens, q, k, v)


def attend_back_kernel(
    lens, q, k, v, mixed, lse, grad_mixed, dq, dk, dv, dk_acc, dv_acc, dq_acc
):
    i = pl.program_id(0)
    count = pl.num_programs(0)
    base = i * ROWS

    @pl.when(i == 0)
    def _():
        dk_acc[...] = jnp.zeros_like(dk_acc)
        dv_acc[...] = jnp.zeros_like(dv_acc)

    rows, starts, first = doc_state(lens, base)
    heads = lax.broadcasted_iota(jnp.int32, (8, 128), 0)
    lanes = lax.broadcasted_iota(jnp.int32, (8, 128), 1)
    pick = (lanes // HD == heads).astype(f32)
    queries, grads, inner, lines = [], [], [], []
    for p in range(3):
        cols = slice(p * 128, (p + 1) * 128)
        queries.append(two_heads(q[:, cols] * bf16(0.125)))
        grads.append(two_heads(grad_mixed[:, cols]))
        product = grad_mixed[:, cols].astype(f32) * mixed[:, cols].astype(f32)
        sums = lax.dot_general(
            pick,
            product,
            (((1,), (1,)), ((), ())),
            precision=lax.Precision.HIGHEST,
            preferred_element_type=f32,
        )
        inner.append(jnp.concatenate([sums[0:1], sums[1:2]], axis=1))
        lines.append(jnp.concatenate([lse[2 * p : 2 * p + 1], lse[2 * p + 1 : 2 * p + 2]], axis=1))
        dq_acc[p] = jnp.zeros((128, 2 * ROWS), f32)

    def step(j, carry):
        at = pl.multiple_of(j * ROWS, ROWS)
        keys = at + lax.broadcasted_iota(jnp.int32, (ROWS, 2 * ROWS), 0)
        seen = (keys >= starts) & (keys <= rows)
        here = pl.ds(at, ROWS)
        for p in range(3):
            cols = slice(p * 128, (p + 1) * 128)
            kb = k[here, cols]
            scores = jnp.where(seen, nt(kb, queries[p]) - lines[p], masked_score)
            probs = jnp.exp(scores)
            grad_probs = nt(v[here, cols], grads[p])
            grad_scores = (probs * (grad_probs - inner[p])).astype(bf16)
            dv_acc[here, cols] += nn(probs.astype(bf16), grads[p])
            dk_acc[here, cols] += nn(grad_scores, queries[p])
            dq_acc[p] += tn(kb, grad_scores)
        return carry

    lax.fori_loop(first // ROWS, i + 1, step, 0)
    for p in range(3):
        dq[:, p * 128 : (p + 1) * 128] = (one_above(dq_acc[p]) * 0.125).astype(bf16)

    @pl.when(i == count - 1)
    def _():
        dk[...] = dk_acc[...].astype(bf16)
        dv[...] = dv_acc[...].astype(bf16)


def attend_back(lens, q, k, v, mixed, lse, grad_mixed):
    seq = q.shape[0]
    count = seq // ROWS
    row = pl.BlockSpec((ROWS, PAIR), lambda i, s: (i, 0))
    wide = jax.ShapeDtypeStruct((seq, PAIR), bf16)
    return pl.pallas_call(
        attend_back_kernel,
        grid_spec=pltpu.PrefetchScalarGridSpec(
            num_scalar_prefetch=1,
            grid=(count,),
            in_specs=[
                row,
                full((seq, PAIR)),
                full((seq, PAIR)),
                row,
                pl.BlockSpec((8, ROWS), lambda i, s: (0, i)),
                row,
            ],
            out_specs=[row, full((seq, PAIR)), full((seq, PAIR))],
            scratch_shapes=[
                pltpu.VMEM((seq, PAIR), f32),
                pltpu.VMEM((seq, PAIR), f32),
                pltpu.VMEM((3, 128, 2 * ROWS), f32),
            ],
        ),
        out_shape=[wide, wide, wide],
        compiler_params=params(),
        cost_estimate=cost(40),
        name="attend_back",
    )(lens, q, k, v, mixed, lse, grad_mixed)


def feed_kernel(
    small, tok, pas, vec, mine, other, cot, wo_mine, wo_other, w1, w2,
    out_send, out_keep, second_keep, grad_second, grad_mixed, sums, g_send, g_keep, o_send, o_keep,
    wom, woo, up, down, gup, gdown, go, core_out, core_in, far_out, far_in, ga_out, ga_in, seconds,
    s_core, r_core, s_far, r_far, s_ga, r_ga,
):
    step = pl.program_id(0)
    half = core_out.shape[0]
    t = lax.axis_index("tensor")
    core, side = t % 2, t // 2
    near, far = side * 2 + (1 - core), (1 - side) * 2 + core
    column = lax.axis_index("dp") % 2 if small else 0

    def copy(src, dst, s_sem, r_sem, j, to):
        return pltpu.make_async_remote_copy(
            src_ref=src.at[j],
            dst_ref=dst.at[j],
            send_sem=s_sem.at[j],
            recv_sem=r_sem.at[j],
            device_id={"tensor": to},
            device_id_type=MESH,
        )

    core_copy = lambda j: copy(core_out, core_in, s_core, r_core, j, near)
    far_copy = lambda j: copy(far_out, far_in, s_far, r_far, j, far)
    ga_copy = lambda j: copy(ga_out, ga_in, s_ga, r_ga, j, near)
    barrier = pltpu.get_barrier_semaphore()

    @pl.when(step == 0)
    def _():
        for to in (near, far):
            pl.semaphore_signal(barrier, inc=1, device_id={"tensor": to}, device_id_type=MESH)
        for h in range(2):
            for m in range(2):
                rows, cols = slice(h * SIDE, (h + 1) * SIDE), slice(m * PAIR, (m + 1) * PAIR)
                wom[rows, cols] = wo_mine[h, m]
                woo[rows, cols] = wo_other[h, m]
        for r in range(4):
            for m in range(2):
                rows, cols = slice(r * SIDE, (r + 1) * SIDE), slice(m * PAIR, (m + 1) * PAIR)
                up[rows, cols] = w1[0, 2 * r + m]
                down[rows, cols] = w2[0, 2 * r + m]
        gup[...] = jnp.zeros_like(gup)
        gdown[...] = jnp.zeros_like(gdown)
        go[...] = jnp.zeros_like(go)
        sums[...] = jnp.zeros_like(sums)
        pl.semaphore_wait(barrier, 2)

    @pl.when(step < 2 * half)
    def _():
        j = step // 2
        owner = jnp.where(step % 2 == 0, 1 - core, core)
        here = pl.ds(pl.multiple_of((owner * half + j) * ROWS, ROWS), ROWS)
        first = embedded(tok[...], pas[...], vec[...])
        second = first + (nn(mine[here, :], wom[...]) + nn(other[...], woo[...]))
        hat, _ = hat_of(second)
        low = (hat * vec[PASSES + 2 : PASSES + 3] + vec[PASSES + 3 : PASSES + 4]).astype(bf16)
        upper = nn(low, up[...])
        square = upper * upper
        bent = jnp.tanh(gelu_coef * upper * (1.0 + 0.044715 * square))
        act = (0.5 * upper * (1.0 + bent)).astype(bf16)
        slope = 0.5 * (1.0 + bent) + (0.5 * gelu_coef) * upper * (1.0 - bent * bent) * (
            1.0 + (3 * 0.044715) * square
        )
        grad_act = nt(cot[...], down[...])
        grad_upper = (grad_act * slope).astype(bf16)
        part = nt(grad_upper, up[...])

        @pl.when(step % 2 == 0)
        def _():
            core_out[j] = part.astype(bf16)
            core_copy(j).start()

        @pl.when(step % 2 == 1)
        def _():
            core_copy(j).wait_recv()
            far_out[j] = (part + core_in[j].astype(f32)).astype(bf16)
            far_copy(j).start()
            second_keep[...] = second
            seconds[j] = second

        gup[...] += tn(low, grad_upper)
        gdown[...] += tn(act, cot[...])
        out_part = nn(act, down[...]).astype(bf16)

        @pl.when(step % 2 == 0)
        def _():
            out_send[...] = out_part

        @pl.when(step % 2 == 1)
        def _():
            out_keep[...] = out_part

    @pl.when(step == 2 * half - 1)
    def _():
        for r in range(4):
            for m in range(2):
                rows, cols = slice(r * SIDE, (r + 1) * SIDE), slice(m * PAIR, (m + 1) * PAIR)
                for at, total in ((8, gup), (16, gdown)):
                    pair = at + 2 * r + m
                    slot, place = (pair // 6 - 1) * 3 + pair % 3, pair // 3 % 2
                    value = total[rows, cols].astype(bf16)

                    @pl.when(column == place)
                    def _():
                        g_keep[slot] = value

                    @pl.when(column != place)
                    def _():
                        g_send[slot] = value
        for slot in range(2):

            @pl.when(column == 0)
            def _():
                g_keep[slot] = jnp.zeros((SIDE, PAIR), bf16)

            @pl.when(column != 0)
            def _():
                g_send[slot] = jnp.zeros((SIDE, PAIR), bf16)

    def through_out(grad, block):
        here = pl.ds(pl.multiple_of(block * ROWS, ROWS), ROWS)
        grad_mixed[here, :] = nt(grad, wom[...]).astype(bf16)
        go[...] += tn(mine[here, :], grad)

    @pl.when((step >= 2 * half) & (step < 3 * half))
    def _():
        j = step - 2 * half
        hat, root = hat_of(seconds[j])
        far_copy(j).wait_recv()
        grad = far_out[j].astype(f32) + far_in[j].astype(f32)
        result = cot[...].astype(f32) + norm_back(hat, root, grad, vec[PASSES + 2 : PASSES + 3])
        low = result.astype(bf16)
        ga_out[j] = low
        ga_copy(j).start()
        grad_second[...] = result
        sums[0:1] += jnp.sum(grad * hat, axis=0, keepdims=True)
        sums[1:2] += jnp.sum(grad, axis=0, keepdims=True)
        through_out(low, core * half + j)

    @pl.when(step > 2 * half)
    def _():
        j = step - 2 * half - 1
        ga_copy(j).wait_recv()
        through_out(ga_in[j], (1 - core) * half + j)

    @pl.when(step == 3 * half)
    def _():
        at = pl.multiple_of(side * SIDE, SIDE)
        for m in range(2):
            value = go[pl.ds(at, SIDE), m * PAIR : (m + 1) * PAIR].astype(bf16)
            none = jnp.zeros_like(value)
            o_keep[m] = jnp.where(column == 0, value, none)
            o_send[m] = jnp.where(column == 0, none, value)
        for j in range(half):
            core_copy(j).wait_send()
            far_copy(j).wait_send()
            ga_copy(j).wait_send()


def feed(small, tokens, passes, vec, mine, other, cotangent, pairs, wo_other):
    seq = tokens.shape[0]
    half = seq // ROWS // 2

    def block(i):
        core = lax.axis_index("tensor") % 2
        work = jnp.minimum(i, 2 * half - 1)
        owner = jnp.where(work % 2 == 0, 1 - core, core)
        return owner * half + work // 2

    def cot_block(i):
        core = lax.axis_index("tensor") % 2
        return jnp.where(i < 2 * half, block(i), core * half + jnp.minimum(i - 2 * half, half - 1))

    side = lambda: lax.axis_index("tensor") // 2
    row = lambda n: pl.BlockSpec((ROWS, n), lambda i: (block(i), 0))
    keep = pl.BlockSpec((ROWS, D), lambda i: (jnp.minimum(i // 2, half - 1), 0))
    last = pl.BlockSpec((ROWS, D), lambda i: (jnp.clip(i - 2 * half, 0, half - 1), 0))
    rows = lambda kind: jax.ShapeDtypeStruct((seq // 2, D), kind)
    gr = lambda n: jax.ShapeDtypeStruct((n, SIDE, PAIR), bf16)
    buffer = pltpu.VMEM((half, ROWS, D), bf16)
    dma = pltpu.SemaphoreType.DMA((half,))
    return pl.pallas_call(
        functools.partial(feed_kernel, small),
        grid=(3 * half + 1,),
        in_specs=[
            row(D),
            pl.BlockSpec((1, ROWS), lambda i: (0, block(i))),
            full((16, D)),
            full((seq, PAIR)),
            row(PAIR),
            pl.BlockSpec((ROWS, D), lambda i: (cot_block(i), 0)),
            pl.BlockSpec((2, 2, SIDE, PAIR), lambda i: (0, 3, 0, 0)),
            full(wo_other.shape),
            pl.BlockSpec((1, 8, SIDE, PAIR), lambda i: (side(), 1, 0, 0)),
            pl.BlockSpec((1, 8, SIDE, PAIR), lambda i: (side(), 2, 0, 0)),
        ],
        out_specs=[
            keep,
            keep,
            keep,
            last,
            full((seq, PAIR)),
            full((8, D)),
            full((9, SIDE, PAIR)),
            full((9, SIDE, PAIR)),
            full((2, SIDE, PAIR)),
            full((2, SIDE, PAIR)),
        ],
        scratch_shapes=[
            pltpu.VMEM((PAIR, D), bf16),
            pltpu.VMEM((PAIR, D), bf16),
            pltpu.VMEM((D, D), bf16),
            pltpu.VMEM((D, D), bf16),
            pltpu.VMEM((D, D), f32),
            pltpu.VMEM((D, D), f32),
            pltpu.VMEM((PAIR, D), f32),
            buffer,
            buffer,
            buffer,
            buffer,
            buffer,
            buffer,
            pltpu.VMEM((half, ROWS, D), f32),
            dma,
            dma,
            dma,
            dma,
            dma,
            dma,
        ],
        out_shape=[
            rows(bf16),
            rows(bf16),
            rows(f32),
            rows(f32),
            jax.ShapeDtypeStruct((seq, PAIR), bf16),
            jax.ShapeDtypeStruct((8, D), f32),
            gr(9),
            gr(9),
            gr(2),
            gr(2),
        ],
        compiler_params=params(collective_id=1, has_side_effects=True),
        cost_estimate=cost(50),
        name="feed_forward",
    )(tokens, passes, vec, mine, other, cotangent, pairs, wo_other, pairs, pairs)


def qkv_grads_kernel(place, norm, dq, dk, dv, g_send, g_keep, acc):
    i = pl.program_id(0)

    @pl.when(i == 0)
    def _():
        acc[...] = jnp.zeros_like(acc)

    for x, grad in enumerate((dq, dk, dv)):
        mine = jnp.where(place[1] == 0, grad[:, :SIDE].astype(f32), grad[:, SIDE:].astype(f32))
        acc[x] += tn(norm[...], mine.astype(bf16))

    @pl.when(i == pl.num_programs(0) - 1)
    def _():
        for x in range(3):
            for m in range(2):
                at = 2 * m * SIDE
                value = jnp.concatenate(
                    [acc[x, at : at + SIDE], acc[x, at + SIDE : at + 2 * SIDE]], axis=1
                ).astype(bf16)
                slot, column = (2 * x + m) % 3, (2 * x + m) // 3

                @pl.when(place[2] == column)
                def _():
                    g_keep[slot] = value

                @pl.when(place[2] != column)
                def _():
                    g_send[slot] = value


def qkv_grads(place, norm, dq, dk, dv):
    seq = norm.shape[0]
    row = lambda n: pl.BlockSpec((ROWS, n), lambda i, s: (i, 0))
    return pl.pallas_call(
        qkv_grads_kernel,
        grid_spec=pltpu.PrefetchScalarGridSpec(
            num_scalar_prefetch=1,
            grid=(seq // ROWS,),
            in_specs=[row(D), row(PAIR), row(PAIR), row(PAIR)],
            out_specs=[full((3, SIDE, PAIR)), full((3, SIDE, PAIR))],
            scratch_shapes=[pltpu.VMEM((3, D, SIDE), f32)],
        ),
        out_shape=[jax.ShapeDtypeStruct((3, SIDE, PAIR), bf16)] * 2,
        compiler_params=params(),
        cost_estimate=cost(8),
        name="qkv_grads",
    )(place, norm, dq, dk, dv)


def project_back_kernel(place, dq, dk, dv, cat, send, keep):
    i = pl.program_id(0)
    count = pl.num_programs(0)
    total = (nt(dq[...], cat[0]) + nt(dk[...], cat[1]) + nt(dv[...], cat[2])).astype(bf16)

    @pl.when(i < count // 2)
    def _():
        send[...] = total

    @pl.when(i >= count // 2)
    def _():
        keep[...] = total


def project_back(place, dq, dk, dv, cat):
    seq = dq.shape[0]
    count = seq // ROWS
    where = lambda i, s: lax.rem(i + (1 - s[0]) * (count // 2), count)
    row = lambda n: pl.BlockSpec((ROWS, n), lambda i, s: (where(i, s), 0))
    send = pl.BlockSpec((ROWS, D), lambda i, s: (jnp.minimum(i, count // 2 - 1), 0))
    keep = pl.BlockSpec((ROWS, D), lambda i, s: (jnp.maximum(i - count // 2, 0), 0))
    half = jax.ShapeDtypeStruct((seq // 2, D), bf16)
    return pl.pallas_call(
        project_back_kernel,
        grid_spec=pltpu.PrefetchScalarGridSpec(
            num_scalar_prefetch=1,
            grid=(count,),
            in_specs=[row(PAIR), row(PAIR), row(PAIR), full(cat.shape)],
            out_specs=[send, keep],
        ),
        out_shape=[half, half],
        compiler_params=params(),
        cost_estimate=cost(8),
        name="project_back",
    )(place, dq, dk, dv, cat)


def first_back_kernel(place, tok, pas, vec, one, two, grad_second, low, sums):
    @pl.when(pl.program_id(0) == 0)
    def _():
        sums[...] = jnp.zeros_like(sums)

    grad = one[...].astype(f32) + two[...].astype(f32)
    hat, root = hat_of(embedded(tok[...], pas[...], vec[...]))
    result = grad_second[...] + norm_back(hat, root, grad, vec[PASSES : PASSES + 1])
    low[...] = result.astype(bf16)
    chosen = one_hot(pas[...])
    high, mid, rest = split_three(result)
    sums[...] += nn(chosen, high) + nn(chosen, mid) + nn(chosen, rest)
    sums[PASSES : PASSES + 1] += jnp.sum(grad * hat, axis=0, keepdims=True)
    sums[PASSES + 1 : PASSES + 2] += jnp.sum(grad, axis=0, keepdims=True)


def first_back(place, tokens, passes, vec, one, two, grad_second):
    rows = one.shape[0]
    count = rows // ROWS
    row = pl.BlockSpec((ROWS, D), lambda i, s: (i, 0))
    mine = pl.BlockSpec((ROWS, D), lambda i, s: (i + s[0] * count, 0))
    return pl.pallas_call(
        first_back_kernel,
        grid_spec=pltpu.PrefetchScalarGridSpec(
            num_scalar_prefetch=1,
            grid=(count,),
            in_specs=[
                mine,
                pl.BlockSpec((1, ROWS), lambda i, s: (0, i + s[0] * count)),
                full((16, D)),
                row,
                row,
                row,
            ],
            out_specs=[row, full((16, D))],
        ),
        out_shape=[
            jax.ShapeDtypeStruct((rows, D), bf16),
            jax.ShapeDtypeStruct((16, D), f32),
        ],
        compiler_params=params(),
        cost_estimate=cost(9),
        name="first_back",
    )(place, tokens, passes, vec, one, two, grad_second)


def precondition(grad, weight, left, right, left_root, right_root):
    high = lax.Precision.HIGHEST
    left_new = decay * left + (1.0 - decay) * jnp.einsum(
        "...ij,...kj->...ik", grad, grad, precision=high
    )
    right_new = decay * right + (1.0 - decay) * jnp.einsum(
        "...ji,...jk->...ik", grad, grad, precision=high
    )
    half = jnp.einsum("...ij,...jk->...ik", left_root, grad, precision=high)
    step = jnp.einsum("...ij,...jk->...ik", half, right_root, precision=high)
    return (left_new, right_new, step, weight - rate_matrix * step)


def to_pairs(blocks):
    n = blocks.shape[0] // 2
    return blocks.reshape(n, 2, SIDE, SIDE).transpose(0, 2, 1, 3).reshape(n, SIDE, PAIR)


def from_pairs(pairs):
    n = pairs.shape[0]
    return pairs.reshape(n, SIDE, 2, SIDE).transpose(0, 2, 1, 3).reshape(2 * n, SIDE, SIDE)


def swap(value, bit):
    return lax.ppermute(value, "tensor", [(t, t ^ bit) for t in range(NT)])


def hop_x(value):
    return lax.ppermute(value, "dp", [(d, d ^ 1) for d in range(8)])


def hop_z(value, turn, ends):
    pairs = [(d, (d + 2 * turn) % 8) for d in range(8) if (d // 2 + turn) % 4 in ends]
    return lax.ppermute(value, "dp", pairs)


def terms_by_turn(keep, near, z, ends):
    both = (keep.astype(f32) + near.astype(f32)).astype(bf16)
    terms = []
    for turn in range(4):
        at = jnp.clip((z + turn) % 4 - ends[0], 0, len(ends) - 1)
        terms.append(lax.dynamic_index_in_dim(both, at, 0, keepdims=False))
    return terms


def hops_z(terms, ends):
    return [hop_z(terms[turn], turn, ends) for turn in (1, 2, 3)]


def total_of(terms, far):
    total = terms[0].astype(f32)
    for value in far:
        total = total + value.astype(f32)
    return total


def tie(*values):
    return lax.optimization_barrier(values)


def on_device(
    tokens,
    pass_ids,
    doc_lengths,
    cotangent,
    block_weights,
    vector_params,
    vector_moment,
    block_left,
    block_right,
    block_left_root,
    block_right_root,
):
    t, dp = lax.axis_index("tensor"), lax.axis_index("dp")
    core, side = t % 2, t // 2
    n_dp = lax.axis_size("dp")
    small = n_dp == 8
    z, column = (dp // 2, dp % 2) if small else (0, 0)
    place = jnp.stack([core, side, jnp.asarray(column, jnp.int32)]).astype(jnp.int32)
    lens = doc_lengths[0]
    seq = tokens.shape[0]
    passes = pass_ids.reshape(1, seq)
    total_blocks = (D // SIDE) * (4 + 2 * (FF // D))
    slots = block_weights.shape[1] * n_dp

    if small:
        pairs, vec = gather(block_weights, vector_params)
    else:
        every = lax.all_gather(block_weights.astype(bf16), "dp", axis=1, tiled=True)[0]
        near = to_pairs(every[:total_blocks])
        far = swap(near, 2)
        pairs = jnp.where(side == 0, jnp.stack([near, far]), jnp.stack([far, near]))
        vec = lax.all_gather(vector_params, "dp", axis=1, tiled=True)
        vec = jnp.pad(vec, ((0, 16 - vec.shape[0]), (0, 0)))
    wo_other = swap(pairs[:, 6:8], 1)

    norm, q, k, v, cat = project(tokens, passes, vec, pairs)
    mine, lse = attend(lens, q, k, v)
    other = swap(mine, 1)
    (
        out_send,
        out_keep,
        second,
        grad_second,
        grad_mixed,
        sums_two,
        w12_send,
        w12_keep,
        o_send,
        o_keep,
    ) = feed(small, tokens, passes, vec, mine, other, cotangent, pairs, wo_other)
    out_chip = (out_keep.astype(f32) + swap(out_send, 1).astype(f32)).astype(bf16)
    out_far = swap(out_chip, 2)
    if small:
        by_z = lambda value: value.reshape(-1, 3, SIDE, PAIR)
        w12_near = hop_x(by_z(w12_send))
        o_near = hop_x(o_send)
    out_chip, grad_mixed = tie(out_chip, grad_mixed)
    dq, dk, dv = attend_back(lens, q, k, v, mine, lse, grad_mixed)
    out_far, dq = tie(out_far, dq)
    if small:
        w12_near, o_near, dq = tie(w12_near, o_near, dq)
        w12_terms = terms_by_turn(by_z(w12_keep), w12_near, z, (1, 2, 3))
        o_terms = terms_by_turn(o_keep[None], o_near[None], z, (1,))
        w12_terms, o_terms, dq = tie(w12_terms, o_terms, dq)
        w12_far = hops_z(w12_terms, (1, 2, 3))
        o_far = hops_z(o_terms, (1,))
    qkv_send, qkv_keep = qkv_grads(place, norm, dq, dk, dv)
    if small:
        qkv_near = hop_x(by_z(qkv_send))
        qkv_keep, dq = tie(qkv_keep, dq)
    g1_send, g1_keep = project_back(place, dq, dk, dv, cat)
    g1_near = swap(g1_send, 1)
    if small:
        qkv_near, g1_keep = tie(qkv_near, g1_keep)
        qkv_terms = terms_by_turn(by_z(qkv_keep), qkv_near, z, (0,))
        qkv_terms, g1_keep = tie(qkv_terms, g1_keep)
        qkv_far = hops_z(qkv_terms, (0,))
    low_half, sums_one = first_back(place, tokens, passes, vec, g1_keep, g1_near, grad_second)
    out_half = (second + (out_chip.astype(f32) + out_far.astype(f32))).astype(bf16)

    def join(half):
        far = swap(half, 1)
        low = jnp.where(core == 0, half, far)
        high = jnp.where(core == 0, far, half)
        return jnp.concatenate([low, high], axis=0)

    output, input_grad = join(out_half), join(low_half)
    vector_part = jnp.concatenate([sums_one[: PASSES + 2], sums_two[:2]], axis=0)
    vector_part = vector_part + swap(vector_part, 1)
    if small:
        o_far, w12_far, qkv_far, low_half = tie(o_far, w12_far, qkv_far, low_half)
        owned = total_of(w12_terms, w12_far)
        late = total_of(qkv_terms, qkv_far)
        o_sum = total_of(o_terms, o_far)
        o_sum = jnp.concatenate([o_sum, jnp.zeros((1, SIDE, PAIR), f32)], axis=0)
        owned = jnp.where(z == 0, late, owned + jnp.where(dp == 2, o_sum, 0.0))
        owned = from_pairs(owned)[None]
        vector_part = vector_part + hop_x(vector_part)
        vector_sum = vector_part
        for turn in (1, 2, 3):
            vector_sum = vector_sum + hop_z(vector_part, turn, (0, 1, 2, 3))
        wide = vector_params.shape[1]
        vector_grad = lax.dynamic_slice_in_dim(vector_sum, dp * wide, wide, 1)
    else:
        up_down = jnp.stack(
            [w12_keep.reshape(3, 3, SIDE, PAIR), w12_send.reshape(3, 3, SIDE, PAIR)], axis=1
        )
        up_down = up_down.reshape(18, SIDE, PAIR)[2:]
        grad_blocks = from_pairs(
            jnp.concatenate([qkv_keep, qkv_send, o_keep, up_down], axis=0)
        ).astype(f32)
        spare = jnp.zeros((slots - total_blocks, SIDE, SIDE), f32)
        grad_blocks = jnp.concatenate([grad_blocks, spare], axis=0)[None]
        owned = lax.psum_scatter(grad_blocks, "dp", scatter_dimension=1, tiled=True)
        vector_grad = lax.psum_scatter(vector_part, "dp", scatter_dimension=1, tiled=True)
    left_new, right_new, step, weight_new = precondition(
        owned, block_weights, block_left, block_right, block_left_root, block_right_root
    )
    moment_new = decay * vector_moment + (1.0 - decay) * vector_grad * vector_grad
    vector_new = vector_params - rate_vector * vector_grad / (jnp.sqrt(moment_new) + moment_eps)
    return (
        output,
        input_grad,
        left_new,
        right_new,
        step,
        weight_new,
        vector_grad,
        moment_new,
        vector_new,
    )


def solution(mesh):
    rows, line = P("dp", None), P(None, "dp")
    block = P("tensor", "dp", None, None)
    return jax.shard_map(
        on_device,
        mesh=mesh,
        in_specs=(rows, P("dp"), rows, rows, block, line, line, block, block, block, block),
        out_specs=(rows, rows, block, block, block, block, line, line, line),
        check_vma=False,
    )
```

```python
import functools

import jax
import jax.numpy as jnp
from jax import lax
from jax.experimental import pallas as pl
from jax.experimental.pallas import tpu as pltpu
from jax.sharding import PartitionSpec as P

D = 768
HD = 64
FF = 3072
PASSES = 5
SIDE = 192
PAIR = 2 * SIDE
ROWS = 256
DOCS = 8
NT = 4

norm_eps = 1e-05
moment_eps = 1e-08
rate_matrix = 0.03
rate_vector = 0.2
decay = 0.5
gelu_coef = 0.7978845608028654
masked_score = -1e30
f32 = jnp.float32
bf16 = jnp.bfloat16
MESH = pl.DeviceIdType.MESH
VMEM_LIMIT = 56 * 1024 * 1024


def nn(a, b):
    return lax.dot_general(a, b, (((1,), (0,)), ((), ())), preferred_element_type=f32)


def nt(a, b):
    return lax.dot_general(a, b, (((1,), (1,)), ((), ())), preferred_element_type=f32)


def tn(a, b):
    return lax.dot_general(a, b, (((0,), (0,)), ((), ())), preferred_element_type=f32)


def split_three(value):
    high = value.astype(bf16)
    rest = value - high.astype(f32)
    mid = rest.astype(bf16)
    return high, mid, (rest - mid.astype(f32)).astype(bf16)


def one_hot(pass_row):
    kinds = lax.broadcasted_iota(jnp.int32, (16, pass_row.shape[1]), 0)
    return (kinds == pass_row).astype(f32).astype(bf16)


def embedded(tokens, pass_row, vec):
    chosen = one_hot(pass_row)
    high, mid, low = split_three(vec)
    return tokens.astype(f32) + (tn(chosen, high) + tn(chosen, mid) + tn(chosen, low))


def hat_of(hidden):
    mean = jnp.mean(hidden, axis=-1, keepdims=True)
    center = hidden - mean
    spread = jnp.mean(center * center, axis=-1, keepdims=True)
    root = lax.rsqrt(spread + norm_eps)
    return center * root, root


def norm_back(hat, root, grad, gain):
    scaled = grad * gain
    first = jnp.mean(scaled, axis=-1, keepdims=True)
    second = jnp.mean(scaled * hat, axis=-1, keepdims=True)
    return root * (scaled - first - hat * second)


def params(**kw):
    return pltpu.CompilerParams(vmem_limit_bytes=VMEM_LIMIT, **kw)


def cost(micros):
    return pl.CostEstimate(flops=int(micros * 1.1e9), bytes_accessed=int(micros * 1e6), transcendentals=0)


def full(shape):
    return pl.BlockSpec(shape, lambda *_: (0,) * len(shape))


def gather_kernel(own, vec_own, all_pairs, vec_out, pack, vec_pack, vec_land, *sems):
    (s_z1, r_z1, s_x1, r_x1, s_y1, r_y1, s_d1, r_d1, s_l, r_l, s_r, r_r, s_x2, r_x2, s_y2, r_y2, s_v, r_v, loc) = sems
    dp, t = lax.axis_index("dp"), lax.axis_index("tensor")
    z, x = dp // 2, dp % 2
    y, core = t // 2, t % 2
    far_x, far_y = z * 2 + (1 - x), (1 - y) * 2 + core

    barrier = pltpu.get_barrier_semaphore()
    peers = [lax.rem(dp + k, 8) for k in range(1, 8)]
    for peer in peers:
        pl.semaphore_signal(barrier, inc=1, device_id={"dp": peer, "tensor": t}, device_id_type=MESH)
    pl.semaphore_signal(barrier, inc=1, device_id={"dp": dp, "tensor": far_y}, device_id_type=MESH)

    for m in range(3):
        pack[m] = jnp.concatenate([own[0, 2 * m], own[0, 2 * m + 1]], axis=1).astype(bf16)
    vec_pack[...] = jnp.zeros_like(vec_pack)
    vec_pack[0 : PASSES + 4, 0 : D // 8] = vec_own[...]
    pl.semaphore_wait(barrier, 8)

    started = []

    def send(src, dst, s_sem, r_sem, dp_to, t_to, cond=None):
        copy = pltpu.make_async_remote_copy(
            src_ref=src,
            dst_ref=dst,
            send_sem=s_sem,
            recv_sem=r_sem,
            device_id={"dp": dp_to, "tensor": t_to},
            device_id_type=MESH,
        )
        started.append((cond, copy))
        if cond is None:
            copy.start()
        else:
            pl.when(cond)(copy.start)

    def arrived(dst, r_sem, cond=None):
        copy = pltpu.make_async_remote_copy(
            src_ref=dst,
            dst_ref=dst,
            send_sem=loc,
            recv_sem=r_sem,
            device_id={"dp": far_x, "tensor": t},
            device_id_type=MESH,
        )
        if cond is None:
            copy.wait_recv()
        else:
            pl.when(cond)(copy.wait_recv)

    own_copy = pltpu.make_async_copy(pack, all_pairs.at[y, pl.ds(3 * dp, 3)], loc)
    own_copy.start()

    for m in range(3):
        send(pack.at[m], all_pairs.at[y, 3 * dp + m], s_l.at[0, m], r_l.at[0, m], dp - 2, t, z > 0)
    for k, peer in enumerate(peers):
        send(vec_pack, vec_land.at[dp], s_v.at[k], r_v.at[dp], peer, t)
    for m in range(3):
        send(pack.at[m], all_pairs.at[y, 3 * dp + m], s_x2.at[z, m], r_x2.at[z, m], far_x, t, z > m)
    own_copy.wait()

    half = SIDE // 2

    def piece(side, column, k):
        return all_pairs.at[side, 3 * column + k // 2, pl.ds((k % 2) * half, half)]

    def diagonal(k):
        arrived(piece(y, 1 - x, k), r_x1.at[k])
        send(piece(y, 1 - x, k), piece(y, 1 - x, k), s_d1.at[k], r_d1.at[k], dp, far_y)

    def from_right(d, m):
        arrived(all_pairs.at[y, 3 * dp + 6 * d + m], r_l.at[d - 1, m], z + d < 4)
        if d < 3:
            ref = all_pairs.at[y, 3 * dp + 6 * d + m]
            send(ref, ref, s_l.at[d, m], r_l.at[d, m], dp - 2, t, (z + d < 4) & (z > 0))

    def right_along_x(d, m):
        ref = all_pairs.at[y, 3 * dp + 6 * d + m]
        send(ref, ref, s_x2.at[z + d, m], r_x2.at[z + d, m], far_x, t, z + d < 4)

    for k in range(6):
        arrived(piece(y, x, k), r_z1.at[k], z > 0)
        send(piece(y, x, k), piece(y, x, k), s_z1.at[k], r_z1.at[k], dp + 2, t, z < 3)
        send(piece(y, x, k), piece(y, x, k), s_x1.at[k], r_x1.at[k], far_x, t)
        send(piece(y, x, k), piece(y, x, k), s_y1.at[k], r_y1.at[k], dp, far_y)
        if k >= 1:
            diagonal(k - 1)
        if k % 2 == 1:
            from_right(1, k // 2)
    diagonal(5)

    for m in range(3):
        send(pack.at[m], all_pairs.at[y, 3 * dp + m], s_x2.at[z, m], r_x2.at[z, m], far_x, t, (z > 0) & (z <= m))
    for m in range(3):
        send(pack.at[m], all_pairs.at[y, 3 * dp + m], s_r.at[0, m], r_r.at[0, m], dp + 2, t, (z > 0) & (z < 3))
    for m in range(3):
        right_along_x(1, m)
    for d in (2, 3):
        for m in range(3):
            from_right(d, m)
            right_along_x(d, m)
    for d in (1, 2):
        for m in range(3):
            ref = all_pairs.at[y, 3 * dp - 6 * d + m]
            arrived(ref, r_r.at[d - 1, m], z - d > 0)
            if d == 1:
                send(ref, ref, s_r.at[1, m], r_r.at[1, m], dp + 2, t, (z - d > 0) & (z < 3))
            send(ref, ref, s_x2.at[z - d, m], r_x2.at[z - d, m], far_x, t, z - d > 0)
    for m in range(2):
        ref = all_pairs.at[y, 6 + m]
        arrived(ref, r_x2.at[1, m], x == 1)
        send(ref, ref, s_y2.at[m], r_y2.at[m], dp, far_y)

    for k in range(6):
        arrived(piece(1 - y, x, k), r_y1.at[k])
        arrived(piece(1 - y, 1 - x, k), r_d1.at[k])
    for w in range(1, 4):
        for m in range(3):
            ref = all_pairs.at[y, 6 * w + 3 * (1 - x) + m]
            if w == 1 and m < 2:
                arrived(ref, r_x2.at[w, m], x == 0)
            else:
                arrived(ref, r_x2.at[w, m])
    for m in range(2):
        arrived(all_pairs.at[1 - y, 6 + m], r_y2.at[m])
    for peer in peers:
        arrived(vec_land.at[peer], r_v.at[peer])
    vec_land[dp] = vec_pack[...]
    vec_out[...] = jnp.concatenate([vec_land[d][:, : D // 8] for d in range(8)], axis=1)
    for cond, copy in started:
        if cond is None:
            copy.wait_send()
        else:
            pl.when(cond)(copy.wait_send)


def gather(block_weights, vector_params):
    dma = pltpu.SemaphoreType.DMA
    sizes = [(6,)] * 8 + [(3, 3)] * 2 + [(2, 3)] * 2 + [(4, 3)] * 2 + [(2,)] * 2 + [(7,), (8,)]
    return pl.pallas_call(
        gather_kernel,
        in_specs=[pl.BlockSpec(memory_space=pltpu.VMEM)] * 2,
        out_specs=[pl.BlockSpec(memory_space=pl.ANY), pl.BlockSpec(memory_space=pltpu.VMEM)],
        out_shape=[
            jax.ShapeDtypeStruct((2, 24, SIDE, PAIR), bf16),
            jax.ShapeDtypeStruct((16, D), f32),
        ],
        scratch_shapes=[
            pltpu.VMEM((3, SIDE, PAIR), bf16),
            pltpu.VMEM((16, 128), f32),
            pltpu.VMEM((8, 16, 128), f32),
        ]
        + [dma(size) for size in sizes]
        + [dma],
        compiler_params=params(collective_id=0, has_side_effects=True),
        name="gather",
    )(block_weights, vector_params)


def project_kernel(tok, pas, vec, wq, norm, q, k, v, cat):
    @pl.when(pl.program_id(0) == 0)
    def _():
        for x in range(3):
            for i in range(4):
                at = (i % 2) * SIDE
                parts = [wq[h, 2 * x + i // 2][:, at : at + SIDE] for h in range(2)]
                cat[x, i * SIDE : (i + 1) * SIDE, :] = jnp.concatenate(parts, axis=1)

    first = embedded(tok[...], pas[...], vec[...])
    hat, _ = hat_of(first)
    low = (hat * vec[PASSES : PASSES + 1] + vec[PASSES + 1 : PASSES + 2]).astype(bf16)
    norm[...] = low
    for x, out in enumerate((q, k, v)):
        out[...] = nn(low, cat[x]).astype(bf16)


def project(tokens, passes, vec, wq):
    seq = tokens.shape[0]
    row = lambda n: pl.BlockSpec((ROWS, n), lambda i: (i, 0))
    wide = jax.ShapeDtypeStruct((seq, PAIR), bf16)
    return pl.pallas_call(
        project_kernel,
        grid=(seq // ROWS,),
        in_specs=[
            row(D),
            pl.BlockSpec((1, ROWS), lambda i: (0, i)),
            full((16, D)),
            full((2, 6, SIDE, PAIR)),
        ],
        out_specs=[row(D), row(PAIR), row(PAIR), row(PAIR), full((3, D, PAIR))],
        out_shape=[
            jax.ShapeDtypeStruct((seq, D), bf16),
            wide,
            wide,
            wide,
            jax.ShapeDtypeStruct((3, D, PAIR), bf16),
        ],
        compiler_params=params(),
        cost_estimate=cost(16),
        name="project",
    )(tokens, passes, vec, wq)


def doc_state(lens, base):
    rows = base + lax.broadcasted_iota(jnp.int32, (1, ROWS), 1)
    rows = jnp.concatenate([rows, rows], axis=1)
    begin = jnp.int32(0)
    first = jnp.int32(0)
    starts = jnp.zeros((1, 2 * ROWS), jnp.int32)
    for c in range(DOCS):
        starts = jnp.where(rows >= begin, begin, starts)
        first = jnp.where(base >= begin, begin, first)
        begin = begin + lens[c]
    return rows, starts, first


def two_heads(block):
    left = lax.broadcasted_iota(jnp.int32, block.shape, 1) < HD
    none = jnp.zeros_like(block)
    return jnp.concatenate([jnp.where(left, block, none), jnp.where(left, none, block)], axis=0)


def one_above(both):
    return jnp.concatenate([both[:HD, :ROWS], both[HD:, ROWS:]], axis=0).T


def attend_kernel(lens, q, k, v, out, lse, top, total, acc):
    i = pl.program_id(0)
    base = i * ROWS
    rows, starts, first = doc_state(lens, base)
    pairs = [two_heads(q[:, p * 128 : (p + 1) * 128] * bf16(0.125)) for p in range(3)]
    for p in range(3):
        top[p] = jnp.full((1, 2 * ROWS), masked_score, f32)
        total[p] = jnp.zeros((1, 2 * ROWS), f32)
        acc[p] = jnp.zeros((128, 2 * ROWS), f32)

    def step(j, carry):
        at = pl.multiple_of(j * ROWS, ROWS)
        keys = at + lax.broadcasted_iota(jnp.int32, (ROWS, 2 * ROWS), 0)
        seen = (keys >= starts) & (keys <= rows)
        for p in range(3):
            cols = slice(p * 128, (p + 1) * 128)
            scores = jnp.where(seen, nt(k[pl.ds(at, ROWS), cols], pairs[p]), masked_score)
            before = top[p]
            now = jnp.maximum(before, jnp.max(scores, axis=0, keepdims=True))
            probs = jnp.exp(scores - now)
            fade = jnp.exp(before - now)
            top[p] = now
            total[p] = total[p] * fade + jnp.sum(probs, axis=0, keepdims=True)
            acc[p] = acc[p] * fade + tn(v[pl.ds(at, ROWS), cols], probs.astype(bf16))
        return carry

    lax.fori_loop(first // ROWS, i + 1, step, 0)
    lines = []
    for p in range(3):
        out[:, p * 128 : (p + 1) * 128] = one_above(acc[p] / total[p]).astype(bf16)
        line = top[p] + jnp.log(total[p])
        lines += [line[:, :ROWS], line[:, ROWS:]]
    lse[...] = jnp.concatenate(lines + lines[:2], axis=0)


def attend(lens, q, k, v):
    seq = q.shape[0]
    row = pl.BlockSpec((ROWS, PAIR), lambda i, s: (i, 0))
    return pl.pallas_call(
        attend_kernel,
        grid_spec=pltpu.PrefetchScalarGridSpec(
            num_scalar_prefetch=1,
            grid=(seq // ROWS,),
            in_specs=[row, full((seq, PAIR)), full((seq, PAIR))],
            out_specs=[row, pl.BlockSpec((8, ROWS), lambda i, s: (0, i))],
            scratch_shapes=[
                pltpu.VMEM((3, 1, 2 * ROWS), f32),
                pltpu.VMEM((3, 1, 2 * ROWS), f32),
                pltpu.VMEM((3, 128, 2 * ROWS), f32),
            ],
        ),
        out_shape=[
            jax.ShapeDtypeStruct((seq, PAIR), bf16),
            jax.ShapeDtypeStruct((8, seq), f32),
        ],
        compiler_params=params(),
        cost_estimate=cost(30),
        name="attend",
    )(lens, q, k, v)


def attend_back_kernel(
    lens, q, k, v, mixed, lse, grad_mixed, dq, dk, dv, dk_acc, dv_acc, dq_acc
):
    i = pl.program_id(0)
    count = pl.num_programs(0)
    base = i * ROWS

    @pl.when(i == 0)
    def _():
        dk_acc[...] = jnp.zeros_like(dk_acc)
        dv_acc[...] = jnp.zeros_like(dv_acc)

    rows, starts, first = doc_state(lens, base)
    heads = lax.broadcasted_iota(jnp.int32, (8, 128), 0)
    lanes = lax.broadcasted_iota(jnp.int32, (8, 128), 1)
    pick = (lanes // HD == heads).astype(f32)
    queries, grads, inner, lines = [], [], [], []
    for p in range(3):
        cols = slice(p * 128, (p + 1) * 128)
        queries.append(two_heads(q[:, cols] * bf16(0.125)))
        grads.append(two_heads(grad_mixed[:, cols]))
        product = grad_mixed[:, cols].astype(f32) * mixed[:, cols].astype(f32)
        sums = lax.dot_general(
            pick,
            product,
            (((1,), (1,)), ((), ())),
            precision=lax.Precision.HIGHEST,
            preferred_element_type=f32,
        )
        inner.append(jnp.concatenate([sums[0:1], sums[1:2]], axis=1))
        lines.append(jnp.concatenate([lse[2 * p : 2 * p + 1], lse[2 * p + 1 : 2 * p + 2]], axis=1))
        dq_acc[p] = jnp.zeros((128, 2 * ROWS), f32)

    def step(j, carry):
        at = pl.multiple_of(j * ROWS, ROWS)
        keys = at + lax.broadcasted_iota(jnp.int32, (ROWS, 2 * ROWS), 0)
        seen = (keys >= starts) & (keys <= rows)
        here = pl.ds(at, ROWS)
        for p in range(3):
            cols = slice(p * 128, (p + 1) * 128)
            kb = k[here, cols]
            scores = jnp.where(seen, nt(kb, queries[p]) - lines[p], masked_score)
            probs = jnp.exp(scores)
            grad_probs = nt(v[here, cols], grads[p])
            grad_scores = (probs * (grad_probs - inner[p])).astype(bf16)
            dv_acc[here, cols] += nn(probs.astype(bf16), grads[p])
            dk_acc[here, cols] += nn(grad_scores, queries[p])
            dq_acc[p] += tn(kb, grad_scores)
        return carry

    lax.fori_loop(first // ROWS, i + 1, step, 0)
    for p in range(3):
        dq[:, p * 128 : (p + 1) * 128] = (one_above(dq_acc[p]) * 0.125).astype(bf16)

    @pl.when(i == count - 1)
    def _():
        dk[...] = dk_acc[...].astype(bf16)
        dv[...] = dv_acc[...].astype(bf16)


def attend_back(lens, q, k, v, mixed, lse, grad_mixed):
    seq = q.shape[0]
    count = seq // ROWS
    row = pl.BlockSpec((ROWS, PAIR), lambda i, s: (i, 0))
    wide = jax.ShapeDtypeStruct((seq, PAIR), bf16)
    return pl.pallas_call(
        attend_back_kernel,
        grid_spec=pltpu.PrefetchScalarGridSpec(
            num_scalar_prefetch=1,
            grid=(count,),
            in_specs=[
                row,
                full((seq, PAIR)),
                full((seq, PAIR)),
                row,
                pl.BlockSpec((8, ROWS), lambda i, s: (0, i)),
                row,
            ],
            out_specs=[row, full((seq, PAIR)), full((seq, PAIR))],
            scratch_shapes=[
                pltpu.VMEM((seq, PAIR), f32),
                pltpu.VMEM((seq, PAIR), f32),
                pltpu.VMEM((3, 128, 2 * ROWS), f32),
            ],
        ),
        out_shape=[wide, wide, wide],
        compiler_params=params(),
        cost_estimate=cost(40),
        name="attend_back",
    )(lens, q, k, v, mixed, lse, grad_mixed)


def feed_kernel(
    small, tok, pas, vec, mine, other, cot, wo_mine, wo_other, w1, w2,
    out_chip, second_keep, grad_second, grad_mixed, sums, o_send, o_keep, *rest,
):
    results, rest = (rest[:4], rest[4:]) if small else (rest[:2], rest[2:])
    (
        wom, woo, up, down, gup, gdown, go, core_out, core_in, far_out, far_in, ga_out, ga_in, oc_out, oc_in, seconds,
        g_send, g_keep, g_in, s_core, r_core, s_far, r_far, s_ga, r_ga, s_oc, r_oc, s_x, r_x,
    ) = rest
    step = pl.program_id(0)
    half = core_out.shape[0]
    t, dp = lax.axis_index("tensor"), lax.axis_index("dp")
    core, side = t % 2, t // 2
    near, far = side * 2 + (1 - core), (1 - side) * 2 + core
    z, column = (dp // 2, dp % 2) if small else (0, 0)
    far_x = z * 2 + 1 - column

    def copy(src, dst, s_sem, r_sem, j, to):
        return pltpu.make_async_remote_copy(
            src_ref=src.at[j],
            dst_ref=dst.at[j],
            send_sem=s_sem.at[j],
            recv_sem=r_sem.at[j],
            device_id={"tensor": to},
            device_id_type=MESH,
        )

    core_copy = lambda j: copy(core_out, core_in, s_core, r_core, j, near)
    far_copy = lambda j: copy(far_out, far_in, s_far, r_far, j, far)
    ga_copy = lambda j: copy(ga_out, ga_in, s_ga, r_ga, j, near)
    oc_copy = lambda j: copy(oc_out, oc_in, s_oc, r_oc, j, near)

    def x_copy(slot):
        return pltpu.make_async_remote_copy(
            src_ref=g_send.at[slot],
            dst_ref=g_in.at[slot],
            send_sem=s_x.at[slot],
            recv_sem=r_x.at[slot],
            device_id={"dp": far_x},
            device_id_type=MESH,
        )

    barrier = pltpu.get_barrier_semaphore()

    @pl.when(step == 0)
    def _():
        for to in (near, far):
            pl.semaphore_signal(barrier, inc=1, device_id={"tensor": to}, device_id_type=MESH)
        if small:
            pl.semaphore_signal(barrier, inc=1, device_id={"dp": far_x}, device_id_type=MESH)
        for h in range(2):
            for m in range(2):
                rows, cols = slice(h * SIDE, (h + 1) * SIDE), slice(m * PAIR, (m + 1) * PAIR)
                wom[rows, cols] = wo_mine[h, m]
                woo[rows, cols] = wo_other[h, m]
        for r in range(4):
            for m in range(2):
                rows, cols = slice(r * SIDE, (r + 1) * SIDE), slice(m * PAIR, (m + 1) * PAIR)
                up[rows, cols] = w1[0, 2 * r + m]
                down[rows, cols] = w2[0, 2 * r + m]
        gup[...] = jnp.zeros_like(gup)
        gdown[...] = jnp.zeros_like(gdown)
        go[...] = jnp.zeros_like(go)
        sums[...] = jnp.zeros_like(sums)
        pl.semaphore_wait(barrier, 3 if small else 2)

    @pl.when(step < 2 * half)
    def _():
        j = step // 2
        owner = jnp.where(step % 2 == 0, 1 - core, core)
        here = pl.ds(pl.multiple_of((owner * half + j) * ROWS, ROWS), ROWS)
        first = embedded(tok[...], pas[...], vec[...])
        second = first + (nn(mine[here, :], wom[...]) + nn(other[...], woo[...]))
        hat, _ = hat_of(second)
        low = (hat * vec[PASSES + 2 : PASSES + 3] + vec[PASSES + 3 : PASSES + 4]).astype(bf16)
        upper = nn(low, up[...])
        square = upper * upper
        bent = jnp.tanh(gelu_coef * upper * (1.0 + 0.044715 * square))
        act = (0.5 * upper * (1.0 + bent)).astype(bf16)
        slope = 0.5 * (1.0 + bent) + (0.5 * gelu_coef) * upper * (1.0 - bent * bent) * (
            1.0 + (3 * 0.044715) * square
        )
        grad_act = nt(cot[...], down[...])
        grad_upper = (grad_act * slope).astype(bf16)
        part = nt(grad_upper, up[...])

        @pl.when(step % 2 == 0)
        def _():
            core_out[j] = part.astype(bf16)
            core_copy(j).start()

        @pl.when(step % 2 == 1)
        def _():
            core_copy(j).wait_recv()
            far_out[j] = (part + core_in[j].astype(f32)).astype(bf16)
            far_copy(j).start()
            second_keep[...] = second
            seconds[j] = second

        gup[...] += tn(low, grad_upper)
        gdown[...] += tn(act, cot[...])
        out_part = nn(act, down[...])

        @pl.when(step % 2 == 0)
        def _():
            oc_out[j] = out_part.astype(bf16)
            oc_copy(j).start()

        @pl.when(step % 2 == 1)
        def _():
            oc_copy(j).wait_recv()
            out_chip[...] = (out_part + oc_in[j].astype(f32)).astype(bf16)

    @pl.when(step == 2 * half - 1)
    def _():
        for r in range(4):
            for m in range(2):
                rows, cols = slice(r * SIDE, (r + 1) * SIDE), slice(m * PAIR, (m + 1) * PAIR)
                for at, total in ((8, gup), (16, gdown)):
                    pair = at + 2 * r + m
                    slot, place = (pair // 6 - 1) * 3 + pair % 3, pair // 3 % 2
                    value = total[rows, cols].astype(bf16)

                    @pl.when(column == place)
                    def _():
                        g_keep[slot] = value

                    @pl.when(column != place)
                    def _():
                        g_send[slot] = value
        if small:
            for slot in range(9):
                pl.when((column == 0) | (slot > 1))(x_copy(slot).start)
        for slot in range(2):

            @pl.when(column == 0)
            def _():
                g_keep[slot] = jnp.zeros((SIDE, PAIR), bf16)

    def through_out(grad, block):
        here = pl.ds(pl.multiple_of(block * ROWS, ROWS), ROWS)
        grad_mixed[here, :] = nt(grad, wom[...]).astype(bf16)
        go[...] += tn(mine[here, :], grad)

    @pl.when((step >= 2 * half) & (step < 3 * half))
    def _():
        j = step - 2 * half
        hat, root = hat_of(seconds[j])
        far_copy(j).wait_recv()
        grad = far_out[j].astype(f32) + far_in[j].astype(f32)
        result = cot[...].astype(f32) + norm_back(hat, root, grad, vec[PASSES + 2 : PASSES + 3])
        low = result.astype(bf16)
        ga_out[j] = low
        ga_copy(j).start()
        grad_second[...] = result
        sums[0:1] += jnp.sum(grad * hat, axis=0, keepdims=True)
        sums[1:2] += jnp.sum(grad, axis=0, keepdims=True)
        through_out(low, core * half + j)

    @pl.when(step > 2 * half)
    def _():
        j = step - 2 * half - 1
        ga_copy(j).wait_recv()
        through_out(ga_in[j], (1 - core) * half + j)

    @pl.when(step == 3 * half)
    def _():
        at = pl.multiple_of(side * SIDE, SIDE)
        for m in range(2):
            value = go[pl.ds(at, SIDE), m * PAIR : (m + 1) * PAIR].astype(bf16)
            none = jnp.zeros_like(value)
            o_keep[m] = jnp.where(column == 0, value, none)
            o_send[m] = jnp.where(column == 0, none, value)
        for j in range(half):
            core_copy(j).wait_send()
            oc_copy(j).wait_send()
            far_copy(j).wait_send()
            ga_copy(j).wait_send()
        if small:
            for slot in range(9):
                pl.when((column == 1) | (slot > 1))(x_copy(slot).wait_recv)
                pl.when((column == 0) | (slot > 1))(x_copy(slot).wait_send)
            for slot in range(9):
                if slot > 1:
                    value = (g_keep[slot].astype(f32) + g_in[slot].astype(f32)).astype(bf16)
                else:
                    other_term = jnp.where(column == 1, g_in[slot], jnp.zeros((SIDE, PAIR), bf16))
                    value = (g_keep[slot].astype(f32) + other_term.astype(f32)).astype(bf16)
                for turn in range(4):

                    @pl.when(z + turn == slot // 3 + 1 + 4 * (z + turn >= 4).astype(jnp.int32))
                    def _():
                        results[turn][slot % 3] = value
        else:
            results[0][...] = g_send[...]
            results[1][...] = g_keep[...]


def feed(small, tokens, passes, vec, mine, other, cotangent, pairs, wo_other):
    seq = tokens.shape[0]
    half = seq // ROWS // 2

    def block(i):
        core = lax.axis_index("tensor") % 2
        work = jnp.minimum(i, 2 * half - 1)
        owner = jnp.where(work % 2 == 0, 1 - core, core)
        return owner * half + work // 2

    def cot_block(i):
        core = lax.axis_index("tensor") % 2
        return jnp.where(i < 2 * half, block(i), core * half + jnp.minimum(i - 2 * half, half - 1))

    side = lambda: lax.axis_index("tensor") // 2
    row = lambda n: pl.BlockSpec((ROWS, n), lambda i: (block(i), 0))
    keep = pl.BlockSpec((ROWS, D), lambda i: (jnp.minimum(i // 2, half - 1), 0))
    last = pl.BlockSpec((ROWS, D), lambda i: (jnp.clip(i - 2 * half, 0, half - 1), 0))
    rows = lambda kind: jax.ShapeDtypeStruct((seq // 2, D), kind)
    gr = lambda n: jax.ShapeDtypeStruct((n, SIDE, PAIR), bf16)
    ends = [(3, SIDE, PAIR)] * 4 if small else [(9, SIDE, PAIR)] * 2
    buffer = pltpu.VMEM((half, ROWS, D), bf16)
    dma = pltpu.SemaphoreType.DMA((half,))
    return pl.pallas_call(
        functools.partial(feed_kernel, small),
        grid=(3 * half + 1,),
        in_specs=[
            row(D),
            pl.BlockSpec((1, ROWS), lambda i: (0, block(i))),
            full((16, D)),
            full((seq, PAIR)),
            row(PAIR),
            pl.BlockSpec((ROWS, D), lambda i: (cot_block(i), 0)),
            pl.BlockSpec((2, 2, SIDE, PAIR), lambda i: (0, 3, 0, 0)),
            full(wo_other.shape),
            pl.BlockSpec((1, 8, SIDE, PAIR), lambda i: (side(), 1, 0, 0)),
            pl.BlockSpec((1, 8, SIDE, PAIR), lambda i: (side(), 2, 0, 0)),
        ],
        out_specs=[
            keep,
            keep,
            last,
            full((seq, PAIR)),
            full((8, D)),
            full((2, SIDE, PAIR)),
            full((2, SIDE, PAIR)),
        ]
        + [full(shape) for shape in ends],
        scratch_shapes=[
            pltpu.VMEM((PAIR, D), bf16),
            pltpu.VMEM((PAIR, D), bf16),
            pltpu.VMEM((D, D), bf16),
            pltpu.VMEM((D, D), bf16),
            pltpu.VMEM((D, D), f32),
            pltpu.VMEM((D, D), f32),
            pltpu.VMEM((PAIR, D), f32),
        ]
        + [buffer] * 8
        + [pltpu.VMEM((half, ROWS, D), f32)]
        + [pltpu.VMEM((9, SIDE, PAIR), bf16)] * 3
        + [dma] * 8
        + [pltpu.SemaphoreType.DMA((9,))] * 2,
        out_shape=[
            rows(bf16),
            rows(f32),
            rows(f32),
            jax.ShapeDtypeStruct((seq, PAIR), bf16),
            jax.ShapeDtypeStruct((8, D), f32),
            gr(2),
            gr(2),
        ]
        + [jax.ShapeDtypeStruct(shape, bf16) for shape in ends],
        compiler_params=params(collective_id=1, has_side_effects=True),
        cost_estimate=cost(50),
        name="feed_forward",
    )(tokens, passes, vec, mine, other, cotangent, pairs, wo_other, pairs, pairs)


def qkv_grads_kernel(place, norm, dq, dk, dv, o_send, o_keep, g_send, g_keep, acc):
    i = pl.program_id(0)

    @pl.when(i == 0)
    def _():
        acc[...] = jnp.zeros_like(acc)

    for x, grad in enumerate((dq, dk, dv)):
        mine = jnp.where(place[1] == 0, grad[:, :SIDE].astype(f32), grad[:, SIDE:].astype(f32))
        acc[x] += tn(norm[...], mine.astype(bf16))

    @pl.when(i == pl.num_programs(0) - 1)
    def _():
        for m in range(2):
            g_send[3 + m] = o_send[m]
            g_keep[3 + m] = o_keep[m]
        for x in range(3):
            for m in range(2):
                at = 2 * m * SIDE
                value = jnp.concatenate(
                    [acc[x, at : at + SIDE], acc[x, at + SIDE : at + 2 * SIDE]], axis=1
                ).astype(bf16)
                slot, column = (2 * x + m) % 3, (2 * x + m) // 3

                @pl.when(place[2] == column)
                def _():
                    g_keep[slot] = value

                @pl.when(place[2] != column)
                def _():
                    g_send[slot] = value


def qkv_grads(place, norm, dq, dk, dv, o_send, o_keep):
    seq = norm.shape[0]
    row = lambda n: pl.BlockSpec((ROWS, n), lambda i, s: (i, 0))
    return pl.pallas_call(
        qkv_grads_kernel,
        grid_spec=pltpu.PrefetchScalarGridSpec(
            num_scalar_prefetch=1,
            grid=(seq // ROWS,),
            in_specs=[row(D), row(PAIR), row(PAIR), row(PAIR)] + [full((2, SIDE, PAIR))] * 2,
            out_specs=[full((5, SIDE, PAIR)), full((5, SIDE, PAIR))],
            scratch_shapes=[pltpu.VMEM((3, D, SIDE), f32)],
        ),
        out_shape=[jax.ShapeDtypeStruct((5, SIDE, PAIR), bf16)] * 2,
        compiler_params=params(),
        cost_estimate=cost(8),
        name="qkv_grads",
    )(place, norm, dq, dk, dv, o_send, o_keep)


CHUNK = SIDE // 2
CHUNKS = 10


def last_kernel(small, dq, dk, dv, cat, tok, pas, vec, grad_second, sums_two, g_send, g_keep, low, *rest):
    if small:
        late, vec_sum = rest[:2]
        rest = rest[2:]
        (
            core_out, core_in, sums, core_sums, x_in, z_in, z_out, up_in, v_out, v_in,
            s_core, r_core, s_sum, r_sum, s_x, r_x, s_z, r_z, s_up, r_up, s_v, r_v,
        ) = rest
    else:
        vec_sum, core_out, core_in, sums, core_sums, s_core, r_core, s_sum, r_sum = rest
    i = pl.program_id(0)
    half = core_out.shape[0]
    t, dp = lax.axis_index("tensor"), lax.axis_index("dp")
    core, side = t % 2, t // 2
    near = side * 2 + (1 - core)
    z, column = (dp // 2, dp % 2) if small else (0, 0)
    far_x = z * 2 + 1 - column
    peers = [lax.rem(dp + k, 8) for k in range(1, 8)]

    def copy(src, dst, s_sem, r_sem, to):
        return pltpu.make_async_remote_copy(
            src_ref=src, dst_ref=dst, send_sem=s_sem, recv_sem=r_sem, device_id=to, device_id_type=MESH
        )

    core_copy = lambda j: copy(core_out.at[j], core_in.at[j], s_core.at[j], r_core.at[j], {"tensor": near})
    sum_copy = lambda: copy(sums, core_sums, s_sum, r_sum, {"tensor": near})

    def part_of(ref, k):
        return ref.at[k // 2, pl.ds((k % 2) * CHUNK, CHUNK)]

    x_copy = lambda k: copy(part_of(g_send, k), x_in.at[k], s_x.at[k], r_x.at[k], {"dp": far_x})
    z_copy = lambda k: copy(z_out.at[k], z_in.at[k], s_z.at[k], r_z.at[k], {"dp": dp - 2})
    up_copy = lambda k: copy(z_out.at[k], up_in.at[k - 6], s_up.at[k - 6], r_up.at[k - 6], {"dp": dp + 2})
    v_copy = lambda n: copy(v_out.at[peers[n]], v_in.at[dp], s_v.at[n], r_v.at[dp], {"dp": peers[n]})
    barrier = pltpu.get_barrier_semaphore()

    @pl.when(i == 0)
    def _():
        pl.semaphore_signal(barrier, inc=1, device_id={"tensor": near}, device_id_type=MESH)
        if small:
            for peer in peers:
                pl.semaphore_signal(barrier, inc=1, device_id={"dp": peer}, device_id_type=MESH)
            late[...] = jnp.zeros_like(late)
        sums[...] = jnp.zeros_like(sums)
        sums[PASSES + 2 : PASSES + 4] = sums_two[0:2]
        pl.semaphore_wait(barrier, 8 if small else 1)
        if small:
            for k in range(CHUNKS):
                if k < 6:
                    x_copy(k).start()
                else:
                    pl.when(column == 1)(x_copy(k).start)

    @pl.when(i < 2 * half)
    def _():
        part = nt(dq[...], cat[0]) + nt(dk[...], cat[1]) + nt(dv[...], cat[2])

        @pl.when(i < half)
        def _():
            core_out[i] = part.astype(bf16)
            core_copy(i).start()

        @pl.when(i >= half)
        def _():
            j = i - half
            hat, root = hat_of(embedded(tok[...], pas[...], vec[...]))
            core_copy(j).wait_recv()
            grad = part + core_in[j].astype(f32)
            result = grad_second[...] + norm_back(hat, root, grad, vec[PASSES : PASSES + 1])
            low[...] = result.astype(bf16)
            chosen = one_hot(pas[...])
            high, mid, tail = split_three(result)
            sums[...] += nn(chosen, high) + nn(chosen, mid) + nn(chosen, tail)
            sums[PASSES : PASSES + 1] += jnp.sum(grad * hat, axis=0, keepdims=True)
            sums[PASSES + 1 : PASSES + 2] += jnp.sum(grad, axis=0, keepdims=True)

    @pl.when(i == 2 * half - 1)
    def _():
        sum_copy().start()

    if small:

        def term_of(k):
            x_copy(k).wait_recv()
            keep = g_keep[k // 2, pl.ds(pl.multiple_of((k % 2) * CHUNK, 16), CHUNK), :]
            return keep.astype(f32) + x_in[k].astype(f32)

        def keep_late(k, pair, total):
            late[pair, pl.ds(pl.multiple_of((k % 2) * CHUNK, 16), CHUNK), :] = total

        k = i - 2 - 2 * (3 - z)

        @pl.when((k >= 0) & (k < 6))
        def _():
            total = term_of(k)

            @pl.when(z == 3)
            def _():
                z_out[k] = total.astype(bf16)
                z_copy(k).start()

            @pl.when((z == 1) | (z == 2))
            def _():
                z_copy(k).wait_recv()
                z_out[k] = (total + z_in[k].astype(f32)).astype(bf16)
                z_copy(k).start()

            @pl.when(z == 0)
            def _():
                z_copy(k).wait_recv()
                keep_late(k, k // 2, total + z_in[k].astype(f32))

        @pl.when((k >= 6) & (k < CHUNKS) & (column == 0) & (z > 0))
        def _():
            total = term_of(k)

            @pl.when(z == 3)
            def _():
                z_out[k] = total.astype(bf16)
                z_copy(k).start()

            @pl.when(z == 2)
            def _():
                z_copy(k).wait_recv()
                z_out[k] = (total + z_in[k].astype(f32)).astype(bf16)
                z_copy(k).start()

            @pl.when(z == 1)
            def _():
                z_copy(k).wait_recv()
                up_copy(k).wait_recv()
                keep_late(k, k // 2 - 3, total + z_in[k].astype(f32) + up_in[k - 6].astype(f32))

        @pl.when((i >= 8) & (i < 12) & (column == 0) & (z == 0))
        def _():
            z_out[i - 2] = term_of(i - 2).astype(bf16)
            up_copy(i - 2).start()

    @pl.when(i == 2 * half + 1)
    def _():
        sum_copy().wait_recv()
        total = sums[...] + core_sums[...]
        if small:
            wide = D // 8
            for d in range(8):
                v_out[d, :, 0:wide] = total[:, d * wide : (d + 1) * wide]
                v_out[d, :, wide:] = jnp.zeros((16, 128 - wide), f32)
            for n in range(7):
                v_copy(n).start()
        else:
            vec_sum[...] = total

    @pl.when(i == pl.num_programs(0) - 1)
    def _():
        for j in range(half):
            core_copy(j).wait_send()
        sum_copy().wait_send()
        if small:
            for peer in peers:
                copy(v_out.at[0], v_in.at[peer], s_v.at[0], r_v.at[peer], {"dp": far_x}).wait_recv()
            v_in[dp] = v_out[dp]
            total = v_in[0]
            for d in range(1, 8):
                total = total + v_in[d]
            vec_sum[...] = total
            for n in range(7):
                v_copy(n).wait_send()
            for k in range(CHUNKS):
                if k < 6:
                    x_copy(k).wait_send()
                    pl.when(z > 0)(z_copy(k).wait_send)
                else:
                    pl.when(column == 1)(x_copy(k).wait_send)
                    pl.when((column == 0) & (z > 1))(z_copy(k).wait_send)
                    pl.when((column == 0) & (z == 0))(up_copy(k).wait_send)


def last(small, dq, dk, dv, cat, tokens, passes, vec, grad_second, sums_two, g_send, g_keep):
    seq = dq.shape[0]
    half = seq // ROWS // 2
    core = lambda: lax.axis_index("tensor") % 2

    def block(i):
        work = jnp.minimum(i, 2 * half - 1)
        return lax.rem(work + (1 - core()) * half, 2 * half)

    own = lambda i: jnp.clip(i - half, 0, half - 1)
    row = pl.BlockSpec((ROWS, PAIR), lambda i: (block(i), 0))
    mine = pl.BlockSpec((ROWS, D), lambda i: (own(i), 0))
    dma = pltpu.SemaphoreType.DMA
    out_specs = [mine]
    out_shape = [jax.ShapeDtypeStruct((seq // 2, D), bf16)]
    scratch = [
        pltpu.VMEM((half, ROWS, D), bf16),
        pltpu.VMEM((half, ROWS, D), bf16),
        pltpu.VMEM((16, D), f32),
        pltpu.VMEM((16, D), f32),
    ]
    sems = [dma((half,)), dma((half,)), dma, dma]
    if small:
        out_specs += [full((3, SIDE, PAIR)), full((16, 128))]
        out_shape += [
            jax.ShapeDtypeStruct((3, SIDE, PAIR), f32),
            jax.ShapeDtypeStruct((16, 128), f32),
        ]
        scratch += [pltpu.VMEM((CHUNKS, CHUNK, PAIR), bf16)] * 3
        scratch += [pltpu.VMEM((4, CHUNK, PAIR), bf16)]
        scratch += [pltpu.VMEM((8, 16, 128), f32)] * 2
        sems += [dma((CHUNKS,))] * 4 + [dma((4,))] * 2 + [dma((7,)), dma((8,))]
    else:
        out_specs += [full((16, D))]
        out_shape += [jax.ShapeDtypeStruct((16, D), f32)]
    return pl.pallas_call(
        functools.partial(last_kernel, small),
        grid=(2 * half + 8 if small else 2 * half + 2,),
        in_specs=[
            row,
            row,
            row,
            full(cat.shape),
            pl.BlockSpec((ROWS, D), lambda i: (core() * half + own(i), 0)),
            pl.BlockSpec((1, ROWS), lambda i: (0, core() * half + own(i))),
            full((16, D)),
            mine,
            full((8, D)),
            full(g_send.shape),
            full(g_keep.shape),
        ],
        out_specs=out_specs,
        out_shape=out_shape,
        scratch_shapes=scratch + sems,
        compiler_params=params(collective_id=2, has_side_effects=True),
        cost_estimate=cost(30),
        name="last",
    )(dq, dk, dv, cat, tokens, passes, vec, grad_second, sums_two, g_send, g_keep)


def precondition(grad, weight, left, right, left_root, right_root):
    high = lax.Precision.HIGHEST
    left_new = decay * left + (1.0 - decay) * jnp.einsum(
        "...ij,...kj->...ik", grad, grad, precision=high
    )
    right_new = decay * right + (1.0 - decay) * jnp.einsum(
        "...ji,...jk->...ik", grad, grad, precision=high
    )
    half = jnp.einsum("...ij,...jk->...ik", left_root, grad, precision=high)
    step = jnp.einsum("...ij,...jk->...ik", half, right_root, precision=high)
    return (left_new, right_new, step, weight - rate_matrix * step)


def to_pairs(blocks):
    n = blocks.shape[0] // 2
    return blocks.reshape(n, 2, SIDE, SIDE).transpose(0, 2, 1, 3).reshape(n, SIDE, PAIR)


def from_pairs(pairs):
    n = pairs.shape[0]
    return pairs.reshape(n, SIDE, 2, SIDE).transpose(0, 2, 1, 3).reshape(2 * n, SIDE, SIDE)


def swap(value, bit):
    return lax.ppermute(value, "tensor", [(t, t ^ bit) for t in range(NT)])


def hop_z(value, turn, ends):
    pairs = [(d, (d + 2 * turn) % 8) for d in range(8) if (d // 2 + turn) % 4 in ends]
    return lax.ppermute(value, "dp", pairs)


def tie(*values):
    return lax.optimization_barrier(values)


def on_device(
    tokens,
    pass_ids,
    doc_lengths,
    cotangent,
    block_weights,
    vector_params,
    vector_moment,
    block_left,
    block_right,
    block_left_root,
    block_right_root,
):
    t, dp = lax.axis_index("tensor"), lax.axis_index("dp")
    core, side = t % 2, t // 2
    n_dp = lax.axis_size("dp")
    small = n_dp == 8
    z, column = (dp // 2, dp % 2) if small else (0, 0)
    place = jnp.stack([core, side, jnp.asarray(column, jnp.int32)]).astype(jnp.int32)
    lens = doc_lengths[0]
    seq = tokens.shape[0]
    passes = pass_ids.reshape(1, seq)
    total_blocks = (D // SIDE) * (4 + 2 * (FF // D))
    slots = block_weights.shape[1] * n_dp

    if small:
        pairs, vec = gather(block_weights, vector_params)
    else:
        every = lax.all_gather(block_weights.astype(bf16), "dp", axis=1, tiled=True)[0]
        near = to_pairs(every[:total_blocks])
        far = swap(near, 2)
        pairs = jnp.where(side == 0, jnp.stack([near, far]), jnp.stack([far, near]))
        vec = lax.all_gather(vector_params, "dp", axis=1, tiled=True)
        vec = jnp.pad(vec, ((0, 16 - vec.shape[0]), (0, 0)))
    wo_other = swap(pairs[:, 6:8], 1)

    norm, q, k, v, cat = project(tokens, passes, vec, pairs)
    mine, lse = attend(lens, q, k, v)
    other = swap(mine, 1)
    out_chip, second, grad_second, grad_mixed, sums_two, o_send, o_keep, *ends = feed(
        small, tokens, passes, vec, mine, other, cotangent, pairs, wo_other
    )
    out_far = swap(out_chip, 2)
    if small:
        far = [hop_z(ends[turn], turn, (1, 2, 3)) for turn in (1, 2, 3)]
    dq, dk, dv = attend_back(lens, q, k, v, mine, lse, grad_mixed)
    g_send, g_keep = qkv_grads(place, norm, dq, dk, dv, o_send, o_keep)
    if small:
        *far, out_far, g_send = tie(*far, out_far, g_send)
    low_half, *sums = last(
        small, dq, dk, dv, cat, tokens, passes, vec, grad_second, sums_two, g_send, g_keep
    )
    out_half = (second + (out_chip.astype(f32) + out_far.astype(f32))).astype(bf16)

    def join(half):
        far = swap(half, 1)
        low = jnp.where(core == 0, half, far)
        high = jnp.where(core == 0, far, half)
        return jnp.concatenate([low, high], axis=0)

    output, input_grad = join(out_half), join(low_half)
    if small:
        late, vector_sum = sums
        early = ends[0].astype(f32)
        for value in far:
            early = early + value.astype(f32)
        owned = from_pairs(late + jnp.where(z == 0, 0.0, early))[None]
        vector_grad = vector_sum[: PASSES + 4, : vector_params.shape[1]]
    else:
        vector_part = sums[0][: PASSES + 4]
        w12_send, w12_keep = ends
        up_down = jnp.stack(
            [w12_keep.reshape(3, 3, SIDE, PAIR), w12_send.reshape(3, 3, SIDE, PAIR)], axis=1
        )
        up_down = up_down.reshape(18, SIDE, PAIR)[2:]
        grad_blocks = from_pairs(
            jnp.concatenate([g_keep[:3], g_send[:3], o_keep, up_down], axis=0)
        ).astype(f32)
        spare = jnp.zeros((slots - total_blocks, SIDE, SIDE), f32)
        grad_blocks = jnp.concatenate([grad_blocks, spare], axis=0)[None]
        owned = lax.psum_scatter(grad_blocks, "dp", scatter_dimension=1, tiled=True)
        vector_grad = lax.psum_scatter(vector_part, "dp", scatter_dimension=1, tiled=True)
    left_new, right_new, step, weight_new = precondition(
        owned, block_weights, block_left, block_right, block_left_root, block_right_root
    )
    moment_new = decay * vector_moment + (1.0 - decay) * vector_grad * vector_grad
    vector_new = vector_params - rate_vector * vector_grad / (jnp.sqrt(moment_new) + moment_eps)
    return (
        output,
        input_grad,
        left_new,
        right_new,
        step,
        weight_new,
        vector_grad,
        moment_new,
        vector_new,
    )


def solution(mesh):
    rows, line = P("dp", None), P(None, "dp")
    block = P("tensor", "dp", None, None)
    return jax.shard_map(
        on_device,
        mesh=mesh,
        in_specs=(rows, P("dp"), rows, rows, block, line, line, block, block, block, block),
        out_specs=(rows, rows, block, block, block, block, line, line, line),
        check_vma=False,
    )
```

```python
import functools

import jax
import jax.numpy as jnp
from jax import lax
from jax.experimental import pallas as pl
from jax.experimental.pallas import tpu as pltpu
from jax.sharding import PartitionSpec as P

D = 768
HD = 64
FF = 3072
PASSES = 5
SIDE = 192
PAIR = 2 * SIDE
ROWS = 256
WIDE = 512
DOCS = 8
NT = 4

norm_eps = 1e-05
moment_eps = 1e-08
rate_matrix = 0.03
rate_vector = 0.2
decay = 0.5
gelu_coef = 0.7978845608028654
masked_score = -1e30
f32 = jnp.float32
bf16 = jnp.bfloat16
MESH = pl.DeviceIdType.MESH
VMEM_LIMIT = 56 * 1024 * 1024


def nn(a, b):
    return lax.dot_general(a, b, (((1,), (0,)), ((), ())), preferred_element_type=f32)


def nt(a, b):
    return lax.dot_general(a, b, (((1,), (1,)), ((), ())), preferred_element_type=f32)


def tn(a, b):
    return lax.dot_general(a, b, (((0,), (0,)), ((), ())), preferred_element_type=f32)


def split_three(value):
    high = value.astype(bf16)
    rest = value - high.astype(f32)
    mid = rest.astype(bf16)
    return high, mid, (rest - mid.astype(f32)).astype(bf16)


def one_hot(pass_row):
    kinds = lax.broadcasted_iota(jnp.int32, (16, pass_row.shape[1]), 0)
    return (kinds == pass_row).astype(f32).astype(bf16)


def embedded(tokens, pass_row, vec):
    chosen = jnp.concatenate([one_hot(pass_row)] * 3, axis=0)
    return tokens.astype(f32) + tn(chosen, jnp.concatenate(split_three(vec), axis=0))


def hat_of(hidden):
    mean = jnp.mean(hidden, axis=-1, keepdims=True)
    center = hidden - mean
    spread = jnp.mean(center * center, axis=-1, keepdims=True)
    root = lax.rsqrt(spread + norm_eps)
    return center * root, root


def norm_back(hat, root, grad, gain):
    scaled = grad * gain
    first = jnp.mean(scaled, axis=-1, keepdims=True)
    second = jnp.mean(scaled * hat, axis=-1, keepdims=True)
    return root * (scaled - first - hat * second)


def params(**kw):
    return pltpu.CompilerParams(vmem_limit_bytes=VMEM_LIMIT, **kw)


def cost(micros):
    return pl.CostEstimate(flops=int(micros * 1.1e9), bytes_accessed=int(micros * 1e6), transcendentals=0)


def full(shape):
    return pl.BlockSpec(shape, lambda *_: (0,) * len(shape))


def gather_kernel(own, vec_own, all_pairs, vec_out, pack, vec_pack, vec_land, *sems):
    (s_z1, r_z1, s_x1, r_x1, s_y1, r_y1, s_d1, r_d1, s_l, r_l, s_r, r_r, s_x2, r_x2, s_y2, r_y2, s_v, r_v, loc) = sems
    dp, t = lax.axis_index("dp"), lax.axis_index("tensor")
    z, x = dp // 2, dp % 2
    y, core = t // 2, t % 2
    far_x, far_y = z * 2 + (1 - x), (1 - y) * 2 + core

    barrier = pltpu.get_barrier_semaphore()
    peers = [lax.rem(dp + k, 8) for k in range(1, 8)]
    for peer in peers:
        pl.semaphore_signal(barrier, inc=1, device_id={"dp": peer, "tensor": t}, device_id_type=MESH)
    pl.semaphore_signal(barrier, inc=1, device_id={"dp": dp, "tensor": far_y}, device_id_type=MESH)

    for m in range(3):
        pack[m] = jnp.concatenate([own[0, 2 * m], own[0, 2 * m + 1]], axis=1).astype(bf16)
    vec_pack[...] = jnp.zeros_like(vec_pack)
    vec_pack[0 : PASSES + 4, 0 : D // 8] = vec_own[...]
    pl.semaphore_wait(barrier, 8)

    started = []

    def send(src, dst, s_sem, r_sem, dp_to, t_to, cond=None):
        copy = pltpu.make_async_remote_copy(
            src_ref=src,
            dst_ref=dst,
            send_sem=s_sem,
            recv_sem=r_sem,
            device_id={"dp": dp_to, "tensor": t_to},
            device_id_type=MESH,
        )
        started.append((cond, copy))
        if cond is None:
            copy.start()
        else:
            pl.when(cond)(copy.start)

    def arrived(dst, r_sem, cond=None):
        copy = pltpu.make_async_remote_copy(
            src_ref=dst,
            dst_ref=dst,
            send_sem=loc,
            recv_sem=r_sem,
            device_id={"dp": far_x, "tensor": t},
            device_id_type=MESH,
        )
        if cond is None:
            copy.wait_recv()
        else:
            pl.when(cond)(copy.wait_recv)

    own_copy = pltpu.make_async_copy(pack, all_pairs.at[y, pl.ds(3 * dp, 3)], loc)
    own_copy.start()

    for m in range(3):
        send(pack.at[m], all_pairs.at[y, 3 * dp + m], s_l.at[0, m], r_l.at[0, m], dp - 2, t, z > 0)
    for k, peer in enumerate(peers):
        send(vec_pack, vec_land.at[dp], s_v.at[k], r_v.at[dp], peer, t)
    for m in range(3):
        send(pack.at[m], all_pairs.at[y, 3 * dp + m], s_x2.at[z, m], r_x2.at[z, m], far_x, t, z > m)
    own_copy.wait()

    half = SIDE // 2

    def piece(side, column, k):
        return all_pairs.at[side, 3 * column + k // 2, pl.ds((k % 2) * half, half)]

    def diagonal(k):
        arrived(piece(y, 1 - x, k), r_x1.at[k])
        send(piece(y, 1 - x, k), piece(y, 1 - x, k), s_d1.at[k], r_d1.at[k], dp, far_y)

    def from_right(d, m):
        arrived(all_pairs.at[y, 3 * dp + 6 * d + m], r_l.at[d - 1, m], z + d < 4)
        if d < 3:
            ref = all_pairs.at[y, 3 * dp + 6 * d + m]
            send(ref, ref, s_l.at[d, m], r_l.at[d, m], dp - 2, t, (z + d < 4) & (z > 0))

    def right_along_x(d, m):
        ref = all_pairs.at[y, 3 * dp + 6 * d + m]
        send(ref, ref, s_x2.at[z + d, m], r_x2.at[z + d, m], far_x, t, z + d < 4)

    for k in range(6):
        arrived(piece(y, x, k), r_z1.at[k], z > 0)
        send(piece(y, x, k), piece(y, x, k), s_z1.at[k], r_z1.at[k], dp + 2, t, z < 3)
        send(piece(y, x, k), piece(y, x, k), s_x1.at[k], r_x1.at[k], far_x, t)
        send(piece(y, x, k), piece(y, x, k), s_y1.at[k], r_y1.at[k], dp, far_y)
        if k >= 1:
            diagonal(k - 1)
        if k % 2 == 1:
            from_right(1, k // 2)
    diagonal(5)

    for m in range(3):
        send(pack.at[m], all_pairs.at[y, 3 * dp + m], s_x2.at[z, m], r_x2.at[z, m], far_x, t, (z > 0) & (z <= m))
    for m in range(3):
        send(pack.at[m], all_pairs.at[y, 3 * dp + m], s_r.at[0, m], r_r.at[0, m], dp + 2, t, (z > 0) & (z < 3))
    for m in range(3):
        right_along_x(1, m)
    for d in (2, 3):
        for m in range(3):
            from_right(d, m)
            right_along_x(d, m)
    for d in (1, 2):
        for m in range(3):
            ref = all_pairs.at[y, 3 * dp - 6 * d + m]
            arrived(ref, r_r.at[d - 1, m], z - d > 0)
            if d == 1:
                send(ref, ref, s_r.at[1, m], r_r.at[1, m], dp + 2, t, (z - d > 0) & (z < 3))
            send(ref, ref, s_x2.at[z - d, m], r_x2.at[z - d, m], far_x, t, z - d > 0)
    for m in range(2):
        ref = all_pairs.at[y, 6 + m]
        arrived(ref, r_x2.at[1, m], x == 1)
        send(ref, ref, s_y2.at[m], r_y2.at[m], dp, far_y)

    for k in range(6):
        arrived(piece(1 - y, x, k), r_y1.at[k])
        arrived(piece(1 - y, 1 - x, k), r_d1.at[k])
    for w in range(1, 4):
        for m in range(3):
            ref = all_pairs.at[y, 6 * w + 3 * (1 - x) + m]
            if w == 1 and m < 2:
                arrived(ref, r_x2.at[w, m], x == 0)
            else:
                arrived(ref, r_x2.at[w, m])
    for m in range(2):
        arrived(all_pairs.at[1 - y, 6 + m], r_y2.at[m])
    for peer in peers:
        arrived(vec_land.at[peer], r_v.at[peer])
    vec_land[dp] = vec_pack[...]
    vec_out[...] = jnp.concatenate([vec_land[d][:, : D // 8] for d in range(8)], axis=1)
    for cond, copy in started:
        if cond is None:
            copy.wait_send()
        else:
            pl.when(cond)(copy.wait_send)


def gather(block_weights, vector_params):
    dma = pltpu.SemaphoreType.DMA
    sizes = [(6,)] * 8 + [(3, 3)] * 2 + [(2, 3)] * 2 + [(4, 3)] * 2 + [(2,)] * 2 + [(7,), (8,)]
    return pl.pallas_call(
        gather_kernel,
        in_specs=[pl.BlockSpec(memory_space=pltpu.VMEM)] * 2,
        out_specs=[pl.BlockSpec(memory_space=pl.ANY), pl.BlockSpec(memory_space=pltpu.VMEM)],
        out_shape=[
            jax.ShapeDtypeStruct((2, 24, SIDE, PAIR), bf16),
            jax.ShapeDtypeStruct((16, D), f32),
        ],
        scratch_shapes=[
            pltpu.VMEM((3, SIDE, PAIR), bf16),
            pltpu.VMEM((16, 128), f32),
            pltpu.VMEM((8, 16, 128), f32),
        ]
        + [dma(size) for size in sizes]
        + [dma],
        compiler_params=params(collective_id=0, has_side_effects=True),
        name="gather",
    )(block_weights, vector_params)


def project_kernel(tok, pas, vec, wq, norm, q, k, v, cat):
    @pl.when(pl.program_id(0) == 0)
    def _():
        for x in range(3):
            for i in range(4):
                at = (i % 2) * SIDE
                parts = [wq[h, 2 * x + i // 2][:, at : at + SIDE] for h in range(2)]
                cat[x, i * SIDE : (i + 1) * SIDE, :] = jnp.concatenate(parts, axis=1)

    first = embedded(tok[...], pas[...], vec[...])
    hat, _ = hat_of(first)
    low = (hat * vec[PASSES : PASSES + 1] + vec[PASSES + 1 : PASSES + 2]).astype(bf16)
    norm[...] = low
    for x, out in enumerate((q, k, v)):
        out[...] = nn(low, cat[x]).astype(bf16)


def project(tokens, passes, vec, wq):
    seq = tokens.shape[0]
    row = lambda n: pl.BlockSpec((WIDE, n), lambda i: (i, 0))
    wide = jax.ShapeDtypeStruct((seq, PAIR), bf16)
    return pl.pallas_call(
        project_kernel,
        grid=(seq // WIDE,),
        in_specs=[
            row(D),
            pl.BlockSpec((1, WIDE), lambda i: (0, i)),
            full((16, D)),
            full((2, 6, SIDE, PAIR)),
        ],
        out_specs=[row(D), row(PAIR), row(PAIR), row(PAIR), full((3, D, PAIR))],
        out_shape=[
            jax.ShapeDtypeStruct((seq, D), bf16),
            wide,
            wide,
            wide,
            jax.ShapeDtypeStruct((3, D, PAIR), bf16),
        ],
        compiler_params=params(),
        cost_estimate=cost(16),
        name="project",
    )(tokens, passes, vec, wq)


def doc_state(lens, base):
    rows = base + lax.broadcasted_iota(jnp.int32, (1, ROWS), 1)
    rows = jnp.concatenate([rows, rows], axis=1)
    begin = jnp.int32(0)
    first = jnp.int32(0)
    starts = jnp.zeros((1, 2 * ROWS), jnp.int32)
    for c in range(DOCS):
        starts = jnp.where(rows >= begin, begin, starts)
        first = jnp.where(base >= begin, begin, first)
        begin = begin + lens[c]
    return rows, starts, first


def two_heads(block):
    left = lax.broadcasted_iota(jnp.int32, block.shape, 1) < HD
    none = jnp.zeros_like(block)
    return jnp.concatenate([jnp.where(left, block, none), jnp.where(left, none, block)], axis=0)


def one_above(both):
    return jnp.concatenate([both[:HD, :ROWS], both[HD:, ROWS:]], axis=0).T


def attend_kernel(lens, q, k, v, out, lse, acc):
    i = pl.program_id(0)
    base = i * ROWS
    rows, starts, first = doc_state(lens, base)
    pairs = [two_heads(q[:, p * 128 : (p + 1) * 128] * bf16(0.125)) for p in range(3)]
    for p in range(3):
        acc[p] = jnp.zeros((128, 2 * ROWS), f32)

    def step(j, carry):
        at = pl.multiple_of(j * ROWS, ROWS)
        keys = at + lax.broadcasted_iota(jnp.int32, (ROWS, 2 * ROWS), 0)
        seen = (keys >= starts) & (keys <= rows)
        here = pl.ds(at, ROWS)
        head = lambda p: slice(p * 128, (p + 1) * 128)
        scores = [jnp.where(seen, nt(k[here, head(p)], pairs[p]), masked_score) for p in range(3)]
        state = []
        for p in range(3):
            before, total = carry[2 * p], carry[2 * p + 1]
            now = jnp.maximum(before, jnp.max(scores[p], axis=0, keepdims=True))
            probs = jnp.exp(scores[p] - now)
            fade = jnp.exp(before - now)
            state += [now, total * fade + jnp.sum(probs, axis=0, keepdims=True)]
            acc[p] = acc[p] * fade + tn(v[here, head(p)], probs.astype(bf16))
        return tuple(state)

    zero = jnp.zeros((1, 2 * ROWS), f32)
    state = lax.fori_loop(first // ROWS, i + 1, step, (zero + masked_score, zero) * 3)
    lines = []
    for p in range(3):
        top, total = state[2 * p], state[2 * p + 1]
        out[:, p * 128 : (p + 1) * 128] = one_above(acc[p] / total).astype(bf16)
        line = top + jnp.log(total)
        lines += [line[:, :ROWS], line[:, ROWS:]]
    lse[...] = jnp.concatenate(lines + lines[:2], axis=0)


def attend(lens, q, k, v):
    seq = q.shape[0]
    row = pl.BlockSpec((ROWS, PAIR), lambda i, s: (i, 0))
    return pl.pallas_call(
        attend_kernel,
        grid_spec=pltpu.PrefetchScalarGridSpec(
            num_scalar_prefetch=1,
            grid=(seq // ROWS,),
            in_specs=[row, full((seq, PAIR)), full((seq, PAIR))],
            out_specs=[row, pl.BlockSpec((8, ROWS), lambda i, s: (0, i))],
            scratch_shapes=[
                pltpu.VMEM((3, 128, 2 * ROWS), f32),
            ],
        ),
        out_shape=[
            jax.ShapeDtypeStruct((seq, PAIR), bf16),
            jax.ShapeDtypeStruct((8, seq), f32),
        ],
        compiler_params=params(),
        cost_estimate=cost(30),
        name="attend",
    )(lens, q, k, v)


def attend_back_kernel(
    lens, q, k, v, mixed, lse, grad_mixed, dq, dk, dv, dk_acc, dv_acc, dq_acc
):
    i = pl.program_id(0)
    count = pl.num_programs(0)
    base = i * ROWS

    @pl.when(i == 0)
    def _():
        dk_acc[...] = jnp.zeros_like(dk_acc)
        dv_acc[...] = jnp.zeros_like(dv_acc)

    rows, starts, first = doc_state(lens, base)
    heads = lax.broadcasted_iota(jnp.int32, (8, 128), 0)
    lanes = lax.broadcasted_iota(jnp.int32, (8, 128), 1)
    pick = (lanes // HD == heads).astype(f32).astype(bf16)
    queries, grads, inner, lines = [], [], [], []
    for p in range(3):
        cols = slice(p * 128, (p + 1) * 128)
        queries.append(two_heads(q[:, cols] * bf16(0.125)))
        grads.append(two_heads(grad_mixed[:, cols]))
        product = grad_mixed[:, cols].astype(f32) * mixed[:, cols].astype(f32)
        high, low, _ = split_three(product)
        sums = nt(pick, high) + nt(pick, low)
        inner.append(jnp.concatenate([sums[0:1], sums[1:2]], axis=1))
        lines.append(jnp.concatenate([lse[2 * p : 2 * p + 1], lse[2 * p + 1 : 2 * p + 2]], axis=1))
        dq_acc[p] = jnp.zeros((128, 2 * ROWS), f32)

    def step(j, carry):
        at = pl.multiple_of(j * ROWS, ROWS)
        keys = at + lax.broadcasted_iota(jnp.int32, (ROWS, 2 * ROWS), 0)
        seen = (keys >= starts) & (keys <= rows)
        here = pl.ds(at, ROWS)
        for p in range(3):
            cols = slice(p * 128, (p + 1) * 128)
            kb = k[here, cols]
            scores = jnp.where(seen, nt(kb, queries[p]) - lines[p], masked_score)
            probs = jnp.exp(scores)
            grad_probs = nt(v[here, cols], grads[p])
            grad_scores = (probs * (grad_probs - inner[p])).astype(bf16)
            dv_acc[here, cols] += nn(probs.astype(bf16), grads[p])
            dk_acc[here, cols] += nn(grad_scores, queries[p])
            dq_acc[p] += tn(kb, grad_scores)
        return carry

    lax.fori_loop(first // ROWS, i + 1, step, 0)
    for p in range(3):
        dq[:, p * 128 : (p + 1) * 128] = (one_above(dq_acc[p]) * 0.125).astype(bf16)

    @pl.when(i == count - 1)
    def _():
        dk[...] = dk_acc[...].astype(bf16)
        dv[...] = dv_acc[...].astype(bf16)


def attend_back(lens, q, k, v, mixed, lse, grad_mixed):
    seq = q.shape[0]
    count = seq // ROWS
    row = pl.BlockSpec((ROWS, PAIR), lambda i, s: (i, 0))
    wide = jax.ShapeDtypeStruct((seq, PAIR), bf16)
    return pl.pallas_call(
        attend_back_kernel,
        grid_spec=pltpu.PrefetchScalarGridSpec(
            num_scalar_prefetch=1,
            grid=(count,),
            in_specs=[
                row,
                full((seq, PAIR)),
                full((seq, PAIR)),
                row,
                pl.BlockSpec((8, ROWS), lambda i, s: (0, i)),
                row,
            ],
            out_specs=[row, full((seq, PAIR)), full((seq, PAIR))],
            scratch_shapes=[
                pltpu.VMEM((seq, PAIR), f32),
                pltpu.VMEM((seq, PAIR), f32),
                pltpu.VMEM((3, 128, 2 * ROWS), f32),
            ],
        ),
        out_shape=[wide, wide, wide],
        compiler_params=params(),
        cost_estimate=cost(40),
        name="attend_back",
    )(lens, q, k, v, mixed, lse, grad_mixed)


def feed_kernel(
    small, tok, pas, vec, mine, other, cot, wo_mine, wo_other, w1, w2,
    out_chip, second_keep, grad_second, grad_mixed, sums, mid_send, mid_keep, *rest,
):
    results, rest = (rest[:4], rest[4:]) if small else (rest[:2], rest[2:])
    (
        wom, woo, up, down, gup, gdown, go, core_out, core_in, far_out, far_in, ga_out, ga_in, oc_out, oc_in, seconds,
        g_send, g_keep, g_in, s_core, r_core, s_far, r_far, s_ga, r_ga, s_oc, r_oc, s_x, r_x,
    ) = rest
    step = pl.program_id(0)
    half = core_out.shape[0]
    t, dp = lax.axis_index("tensor"), lax.axis_index("dp")
    core, side = t % 2, t // 2
    near, far = side * 2 + (1 - core), (1 - side) * 2 + core
    z, column = (dp // 2, dp % 2) if small else (0, 0)
    far_x = z * 2 + 1 - column

    def copy(src, dst, s_sem, r_sem, j, to):
        return pltpu.make_async_remote_copy(
            src_ref=src.at[j],
            dst_ref=dst.at[j],
            send_sem=s_sem.at[j],
            recv_sem=r_sem.at[j],
            device_id={"tensor": to},
            device_id_type=MESH,
        )

    core_copy = lambda j: copy(core_out, core_in, s_core, r_core, j, near)
    far_copy = lambda j: copy(far_out, far_in, s_far, r_far, j, far)
    ga_copy = lambda j: copy(ga_out, ga_in, s_ga, r_ga, j, near)
    oc_copy = lambda j: copy(oc_out, oc_in, s_oc, r_oc, j, near)

    def x_copy(slot):
        return pltpu.make_async_remote_copy(
            src_ref=g_send.at[slot],
            dst_ref=g_in.at[slot],
            send_sem=s_x.at[slot],
            recv_sem=r_x.at[slot],
            device_id={"dp": far_x},
            device_id_type=MESH,
        )

    barrier = pltpu.get_barrier_semaphore()

    @pl.when(step == 0)
    def _():
        for to in (near, far):
            pl.semaphore_signal(barrier, inc=1, device_id={"tensor": to}, device_id_type=MESH)
        if small:
            pl.semaphore_signal(barrier, inc=1, device_id={"dp": far_x}, device_id_type=MESH)
        for h in range(2):
            for m in range(2):
                rows, cols = slice(h * SIDE, (h + 1) * SIDE), slice(m * PAIR, (m + 1) * PAIR)
                wom[rows, cols] = wo_mine[h, m]
                woo[rows, cols] = wo_other[h, m]
        for r in range(4):
            for m in range(2):
                rows, cols = slice(r * SIDE, (r + 1) * SIDE), slice(m * PAIR, (m + 1) * PAIR)
                up[rows, cols] = w1[0, 2 * r + m]
                down[rows, cols] = w2[0, 2 * r + m]
        gup[...] = jnp.zeros_like(gup)
        gdown[...] = jnp.zeros_like(gdown)
        go[...] = jnp.zeros_like(go)
        sums[...] = jnp.zeros_like(sums)
        pl.semaphore_wait(barrier, 3 if small else 2)

    @pl.when(step < 2 * half)
    def _():
        j = step // 2
        owner = jnp.where(step % 2 == 0, 1 - core, core)
        here = pl.ds(pl.multiple_of((owner * half + j) * ROWS, ROWS), ROWS)
        first = embedded(tok[...], pas[...], vec[...])
        second = first + (nn(mine[here, :], wom[...]) + nn(other[...], woo[...]))
        hat, _ = hat_of(second)
        low = (hat * vec[PASSES + 2 : PASSES + 3] + vec[PASSES + 3 : PASSES + 4]).astype(bf16)
        upper = nn(low, up[...])
        square = upper * upper
        bent = jnp.tanh(gelu_coef * upper * (1.0 + 0.044715 * square))
        act = (0.5 * upper * (1.0 + bent)).astype(bf16)
        slope = 0.5 * (1.0 + bent) + (0.5 * gelu_coef) * upper * (1.0 - bent * bent) * (
            1.0 + (3 * 0.044715) * square
        )
        grad_act = nt(cot[...], down[...])
        grad_upper = (grad_act * slope).astype(bf16)
        part = nt(grad_upper, up[...])

        @pl.when(step % 2 == 0)
        def _():
            core_out[j] = part.astype(bf16)
            core_copy(j).start()

        @pl.when(step % 2 == 1)
        def _():
            core_copy(j).wait_recv()
            far_out[j] = (part + core_in[j].astype(f32)).astype(bf16)
            far_copy(j).start()
            second_keep[...] = second
            seconds[j] = second

        gup[...] += tn(low, grad_upper)
        gdown[...] += tn(act, cot[...])
        out_part = nn(act, down[...])

        @pl.when(step % 2 == 0)
        def _():
            oc_out[j] = out_part.astype(bf16)
            oc_copy(j).start()

        @pl.when(step % 2 == 1)
        def _():
            oc_copy(j).wait_recv()
            out_chip[...] = (out_part + oc_in[j].astype(f32)).astype(bf16)

    @pl.when(step == 2 * half - 1)
    def _():
        for r in range(4):
            for m in range(2):
                rows, cols = slice(r * SIDE, (r + 1) * SIDE), slice(m * PAIR, (m + 1) * PAIR)
                for at, total in ((8, gup), (16, gdown)):
                    pair = at + 2 * r + m
                    slot, place = (pair // 6 - 1) * 3 + pair % 3, pair // 3 % 2
                    value = total[rows, cols].astype(bf16)
                    kept, sent, n = (mid_keep, mid_send, slot) if slot < 3 else (g_keep, g_send, slot - 3)

                    @pl.when(column == place)
                    def _():
                        kept[n] = value

                    @pl.when(column != place)
                    def _():
                        sent[n] = value
        if small:
            for n in range(6):
                x_copy(n).start()

    def through_out(grad, block):
        here = pl.ds(pl.multiple_of(block * ROWS, ROWS), ROWS)
        grad_mixed[here, :] = nt(grad, wom[...]).astype(bf16)
        go[...] += tn(mine[here, :], grad)

    @pl.when((step >= 2 * half) & (step < 3 * half))
    def _():
        j = step - 2 * half
        hat, root = hat_of(seconds[j])
        far_copy(j).wait_recv()
        grad = far_out[j].astype(f32) + far_in[j].astype(f32)
        result = cot[...].astype(f32) + norm_back(hat, root, grad, vec[PASSES + 2 : PASSES + 3])
        low = result.astype(bf16)
        ga_out[j] = low
        ga_copy(j).start()
        grad_second[...] = result
        sums[0:1] += jnp.sum(grad * hat, axis=0, keepdims=True)
        sums[1:2] += jnp.sum(grad, axis=0, keepdims=True)
        through_out(low, core * half + j)

    @pl.when(step > 2 * half)
    def _():
        j = step - 2 * half - 1
        ga_copy(j).wait_recv()
        through_out(ga_in[j], (1 - core) * half + j)

    @pl.when(step == 3 * half)
    def _():
        at = pl.multiple_of(side * SIDE, SIDE)
        for m in range(2):
            value = go[pl.ds(at, SIDE), m * PAIR : (m + 1) * PAIR].astype(bf16)

            @pl.when(column == 0)
            def _():
                mid_keep[m] = value

            @pl.when(column != 0)
            def _():
                mid_send[m] = value

        for j in range(half):
            core_copy(j).wait_send()
            oc_copy(j).wait_send()
            far_copy(j).wait_send()
            ga_copy(j).wait_send()
        if small:
            for n in range(6):
                x_copy(n).wait_send()
                x_copy(n).wait_recv()
                value = (g_keep[n].astype(f32) + g_in[n].astype(f32)).astype(bf16)
                for turn in range(4):

                    @pl.when(lax.rem(z + turn, 4) == n // 3 + 2)
                    def _():
                        results[turn][n % 3] = value
        else:
            results[0][...] = g_send[...]
            results[1][...] = g_keep[...]


def feed(small, tokens, passes, vec, mine, other, cotangent, pairs, wo_other):
    seq = tokens.shape[0]
    half = seq // ROWS // 2

    def block(i):
        core = lax.axis_index("tensor") % 2
        work = jnp.minimum(i, 2 * half - 1)
        owner = jnp.where(work % 2 == 0, 1 - core, core)
        return owner * half + work // 2

    def cot_block(i):
        core = lax.axis_index("tensor") % 2
        return jnp.where(i < 2 * half, block(i), core * half + jnp.minimum(i - 2 * half, half - 1))

    side = lambda: lax.axis_index("tensor") // 2
    row = lambda n: pl.BlockSpec((ROWS, n), lambda i: (block(i), 0))
    keep = pl.BlockSpec((ROWS, D), lambda i: (jnp.minimum(i // 2, half - 1), 0))
    last = pl.BlockSpec((ROWS, D), lambda i: (jnp.clip(i - 2 * half, 0, half - 1), 0))
    rows = lambda kind: jax.ShapeDtypeStruct((seq // 2, D), kind)
    gr = lambda n: jax.ShapeDtypeStruct((n, SIDE, PAIR), bf16)
    ends = [(3, SIDE, PAIR)] * 4 if small else [(6, SIDE, PAIR)] * 2
    buffer = pltpu.VMEM((half, ROWS, D), bf16)
    dma = pltpu.SemaphoreType.DMA((half,))
    return pl.pallas_call(
        functools.partial(feed_kernel, small),
        grid=(3 * half + 1,),
        in_specs=[
            row(D),
            pl.BlockSpec((1, ROWS), lambda i: (0, block(i))),
            full((16, D)),
            full((seq, PAIR)),
            row(PAIR),
            pl.BlockSpec((ROWS, D), lambda i: (cot_block(i), 0)),
            pl.BlockSpec((2, 2, SIDE, PAIR), lambda i: (0, 3, 0, 0)),
            full(wo_other.shape),
            pl.BlockSpec((1, 8, SIDE, PAIR), lambda i: (side(), 1, 0, 0)),
            pl.BlockSpec((1, 8, SIDE, PAIR), lambda i: (side(), 2, 0, 0)),
        ],
        out_specs=[
            keep,
            keep,
            last,
            full((seq, PAIR)),
            full((8, D)),
            full((3, SIDE, PAIR)),
            full((3, SIDE, PAIR)),
        ]
        + [full(shape) for shape in ends],
        scratch_shapes=[
            pltpu.VMEM((PAIR, D), bf16),
            pltpu.VMEM((PAIR, D), bf16),
            pltpu.VMEM((D, D), bf16),
            pltpu.VMEM((D, D), bf16),
            pltpu.VMEM((D, D), f32),
            pltpu.VMEM((D, D), f32),
            pltpu.VMEM((PAIR, D), f32),
        ]
        + [buffer] * 8
        + [pltpu.VMEM((half, ROWS, D), f32)]
        + [pltpu.VMEM((6, SIDE, PAIR), bf16)] * 3
        + [dma] * 8
        + [pltpu.SemaphoreType.DMA((6,))] * 2,
        out_shape=[
            rows(bf16),
            rows(f32),
            rows(f32),
            jax.ShapeDtypeStruct((seq, PAIR), bf16),
            jax.ShapeDtypeStruct((8, D), f32),
            gr(3),
            gr(3),
        ]
        + [jax.ShapeDtypeStruct(shape, bf16) for shape in ends],
        compiler_params=params(collective_id=1, has_side_effects=True),
        cost_estimate=cost(50),
        name="feed_forward",
    )(tokens, passes, vec, mine, other, cotangent, pairs, wo_other, pairs, pairs)


def qkv_grads_kernel(place, norm, dq, dk, dv, mid_send, mid_keep, g_send, g_keep, acc):
    i = pl.program_id(0)

    @pl.when(i == 0)
    def _():
        acc[...] = jnp.zeros_like(acc)

    mine = [jnp.where(place[1] == 0, grad[:, :SIDE], grad[:, SIDE:]) for grad in (dq, dk, dv)]
    acc[...] += tn(jnp.concatenate(mine, axis=1), norm[...])

    @pl.when(i == pl.num_programs(0) - 1)
    def _():
        for m in range(3):
            g_send[3 + m] = mid_send[m]
            g_keep[3 + m] = mid_keep[m]
        for x in range(3):
            for m in range(2):
                value = acc[x * SIDE : (x + 1) * SIDE, m * PAIR : (m + 1) * PAIR].astype(bf16)
                slot, column = (2 * x + m) % 3, (2 * x + m) // 3

                @pl.when(place[2] == column)
                def _():
                    g_keep[slot] = value

                @pl.when(place[2] != column)
                def _():
                    g_send[slot] = value


def qkv_grads(place, norm, dq, dk, dv, mid_send, mid_keep):
    seq = norm.shape[0]
    row = lambda n: pl.BlockSpec((WIDE, n), lambda i, s: (i, 0))
    return pl.pallas_call(
        qkv_grads_kernel,
        grid_spec=pltpu.PrefetchScalarGridSpec(
            num_scalar_prefetch=1,
            grid=(seq // WIDE,),
            in_specs=[row(D), row(PAIR), row(PAIR), row(PAIR)] + [full((3, SIDE, PAIR))] * 2,
            out_specs=[full((6, SIDE, PAIR)), full((6, SIDE, PAIR))],
            scratch_shapes=[pltpu.VMEM((3 * SIDE, D), f32)],
        ),
        out_shape=[jax.ShapeDtypeStruct((6, SIDE, PAIR), bf16)] * 2,
        compiler_params=params(),
        cost_estimate=cost(8),
        name="qkv_grads",
    )(place, norm, dq, dk, dv, mid_send, mid_keep)


CHUNK = SIDE // 2
CHUNKS = 12


def last_kernel(small, dq, dk, dv, cat, tok, pas, vec, grad_second, sums_two, g_send, g_keep, low, *rest):
    if small:
        late, vec_sum = rest[:2]
        rest = rest[2:]
        (
            core_out, core_in, sums, core_sums, x_in, z_in, z_out, up_in, v_out, v_in,
            s_core, r_core, s_sum, r_sum, s_x, r_x, s_z, r_z, s_up, r_up, s_v, r_v,
        ) = rest
    else:
        vec_sum, core_out, core_in, sums, core_sums, s_core, r_core, s_sum, r_sum = rest
    i = pl.program_id(0)
    half = core_out.shape[0]
    t, dp = lax.axis_index("tensor"), lax.axis_index("dp")
    core, side = t % 2, t // 2
    near = side * 2 + (1 - core)
    z, column = (dp // 2, dp % 2) if small else (0, 0)
    far_x = z * 2 + 1 - column
    peers = [lax.rem(dp + k, 8) for k in range(1, 8)]

    def copy(src, dst, s_sem, r_sem, to):
        return pltpu.make_async_remote_copy(
            src_ref=src, dst_ref=dst, send_sem=s_sem, recv_sem=r_sem, device_id=to, device_id_type=MESH
        )

    core_copy = lambda j: copy(core_out.at[j], core_in.at[j], s_core.at[j], r_core.at[j], {"tensor": near})
    sum_copy = lambda: copy(sums, core_sums, s_sum, r_sum, {"tensor": near})

    def part_of(ref, k):
        return ref.at[k // 2, pl.ds((k % 2) * CHUNK, CHUNK)]

    x_copy = lambda k: copy(part_of(g_send, k), x_in.at[k], s_x.at[k], r_x.at[k], {"dp": far_x})
    z_copy = lambda k: copy(z_out.at[k], z_in.at[k], s_z.at[k], r_z.at[k], {"dp": dp - 2})
    up_copy = lambda k: copy(z_out.at[k], up_in.at[k - 6], s_up.at[k - 6], r_up.at[k - 6], {"dp": dp + 2})
    v_copy = lambda n: copy(v_out.at[peers[n]], v_in.at[dp], s_v.at[n], r_v.at[dp], {"dp": peers[n]})
    barrier = pltpu.get_barrier_semaphore()

    @pl.when(i == 0)
    def _():
        pl.semaphore_signal(barrier, inc=1, device_id={"tensor": near}, device_id_type=MESH)
        if small:
            for peer in peers:
                pl.semaphore_signal(barrier, inc=1, device_id={"dp": peer}, device_id_type=MESH)
            late[...] = jnp.zeros_like(late)
        sums[...] = jnp.zeros_like(sums)
        sums[PASSES + 2 : PASSES + 4] = sums_two[0:2]
        pl.semaphore_wait(barrier, 8 if small else 1)
        if small:
            for k in range(CHUNKS):
                x_copy(k).start()

    @pl.when(i < 2 * half)
    def _():
        part = nt(dq[...], cat[0]) + nt(dk[...], cat[1]) + nt(dv[...], cat[2])

        @pl.when(i < half)
        def _():
            core_out[i] = part.astype(bf16)
            core_copy(i).start()

        @pl.when(i >= half)
        def _():
            j = i - half
            hat, root = hat_of(embedded(tok[...], pas[...], vec[...]))
            core_copy(j).wait_recv()
            grad = part + core_in[j].astype(f32)
            result = grad_second[...] + norm_back(hat, root, grad, vec[PASSES : PASSES + 1])
            low[...] = result.astype(bf16)
            chosen = one_hot(pas[...])
            high, mid, _ = split_three(result)
            sums[...] += nn(chosen, high) + nn(chosen, mid)
            sums[PASSES : PASSES + 1] += jnp.sum(grad * hat, axis=0, keepdims=True)
            sums[PASSES + 1 : PASSES + 2] += jnp.sum(grad, axis=0, keepdims=True)

    @pl.when(i == 2 * half - 1)
    def _():
        sum_copy().start()

    if small:

        def term_of(k):
            x_copy(k).wait_recv()
            keep = g_keep[k // 2, pl.ds(pl.multiple_of((k % 2) * CHUNK, 16), CHUNK), :]
            return keep.astype(f32) + x_in[k].astype(f32)

        def keep_late(k, pair, total):
            late[pair, pl.ds(pl.multiple_of((k % 2) * CHUNK, 16), CHUNK), :] = total

        k = i - 1 - (3 - z)

        @pl.when((k >= 0) & (k < CHUNKS) & ((z > 0) | (k < 6)))
        def _():
            total = term_of(k)

            @pl.when(z < 3)
            def _():
                z_copy(k).wait_recv()

            below = jnp.where(z < 3, z_in[k].astype(f32), 0.0)
            passed = total + below

            @pl.when((z > 1) | ((z == 1) & (k < 6)))
            def _():
                z_out[k] = passed.astype(bf16)
                z_copy(k).start()

            @pl.when(z == 0)
            def _():
                keep_late(k, k // 2, passed)

            @pl.when((z == 1) & (k >= 6))
            def _():
                up_copy(k).wait_recv()
                keep_late(k, k // 2 - 3, passed + up_in[k - 6].astype(f32))

        @pl.when((i >= 7) & (i < 13) & (z == 0))
        def _():
            z_out[i - 1] = term_of(i - 1).astype(bf16)
            up_copy(i - 1).start()

    @pl.when(i == 2 * half + 1)
    def _():
        sum_copy().wait_recv()
        total = sums[...] + core_sums[...]
        if small:
            wide = D // 8
            for d in range(8):
                v_out[d, :, 0:wide] = total[:, d * wide : (d + 1) * wide]
                v_out[d, :, wide:] = jnp.zeros((16, 128 - wide), f32)
            for n in range(7):
                v_copy(n).start()
        else:
            vec_sum[...] = total

    @pl.when(i == pl.num_programs(0) - 1)
    def _():
        for j in range(half):
            core_copy(j).wait_send()
        sum_copy().wait_send()
        if small:
            for peer in peers:
                copy(v_out.at[0], v_in.at[peer], s_v.at[0], r_v.at[peer], {"dp": far_x}).wait_recv()
            v_in[dp] = v_out[dp]
            total = v_in[0]
            for d in range(1, 8):
                total = total + v_in[d]
            vec_sum[...] = total
            for n in range(7):
                v_copy(n).wait_send()
            for k in range(CHUNKS):
                x_copy(k).wait_send()
                if k < 6:
                    pl.when(z > 0)(z_copy(k).wait_send)
                else:
                    pl.when(z > 1)(z_copy(k).wait_send)
                    pl.when(z == 0)(up_copy(k).wait_send)


def last(small, dq, dk, dv, cat, tokens, passes, vec, grad_second, sums_two, g_send, g_keep):
    seq = dq.shape[0]
    half = seq // ROWS // 2
    core = lambda: lax.axis_index("tensor") % 2

    def block(i):
        work = jnp.minimum(i, 2 * half - 1)
        return lax.rem(work + (1 - core()) * half, 2 * half)

    own = lambda i: jnp.clip(i - half, 0, half - 1)
    row = pl.BlockSpec((ROWS, PAIR), lambda i: (block(i), 0))
    mine = pl.BlockSpec((ROWS, D), lambda i: (own(i), 0))
    dma = pltpu.SemaphoreType.DMA
    out_specs = [mine]
    out_shape = [jax.ShapeDtypeStruct((seq // 2, D), bf16)]
    scratch = [
        pltpu.VMEM((half, ROWS, D), bf16),
        pltpu.VMEM((half, ROWS, D), bf16),
        pltpu.VMEM((16, D), f32),
        pltpu.VMEM((16, D), f32),
    ]
    sems = [dma((half,)), dma((half,)), dma, dma]
    if small:
        out_specs += [full((3, SIDE, PAIR)), full((16, 128))]
        out_shape += [
            jax.ShapeDtypeStruct((3, SIDE, PAIR), f32),
            jax.ShapeDtypeStruct((16, 128), f32),
        ]
        scratch += [pltpu.VMEM((CHUNKS, CHUNK, PAIR), bf16)] * 3
        scratch += [pltpu.VMEM((6, CHUNK, PAIR), bf16)]
        scratch += [pltpu.VMEM((8, 16, 128), f32)] * 2
        sems += [dma((CHUNKS,))] * 4 + [dma((6,))] * 2 + [dma((7,)), dma((8,))]
    else:
        out_specs += [full((16, D))]
        out_shape += [jax.ShapeDtypeStruct((16, D), f32)]
    return pl.pallas_call(
        functools.partial(last_kernel, small),
        grid=(2 * half + 7 if small else 2 * half + 2,),
        in_specs=[
            row,
            row,
            row,
            full(cat.shape),
            pl.BlockSpec((ROWS, D), lambda i: (core() * half + own(i), 0)),
            pl.BlockSpec((1, ROWS), lambda i: (0, core() * half + own(i))),
            full((16, D)),
            mine,
            full((8, D)),
            full(g_send.shape),
            full(g_keep.shape),
        ],
        out_specs=out_specs,
        out_shape=out_shape,
        scratch_shapes=scratch + sems,
        compiler_params=params(collective_id=2, has_side_effects=True),
        cost_estimate=cost(30),
        name="last",
    )(dq, dk, dv, cat, tokens, passes, vec, grad_second, sums_two, g_send, g_keep)


def precondition(grad, weight, left, right, left_root, right_root):
    high = lax.Precision.HIGHEST
    left_new = decay * left + (1.0 - decay) * jnp.einsum(
        "...ij,...kj->...ik", grad, grad, precision=high
    )
    right_new = decay * right + (1.0 - decay) * jnp.einsum(
        "...ji,...jk->...ik", grad, grad, precision=high
    )
    half = jnp.einsum("...ij,...jk->...ik", left_root, grad, precision=high)
    step = jnp.einsum("...ij,...jk->...ik", half, right_root, precision=high)
    return (left_new, right_new, step, weight - rate_matrix * step)


def two_part(value):
    high = value.astype(bf16)
    return high, (value - high.astype(f32)).astype(bf16)


def dot_three(dot, a, b):
    return dot(a[0], b[0]) + (dot(a[0], b[1]) + dot(a[1], b[0]))


def renew_kernel(place, late, own, one, two, three, weight, left, right, left_root, right_root, left_new, right_new, step, new):
    early = own[0].astype(f32) + one[0].astype(f32) + two[0].astype(f32) + three[0].astype(f32)
    z = place[3]
    both = late[0] + jnp.where(z > 1, early, 0.0)
    for n in range(2):
        grad = both[:, n * SIDE : (n + 1) * SIDE]
        grad = two_part(jnp.where(z == 0, grad.T, grad))
        left_new[0, n] = decay * left[0, n] + (1.0 - decay) * dot_three(nt, grad, grad)
        right_new[0, n] = decay * right[0, n] + (1.0 - decay) * dot_three(tn, grad, grad)
        half = dot_three(nn, two_part(left_root[0, n]), grad)
        value = dot_three(nn, two_part(half), two_part(right_root[0, n]))
        step[0, n] = value
        new[0, n] = weight[0, n] - rate_matrix * value


def renew(place, late, own, far, weight, left, right, left_root, right_root):
    pair = pl.BlockSpec((1, SIDE, PAIR), lambda i, s: (i, 0, 0))
    slot = pl.BlockSpec((1, 2, SIDE, SIDE), lambda i, s: (0, i, 0, 0))
    return pl.pallas_call(
        renew_kernel,
        grid_spec=pltpu.PrefetchScalarGridSpec(
            num_scalar_prefetch=1,
            grid=(3,),
            in_specs=[pair] * 5 + [slot] * 5,
            out_specs=[slot] * 4,
        ),
        out_shape=[jax.ShapeDtypeStruct(weight.shape, f32)] * 4,
        compiler_params=params(),
        cost_estimate=cost(5),
        name="renew",
    )(place, late, own, *far, weight, left, right, left_root, right_root)


def to_pairs(blocks):
    n = blocks.shape[0] // 2
    return blocks.reshape(n, 2, SIDE, SIDE).transpose(0, 2, 1, 3).reshape(n, SIDE, PAIR)


def from_pairs(pairs):
    n = pairs.shape[0]
    return pairs.reshape(n, SIDE, 2, SIDE).transpose(0, 2, 1, 3).reshape(2 * n, SIDE, SIDE)


def swap(value, bit):
    return lax.ppermute(value, "tensor", [(t, t ^ bit) for t in range(NT)])


def hop_z(value, turn, ends):
    pairs = [(d, (d + 2 * turn) % 8) for d in range(8) if (d // 2 + turn) % 4 in ends]
    return lax.ppermute(value, "dp", pairs)


def tie(*values):
    return lax.optimization_barrier(values)


def on_device(
    tokens,
    pass_ids,
    doc_lengths,
    cotangent,
    block_weights,
    vector_params,
    vector_moment,
    block_left,
    block_right,
    block_left_root,
    block_right_root,
):
    t, dp = lax.axis_index("tensor"), lax.axis_index("dp")
    core, side = t % 2, t // 2
    n_dp = lax.axis_size("dp")
    small = n_dp == 8
    z, column = (dp // 2, dp % 2) if small else (0, 0)
    place = jnp.stack([core, side, jnp.asarray(column), jnp.asarray(z)]).astype(jnp.int32)
    lens = doc_lengths[0]
    seq = tokens.shape[0]
    passes = pass_ids.reshape(1, seq)
    total_blocks = (D // SIDE) * (4 + 2 * (FF // D))
    slots = block_weights.shape[1] * n_dp

    if small:
        pairs, vec = gather(block_weights, vector_params)
    else:
        every = lax.all_gather(block_weights.astype(bf16), "dp", axis=1, tiled=True)[0]
        near = to_pairs(every[:total_blocks])
        far = swap(near, 2)
        pairs = jnp.where(side == 0, jnp.stack([near, far]), jnp.stack([far, near]))
        vec = lax.all_gather(vector_params, "dp", axis=1, tiled=True)
        vec = jnp.pad(vec, ((0, 16 - vec.shape[0]), (0, 0)))
    wo_other = swap(pairs[:, 6:8], 1)

    norm, q, k, v, cat = project(tokens, passes, vec, pairs)
    mine, lse = attend(lens, q, k, v)
    other = swap(mine, 1)
    out_chip, second, grad_second, grad_mixed, sums_two, mid_send, mid_keep, *ends = feed(
        small, tokens, passes, vec, mine, other, cotangent, pairs, wo_other
    )
    out_far = swap(out_chip, 2)
    if small:
        far = [hop_z(ends[turn], turn, (2, 3)) for turn in (1, 2, 3)]
    dq, dk, dv = attend_back(lens, q, k, v, mine, lse, grad_mixed)
    g_send, g_keep = qkv_grads(place, norm, dq, dk, dv, mid_send, mid_keep)
    if small:
        *far, out_far, g_send = tie(*far, out_far, g_send)
    low_half, *sums = last(
        small, dq, dk, dv, cat, tokens, passes, vec, grad_second, sums_two, g_send, g_keep
    )
    out_half = (second + (out_chip.astype(f32) + out_far.astype(f32))).astype(bf16)

    def join(half):
        far = swap(half, 1)
        low = jnp.where(core == 0, half, far)
        high = jnp.where(core == 0, far, half)
        return jnp.concatenate([low, high], axis=0)

    output, input_grad = join(out_half), join(low_half)
    if small:
        late, vector_sum = sums
        left_new, right_new, step, weight_new = renew(
            place, late, ends[0], far, block_weights, block_left, block_right, block_left_root, block_right_root
        )
        vector_grad = vector_sum[: PASSES + 4, : vector_params.shape[1]]
    else:
        vector_part = sums[0][: PASSES + 4]
        send, keep = ends
        rest = jnp.stack(
            [
                jnp.concatenate([mid_keep, keep]).reshape(3, 3, SIDE, PAIR),
                jnp.concatenate([mid_send, send]).reshape(3, 3, SIDE, PAIR),
            ],
            axis=1,
        )
        grad_qkv = from_pairs(jnp.concatenate([g_keep[:3], g_send[:3]], axis=0)).swapaxes(1, 2)
        grad_rest = from_pairs(rest.reshape(18, SIDE, PAIR))
        spare = jnp.zeros((slots - total_blocks, SIDE, SIDE), bf16)
        grad_blocks = jnp.concatenate([grad_qkv, grad_rest, spare], axis=0)[None].astype(f32)
        owned = lax.psum_scatter(grad_blocks, "dp", scatter_dimension=1, tiled=True)
        vector_grad = lax.psum_scatter(vector_part, "dp", scatter_dimension=1, tiled=True)
        left_new, right_new, step, weight_new = precondition(
            owned, block_weights, block_left, block_right, block_left_root, block_right_root
        )
    moment_new = decay * vector_moment + (1.0 - decay) * vector_grad * vector_grad
    vector_new = vector_params - rate_vector * vector_grad / (jnp.sqrt(moment_new) + moment_eps)
    return (
        output,
        input_grad,
        left_new,
        right_new,
        step,
        weight_new,
        vector_grad,
        moment_new,
        vector_new,
    )


def solution(mesh):
    rows, line = P("dp", None), P(None, "dp")
    block = P("tensor", "dp", None, None)
    return jax.shard_map(
        on_device,
        mesh=mesh,
        in_specs=(rows, P("dp"), rows, rows, block, line, line, block, block, block, block),
        out_specs=(rows, rows, block, block, block, block, line, line, line),
        check_vma=False,
    )
```

```python
import functools

import jax
import jax.numpy as jnp
from jax import lax
from jax.experimental import pallas as pl
from jax.experimental.pallas import tpu as pltpu
from jax.sharding import PartitionSpec as P

D = 768
HD = 64
FF = 3072
PASSES = 5
SIDE = 192
PAIR = 2 * SIDE
ROWS = 256
WIDE = 512
DOCS = 8
NT = 4

norm_eps = 1e-05
moment_eps = 1e-08
rate_matrix = 0.03
rate_vector = 0.2
decay = 0.5
gelu_coef = 0.7978845608028654
masked_score = -1e30
f32 = jnp.float32
bf16 = jnp.bfloat16
MESH = pl.DeviceIdType.MESH
VMEM_LIMIT = 56 * 1024 * 1024


def nn(a, b):
    return lax.dot_general(a, b, (((1,), (0,)), ((), ())), preferred_element_type=f32)


def nt(a, b):
    return lax.dot_general(a, b, (((1,), (1,)), ((), ())), preferred_element_type=f32)


def tn(a, b):
    return lax.dot_general(a, b, (((0,), (0,)), ((), ())), preferred_element_type=f32)


def split_three(value):
    high = value.astype(bf16)
    rest = value - high.astype(f32)
    mid = rest.astype(bf16)
    return high, mid, (rest - mid.astype(f32)).astype(bf16)


def one_hot(pass_row):
    kinds = lax.broadcasted_iota(jnp.int32, (16, pass_row.shape[1]), 0)
    return (kinds == pass_row).astype(f32).astype(bf16)


def embedded(tokens, pass_row, vec):
    chosen = jnp.concatenate([one_hot(pass_row)] * 3, axis=0)
    return tokens.astype(f32) + tn(chosen, jnp.concatenate(split_three(vec), axis=0))


def hat_of(hidden):
    mean = jnp.mean(hidden, axis=-1, keepdims=True)
    center = hidden - mean
    spread = jnp.mean(center * center, axis=-1, keepdims=True)
    root = lax.rsqrt(spread + norm_eps)
    return center * root, root


def norm_back(hat, root, grad, gain):
    scaled = grad * gain
    first = jnp.mean(scaled, axis=-1, keepdims=True)
    second = jnp.mean(scaled * hat, axis=-1, keepdims=True)
    return root * (scaled - first - hat * second)


def params(**kw):
    return pltpu.CompilerParams(vmem_limit_bytes=VMEM_LIMIT, **kw)


def cost(micros):
    return pl.CostEstimate(flops=int(micros * 1.1e9), bytes_accessed=int(micros * 1e6), transcendentals=0)


def full(shape):
    return pl.BlockSpec(shape, lambda *_: (0,) * len(shape))


def gather_kernel(
    own, vec_own, tokens, passes,
    all_pairs, wo_other, vec_out, norm, q, k_out, v, cat,
    pack, vec_pack, vec_land, wq, tok, norm_s, qkv_s, cat_s, *sems,
):
    (
        s_z1, r_z1, s_x1, r_x1, s_y1, r_y1, s_d1, r_d1, s_l, r_l, s_r, r_r, s_x2, r_x2, s_y2, r_y2, s_v, r_v, s_c, r_c,
        s_out, s_cat, s_tok, loc,
    ) = sems
    dp, t = lax.axis_index("dp"), lax.axis_index("tensor")
    z, x = dp // 2, dp % 2
    y, core = t // 2, t % 2
    far_x, far_y, near = z * 2 + (1 - x), (1 - y) * 2 + core, y * 2 + (1 - core)

    barrier = pltpu.get_barrier_semaphore()
    peers = [lax.rem(dp + n, 8) for n in range(1, 8)]
    for peer in peers:
        pl.semaphore_signal(barrier, inc=1, device_id={"dp": peer}, device_id_type=MESH)
    for to in (far_y, near):
        pl.semaphore_signal(barrier, inc=1, device_id={"tensor": to}, device_id_type=MESH)

    tok_copy = pltpu.make_async_copy(tokens, tok, s_tok)
    tok_copy.start()
    for m in range(3):
        pair = jnp.concatenate([own[0, 2 * m], own[0, 2 * m + 1]], axis=1).astype(bf16)
        pack[m] = pair

        @pl.when(z == 0)
        def _():
            wq[y, 3 * x + m] = pair

    vec_pack[...] = jnp.zeros_like(vec_pack)
    vec_pack[0 : PASSES + 4, 0 : D // 8] = vec_own[...]
    pl.semaphore_wait(barrier, 9)

    started = []

    def send(src, dst, s_sem, r_sem, to, cond=None):
        copy = pltpu.make_async_remote_copy(
            src_ref=src, dst_ref=dst, send_sem=s_sem, recv_sem=r_sem, device_id=to, device_id_type=MESH
        )
        started.append((cond, copy))
        if cond is None:
            copy.start()
        else:
            pl.when(cond)(copy.start)

    def arrived(dst, r_sem, cond=None):
        copy = pltpu.make_async_remote_copy(
            src_ref=dst, dst_ref=dst, send_sem=loc, recv_sem=r_sem, device_id={"dp": far_x}, device_id_type=MESH
        )
        if cond is None:
            copy.wait_recv()
        else:
            pl.when(cond)(copy.wait_recv)

    to_x, to_y, to_left, to_right = {"dp": far_x}, {"tensor": far_y}, {"dp": dp - 2}, {"dp": dp + 2}
    half = SIDE // 2

    def piece(side, column, k):
        return wq.at[side, 3 * column + k // 2, pl.ds((k % 2) * half, half)]

    def at_z(d, m):
        return all_pairs.at[y, 3 * dp + 6 * d + m]

    own_copy = pltpu.make_async_copy(pack, all_pairs.at[y, pl.ds(3 * dp, 3)], loc)
    pl.when(z > 0)(own_copy.start)

    for m in range(3):
        send(pack.at[m], at_z(0, m), s_l.at[0, m], r_l.at[0, m], to_left, z > 0)
    for n, peer in enumerate(peers):
        send(vec_pack, vec_land.at[dp], s_v.at[n], r_v.at[dp], {"dp": peer})
    for m in range(3):
        send(pack.at[m], at_z(0, m), s_x2.at[z, m], r_x2.at[z, m], to_x, z > m)

    def diagonal(k):
        arrived(piece(y, 1 - x, k), r_x1.at[k])
        send(piece(y, 1 - x, k), piece(y, 1 - x, k), s_d1.at[k], r_d1.at[k], to_y)

    def from_right(d, m):
        arrived(at_z(d, m), r_l.at[d - 1, m], z + d < 4)
        if d < 3:
            send(at_z(d, m), at_z(d, m), s_l.at[d, m], r_l.at[d, m], to_left, (z + d < 4) & (z > 0))

    def from_left(d, m):
        arrived(at_z(-d, m), r_r.at[d - 1, m], z - d > 0)
        if d == 1:
            send(at_z(-d, m), at_z(-d, m), s_r.at[1, m], r_r.at[1, m], to_right, (z - d > 0) & (z < 3))

    def along_x(d, m, cond):
        send(at_z(d, m), at_z(d, m), s_x2.at[z + d, m], r_x2.at[z + d, m], to_x, cond)

    for k in range(6):
        arrived(piece(y, x, k), r_z1.at[k], z > 0)
        send(piece(y, x, k), piece(y, x, k), s_z1.at[k], r_z1.at[k], to_right, z < 3)
        send(piece(y, x, k), piece(y, x, k), s_x1.at[k], r_x1.at[k], to_x)
        send(piece(y, x, k), piece(y, x, k), s_y1.at[k], r_y1.at[k], to_y)
        if k == 5:
            for m in range(3):
                send(pack.at[m], at_z(0, m), s_r.at[0, m], r_r.at[0, m], to_right, (z > 0) & (z < 3))
                send(pack.at[m], at_z(0, m), s_x2.at[z, m], r_x2.at[z, m], to_x, (z > 0) & (z <= m))
        if k >= 1:
            diagonal(k - 1)
        if k % 2 == 1:
            from_right(1, k // 2)
    diagonal(5)
    pl.when(z > 0)(own_copy.wait)
    for m in range(3):
        along_x(1, m, z + 1 < 4)
    for m in range(3):
        from_right(2, m)
    for k in range(6):
        arrived(piece(1 - y, x, k), r_y1.at[k])
        arrived(piece(1 - y, 1 - x, k), r_d1.at[k])
    for peer in peers:
        arrived(vec_land.at[peer], r_v.at[peer])
    vec_land[dp] = vec_pack[...]
    vec = jnp.concatenate([vec_land[d][:, : D // 8] for d in range(8)], axis=1)
    vec_out[...] = vec
    for n in range(3):
        for i in range(4):
            at = (i % 2) * SIDE
            parts = [wq[h, 2 * n + i // 2][:, at : at + SIDE] for h in range(2)]
            cat_s[n, i * SIDE : (i + 1) * SIDE, :] = jnp.concatenate(parts, axis=1)
    writes = [pltpu.make_async_copy(cat_s, cat, s_cat)]
    writes[0].start()
    tok_copy.wait()

    def rows_of(b):
        rows = slice(b * WIDE, (b + 1) * WIDE)
        hat, _ = hat_of(embedded(tok[rows, :], passes[:, rows], vec))
        low = (hat * vec[PASSES : PASSES + 1] + vec[PASSES + 1 : PASSES + 2]).astype(bf16)
        norm_s[rows, :] = low
        writes.append(pltpu.make_async_copy(norm_s.at[rows, :], norm.at[rows, :], s_out.at[b, 3]))
        writes[-1].start()
        for n, out in enumerate((q, k_out, v)):
            qkv_s[n, rows, :] = nn(low, cat_s[n]).astype(bf16)
            writes.append(pltpu.make_async_copy(qkv_s.at[n, rows, :], out.at[rows, :], s_out.at[b, n]))
            writes[-1].start()

    count = tok.shape[0] // WIDE
    for b in range(count):
        rows_of(b)
        if b == 0:
            for m in range(3):
                from_left(1, m)
                along_x(-1, m, z - 1 > 0)
                along_x(2, m, z + 2 < 4)
        if b == 1:
            for m in range(3):
                from_right(3, m)
                along_x(3, m, z + 3 < 4)
        if b == 2:
            for m in range(3):
                from_left(2, m)
                along_x(-2, m, z - 2 > 0)
        if b == 3:
            for m in range(2):
                ref = all_pairs.at[y, 6 + m]
                arrived(ref, r_x2.at[1, m], x == 1)
                send(ref, ref, s_y2.at[m], r_y2.at[m], to_y)
                send(ref, wo_other.at[y, m], s_c.at[0, m], r_c.at[y, m], {"tensor": near})
    for m in range(2):
        ref = all_pairs.at[1 - y, 6 + m]
        arrived(ref, r_y2.at[m])
        send(ref, wo_other.at[1 - y, m], s_c.at[1, m], r_c.at[1 - y, m], {"tensor": near})
    for w in range(1, 4):
        for m in range(3):
            ref = all_pairs.at[y, 6 * w + 3 * (1 - x) + m]
            if w == 1 and m < 2:
                arrived(ref, r_x2.at[w, m], x == 0)
            else:
                arrived(ref, r_x2.at[w, m])
    for h in range(2):
        for m in range(2):
            arrived(wo_other.at[h, m], r_c.at[h, m])
    for copy in writes:
        copy.wait()
    for cond, copy in started:
        if cond is None:
            copy.wait_send()
        else:
            pl.when(cond)(copy.wait_send)


def gather(block_weights, vector_params, tokens, passes):
    seq = tokens.shape[0]
    dma = pltpu.SemaphoreType.DMA
    sizes = [(6,)] * 8 + [(3, 3)] * 2 + [(2, 3)] * 2 + [(4, 3)] * 2 + [(2,)] * 2 + [(7,), (8,)] + [(2, 2)] * 2
    sizes += [(seq // WIDE, 4)]
    vmem, far = pl.BlockSpec(memory_space=pltpu.VMEM), pl.BlockSpec(memory_space=pl.ANY)
    wide = jax.ShapeDtypeStruct((seq, PAIR), bf16)
    return pl.pallas_call(
        gather_kernel,
        in_specs=[vmem, vmem, far, vmem],
        out_specs=[far, far, vmem, far, far, far, far, far],
        out_shape=[
            jax.ShapeDtypeStruct((2, 24, SIDE, PAIR), bf16),
            jax.ShapeDtypeStruct((2, 2, SIDE, PAIR), bf16),
            jax.ShapeDtypeStruct((16, D), f32),
            jax.ShapeDtypeStruct((seq, D), bf16),
            wide,
            wide,
            wide,
            jax.ShapeDtypeStruct((3, D, PAIR), bf16),
        ],
        scratch_shapes=[
            pltpu.VMEM((3, SIDE, PAIR), bf16),
            pltpu.VMEM((16, 128), f32),
            pltpu.VMEM((8, 16, 128), f32),
            pltpu.VMEM((2, 6, SIDE, PAIR), bf16),
            pltpu.VMEM((seq, D), bf16),
            pltpu.VMEM((seq, D), bf16),
            pltpu.VMEM((3, seq, PAIR), bf16),
            pltpu.VMEM((3, D, PAIR), bf16),
        ]
        + [dma(size) for size in sizes]
        + [dma] * 3,
        compiler_params=params(collective_id=0, has_side_effects=True),
        cost_estimate=cost(60),
        name="gather",
    )(block_weights, vector_params, tokens, passes)


def project_kernel(tok, pas, vec, wq, norm, q, k, v, cat):
    @pl.when(pl.program_id(0) == 0)
    def _():
        for x in range(3):
            for i in range(4):
                at = (i % 2) * SIDE
                parts = [wq[h, 2 * x + i // 2][:, at : at + SIDE] for h in range(2)]
                cat[x, i * SIDE : (i + 1) * SIDE, :] = jnp.concatenate(parts, axis=1)

    first = embedded(tok[...], pas[...], vec[...])
    hat, _ = hat_of(first)
    low = (hat * vec[PASSES : PASSES + 1] + vec[PASSES + 1 : PASSES + 2]).astype(bf16)
    norm[...] = low
    for x, out in enumerate((q, k, v)):
        out[...] = nn(low, cat[x]).astype(bf16)


def project(tokens, passes, vec, wq):
    seq = tokens.shape[0]
    row = lambda n: pl.BlockSpec((WIDE, n), lambda i: (i, 0))
    wide = jax.ShapeDtypeStruct((seq, PAIR), bf16)
    return pl.pallas_call(
        project_kernel,
        grid=(seq // WIDE,),
        in_specs=[
            row(D),
            pl.BlockSpec((1, WIDE), lambda i: (0, i)),
            full((16, D)),
            full((2, 6, SIDE, PAIR)),
        ],
        out_specs=[row(D), row(PAIR), row(PAIR), row(PAIR), full((3, D, PAIR))],
        out_shape=[
            jax.ShapeDtypeStruct((seq, D), bf16),
            wide,
            wide,
            wide,
            jax.ShapeDtypeStruct((3, D, PAIR), bf16),
        ],
        compiler_params=params(),
        cost_estimate=cost(16),
        name="project",
    )(tokens, passes, vec, wq)


def doc_state(lens, base):
    rows = base + lax.broadcasted_iota(jnp.int32, (1, ROWS), 1)
    rows = jnp.concatenate([rows, rows], axis=1)
    begin = jnp.int32(0)
    first = jnp.int32(0)
    starts = jnp.zeros((1, 2 * ROWS), jnp.int32)
    for c in range(DOCS):
        starts = jnp.where(rows >= begin, begin, starts)
        first = jnp.where(base >= begin, begin, first)
        begin = begin + lens[c]
    return rows, starts, first


def two_heads(block):
    left = lax.broadcasted_iota(jnp.int32, block.shape, 1) < HD
    none = jnp.zeros_like(block)
    return jnp.concatenate([jnp.where(left, block, none), jnp.where(left, none, block)], axis=0)


def one_above(both):
    return jnp.concatenate([both[:HD, :ROWS], both[HD:, ROWS:]], axis=0).T


def attend_kernel(lens, q, k, v, out, lse, acc):
    i = pl.program_id(0)
    base = i * ROWS
    rows, starts, first = doc_state(lens, base)
    pairs = [two_heads(q[:, p * 128 : (p + 1) * 128] * bf16(0.125)) for p in range(3)]
    for p in range(3):
        acc[p] = jnp.zeros((128, 2 * ROWS), f32)

    def step(j, carry):
        at = pl.multiple_of(j * ROWS, ROWS)
        keys = at + lax.broadcasted_iota(jnp.int32, (ROWS, 2 * ROWS), 0)
        seen = (keys >= starts) & (keys <= rows)
        here = pl.ds(at, ROWS)
        head = lambda p: slice(p * 128, (p + 1) * 128)
        scores = [jnp.where(seen, nt(k[here, head(p)], pairs[p]), masked_score) for p in range(3)]
        state = []
        for p in range(3):
            before, total = carry[2 * p], carry[2 * p + 1]
            now = jnp.maximum(before, jnp.max(scores[p], axis=0, keepdims=True))
            probs = jnp.exp(scores[p] - now)
            fade = jnp.exp(before - now)
            state += [now, total * fade + jnp.sum(probs, axis=0, keepdims=True)]
            acc[p] = acc[p] * fade + tn(v[here, head(p)], probs.astype(bf16))
        return tuple(state)

    zero = jnp.zeros((1, 2 * ROWS), f32)
    state = lax.fori_loop(first // ROWS, i + 1, step, (zero + masked_score, zero) * 3)
    lines = []
    for p in range(3):
        top, total = state[2 * p], state[2 * p + 1]
        out[:, p * 128 : (p + 1) * 128] = one_above(acc[p] / total).astype(bf16)
        line = top + jnp.log(total)
        lines += [line[:, :ROWS], line[:, ROWS:]]
    lse[...] = jnp.concatenate(lines + lines[:2], axis=0)


def attend(lens, q, k, v):
    seq = q.shape[0]
    row = pl.BlockSpec((ROWS, PAIR), lambda i, s: (i, 0))
    return pl.pallas_call(
        attend_kernel,
        grid_spec=pltpu.PrefetchScalarGridSpec(
            num_scalar_prefetch=1,
            grid=(seq // ROWS,),
            in_specs=[row, full((seq, PAIR)), full((seq, PAIR))],
            out_specs=[row, pl.BlockSpec((8, ROWS), lambda i, s: (0, i))],
            scratch_shapes=[
                pltpu.VMEM((3, 128, 2 * ROWS), f32),
            ],
        ),
        out_shape=[
            jax.ShapeDtypeStruct((seq, PAIR), bf16),
            jax.ShapeDtypeStruct((8, seq), f32),
        ],
        compiler_params=params(),
        cost_estimate=cost(30),
        name="attend",
    )(lens, q, k, v)


def attend_back_kernel(
    lens, q, k, v, mixed, lse, grad_mixed, dq, dk, dv, dk_acc, dv_acc, dq_acc
):
    i = pl.program_id(0)
    count = pl.num_programs(0)
    base = i * ROWS

    @pl.when(i == 0)
    def _():
        dk_acc[...] = jnp.zeros_like(dk_acc)
        dv_acc[...] = jnp.zeros_like(dv_acc)

    rows, starts, first = doc_state(lens, base)
    heads = lax.broadcasted_iota(jnp.int32, (8, 128), 0)
    lanes = lax.broadcasted_iota(jnp.int32, (8, 128), 1)
    pick = (lanes // HD == heads).astype(f32).astype(bf16)
    queries, grads, inner, lines = [], [], [], []
    for p in range(3):
        cols = slice(p * 128, (p + 1) * 128)
        queries.append(two_heads(q[:, cols] * bf16(0.125)))
        grads.append(two_heads(grad_mixed[:, cols]))
        product = grad_mixed[:, cols].astype(f32) * mixed[:, cols].astype(f32)
        high, low, _ = split_three(product)
        sums = nt(pick, high) + nt(pick, low)
        inner.append(jnp.concatenate([sums[0:1], sums[1:2]], axis=1))
        lines.append(jnp.concatenate([lse[2 * p : 2 * p + 1], lse[2 * p + 1 : 2 * p + 2]], axis=1))
        dq_acc[p] = jnp.zeros((128, 2 * ROWS), f32)

    def step(j, carry):
        at = pl.multiple_of(j * ROWS, ROWS)
        keys = at + lax.broadcasted_iota(jnp.int32, (ROWS, 2 * ROWS), 0)
        seen = (keys >= starts) & (keys <= rows)
        here = pl.ds(at, ROWS)
        for p in range(3):
            cols = slice(p * 128, (p + 1) * 128)
            kb = k[here, cols]
            scores = jnp.where(seen, nt(kb, queries[p]) - lines[p], masked_score)
            probs = jnp.exp(scores)
            grad_probs = nt(v[here, cols], grads[p])
            grad_scores = (probs * (grad_probs - inner[p])).astype(bf16)
            dv_acc[here, cols] += nn(probs.astype(bf16), grads[p])
            dk_acc[here, cols] += nn(grad_scores, queries[p])
            dq_acc[p] += tn(kb, grad_scores)
        return carry

    lax.fori_loop(first // ROWS, i + 1, step, 0)
    for p in range(3):
        dq[:, p * 128 : (p + 1) * 128] = (one_above(dq_acc[p]) * 0.125).astype(bf16)

    @pl.when(i == count - 1)
    def _():
        dk[...] = dk_acc[...].astype(bf16)
        dv[...] = dv_acc[...].astype(bf16)


def attend_back(lens, q, k, v, mixed, lse, grad_mixed):
    seq = q.shape[0]
    count = seq // ROWS
    row = pl.BlockSpec((ROWS, PAIR), lambda i, s: (i, 0))
    wide = jax.ShapeDtypeStruct((seq, PAIR), bf16)
    return pl.pallas_call(
        attend_back_kernel,
        grid_spec=pltpu.PrefetchScalarGridSpec(
            num_scalar_prefetch=1,
            grid=(count,),
            in_specs=[
                row,
                full((seq, PAIR)),
                full((seq, PAIR)),
                row,
                pl.BlockSpec((8, ROWS), lambda i, s: (0, i)),
                row,
            ],
            out_specs=[row, full((seq, PAIR)), full((seq, PAIR))],
            scratch_shapes=[
                pltpu.VMEM((seq, PAIR), f32),
                pltpu.VMEM((seq, PAIR), f32),
                pltpu.VMEM((3, 128, 2 * ROWS), f32),
            ],
        ),
        out_shape=[wide, wide, wide],
        compiler_params=params(),
        cost_estimate=cost(40),
        name="attend_back",
    )(lens, q, k, v, mixed, lse, grad_mixed)


def feed_kernel(
    small, tok, pas, vec, mine, cot, wo_mine, wo_other, w1, w2,
    out_chip, second_keep, grad_second, grad_mixed, sums, mid_send, mid_keep, *rest,
):
    results, rest = (rest[:4], rest[4:]) if small else (rest[:2], rest[2:])
    (
        wo, other, up, down, gup, gdown, go, core_out, core_in, far_out, far_in, ga_out, ga_in, oc_out, oc_in,
        g_send, g_keep, g_in, s_core, r_core, s_far, r_far, s_ga, r_ga, s_oc, r_oc, s_x, r_x, s_m, r_m,
    ) = rest
    step = pl.program_id(0)
    half = core_out.shape[0]
    t, dp = lax.axis_index("tensor"), lax.axis_index("dp")
    core, side = t % 2, t // 2
    near, far = side * 2 + (1 - core), (1 - side) * 2 + core
    z, column = (dp // 2, dp % 2) if small else (0, 0)
    far_x = z * 2 + 1 - column

    def copy(src, dst, s_sem, r_sem, j, to):
        return pltpu.make_async_remote_copy(
            src_ref=src.at[j],
            dst_ref=dst.at[j],
            send_sem=s_sem.at[j],
            recv_sem=r_sem.at[j],
            device_id={"tensor": to},
            device_id_type=MESH,
        )

    core_copy = lambda j: copy(core_out, core_in, s_core, r_core, j, near)
    far_copy = lambda j: copy(far_out, far_in, s_far, r_far, j, far)
    ga_copy = lambda j: copy(ga_out, ga_in, s_ga, r_ga, j, near)
    oc_copy = lambda j: copy(oc_out, oc_in, s_oc, r_oc, j, near)

    def x_copy(slot):
        return pltpu.make_async_remote_copy(
            src_ref=g_send.at[slot],
            dst_ref=g_in.at[slot],
            send_sem=s_x.at[slot],
            recv_sem=r_x.at[slot],
            device_id={"dp": far_x},
            device_id_type=MESH,
        )

    def mixed_copy(block):
        rows = pl.ds(pl.multiple_of(block * ROWS, ROWS), ROWS)
        return pltpu.make_async_remote_copy(
            src_ref=mine.at[rows],
            dst_ref=other.at[rows],
            send_sem=s_m.at[block],
            recv_sem=r_m.at[block],
            device_id={"tensor": near},
            device_id_type=MESH,
        )

    barrier = pltpu.get_barrier_semaphore()

    @pl.when(step == 0)
    def _():
        for to in (near, far):
            pl.semaphore_signal(barrier, inc=1, device_id={"tensor": to}, device_id_type=MESH)
        if small:
            pl.semaphore_signal(barrier, inc=1, device_id={"dp": far_x}, device_id_type=MESH)
        for h in range(2):
            for m in range(2):
                rows, cols = slice(h * SIDE, (h + 1) * SIDE), slice(m * PAIR, (m + 1) * PAIR)
                wo[rows, cols] = wo_mine[h, m]
                wo[PAIR + h * SIDE : PAIR + (h + 1) * SIDE, cols] = wo_other[h, m]
        for r in range(4):
            for m in range(2):
                rows, cols = slice(r * SIDE, (r + 1) * SIDE), slice(m * PAIR, (m + 1) * PAIR)
                up[rows, cols] = w1[0, 2 * r + m]
                down[rows, cols] = w2[0, 2 * r + m]
        pl.semaphore_wait(barrier, 3 if small else 2)
        for j in range(half):
            mixed_copy(core * half + j).start()
            mixed_copy((1 - core) * half + j).start()
        gup[...] = jnp.zeros_like(gup)
        gdown[...] = jnp.zeros_like(gdown)
        go[...] = jnp.zeros_like(go)
        sums[...] = jnp.zeros_like(sums)

    @pl.when(step < 2 * half)
    def _():
        j = step // 2
        owner = jnp.where(step % 2 == 0, 1 - core, core)
        here = pl.ds(pl.multiple_of((owner * half + j) * ROWS, ROWS), ROWS)
        first = embedded(tok[...], pas[...], vec[...])
        mixed_copy(owner * half + j).wait_recv()
        second = first + nn(jnp.concatenate([mine[here, :], other[here, :]], axis=1), wo[...])
        hat, _ = hat_of(second)
        low = (hat * vec[PASSES + 2 : PASSES + 3] + vec[PASSES + 3 : PASSES + 4]).astype(bf16)
        upper = nn(low, up[...])
        square = upper * upper
        bent = jnp.tanh(gelu_coef * upper * (1.0 + 0.044715 * square))
        act = (0.5 * upper * (1.0 + bent)).astype(bf16)
        slope = 0.5 * (1.0 + bent) + (0.5 * gelu_coef) * upper * (1.0 - bent * bent) * (
            1.0 + (3 * 0.044715) * square
        )
        grad_act = nt(cot[...], down[...])
        grad_upper = (grad_act * slope).astype(bf16)
        part = nt(grad_upper, up[...])

        @pl.when(step % 2 == 0)
        def _():
            core_out[j] = part.astype(bf16)
            core_copy(j).start()

        @pl.when(step % 2 == 1)
        def _():
            core_copy(j).wait_recv()
            far_out[j] = (part + core_in[j].astype(f32)).astype(bf16)
            far_copy(j).start()
            second_keep[pl.ds(pl.multiple_of(j * ROWS, ROWS), ROWS), :] = second

        gup[...] += tn(low, grad_upper)
        gdown[...] += tn(act, cot[...])
        out_part = nn(act, down[...])

        @pl.when(step % 2 == 0)
        def _():
            oc_out[j] = out_part.astype(bf16)
            oc_copy(j).start()

        @pl.when(step % 2 == 1)
        def _():
            oc_copy(j).wait_recv()
            out_chip[...] = (out_part + oc_in[j].astype(f32)).astype(bf16)

    @pl.when(step == 2 * half - 1)
    def _():
        for r in range(4):
            for m in range(2):
                rows, cols = slice(r * SIDE, (r + 1) * SIDE), slice(m * PAIR, (m + 1) * PAIR)
                for at, total in ((8, gup), (16, gdown)):
                    pair = at + 2 * r + m
                    slot, place = (pair // 6 - 1) * 3 + pair % 3, pair // 3 % 2
                    value = total[rows, cols].astype(bf16)
                    kept, sent, n = (mid_keep, mid_send, slot) if slot < 3 else (g_keep, g_send, slot - 3)

                    @pl.when(column == place)
                    def _():
                        kept[n] = value

                    @pl.when(column != place)
                    def _():
                        sent[n] = value
        if small:
            for n in range(6):
                x_copy(n).start()

    def through_out(grad, block):
        here = pl.ds(pl.multiple_of(block * ROWS, ROWS), ROWS)
        grad_mixed[here, :] = nt(grad, wo[:PAIR, :]).astype(bf16)
        go[...] += tn(mine[here, :], grad)

    @pl.when((step >= 2 * half) & (step < 3 * half))
    def _():
        j = step - 2 * half
        hat, root = hat_of(second_keep[pl.ds(pl.multiple_of(j * ROWS, ROWS), ROWS), :])
        far_copy(j).wait_recv()
        grad = far_out[j].astype(f32) + far_in[j].astype(f32)
        result = cot[...].astype(f32) + norm_back(hat, root, grad, vec[PASSES + 2 : PASSES + 3])
        low = result.astype(bf16)
        ga_out[j] = low
        ga_copy(j).start()
        grad_second[...] = result
        sums[0:1] += jnp.sum(grad * hat, axis=0, keepdims=True)
        sums[1:2] += jnp.sum(grad, axis=0, keepdims=True)
        through_out(low, core * half + j)

    @pl.when(step > 2 * half)
    def _():
        j = step - 2 * half - 1
        ga_copy(j).wait_recv()
        through_out(ga_in[j], (1 - core) * half + j)

    @pl.when(step == 3 * half)
    def _():
        at = pl.multiple_of(side * SIDE, SIDE)
        for m in range(2):
            value = go[pl.ds(at, SIDE), m * PAIR : (m + 1) * PAIR].astype(bf16)

            @pl.when(column == 0)
            def _():
                mid_keep[m] = value

            @pl.when(column != 0)
            def _():
                mid_send[m] = value

        for j in range(half):
            core_copy(j).wait_send()
            oc_copy(j).wait_send()
            mixed_copy(j).wait_send()
            mixed_copy(half + j).wait_send()
            far_copy(j).wait_send()
            ga_copy(j).wait_send()
        if small:
            for n in range(6):
                x_copy(n).wait_send()
                x_copy(n).wait_recv()
                value = (g_keep[n].astype(f32) + g_in[n].astype(f32)).astype(bf16)
                for turn in range(4):

                    @pl.when(lax.rem(z + turn, 4) == n // 3 + 2)
                    def _():
                        results[turn][n % 3] = value
        else:
            results[0][...] = g_send[...]
            results[1][...] = g_keep[...]


def feed(small, tokens, passes, vec, mine, cotangent, pairs, wo_other):
    seq = tokens.shape[0]
    half = seq // ROWS // 2

    def block(i):
        core = lax.axis_index("tensor") % 2
        work = jnp.minimum(i, 2 * half - 1)
        owner = jnp.where(work % 2 == 0, 1 - core, core)
        return owner * half + work // 2

    def cot_block(i):
        core = lax.axis_index("tensor") % 2
        return jnp.where(i < 2 * half, block(i), core * half + jnp.minimum(i - 2 * half, half - 1))

    side = lambda: lax.axis_index("tensor") // 2
    row = lambda n: pl.BlockSpec((ROWS, n), lambda i: (block(i), 0))
    keep = pl.BlockSpec((ROWS, D), lambda i: (jnp.minimum(i // 2, half - 1), 0))
    last = pl.BlockSpec((ROWS, D), lambda i: (jnp.clip(i - 2 * half, 0, half - 1), 0))
    rows = lambda kind: jax.ShapeDtypeStruct((seq // 2, D), kind)
    gr = lambda n: jax.ShapeDtypeStruct((n, SIDE, PAIR), bf16)
    ends = [(3, SIDE, PAIR)] * 4 if small else [(6, SIDE, PAIR)] * 2
    buffer = pltpu.VMEM((half, ROWS, D), bf16)
    dma = pltpu.SemaphoreType.DMA((half,))
    return pl.pallas_call(
        functools.partial(feed_kernel, small),
        grid=(3 * half + 1,),
        in_specs=[
            row(D),
            pl.BlockSpec((1, ROWS), lambda i: (0, block(i))),
            full((16, D)),
            full((seq, PAIR)),
            pl.BlockSpec((ROWS, D), lambda i: (cot_block(i), 0)),
            pl.BlockSpec((2, 2, SIDE, PAIR), lambda i: (0, 3, 0, 0)),
            full(wo_other.shape),
            pl.BlockSpec((1, 8, SIDE, PAIR), lambda i: (side(), 1, 0, 0)),
            pl.BlockSpec((1, 8, SIDE, PAIR), lambda i: (side(), 2, 0, 0)),
        ],
        out_specs=[
            keep,
            full((seq // 2, D)),
            last,
            full((seq, PAIR)),
            full((8, D)),
            full((3, SIDE, PAIR)),
            full((3, SIDE, PAIR)),
        ]
        + [full(shape) for shape in ends],
        scratch_shapes=[
            pltpu.VMEM((D, D), bf16),
            pltpu.VMEM((seq, PAIR), bf16),
            pltpu.VMEM((D, D), bf16),
            pltpu.VMEM((D, D), bf16),
            pltpu.VMEM((D, D), f32),
            pltpu.VMEM((D, D), f32),
            pltpu.VMEM((PAIR, D), f32),
        ]
        + [buffer] * 8
        + [pltpu.VMEM((6, SIDE, PAIR), bf16)] * 3
        + [dma] * 8
        + [pltpu.SemaphoreType.DMA((6,))] * 2
        + [pltpu.SemaphoreType.DMA((2 * half,))] * 2,
        out_shape=[
            rows(bf16),
            rows(f32),
            rows(f32),
            jax.ShapeDtypeStruct((seq, PAIR), bf16),
            jax.ShapeDtypeStruct((8, D), f32),
            gr(3),
            gr(3),
        ]
        + [jax.ShapeDtypeStruct(shape, bf16) for shape in ends],
        compiler_params=params(collective_id=1, has_side_effects=True),
        cost_estimate=cost(50),
        name="feed_forward",
    )(tokens, passes, vec, mine, cotangent, pairs, wo_other, pairs, pairs)


def qkv_grads_kernel(place, norm, dq, dk, dv, mid_send, mid_keep, g_send, g_keep, acc):
    i = pl.program_id(0)

    @pl.when(i == 0)
    def _():
        acc[...] = jnp.zeros_like(acc)

    mine = [jnp.where(place[1] == 0, grad[:, :SIDE], grad[:, SIDE:]) for grad in (dq, dk, dv)]
    acc[...] += tn(jnp.concatenate(mine, axis=1), norm[...])

    @pl.when(i == pl.num_programs(0) - 1)
    def _():
        for m in range(3):
            g_send[3 + m] = mid_send[m]
            g_keep[3 + m] = mid_keep[m]
        for x in range(3):
            for m in range(2):
                value = acc[x * SIDE : (x + 1) * SIDE, m * PAIR : (m + 1) * PAIR].astype(bf16)
                slot, column = (2 * x + m) % 3, (2 * x + m) // 3

                @pl.when(place[2] == column)
                def _():
                    g_keep[slot] = value

                @pl.when(place[2] != column)
                def _():
                    g_send[slot] = value


def qkv_grads(place, norm, dq, dk, dv, mid_send, mid_keep):
    seq = norm.shape[0]
    row = lambda n: pl.BlockSpec((WIDE, n), lambda i, s: (i, 0))
    return pl.pallas_call(
        qkv_grads_kernel,
        grid_spec=pltpu.PrefetchScalarGridSpec(
            num_scalar_prefetch=1,
            grid=(seq // WIDE,),
            in_specs=[row(D), row(PAIR), row(PAIR), row(PAIR)] + [full((3, SIDE, PAIR))] * 2,
            out_specs=[full((6, SIDE, PAIR)), full((6, SIDE, PAIR))],
            scratch_shapes=[pltpu.VMEM((3 * SIDE, D), f32)],
        ),
        out_shape=[jax.ShapeDtypeStruct((6, SIDE, PAIR), bf16)] * 2,
        compiler_params=params(),
        cost_estimate=cost(8),
        name="qkv_grads",
    )(place, norm, dq, dk, dv, mid_send, mid_keep)


CHUNK = SIDE // 2
CHUNKS = 12


def last_kernel(small, dq, dk, dv, cat, tok, pas, vec, grad_second, sums_two, g_send, g_keep, low, *rest):
    if small:
        late, vec_sum = rest[:2]
        rest = rest[2:]
        (
            core_out, core_in, sums, core_sums, x_in, z_in, z_out, up_in, v_out, v_in,
            s_core, r_core, s_sum, r_sum, s_x, r_x, s_z, r_z, s_up, r_up, s_v, r_v,
        ) = rest
    else:
        vec_sum, core_out, core_in, sums, core_sums, s_core, r_core, s_sum, r_sum = rest
    i = pl.program_id(0)
    half = core_out.shape[0]
    t, dp = lax.axis_index("tensor"), lax.axis_index("dp")
    core, side = t % 2, t // 2
    near = side * 2 + (1 - core)
    z, column = (dp // 2, dp % 2) if small else (0, 0)
    far_x = z * 2 + 1 - column
    peers = [lax.rem(dp + k, 8) for k in range(1, 8)]

    def copy(src, dst, s_sem, r_sem, to):
        return pltpu.make_async_remote_copy(
            src_ref=src, dst_ref=dst, send_sem=s_sem, recv_sem=r_sem, device_id=to, device_id_type=MESH
        )

    core_copy = lambda j: copy(core_out.at[j], core_in.at[j], s_core.at[j], r_core.at[j], {"tensor": near})
    sum_copy = lambda: copy(sums, core_sums, s_sum, r_sum, {"tensor": near})

    def part_of(ref, k):
        return ref.at[k // 2, pl.ds((k % 2) * CHUNK, CHUNK)]

    x_copy = lambda k: copy(part_of(g_send, k), x_in.at[k], s_x.at[k], r_x.at[k], {"dp": far_x})
    z_copy = lambda k: copy(z_out.at[k], z_in.at[k], s_z.at[k], r_z.at[k], {"dp": dp - 2})
    up_copy = lambda k: copy(z_out.at[k], up_in.at[k - 6], s_up.at[k - 6], r_up.at[k - 6], {"dp": dp + 2})
    v_copy = lambda n: copy(v_out.at[peers[n]], v_in.at[dp], s_v.at[n], r_v.at[dp], {"dp": peers[n]})
    barrier = pltpu.get_barrier_semaphore()

    @pl.when(i == 0)
    def _():
        pl.semaphore_signal(barrier, inc=1, device_id={"tensor": near}, device_id_type=MESH)
        if small:
            for peer in peers:
                pl.semaphore_signal(barrier, inc=1, device_id={"dp": peer}, device_id_type=MESH)
            late[...] = jnp.zeros_like(late)
        sums[...] = jnp.zeros_like(sums)
        sums[PASSES + 2 : PASSES + 4] = sums_two[0:2]
        pl.semaphore_wait(barrier, 8 if small else 1)
        if small:
            for k in range(6):
                x_copy(k).start()

    @pl.when(i < 2 * half)
    def _():
        part = nt(dq[...], cat[0]) + nt(dk[...], cat[1]) + nt(dv[...], cat[2])

        @pl.when(i < half)
        def _():
            core_out[i] = part.astype(bf16)
            core_copy(i).start()

        @pl.when(i >= half)
        def _():
            j = i - half
            hat, root = hat_of(embedded(tok[...], pas[...], vec[...]))
            core_copy(j).wait_recv()
            grad = part + core_in[j].astype(f32)
            result = grad_second[...] + norm_back(hat, root, grad, vec[PASSES : PASSES + 1])
            low[...] = result.astype(bf16)
            chosen = one_hot(pas[...])
            high, mid, _ = split_three(result)
            sums[...] += nn(chosen, high) + nn(chosen, mid)
            sums[PASSES : PASSES + 1] += jnp.sum(grad * hat, axis=0, keepdims=True)
            sums[PASSES + 1 : PASSES + 2] += jnp.sum(grad, axis=0, keepdims=True)

    @pl.when(i == 2 * half - 1)
    def _():
        sum_copy().start()

    if small:

        def term_of(k):
            rows = pl.ds(pl.multiple_of((k % 2) * CHUNK, 16), CHUNK)

            @pl.when(k < 6)
            def _():
                x_copy(k).wait_recv()

            @pl.when(k >= 6)
            def _():
                x_in[k] = g_send[k // 2, rows, :]

            return g_keep[k // 2, rows, :].astype(f32) + x_in[k].astype(f32)

        def keep_late(k, pair, total):
            late[pair, pl.ds(pl.multiple_of((k % 2) * CHUNK, 16), CHUNK), :] = total

        k = i - 1 - (3 - z)

        @pl.when((k >= 0) & (k < CHUNKS) & ((z > 0) | (k < 6)))
        def _():
            total = term_of(k)

            @pl.when(z < 3)
            def _():
                z_copy(k).wait_recv()

            below = jnp.where(z < 3, z_in[k].astype(f32), 0.0)
            passed = total + below

            @pl.when((z > 1) | ((z == 1) & (k < 6)))
            def _():
                z_out[k] = passed.astype(bf16)
                z_copy(k).start()

            @pl.when(z == 0)
            def _():
                keep_late(k, k // 2, passed)

            @pl.when((z == 1) & (k >= 6))
            def _():
                up_copy(k).wait_recv()
                keep_late(k, k // 2 - 3, passed + up_in[k - 6].astype(f32))

        @pl.when((i >= 7) & (i < 13) & (z == 0))
        def _():
            z_out[i - 1] = term_of(i - 1).astype(bf16)
            up_copy(i - 1).start()

    @pl.when(i == 2 * half + 1)
    def _():
        sum_copy().wait_recv()
        total = sums[...] + core_sums[...]
        if small:
            wide = D // 8
            for d in range(8):
                v_out[d, :, 0:wide] = total[:, d * wide : (d + 1) * wide]
                v_out[d, :, wide:] = jnp.zeros((16, 128 - wide), f32)
            for n in range(7):
                v_copy(n).start()
        else:
            vec_sum[...] = total

    @pl.when(i == pl.num_programs(0) - 1)
    def _():
        for j in range(half):
            core_copy(j).wait_send()
        sum_copy().wait_send()
        if small:
            for peer in peers:
                copy(v_out.at[0], v_in.at[peer], s_v.at[0], r_v.at[peer], {"dp": far_x}).wait_recv()
            v_in[dp] = v_out[dp]
            total = v_in[0]
            for d in range(1, 8):
                total = total + v_in[d]
            vec_sum[...] = total
            for n in range(7):
                v_copy(n).wait_send()
            for k in range(CHUNKS):
                if k < 6:
                    x_copy(k).wait_send()
                    pl.when(z > 0)(z_copy(k).wait_send)
                else:
                    pl.when(z > 1)(z_copy(k).wait_send)
                    pl.when(z == 0)(up_copy(k).wait_send)


def last(small, dq, dk, dv, cat, tokens, passes, vec, grad_second, sums_two, g_send, g_keep):
    seq = dq.shape[0]
    half = seq // ROWS // 2
    core = lambda: lax.axis_index("tensor") % 2

    def block(i):
        work = jnp.minimum(i, 2 * half - 1)
        return lax.rem(work + (1 - core()) * half, 2 * half)

    own = lambda i: jnp.clip(i - half, 0, half - 1)
    row = pl.BlockSpec((ROWS, PAIR), lambda i: (block(i), 0))
    mine = pl.BlockSpec((ROWS, D), lambda i: (own(i), 0))
    dma = pltpu.SemaphoreType.DMA
    out_specs = [mine]
    out_shape = [jax.ShapeDtypeStruct((seq // 2, D), bf16)]
    scratch = [
        pltpu.VMEM((half, ROWS, D), bf16),
        pltpu.VMEM((half, ROWS, D), bf16),
        pltpu.VMEM((16, D), f32),
        pltpu.VMEM((16, D), f32),
    ]
    sems = [dma((half,)), dma((half,)), dma, dma]
    if small:
        out_specs += [full((3, SIDE, PAIR)), full((16, 128))]
        out_shape += [
            jax.ShapeDtypeStruct((3, SIDE, PAIR), f32),
            jax.ShapeDtypeStruct((16, 128), f32),
        ]
        scratch += [pltpu.VMEM((CHUNKS, CHUNK, PAIR), bf16)] * 3
        scratch += [pltpu.VMEM((6, CHUNK, PAIR), bf16)]
        scratch += [pltpu.VMEM((8, 16, 128), f32)] * 2
        sems += [dma((6,))] * 2 + [dma((CHUNKS,))] * 2 + [dma((6,))] * 2 + [dma((7,)), dma((8,))]
    else:
        out_specs += [full((16, D))]
        out_shape += [jax.ShapeDtypeStruct((16, D), f32)]
    return pl.pallas_call(
        functools.partial(last_kernel, small),
        grid=(2 * half + 7 if small else 2 * half + 2,),
        in_specs=[
            row,
            row,
            row,
            full(cat.shape),
            pl.BlockSpec((ROWS, D), lambda i: (core() * half + own(i), 0)),
            pl.BlockSpec((1, ROWS), lambda i: (0, core() * half + own(i))),
            full((16, D)),
            mine,
            full((8, D)),
            full(g_send.shape),
            full(g_keep.shape),
        ],
        out_specs=out_specs,
        out_shape=out_shape,
        scratch_shapes=scratch + sems,
        compiler_params=params(collective_id=2, has_side_effects=True),
        cost_estimate=cost(30),
        name="last",
    )(dq, dk, dv, cat, tokens, passes, vec, grad_second, sums_two, g_send, g_keep)


def precondition(grad, weight, left, right, left_root, right_root):
    high = lax.Precision.HIGHEST
    left_new = decay * left + (1.0 - decay) * jnp.einsum(
        "...ij,...kj->...ik", grad, grad, precision=high
    )
    right_new = decay * right + (1.0 - decay) * jnp.einsum(
        "...ji,...jk->...ik", grad, grad, precision=high
    )
    half = jnp.einsum("...ij,...jk->...ik", left_root, grad, precision=high)
    step = jnp.einsum("...ij,...jk->...ik", half, right_root, precision=high)
    return (left_new, right_new, step, weight - rate_matrix * step)


def two_part(value):
    high = value.astype(bf16)
    return high, (value - high.astype(f32)).astype(bf16)


def dot_three(dot, a, b):
    return dot(a[0], b[0]) + (dot(a[0], b[1]) + dot(a[1], b[0]))


def renew_kernel(place, late, own, one, two, three, weight, left, right, left_root, right_root, left_new, right_new, step, new):
    early = own[0].astype(f32) + one[0].astype(f32) + two[0].astype(f32) + three[0].astype(f32)
    z = place[3]
    both = late[0] + jnp.where(z > 1, early, 0.0)
    for n in range(2):
        grad = both[:, n * SIDE : (n + 1) * SIDE]
        grad = two_part(jnp.where(z == 0, grad.T, grad))
        left_new[0, n] = decay * left[0, n] + (1.0 - decay) * dot_three(nt, grad, grad)
        right_new[0, n] = decay * right[0, n] + (1.0 - decay) * dot_three(tn, grad, grad)
        half = dot_three(nn, two_part(left_root[0, n]), grad)
        value = dot_three(nn, two_part(half), two_part(right_root[0, n]))
        step[0, n] = value
        new[0, n] = weight[0, n] - rate_matrix * value


def renew(place, late, own, far, weight, left, right, left_root, right_root):
    pair = pl.BlockSpec((1, SIDE, PAIR), lambda i, s: (i, 0, 0))
    slot = pl.BlockSpec((1, 2, SIDE, SIDE), lambda i, s: (0, i, 0, 0))
    return pl.pallas_call(
        renew_kernel,
        grid_spec=pltpu.PrefetchScalarGridSpec(
            num_scalar_prefetch=1,
            grid=(3,),
            in_specs=[pair] * 5 + [slot] * 5,
            out_specs=[slot] * 4,
        ),
        out_shape=[jax.ShapeDtypeStruct(weight.shape, f32)] * 4,
        compiler_params=params(),
        cost_estimate=cost(5),
        name="renew",
    )(place, late, own, *far, weight, left, right, left_root, right_root)


def to_pairs(blocks):
    n = blocks.shape[0] // 2
    return blocks.reshape(n, 2, SIDE, SIDE).transpose(0, 2, 1, 3).reshape(n, SIDE, PAIR)


def from_pairs(pairs):
    n = pairs.shape[0]
    return pairs.reshape(n, SIDE, 2, SIDE).transpose(0, 2, 1, 3).reshape(2 * n, SIDE, SIDE)


def swap(value, bit):
    return lax.ppermute(value, "tensor", [(t, t ^ bit) for t in range(NT)])


def hop_x(value):
    return lax.ppermute(value, "dp", [(d, d ^ 1) for d in range(8)])


def hop_z(value, turn, ends):
    pairs = [(d, (d + 2 * turn) % 8) for d in range(8) if (d // 2 + turn) % 4 in ends]
    return lax.ppermute(value, "dp", pairs)


def tie(*values):
    return lax.optimization_barrier(values)


def on_device(
    tokens,
    pass_ids,
    doc_lengths,
    cotangent,
    block_weights,
    vector_params,
    vector_moment,
    block_left,
    block_right,
    block_left_root,
    block_right_root,
):
    t, dp = lax.axis_index("tensor"), lax.axis_index("dp")
    core, side = t % 2, t // 2
    n_dp = lax.axis_size("dp")
    small = n_dp == 8
    z, column = (dp // 2, dp % 2) if small else (0, 0)
    place = jnp.stack([core, side, jnp.asarray(column), jnp.asarray(z)]).astype(jnp.int32)
    lens = doc_lengths[0]
    seq = tokens.shape[0]
    passes = pass_ids.reshape(1, seq)
    total_blocks = (D // SIDE) * (4 + 2 * (FF // D))
    slots = block_weights.shape[1] * n_dp

    if small:
        pairs, wo_other, vec, norm, q, k, v, cat = gather(block_weights, vector_params, tokens, passes)
    else:
        every = lax.all_gather(block_weights.astype(bf16), "dp", axis=1, tiled=True)[0]
        near = to_pairs(every[:total_blocks])
        far = swap(near, 2)
        pairs = jnp.where(side == 0, jnp.stack([near, far]), jnp.stack([far, near]))
        vec = lax.all_gather(vector_params, "dp", axis=1, tiled=True)
        vec = jnp.pad(vec, ((0, 16 - vec.shape[0]), (0, 0)))
        wo_other = swap(pairs[:, 6:8], 1)
        norm, q, k, v, cat = project(tokens, passes, vec, pairs)
    mine, lse = attend(lens, q, k, v)
    out_chip, second, grad_second, grad_mixed, sums_two, mid_send, mid_keep, *ends = feed(
        small, tokens, passes, vec, mine, cotangent, pairs, wo_other
    )
    out_far = swap(out_chip, 2)
    if small:
        far = [hop_z(ends[turn], turn, (2, 3)) for turn in (1, 2, 3)]
        mid_send = hop_x(mid_send)
    dq, dk, dv = attend_back(lens, q, k, v, mine, lse, grad_mixed)
    g_send, g_keep = qkv_grads(place, norm, dq, dk, dv, mid_send, mid_keep)
    if small:
        *far, out_far, g_send = tie(*far, out_far, g_send)
    low_half, *sums = last(
        small, dq, dk, dv, cat, tokens, passes, vec, grad_second, sums_two, g_send, g_keep
    )
    out_half = (second + (out_chip.astype(f32) + out_far.astype(f32))).astype(bf16)

    def join(half):
        far = swap(half, 1)
        low = jnp.where(core == 0, half, far)
        high = jnp.where(core == 0, far, half)
        return jnp.concatenate([low, high], axis=0)

    output, input_grad = join(out_half), join(low_half)
    if small:
        late, vector_sum = sums
        left_new, right_new, step, weight_new = renew(
            place, late, ends[0], far, block_weights, block_left, block_right, block_left_root, block_right_root
        )
        vector_grad = vector_sum[: PASSES + 4, : vector_params.shape[1]]
    else:
        vector_part = sums[0][: PASSES + 4]
        send, keep = ends
        rest = jnp.stack(
            [
                jnp.concatenate([mid_keep, keep]).reshape(3, 3, SIDE, PAIR),
                jnp.concatenate([mid_send, send]).reshape(3, 3, SIDE, PAIR),
            ],
            axis=1,
        )
        grad_qkv = from_pairs(jnp.concatenate([g_keep[:3], g_send[:3]], axis=0)).swapaxes(1, 2)
        grad_rest = from_pairs(rest.reshape(18, SIDE, PAIR))
        spare = jnp.zeros((slots - total_blocks, SIDE, SIDE), bf16)
        grad_blocks = jnp.concatenate([grad_qkv, grad_rest, spare], axis=0)[None].astype(f32)
        owned = lax.psum_scatter(grad_blocks, "dp", scatter_dimension=1, tiled=True)
        vector_grad = lax.psum_scatter(vector_part, "dp", scatter_dimension=1, tiled=True)
        left_new, right_new, step, weight_new = precondition(
            owned, block_weights, block_left, block_right, block_left_root, block_right_root
        )
    moment_new = decay * vector_moment + (1.0 - decay) * vector_grad * vector_grad
    vector_new = vector_params - rate_vector * vector_grad / (jnp.sqrt(moment_new) + moment_eps)
    return (
        output,
        input_grad,
        left_new,
        right_new,
        step,
        weight_new,
        vector_grad,
        moment_new,
        vector_new,
    )


def solution(mesh):
    rows, line = P("dp", None), P(None, "dp")
    block = P("tensor", "dp", None, None)
    return jax.shard_map(
        on_device,
        mesh=mesh,
        in_specs=(rows, P("dp"), rows, rows, block, line, line, block, block, block, block),
        out_specs=(rows, rows, block, block, block, block, line, line, line),
        check_vma=False,
    )
```

```python
import functools

import jax
import jax.numpy as jnp
from jax import lax
from jax.experimental import pallas as pl
from jax.experimental.pallas import tpu as pltpu
from jax.sharding import PartitionSpec as P

D = 768
HD = 64
FF = 3072
PASSES = 5
SIDE = 192
PAIR = 2 * SIDE
ROWS = 256
WIDE = 512
DOCS = 8
NT = 4

norm_eps = 1e-05
moment_eps = 1e-08
rate_matrix = 0.03
rate_vector = 0.2
decay = 0.5
gelu_coef = 0.7978845608028654
masked_score = -1e30
f32 = jnp.float32
bf16 = jnp.bfloat16
MESH = pl.DeviceIdType.MESH
VMEM_LIMIT = 56 * 1024 * 1024


def nn(a, b):
    return lax.dot_general(a, b, (((1,), (0,)), ((), ())), preferred_element_type=f32)


def nt(a, b):
    return lax.dot_general(a, b, (((1,), (1,)), ((), ())), preferred_element_type=f32)


def tn(a, b):
    return lax.dot_general(a, b, (((0,), (0,)), ((), ())), preferred_element_type=f32)


def split_three(value):
    high = value.astype(bf16)
    rest = value - high.astype(f32)
    mid = rest.astype(bf16)
    return high, mid, (rest - mid.astype(f32)).astype(bf16)


def one_hot(pass_row):
    kinds = lax.broadcasted_iota(jnp.int32, (16, pass_row.shape[1]), 0)
    return (kinds == pass_row).astype(f32).astype(bf16)


def embedded(tokens, pass_row, vec):
    chosen = jnp.concatenate([one_hot(pass_row)] * 3, axis=0)
    return tokens.astype(f32) + tn(chosen, jnp.concatenate(split_three(vec), axis=0))


def hat_of(hidden):
    mean = jnp.mean(hidden, axis=-1, keepdims=True)
    center = hidden - mean
    spread = jnp.mean(center * center, axis=-1, keepdims=True)
    root = lax.rsqrt(spread + norm_eps)
    return center * root, root


def norm_back(hat, root, grad, gain):
    scaled = grad * gain
    first = jnp.mean(scaled, axis=-1, keepdims=True)
    second = jnp.mean(scaled * hat, axis=-1, keepdims=True)
    return root * (scaled - first - hat * second)


def params(**kw):
    return pltpu.CompilerParams(vmem_limit_bytes=VMEM_LIMIT, **kw)


def cost(micros):
    return pl.CostEstimate(flops=int(micros * 1.1e9), bytes_accessed=int(micros * 1e6), transcendentals=0)


def full(shape):
    return pl.BlockSpec(shape, lambda *_: (0,) * len(shape))


def gather_kernel(
    own, vec_own, tokens, passes,
    all_pairs, wo_other, vec_out, norm, q, k_out, v, cat,
    pack, vec_pack, vec_land, wq, tok, norm_s, qkv_s, cat_s, *sems,
):
    (
        s_z1, r_z1, s_x1, r_x1, s_y1, r_y1, s_d1, r_d1, s_l, r_l, s_r, r_r, s_x2, r_x2, s_y2, r_y2, s_v, r_v, s_c, r_c,
        s_out, s_cat, s_tok, loc,
    ) = sems
    dp, t = lax.axis_index("dp"), lax.axis_index("tensor")
    z, x = dp // 2, dp % 2
    y, core = t // 2, t % 2
    far_x, far_y, near = z * 2 + (1 - x), (1 - y) * 2 + core, y * 2 + (1 - core)

    barrier = pltpu.get_barrier_semaphore()
    peers = [lax.rem(dp + n, 8) for n in range(1, 8)]
    for peer in peers:
        pl.semaphore_signal(barrier, inc=1, device_id={"dp": peer}, device_id_type=MESH)
    for to in (far_y, near):
        pl.semaphore_signal(barrier, inc=1, device_id={"tensor": to}, device_id_type=MESH)

    tok_copy = pltpu.make_async_copy(tokens, tok, s_tok)
    tok_copy.start()
    for m in range(3):
        pair = jnp.concatenate([own[0, 2 * m], own[0, 2 * m + 1]], axis=1).astype(bf16)
        pack[m] = pair

        @pl.when(z == 0)
        def _():
            wq[y, 3 * x + m] = pair

    vec_pack[...] = jnp.zeros_like(vec_pack)
    vec_pack[0 : PASSES + 4, 0 : D // 8] = vec_own[...]
    pl.semaphore_wait(barrier, 9)

    started = []

    def send(src, dst, s_sem, r_sem, to, cond=None):
        copy = pltpu.make_async_remote_copy(
            src_ref=src, dst_ref=dst, send_sem=s_sem, recv_sem=r_sem, device_id=to, device_id_type=MESH
        )
        started.append((cond, copy))
        if cond is None:
            copy.start()
        else:
            pl.when(cond)(copy.start)

    def arrived(dst, r_sem, cond=None):
        copy = pltpu.make_async_remote_copy(
            src_ref=dst, dst_ref=dst, send_sem=loc, recv_sem=r_sem, device_id={"dp": far_x}, device_id_type=MESH
        )
        if cond is None:
            copy.wait_recv()
        else:
            pl.when(cond)(copy.wait_recv)

    to_x, to_y, to_left, to_right = {"dp": far_x}, {"tensor": far_y}, {"dp": dp - 2}, {"dp": dp + 2}
    half = SIDE // 2

    def piece(side, column, k):
        return wq.at[side, 3 * column + k // 2, pl.ds((k % 2) * half, half)]

    def at_z(d, m):
        return all_pairs.at[y, 3 * dp + 6 * d + m]

    own_copy = pltpu.make_async_copy(pack, all_pairs.at[y, pl.ds(3 * dp, 3)], loc)
    pl.when(z > 0)(own_copy.start)

    for m in range(3):
        send(pack.at[m], at_z(0, m), s_l.at[0, m], r_l.at[0, m], to_left, z > 0)
    for n, peer in enumerate(peers):
        send(vec_pack, vec_land.at[dp], s_v.at[n], r_v.at[dp], {"dp": peer})
    for m in range(3):
        send(pack.at[m], at_z(0, m), s_x2.at[z, m], r_x2.at[z, m], to_x, z > m)

    def diagonal(k):
        arrived(piece(y, 1 - x, k), r_x1.at[k])
        send(piece(y, 1 - x, k), piece(y, 1 - x, k), s_d1.at[k], r_d1.at[k], to_y)

    def from_right(d, m):
        arrived(at_z(d, m), r_l.at[d - 1, m], z + d < 4)
        if d < 3:
            send(at_z(d, m), at_z(d, m), s_l.at[d, m], r_l.at[d, m], to_left, (z + d < 4) & (z > 0))

    def from_left(d, m):
        arrived(at_z(-d, m), r_r.at[d - 1, m], z - d > 0)
        if d == 1:
            send(at_z(-d, m), at_z(-d, m), s_r.at[1, m], r_r.at[1, m], to_right, (z - d > 0) & (z < 3))

    def along_x(d, m, cond):
        send(at_z(d, m), at_z(d, m), s_x2.at[z + d, m], r_x2.at[z + d, m], to_x, cond)

    for k in range(6):
        arrived(piece(y, x, k), r_z1.at[k], z > 0)
        send(piece(y, x, k), piece(y, x, k), s_z1.at[k], r_z1.at[k], to_right, z < 3)
        send(piece(y, x, k), piece(y, x, k), s_x1.at[k], r_x1.at[k], to_x)
        send(piece(y, x, k), piece(y, x, k), s_y1.at[k], r_y1.at[k], to_y)
        if k == 5:
            for m in range(3):
                send(pack.at[m], at_z(0, m), s_r.at[0, m], r_r.at[0, m], to_right, (z > 0) & (z < 3))
                send(pack.at[m], at_z(0, m), s_x2.at[z, m], r_x2.at[z, m], to_x, (z > 0) & (z <= m))
        if k >= 1:
            diagonal(k - 1)
        if k % 2 == 1:
            from_right(1, k // 2)
    diagonal(5)
    pl.when(z > 0)(own_copy.wait)
    for m in range(3):
        along_x(1, m, z + 1 < 4)
    for m in range(3):
        from_left(1, m)
        along_x(-1, m, z - 1 > 0)
        from_right(2, m)
        along_x(2, m, z + 2 < 4)
    for k in range(6):
        arrived(piece(1 - y, x, k), r_y1.at[k])
        arrived(piece(1 - y, 1 - x, k), r_d1.at[k])
    for peer in peers:
        arrived(vec_land.at[peer], r_v.at[peer])
    vec_land[dp] = vec_pack[...]
    vec = jnp.concatenate([vec_land[d][:, : D // 8] for d in range(8)], axis=1)
    vec_out[...] = vec
    for n in range(3):
        for i in range(4):
            at = (i % 2) * SIDE
            parts = [wq[h, 2 * n + i // 2][:, at : at + SIDE] for h in range(2)]
            cat_s[n, i * SIDE : (i + 1) * SIDE, :] = jnp.concatenate(parts, axis=1)
    writes = [pltpu.make_async_copy(cat_s, cat, s_cat)]
    writes[0].start()
    tok_copy.wait()

    def rows_of(b):
        rows = slice(b * WIDE, (b + 1) * WIDE)
        hat, _ = hat_of(embedded(tok[rows, :], passes[:, rows], vec))
        low = (hat * vec[PASSES : PASSES + 1] + vec[PASSES + 1 : PASSES + 2]).astype(bf16)
        norm_s[rows, :] = low
        writes.append(pltpu.make_async_copy(norm_s.at[rows, :], norm.at[rows, :], s_out.at[b, 3]))
        writes[-1].start()
        for n, out in enumerate((q, k_out, v)):
            qkv_s[n, rows, :] = nn(low, cat_s[n]).astype(bf16)
            writes.append(pltpu.make_async_copy(qkv_s.at[n, rows, :], out.at[rows, :], s_out.at[b, n]))
            writes[-1].start()

    count = tok.shape[0] // WIDE
    for b in range(count):
        rows_of(b)
        if b == 0:
            for m in range(3):
                from_right(3, m)
                along_x(3, m, z + 3 < 4)
        if b == 1:
            for m in range(3):
                from_left(2, m)
                along_x(-2, m, z - 2 > 0)
        if b == 2:
            for m in range(2):
                ref = all_pairs.at[y, 6 + m]
                arrived(ref, r_x2.at[1, m], x == 1)
                send(ref, ref, s_y2.at[m], r_y2.at[m], to_y)
                send(ref, wo_other.at[y, m], s_c.at[0, m], r_c.at[y, m], {"tensor": near})
    for m in range(2):
        ref = all_pairs.at[1 - y, 6 + m]
        arrived(ref, r_y2.at[m])
        send(ref, wo_other.at[1 - y, m], s_c.at[1, m], r_c.at[1 - y, m], {"tensor": near})
    for w in range(1, 4):
        for m in range(3):
            ref = all_pairs.at[y, 6 * w + 3 * (1 - x) + m]
            if w == 1 and m < 2:
                arrived(ref, r_x2.at[w, m], x == 0)
            else:
                arrived(ref, r_x2.at[w, m])
    for h in range(2):
        for m in range(2):
            arrived(wo_other.at[h, m], r_c.at[h, m])
    for copy in writes:
        copy.wait()
    for cond, copy in started:
        if cond is None:
            copy.wait_send()
        else:
            pl.when(cond)(copy.wait_send)


def gather(block_weights, vector_params, tokens, passes):
    seq = tokens.shape[0]
    dma = pltpu.SemaphoreType.DMA
    sizes = [(6,)] * 8 + [(3, 3)] * 2 + [(2, 3)] * 2 + [(4, 3)] * 2 + [(2,)] * 2 + [(7,), (8,)] + [(2, 2)] * 2
    sizes += [(seq // WIDE, 4)]
    vmem, far = pl.BlockSpec(memory_space=pltpu.VMEM), pl.BlockSpec(memory_space=pl.ANY)
    wide = jax.ShapeDtypeStruct((seq, PAIR), bf16)
    return pl.pallas_call(
        gather_kernel,
        in_specs=[vmem, vmem, far, vmem],
        out_specs=[far, far, vmem, far, far, far, far, far],
        out_shape=[
            jax.ShapeDtypeStruct((2, 24, SIDE, PAIR), bf16),
            jax.ShapeDtypeStruct((2, 2, SIDE, PAIR), bf16),
            jax.ShapeDtypeStruct((16, D), f32),
            jax.ShapeDtypeStruct((seq, D), bf16),
            wide,
            wide,
            wide,
            jax.ShapeDtypeStruct((3, D, PAIR), bf16),
        ],
        scratch_shapes=[
            pltpu.VMEM((3, SIDE, PAIR), bf16),
            pltpu.VMEM((16, 128), f32),
            pltpu.VMEM((8, 16, 128), f32),
            pltpu.VMEM((2, 6, SIDE, PAIR), bf16),
            pltpu.VMEM((seq, D), bf16),
            pltpu.VMEM((seq, D), bf16),
            pltpu.VMEM((3, seq, PAIR), bf16),
            pltpu.VMEM((3, D, PAIR), bf16),
        ]
        + [dma(size) for size in sizes]
        + [dma] * 3,
        compiler_params=params(collective_id=0, has_side_effects=True),
        cost_estimate=cost(60),
        name="gather",
    )(block_weights, vector_params, tokens, passes)


def project_kernel(tok, pas, vec, wq, norm, q, k, v, cat):
    @pl.when(pl.program_id(0) == 0)
    def _():
        for x in range(3):
            for i in range(4):
                at = (i % 2) * SIDE
                parts = [wq[h, 2 * x + i // 2][:, at : at + SIDE] for h in range(2)]
                cat[x, i * SIDE : (i + 1) * SIDE, :] = jnp.concatenate(parts, axis=1)

    first = embedded(tok[...], pas[...], vec[...])
    hat, _ = hat_of(first)
    low = (hat * vec[PASSES : PASSES + 1] + vec[PASSES + 1 : PASSES + 2]).astype(bf16)
    norm[...] = low
    for x, out in enumerate((q, k, v)):
        out[...] = nn(low, cat[x]).astype(bf16)


def project(tokens, passes, vec, wq):
    seq = tokens.shape[0]
    row = lambda n: pl.BlockSpec((WIDE, n), lambda i: (i, 0))
    wide = jax.ShapeDtypeStruct((seq, PAIR), bf16)
    return pl.pallas_call(
        project_kernel,
        grid=(seq // WIDE,),
        in_specs=[
            row(D),
            pl.BlockSpec((1, WIDE), lambda i: (0, i)),
            full((16, D)),
            full((2, 6, SIDE, PAIR)),
        ],
        out_specs=[row(D), row(PAIR), row(PAIR), row(PAIR), full((3, D, PAIR))],
        out_shape=[
            jax.ShapeDtypeStruct((seq, D), bf16),
            wide,
            wide,
            wide,
            jax.ShapeDtypeStruct((3, D, PAIR), bf16),
        ],
        compiler_params=params(),
        cost_estimate=cost(16),
        name="project",
    )(tokens, passes, vec, wq)


def doc_state(lens, base):
    rows = base + lax.broadcasted_iota(jnp.int32, (1, ROWS), 1)
    rows = jnp.concatenate([rows, rows], axis=1)
    begin = jnp.int32(0)
    first = jnp.int32(0)
    starts = jnp.zeros((1, 2 * ROWS), jnp.int32)
    for c in range(DOCS):
        starts = jnp.where(rows >= begin, begin, starts)
        first = jnp.where(base >= begin, begin, first)
        begin = begin + lens[c]
    return rows, starts, first


def two_heads(block):
    left = lax.broadcasted_iota(jnp.int32, block.shape, 1) < HD
    none = jnp.zeros_like(block)
    return jnp.concatenate([jnp.where(left, block, none), jnp.where(left, none, block)], axis=0)


def one_above(both):
    return jnp.concatenate([both[:HD, :ROWS], both[HD:, ROWS:]], axis=0).T


def attend_kernel(lens, q, k, v, out, lse, acc):
    i = pl.program_id(0)
    base = i * ROWS
    rows, starts, first = doc_state(lens, base)
    pairs = [two_heads(q[:, p * 128 : (p + 1) * 128] * bf16(0.125)) for p in range(3)]
    for p in range(3):
        acc[p] = jnp.zeros((128, 2 * ROWS), f32)

    def step(j, carry):
        at = pl.multiple_of(j * ROWS, ROWS)
        keys = at + lax.broadcasted_iota(jnp.int32, (ROWS, 2 * ROWS), 0)
        seen = (keys >= starts) & (keys <= rows)
        here = pl.ds(at, ROWS)
        head = lambda p: slice(p * 128, (p + 1) * 128)
        scores = [jnp.where(seen, nt(k[here, head(p)], pairs[p]), masked_score) for p in range(3)]
        state = []
        for p in range(3):
            before, total = carry[2 * p], carry[2 * p + 1]
            now = jnp.maximum(before, jnp.max(scores[p], axis=0, keepdims=True))
            probs = jnp.exp(scores[p] - now)
            fade = jnp.exp(before - now)
            state += [now, total * fade + jnp.sum(probs, axis=0, keepdims=True)]
            acc[p] = acc[p] * fade + tn(v[here, head(p)], probs.astype(bf16))
        return tuple(state)

    zero = jnp.zeros((1, 2 * ROWS), f32)
    state = lax.fori_loop(first // ROWS, i + 1, step, (zero + masked_score, zero) * 3)
    lines = []
    for p in range(3):
        top, total = state[2 * p], state[2 * p + 1]
        out[:, p * 128 : (p + 1) * 128] = one_above(acc[p] / total).astype(bf16)
        line = top + jnp.log(total)
        lines += [line[:, :ROWS], line[:, ROWS:]]
    lse[...] = jnp.concatenate(lines + lines[:2], axis=0)


def attend(lens, q, k, v):
    seq = q.shape[0]
    row = pl.BlockSpec((ROWS, PAIR), lambda i, s: (i, 0))
    return pl.pallas_call(
        attend_kernel,
        grid_spec=pltpu.PrefetchScalarGridSpec(
            num_scalar_prefetch=1,
            grid=(seq // ROWS,),
            in_specs=[row, full((seq, PAIR)), full((seq, PAIR))],
            out_specs=[row, pl.BlockSpec((8, ROWS), lambda i, s: (0, i))],
            scratch_shapes=[
                pltpu.VMEM((3, 128, 2 * ROWS), f32),
            ],
        ),
        out_shape=[
            jax.ShapeDtypeStruct((seq, PAIR), bf16),
            jax.ShapeDtypeStruct((8, seq), f32),
        ],
        compiler_params=params(),
        cost_estimate=cost(30),
        name="attend",
    )(lens, q, k, v)


def attend_back_kernel(
    lens, q, k, v, mixed, lse, grad_mixed, dq, dk, dv, dk_acc, dv_acc, dq_acc
):
    i = pl.program_id(0)
    count = pl.num_programs(0)
    base = i * ROWS

    @pl.when(i == 0)
    def _():
        dk_acc[...] = jnp.zeros_like(dk_acc)
        dv_acc[...] = jnp.zeros_like(dv_acc)

    rows, starts, first = doc_state(lens, base)
    heads = lax.broadcasted_iota(jnp.int32, (8, 128), 0)
    lanes = lax.broadcasted_iota(jnp.int32, (8, 128), 1)
    pick = (lanes // HD == heads).astype(f32).astype(bf16)
    queries, grads, inner, lines = [], [], [], []
    for p in range(3):
        cols = slice(p * 128, (p + 1) * 128)
        queries.append(two_heads(q[:, cols] * bf16(0.125)))
        grads.append(two_heads(grad_mixed[:, cols]))
        product = grad_mixed[:, cols].astype(f32) * mixed[:, cols].astype(f32)
        high, low, _ = split_three(product)
        sums = nt(pick, high) + nt(pick, low)
        inner.append(jnp.concatenate([sums[0:1], sums[1:2]], axis=1))
        lines.append(jnp.concatenate([lse[2 * p : 2 * p + 1], lse[2 * p + 1 : 2 * p + 2]], axis=1))
        dq_acc[p] = jnp.zeros((128, 2 * ROWS), f32)

    def step(j, carry):
        at = pl.multiple_of(j * ROWS, ROWS)
        keys = at + lax.broadcasted_iota(jnp.int32, (ROWS, 2 * ROWS), 0)
        seen = (keys >= starts) & (keys <= rows)
        here = pl.ds(at, ROWS)
        for p in range(3):
            cols = slice(p * 128, (p + 1) * 128)
            kb = k[here, cols]
            scores = jnp.where(seen, nt(kb, queries[p]) - lines[p], masked_score)
            probs = jnp.exp(scores)
            grad_probs = nt(v[here, cols], grads[p])
            grad_scores = (probs * (grad_probs - inner[p])).astype(bf16)
            dv_acc[here, cols] += nn(probs.astype(bf16), grads[p])
            dk_acc[here, cols] += nn(grad_scores, queries[p])
            dq_acc[p] += tn(kb, grad_scores)
        return carry

    lax.fori_loop(first // ROWS, i + 1, step, 0)
    for p in range(3):
        dq[:, p * 128 : (p + 1) * 128] = (one_above(dq_acc[p]) * 0.125).astype(bf16)

    @pl.when(i == count - 1)
    def _():
        dk[...] = dk_acc[...].astype(bf16)
        dv[...] = dv_acc[...].astype(bf16)


def attend_back(lens, q, k, v, mixed, lse, grad_mixed):
    seq = q.shape[0]
    count = seq // ROWS
    row = pl.BlockSpec((ROWS, PAIR), lambda i, s: (i, 0))
    wide = jax.ShapeDtypeStruct((seq, PAIR), bf16)
    return pl.pallas_call(
        attend_back_kernel,
        grid_spec=pltpu.PrefetchScalarGridSpec(
            num_scalar_prefetch=1,
            grid=(count,),
            in_specs=[
                row,
                full((seq, PAIR)),
                full((seq, PAIR)),
                row,
                pl.BlockSpec((8, ROWS), lambda i, s: (0, i)),
                row,
            ],
            out_specs=[row, full((seq, PAIR)), full((seq, PAIR))],
            scratch_shapes=[
                pltpu.VMEM((seq, PAIR), f32),
                pltpu.VMEM((seq, PAIR), f32),
                pltpu.VMEM((3, 128, 2 * ROWS), f32),
            ],
        ),
        out_shape=[wide, wide, wide],
        compiler_params=params(),
        cost_estimate=cost(40),
        name="attend_back",
    )(lens, q, k, v, mixed, lse, grad_mixed)


def feed_kernel(
    small, tok, pas, vec, mine, cot, wo_mine, wo_other, w1, w2,
    out_chip, second_keep, grad_second, grad_mixed, sums, mid_send, mid_keep, *rest,
):
    results, rest = (rest[:4], rest[4:]) if small else (rest[:2], rest[2:])
    (
        wo, other, up, down, gup, gdown, go, core_out, core_in, far_out, far_in, ga_out, ga_in, oc_out, oc_in,
        g_send, g_keep, g_in, s_core, r_core, s_far, r_far, s_ga, r_ga, s_oc, r_oc, s_x, r_x, s_m, r_m,
    ) = rest
    step = pl.program_id(0)
    half = core_out.shape[0]
    t, dp = lax.axis_index("tensor"), lax.axis_index("dp")
    core, side = t % 2, t // 2
    near, far = side * 2 + (1 - core), (1 - side) * 2 + core
    z, column = (dp // 2, dp % 2) if small else (0, 0)
    far_x = z * 2 + 1 - column

    def copy(src, dst, s_sem, r_sem, j, to):
        return pltpu.make_async_remote_copy(
            src_ref=src.at[j],
            dst_ref=dst.at[j],
            send_sem=s_sem.at[j],
            recv_sem=r_sem.at[j],
            device_id={"tensor": to},
            device_id_type=MESH,
        )

    core_copy = lambda j: copy(core_out, core_in, s_core, r_core, j, near)
    far_copy = lambda j: copy(far_out, far_in, s_far, r_far, j, far)
    ga_copy = lambda j: copy(ga_out, ga_in, s_ga, r_ga, j, near)
    oc_copy = lambda j: copy(oc_out, oc_in, s_oc, r_oc, j, near)

    def x_copy(slot):
        return pltpu.make_async_remote_copy(
            src_ref=g_send.at[slot],
            dst_ref=g_in.at[slot],
            send_sem=s_x.at[slot],
            recv_sem=r_x.at[slot],
            device_id={"dp": far_x},
            device_id_type=MESH,
        )

    def mixed_copy(block):
        rows = pl.ds(pl.multiple_of(block * ROWS, ROWS), ROWS)
        return pltpu.make_async_remote_copy(
            src_ref=mine.at[rows],
            dst_ref=other.at[rows],
            send_sem=s_m.at[block],
            recv_sem=r_m.at[block],
            device_id={"tensor": near},
            device_id_type=MESH,
        )

    barrier = pltpu.get_barrier_semaphore()

    @pl.when(step == 0)
    def _():
        for to in (near, far):
            pl.semaphore_signal(barrier, inc=1, device_id={"tensor": to}, device_id_type=MESH)
        if small:
            pl.semaphore_signal(barrier, inc=1, device_id={"dp": far_x}, device_id_type=MESH)
        for h in range(2):
            for m in range(2):
                rows, cols = slice(h * SIDE, (h + 1) * SIDE), slice(m * PAIR, (m + 1) * PAIR)
                wo[rows, cols] = wo_mine[h, m]
                wo[PAIR + h * SIDE : PAIR + (h + 1) * SIDE, cols] = wo_other[h, m]
        for r in range(4):
            for m in range(2):
                rows, cols = slice(r * SIDE, (r + 1) * SIDE), slice(m * PAIR, (m + 1) * PAIR)
                up[rows, cols] = w1[0, 2 * r + m]
                down[rows, cols] = w2[0, 2 * r + m]
        pl.semaphore_wait(barrier, 3 if small else 2)
        for j in range(half):
            mixed_copy(core * half + j).start()
            mixed_copy((1 - core) * half + j).start()
        gup[...] = jnp.zeros_like(gup)
        gdown[...] = jnp.zeros_like(gdown)
        go[...] = jnp.zeros_like(go)
        sums[...] = jnp.zeros_like(sums)

    @pl.when(step < 2 * half)
    def _():
        j = step // 2
        owner = jnp.where(step % 2 == 0, 1 - core, core)
        here = pl.ds(pl.multiple_of((owner * half + j) * ROWS, ROWS), ROWS)
        first = embedded(tok[...], pas[...], vec[...])
        mixed_copy(owner * half + j).wait_recv()
        second = first + nn(jnp.concatenate([mine[here, :], other[here, :]], axis=1), wo[...])
        hat, _ = hat_of(second)
        low = (hat * vec[PASSES + 2 : PASSES + 3] + vec[PASSES + 3 : PASSES + 4]).astype(bf16)
        upper = nn(low, up[...])
        square = upper * upper
        bent = jnp.tanh(gelu_coef * upper * (1.0 + 0.044715 * square))
        act = (0.5 * upper * (1.0 + bent)).astype(bf16)
        slope = 0.5 * (1.0 + bent) + (0.5 * gelu_coef) * upper * (1.0 - bent * bent) * (
            1.0 + (3 * 0.044715) * square
        )
        grad_act = nt(cot[...], down[...])
        grad_upper = (grad_act * slope).astype(bf16)
        part = nt(grad_upper, up[...])

        @pl.when(step % 2 == 0)
        def _():
            core_out[j] = part.astype(bf16)
            core_copy(j).start()

        @pl.when(step % 2 == 1)
        def _():
            core_copy(j).wait_recv()
            far_out[j] = (part + core_in[j].astype(f32)).astype(bf16)
            far_copy(j).start()
            second_keep[pl.ds(pl.multiple_of(j * ROWS, ROWS), ROWS), :] = second

        gup[...] += tn(low, grad_upper)
        gdown[...] += tn(act, cot[...])
        out_part = nn(act, down[...])

        @pl.when(step % 2 == 0)
        def _():
            oc_out[j] = out_part.astype(bf16)
            oc_copy(j).start()

        @pl.when(step % 2 == 1)
        def _():
            oc_copy(j).wait_recv()
            out_chip[...] = (out_part + oc_in[j].astype(f32)).astype(bf16)

    @pl.when(step == 2 * half - 1)
    def _():
        for r in range(4):
            for m in range(2):
                rows, cols = slice(r * SIDE, (r + 1) * SIDE), slice(m * PAIR, (m + 1) * PAIR)
                for at, total in ((8, gup), (16, gdown)):
                    pair = at + 2 * r + m
                    slot, place = (pair // 6 - 1) * 3 + pair % 3, pair // 3 % 2
                    value = total[rows, cols].astype(bf16)
                    kept, sent, n = (mid_keep, mid_send, slot) if slot < 3 else (g_keep, g_send, slot - 3)

                    @pl.when(column == place)
                    def _():
                        kept[n] = value

                    @pl.when(column != place)
                    def _():
                        sent[n] = value
        if small:
            for n in range(6):
                x_copy(n).start()

    def through_out(grad, block):
        here = pl.ds(pl.multiple_of(block * ROWS, ROWS), ROWS)
        grad_mixed[here, :] = nt(grad, wo[:PAIR, :]).astype(bf16)
        go[...] += tn(mine[here, :], grad)

    @pl.when((step >= 2 * half) & (step < 3 * half))
    def _():
        j = step - 2 * half
        hat, root = hat_of(second_keep[pl.ds(pl.multiple_of(j * ROWS, ROWS), ROWS), :])
        far_copy(j).wait_recv()
        grad = far_out[j].astype(f32) + far_in[j].astype(f32)
        result = cot[...].astype(f32) + norm_back(hat, root, grad, vec[PASSES + 2 : PASSES + 3])
        low = result.astype(bf16)
        ga_out[j] = low
        ga_copy(j).start()
        grad_second[...] = result
        sums[0:1] += jnp.sum(grad * hat, axis=0, keepdims=True)
        sums[1:2] += jnp.sum(grad, axis=0, keepdims=True)
        through_out(low, core * half + j)

    @pl.when(step > 2 * half)
    def _():
        j = step - 2 * half - 1
        ga_copy(j).wait_recv()
        through_out(ga_in[j], (1 - core) * half + j)

    @pl.when(step == 3 * half)
    def _():
        at = pl.multiple_of(side * SIDE, SIDE)
        for m in range(2):
            value = go[pl.ds(at, SIDE), m * PAIR : (m + 1) * PAIR].astype(bf16)

            @pl.when(column == 0)
            def _():
                mid_keep[m] = value

            @pl.when(column != 0)
            def _():
                mid_send[m] = value

        for j in range(half):
            core_copy(j).wait_send()
            oc_copy(j).wait_send()
            mixed_copy(j).wait_send()
            mixed_copy(half + j).wait_send()
            far_copy(j).wait_send()
            ga_copy(j).wait_send()
        if small:
            for n in range(6):
                x_copy(n).wait_send()
                x_copy(n).wait_recv()
                value = (g_keep[n].astype(f32) + g_in[n].astype(f32)).astype(bf16)
                for turn in range(4):

                    @pl.when(lax.rem(z + turn, 4) == n // 3 + 2)
                    def _():
                        results[turn][n % 3] = value
        else:
            results[0][...] = g_send[...]
            results[1][...] = g_keep[...]


def feed(small, tokens, passes, vec, mine, cotangent, pairs, wo_other):
    seq = tokens.shape[0]
    half = seq // ROWS // 2

    def block(i):
        core = lax.axis_index("tensor") % 2
        work = jnp.minimum(i, 2 * half - 1)
        owner = jnp.where(work % 2 == 0, 1 - core, core)
        return owner * half + work // 2

    def cot_block(i):
        core = lax.axis_index("tensor") % 2
        return jnp.where(i < 2 * half, block(i), core * half + jnp.minimum(i - 2 * half, half - 1))

    side = lambda: lax.axis_index("tensor") // 2
    row = lambda n: pl.BlockSpec((ROWS, n), lambda i: (block(i), 0))
    keep = pl.BlockSpec((ROWS, D), lambda i: (jnp.minimum(i // 2, half - 1), 0))
    last = pl.BlockSpec((ROWS, D), lambda i: (jnp.clip(i - 2 * half, 0, half - 1), 0))
    rows = lambda kind: jax.ShapeDtypeStruct((seq // 2, D), kind)
    gr = lambda n: jax.ShapeDtypeStruct((n, SIDE, PAIR), bf16)
    ends = [(3, SIDE, PAIR)] * 4 if small else [(6, SIDE, PAIR)] * 2
    buffer = pltpu.VMEM((half, ROWS, D), bf16)
    dma = pltpu.SemaphoreType.DMA((half,))
    return pl.pallas_call(
        functools.partial(feed_kernel, small),
        grid=(3 * half + 1,),
        in_specs=[
            row(D),
            pl.BlockSpec((1, ROWS), lambda i: (0, block(i))),
            full((16, D)),
            full((seq, PAIR)),
            pl.BlockSpec((ROWS, D), lambda i: (cot_block(i), 0)),
            pl.BlockSpec((2, 2, SIDE, PAIR), lambda i: (0, 3, 0, 0)),
            full(wo_other.shape),
            pl.BlockSpec((1, 8, SIDE, PAIR), lambda i: (side(), 1, 0, 0)),
            pl.BlockSpec((1, 8, SIDE, PAIR), lambda i: (side(), 2, 0, 0)),
        ],
        out_specs=[
            keep,
            full((seq // 2, D)),
            last,
            full((seq, PAIR)),
            full((8, D)),
            full((3, SIDE, PAIR)),
            full((3, SIDE, PAIR)),
        ]
        + [full(shape) for shape in ends],
        scratch_shapes=[
            pltpu.VMEM((D, D), bf16),
            pltpu.VMEM((seq, PAIR), bf16),
            pltpu.VMEM((D, D), bf16),
            pltpu.VMEM((D, D), bf16),
            pltpu.VMEM((D, D), f32),
            pltpu.VMEM((D, D), f32),
            pltpu.VMEM((PAIR, D), f32),
        ]
        + [buffer] * 8
        + [pltpu.VMEM((6, SIDE, PAIR), bf16)] * 3
        + [dma] * 8
        + [pltpu.SemaphoreType.DMA((6,))] * 2
        + [pltpu.SemaphoreType.DMA((2 * half,))] * 2,
        out_shape=[
            rows(bf16),
            rows(f32),
            rows(f32),
            jax.ShapeDtypeStruct((seq, PAIR), bf16),
            jax.ShapeDtypeStruct((8, D), f32),
            gr(3),
            gr(3),
        ]
        + [jax.ShapeDtypeStruct(shape, bf16) for shape in ends],
        compiler_params=params(collective_id=1, has_side_effects=True),
        cost_estimate=cost(50),
        name="feed_forward",
    )(tokens, passes, vec, mine, cotangent, pairs, wo_other, pairs, pairs)


def qkv_grads_kernel(place, norm, dq, dk, dv, mid_send, mid_keep, g_send, g_keep, acc):
    i = pl.program_id(0)

    @pl.when(i == 0)
    def _():
        acc[...] = jnp.zeros_like(acc)

    mine = [jnp.where(place[1] == 0, grad[:, :SIDE], grad[:, SIDE:]) for grad in (dq, dk, dv)]
    acc[...] += tn(jnp.concatenate(mine, axis=1), norm[...])

    @pl.when(i == pl.num_programs(0) - 1)
    def _():
        for m in range(3):
            g_send[3 + m] = mid_send[m]
            g_keep[3 + m] = mid_keep[m]
        for x in range(3):
            for m in range(2):
                value = acc[x * SIDE : (x + 1) * SIDE, m * PAIR : (m + 1) * PAIR].astype(bf16)
                slot, column = (2 * x + m) % 3, (2 * x + m) // 3

                @pl.when(place[2] == column)
                def _():
                    g_keep[slot] = value

                @pl.when(place[2] != column)
                def _():
                    g_send[slot] = value


def qkv_grads(place, norm, dq, dk, dv, mid_send, mid_keep):
    seq = norm.shape[0]
    row = lambda n: pl.BlockSpec((WIDE, n), lambda i, s: (i, 0))
    return pl.pallas_call(
        qkv_grads_kernel,
        grid_spec=pltpu.PrefetchScalarGridSpec(
            num_scalar_prefetch=1,
            grid=(seq // WIDE,),
            in_specs=[row(D), row(PAIR), row(PAIR), row(PAIR)] + [full((3, SIDE, PAIR))] * 2,
            out_specs=[full((6, SIDE, PAIR)), full((6, SIDE, PAIR))],
            scratch_shapes=[pltpu.VMEM((3 * SIDE, D), f32)],
        ),
        out_shape=[jax.ShapeDtypeStruct((6, SIDE, PAIR), bf16)] * 2,
        compiler_params=params(),
        cost_estimate=cost(8),
        name="qkv_grads",
    )(place, norm, dq, dk, dv, mid_send, mid_keep)


CHUNK = SIDE // 2
CHUNKS = 12


def last_kernel(
    small, dq, dk, dv, cat, tok, pas, vec, grad_second, sums_two, second, chip, far, g_send, g_keep, output, input_grad, *rest
):
    if small:
        late, vec_sum = rest[:2]
        rest = rest[2:]
        (
            core_out, core_in, sums, core_sums, x_in, z_in, z_out, up_in, v_out, v_in,
            s_core, r_core, s_sum, r_sum, s_x, r_x, s_z, r_z, s_up, r_up, s_v, r_v, ready, s_own, s_res, r_res,
        ) = rest
    else:
        (
            vec_sum, core_out, core_in, sums, core_sums, s_core, r_core, s_sum, r_sum, ready, s_own, s_res, r_res,
        ) = rest
    i = pl.program_id(0)
    half = core_out.shape[0]
    t, dp = lax.axis_index("tensor"), lax.axis_index("dp")
    core, side = t % 2, t // 2
    near = side * 2 + (1 - core)
    z, column = (dp // 2, dp % 2) if small else (0, 0)
    far_x = z * 2 + 1 - column
    peers = [lax.rem(dp + k, 8) for k in range(1, 8)]

    def copy(src, dst, s_sem, r_sem, to):
        return pltpu.make_async_remote_copy(
            src_ref=src, dst_ref=dst, send_sem=s_sem, recv_sem=r_sem, device_id=to, device_id_type=MESH
        )

    core_copy = lambda j: copy(core_out.at[j], core_in.at[j], s_core.at[j], r_core.at[j], {"tensor": near})
    sum_copy = lambda: copy(sums, core_sums, s_sum, r_sum, {"tensor": near})

    def rows_at(n, j, owner):
        rows = pl.ds(pl.multiple_of((owner * half + j) * ROWS, ROWS), ROWS)
        return (output, input_grad)[n].at[rows]

    own_result = lambda n, j: pltpu.make_async_copy(ready.at[n, j], rows_at(n, j, core), s_own.at[n, j])
    near_result = lambda n, j, owner: copy(
        ready.at[n, j], rows_at(n, j, owner), s_res.at[n, j], r_res.at[n, j], {"tensor": near}
    )

    def part_of(ref, k):
        return ref.at[k // 2, pl.ds((k % 2) * CHUNK, CHUNK)]

    x_copy = lambda k: copy(part_of(g_send, k), x_in.at[k], s_x.at[k], r_x.at[k], {"dp": far_x})
    z_copy = lambda k: copy(z_out.at[k], z_in.at[k], s_z.at[k], r_z.at[k], {"dp": dp - 2})
    up_copy = lambda k: copy(z_out.at[k], up_in.at[k - 6], s_up.at[k - 6], r_up.at[k - 6], {"dp": dp + 2})
    v_copy = lambda n: copy(v_out.at[peers[n]], v_in.at[dp], s_v.at[n], r_v.at[dp], {"dp": peers[n]})
    barrier = pltpu.get_barrier_semaphore()

    @pl.when(i == 0)
    def _():
        pl.semaphore_signal(barrier, inc=1, device_id={"tensor": near}, device_id_type=MESH)
        if small:
            for peer in peers:
                pl.semaphore_signal(barrier, inc=1, device_id={"dp": peer}, device_id_type=MESH)
            late[...] = jnp.zeros_like(late)
        sums[...] = jnp.zeros_like(sums)
        sums[PASSES + 2 : PASSES + 4] = sums_two[0:2]
        pl.semaphore_wait(barrier, 8 if small else 1)
        if small:
            for k in range(6):
                x_copy(k).start()

    @pl.when(i < 2 * half)
    def _():
        part = nt(dq[...], cat[0]) + nt(dk[...], cat[1]) + nt(dv[...], cat[2])

        @pl.when(i < half)
        def _():
            core_out[i] = part.astype(bf16)
            core_copy(i).start()

        @pl.when(i >= half)
        def _():
            j = i - half
            hat, root = hat_of(embedded(tok[...], pas[...], vec[...]))
            core_copy(j).wait_recv()
            grad = part + core_in[j].astype(f32)
            result = grad_second[...] + norm_back(hat, root, grad, vec[PASSES : PASSES + 1])
            ready[0, j] = (second[...] + (chip[...].astype(f32) + far[...].astype(f32))).astype(bf16)
            ready[1, j] = result.astype(bf16)
            for n in range(2):
                own_result(n, j).start()
                near_result(n, j, core).start()
            chosen = one_hot(pas[...])
            high, mid, _ = split_three(result)
            sums[...] += nn(chosen, high) + nn(chosen, mid)
            sums[PASSES : PASSES + 1] += jnp.sum(grad * hat, axis=0, keepdims=True)
            sums[PASSES + 1 : PASSES + 2] += jnp.sum(grad, axis=0, keepdims=True)

    @pl.when(i == 2 * half - 1)
    def _():
        sum_copy().start()

    if small:

        def term_of(k):
            rows = pl.ds(pl.multiple_of((k % 2) * CHUNK, 16), CHUNK)

            @pl.when(k < 6)
            def _():
                x_copy(k).wait_recv()

            @pl.when(k >= 6)
            def _():
                x_in[k] = g_send[k // 2, rows, :]

            return g_keep[k // 2, rows, :].astype(f32) + x_in[k].astype(f32)

        def keep_late(k, pair, total):
            late[pair, pl.ds(pl.multiple_of((k % 2) * CHUNK, 16), CHUNK), :] = total

        def pass_on(k):
            total = term_of(k)

            @pl.when(z < 3)
            def _():
                z_copy(k).wait_recv()

            below = jnp.where(z < 3, z_in[k].astype(f32), 0.0)
            passed = total + below

            @pl.when((z > 1) | ((z == 1) & (k < 6)))
            def _():
                z_out[k] = passed.astype(bf16)
                z_copy(k).start()

            @pl.when(z == 0)
            def _():
                keep_late(k, k // 2, passed)

            @pl.when((z == 1) & (k >= 6))
            def _():
                up_copy(k).wait_recv()
                keep_late(k, k // 2 - 3, passed + up_in[k - 6].astype(f32))

        for n in range(2):
            at = 2 * (i - 1 - (3 - z)) + n
            k = jnp.where(at < 4, at + 6, jnp.where(at < 10, at - 4, at))

            @pl.when((at >= 0) & (at < CHUNKS) & ((z > 0) | (k < 6)))
            def _(k=k):
                pass_on(k)

        @pl.when((i >= 1) & (i < 7) & (z == 0))
        def _():
            z_out[i + 5] = term_of(i + 5).astype(bf16)
            up_copy(i + 5).start()

    @pl.when(i == 2 * half + 1)
    def _():
        sum_copy().wait_recv()
        total = sums[...] + core_sums[...]
        if small:
            wide = D // 8
            for d in range(8):
                v_out[d, :, 0:wide] = total[:, d * wide : (d + 1) * wide]
                v_out[d, :, wide:] = jnp.zeros((16, 128 - wide), f32)
            for n in range(7):
                v_copy(n).start()
        else:
            vec_sum[...] = total

    @pl.when(i == pl.num_programs(0) - 1)
    def _():
        for j in range(half):
            core_copy(j).wait_send()
            for n in range(2):
                own_result(n, j).wait()
                near_result(n, j, core).wait_send()
                near_result(n, j, 1 - core).wait_recv()
        sum_copy().wait_send()
        if small:
            for peer in peers:
                copy(v_out.at[0], v_in.at[peer], s_v.at[0], r_v.at[peer], {"dp": far_x}).wait_recv()
            v_in[dp] = v_out[dp]
            total = v_in[0]
            for d in range(1, 8):
                total = total + v_in[d]
            vec_sum[...] = total
            for n in range(7):
                v_copy(n).wait_send()
            for k in range(CHUNKS):
                if k < 6:
                    x_copy(k).wait_send()
                    pl.when(z > 0)(z_copy(k).wait_send)
                else:
                    pl.when(z > 1)(z_copy(k).wait_send)
                    pl.when(z == 0)(up_copy(k).wait_send)


def last(
    small, dq, dk, dv, cat, tokens, passes, vec, grad_second, sums_two, second, chip, far, g_send, g_keep
):
    seq = dq.shape[0]
    half = seq // ROWS // 2
    core = lambda: lax.axis_index("tensor") % 2

    def block(i):
        work = jnp.minimum(i, 2 * half - 1)
        return lax.rem(work + (1 - core()) * half, 2 * half)

    own = lambda i: jnp.clip(i - half, 0, half - 1)
    row = pl.BlockSpec((ROWS, PAIR), lambda i: (block(i), 0))
    mine = pl.BlockSpec((ROWS, D), lambda i: (own(i), 0))
    dma = pltpu.SemaphoreType.DMA
    out_specs = [pl.BlockSpec(memory_space=pl.ANY)] * 2
    out_shape = [jax.ShapeDtypeStruct((seq, D), bf16)] * 2
    scratch = [
        pltpu.VMEM((half, ROWS, D), bf16),
        pltpu.VMEM((half, ROWS, D), bf16),
        pltpu.VMEM((16, D), f32),
        pltpu.VMEM((16, D), f32),
    ]
    sems = [dma((half,)), dma((half,)), dma, dma]
    if small:
        out_specs += [full((3, SIDE, PAIR)), full((16, 128))]
        out_shape += [
            jax.ShapeDtypeStruct((3, SIDE, PAIR), f32),
            jax.ShapeDtypeStruct((16, 128), f32),
        ]
        scratch += [pltpu.VMEM((CHUNKS, CHUNK, PAIR), bf16)] * 3
        scratch += [pltpu.VMEM((6, CHUNK, PAIR), bf16)]
        scratch += [pltpu.VMEM((8, 16, 128), f32)] * 2
        sems += [dma((6,))] * 2 + [dma((CHUNKS,))] * 2 + [dma((6,))] * 2 + [dma((7,)), dma((8,))]
    else:
        out_specs += [full((16, D))]
        out_shape += [jax.ShapeDtypeStruct((16, D), f32)]
    scratch_more = [pltpu.VMEM((2, half, ROWS, D), bf16)] + [dma((2, half))] * 3
    return pl.pallas_call(
        functools.partial(last_kernel, small),
        grid=(2 * half + 3 if small else 2 * half + 2,),
        in_specs=[
            row,
            row,
            row,
            full(cat.shape),
            pl.BlockSpec((ROWS, D), lambda i: (core() * half + own(i), 0)),
            pl.BlockSpec((1, ROWS), lambda i: (0, core() * half + own(i))),
            full((16, D)),
            mine,
            full((8, D)),
            mine,
            mine,
            mine,
            full(g_send.shape),
            full(g_keep.shape),
        ],
        out_specs=out_specs,
        out_shape=out_shape,
        scratch_shapes=scratch + sems + scratch_more,
        compiler_params=params(collective_id=2, has_side_effects=True),
        cost_estimate=cost(30),
        name="last",
    )(dq, dk, dv, cat, tokens, passes, vec, grad_second, sums_two, second, chip, far, g_send, g_keep)


def precondition(grad, weight, left, right, left_root, right_root):
    high = lax.Precision.HIGHEST
    left_new = decay * left + (1.0 - decay) * jnp.einsum(
        "...ij,...kj->...ik", grad, grad, precision=high
    )
    right_new = decay * right + (1.0 - decay) * jnp.einsum(
        "...ji,...jk->...ik", grad, grad, precision=high
    )
    half = jnp.einsum("...ij,...jk->...ik", left_root, grad, precision=high)
    step = jnp.einsum("...ij,...jk->...ik", half, right_root, precision=high)
    return (left_new, right_new, step, weight - rate_matrix * step)


def two_part(value):
    high = value.astype(bf16)
    return high, (value - high.astype(f32)).astype(bf16)


def dot_three(dot, a, b):
    return dot(a[0], b[0]) + (dot(a[0], b[1]) + dot(a[1], b[0]))


def renew_kernel(place, late, own, one, two, three, weight, left, right, left_root, right_root, left_new, right_new, step, new):
    early = own[0].astype(f32) + one[0].astype(f32) + two[0].astype(f32) + three[0].astype(f32)
    z = place[3]
    both = late[0] + jnp.where(z > 1, early, 0.0)
    for n in range(2):
        grad = both[:, n * SIDE : (n + 1) * SIDE]
        grad = two_part(jnp.where(z == 0, grad.T, grad))
        left_new[0, n] = decay * left[0, n] + (1.0 - decay) * dot_three(nt, grad, grad)
        right_new[0, n] = decay * right[0, n] + (1.0 - decay) * dot_three(tn, grad, grad)
        half = dot_three(nn, two_part(left_root[0, n]), grad)
        value = dot_three(nn, two_part(half), two_part(right_root[0, n]))
        step[0, n] = value
        new[0, n] = weight[0, n] - rate_matrix * value


def renew(place, late, own, far, weight, left, right, left_root, right_root):
    pair = pl.BlockSpec((1, SIDE, PAIR), lambda i, s: (i, 0, 0))
    slot = pl.BlockSpec((1, 2, SIDE, SIDE), lambda i, s: (0, i, 0, 0))
    return pl.pallas_call(
        renew_kernel,
        grid_spec=pltpu.PrefetchScalarGridSpec(
            num_scalar_prefetch=1,
            grid=(3,),
            in_specs=[pair] * 5 + [slot] * 5,
            out_specs=[slot] * 4,
        ),
        out_shape=[jax.ShapeDtypeStruct(weight.shape, f32)] * 4,
        compiler_params=params(),
        cost_estimate=cost(5),
        name="renew",
    )(place, late, own, *far, weight, left, right, left_root, right_root)


def to_pairs(blocks):
    n = blocks.shape[0] // 2
    return blocks.reshape(n, 2, SIDE, SIDE).transpose(0, 2, 1, 3).reshape(n, SIDE, PAIR)


def from_pairs(pairs):
    n = pairs.shape[0]
    return pairs.reshape(n, SIDE, 2, SIDE).transpose(0, 2, 1, 3).reshape(2 * n, SIDE, SIDE)


def swap(value, bit):
    return lax.ppermute(value, "tensor", [(t, t ^ bit) for t in range(NT)])


def hop_x(value):
    return lax.ppermute(value, "dp", [(d, d ^ 1) for d in range(8)])


def hop_z(value, turn, ends):
    pairs = [(d, (d + 2 * turn) % 8) for d in range(8) if (d // 2 + turn) % 4 in ends]
    return lax.ppermute(value, "dp", pairs)


def tie(*values):
    return lax.optimization_barrier(values)


def on_device(
    tokens,
    pass_ids,
    doc_lengths,
    cotangent,
    block_weights,
    vector_params,
    vector_moment,
    block_left,
    block_right,
    block_left_root,
    block_right_root,
):
    t, dp = lax.axis_index("tensor"), lax.axis_index("dp")
    core, side = t % 2, t // 2
    n_dp = lax.axis_size("dp")
    small = n_dp == 8
    z, column = (dp // 2, dp % 2) if small else (0, 0)
    place = jnp.stack([core, side, jnp.asarray(column), jnp.asarray(z)]).astype(jnp.int32)
    lens = doc_lengths[0]
    seq = tokens.shape[0]
    passes = pass_ids.reshape(1, seq)
    total_blocks = (D // SIDE) * (4 + 2 * (FF // D))
    slots = block_weights.shape[1] * n_dp

    if small:
        pairs, wo_other, vec, norm, q, k, v, cat = gather(block_weights, vector_params, tokens, passes)
    else:
        every = lax.all_gather(block_weights.astype(bf16), "dp", axis=1, tiled=True)[0]
        near = to_pairs(every[:total_blocks])
        far = swap(near, 2)
        pairs = jnp.where(side == 0, jnp.stack([near, far]), jnp.stack([far, near]))
        vec = lax.all_gather(vector_params, "dp", axis=1, tiled=True)
        vec = jnp.pad(vec, ((0, 16 - vec.shape[0]), (0, 0)))
        wo_other = swap(pairs[:, 6:8], 1)
        norm, q, k, v, cat = project(tokens, passes, vec, pairs)
    mine, lse = attend(lens, q, k, v)
    out_chip, second, grad_second, grad_mixed, sums_two, mid_send, mid_keep, *ends = feed(
        small, tokens, passes, vec, mine, cotangent, pairs, wo_other
    )
    out_far = swap(out_chip, 2)
    if small:
        far = [hop_z(ends[turn], turn, (2, 3)) for turn in (1, 2, 3)]
        mid_send = hop_x(mid_send)
    dq, dk, dv = attend_back(lens, q, k, v, mine, lse, grad_mixed)
    g_send, g_keep = qkv_grads(place, norm, dq, dk, dv, mid_send, mid_keep)
    if small:
        *far, out_far, g_send = tie(*far, out_far, g_send)
    output, input_grad, *sums = last(
        small, dq, dk, dv, cat, tokens, passes, vec, grad_second, sums_two, second, out_chip, out_far, g_send, g_keep
    )
    if small:
        late, vector_sum = sums
        left_new, right_new, step, weight_new = renew(
            place, late, ends[0], far, block_weights, block_left, block_right, block_left_root, block_right_root
        )
        vector_grad = vector_sum[: PASSES + 4, : vector_params.shape[1]]
    else:
        vector_part = sums[0][: PASSES + 4]
        send, keep = ends
        rest = jnp.stack(
            [
                jnp.concatenate([mid_keep, keep]).reshape(3, 3, SIDE, PAIR),
                jnp.concatenate([mid_send, send]).reshape(3, 3, SIDE, PAIR),
            ],
            axis=1,
        )
        grad_qkv = from_pairs(jnp.concatenate([g_keep[:3], g_send[:3]], axis=0)).swapaxes(1, 2)
        grad_rest = from_pairs(rest.reshape(18, SIDE, PAIR))
        spare = jnp.zeros((slots - total_blocks, SIDE, SIDE), bf16)
        grad_blocks = jnp.concatenate([grad_qkv, grad_rest, spare], axis=0)[None].astype(f32)
        owned = lax.psum_scatter(grad_blocks, "dp", scatter_dimension=1, tiled=True)
        vector_grad = lax.psum_scatter(vector_part, "dp", scatter_dimension=1, tiled=True)
        left_new, right_new, step, weight_new = precondition(
            owned, block_weights, block_left, block_right, block_left_root, block_right_root
        )
    moment_new = decay * vector_moment + (1.0 - decay) * vector_grad * vector_grad
    vector_new = vector_params - rate_vector * vector_grad / (jnp.sqrt(moment_new) + moment_eps)
    return (
        output,
        input_grad,
        left_new,
        right_new,
        step,
        weight_new,
        vector_grad,
        moment_new,
        vector_new,
    )


def solution(mesh):
    rows, line = P("dp", None), P(None, "dp")
    block = P("tensor", "dp", None, None)
    return jax.shard_map(
        on_device,
        mesh=mesh,
        in_specs=(rows, P("dp"), rows, rows, block, line, line, block, block, block, block),
        out_specs=(rows, rows, block, block, block, block, line, line, line),
        check_vma=False,
    )
```

```python
import functools

import jax
import jax.numpy as jnp
from jax import lax
from jax.experimental import pallas as pl
from jax.experimental.pallas import tpu as pltpu
from jax.sharding import PartitionSpec as P

D = 768
HD = 64
FF = 3072
PASSES = 5
SIDE = 192
PAIR = 2 * SIDE
ROWS = 256
WIDE = 512
DOCS = 8
NT = 4

norm_eps = 1e-05
moment_eps = 1e-08
rate_matrix = 0.03
rate_vector = 0.2
decay = 0.5
gelu_coef = 0.7978845608028654
masked_score = -1e30
f32 = jnp.float32
bf16 = jnp.bfloat16
MESH = pl.DeviceIdType.MESH


def nn(a, b):
    return lax.dot_general(a, b, (((1,), (0,)), ((), ())), preferred_element_type=f32)


def nt(a, b):
    return lax.dot_general(a, b, (((1,), (1,)), ((), ())), preferred_element_type=f32)


def tn(a, b):
    return lax.dot_general(a, b, (((0,), (0,)), ((), ())), preferred_element_type=f32)


def split_three(value):
    high = value.astype(bf16)
    rest = value - high.astype(f32)
    mid = rest.astype(bf16)
    return high, mid, (rest - mid.astype(f32)).astype(bf16)


def one_hot(pass_row):
    kinds = lax.broadcasted_iota(jnp.int32, (16, pass_row.shape[1]), 0)
    return (kinds == pass_row).astype(f32).astype(bf16)


def embedded(tokens, pass_row, vec):
    chosen = jnp.concatenate([one_hot(pass_row)] * 3, axis=0)
    return tokens.astype(f32) + tn(chosen, jnp.concatenate(split_three(vec), axis=0))


def hat_of(hidden):
    mean = jnp.mean(hidden, axis=-1, keepdims=True)
    center = hidden - mean
    spread = jnp.mean(center * center, axis=-1, keepdims=True)
    root = lax.rsqrt(spread + norm_eps)
    return center * root, root


def norm_back(hat, root, grad, gain):
    scaled = grad * gain
    first = jnp.mean(scaled, axis=-1, keepdims=True)
    second = jnp.mean(scaled * hat, axis=-1, keepdims=True)
    return root * (scaled - first - hat * second)


def params(mebibytes=56, **kw):
    return pltpu.CompilerParams(vmem_limit_bytes=mebibytes * 1024 * 1024, **kw)


def cost(micros):
    return pl.CostEstimate(flops=int(micros * 1.1e9), bytes_accessed=int(micros * 1e6), transcendentals=0)


def full(shape):
    return pl.BlockSpec(shape, lambda *_: (0,) * len(shape))


def gather_kernel(
    own, vec_own, tokens, passes,
    all_pairs, wo_other, vec_out, norm, q, k_out, v, cat,
    pack, vec_pack, vec_land, wq, tok, norm_s, qkv_s, cat_s, *sems,
):
    (
        s_z1, r_z1, s_x1, r_x1, s_y1, r_y1, s_d1, r_d1, s_l, r_l, s_r, r_r, s_x2, r_x2, s_y2, r_y2, s_v, r_v, s_c, r_c,
        s_out, s_cat, s_tok, loc,
    ) = sems
    dp, t = lax.axis_index("dp"), lax.axis_index("tensor")
    z, x = dp // 2, dp % 2
    y, core = t // 2, t % 2
    far_x, far_y, near = z * 2 + (1 - x), (1 - y) * 2 + core, y * 2 + (1 - core)

    barrier = pltpu.get_barrier_semaphore()
    peers = [lax.rem(dp + n, 8) for n in range(1, 8)]
    for peer in peers:
        pl.semaphore_signal(barrier, inc=1, device_id={"dp": peer}, device_id_type=MESH)
    for to in (far_y, near):
        pl.semaphore_signal(barrier, inc=1, device_id={"tensor": to}, device_id_type=MESH)

    tok_copy = pltpu.make_async_copy(tokens, tok, s_tok)
    tok_copy.start()
    for m in range(3):
        pair = jnp.concatenate([own[0, 2 * m], own[0, 2 * m + 1]], axis=1).astype(bf16)
        pack[m] = pair

        @pl.when(z == 0)
        def _():
            wq[y, 3 * x + m] = pair

    vec_pack[...] = jnp.zeros_like(vec_pack)
    vec_pack[0 : PASSES + 4, 0 : D // 8] = vec_own[...]
    pl.semaphore_wait(barrier, 9)

    started = []

    def send(src, dst, s_sem, r_sem, to, cond=None):
        copy = pltpu.make_async_remote_copy(
            src_ref=src, dst_ref=dst, send_sem=s_sem, recv_sem=r_sem, device_id=to, device_id_type=MESH
        )
        started.append((cond, copy))
        if cond is None:
            copy.start()
        else:
            pl.when(cond)(copy.start)

    def arrived(dst, r_sem, cond=None):
        copy = pltpu.make_async_remote_copy(
            src_ref=dst, dst_ref=dst, send_sem=loc, recv_sem=r_sem, device_id={"dp": far_x}, device_id_type=MESH
        )
        if cond is None:
            copy.wait_recv()
        else:
            pl.when(cond)(copy.wait_recv)

    to_x, to_y, to_left, to_right = {"dp": far_x}, {"tensor": far_y}, {"dp": dp - 2}, {"dp": dp + 2}
    half = SIDE // 2

    def piece(side, column, k):
        return wq.at[side, 3 * column + k // 2, pl.ds((k % 2) * half, half)]

    def at_z(d, m):
        return all_pairs.at[y, 3 * dp + 6 * d + m]

    own_copy = pltpu.make_async_copy(pack, all_pairs.at[y, pl.ds(3 * dp, 3)], loc)
    pl.when(z > 0)(own_copy.start)

    for m in range(3):
        send(pack.at[m], at_z(0, m), s_l.at[0, m], r_l.at[0, m], to_left, z > 0)
    for n, peer in enumerate(peers):
        send(vec_pack, vec_land.at[dp], s_v.at[n], r_v.at[dp], {"dp": peer})
    for m in range(3):
        send(pack.at[m], at_z(0, m), s_x2.at[z, m], r_x2.at[z, m], to_x, z > m)

    def diagonal(k):
        arrived(piece(y, 1 - x, k), r_x1.at[k])
        send(piece(y, 1 - x, k), piece(y, 1 - x, k), s_d1.at[k], r_d1.at[k], to_y)

    def from_right(d, m):
        arrived(at_z(d, m), r_l.at[d - 1, m], z + d < 4)
        if d < 3:
            send(at_z(d, m), at_z(d, m), s_l.at[d, m], r_l.at[d, m], to_left, (z + d < 4) & (z > 0))

    def from_left(d, m):
        arrived(at_z(-d, m), r_r.at[d - 1, m], z - d > 0)
        if d == 1:
            send(at_z(-d, m), at_z(-d, m), s_r.at[1, m], r_r.at[1, m], to_right, (z - d > 0) & (z < 3))

    def along_x(d, m, cond):
        send(at_z(d, m), at_z(d, m), s_x2.at[z + d, m], r_x2.at[z + d, m], to_x, cond)

    for k in range(6):
        arrived(piece(y, x, k), r_z1.at[k], z > 0)
        send(piece(y, x, k), piece(y, x, k), s_z1.at[k], r_z1.at[k], to_right, z < 3)
        send(piece(y, x, k), piece(y, x, k), s_x1.at[k], r_x1.at[k], to_x)
        send(piece(y, x, k), piece(y, x, k), s_y1.at[k], r_y1.at[k], to_y)
        if k == 5:
            for m in range(3):
                send(pack.at[m], at_z(0, m), s_r.at[0, m], r_r.at[0, m], to_right, (z > 0) & (z < 3))
                send(pack.at[m], at_z(0, m), s_x2.at[z, m], r_x2.at[z, m], to_x, (z > 0) & (z <= m))
        if k >= 1:
            diagonal(k - 1)
        if k % 2 == 1:
            from_right(1, k // 2)
    diagonal(5)
    pl.when(z > 0)(own_copy.wait)
    for m in range(3):
        along_x(1, m, z + 1 < 4)
    for m in range(3):
        from_left(1, m)
        along_x(-1, m, z - 1 > 0)
        from_right(2, m)
        along_x(2, m, z + 2 < 4)
    for k in range(6):
        arrived(piece(1 - y, x, k), r_y1.at[k])
        arrived(piece(1 - y, 1 - x, k), r_d1.at[k])
    for peer in peers:
        arrived(vec_land.at[peer], r_v.at[peer])
    vec_land[dp] = vec_pack[...]
    vec = jnp.concatenate([vec_land[d][:, : D // 8] for d in range(8)], axis=1)
    vec_out[...] = vec
    for n in range(3):
        for i in range(4):
            at = (i % 2) * SIDE
            parts = [wq[h, 2 * n + i // 2][:, at : at + SIDE] for h in range(2)]
            cat_s[n, i * SIDE : (i + 1) * SIDE, :] = jnp.concatenate(parts, axis=1)
    writes = [pltpu.make_async_copy(cat_s, cat, s_cat)]
    writes[0].start()
    tok_copy.wait()

    def rows_of(b):
        rows = slice(b * WIDE, (b + 1) * WIDE)
        hat, _ = hat_of(embedded(tok[rows, :], passes[:, rows], vec))
        low = (hat * vec[PASSES : PASSES + 1] + vec[PASSES + 1 : PASSES + 2]).astype(bf16)
        norm_s[rows, :] = low
        writes.append(pltpu.make_async_copy(norm_s.at[rows, :], norm.at[rows, :], s_out.at[b, 3]))
        writes[-1].start()
        for n, out in enumerate((q, k_out, v)):
            qkv_s[n, rows, :] = nn(low, cat_s[n]).astype(bf16)
            writes.append(pltpu.make_async_copy(qkv_s.at[n, rows, :], out.at[rows, :], s_out.at[b, n]))
            writes[-1].start()

    count = tok.shape[0] // WIDE
    for b in range(count):
        rows_of(b)
        if b == 0:
            for m in range(3):
                from_right(3, m)
                along_x(3, m, z + 3 < 4)
        if b == 1:
            for m in range(3):
                from_left(2, m)
                along_x(-2, m, z - 2 > 0)
        if b == 2:
            for m in range(2):
                ref = all_pairs.at[y, 6 + m]
                arrived(ref, r_x2.at[1, m], x == 1)
                send(ref, ref, s_y2.at[m], r_y2.at[m], to_y)
                send(ref, wo_other.at[y, m], s_c.at[0, m], r_c.at[y, m], {"tensor": near})
    for m in range(2):
        ref = all_pairs.at[1 - y, 6 + m]
        arrived(ref, r_y2.at[m])
        send(ref, wo_other.at[1 - y, m], s_c.at[1, m], r_c.at[1 - y, m], {"tensor": near})
    for w in range(1, 4):
        for m in range(3):
            ref = all_pairs.at[y, 6 * w + 3 * (1 - x) + m]
            if w == 1 and m < 2:
                arrived(ref, r_x2.at[w, m], x == 0)
            else:
                arrived(ref, r_x2.at[w, m])
    for h in range(2):
        for m in range(2):
            arrived(wo_other.at[h, m], r_c.at[h, m])
    for copy in writes:
        copy.wait()
    for cond, copy in started:
        if cond is None:
            copy.wait_send()
        else:
            pl.when(cond)(copy.wait_send)


def gather(block_weights, vector_params, tokens, passes):
    seq = tokens.shape[0]
    dma = pltpu.SemaphoreType.DMA
    sizes = [(6,)] * 8 + [(3, 3)] * 2 + [(2, 3)] * 2 + [(4, 3)] * 2 + [(2,)] * 2 + [(7,), (8,)] + [(2, 2)] * 2
    sizes += [(seq // WIDE, 4)]
    vmem, far = pl.BlockSpec(memory_space=pltpu.VMEM), pl.BlockSpec(memory_space=pl.ANY)
    wide = jax.ShapeDtypeStruct((seq, PAIR), bf16)
    return pl.pallas_call(
        gather_kernel,
        in_specs=[vmem, vmem, far, vmem],
        out_specs=[far, far, vmem, far, far, far, far, far],
        out_shape=[
            jax.ShapeDtypeStruct((2, 24, SIDE, PAIR), bf16),
            jax.ShapeDtypeStruct((2, 2, SIDE, PAIR), bf16),
            jax.ShapeDtypeStruct((16, D), f32),
            jax.ShapeDtypeStruct((seq, D), bf16),
            wide,
            wide,
            wide,
            jax.ShapeDtypeStruct((3, D, PAIR), bf16),
        ],
        scratch_shapes=[
            pltpu.VMEM((3, SIDE, PAIR), bf16),
            pltpu.VMEM((16, 128), f32),
            pltpu.VMEM((8, 16, 128), f32),
            pltpu.VMEM((2, 6, SIDE, PAIR), bf16),
            pltpu.VMEM((seq, D), bf16),
            pltpu.VMEM((seq, D), bf16),
            pltpu.VMEM((3, seq, PAIR), bf16),
            pltpu.VMEM((3, D, PAIR), bf16),
        ]
        + [dma(size) for size in sizes]
        + [dma] * 3,
        compiler_params=params(collective_id=0, has_side_effects=True),
        cost_estimate=cost(60),
        name="gather",
    )(block_weights, vector_params, tokens, passes)


def project_kernel(tok, pas, vec, wq, norm, q, k, v, cat):
    @pl.when(pl.program_id(0) == 0)
    def _():
        for x in range(3):
            for i in range(4):
                at = (i % 2) * SIDE
                parts = [wq[h, 2 * x + i // 2][:, at : at + SIDE] for h in range(2)]
                cat[x, i * SIDE : (i + 1) * SIDE, :] = jnp.concatenate(parts, axis=1)

    first = embedded(tok[...], pas[...], vec[...])
    hat, _ = hat_of(first)
    low = (hat * vec[PASSES : PASSES + 1] + vec[PASSES + 1 : PASSES + 2]).astype(bf16)
    norm[...] = low
    for x, out in enumerate((q, k, v)):
        out[...] = nn(low, cat[x]).astype(bf16)


def project(tokens, passes, vec, wq):
    seq = tokens.shape[0]
    row = lambda n: pl.BlockSpec((WIDE, n), lambda i: (i, 0))
    wide = jax.ShapeDtypeStruct((seq, PAIR), bf16)
    return pl.pallas_call(
        project_kernel,
        grid=(seq // WIDE,),
        in_specs=[
            row(D),
            pl.BlockSpec((1, WIDE), lambda i: (0, i)),
            full((16, D)),
            full((2, 6, SIDE, PAIR)),
        ],
        out_specs=[row(D), row(PAIR), row(PAIR), row(PAIR), full((3, D, PAIR))],
        out_shape=[
            jax.ShapeDtypeStruct((seq, D), bf16),
            wide,
            wide,
            wide,
            jax.ShapeDtypeStruct((3, D, PAIR), bf16),
        ],
        compiler_params=params(),
        cost_estimate=cost(16),
        name="project",
    )(tokens, passes, vec, wq)


def doc_state(lens, base):
    rows = base + lax.broadcasted_iota(jnp.int32, (1, ROWS), 1)
    rows = jnp.concatenate([rows, rows], axis=1)
    begin = jnp.int32(0)
    first = jnp.int32(0)
    starts = jnp.zeros((1, 2 * ROWS), jnp.int32)
    for c in range(DOCS):
        starts = jnp.where(rows >= begin, begin, starts)
        first = jnp.where(base >= begin, begin, first)
        begin = begin + lens[c]
    return rows, starts, first


def two_heads(block):
    left = lax.broadcasted_iota(jnp.int32, block.shape, 1) < HD
    none = jnp.zeros_like(block)
    return jnp.concatenate([jnp.where(left, block, none), jnp.where(left, none, block)], axis=0)


def one_above(both):
    return jnp.concatenate([both[:HD, :ROWS], both[HD:, ROWS:]], axis=0).T


def attend_kernel(lens, q, k, v, out, lse, acc):
    i = pl.program_id(0)
    base = i * ROWS
    rows, starts, first = doc_state(lens, base)
    pairs = [two_heads(q[:, p * 128 : (p + 1) * 128] * bf16(0.125)) for p in range(3)]
    for p in range(3):
        acc[p] = jnp.zeros((128, 2 * ROWS), f32)

    def step(j, carry):
        at = pl.multiple_of(j * ROWS, ROWS)
        keys = at + lax.broadcasted_iota(jnp.int32, (ROWS, 2 * ROWS), 0)
        seen = (keys >= starts) & (keys <= rows)
        here = pl.ds(at, ROWS)
        head = lambda p: slice(p * 128, (p + 1) * 128)
        scores = [jnp.where(seen, nt(k[here, head(p)], pairs[p]), masked_score) for p in range(3)]
        state = []
        for p in range(3):
            before, total = carry[2 * p], carry[2 * p + 1]
            now = jnp.maximum(before, jnp.max(scores[p], axis=0, keepdims=True))
            probs = jnp.exp(scores[p] - now)
            fade = jnp.exp(before - now)
            state += [now, total * fade + jnp.sum(probs, axis=0, keepdims=True)]
            acc[p] = acc[p] * fade + tn(v[here, head(p)], probs.astype(bf16))
        return tuple(state)

    zero = jnp.zeros((1, 2 * ROWS), f32)
    state = lax.fori_loop(first // ROWS, i + 1, step, (zero + masked_score, zero) * 3)
    lines = []
    for p in range(3):
        top, total = state[2 * p], state[2 * p + 1]
        out[:, p * 128 : (p + 1) * 128] = one_above(acc[p] / total).astype(bf16)
        line = top + jnp.log(total)
        lines += [line[:, :ROWS], line[:, ROWS:]]
    lse[...] = jnp.concatenate(lines + lines[:2], axis=0)


def attend(lens, q, k, v):
    seq = q.shape[0]
    row = pl.BlockSpec((ROWS, PAIR), lambda i, s: (i, 0))
    return pl.pallas_call(
        attend_kernel,
        grid_spec=pltpu.PrefetchScalarGridSpec(
            num_scalar_prefetch=1,
            grid=(seq // ROWS,),
            in_specs=[row, full((seq, PAIR)), full((seq, PAIR))],
            out_specs=[row, pl.BlockSpec((8, ROWS), lambda i, s: (0, i))],
            scratch_shapes=[
                pltpu.VMEM((3, 128, 2 * ROWS), f32),
            ],
        ),
        out_shape=[
            jax.ShapeDtypeStruct((seq, PAIR), bf16),
            jax.ShapeDtypeStruct((8, seq), f32),
        ],
        compiler_params=params(),
        cost_estimate=cost(30),
        name="attend",
    )(lens, q, k, v)


def attend_back_kernel(
    lens, q, k, v, mixed, lse, grad_mixed, dq, dk, dv, dk_acc, dv_acc, dq_acc
):
    i = pl.program_id(0)
    count = pl.num_programs(0)
    base = i * ROWS

    @pl.when(i == 0)
    def _():
        dk_acc[...] = jnp.zeros_like(dk_acc)
        dv_acc[...] = jnp.zeros_like(dv_acc)

    rows, starts, first = doc_state(lens, base)
    heads = lax.broadcasted_iota(jnp.int32, (8, 128), 0)
    lanes = lax.broadcasted_iota(jnp.int32, (8, 128), 1)
    pick = (lanes // HD == heads).astype(f32).astype(bf16)
    queries, grads, inner, lines = [], [], [], []
    for p in range(3):
        cols = slice(p * 128, (p + 1) * 128)
        queries.append(two_heads(q[:, cols] * bf16(0.125)))
        grads.append(two_heads(grad_mixed[:, cols]))
        product = grad_mixed[:, cols].astype(f32) * mixed[:, cols].astype(f32)
        high, low, _ = split_three(product)
        sums = nt(pick, high) + nt(pick, low)
        inner.append(jnp.concatenate([sums[0:1], sums[1:2]], axis=1))
        lines.append(jnp.concatenate([lse[2 * p : 2 * p + 1], lse[2 * p + 1 : 2 * p + 2]], axis=1))
        dq_acc[p] = jnp.zeros((128, 2 * ROWS), f32)

    def step(j, carry):
        at = pl.multiple_of(j * ROWS, ROWS)
        keys = at + lax.broadcasted_iota(jnp.int32, (ROWS, 2 * ROWS), 0)
        seen = (keys >= starts) & (keys <= rows)
        here = pl.ds(at, ROWS)
        for p in range(3):
            cols = slice(p * 128, (p + 1) * 128)
            kb = k[here, cols]
            scores = jnp.where(seen, nt(kb, queries[p]) - lines[p], masked_score)
            probs = jnp.exp(scores)
            grad_probs = nt(v[here, cols], grads[p])
            grad_scores = (probs * (grad_probs - inner[p])).astype(bf16)
            dv_acc[here, cols] += nn(probs.astype(bf16), grads[p])
            dk_acc[here, cols] += nn(grad_scores, queries[p])
            dq_acc[p] += tn(kb, grad_scores)
        return carry

    lax.fori_loop(first // ROWS, i + 1, step, 0)
    for p in range(3):
        dq[:, p * 128 : (p + 1) * 128] = (one_above(dq_acc[p]) * 0.125).astype(bf16)

    @pl.when(i == count - 1)
    def _():
        dk[...] = dk_acc[...].astype(bf16)
        dv[...] = dv_acc[...].astype(bf16)


def attend_back(lens, q, k, v, mixed, lse, grad_mixed):
    seq = q.shape[0]
    count = seq // ROWS
    row = pl.BlockSpec((ROWS, PAIR), lambda i, s: (i, 0))
    wide = jax.ShapeDtypeStruct((seq, PAIR), bf16)
    return pl.pallas_call(
        attend_back_kernel,
        grid_spec=pltpu.PrefetchScalarGridSpec(
            num_scalar_prefetch=1,
            grid=(count,),
            in_specs=[
                row,
                full((seq, PAIR)),
                full((seq, PAIR)),
                row,
                pl.BlockSpec((8, ROWS), lambda i, s: (0, i)),
                row,
            ],
            out_specs=[row, full((seq, PAIR)), full((seq, PAIR))],
            scratch_shapes=[
                pltpu.VMEM((seq, PAIR), f32),
                pltpu.VMEM((seq, PAIR), f32),
                pltpu.VMEM((3, 128, 2 * ROWS), f32),
            ],
        ),
        out_shape=[wide, wide, wide],
        compiler_params=params(),
        cost_estimate=cost(40),
        name="attend_back",
    )(lens, q, k, v, mixed, lse, grad_mixed)


def feed_kernel(
    small, tok, pas, vec, mine, cot, wo_mine, wo_other, w1, w2,
    out_chip, second_keep, grad_second, grad_mixed, sums, mid_send, mid_keep, *rest,
):
    results, rest = (rest[:4], rest[4:]) if small else (rest[:2], rest[2:])
    (
        wo, other, up, down, gup, gdown, go, core_out, core_in, far_out, far_in, ga_out, ga_in, oc_out, oc_in,
        g_send, g_keep, g_in, s_core, r_core, s_far, r_far, s_ga, r_ga, s_oc, r_oc, s_x, r_x, s_m, r_m,
    ) = rest
    step = pl.program_id(0)
    half = core_out.shape[0]
    t, dp = lax.axis_index("tensor"), lax.axis_index("dp")
    core, side = t % 2, t // 2
    near, far = side * 2 + (1 - core), (1 - side) * 2 + core
    z, column = (dp // 2, dp % 2) if small else (0, 0)
    far_x = z * 2 + 1 - column

    def copy(src, dst, s_sem, r_sem, j, to):
        return pltpu.make_async_remote_copy(
            src_ref=src.at[j],
            dst_ref=dst.at[j],
            send_sem=s_sem.at[j],
            recv_sem=r_sem.at[j],
            device_id={"tensor": to},
            device_id_type=MESH,
        )

    core_copy = lambda j: copy(core_out, core_in, s_core, r_core, j, near)
    far_copy = lambda j: copy(far_out, far_in, s_far, r_far, j, far)
    ga_copy = lambda j: copy(ga_out, ga_in, s_ga, r_ga, j, near)
    oc_copy = lambda j: copy(oc_out, oc_in, s_oc, r_oc, j, near)

    def x_copy(slot):
        return pltpu.make_async_remote_copy(
            src_ref=g_send.at[slot],
            dst_ref=g_in.at[slot],
            send_sem=s_x.at[slot],
            recv_sem=r_x.at[slot],
            device_id={"dp": far_x},
            device_id_type=MESH,
        )

    def mixed_copy(block):
        rows = pl.ds(pl.multiple_of(block * ROWS, ROWS), ROWS)
        return pltpu.make_async_remote_copy(
            src_ref=mine.at[rows],
            dst_ref=other.at[rows],
            send_sem=s_m.at[block],
            recv_sem=r_m.at[block],
            device_id={"tensor": near},
            device_id_type=MESH,
        )

    barrier = pltpu.get_barrier_semaphore()

    @pl.when(step == 0)
    def _():
        for to in (near, far):
            pl.semaphore_signal(barrier, inc=1, device_id={"tensor": to}, device_id_type=MESH)
        if small:
            pl.semaphore_signal(barrier, inc=1, device_id={"dp": far_x}, device_id_type=MESH)
        for h in range(2):
            for m in range(2):
                rows, cols = slice(h * SIDE, (h + 1) * SIDE), slice(m * PAIR, (m + 1) * PAIR)
                wo[rows, cols] = wo_mine[h, m]
                wo[PAIR + h * SIDE : PAIR + (h + 1) * SIDE, cols] = wo_other[h, m]
        for r in range(4):
            for m in range(2):
                rows, cols = slice(r * SIDE, (r + 1) * SIDE), slice(m * PAIR, (m + 1) * PAIR)
                up[rows, cols] = w1[0, 2 * r + m]
                down[rows, cols] = w2[0, 2 * r + m]
        pl.semaphore_wait(barrier, 3 if small else 2)
        for j in range(half):
            mixed_copy(core * half + j).start()
            mixed_copy((1 - core) * half + j).start()
        gup[...] = jnp.zeros_like(gup)
        gdown[...] = jnp.zeros_like(gdown)
        go[...] = jnp.zeros_like(go)
        sums[...] = jnp.zeros_like(sums)

    @pl.when(step < 2 * half)
    def _():
        j = step // 2
        owner = jnp.where(step % 2 == 0, 1 - core, core)
        here = pl.ds(pl.multiple_of((owner * half + j) * ROWS, ROWS), ROWS)
        first = embedded(tok[...], pas[...], vec[...])
        mixed_copy(owner * half + j).wait_recv()
        second = first + nn(jnp.concatenate([mine[here, :], other[here, :]], axis=1), wo[...])
        hat, _ = hat_of(second)
        low = (hat * vec[PASSES + 2 : PASSES + 3] + vec[PASSES + 3 : PASSES + 4]).astype(bf16)
        upper = nn(low, up[...])
        square = upper * upper
        bent = jnp.tanh(gelu_coef * upper * (1.0 + 0.044715 * square))
        act = (0.5 * upper * (1.0 + bent)).astype(bf16)
        slope = 0.5 * (1.0 + bent) + (0.5 * gelu_coef) * upper * (1.0 - bent * bent) * (
            1.0 + (3 * 0.044715) * square
        )
        grad_act = nt(cot[...], down[...])
        grad_upper = (grad_act * slope).astype(bf16)
        part = nt(grad_upper, up[...])

        @pl.when(step % 2 == 0)
        def _():
            core_out[j] = part.astype(bf16)
            core_copy(j).start()

        @pl.when(step % 2 == 1)
        def _():
            core_copy(j).wait_recv()
            far_out[j] = (part + core_in[j].astype(f32)).astype(bf16)
            far_copy(j).start()
            second_keep[pl.ds(pl.multiple_of(j * ROWS, ROWS), ROWS), :] = second

        gup[...] += tn(low, grad_upper)
        gdown[...] += tn(act, cot[...])
        out_part = nn(act, down[...])

        @pl.when(step % 2 == 0)
        def _():
            oc_out[j] = out_part.astype(bf16)
            oc_copy(j).start()

        @pl.when(step % 2 == 1)
        def _():
            oc_copy(j).wait_recv()
            out_chip[...] = (out_part + oc_in[j].astype(f32)).astype(bf16)

    @pl.when(step == 2 * half - 1)
    def _():
        for r in range(4):
            for m in range(2):
                rows, cols = slice(r * SIDE, (r + 1) * SIDE), slice(m * PAIR, (m + 1) * PAIR)
                for at, total in ((8, gup), (16, gdown)):
                    pair = at + 2 * r + m
                    slot, place = (pair // 6 - 1) * 3 + pair % 3, pair // 3 % 2
                    value = total[rows, cols].astype(bf16)
                    kept, sent, n = (mid_keep, mid_send, slot) if slot < 3 else (g_keep, g_send, slot - 3)

                    @pl.when(column == place)
                    def _():
                        kept[n] = value

                    @pl.when(column != place)
                    def _():
                        sent[n] = value
        if small:
            for n in range(6):
                x_copy(n).start()

    def through_out(grad, block):
        here = pl.ds(pl.multiple_of(block * ROWS, ROWS), ROWS)
        grad_mixed[here, :] = nt(grad, wo[:PAIR, :]).astype(bf16)
        go[...] += tn(mine[here, :], grad)

    @pl.when((step >= 2 * half) & (step < 3 * half))
    def _():
        j = step - 2 * half
        hat, root = hat_of(second_keep[pl.ds(pl.multiple_of(j * ROWS, ROWS), ROWS), :])
        far_copy(j).wait_recv()
        grad = far_out[j].astype(f32) + far_in[j].astype(f32)
        result = cot[...].astype(f32) + norm_back(hat, root, grad, vec[PASSES + 2 : PASSES + 3])
        low = result.astype(bf16)
        ga_out[j] = low
        ga_copy(j).start()
        grad_second[...] = result
        sums[0:1] += jnp.sum(grad * hat, axis=0, keepdims=True)
        sums[1:2] += jnp.sum(grad, axis=0, keepdims=True)
        through_out(low, core * half + j)

    @pl.when(step > 2 * half)
    def _():
        j = step - 2 * half - 1
        ga_copy(j).wait_recv()
        through_out(ga_in[j], (1 - core) * half + j)

    @pl.when(step == 3 * half)
    def _():
        at = pl.multiple_of(side * SIDE, SIDE)
        for m in range(2):
            value = go[pl.ds(at, SIDE), m * PAIR : (m + 1) * PAIR].astype(bf16)

            @pl.when(column == 0)
            def _():
                mid_keep[m] = value

            @pl.when(column != 0)
            def _():
                mid_send[m] = value

        for j in range(half):
            core_copy(j).wait_send()
            oc_copy(j).wait_send()
            mixed_copy(j).wait_send()
            mixed_copy(half + j).wait_send()
            far_copy(j).wait_send()
            ga_copy(j).wait_send()
        if small:
            for n in range(6):
                x_copy(n).wait_send()
                x_copy(n).wait_recv()
                value = (g_keep[n].astype(f32) + g_in[n].astype(f32)).astype(bf16)
                for turn in range(4):

                    @pl.when(lax.rem(z + turn, 4) == n // 3 + 2)
                    def _():
                        results[turn][n % 3] = value
        else:
            results[0][...] = g_send[...]
            results[1][...] = g_keep[...]


def feed(small, tokens, passes, vec, mine, cotangent, pairs, wo_other):
    seq = tokens.shape[0]
    half = seq // ROWS // 2

    def block(i):
        core = lax.axis_index("tensor") % 2
        work = jnp.minimum(i, 2 * half - 1)
        owner = jnp.where(work % 2 == 0, 1 - core, core)
        return owner * half + work // 2

    def cot_block(i):
        core = lax.axis_index("tensor") % 2
        return jnp.where(i < 2 * half, block(i), core * half + jnp.minimum(i - 2 * half, half - 1))

    side = lambda: lax.axis_index("tensor") // 2
    row = lambda n: pl.BlockSpec((ROWS, n), lambda i: (block(i), 0))
    keep = pl.BlockSpec((ROWS, D), lambda i: (jnp.minimum(i // 2, half - 1), 0))
    last = pl.BlockSpec((ROWS, D), lambda i: (jnp.clip(i - 2 * half, 0, half - 1), 0))
    rows = lambda kind: jax.ShapeDtypeStruct((seq // 2, D), kind)
    gr = lambda n: jax.ShapeDtypeStruct((n, SIDE, PAIR), bf16)
    ends = [(3, SIDE, PAIR)] * 4 if small else [(6, SIDE, PAIR)] * 2
    buffer = pltpu.VMEM((half, ROWS, D), bf16)
    dma = pltpu.SemaphoreType.DMA((half,))
    return pl.pallas_call(
        functools.partial(feed_kernel, small),
        grid=(3 * half + 1,),
        in_specs=[
            row(D),
            pl.BlockSpec((1, ROWS), lambda i: (0, block(i))),
            full((16, D)),
            full((seq, PAIR)),
            pl.BlockSpec((ROWS, D), lambda i: (cot_block(i), 0)),
            pl.BlockSpec((2, 2, SIDE, PAIR), lambda i: (0, 3, 0, 0)),
            full(wo_other.shape),
            pl.BlockSpec((1, 8, SIDE, PAIR), lambda i: (side(), 1, 0, 0)),
            pl.BlockSpec((1, 8, SIDE, PAIR), lambda i: (side(), 2, 0, 0)),
        ],
        out_specs=[
            keep,
            full((seq // 2, D)),
            last,
            full((seq, PAIR)),
            full((8, D)),
            full((3, SIDE, PAIR)),
            full((3, SIDE, PAIR)),
        ]
        + [full(shape) for shape in ends],
        scratch_shapes=[
            pltpu.VMEM((D, D), bf16),
            pltpu.VMEM((seq, PAIR), bf16),
            pltpu.VMEM((D, D), bf16),
            pltpu.VMEM((D, D), bf16),
            pltpu.VMEM((D, D), f32),
            pltpu.VMEM((D, D), f32),
            pltpu.VMEM((PAIR, D), f32),
        ]
        + [buffer] * 8
        + [pltpu.VMEM((6, SIDE, PAIR), bf16)] * 3
        + [dma] * 8
        + [pltpu.SemaphoreType.DMA((6,))] * 2
        + [pltpu.SemaphoreType.DMA((2 * half,))] * 2,
        out_shape=[
            rows(bf16),
            rows(f32),
            rows(f32),
            jax.ShapeDtypeStruct((seq, PAIR), bf16),
            jax.ShapeDtypeStruct((8, D), f32),
            gr(3),
            gr(3),
        ]
        + [jax.ShapeDtypeStruct(shape, bf16) for shape in ends],
        compiler_params=params(collective_id=1, has_side_effects=True),
        cost_estimate=cost(50),
        name="feed_forward",
    )(tokens, passes, vec, mine, cotangent, pairs, wo_other, pairs, pairs)


def qkv_grads_kernel(place, norm, dq, dk, dv, mid_send, mid_keep, g_send, g_keep, acc):
    i = pl.program_id(0)

    @pl.when(i == 0)
    def _():
        acc[...] = jnp.zeros_like(acc)

    mine = [jnp.where(place[1] == 0, grad[:, :SIDE], grad[:, SIDE:]) for grad in (dq, dk, dv)]
    acc[...] += tn(jnp.concatenate(mine, axis=1), norm[...])

    @pl.when(i == pl.num_programs(0) - 1)
    def _():
        for m in range(3):
            g_send[3 + m] = mid_send[m]
            g_keep[3 + m] = mid_keep[m]
        for x in range(3):
            for m in range(2):
                value = acc[x * SIDE : (x + 1) * SIDE, m * PAIR : (m + 1) * PAIR].astype(bf16)
                slot, column = (2 * x + m) % 3, (2 * x + m) // 3

                @pl.when(place[2] == column)
                def _():
                    g_keep[slot] = value

                @pl.when(place[2] != column)
                def _():
                    g_send[slot] = value


def qkv_grads(place, norm, dq, dk, dv, mid_send, mid_keep):
    seq = norm.shape[0]
    row = lambda n: pl.BlockSpec((WIDE, n), lambda i, s: (i, 0))
    return pl.pallas_call(
        qkv_grads_kernel,
        grid_spec=pltpu.PrefetchScalarGridSpec(
            num_scalar_prefetch=1,
            grid=(seq // WIDE,),
            in_specs=[row(D), row(PAIR), row(PAIR), row(PAIR)] + [full((3, SIDE, PAIR))] * 2,
            out_specs=[full((6, SIDE, PAIR)), full((6, SIDE, PAIR))],
            scratch_shapes=[pltpu.VMEM((3 * SIDE, D), f32)],
        ),
        out_shape=[jax.ShapeDtypeStruct((6, SIDE, PAIR), bf16)] * 2,
        compiler_params=params(),
        cost_estimate=cost(8),
        name="qkv_grads",
    )(place, norm, dq, dk, dv, mid_send, mid_keep)


CHUNK = SIDE // 2
CHUNKS = 12
TAKEN = (
    ((8, 4), (9, 12)),
    ((5, 1), (6, 3), (7, 4), (8, 7), (9, 12)),
    ((3, 1), (4, 3), (5, 4), (6, 5), (7, 6), (8, 9), (9, 12)),
    ((1, 2), (2, 3), (3, 5), (4, 6), (5, 8), (6, 10), (7, 12)),
)


def last_kernel(
    small, dq, dk, dv, cat, tok, pas, vec, grad_second, sums_two, second, chip, far, g_send, g_keep, output, input_grad, *rest
):
    if small:
        late, vec_sum = rest[:2]
        rest = rest[2:]
        (
            core_out, core_in, sums, core_sums, x_in, z_in, z_out, up_in, v_out, v_in,
            s_core, r_core, s_sum, r_sum, s_x, r_x, s_z, r_z, s_up, r_up, s_v, r_v, ready, s_own, s_res, r_res,
        ) = rest
    else:
        (
            vec_sum, core_out, core_in, sums, core_sums, s_core, r_core, s_sum, r_sum, ready, s_own, s_res, r_res,
        ) = rest
    i = pl.program_id(0)
    half = core_out.shape[0]
    t, dp = lax.axis_index("tensor"), lax.axis_index("dp")
    core, side = t % 2, t // 2
    near = side * 2 + (1 - core)
    z, column = (dp // 2, dp % 2) if small else (0, 0)
    far_x = z * 2 + 1 - column
    peers = [lax.rem(dp + k, 8) for k in range(1, 8)]

    def copy(src, dst, s_sem, r_sem, to):
        return pltpu.make_async_remote_copy(
            src_ref=src, dst_ref=dst, send_sem=s_sem, recv_sem=r_sem, device_id=to, device_id_type=MESH
        )

    core_copy = lambda j: copy(core_out.at[j], core_in.at[j], s_core.at[j], r_core.at[j], {"tensor": near})
    sum_copy = lambda: copy(sums, core_sums, s_sum, r_sum, {"tensor": near})

    def rows_at(n, j, owner):
        rows = pl.ds(pl.multiple_of((owner * half + j) * ROWS, ROWS), ROWS)
        return (output, input_grad)[n].at[rows]

    own_result = lambda n, j: pltpu.make_async_copy(ready.at[n, j], rows_at(n, j, core), s_own.at[n, j])
    near_result = lambda n, j, owner: copy(
        ready.at[n, j], rows_at(n, j, owner), s_res.at[n, j], r_res.at[n, j], {"tensor": near}
    )

    def part_of(ref, k):
        return ref.at[k // 2, pl.ds((k % 2) * CHUNK, CHUNK)]

    x_copy = lambda k: copy(part_of(g_send, k), x_in.at[k], s_x.at[k], r_x.at[k], {"dp": far_x})
    z_copy = lambda k: copy(z_out.at[k], z_in.at[k], s_z.at[k], r_z.at[k], {"dp": dp - 2})
    up_copy = lambda k: copy(z_out.at[k], up_in.at[k - 6], s_up.at[k - 6], r_up.at[k - 6], {"dp": dp + 2})
    v_copy = lambda n: copy(v_out.at[peers[n]], v_in.at[dp], s_v.at[n], r_v.at[dp], {"dp": peers[n]})
    barrier = pltpu.get_barrier_semaphore()

    @pl.when(i == 0)
    def _():
        pl.semaphore_signal(barrier, inc=1, device_id={"tensor": near}, device_id_type=MESH)
        if small:
            for peer in peers:
                pl.semaphore_signal(barrier, inc=1, device_id={"dp": peer}, device_id_type=MESH)
            late[...] = jnp.zeros_like(late)
        sums[...] = jnp.zeros_like(sums)
        sums[PASSES + 2 : PASSES + 4] = sums_two[0:2]
        pl.semaphore_wait(barrier, 8 if small else 1)
        if small:
            for k in range(6):
                x_copy(k).start()

    @pl.when(i < 2 * half)
    def _():
        part = nt(dq[...], cat[0]) + nt(dk[...], cat[1]) + nt(dv[...], cat[2])

        @pl.when(i < half)
        def _():
            core_out[i] = part.astype(bf16)
            core_copy(i).start()

        @pl.when(i >= half)
        def _():
            j = i - half
            hat, root = hat_of(embedded(tok[...], pas[...], vec[...]))
            core_copy(j).wait_recv()
            grad = part + core_in[j].astype(f32)
            result = grad_second[...] + norm_back(hat, root, grad, vec[PASSES : PASSES + 1])
            ready[0, j] = (second[...] + (chip[...].astype(f32) + far[...].astype(f32))).astype(bf16)
            ready[1, j] = result.astype(bf16)
            for n in range(2):
                own_result(n, j).start()
                near_result(n, j, core).start()
            chosen = one_hot(pas[...])
            high, mid, _ = split_three(result)
            sums[...] += nn(chosen, high) + nn(chosen, mid)
            sums[PASSES : PASSES + 1] += jnp.sum(grad * hat, axis=0, keepdims=True)
            sums[PASSES + 1 : PASSES + 2] += jnp.sum(grad, axis=0, keepdims=True)

    @pl.when(i == 2 * half - 1)
    def _():
        sum_copy().start()

    @pl.when(i == 2 * half)
    def _():
        sum_copy().wait_recv()
        total = sums[...] + core_sums[...]
        if small:
            wide = D // 8
            for d in range(8):
                v_out[d, :, 0:wide] = total[:, d * wide : (d + 1) * wide]
                v_out[d, :, wide:] = jnp.zeros((16, 128 - wide), f32)
            for n in range(7):
                v_copy(n).start()
        else:
            vec_sum[...] = total

    if small:

        def term_of(k):
            rows = pl.ds(pl.multiple_of((k % 2) * CHUNK, 16), CHUNK)

            @pl.when(jnp.asarray(k) < 6)
            def _():
                x_copy(k).wait_recv()

            @pl.when(jnp.asarray(k) >= 6)
            def _():
                x_in[k] = g_send[k // 2, rows, :]

            return g_keep[k // 2, rows, :].astype(f32) + x_in[k].astype(f32)

        def keep_late(k, pair, total):
            late[pair, pl.ds(pl.multiple_of((k % 2) * CHUNK, 16), CHUNK), :] = total

        def pass_on(k):
            total = term_of(k)

            @pl.when(z < 3)
            def _():
                z_copy(k).wait_recv()

            below = jnp.where(z < 3, z_in[k].astype(f32), 0.0)
            passed = total + below

            @pl.when((z > 1) | ((z == 1) & (k < 6)))
            def _():
                z_out[k] = passed.astype(bf16)
                z_copy(k).start()

            @pl.when(z == 0)
            def _():
                keep_late(k, k // 2, passed)

            @pl.when((z == 1) & (k >= 6))
            def _():
                up_copy(k).wait_recv()
                keep_late(k, k // 2 - 3, passed + up_in[k - 6].astype(f32))

        def at_position(p, carry):
            k = jnp.where(p < 2, p + 6, jnp.where(p < 8, p - 2, p))

            @pl.when((z > 0) | (k < 6))
            def _():
                pass_on(k)

            return carry

        begin, end = jnp.int32(0), jnp.int32(0)
        for place, line in enumerate(TAKEN):
            for at, upto in line:
                begin = jnp.where((z == place) & (i > at), upto, begin)
                end = jnp.where((z == place) & (i >= at), upto, end)
        lax.fori_loop(begin, end, at_position, 0)

        @pl.when((i == 1) & (z == 0))
        def _():
            for k in range(6, CHUNKS):
                z_out[k] = term_of(k).astype(bf16)
                up_copy(k).start()

    @pl.when(i == pl.num_programs(0) - 1)
    def _():
        for j in range(half):
            core_copy(j).wait_send()
            for n in range(2):
                own_result(n, j).wait()
                near_result(n, j, core).wait_send()
                near_result(n, j, 1 - core).wait_recv()
        sum_copy().wait_send()
        if small:
            for peer in peers:
                copy(v_out.at[0], v_in.at[peer], s_v.at[0], r_v.at[peer], {"dp": far_x}).wait_recv()
            v_in[dp] = v_out[dp]
            total = v_in[0]
            for d in range(1, 8):
                total = total + v_in[d]
            vec_sum[...] = total
            for n in range(7):
                v_copy(n).wait_send()
            for k in range(CHUNKS):
                if k < 6:
                    x_copy(k).wait_send()
                    pl.when(z > 0)(z_copy(k).wait_send)
                else:
                    pl.when(z > 1)(z_copy(k).wait_send)
                    pl.when(z == 0)(up_copy(k).wait_send)


def last(
    small, dq, dk, dv, cat, tokens, passes, vec, grad_second, sums_two, second, chip, far, g_send, g_keep
):
    seq = dq.shape[0]
    half = seq // ROWS // 2
    core = lambda: lax.axis_index("tensor") % 2

    def block(i):
        work = jnp.minimum(i, 2 * half - 1)
        return lax.rem(work + (1 - core()) * half, 2 * half)

    own = lambda i: jnp.clip(i - half, 0, half - 1)
    row = pl.BlockSpec((ROWS, PAIR), lambda i: (block(i), 0))
    mine = pl.BlockSpec((ROWS, D), lambda i: (own(i), 0))
    dma = pltpu.SemaphoreType.DMA
    out_specs = [pl.BlockSpec(memory_space=pl.ANY)] * 2
    out_shape = [jax.ShapeDtypeStruct((seq, D), bf16)] * 2
    scratch = [
        pltpu.VMEM((half, ROWS, D), bf16),
        pltpu.VMEM((half, ROWS, D), bf16),
        pltpu.VMEM((16, D), f32),
        pltpu.VMEM((16, D), f32),
    ]
    sems = [dma((half,)), dma((half,)), dma, dma]
    if small:
        out_specs += [full((3, SIDE, PAIR)), full((16, 128))]
        out_shape += [
            jax.ShapeDtypeStruct((3, SIDE, PAIR), f32),
            jax.ShapeDtypeStruct((16, 128), f32),
        ]
        scratch += [pltpu.VMEM((CHUNKS, CHUNK, PAIR), bf16)] * 3
        scratch += [pltpu.VMEM((6, CHUNK, PAIR), bf16)]
        scratch += [pltpu.VMEM((8, 16, 128), f32)] * 2
        sems += [dma((6,))] * 2 + [dma((CHUNKS,))] * 2 + [dma((6,))] * 2 + [dma((7,)), dma((8,))]
    else:
        out_specs += [full((16, D))]
        out_shape += [jax.ShapeDtypeStruct((16, D), f32)]
    scratch_more = [pltpu.VMEM((2, half, ROWS, D), bf16)] + [dma((2, half))] * 3
    return pl.pallas_call(
        functools.partial(last_kernel, small),
        grid=(2 * half + 2,),
        in_specs=[
            row,
            row,
            row,
            full(cat.shape),
            pl.BlockSpec((ROWS, D), lambda i: (core() * half + own(i), 0)),
            pl.BlockSpec((1, ROWS), lambda i: (0, core() * half + own(i))),
            full((16, D)),
            mine,
            full((8, D)),
            mine,
            mine,
            mine,
            full(g_send.shape),
            full(g_keep.shape),
        ],
        out_specs=out_specs,
        out_shape=out_shape,
        scratch_shapes=scratch + sems + scratch_more,
        compiler_params=params(collective_id=2, has_side_effects=True),
        cost_estimate=cost(30),
        name="last",
    )(dq, dk, dv, cat, tokens, passes, vec, grad_second, sums_two, second, chip, far, g_send, g_keep)


def precondition(grad, weight, left, right, left_root, right_root):
    high = lax.Precision.HIGHEST
    left_new = decay * left + (1.0 - decay) * jnp.einsum(
        "...ij,...kj->...ik", grad, grad, precision=high
    )
    right_new = decay * right + (1.0 - decay) * jnp.einsum(
        "...ji,...jk->...ik", grad, grad, precision=high
    )
    half = jnp.einsum("...ij,...jk->...ik", left_root, grad, precision=high)
    step = jnp.einsum("...ij,...jk->...ik", half, right_root, precision=high)
    return (left_new, right_new, step, weight - rate_matrix * step)


def two_part(value):
    high = value.astype(bf16)
    return high, (value - high.astype(f32)).astype(bf16)


def dot_three(dot, a, b):
    return dot(a[0], b[0]) + (dot(a[0], b[1]) + dot(a[1], b[0]))


def renew_kernel(
    place, late, own, one, two, three, weight, left, right, left_root, right_root, output, input_grad,
    left_new, right_new, step, new, output_new, input_grad_new, sems,
):
    i = pl.program_id(0)
    copies = [
        pltpu.make_async_copy(output, output_new, sems.at[0]),
        pltpu.make_async_copy(input_grad, input_grad_new, sems.at[1]),
    ]

    @pl.when(i == 0)
    def _():
        for copy in copies:
            copy.start()

    early = own[0].astype(f32) + one[0].astype(f32) + two[0].astype(f32) + three[0].astype(f32)
    z = place[3]
    both = late[0] + jnp.where(z > 1, early, 0.0)
    for n in range(2):
        grad = both[:, n * SIDE : (n + 1) * SIDE]
        grad = two_part(jnp.where(z == 0, grad.T, grad))
        left_new[0, n] = decay * left[0, n] + (1.0 - decay) * dot_three(nt, grad, grad)
        right_new[0, n] = decay * right[0, n] + (1.0 - decay) * dot_three(tn, grad, grad)
        half = dot_three(nn, two_part(left_root[0, n]), grad)
        value = dot_three(nn, two_part(half), two_part(right_root[0, n]))
        step[0, n] = value
        new[0, n] = weight[0, n] - rate_matrix * value

    @pl.when(i == pl.num_programs(0) - 1)
    def _():
        for copy in copies:
            copy.wait()


def renew(place, late, own, far, weight, left, right, left_root, right_root, output, input_grad):
    pair = pl.BlockSpec((1, SIDE, PAIR), lambda i, s: (i, 0, 0))
    slot = pl.BlockSpec((1, 2, SIDE, SIDE), lambda i, s: (0, i, 0, 0))
    return pl.pallas_call(
        renew_kernel,
        grid_spec=pltpu.PrefetchScalarGridSpec(
            num_scalar_prefetch=1,
            grid=(3,),
            in_specs=[pair] * 5 + [slot] * 5 + [pl.BlockSpec(memory_space=pltpu.HBM)] * 2,
            out_specs=[slot] * 4 + [pl.BlockSpec(memory_space=pltpu.HBM)] * 2,
            scratch_shapes=[pltpu.SemaphoreType.DMA((2,))],
        ),
        out_shape=[jax.ShapeDtypeStruct(weight.shape, f32)] * 4
        + [jax.ShapeDtypeStruct(value.shape, value.dtype) for value in (output, input_grad)],
        compiler_params=params(56),
        cost_estimate=cost(5),
        name="renew",
    )(place, late, own, *far, weight, left, right, left_root, right_root, output, input_grad)


def to_pairs(blocks):
    n = blocks.shape[0] // 2
    return blocks.reshape(n, 2, SIDE, SIDE).transpose(0, 2, 1, 3).reshape(n, SIDE, PAIR)


def from_pairs(pairs):
    n = pairs.shape[0]
    return pairs.reshape(n, SIDE, 2, SIDE).transpose(0, 2, 1, 3).reshape(2 * n, SIDE, SIDE)


def swap(value, bit):
    return lax.ppermute(value, "tensor", [(t, t ^ bit) for t in range(NT)])


def hop_x(value):
    return lax.ppermute(value, "dp", [(d, d ^ 1) for d in range(8)])


def hop_z(value, turn, ends):
    pairs = [(d, (d + 2 * turn) % 8) for d in range(8) if (d // 2 + turn) % 4 in ends]
    return lax.ppermute(value, "dp", pairs)


def tie(*values):
    return lax.optimization_barrier(values)


def on_device(
    tokens,
    pass_ids,
    doc_lengths,
    cotangent,
    block_weights,
    vector_params,
    vector_moment,
    block_left,
    block_right,
    block_left_root,
    block_right_root,
):
    t, dp = lax.axis_index("tensor"), lax.axis_index("dp")
    core, side = t % 2, t // 2
    n_dp = lax.axis_size("dp")
    small = n_dp == 8
    z, column = (dp // 2, dp % 2) if small else (0, 0)
    place = jnp.stack([core, side, jnp.asarray(column), jnp.asarray(z)]).astype(jnp.int32)
    lens = doc_lengths[0]
    seq = tokens.shape[0]
    passes = pass_ids.reshape(1, seq)
    total_blocks = (D // SIDE) * (4 + 2 * (FF // D))
    slots = block_weights.shape[1] * n_dp

    if small:
        pairs, wo_other, vec, norm, q, k, v, cat = gather(block_weights, vector_params, tokens, passes)
    else:
        every = lax.all_gather(block_weights.astype(bf16), "dp", axis=1, tiled=True)[0]
        near = to_pairs(every[:total_blocks])
        far = swap(near, 2)
        pairs = jnp.where(side == 0, jnp.stack([near, far]), jnp.stack([far, near]))
        vec = lax.all_gather(vector_params, "dp", axis=1, tiled=True)
        vec = jnp.pad(vec, ((0, 16 - vec.shape[0]), (0, 0)))
        wo_other = swap(pairs[:, 6:8], 1)
        norm, q, k, v, cat = project(tokens, passes, vec, pairs)
    mine, lse = attend(lens, q, k, v)
    out_chip, second, grad_second, grad_mixed, sums_two, mid_send, mid_keep, *ends = feed(
        small, tokens, passes, vec, mine, cotangent, pairs, wo_other
    )
    out_far = swap(out_chip, 2)
    if small:
        far = [hop_z(ends[turn], turn, (2, 3)) for turn in (1, 2, 3)]
        mid_send = hop_x(mid_send)
    dq, dk, dv = attend_back(lens, q, k, v, mine, lse, grad_mixed)
    g_send, g_keep = qkv_grads(place, norm, dq, dk, dv, mid_send, mid_keep)
    if small:
        *far, out_far, g_send = tie(*far, out_far, g_send)
    output, input_grad, *sums = last(
        small, dq, dk, dv, cat, tokens, passes, vec, grad_second, sums_two, second, out_chip, out_far, g_send, g_keep
    )
    if small:
        late, vector_sum = sums
        left_new, right_new, step, weight_new, output, input_grad = renew(
            place, late, ends[0], far, block_weights, block_left, block_right, block_left_root, block_right_root,
            output, input_grad,
        )
        vector_grad = vector_sum[: PASSES + 4, : vector_params.shape[1]]
    else:
        vector_part = sums[0][: PASSES + 4]
        send, keep = ends
        rest = jnp.stack(
            [
                jnp.concatenate([mid_keep, keep]).reshape(3, 3, SIDE, PAIR),
                jnp.concatenate([mid_send, send]).reshape(3, 3, SIDE, PAIR),
            ],
            axis=1,
        )
        grad_qkv = from_pairs(jnp.concatenate([g_keep[:3], g_send[:3]], axis=0)).swapaxes(1, 2)
        grad_rest = from_pairs(rest.reshape(18, SIDE, PAIR))
        spare = jnp.zeros((slots - total_blocks, SIDE, SIDE), bf16)
        grad_blocks = jnp.concatenate([grad_qkv, grad_rest, spare], axis=0)[None].astype(f32)
        owned = lax.psum_scatter(grad_blocks, "dp", scatter_dimension=1, tiled=True)
        vector_grad = lax.psum_scatter(vector_part, "dp", scatter_dimension=1, tiled=True)
        left_new, right_new, step, weight_new = precondition(
            owned, block_weights, block_left, block_right, block_left_root, block_right_root
        )
    moment_new = decay * vector_moment + (1.0 - decay) * vector_grad * vector_grad
    vector_new = vector_params - rate_vector * vector_grad / (jnp.sqrt(moment_new) + moment_eps)
    return (
        output,
        input_grad,
        left_new,
        right_new,
        step,
        weight_new,
        vector_grad,
        moment_new,
        vector_new,
    )


def solution(mesh):
    rows, line = P("dp", None), P(None, "dp")
    block = P("tensor", "dp", None, None)
    return jax.shard_map(
        on_device,
        mesh=mesh,
        in_specs=(rows, P("dp"), rows, rows, block, line, line, block, block, block, block),
        out_specs=(rows, rows, block, block, block, block, line, line, line),
        check_vma=False,
    )
```

```python
import functools

import jax
import jax.numpy as jnp
from jax import lax
from jax.experimental import pallas as pl
from jax.experimental.pallas import tpu as pltpu
from jax.sharding import PartitionSpec as P

D = 768
HD = 64
FF = 3072
PASSES = 5
SIDE = 192
PAIR = 2 * SIDE
ROWS = 256
WIDE = 512
DOCS = 8
NT = 4

norm_eps = 1e-05
moment_eps = 1e-08
rate_matrix = 0.03
rate_vector = 0.2
decay = 0.5
gelu_coef = 0.7978845608028654
masked_score = -1e30
f32 = jnp.float32
bf16 = jnp.bfloat16
MESH = pl.DeviceIdType.MESH


def nn(a, b):
    return lax.dot_general(a, b, (((1,), (0,)), ((), ())), preferred_element_type=f32)


def nt(a, b):
    return lax.dot_general(a, b, (((1,), (1,)), ((), ())), preferred_element_type=f32)


def tn(a, b):
    return lax.dot_general(a, b, (((0,), (0,)), ((), ())), preferred_element_type=f32)


def split_three(value):
    high = value.astype(bf16)
    rest = value - high.astype(f32)
    mid = rest.astype(bf16)
    return high, mid, (rest - mid.astype(f32)).astype(bf16)


def one_hot(pass_row):
    kinds = lax.broadcasted_iota(jnp.int32, (16, pass_row.shape[1]), 0)
    return (kinds == pass_row).astype(f32).astype(bf16)


def embedded(tokens, pass_row, vec):
    chosen = jnp.concatenate([one_hot(pass_row)] * 3, axis=0)
    return tokens.astype(f32) + tn(chosen, jnp.concatenate(split_three(vec), axis=0))


def hat_of(hidden):
    mean = jnp.mean(hidden, axis=-1, keepdims=True)
    center = hidden - mean
    spread = jnp.mean(center * center, axis=-1, keepdims=True)
    root = lax.rsqrt(spread + norm_eps)
    return center * root, root


def norm_back(hat, root, grad, gain):
    scaled = grad * gain
    first = jnp.mean(scaled, axis=-1, keepdims=True)
    second = jnp.mean(scaled * hat, axis=-1, keepdims=True)
    return root * (scaled - first - hat * second)


def params(mebibytes=56, **kw):
    return pltpu.CompilerParams(vmem_limit_bytes=mebibytes * 1024 * 1024, **kw)


def cost(micros):
    return pl.CostEstimate(flops=int(micros * 1.1e9), bytes_accessed=int(micros * 1e6), transcendentals=0)


def full(shape):
    return pl.BlockSpec(shape, lambda *_: (0,) * len(shape))


def gather_kernel(
    own, vec_own, tokens, passes,
    all_pairs, wo_other, vec_out, norm, q, k_out, v, cat,
    pack, vec_pack, vec_land, wq, tok, norm_s, qkv_s, cat_s, *sems,
):
    (
        s_z1, r_z1, s_x1, r_x1, s_y1, r_y1, s_d1, r_d1, s_l, r_l, s_r, r_r, s_x2, r_x2, s_y2, r_y2, s_v, r_v, s_c, r_c,
        s_out, s_cat, s_tok, loc,
    ) = sems
    dp, t = lax.axis_index("dp"), lax.axis_index("tensor")
    z, x = dp // 2, dp % 2
    y, core = t // 2, t % 2
    far_x, far_y, near = z * 2 + (1 - x), (1 - y) * 2 + core, y * 2 + (1 - core)

    barrier = pltpu.get_barrier_semaphore()
    peers = [lax.rem(dp + n, 8) for n in range(1, 8)]
    for peer in peers:
        pl.semaphore_signal(barrier, inc=1, device_id={"dp": peer}, device_id_type=MESH)
    for to in (far_y, near):
        pl.semaphore_signal(barrier, inc=1, device_id={"tensor": to}, device_id_type=MESH)

    tok_copy = pltpu.make_async_copy(tokens, tok, s_tok)
    tok_copy.start()
    for m in range(3):
        pair = jnp.concatenate([own[0, 2 * m], own[0, 2 * m + 1]], axis=1).astype(bf16)
        pack[m] = pair

        @pl.when(z == 0)
        def _():
            wq[y, 3 * x + m] = pair

    vec_pack[...] = jnp.zeros_like(vec_pack)
    vec_pack[0 : PASSES + 4, 0 : D // 8] = vec_own[...]
    pl.semaphore_wait(barrier, 9)

    started = []

    def send(src, dst, s_sem, r_sem, to, cond=None):
        copy = pltpu.make_async_remote_copy(
            src_ref=src, dst_ref=dst, send_sem=s_sem, recv_sem=r_sem, device_id=to, device_id_type=MESH
        )
        started.append((cond, copy))
        if cond is None:
            copy.start()
        else:
            pl.when(cond)(copy.start)

    def arrived(dst, r_sem, cond=None):
        copy = pltpu.make_async_remote_copy(
            src_ref=dst, dst_ref=dst, send_sem=loc, recv_sem=r_sem, device_id={"dp": far_x}, device_id_type=MESH
        )
        if cond is None:
            copy.wait_recv()
        else:
            pl.when(cond)(copy.wait_recv)

    to_x, to_y, to_left, to_right = {"dp": far_x}, {"tensor": far_y}, {"dp": dp - 2}, {"dp": dp + 2}
    half = SIDE // 2

    def piece(side, column, k):
        return wq.at[side, 3 * column + k // 2, pl.ds((k % 2) * half, half)]

    def at_z(d, m):
        return all_pairs.at[y, 3 * dp + 6 * d + m]

    own_copy = pltpu.make_async_copy(pack, all_pairs.at[y, pl.ds(3 * dp, 3)], loc)
    pl.when(z > 0)(own_copy.start)

    for m in range(3):
        send(pack.at[m], at_z(0, m), s_l.at[0, m], r_l.at[0, m], to_left, z > 0)
    for n, peer in enumerate(peers):
        send(vec_pack, vec_land.at[dp], s_v.at[n], r_v.at[dp], {"dp": peer})
    for m in range(3):
        send(pack.at[m], at_z(0, m), s_x2.at[z, m], r_x2.at[z, m], to_x, z > m)

    def diagonal(k):
        arrived(piece(y, 1 - x, k), r_x1.at[k])
        send(piece(y, 1 - x, k), piece(y, 1 - x, k), s_d1.at[k], r_d1.at[k], to_y)

    def from_right(d, m):
        arrived(at_z(d, m), r_l.at[d - 1, m], z + d < 4)
        if d < 3:
            send(at_z(d, m), at_z(d, m), s_l.at[d, m], r_l.at[d, m], to_left, (z + d < 4) & (z > 0))

    def from_left(d, m):
        arrived(at_z(-d, m), r_r.at[d - 1, m], z - d > 0)
        if d == 1:
            send(at_z(-d, m), at_z(-d, m), s_r.at[1, m], r_r.at[1, m], to_right, (z - d > 0) & (z < 3))

    def along_x(d, m, cond):
        send(at_z(d, m), at_z(d, m), s_x2.at[z + d, m], r_x2.at[z + d, m], to_x, cond)

    for k in range(6):
        arrived(piece(y, x, k), r_z1.at[k], z > 0)
        send(piece(y, x, k), piece(y, x, k), s_z1.at[k], r_z1.at[k], to_right, z < 3)
        send(piece(y, x, k), piece(y, x, k), s_x1.at[k], r_x1.at[k], to_x)
        send(piece(y, x, k), piece(y, x, k), s_y1.at[k], r_y1.at[k], to_y)
        if k == 5:
            for m in range(3):
                send(pack.at[m], at_z(0, m), s_r.at[0, m], r_r.at[0, m], to_right, (z > 0) & (z < 3))
                send(pack.at[m], at_z(0, m), s_x2.at[z, m], r_x2.at[z, m], to_x, (z > 0) & (z <= m))
        if k >= 1:
            diagonal(k - 1)
        if k % 2 == 1:
            from_right(1, k // 2)
    diagonal(5)
    pl.when(z > 0)(own_copy.wait)
    for m in range(3):
        along_x(1, m, z + 1 < 4)
    for m in range(3):
        from_left(1, m)
        along_x(-1, m, z - 1 > 0)
        from_right(2, m)
        along_x(2, m, z + 2 < 4)
    for k in range(6):
        arrived(piece(1 - y, x, k), r_y1.at[k])
        arrived(piece(1 - y, 1 - x, k), r_d1.at[k])
    for peer in peers:
        arrived(vec_land.at[peer], r_v.at[peer])
    vec_land[dp] = vec_pack[...]
    vec = jnp.concatenate([vec_land[d][:, : D // 8] for d in range(8)], axis=1)
    vec_out[...] = vec
    for n in range(3):
        for i in range(4):
            at = (i % 2) * SIDE
            parts = [wq[h, 2 * n + i // 2][:, at : at + SIDE] for h in range(2)]
            cat_s[n, i * SIDE : (i + 1) * SIDE, :] = jnp.concatenate(parts, axis=1)
    writes = [pltpu.make_async_copy(cat_s, cat, s_cat)]
    writes[0].start()
    tok_copy.wait()

    def rows_of(b):
        rows = slice(b * WIDE, (b + 1) * WIDE)
        hat, _ = hat_of(embedded(tok[rows, :], passes[:, rows], vec))
        low = (hat * vec[PASSES : PASSES + 1] + vec[PASSES + 1 : PASSES + 2]).astype(bf16)
        norm_s[rows, :] = low
        writes.append(pltpu.make_async_copy(norm_s.at[rows, :], norm.at[rows, :], s_out.at[b, 3]))
        writes[-1].start()
        for n, out in enumerate((q, k_out, v)):
            qkv_s[n, rows, :] = nn(low, cat_s[n]).astype(bf16)
            writes.append(pltpu.make_async_copy(qkv_s.at[n, rows, :], out.at[rows, :], s_out.at[b, n]))
            writes[-1].start()

    count = tok.shape[0] // WIDE
    for b in range(count):
        rows_of(b)
        if b == 0:
            for m in range(3):
                from_right(3, m)
                along_x(3, m, z + 3 < 4)
        if b == 1:
            for m in range(3):
                from_left(2, m)
                along_x(-2, m, z - 2 > 0)
        if b == 2:
            for m in range(2):
                ref = all_pairs.at[y, 6 + m]
                arrived(ref, r_x2.at[1, m], x == 1)
                send(ref, ref, s_y2.at[m], r_y2.at[m], to_y)
                send(ref, wo_other.at[y, m], s_c.at[0, m], r_c.at[y, m], {"tensor": near})
    for m in range(2):
        ref = all_pairs.at[1 - y, 6 + m]
        arrived(ref, r_y2.at[m])
        send(ref, wo_other.at[1 - y, m], s_c.at[1, m], r_c.at[1 - y, m], {"tensor": near})
    for w in range(1, 4):
        for m in range(3):
            ref = all_pairs.at[y, 6 * w + 3 * (1 - x) + m]
            if w == 1 and m < 2:
                arrived(ref, r_x2.at[w, m], x == 0)
            else:
                arrived(ref, r_x2.at[w, m])
    for h in range(2):
        for m in range(2):
            arrived(wo_other.at[h, m], r_c.at[h, m])
    for copy in writes:
        copy.wait()
    for cond, copy in started:
        if cond is None:
            copy.wait_send()
        else:
            pl.when(cond)(copy.wait_send)


def gather(block_weights, vector_params, tokens, passes):
    seq = tokens.shape[0]
    dma = pltpu.SemaphoreType.DMA
    sizes = [(6,)] * 8 + [(3, 3)] * 2 + [(2, 3)] * 2 + [(4, 3)] * 2 + [(2,)] * 2 + [(7,), (8,)] + [(2, 2)] * 2
    sizes += [(seq // WIDE, 4)]
    vmem, far = pl.BlockSpec(memory_space=pltpu.VMEM), pl.BlockSpec(memory_space=pl.ANY)
    wide = jax.ShapeDtypeStruct((seq, PAIR), bf16)
    return pl.pallas_call(
        gather_kernel,
        in_specs=[vmem, vmem, far, vmem],
        out_specs=[far, far, vmem, far, far, far, far, far],
        out_shape=[
            jax.ShapeDtypeStruct((2, 24, SIDE, PAIR), bf16),
            jax.ShapeDtypeStruct((2, 2, SIDE, PAIR), bf16),
            jax.ShapeDtypeStruct((16, D), f32),
            jax.ShapeDtypeStruct((seq, D), bf16),
            wide,
            wide,
            wide,
            jax.ShapeDtypeStruct((3, D, PAIR), bf16),
        ],
        scratch_shapes=[
            pltpu.VMEM((3, SIDE, PAIR), bf16),
            pltpu.VMEM((16, 128), f32),
            pltpu.VMEM((8, 16, 128), f32),
            pltpu.VMEM((2, 6, SIDE, PAIR), bf16),
            pltpu.VMEM((seq, D), bf16),
            pltpu.VMEM((seq, D), bf16),
            pltpu.VMEM((3, seq, PAIR), bf16),
            pltpu.VMEM((3, D, PAIR), bf16),
        ]
        + [dma(size) for size in sizes]
        + [dma] * 3,
        compiler_params=params(collective_id=0, has_side_effects=True),
        cost_estimate=cost(60),
        name="gather",
    )(block_weights, vector_params, tokens, passes)


def project_kernel(tok, pas, vec, wq, norm, q, k, v, cat):
    @pl.when(pl.program_id(0) == 0)
    def _():
        for x in range(3):
            for i in range(4):
                at = (i % 2) * SIDE
                parts = [wq[h, 2 * x + i // 2][:, at : at + SIDE] for h in range(2)]
                cat[x, i * SIDE : (i + 1) * SIDE, :] = jnp.concatenate(parts, axis=1)

    first = embedded(tok[...], pas[...], vec[...])
    hat, _ = hat_of(first)
    low = (hat * vec[PASSES : PASSES + 1] + vec[PASSES + 1 : PASSES + 2]).astype(bf16)
    norm[...] = low
    for x, out in enumerate((q, k, v)):
        out[...] = nn(low, cat[x]).astype(bf16)


def project(tokens, passes, vec, wq):
    seq = tokens.shape[0]
    row = lambda n: pl.BlockSpec((WIDE, n), lambda i: (i, 0))
    wide = jax.ShapeDtypeStruct((seq, PAIR), bf16)
    return pl.pallas_call(
        project_kernel,
        grid=(seq // WIDE,),
        in_specs=[
            row(D),
            pl.BlockSpec((1, WIDE), lambda i: (0, i)),
            full((16, D)),
            full((2, 6, SIDE, PAIR)),
        ],
        out_specs=[row(D), row(PAIR), row(PAIR), row(PAIR), full((3, D, PAIR))],
        out_shape=[
            jax.ShapeDtypeStruct((seq, D), bf16),
            wide,
            wide,
            wide,
            jax.ShapeDtypeStruct((3, D, PAIR), bf16),
        ],
        compiler_params=params(),
        cost_estimate=cost(16),
        name="project",
    )(tokens, passes, vec, wq)


def doc_state(lens, base):
    rows = base + lax.broadcasted_iota(jnp.int32, (1, ROWS), 1)
    rows = jnp.concatenate([rows, rows], axis=1)
    begin = jnp.int32(0)
    first = jnp.int32(0)
    starts = jnp.zeros((1, 2 * ROWS), jnp.int32)
    for c in range(DOCS):
        starts = jnp.where(rows >= begin, begin, starts)
        first = jnp.where(base >= begin, begin, first)
        begin = begin + lens[c]
    return rows, starts, first


def two_heads(block):
    left = lax.broadcasted_iota(jnp.int32, block.shape, 1) < HD
    none = jnp.zeros_like(block)
    return jnp.concatenate([jnp.where(left, block, none), jnp.where(left, none, block)], axis=0)


def one_above(both):
    return jnp.concatenate([both[:HD, :ROWS], both[HD:, ROWS:]], axis=0).T


def attend_kernel(lens, q, k, v, out, lse, acc):
    i = pl.program_id(0)
    base = i * ROWS
    rows, starts, first = doc_state(lens, base)
    pairs = [two_heads(q[:, p * 128 : (p + 1) * 128] * bf16(0.125)) for p in range(3)]
    for p in range(3):
        acc[p] = jnp.zeros((128, 2 * ROWS), f32)

    def step(j, carry):
        at = pl.multiple_of(j * ROWS, ROWS)
        keys = at + lax.broadcasted_iota(jnp.int32, (ROWS, 2 * ROWS), 0)
        seen = (keys >= starts) & (keys <= rows)
        here = pl.ds(at, ROWS)
        head = lambda p: slice(p * 128, (p + 1) * 128)
        scores = [jnp.where(seen, nt(k[here, head(p)], pairs[p]), masked_score) for p in range(3)]
        state = []
        for p in range(3):
            before, total = carry[2 * p], carry[2 * p + 1]
            now = jnp.maximum(before, jnp.max(scores[p], axis=0, keepdims=True))
            probs = jnp.exp(scores[p] - now)
            fade = jnp.exp(before - now)
            state += [now, total * fade + jnp.sum(probs, axis=0, keepdims=True)]
            acc[p] = acc[p] * fade + tn(v[here, head(p)], probs.astype(bf16))
        return tuple(state)

    zero = jnp.zeros((1, 2 * ROWS), f32)
    state = lax.fori_loop(first // ROWS, i + 1, step, (zero + masked_score, zero) * 3)
    lines = []
    for p in range(3):
        top, total = state[2 * p], state[2 * p + 1]
        out[:, p * 128 : (p + 1) * 128] = one_above(acc[p] / total).astype(bf16)
        line = top + jnp.log(total)
        lines += [line[:, :ROWS], line[:, ROWS:]]
    lse[...] = jnp.concatenate(lines + lines[:2], axis=0)


def attend(lens, q, k, v):
    seq = q.shape[0]
    row = pl.BlockSpec((ROWS, PAIR), lambda i, s: (i, 0))
    return pl.pallas_call(
        attend_kernel,
        grid_spec=pltpu.PrefetchScalarGridSpec(
            num_scalar_prefetch=1,
            grid=(seq // ROWS,),
            in_specs=[row, full((seq, PAIR)), full((seq, PAIR))],
            out_specs=[row, pl.BlockSpec((8, ROWS), lambda i, s: (0, i))],
            scratch_shapes=[
                pltpu.VMEM((3, 128, 2 * ROWS), f32),
            ],
        ),
        out_shape=[
            jax.ShapeDtypeStruct((seq, PAIR), bf16),
            jax.ShapeDtypeStruct((8, seq), f32),
        ],
        compiler_params=params(),
        cost_estimate=cost(30),
        name="attend",
    )(lens, q, k, v)


def attend_back_kernel(
    lens, q, k, v, mixed, lse, grad_mixed, dq, dk, dv, dk_acc, dv_acc, dq_acc
):
    i = pl.program_id(0)
    count = pl.num_programs(0)
    base = i * ROWS

    @pl.when(i == 0)
    def _():
        dk_acc[...] = jnp.zeros_like(dk_acc)
        dv_acc[...] = jnp.zeros_like(dv_acc)

    rows, starts, first = doc_state(lens, base)
    heads = lax.broadcasted_iota(jnp.int32, (8, 128), 0)
    lanes = lax.broadcasted_iota(jnp.int32, (8, 128), 1)
    pick = (lanes // HD == heads).astype(f32).astype(bf16)
    queries, grads, inner, lines = [], [], [], []
    for p in range(3):
        cols = slice(p * 128, (p + 1) * 128)
        queries.append(two_heads(q[:, cols] * bf16(0.125)))
        grads.append(two_heads(grad_mixed[:, cols]))
        product = grad_mixed[:, cols].astype(f32) * mixed[:, cols].astype(f32)
        high, low, _ = split_three(product)
        sums = nt(pick, high) + nt(pick, low)
        inner.append(jnp.concatenate([sums[0:1], sums[1:2]], axis=1))
        lines.append(jnp.concatenate([lse[2 * p : 2 * p + 1], lse[2 * p + 1 : 2 * p + 2]], axis=1))
        dq_acc[p] = jnp.zeros((128, 2 * ROWS), f32)

    def step(j, carry):
        at = pl.multiple_of(j * ROWS, ROWS)
        keys = at + lax.broadcasted_iota(jnp.int32, (ROWS, 2 * ROWS), 0)
        seen = (keys >= starts) & (keys <= rows)
        here = pl.ds(at, ROWS)
        for p in range(3):
            cols = slice(p * 128, (p + 1) * 128)
            kb = k[here, cols]
            scores = jnp.where(seen, nt(kb, queries[p]) - lines[p], masked_score)
            probs = jnp.exp(scores)
            grad_probs = nt(v[here, cols], grads[p])
            grad_scores = (probs * (grad_probs - inner[p])).astype(bf16)
            dv_acc[here, cols] += nn(probs.astype(bf16), grads[p])
            dk_acc[here, cols] += nn(grad_scores, queries[p])
            dq_acc[p] += tn(kb, grad_scores)
        return carry

    lax.fori_loop(first // ROWS, i + 1, step, 0)
    for p in range(3):
        dq[:, p * 128 : (p + 1) * 128] = (one_above(dq_acc[p]) * 0.125).astype(bf16)

    @pl.when(i == count - 1)
    def _():
        dk[...] = dk_acc[...].astype(bf16)
        dv[...] = dv_acc[...].astype(bf16)


def attend_back(lens, q, k, v, mixed, lse, grad_mixed):
    seq = q.shape[0]
    count = seq // ROWS
    row = pl.BlockSpec((ROWS, PAIR), lambda i, s: (i, 0))
    wide = jax.ShapeDtypeStruct((seq, PAIR), bf16)
    return pl.pallas_call(
        attend_back_kernel,
        grid_spec=pltpu.PrefetchScalarGridSpec(
            num_scalar_prefetch=1,
            grid=(count,),
            in_specs=[
                row,
                full((seq, PAIR)),
                full((seq, PAIR)),
                row,
                pl.BlockSpec((8, ROWS), lambda i, s: (0, i)),
                row,
            ],
            out_specs=[row, full((seq, PAIR)), full((seq, PAIR))],
            scratch_shapes=[
                pltpu.VMEM((seq, PAIR), f32),
                pltpu.VMEM((seq, PAIR), f32),
                pltpu.VMEM((3, 128, 2 * ROWS), f32),
            ],
        ),
        out_shape=[wide, wide, wide],
        compiler_params=params(),
        cost_estimate=cost(40),
        name="attend_back",
    )(lens, q, k, v, mixed, lse, grad_mixed)


def feed_kernel(
    small, tok, pas, vec, mine, cot, wo_mine, wo_other, w1, w2,
    out_chip, second_keep, grad_second, grad_mixed, sums, mid_send, mid_keep, *rest,
):
    results, rest = (rest[:4], rest[4:]) if small else (rest[:2], rest[2:])
    (
        wo, other, up, down, gup, gdown, go, core_out, core_in, far_out, far_in, ga_out, ga_in, oc_out, oc_in,
        g_send, g_keep, g_in, s_core, r_core, s_far, r_far, s_ga, r_ga, s_oc, r_oc, s_x, r_x, s_m, r_m,
    ) = rest
    step = pl.program_id(0)
    half = core_out.shape[0]
    t, dp = lax.axis_index("tensor"), lax.axis_index("dp")
    core, side = t % 2, t // 2
    near, far = side * 2 + (1 - core), (1 - side) * 2 + core
    z, column = (dp // 2, dp % 2) if small else (0, 0)
    far_x = z * 2 + 1 - column

    def copy(src, dst, s_sem, r_sem, j, to):
        return pltpu.make_async_remote_copy(
            src_ref=src.at[j],
            dst_ref=dst.at[j],
            send_sem=s_sem.at[j],
            recv_sem=r_sem.at[j],
            device_id={"tensor": to},
            device_id_type=MESH,
        )

    core_copy = lambda j: copy(core_out, core_in, s_core, r_core, j, near)
    far_copy = lambda j: copy(far_out, far_in, s_far, r_far, j, far)
    ga_copy = lambda j: copy(ga_out, ga_in, s_ga, r_ga, j, near)
    oc_copy = lambda j: copy(oc_out, oc_in, s_oc, r_oc, j, near)

    def x_copy(slot):
        return pltpu.make_async_remote_copy(
            src_ref=g_send.at[slot],
            dst_ref=g_in.at[slot],
            send_sem=s_x.at[slot],
            recv_sem=r_x.at[slot],
            device_id={"dp": far_x},
            device_id_type=MESH,
        )

    def mixed_copy(block):
        rows = pl.ds(pl.multiple_of(block * ROWS, ROWS), ROWS)
        return pltpu.make_async_remote_copy(
            src_ref=mine.at[rows],
            dst_ref=other.at[rows],
            send_sem=s_m.at[block],
            recv_sem=r_m.at[block],
            device_id={"tensor": near},
            device_id_type=MESH,
        )

    barrier = pltpu.get_barrier_semaphore()

    @pl.when(step == 0)
    def _():
        for to in (near, far):
            pl.semaphore_signal(barrier, inc=1, device_id={"tensor": to}, device_id_type=MESH)
        if small:
            pl.semaphore_signal(barrier, inc=1, device_id={"dp": far_x}, device_id_type=MESH)
        for h in range(2):
            for m in range(2):
                rows, cols = slice(h * SIDE, (h + 1) * SIDE), slice(m * PAIR, (m + 1) * PAIR)
                wo[rows, cols] = wo_mine[h, m]
                wo[PAIR + h * SIDE : PAIR + (h + 1) * SIDE, cols] = wo_other[h, m]
        for r in range(4):
            for m in range(2):
                rows, cols = slice(r * SIDE, (r + 1) * SIDE), slice(m * PAIR, (m + 1) * PAIR)
                up[rows, cols] = w1[0, 2 * r + m]
                down[rows, cols] = w2[0, 2 * r + m]
        pl.semaphore_wait(barrier, 3 if small else 2)
        for j in range(half):
            mixed_copy(core * half + j).start()
            mixed_copy((1 - core) * half + j).start()
        gup[...] = jnp.zeros_like(gup)
        gdown[...] = jnp.zeros_like(gdown)
        go[...] = jnp.zeros_like(go)
        sums[...] = jnp.zeros_like(sums)

    @pl.when(step < 2 * half)
    def _():
        j = step // 2
        owner = jnp.where(step % 2 == 0, 1 - core, core)
        here = pl.ds(pl.multiple_of((owner * half + j) * ROWS, ROWS), ROWS)
        first = embedded(tok[...], pas[...], vec[...])
        mixed_copy(owner * half + j).wait_recv()
        second = first + nn(jnp.concatenate([mine[here, :], other[here, :]], axis=1), wo[...])
        hat, _ = hat_of(second)
        low = (hat * vec[PASSES + 2 : PASSES + 3] + vec[PASSES + 3 : PASSES + 4]).astype(bf16)
        upper = nn(low, up[...])
        square = upper * upper
        bent = jnp.tanh(gelu_coef * upper * (1.0 + 0.044715 * square))
        act = (0.5 * upper * (1.0 + bent)).astype(bf16)
        slope = 0.5 * (1.0 + bent) + (0.5 * gelu_coef) * upper * (1.0 - bent * bent) * (
            1.0 + (3 * 0.044715) * square
        )
        grad_act = nt(cot[...], down[...])
        grad_upper = (grad_act * slope).astype(bf16)
        part = nt(grad_upper, up[...])

        @pl.when(step % 2 == 0)
        def _():
            core_out[j] = part.astype(bf16)
            core_copy(j).start()

        @pl.when(step % 2 == 1)
        def _():
            core_copy(j).wait_recv()
            far_out[j] = (part + core_in[j].astype(f32)).astype(bf16)
            far_copy(j).start()
            second_keep[pl.ds(pl.multiple_of(j * ROWS, ROWS), ROWS), :] = second

        gup[...] += tn(low, grad_upper)
        gdown[...] += tn(act, cot[...])
        out_part = nn(act, down[...])

        @pl.when(step % 2 == 0)
        def _():
            oc_out[j] = out_part.astype(bf16)
            oc_copy(j).start()

        @pl.when(step % 2 == 1)
        def _():
            oc_copy(j).wait_recv()
            out_chip[...] = (out_part + oc_in[j].astype(f32)).astype(bf16)

    @pl.when(step == 2 * half - 1)
    def _():
        for r in range(4):
            for m in range(2):
                rows, cols = slice(r * SIDE, (r + 1) * SIDE), slice(m * PAIR, (m + 1) * PAIR)
                for at, total in ((8, gup), (16, gdown)):
                    pair = at + 2 * r + m
                    slot, place = (pair // 6 - 1) * 3 + pair % 3, pair // 3 % 2
                    value = total[rows, cols].astype(bf16)
                    kept, sent, n = (mid_keep, mid_send, slot) if slot < 3 else (g_keep, g_send, slot - 3)

                    @pl.when(column == place)
                    def _():
                        kept[n] = value

                    @pl.when(column != place)
                    def _():
                        sent[n] = value
        if small:
            for n in range(6):
                x_copy(n).start()

    def through_out(grad, block):
        here = pl.ds(pl.multiple_of(block * ROWS, ROWS), ROWS)
        grad_mixed[here, :] = nt(grad, wo[:PAIR, :]).astype(bf16)
        go[...] += tn(mine[here, :], grad)

    @pl.when((step >= 2 * half) & (step < 3 * half))
    def _():
        j = step - 2 * half
        hat, root = hat_of(second_keep[pl.ds(pl.multiple_of(j * ROWS, ROWS), ROWS), :])
        far_copy(j).wait_recv()
        grad = far_out[j].astype(f32) + far_in[j].astype(f32)
        result = cot[...].astype(f32) + norm_back(hat, root, grad, vec[PASSES + 2 : PASSES + 3])
        low = result.astype(bf16)
        ga_out[j] = low
        ga_copy(j).start()
        grad_second[...] = result
        sums[0:1] += jnp.sum(grad * hat, axis=0, keepdims=True)
        sums[1:2] += jnp.sum(grad, axis=0, keepdims=True)
        through_out(low, core * half + j)

    @pl.when(step > 2 * half)
    def _():
        j = step - 2 * half - 1
        ga_copy(j).wait_recv()
        through_out(ga_in[j], (1 - core) * half + j)

    @pl.when(step == 3 * half)
    def _():
        at = pl.multiple_of(side * SIDE, SIDE)
        for m in range(2):
            value = go[pl.ds(at, SIDE), m * PAIR : (m + 1) * PAIR].astype(bf16)

            @pl.when(column == 0)
            def _():
                mid_keep[m] = value

            @pl.when(column != 0)
            def _():
                mid_send[m] = value

        for j in range(half):
            core_copy(j).wait_send()
            oc_copy(j).wait_send()
            mixed_copy(j).wait_send()
            mixed_copy(half + j).wait_send()
            far_copy(j).wait_send()
            ga_copy(j).wait_send()
        if small:
            for n in range(6):
                x_copy(n).wait_send()
                x_copy(n).wait_recv()
                value = (g_keep[n].astype(f32) + g_in[n].astype(f32)).astype(bf16)
                for turn in range(4):

                    @pl.when(lax.rem(z + turn, 4) == n // 3 + 2)
                    def _():
                        results[turn][n % 3] = value
        else:
            results[0][...] = g_send[...]
            results[1][...] = g_keep[...]


def feed(small, tokens, passes, vec, mine, cotangent, pairs, wo_other):
    seq = tokens.shape[0]
    half = seq // ROWS // 2

    def block(i):
        core = lax.axis_index("tensor") % 2
        work = jnp.minimum(i, 2 * half - 1)
        owner = jnp.where(work % 2 == 0, 1 - core, core)
        return owner * half + work // 2

    def cot_block(i):
        core = lax.axis_index("tensor") % 2
        return jnp.where(i < 2 * half, block(i), core * half + jnp.minimum(i - 2 * half, half - 1))

    side = lambda: lax.axis_index("tensor") // 2
    row = lambda n: pl.BlockSpec((ROWS, n), lambda i: (block(i), 0))
    keep = pl.BlockSpec((ROWS, D), lambda i: (jnp.minimum(i // 2, half - 1), 0))
    last = pl.BlockSpec((ROWS, D), lambda i: (jnp.clip(i - 2 * half, 0, half - 1), 0))
    rows = lambda kind: jax.ShapeDtypeStruct((seq // 2, D), kind)
    gr = lambda n: jax.ShapeDtypeStruct((n, SIDE, PAIR), bf16)
    ends = [(3, SIDE, PAIR)] * 4 if small else [(6, SIDE, PAIR)] * 2
    buffer = pltpu.VMEM((half, ROWS, D), bf16)
    dma = pltpu.SemaphoreType.DMA((half,))
    return pl.pallas_call(
        functools.partial(feed_kernel, small),
        grid=(3 * half + 1,),
        in_specs=[
            row(D),
            pl.BlockSpec((1, ROWS), lambda i: (0, block(i))),
            full((16, D)),
            full((seq, PAIR)),
            pl.BlockSpec((ROWS, D), lambda i: (cot_block(i), 0)),
            pl.BlockSpec((2, 2, SIDE, PAIR), lambda i: (0, 3, 0, 0)),
            full(wo_other.shape),
            pl.BlockSpec((1, 8, SIDE, PAIR), lambda i: (side(), 1, 0, 0)),
            pl.BlockSpec((1, 8, SIDE, PAIR), lambda i: (side(), 2, 0, 0)),
        ],
        out_specs=[
            keep,
            full((seq // 2, D)),
            last,
            full((seq, PAIR)),
            full((8, D)),
            full((3, SIDE, PAIR)),
            full((3, SIDE, PAIR)),
        ]
        + [full(shape) for shape in ends],
        scratch_shapes=[
            pltpu.VMEM((D, D), bf16),
            pltpu.VMEM((seq, PAIR), bf16),
            pltpu.VMEM((D, D), bf16),
            pltpu.VMEM((D, D), bf16),
            pltpu.VMEM((D, D), f32),
            pltpu.VMEM((D, D), f32),
            pltpu.VMEM((PAIR, D), f32),
        ]
        + [buffer] * 8
        + [pltpu.VMEM((6, SIDE, PAIR), bf16)] * 3
        + [dma] * 8
        + [pltpu.SemaphoreType.DMA((6,))] * 2
        + [pltpu.SemaphoreType.DMA((2 * half,))] * 2,
        out_shape=[
            rows(bf16),
            rows(f32),
            rows(f32),
            jax.ShapeDtypeStruct((seq, PAIR), bf16),
            jax.ShapeDtypeStruct((8, D), f32),
            gr(3),
            gr(3),
        ]
        + [jax.ShapeDtypeStruct(shape, bf16) for shape in ends],
        compiler_params=params(collective_id=1, has_side_effects=True),
        cost_estimate=cost(50),
        name="feed_forward",
    )(tokens, passes, vec, mine, cotangent, pairs, wo_other, pairs, pairs)


CHUNK = SIDE // 2
CHUNKS = 12
TAKEN = (
    ((12, 12),),
    ((4, 1), (5, 2), (6, 3), (7, 5), (8, 6), (10, 7), (11, 8), (12, 12)),
    ((2, 1), (3, 2), (4, 4), (5, 5), (6, 6), (8, 7), (9, 8), (10, 9), (11, 11), (12, 12)),
    ((0, 2), (1, 4), (2, 6), (6, 7), (7, 8), (8, 10), (9, 11), (10, 12)),
)
GRAD_STEPS = 4


def last_kernel(
    small, norm, dq_wide, dk_wide, dv_wide, dq, dk, dv, cat, tok, pas, vec, grad_second, sums_two, second, chip, far,
    mid_near, mid_keep, output, input_grad, *rest,
):
    if small:
        late, vec_sum = rest[:2]
        rest = rest[2:]
        (
            core_out, core_in, sums, core_sums, x_in, z_in, z_out, up_in, v_out, v_in, total,
            s_core, r_core, s_sum, r_sum, s_x, r_x, s_z, r_z, s_up, r_up, s_v, r_v, ready, acc, g_send, g_keep,
            s_own, s_res, r_res,
        ) = rest
    else:
        (
            vec_sum, send_out, keep_out, core_out, core_in, sums, core_sums, s_core, r_core, s_sum, r_sum, ready, acc,
            g_send, g_keep, s_own, s_res, r_res,
        ) = rest
    step = pl.program_id(0)
    i = step - GRAD_STEPS
    half = core_out.shape[0]
    t, dp = lax.axis_index("tensor"), lax.axis_index("dp")
    core, side = t % 2, t // 2
    near = side * 2 + (1 - core)
    z, column = (dp // 2, dp % 2) if small else (0, 0)
    far_x = z * 2 + 1 - column
    peers = [lax.rem(dp + k, 8) for k in range(1, 8)]

    def copy(src, dst, s_sem, r_sem, to):
        return pltpu.make_async_remote_copy(
            src_ref=src, dst_ref=dst, send_sem=s_sem, recv_sem=r_sem, device_id=to, device_id_type=MESH
        )

    core_copy = lambda j: copy(core_out.at[j], core_in.at[j], s_core.at[j], r_core.at[j], {"tensor": near})
    sum_copy = lambda: copy(sums, core_sums, s_sum, r_sum, {"tensor": near})

    def rows_at(n, j, owner):
        rows = pl.ds(pl.multiple_of((owner * half + j) * ROWS, ROWS), ROWS)
        return (output, input_grad)[n].at[rows]

    own_result = lambda n, j: pltpu.make_async_copy(ready.at[n, j], rows_at(n, j, core), s_own.at[n, j])
    near_result = lambda n, j, owner: copy(
        ready.at[n, j], rows_at(n, j, owner), s_res.at[n, j], r_res.at[n, j], {"tensor": near}
    )

    def part_of(ref, k):
        return ref.at[k // 2, pl.ds((k % 2) * CHUNK, CHUNK)]

    x_copy = lambda k: copy(part_of(g_send, k), x_in.at[k], s_x.at[k], r_x.at[k], {"dp": far_x})
    z_copy = lambda k: copy(z_out.at[k], z_in.at[k], s_z.at[k], r_z.at[k], {"dp": dp - 2})
    up_copy = lambda k: copy(z_out.at[k], up_in.at[k - 6], s_up.at[k - 6], r_up.at[k - 6], {"dp": dp + 2})
    v_copy = lambda n: copy(v_out.at[peers[n]], v_in.at[dp], s_v.at[n], r_v.at[dp], {"dp": peers[n]})
    barrier = pltpu.get_barrier_semaphore()

    @pl.when(step == 0)
    def _():
        pl.semaphore_signal(barrier, inc=1, device_id={"tensor": near}, device_id_type=MESH)
        if small:
            for peer in peers:
                pl.semaphore_signal(barrier, inc=1, device_id={"dp": peer}, device_id_type=MESH)
            late[...] = jnp.zeros_like(late)
        sums[...] = jnp.zeros_like(sums)
        sums[PASSES + 2 : PASSES + 4] = sums_two[0:2]
        acc[...] = jnp.zeros_like(acc)
        pl.semaphore_wait(barrier, 8 if small else 1)

    @pl.when(step < GRAD_STEPS)
    def _():
        mine = [jnp.where(side == 0, grad[:, :SIDE], grad[:, SIDE:]) for grad in (dq_wide, dk_wide, dv_wide)]
        acc[...] += tn(jnp.concatenate(mine, axis=1), norm[...])

    @pl.when(step == GRAD_STEPS - 1)
    def _():
        for n in range(3):
            for m in range(2):
                value = acc[n * SIDE : (n + 1) * SIDE, m * PAIR : (m + 1) * PAIR].astype(bf16)
                slot, place = (2 * n + m) % 3, (2 * n + m) // 3

                @pl.when(column == place)
                def _():
                    g_keep[slot] = value

                @pl.when(column != place)
                def _():
                    g_send[slot] = value
        if small:
            for k in range(6):
                x_copy(k).start()
        else:
            send_out[...] = g_send[...]
            keep_out[...] = g_keep[...]

    @pl.when((i >= 0) & (i < 2 * half))
    def _():
        part = nt(dq[...], cat[0]) + nt(dk[...], cat[1]) + nt(dv[...], cat[2])

        @pl.when(i < half)
        def _():
            core_out[i] = part.astype(bf16)
            core_copy(i).start()

        @pl.when(i >= half)
        def _():
            j = i - half
            hat, root = hat_of(embedded(tok[...], pas[...], vec[...]))
            core_copy(j).wait_recv()
            grad = part + core_in[j].astype(f32)
            result = grad_second[...] + norm_back(hat, root, grad, vec[PASSES : PASSES + 1])
            ready[0, j] = (second[...] + (chip[...].astype(f32) + far[...].astype(f32))).astype(bf16)
            ready[1, j] = result.astype(bf16)
            for n in range(2):
                own_result(n, j).start()
                near_result(n, j, core).start()
            chosen = one_hot(pas[...])
            high, mid, _ = split_three(result)
            sums[...] += nn(chosen, high) + nn(chosen, mid)
            sums[PASSES : PASSES + 1] += jnp.sum(grad * hat, axis=0, keepdims=True)
            sums[PASSES + 1 : PASSES + 2] += jnp.sum(grad, axis=0, keepdims=True)

    @pl.when(i == 2 * half - 1)
    def _():
        sum_copy().start()

    @pl.when(i == 2 * half)
    def _():
        sum_copy().wait_recv()
        total = sums[...] + core_sums[...]
        if small:
            wide = D // 8
            for d in range(8):
                v_out[d, :, 0:wide] = total[:, d * wide : (d + 1) * wide]
                v_out[d, :, wide:] = jnp.zeros((16, 128 - wide), f32)
            for n in range(7):
                v_copy(n).start()
        else:
            vec_sum[...] = total

    if small:

        def term_of(k):
            rows = pl.ds(pl.multiple_of((k % 2) * CHUNK, 16), CHUNK)

            @pl.when(jnp.asarray(k) < 6)
            def _():
                x_copy(k).wait_recv()
                total[...] = g_keep[k // 2, rows, :].astype(f32) + x_in[k].astype(f32)

            @pl.when(jnp.asarray(k) >= 6)
            def _():
                total[...] = mid_keep[k // 2 - 3, rows, :].astype(f32) + mid_near[k // 2 - 3, rows, :].astype(f32)

            return total[...]

        def keep_late(k, pair, total):
            late[pair, pl.ds(pl.multiple_of((k % 2) * CHUNK, 16), CHUNK), :] = total

        def pass_on(k):
            term = term_of(k)

            @pl.when(z < 3)
            def _():
                z_copy(k).wait_recv()

            below = jnp.where(z < 3, z_in[k].astype(f32), 0.0)
            passed = term + below

            @pl.when((z > 1) | ((z == 1) & (k < 6)))
            def _():
                z_out[k] = passed.astype(bf16)
                z_copy(k).start()

            @pl.when(z == 0)
            def _():
                keep_late(k, k // 2, passed)

            @pl.when((z == 1) & (k >= 6))
            def _():
                up_copy(k).wait_recv()
                keep_late(k, k // 2 - 3, passed + up_in[k - 6].astype(f32))

        def at_position(p, carry):
            k = jnp.where(p < 6, p + 6, p - 6)

            @pl.when((z > 0) | (k < 6))
            def _():
                pass_on(k)

            return carry

        begin, end = jnp.int32(0), jnp.int32(0)
        for place, line in enumerate(TAKEN):
            for at, upto in line:
                begin = jnp.where((z == place) & (step > at), upto, begin)
                end = jnp.where((z == place) & (step >= at), upto, end)
        lax.fori_loop(begin, end, at_position, 0)

        @pl.when((step == 0) & (z == 0))
        def _():
            for k in range(6, CHUNKS):
                z_out[k] = term_of(k).astype(bf16)
                up_copy(k).start()

    @pl.when(step == pl.num_programs(0) - 1)
    def _():
        for j in range(half):
            core_copy(j).wait_send()
            for n in range(2):
                own_result(n, j).wait()
                near_result(n, j, core).wait_send()
                near_result(n, j, 1 - core).wait_recv()
        sum_copy().wait_send()
        if small:
            for peer in peers:
                copy(v_out.at[0], v_in.at[peer], s_v.at[0], r_v.at[peer], {"dp": far_x}).wait_recv()
            v_in[dp] = v_out[dp]
            total = v_in[0]
            for d in range(1, 8):
                total = total + v_in[d]
            vec_sum[...] = total
            for n in range(7):
                v_copy(n).wait_send()
            for k in range(CHUNKS):
                if k < 6:
                    x_copy(k).wait_send()
                    pl.when(z > 0)(z_copy(k).wait_send)
                else:
                    pl.when(z > 1)(z_copy(k).wait_send)
                    pl.when(z == 0)(up_copy(k).wait_send)


def last(
    small, norm, dq, dk, dv, cat, tokens, passes, vec, grad_second, sums_two, second, chip, far, mid_near, mid_keep
):
    seq = dq.shape[0]
    half = seq // ROWS // 2
    core = lambda: lax.axis_index("tensor") % 2

    def block(i):
        work = jnp.clip(i - GRAD_STEPS, 0, 2 * half - 1)
        return lax.rem(work + (1 - core()) * half, 2 * half)

    own = lambda i: jnp.clip(i - GRAD_STEPS - half, 0, half - 1)
    tall = seq // GRAD_STEPS
    wide = lambda n: pl.BlockSpec((tall, n), lambda i: (jnp.minimum(i, GRAD_STEPS - 1), 0))
    row = pl.BlockSpec((ROWS, PAIR), lambda i: (block(i), 0))
    mine = pl.BlockSpec((ROWS, D), lambda i: (own(i), 0))
    dma = pltpu.SemaphoreType.DMA
    out_specs = [pl.BlockSpec(memory_space=pl.ANY)] * 2
    out_shape = [jax.ShapeDtypeStruct((seq, D), bf16)] * 2
    scratch = [
        pltpu.VMEM((half, ROWS, D), bf16),
        pltpu.VMEM((half, ROWS, D), bf16),
        pltpu.VMEM((16, D), f32),
        pltpu.VMEM((16, D), f32),
    ]
    sems = [dma((half,)), dma((half,)), dma, dma]
    if small:
        out_specs += [full((3, SIDE, PAIR)), full((16, 128))]
        out_shape += [
            jax.ShapeDtypeStruct((3, SIDE, PAIR), f32),
            jax.ShapeDtypeStruct((16, 128), f32),
        ]
        scratch += [pltpu.VMEM((CHUNKS, CHUNK, PAIR), bf16)] * 3
        scratch += [pltpu.VMEM((6, CHUNK, PAIR), bf16)]
        scratch += [pltpu.VMEM((8, 16, 128), f32)] * 2 + [pltpu.VMEM((CHUNK, PAIR), f32)]
        sems += [dma((6,))] * 2 + [dma((CHUNKS,))] * 2 + [dma((6,))] * 2 + [dma((7,)), dma((8,))]
    else:
        out_specs += [full((16, D)), full((3, SIDE, PAIR)), full((3, SIDE, PAIR))]
        out_shape += [jax.ShapeDtypeStruct((16, D), f32)] + [jax.ShapeDtypeStruct((3, SIDE, PAIR), bf16)] * 2
    scratch_more = [pltpu.VMEM((2, half, ROWS, D), bf16), pltpu.VMEM((3 * SIDE, D), f32)]
    scratch_more += [pltpu.VMEM((3, SIDE, PAIR), bf16)] * 2 + [dma((2, half))] * 3
    return pl.pallas_call(
        functools.partial(last_kernel, small),
        grid=(GRAD_STEPS + 2 * half + 2,),
        in_specs=[
            wide(D),
            wide(PAIR),
            wide(PAIR),
            wide(PAIR),
            row,
            row,
            row,
            full(cat.shape),
            pl.BlockSpec((ROWS, D), lambda i: (core() * half + own(i), 0)),
            pl.BlockSpec((1, ROWS), lambda i: (0, core() * half + own(i))),
            full((16, D)),
            mine,
            full((8, D)),
            mine,
            mine,
            mine,
            full(mid_near.shape),
            full(mid_keep.shape),
        ],
        out_specs=out_specs,
        out_shape=out_shape,
        scratch_shapes=scratch + sems + scratch_more,
        compiler_params=params(collective_id=2, has_side_effects=True),
        cost_estimate=cost(38),
        name="last",
    )(norm, dq, dk, dv, dq, dk, dv, cat, tokens, passes, vec, grad_second, sums_two, second, chip, far, mid_near, mid_keep)


def precondition(grad, weight, left, right, left_root, right_root):
    high = lax.Precision.HIGHEST
    left_new = decay * left + (1.0 - decay) * jnp.einsum(
        "...ij,...kj->...ik", grad, grad, precision=high
    )
    right_new = decay * right + (1.0 - decay) * jnp.einsum(
        "...ji,...jk->...ik", grad, grad, precision=high
    )
    half = jnp.einsum("...ij,...jk->...ik", left_root, grad, precision=high)
    step = jnp.einsum("...ij,...jk->...ik", half, right_root, precision=high)
    return (left_new, right_new, step, weight - rate_matrix * step)


def two_part(value):
    high = value.astype(bf16)
    return high, (value - high.astype(f32)).astype(bf16)


def dot_three(dot, a, b):
    return dot(a[0], b[0]) + (dot(a[0], b[1]) + dot(a[1], b[0]))


def renew_kernel(
    late, own, one, two, three, weight, left, right, left_root, right_root, output, input_grad,
    left_new, right_new, step, new, output_new, input_grad_new,
):
    output_new[...] = output[...]
    input_grad_new[...] = input_grad[...]

    @pl.when(pl.program_id(0) < 3)
    def _():
        early = own[0].astype(f32) + one[0].astype(f32) + two[0].astype(f32) + three[0].astype(f32)
        z = lax.axis_index("dp") // 2
        both = late[0] + jnp.where(z > 1, early, 0.0)
        for n in range(2):
            grad = both[:, n * SIDE : (n + 1) * SIDE]
            grad = two_part(jnp.where(z == 0, grad.T, grad))
            left_new[0, n] = decay * left[0, n] + (1.0 - decay) * dot_three(nt, grad, grad)
            right_new[0, n] = decay * right[0, n] + (1.0 - decay) * dot_three(tn, grad, grad)
            half = dot_three(nn, two_part(left_root[0, n]), grad)
            value = dot_three(nn, two_part(half), two_part(right_root[0, n]))
            step[0, n] = value
            new[0, n] = weight[0, n] - rate_matrix * value


def renew(late, own, far, weight, left, right, left_root, right_root, output, input_grad):
    pair = pl.BlockSpec((1, SIDE, PAIR), lambda i: (jnp.minimum(i, 2), 0, 0))
    slot = pl.BlockSpec((1, 2, SIDE, SIDE), lambda i: (0, jnp.minimum(i, 2), 0, 0))
    rows = pl.BlockSpec((output.shape[0] // 4, D), lambda i: (i, 0))
    return pl.pallas_call(
        renew_kernel,
        grid=(4,),
        in_specs=[pair] * 5 + [slot] * 5 + [rows] * 2,
        out_specs=[slot] * 4 + [rows] * 2,
        out_shape=[jax.ShapeDtypeStruct(weight.shape, f32)] * 4
        + [jax.ShapeDtypeStruct(value.shape, value.dtype) for value in (output, input_grad)],
        compiler_params=params(),
        cost_estimate=cost(8),
        name="renew",
    )(late, own, *far, weight, left, right, left_root, right_root, output, input_grad)


def to_pairs(blocks):
    n = blocks.shape[0] // 2
    return blocks.reshape(n, 2, SIDE, SIDE).transpose(0, 2, 1, 3).reshape(n, SIDE, PAIR)


def from_pairs(pairs):
    n = pairs.shape[0]
    return pairs.reshape(n, SIDE, 2, SIDE).transpose(0, 2, 1, 3).reshape(2 * n, SIDE, SIDE)


def swap(value, bit):
    return lax.ppermute(value, "tensor", [(t, t ^ bit) for t in range(NT)])


def hop_x(value):
    return lax.ppermute(value, "dp", [(d, d ^ 1) for d in range(8)])


def hop_z(value, turn, ends):
    pairs = [(d, (d + 2 * turn) % 8) for d in range(8) if (d // 2 + turn) % 4 in ends]
    return lax.ppermute(value, "dp", pairs)


def tie(*values):
    return lax.optimization_barrier(values)


def on_device(
    tokens,
    pass_ids,
    doc_lengths,
    cotangent,
    block_weights,
    vector_params,
    vector_moment,
    block_left,
    block_right,
    block_left_root,
    block_right_root,
):
    t, dp = lax.axis_index("tensor"), lax.axis_index("dp")
    core, side = t % 2, t // 2
    n_dp = lax.axis_size("dp")
    small = n_dp == 8
    z, column = (dp // 2, dp % 2) if small else (0, 0)
    lens = doc_lengths[0]
    seq = tokens.shape[0]
    passes = pass_ids.reshape(1, seq)
    total_blocks = (D // SIDE) * (4 + 2 * (FF // D))
    slots = block_weights.shape[1] * n_dp

    if small:
        pairs, wo_other, vec, norm, q, k, v, cat = gather(block_weights, vector_params, tokens, passes)
    else:
        every = lax.all_gather(block_weights.astype(bf16), "dp", axis=1, tiled=True)[0]
        near = to_pairs(every[:total_blocks])
        far = swap(near, 2)
        pairs = jnp.where(side == 0, jnp.stack([near, far]), jnp.stack([far, near]))
        vec = lax.all_gather(vector_params, "dp", axis=1, tiled=True)
        vec = jnp.pad(vec, ((0, 16 - vec.shape[0]), (0, 0)))
        wo_other = swap(pairs[:, 6:8], 1)
        norm, q, k, v, cat = project(tokens, passes, vec, pairs)
    mine, lse = attend(lens, q, k, v)
    out_chip, second, grad_second, grad_mixed, sums_two, mid_send, mid_keep, *ends = feed(
        small, tokens, passes, vec, mine, cotangent, pairs, wo_other
    )
    out_far = swap(out_chip, 2)
    if small:
        far = [hop_z(ends[turn], turn, (2, 3)) for turn in (1, 2, 3)]
        mid_send = hop_x(mid_send)
    dq, dk, dv = attend_back(lens, q, k, v, mine, lse, grad_mixed)
    if small:
        *far, out_far, mid_send, dq = tie(*far, out_far, mid_send, dq)
    output, input_grad, *sums = last(
        small, norm, dq, dk, dv, cat, tokens, passes, vec, grad_second, sums_two, second, out_chip, out_far,
        mid_send, mid_keep,
    )
    if small:
        late, vector_sum = sums
        left_new, right_new, step, weight_new, output, input_grad = renew(
            late, ends[0], far, block_weights, block_left, block_right, block_left_root, block_right_root,
            output, input_grad,
        )
        vector_grad = vector_sum[: PASSES + 4, : vector_params.shape[1]]
    else:
        vector_part, g_send, g_keep = sums[0][: PASSES + 4], *sums[1:]
        send, keep = ends
        rest = jnp.stack(
            [
                jnp.concatenate([mid_keep, keep]).reshape(3, 3, SIDE, PAIR),
                jnp.concatenate([mid_send, send]).reshape(3, 3, SIDE, PAIR),
            ],
            axis=1,
        )
        grad_qkv = from_pairs(jnp.concatenate([g_keep, g_send], axis=0)).swapaxes(1, 2)
        grad_rest = from_pairs(rest.reshape(18, SIDE, PAIR))
        spare = jnp.zeros((slots - total_blocks, SIDE, SIDE), bf16)
        grad_blocks = jnp.concatenate([grad_qkv, grad_rest, spare], axis=0)[None].astype(f32)
        owned = lax.psum_scatter(grad_blocks, "dp", scatter_dimension=1, tiled=True)
        vector_grad = lax.psum_scatter(vector_part, "dp", scatter_dimension=1, tiled=True)
        left_new, right_new, step, weight_new = precondition(
            owned, block_weights, block_left, block_right, block_left_root, block_right_root
        )
    moment_new = decay * vector_moment + (1.0 - decay) * vector_grad * vector_grad
    vector_new = vector_params - rate_vector * vector_grad / (jnp.sqrt(moment_new) + moment_eps)
    return (
        output,
        input_grad,
        left_new,
        right_new,
        step,
        weight_new,
        vector_grad,
        moment_new,
        vector_new,
    )


def solution(mesh):
    rows, line = P("dp", None), P(None, "dp")
    block = P("tensor", "dp", None, None)
    return jax.shard_map(
        on_device,
        mesh=mesh,
        in_specs=(rows, P("dp"), rows, rows, block, line, line, block, block, block, block),
        out_specs=(rows, rows, block, block, block, block, line, line, line),
        check_vma=False,
    )
```

```python
import functools

import jax
import jax.numpy as jnp
from jax import lax
from jax.experimental import pallas as pl
from jax.experimental.pallas import tpu as pltpu
from jax.sharding import PartitionSpec as P

D = 768
HD = 64
FF = 3072
PASSES = 5
SIDE = 192
PAIR = 2 * SIDE
ROWS = 256
WIDE = 512
DOCS = 8
NT = 4

norm_eps = 1e-05
moment_eps = 1e-08
rate_matrix = 0.03
rate_vector = 0.2
decay = 0.5
gelu_coef = 0.7978845608028654
masked_score = -1e30
f32 = jnp.float32
bf16 = jnp.bfloat16
MESH = pl.DeviceIdType.MESH


def nn(a, b):
    return lax.dot_general(a, b, (((1,), (0,)), ((), ())), preferred_element_type=f32)


def nt(a, b):
    return lax.dot_general(a, b, (((1,), (1,)), ((), ())), preferred_element_type=f32)


def tn(a, b):
    return lax.dot_general(a, b, (((0,), (0,)), ((), ())), preferred_element_type=f32)


def split_three(value):
    high = value.astype(bf16)
    rest = value - high.astype(f32)
    mid = rest.astype(bf16)
    return high, mid, (rest - mid.astype(f32)).astype(bf16)


def one_hot(pass_row):
    kinds = lax.broadcasted_iota(jnp.int32, (16, pass_row.shape[1]), 0)
    return (kinds == pass_row).astype(f32).astype(bf16)


def embedded(tokens, pass_row, vec):
    chosen = jnp.concatenate([one_hot(pass_row)] * 3, axis=0)
    return tokens.astype(f32) + tn(chosen, jnp.concatenate(split_three(vec), axis=0))


def hat_of(hidden):
    mean = jnp.mean(hidden, axis=-1, keepdims=True)
    center = hidden - mean
    spread = jnp.mean(center * center, axis=-1, keepdims=True)
    root = lax.rsqrt(spread + norm_eps)
    return center * root, root


def norm_back(hat, root, grad, gain):
    scaled = grad * gain
    first = jnp.mean(scaled, axis=-1, keepdims=True)
    second = jnp.mean(scaled * hat, axis=-1, keepdims=True)
    return root * (scaled - first - hat * second)


def params(mebibytes=56, **kw):
    return pltpu.CompilerParams(vmem_limit_bytes=mebibytes * 1024 * 1024, **kw)


def cost(micros):
    return pl.CostEstimate(flops=int(micros * 1.1e9), bytes_accessed=int(micros * 1e6), transcendentals=0)


def full(shape):
    return pl.BlockSpec(shape, lambda *_: (0,) * len(shape))


def gather_kernel(
    own, vec_own, tokens, passes,
    all_pairs, wo_other, vec_out, norm, q, k_out, v, cat,
    pack, vec_pack, vec_land, wq, tok, norm_s, qkv_s, cat_s, *sems,
):
    (
        s_z1, r_z1, s_x1, r_x1, s_y1, r_y1, s_d1, r_d1, s_l, r_l, s_r, r_r, s_x2, r_x2, s_y2, r_y2, s_v, r_v, s_c, r_c,
        s_out, s_cat, s_tok, loc,
    ) = sems
    dp, t = lax.axis_index("dp"), lax.axis_index("tensor")
    z, x = dp // 2, dp % 2
    y, core = t // 2, t % 2
    far_x, far_y, near = z * 2 + (1 - x), (1 - y) * 2 + core, y * 2 + (1 - core)

    barrier = pltpu.get_barrier_semaphore()
    peers = [lax.rem(dp + n, 8) for n in range(1, 8)]
    for peer in peers:
        pl.semaphore_signal(barrier, inc=1, device_id={"dp": peer}, device_id_type=MESH)
    for to in (far_y, near):
        pl.semaphore_signal(barrier, inc=1, device_id={"tensor": to}, device_id_type=MESH)

    tok_copy = pltpu.make_async_copy(tokens, tok, s_tok)
    tok_copy.start()
    for m in range(3):
        pair = jnp.concatenate([own[0, 2 * m], own[0, 2 * m + 1]], axis=1).astype(bf16)
        pack[m] = pair

        @pl.when(z == 0)
        def _():
            wq[y, 3 * x + m] = pair

    vec_pack[...] = jnp.zeros_like(vec_pack)
    vec_pack[0 : PASSES + 4, 0 : D // 8] = vec_own[...]
    pl.semaphore_wait(barrier, 9)

    started = []

    def send(src, dst, s_sem, r_sem, to, cond=None):
        copy = pltpu.make_async_remote_copy(
            src_ref=src, dst_ref=dst, send_sem=s_sem, recv_sem=r_sem, device_id=to, device_id_type=MESH
        )
        started.append((cond, copy))
        if cond is None:
            copy.start()
        else:
            pl.when(cond)(copy.start)

    def arrived(dst, r_sem, cond=None):
        copy = pltpu.make_async_remote_copy(
            src_ref=dst, dst_ref=dst, send_sem=loc, recv_sem=r_sem, device_id={"dp": far_x}, device_id_type=MESH
        )
        if cond is None:
            copy.wait_recv()
        else:
            pl.when(cond)(copy.wait_recv)

    to_x, to_y, to_left, to_right = {"dp": far_x}, {"tensor": far_y}, {"dp": dp - 2}, {"dp": dp + 2}
    half = SIDE // 2

    def piece(side, column, k):
        return wq.at[side, 3 * column + k // 2, pl.ds((k % 2) * half, half)]

    def at_z(d, m):
        return all_pairs.at[y, 3 * dp + 6 * d + m]

    own_copy = pltpu.make_async_copy(pack, all_pairs.at[y, pl.ds(3 * dp, 3)], loc)
    pl.when(z > 0)(own_copy.start)

    for m in range(3):
        send(pack.at[m], at_z(0, m), s_l.at[0, m], r_l.at[0, m], to_left, z > 0)
    for n, peer in enumerate(peers):
        send(vec_pack, vec_land.at[dp], s_v.at[n], r_v.at[dp], {"dp": peer})
    send(pack.at[0], at_z(0, 0), s_r.at[0, 0], r_r.at[0, 0], to_right, z == 2)
    for m in range(3):
        send(pack.at[m], at_z(0, m), s_x2.at[z, m], r_x2.at[z, m], to_x, z > m)

    def diagonal(k):
        arrived(piece(y, 1 - x, k), r_x1.at[k])
        send(piece(y, 1 - x, k), piece(y, 1 - x, k), s_d1.at[k], r_d1.at[k], to_y)

    def from_right(d, m):
        arrived(at_z(d, m), r_l.at[d - 1, m], z + d < 4)
        if d < 3:
            send(at_z(d, m), at_z(d, m), s_l.at[d, m], r_l.at[d, m], to_left, (z + d < 4) & (z > 0))

    def from_left(d, m, cond):
        arrived(at_z(-d, m), r_r.at[d - 1, m], cond)
        if d == 1:
            send(at_z(-d, m), at_z(-d, m), s_r.at[1, m], r_r.at[1, m], to_right, cond & (z < 3))
        along_x(-d, m, cond)

    def along_x(d, m, cond):
        send(at_z(d, m), at_z(d, m), s_x2.at[z + d, m], r_x2.at[z + d, m], to_x, cond)

    for k in range(6):
        arrived(piece(y, x, k), r_z1.at[k], z > 0)
        send(piece(y, x, k), piece(y, x, k), s_z1.at[k], r_z1.at[k], to_right, z < 3)
        send(piece(y, x, k), piece(y, x, k), s_x1.at[k], r_x1.at[k], to_x)
        send(piece(y, x, k), piece(y, x, k), s_y1.at[k], r_y1.at[k], to_y)
        if k == 5:
            for m in range(3):
                send(pack.at[m], at_z(0, m), s_r.at[0, m], r_r.at[0, m], to_right, (z == 1) | ((z == 2) & (m > 0)))
                send(pack.at[m], at_z(0, m), s_x2.at[z, m], r_x2.at[z, m], to_x, (z > 0) & (z <= m))
        if k >= 1:
            diagonal(k - 1)
        if k % 2 == 1:
            from_right(1, k // 2)
    diagonal(5)
    pl.when(z > 0)(own_copy.wait)
    for m in range(3):
        along_x(1, m, z + 1 < 4)
    for m in range(3):
        from_left(1, m, z > 1)
        from_right(2, m)
        along_x(2, m, z + 2 < 4)
    for k in range(6):
        arrived(piece(1 - y, x, k), r_y1.at[k])
        arrived(piece(1 - y, 1 - x, k), r_d1.at[k])
    for peer in peers:
        arrived(vec_land.at[peer], r_v.at[peer])
    vec_land[dp] = vec_pack[...]
    vec = jnp.concatenate([vec_land[d][:, : D // 8] for d in range(8)], axis=1)
    vec_out[...] = vec
    for n in range(3):
        for i in range(4):
            at = (i % 2) * SIDE
            parts = [wq[h, 2 * n + i // 2][:, at : at + SIDE] for h in range(2)]
            cat_s[n, i * SIDE : (i + 1) * SIDE, :] = jnp.concatenate(parts, axis=1)
    writes = [pltpu.make_async_copy(cat_s, cat, s_cat)]
    writes[0].start()
    tok_copy.wait()

    def rows_of(b):
        rows = slice(b * WIDE, (b + 1) * WIDE)
        hat, _ = hat_of(embedded(tok[rows, :], passes[:, rows], vec))
        low = (hat * vec[PASSES : PASSES + 1] + vec[PASSES + 1 : PASSES + 2]).astype(bf16)
        norm_s[rows, :] = low
        writes.append(pltpu.make_async_copy(norm_s.at[rows, :], norm.at[rows, :], s_out.at[b, 3]))
        writes[-1].start()
        for n, out in enumerate((q, k_out, v)):
            qkv_s[n, rows, :] = nn(low, cat_s[n]).astype(bf16)
            writes.append(pltpu.make_async_copy(qkv_s.at[n, rows, :], out.at[rows, :], s_out.at[b, n]))
            writes[-1].start()

    count = tok.shape[0] // WIDE
    for b in range(count):
        rows_of(b)
        if b == 0:
            for m in range(3):
                from_right(3, m)
                along_x(3, m, z + 3 < 4)
        if b == 1:
            for m in range(3):
                from_left(2, m, z == 3)
        if b == 2:
            for m in range(2):
                ref = all_pairs.at[y, 6 + m]
                arrived(ref, r_x2.at[1, m], x == 1)
                send(ref, ref, s_y2.at[m], r_y2.at[m], to_y)
                send(ref, wo_other.at[y, m], s_c.at[0, m], r_c.at[y, m], {"tensor": near})
    for m in range(2):
        ref = all_pairs.at[1 - y, 6 + m]
        arrived(ref, r_y2.at[m])
        send(ref, wo_other.at[1 - y, m], s_c.at[1, m], r_c.at[1 - y, m], {"tensor": near})
    for w in range(1, 4):
        for m in range(3):
            ref = all_pairs.at[y, 6 * w + 3 * (1 - x) + m]
            if w == 1 and m < 2:
                arrived(ref, r_x2.at[w, m], x == 0)
            else:
                arrived(ref, r_x2.at[w, m])
    for h in range(2):
        for m in range(2):
            arrived(wo_other.at[h, m], r_c.at[h, m])
    for copy in writes:
        copy.wait()
    for cond, copy in started:
        if cond is None:
            copy.wait_send()
        else:
            pl.when(cond)(copy.wait_send)


def gather(block_weights, vector_params, tokens, passes):
    seq = tokens.shape[0]
    dma = pltpu.SemaphoreType.DMA
    sizes = [(6,)] * 8 + [(3, 3)] * 2 + [(2, 3)] * 2 + [(4, 3)] * 2 + [(2,)] * 2 + [(7,), (8,)] + [(2, 2)] * 2
    sizes += [(seq // WIDE, 4)]
    vmem, far = pl.BlockSpec(memory_space=pltpu.VMEM), pl.BlockSpec(memory_space=pl.ANY)
    wide = jax.ShapeDtypeStruct((seq, PAIR), bf16)
    return pl.pallas_call(
        gather_kernel,
        in_specs=[vmem, vmem, far, vmem],
        out_specs=[far, far, vmem, far, far, far, far, far],
        out_shape=[
            jax.ShapeDtypeStruct((2, 24, SIDE, PAIR), bf16),
            jax.ShapeDtypeStruct((2, 2, SIDE, PAIR), bf16),
            jax.ShapeDtypeStruct((16, D), f32),
            jax.ShapeDtypeStruct((seq, D), bf16),
            wide,
            wide,
            wide,
            jax.ShapeDtypeStruct((3, D, PAIR), bf16),
        ],
        scratch_shapes=[
            pltpu.VMEM((3, SIDE, PAIR), bf16),
            pltpu.VMEM((16, 128), f32),
            pltpu.VMEM((8, 16, 128), f32),
            pltpu.VMEM((2, 6, SIDE, PAIR), bf16),
            pltpu.VMEM((seq, D), bf16),
            pltpu.VMEM((seq, D), bf16),
            pltpu.VMEM((3, seq, PAIR), bf16),
            pltpu.VMEM((3, D, PAIR), bf16),
        ]
        + [dma(size) for size in sizes]
        + [dma] * 3,
        compiler_params=params(collective_id=0, has_side_effects=True),
        cost_estimate=cost(60),
        name="gather",
    )(block_weights, vector_params, tokens, passes)


def project_kernel(tok, pas, vec, wq, norm, q, k, v, cat):
    @pl.when(pl.program_id(0) == 0)
    def _():
        for x in range(3):
            for i in range(4):
                at = (i % 2) * SIDE
                parts = [wq[h, 2 * x + i // 2][:, at : at + SIDE] for h in range(2)]
                cat[x, i * SIDE : (i + 1) * SIDE, :] = jnp.concatenate(parts, axis=1)

    first = embedded(tok[...], pas[...], vec[...])
    hat, _ = hat_of(first)
    low = (hat * vec[PASSES : PASSES + 1] + vec[PASSES + 1 : PASSES + 2]).astype(bf16)
    norm[...] = low
    for x, out in enumerate((q, k, v)):
        out[...] = nn(low, cat[x]).astype(bf16)


def project(tokens, passes, vec, wq):
    seq = tokens.shape[0]
    row = lambda n: pl.BlockSpec((WIDE, n), lambda i: (i, 0))
    wide = jax.ShapeDtypeStruct((seq, PAIR), bf16)
    return pl.pallas_call(
        project_kernel,
        grid=(seq // WIDE,),
        in_specs=[
            row(D),
            pl.BlockSpec((1, WIDE), lambda i: (0, i)),
            full((16, D)),
            full((2, 6, SIDE, PAIR)),
        ],
        out_specs=[row(D), row(PAIR), row(PAIR), row(PAIR), full((3, D, PAIR))],
        out_shape=[
            jax.ShapeDtypeStruct((seq, D), bf16),
            wide,
            wide,
            wide,
            jax.ShapeDtypeStruct((3, D, PAIR), bf16),
        ],
        compiler_params=params(),
        cost_estimate=cost(16),
        name="project",
    )(tokens, passes, vec, wq)


def doc_state(lens, base):
    rows = base + lax.broadcasted_iota(jnp.int32, (1, ROWS), 1)
    rows = jnp.concatenate([rows, rows], axis=1)
    begin = jnp.int32(0)
    first = jnp.int32(0)
    starts = jnp.zeros((1, 2 * ROWS), jnp.int32)
    for c in range(DOCS):
        starts = jnp.where(rows >= begin, begin, starts)
        first = jnp.where(base >= begin, begin, first)
        begin = begin + lens[c]
    return rows, starts, first


def two_heads(block):
    left = lax.broadcasted_iota(jnp.int32, block.shape, 1) < HD
    none = jnp.zeros_like(block)
    return jnp.concatenate([jnp.where(left, block, none), jnp.where(left, none, block)], axis=0)


def one_above(both):
    return jnp.concatenate([both[:HD, :ROWS], both[HD:, ROWS:]], axis=0).T


def attend_kernel(lens, q, k, v, out, lse, acc):
    i = pl.program_id(0)
    base = i * ROWS
    rows, starts, first = doc_state(lens, base)
    pairs = [two_heads(q[:, p * 128 : (p + 1) * 128] * bf16(0.125)) for p in range(3)]
    for p in range(3):
        acc[p] = jnp.zeros((128, 2 * ROWS), f32)

    def step(j, carry):
        at = pl.multiple_of(j * ROWS, ROWS)
        keys = at + lax.broadcasted_iota(jnp.int32, (ROWS, 2 * ROWS), 0)
        seen = (keys >= starts) & (keys <= rows)
        here = pl.ds(at, ROWS)
        head = lambda p: slice(p * 128, (p + 1) * 128)
        scores = [jnp.where(seen, nt(k[here, head(p)], pairs[p]), masked_score) for p in range(3)]
        state = []
        for p in range(3):
            before, total = carry[2 * p], carry[2 * p + 1]
            now = jnp.maximum(before, jnp.max(scores[p], axis=0, keepdims=True))
            probs = jnp.exp(scores[p] - now)
            fade = jnp.exp(before - now)
            state += [now, total * fade + jnp.sum(probs, axis=0, keepdims=True)]
            acc[p] = acc[p] * fade + tn(v[here, head(p)], probs.astype(bf16))
        return tuple(state)

    zero = jnp.zeros((1, 2 * ROWS), f32)
    state = lax.fori_loop(first // ROWS, i + 1, step, (zero + masked_score, zero) * 3)
    lines = []
    for p in range(3):
        top, total = state[2 * p], state[2 * p + 1]
        out[:, p * 128 : (p + 1) * 128] = one_above(acc[p] / total).astype(bf16)
        line = top + jnp.log(total)
        lines += [line[:, :ROWS], line[:, ROWS:]]
    lse[...] = jnp.concatenate(lines + lines[:2], axis=0)


def attend(lens, q, k, v):
    seq = q.shape[0]
    row = pl.BlockSpec((ROWS, PAIR), lambda i, s: (i, 0))
    return pl.pallas_call(
        attend_kernel,
        grid_spec=pltpu.PrefetchScalarGridSpec(
            num_scalar_prefetch=1,
            grid=(seq // ROWS,),
            in_specs=[row, full((seq, PAIR)), full((seq, PAIR))],
            out_specs=[row, pl.BlockSpec((8, ROWS), lambda i, s: (0, i))],
            scratch_shapes=[
                pltpu.VMEM((3, 128, 2 * ROWS), f32),
            ],
        ),
        out_shape=[
            jax.ShapeDtypeStruct((seq, PAIR), bf16),
            jax.ShapeDtypeStruct((8, seq), f32),
        ],
        compiler_params=params(),
        cost_estimate=cost(30),
        name="attend",
    )(lens, q, k, v)


def attend_back_kernel(
    lens, q, k, v, mixed, lse, grad_mixed, dq, dk, dv, dk_acc, dv_acc, dq_acc
):
    i = pl.program_id(0)
    count = pl.num_programs(0)
    base = i * ROWS

    @pl.when(i == 0)
    def _():
        dk_acc[...] = jnp.zeros_like(dk_acc)
        dv_acc[...] = jnp.zeros_like(dv_acc)

    rows, starts, first = doc_state(lens, base)
    heads = lax.broadcasted_iota(jnp.int32, (8, 128), 0)
    lanes = lax.broadcasted_iota(jnp.int32, (8, 128), 1)
    pick = (lanes // HD == heads).astype(f32).astype(bf16)
    queries, grads, inner, lines = [], [], [], []
    for p in range(3):
        cols = slice(p * 128, (p + 1) * 128)
        queries.append(two_heads(q[:, cols] * bf16(0.125)))
        grads.append(two_heads(grad_mixed[:, cols]))
        product = grad_mixed[:, cols].astype(f32) * mixed[:, cols].astype(f32)
        high, low, _ = split_three(product)
        sums = nt(pick, high) + nt(pick, low)
        inner.append(jnp.concatenate([sums[0:1], sums[1:2]], axis=1))
        lines.append(jnp.concatenate([lse[2 * p : 2 * p + 1], lse[2 * p + 1 : 2 * p + 2]], axis=1))
        dq_acc[p] = jnp.zeros((128, 2 * ROWS), f32)

    def step(j, carry):
        at = pl.multiple_of(j * ROWS, ROWS)
        keys = at + lax.broadcasted_iota(jnp.int32, (ROWS, 2 * ROWS), 0)
        seen = (keys >= starts) & (keys <= rows)
        here = pl.ds(at, ROWS)
        for p in range(3):
            cols = slice(p * 128, (p + 1) * 128)
            kb = k[here, cols]
            scores = jnp.where(seen, nt(kb, queries[p]) - lines[p], masked_score)
            probs = jnp.exp(scores)
            grad_probs = nt(v[here, cols], grads[p])
            grad_scores = (probs * (grad_probs - inner[p])).astype(bf16)
            dv_acc[here, cols] += nn(probs.astype(bf16), grads[p])
            dk_acc[here, cols] += nn(grad_scores, queries[p])
            dq_acc[p] += tn(kb, grad_scores)
        return carry

    lax.fori_loop(first // ROWS, i + 1, step, 0)
    for p in range(3):
        dq[:, p * 128 : (p + 1) * 128] = (one_above(dq_acc[p]) * 0.125).astype(bf16)

    @pl.when(i == count - 1)
    def _():
        dk[...] = dk_acc[...].astype(bf16)
        dv[...] = dv_acc[...].astype(bf16)


def attend_back(lens, q, k, v, mixed, lse, grad_mixed):
    seq = q.shape[0]
    count = seq // ROWS
    row = pl.BlockSpec((ROWS, PAIR), lambda i, s: (i, 0))
    wide = jax.ShapeDtypeStruct((seq, PAIR), bf16)
    return pl.pallas_call(
        attend_back_kernel,
        grid_spec=pltpu.PrefetchScalarGridSpec(
            num_scalar_prefetch=1,
            grid=(count,),
            in_specs=[
                row,
                full((seq, PAIR)),
                full((seq, PAIR)),
                row,
                pl.BlockSpec((8, ROWS), lambda i, s: (0, i)),
                row,
            ],
            out_specs=[row, full((seq, PAIR)), full((seq, PAIR))],
            scratch_shapes=[
                pltpu.VMEM((seq, PAIR), f32),
                pltpu.VMEM((seq, PAIR), f32),
                pltpu.VMEM((3, 128, 2 * ROWS), f32),
            ],
        ),
        out_shape=[wide, wide, wide],
        compiler_params=params(),
        cost_estimate=cost(40),
        name="attend_back",
    )(lens, q, k, v, mixed, lse, grad_mixed)


def feed_kernel(
    small, tok, pas, vec, mine, cot, wo_mine, wo_other, w1, w2,
    out_chip, second_keep, grad_second, grad_mixed, sums, mid_send, mid_keep, *rest,
):
    results, rest = (rest[:4], rest[4:]) if small else (rest[:2], rest[2:])
    (
        wo, other, up, down, gup, gdown, go, core_out, core_in, far_out, far_in, ga_out, ga_in, oc_out, oc_in,
        g_send, g_keep, g_in, s_core, r_core, s_far, r_far, s_ga, r_ga, s_oc, r_oc, s_x, r_x, s_m, r_m,
    ) = rest
    step = pl.program_id(0)
    half = core_out.shape[0]
    t, dp = lax.axis_index("tensor"), lax.axis_index("dp")
    core, side = t % 2, t // 2
    near, far = side * 2 + (1 - core), (1 - side) * 2 + core
    z, column = (dp // 2, dp % 2) if small else (0, 0)
    far_x = z * 2 + 1 - column

    def copy(src, dst, s_sem, r_sem, j, to):
        return pltpu.make_async_remote_copy(
            src_ref=src.at[j],
            dst_ref=dst.at[j],
            send_sem=s_sem.at[j],
            recv_sem=r_sem.at[j],
            device_id={"tensor": to},
            device_id_type=MESH,
        )

    core_copy = lambda j: copy(core_out, core_in, s_core, r_core, j, near)
    far_copy = lambda j: copy(far_out, far_in, s_far, r_far, j, far)
    ga_copy = lambda j: copy(ga_out, ga_in, s_ga, r_ga, j, near)
    oc_copy = lambda j: copy(oc_out, oc_in, s_oc, r_oc, j, near)

    def x_copy(slot):
        return pltpu.make_async_remote_copy(
            src_ref=g_send.at[slot],
            dst_ref=g_in.at[slot],
            send_sem=s_x.at[slot],
            recv_sem=r_x.at[slot],
            device_id={"dp": far_x},
            device_id_type=MESH,
        )

    def mixed_copy(block):
        rows = pl.ds(pl.multiple_of(block * ROWS, ROWS), ROWS)
        return pltpu.make_async_remote_copy(
            src_ref=mine.at[rows],
            dst_ref=other.at[rows],
            send_sem=s_m.at[block],
            recv_sem=r_m.at[block],
            device_id={"tensor": near},
            device_id_type=MESH,
        )

    barrier = pltpu.get_barrier_semaphore()

    @pl.when(step == 0)
    def _():
        for to in (near, far):
            pl.semaphore_signal(barrier, inc=1, device_id={"tensor": to}, device_id_type=MESH)
        if small:
            pl.semaphore_signal(barrier, inc=1, device_id={"dp": far_x}, device_id_type=MESH)
        for h in range(2):
            for m in range(2):
                rows, cols = slice(h * SIDE, (h + 1) * SIDE), slice(m * PAIR, (m + 1) * PAIR)
                wo[rows, cols] = wo_mine[h, m]
                wo[PAIR + h * SIDE : PAIR + (h + 1) * SIDE, cols] = wo_other[h, m]
        for r in range(4):
            for m in range(2):
                rows, cols = slice(r * SIDE, (r + 1) * SIDE), slice(m * PAIR, (m + 1) * PAIR)
                up[rows, cols] = w1[0, 2 * r + m]
                down[rows, cols] = w2[0, 2 * r + m]
        pl.semaphore_wait(barrier, 3 if small else 2)
        for j in range(half):
            mixed_copy(core * half + j).start()
            mixed_copy((1 - core) * half + j).start()
        gup[...] = jnp.zeros_like(gup)
        gdown[...] = jnp.zeros_like(gdown)
        go[...] = jnp.zeros_like(go)
        sums[...] = jnp.zeros_like(sums)

    @pl.when(step < 2 * half)
    def _():
        j = step // 2
        owner = jnp.where(step % 2 == 0, 1 - core, core)
        here = pl.ds(pl.multiple_of((owner * half + j) * ROWS, ROWS), ROWS)
        first = embedded(tok[...], pas[...], vec[...])
        mixed_copy(owner * half + j).wait_recv()
        second = first + nn(jnp.concatenate([mine[here, :], other[here, :]], axis=1), wo[...])
        hat, _ = hat_of(second)
        low = (hat * vec[PASSES + 2 : PASSES + 3] + vec[PASSES + 3 : PASSES + 4]).astype(bf16)
        upper = nn(low, up[...])
        square = upper * upper
        bent = jnp.tanh(gelu_coef * upper * (1.0 + 0.044715 * square))
        act = (0.5 * upper * (1.0 + bent)).astype(bf16)
        slope = 0.5 * (1.0 + bent) + (0.5 * gelu_coef) * upper * (1.0 - bent * bent) * (
            1.0 + (3 * 0.044715) * square
        )
        grad_act = nt(cot[...], down[...])
        grad_upper = (grad_act * slope).astype(bf16)
        part = nt(grad_upper, up[...])

        @pl.when(step % 2 == 0)
        def _():
            core_out[j] = part.astype(bf16)
            core_copy(j).start()

        @pl.when(step % 2 == 1)
        def _():
            core_copy(j).wait_recv()
            far_out[j] = (part + core_in[j].astype(f32)).astype(bf16)
            far_copy(j).start()
            second_keep[pl.ds(pl.multiple_of(j * ROWS, ROWS), ROWS), :] = second

        gup[...] += tn(low, grad_upper)
        gdown[...] += tn(act, cot[...])
        out_part = nn(act, down[...])

        @pl.when(step % 2 == 0)
        def _():
            oc_out[j] = out_part.astype(bf16)
            oc_copy(j).start()

        @pl.when(step % 2 == 1)
        def _():
            oc_copy(j).wait_recv()
            out_chip[...] = (out_part + oc_in[j].astype(f32)).astype(bf16)

    @pl.when(step == 2 * half - 1)
    def _():
        for r in range(4):
            for m in range(2):
                rows, cols = slice(r * SIDE, (r + 1) * SIDE), slice(m * PAIR, (m + 1) * PAIR)
                for at, total in ((8, gup), (16, gdown)):
                    pair = at + 2 * r + m
                    slot, place = (pair // 6 - 1) * 3 + pair % 3, pair // 3 % 2
                    value = total[rows, cols].astype(bf16)
                    kept, sent, n = (mid_keep, mid_send, slot) if slot < 3 else (g_keep, g_send, slot - 3)

                    @pl.when(column == place)
                    def _():
                        kept[n] = value

                    @pl.when(column != place)
                    def _():
                        sent[n] = value
        if small:
            for n in range(6):
                x_copy(n).start()

    def through_out(grad, block):
        here = pl.ds(pl.multiple_of(block * ROWS, ROWS), ROWS)
        grad_mixed[here, :] = nt(grad, wo[:PAIR, :]).astype(bf16)
        go[...] += tn(mine[here, :], grad)

    @pl.when((step >= 2 * half) & (step < 3 * half))
    def _():
        j = step - 2 * half
        hat, root = hat_of(second_keep[pl.ds(pl.multiple_of(j * ROWS, ROWS), ROWS), :])
        far_copy(j).wait_recv()
        grad = far_out[j].astype(f32) + far_in[j].astype(f32)
        result = cot[...].astype(f32) + norm_back(hat, root, grad, vec[PASSES + 2 : PASSES + 3])
        low = result.astype(bf16)
        ga_out[j] = low
        ga_copy(j).start()
        grad_second[...] = result
        sums[0:1] += jnp.sum(grad * hat, axis=0, keepdims=True)
        sums[1:2] += jnp.sum(grad, axis=0, keepdims=True)
        through_out(low, core * half + j)

    @pl.when(step > 2 * half)
    def _():
        j = step - 2 * half - 1
        ga_copy(j).wait_recv()
        through_out(ga_in[j], (1 - core) * half + j)

    @pl.when(step == 3 * half)
    def _():
        at = pl.multiple_of(side * SIDE, SIDE)
        for m in range(2):
            value = go[pl.ds(at, SIDE), m * PAIR : (m + 1) * PAIR].astype(bf16)

            @pl.when(column == 0)
            def _():
                mid_keep[m] = value

            @pl.when(column != 0)
            def _():
                mid_send[m] = value

        for j in range(half):
            core_copy(j).wait_send()
            oc_copy(j).wait_send()
            mixed_copy(j).wait_send()
            mixed_copy(half + j).wait_send()
            far_copy(j).wait_send()
            ga_copy(j).wait_send()
        if small:
            for n in range(6):
                x_copy(n).wait_send()
                x_copy(n).wait_recv()
                value = (g_keep[n].astype(f32) + g_in[n].astype(f32)).astype(bf16)
                for turn in range(4):

                    @pl.when(lax.rem(z + turn, 4) == n // 3 + 2)
                    def _():
                        results[turn][n % 3] = value
        else:
            results[0][...] = g_send[...]
            results[1][...] = g_keep[...]


def feed(small, tokens, passes, vec, mine, cotangent, pairs, wo_other):
    seq = tokens.shape[0]
    half = seq // ROWS // 2

    def block(i):
        core = lax.axis_index("tensor") % 2
        work = jnp.minimum(i, 2 * half - 1)
        owner = jnp.where(work % 2 == 0, 1 - core, core)
        return owner * half + work // 2

    def cot_block(i):
        core = lax.axis_index("tensor") % 2
        return jnp.where(i < 2 * half, block(i), core * half + jnp.minimum(i - 2 * half, half - 1))

    side = lambda: lax.axis_index("tensor") // 2
    row = lambda n: pl.BlockSpec((ROWS, n), lambda i: (block(i), 0))
    keep = pl.BlockSpec((ROWS, D), lambda i: (jnp.minimum(i // 2, half - 1), 0))
    last = pl.BlockSpec((ROWS, D), lambda i: (jnp.clip(i - 2 * half, 0, half - 1), 0))
    rows = lambda kind: jax.ShapeDtypeStruct((seq // 2, D), kind)
    gr = lambda n: jax.ShapeDtypeStruct((n, SIDE, PAIR), bf16)
    ends = [(3, SIDE, PAIR)] * 4 if small else [(6, SIDE, PAIR)] * 2
    buffer = pltpu.VMEM((half, ROWS, D), bf16)
    dma = pltpu.SemaphoreType.DMA((half,))
    return pl.pallas_call(
        functools.partial(feed_kernel, small),
        grid=(3 * half + 1,),
        in_specs=[
            row(D),
            pl.BlockSpec((1, ROWS), lambda i: (0, block(i))),
            full((16, D)),
            full((seq, PAIR)),
            pl.BlockSpec((ROWS, D), lambda i: (cot_block(i), 0)),
            pl.BlockSpec((2, 2, SIDE, PAIR), lambda i: (0, 3, 0, 0)),
            full(wo_other.shape),
            pl.BlockSpec((1, 8, SIDE, PAIR), lambda i: (side(), 1, 0, 0)),
            pl.BlockSpec((1, 8, SIDE, PAIR), lambda i: (side(), 2, 0, 0)),
        ],
        out_specs=[
            keep,
            full((seq // 2, D)),
            last,
            full((seq, PAIR)),
            full((8, D)),
            full((3, SIDE, PAIR)),
            full((3, SIDE, PAIR)),
        ]
        + [full(shape) for shape in ends],
        scratch_shapes=[
            pltpu.VMEM((D, D), bf16),
            pltpu.VMEM((seq, PAIR), bf16),
            pltpu.VMEM((D, D), bf16),
            pltpu.VMEM((D, D), bf16),
            pltpu.VMEM((D, D), f32),
            pltpu.VMEM((D, D), f32),
            pltpu.VMEM((PAIR, D), f32),
        ]
        + [buffer] * 8
        + [pltpu.VMEM((6, SIDE, PAIR), bf16)] * 3
        + [dma] * 8
        + [pltpu.SemaphoreType.DMA((6,))] * 2
        + [pltpu.SemaphoreType.DMA((2 * half,))] * 2,
        out_shape=[
            rows(bf16),
            rows(f32),
            rows(f32),
            jax.ShapeDtypeStruct((seq, PAIR), bf16),
            jax.ShapeDtypeStruct((8, D), f32),
            gr(3),
            gr(3),
        ]
        + [jax.ShapeDtypeStruct(shape, bf16) for shape in ends],
        compiler_params=params(collective_id=1, has_side_effects=True),
        cost_estimate=cost(50),
        name="feed_forward",
    )(tokens, passes, vec, mine, cotangent, pairs, wo_other, pairs, pairs)


CHUNK = SIDE // 2
CHUNKS = 12
TAKEN = (
    ((8, 3), (10, 4), (12, 12)),
    ((5, 1), (7, 3), (8, 4), (9, 6), (10, 7), (11, 8), (12, 12)),
    ((2, 2), (4, 3), (5, 4), (7, 6), (8, 8), (9, 9), (10, 11), (12, 12)),
    ((0, 3), (2, 5), (4, 6), (5, 7), (6, 8), (7, 12)),
)
GRAD_STEPS = 3


def last_kernel(
    small, norm_all, dq_all, dk_all, dv_all, cat, tok, pas, vec, grad_second, sums_two, second, chip, far,
    mid_near, mid_keep, output, input_grad, *rest,
):
    if small:
        late, vec_sum = rest[:2]
        rest = rest[2:]
        (
            core_out, core_in, sums, core_sums, x_in, z_in, z_out, up_in, v_out, v_in, total,
            s_core, r_core, s_sum, r_sum, s_x, r_x, s_z, r_z, s_up, r_up, s_v, r_v, ready, norm, dq, dk, dv, g_send, g_keep,
            s_own, s_res, r_res, s_in,
        ) = rest
    else:
        (
            vec_sum, send_out, keep_out, core_out, core_in, sums, core_sums, s_core, r_core, s_sum, r_sum, ready,
            norm, dq, dk, dv, g_send, g_keep, s_own, s_res, r_res, s_in,
        ) = rest
    step = pl.program_id(0)
    i = step - GRAD_STEPS
    half = core_out.shape[0]
    t, dp = lax.axis_index("tensor"), lax.axis_index("dp")
    core, side = t % 2, t // 2
    near = side * 2 + (1 - core)
    z, column = (dp // 2, dp % 2) if small else (0, 0)
    far_x = z * 2 + 1 - column
    peers = [lax.rem(dp + k, 8) for k in range(1, 8)]

    def copy(src, dst, s_sem, r_sem, to):
        return pltpu.make_async_remote_copy(
            src_ref=src, dst_ref=dst, send_sem=s_sem, recv_sem=r_sem, device_id=to, device_id_type=MESH
        )

    core_copy = lambda j: copy(core_out.at[j], core_in.at[j], s_core.at[j], r_core.at[j], {"tensor": near})
    sum_copy = lambda: copy(sums, core_sums, s_sum, r_sum, {"tensor": near})

    def rows_at(n, j, owner):
        rows = pl.ds(pl.multiple_of((owner * half + j) * ROWS, ROWS), ROWS)
        return (output, input_grad)[n].at[rows]

    own_result = lambda n, j: pltpu.make_async_copy(ready.at[n, j], rows_at(n, j, core), s_own.at[n, j])
    near_result = lambda n, j, owner: copy(
        ready.at[n, j], rows_at(n, j, owner), s_res.at[n, j], r_res.at[n, j], {"tensor": near}
    )

    def part_of(ref, k):
        return ref.at[k // 2, pl.ds((k % 2) * CHUNK, CHUNK)]

    x_copy = lambda k: copy(part_of(g_send, k), x_in.at[k], s_x.at[k], r_x.at[k], {"dp": far_x})
    z_copy = lambda k: copy(z_out.at[k], z_in.at[k], s_z.at[k], r_z.at[k], {"dp": dp - 2})
    up_copy = lambda k: copy(z_out.at[k], up_in.at[k - 6], s_up.at[k - 6], r_up.at[k - 6], {"dp": dp + 2})
    v_copy = lambda n: copy(v_out.at[peers[n]], v_in.at[dp], s_v.at[n], r_v.at[dp], {"dp": peers[n]})
    barrier = pltpu.get_barrier_semaphore()

    loads = [
        pltpu.make_async_copy(src, dst, s_in.at[n])
        for n, (src, dst) in enumerate(((norm_all, norm), (dq_all, dq), (dv_all, dv), (dk_all, dk)))
    ]

    @pl.when(step == 0)
    def _():
        for load in loads:
            load.start()
        pl.semaphore_signal(barrier, inc=1, device_id={"tensor": near}, device_id_type=MESH)
        if small:
            for peer in peers:
                pl.semaphore_signal(barrier, inc=1, device_id={"dp": peer}, device_id_type=MESH)
            late[...] = jnp.zeros_like(late)
        sums[...] = jnp.zeros_like(sums)
        sums[PASSES + 2 : PASSES + 4] = sums_two[0:2]
        pl.semaphore_wait(barrier, 8 if small else 1)

    def mine_of(grad):
        return jnp.where(side == 0, grad[:, :SIDE], grad[:, SIDE:])

    def pairs_of(grad):
        value = tn(grad, norm[...]).astype(bf16)
        return value[:, :PAIR], value[:, PAIR:]

    second_two = jnp.where(jnp.asarray(column) == 0, 1, 0)

    @pl.when(step == 0)
    def _():
        for load in loads[:3]:
            load.wait()
        both = pairs_of(jnp.where(jnp.asarray(column) == 0, mine_of(dv), mine_of(dq)))
        for m in range(2):
            g_send[second_two + m] = both[m]
        if small:
            for m in range(4):
                x_copy(2 * second_two + m).start()

    @pl.when(step == 1)
    def _():
        loads[3].wait()
        both = pairs_of(mine_of(dk))
        for place, (kept, sent) in enumerate(((0, 1), (1, 0))):

            @pl.when(jnp.asarray(column) == place)
            def _():
                g_keep[2 - 2 * place] = both[kept]
                g_send[2 * place] = both[sent]

        if small:
            for m in range(2):
                x_copy(4 * column + m).start()

    @pl.when(step == 2)
    def _():
        both = pairs_of(jnp.where(jnp.asarray(column) == 0, mine_of(dq), mine_of(dv)))
        for m in range(2):
            g_keep[1 - second_two + m] = both[m]
        if not small:
            send_out[...] = g_send[...]
            keep_out[...] = g_keep[...]

    @pl.when((i >= 0) & (i < 2 * half))
    def _():
        block = lax.rem(i + (1 - core) * half, 2 * half)
        rows = pl.ds(pl.multiple_of(block * ROWS, ROWS), ROWS)
        part = nt(dq[rows, :], cat[0]) + nt(dk[rows, :], cat[1]) + nt(dv[rows, :], cat[2])

        @pl.when(i < half)
        def _():
            core_out[i] = part.astype(bf16)
            core_copy(i).start()

        @pl.when(i >= half)
        def _():
            j = i - half
            hat, root = hat_of(embedded(tok[...], pas[...], vec[...]))
            core_copy(j).wait_recv()
            grad = part + core_in[j].astype(f32)
            result = grad_second[...] + norm_back(hat, root, grad, vec[PASSES : PASSES + 1])
            ready[0, j] = (second[...] + (chip[...].astype(f32) + far[...].astype(f32))).astype(bf16)
            ready[1, j] = result.astype(bf16)
            for n in range(2):
                own_result(n, j).start()
                near_result(n, j, core).start()
            chosen = one_hot(pas[...])
            high, mid, _ = split_three(result)
            sums[...] += nn(chosen, high) + nn(chosen, mid)
            sums[PASSES : PASSES + 1] += jnp.sum(grad * hat, axis=0, keepdims=True)
            sums[PASSES + 1 : PASSES + 2] += jnp.sum(grad, axis=0, keepdims=True)

    @pl.when(i == 2 * half - 1)
    def _():
        sum_copy().start()

    if small:

        def term_of(k):
            rows = pl.ds(pl.multiple_of((k % 2) * CHUNK, 16), CHUNK)

            @pl.when(jnp.asarray(k) < 6)
            def _():
                x_copy(k).wait_recv()
                total[...] = g_keep[k // 2, rows, :].astype(f32) + x_in[k].astype(f32)

            @pl.when(jnp.asarray(k) >= 6)
            def _():
                total[...] = mid_keep[k // 2 - 3, rows, :].astype(f32) + mid_near[k // 2 - 3, rows, :].astype(f32)

            return total[...]

        def keep_late(k, pair, total):
            late[pair, pl.ds(pl.multiple_of((k % 2) * CHUNK, 16), CHUNK), :] = total

        def pass_on(k):
            term = term_of(k)

            @pl.when(z < 3)
            def _():
                z_copy(k).wait_recv()

            below = jnp.where(z < 3, z_in[k].astype(f32), 0.0)
            passed = term + below

            @pl.when((z > 1) | ((z == 1) & (k < 6)))
            def _():
                z_out[k] = passed.astype(bf16)
                z_copy(k).start()

            @pl.when(z == 0)
            def _():
                keep_late(k, k // 2, passed)

            @pl.when((z == 1) & (k >= 6))
            def _():
                up_copy(k).wait_recv()
                keep_late(k, k // 2 - 3, passed + up_in[k - 6].astype(f32))

        def at_position(p, carry):
            k = jnp.where(p < 3, p + 6, jnp.where(p < 9, lax.rem(p + 3 + 2 * column, 6), p))

            @pl.when((z > 0) | (k < 6))
            def _():
                pass_on(k)

            return carry

        begin, end = jnp.int32(0), jnp.int32(0)
        for place, line in enumerate(TAKEN):
            for at, upto in line:
                begin = jnp.where((z == place) & (step > at), upto, begin)
                end = jnp.where((z == place) & (step >= at), upto, end)
        lax.fori_loop(begin, end, at_position, 0)

        @pl.when((step == 0) & (z == 0))
        def _():
            for k in range(6, CHUNKS):
                z_out[k] = term_of(k).astype(bf16)
                up_copy(k).start()

    @pl.when(i == 2 * half)
    def _():
        sum_copy().wait_recv()
        total = sums[...] + core_sums[...]
        if small:
            wide = D // 8
            for d in range(8):
                v_out[d, :, 0:wide] = total[:, d * wide : (d + 1) * wide]
                v_out[d, :, wide:] = jnp.zeros((16, 128 - wide), f32)
            for n in range(7):
                v_copy(n).start()
        else:
            vec_sum[...] = total

    @pl.when(step == pl.num_programs(0) - 1)
    def _():
        for j in range(half):
            core_copy(j).wait_send()
            for n in range(2):
                own_result(n, j).wait()
                near_result(n, j, core).wait_send()
                near_result(n, j, 1 - core).wait_recv()
        sum_copy().wait_send()
        if small:
            for peer in peers:
                copy(v_out.at[0], v_in.at[peer], s_v.at[0], r_v.at[peer], {"dp": far_x}).wait_recv()
            v_in[dp] = v_out[dp]
            total = v_in[0]
            for d in range(1, 8):
                total = total + v_in[d]
            vec_sum[...] = total
            for n in range(7):
                v_copy(n).wait_send()
            for k in range(CHUNKS):
                if k < 6:
                    x_copy(k).wait_send()
                    pl.when(z > 0)(z_copy(k).wait_send)
                else:
                    pl.when(z > 1)(z_copy(k).wait_send)
                    pl.when(z == 0)(up_copy(k).wait_send)


def last(
    small, norm, dq, dk, dv, cat, tokens, passes, vec, grad_second, sums_two, second, chip, far, mid_near, mid_keep
):
    seq = dq.shape[0]
    half = seq // ROWS // 2
    core = lambda: lax.axis_index("tensor") % 2

    own = lambda i: jnp.clip(i - GRAD_STEPS - half, 0, half - 1)
    mine = pl.BlockSpec((ROWS, D), lambda i: (own(i), 0))
    dma = pltpu.SemaphoreType.DMA
    out_specs = [pl.BlockSpec(memory_space=pl.ANY)] * 2
    out_shape = [jax.ShapeDtypeStruct((seq, D), bf16)] * 2
    scratch = [
        pltpu.VMEM((half, ROWS, D), bf16),
        pltpu.VMEM((half, ROWS, D), bf16),
        pltpu.VMEM((16, D), f32),
        pltpu.VMEM((16, D), f32),
    ]
    sems = [dma((half,)), dma((half,)), dma, dma]
    if small:
        out_specs += [full((3, SIDE, PAIR)), full((16, 128))]
        out_shape += [
            jax.ShapeDtypeStruct((3, SIDE, PAIR), f32),
            jax.ShapeDtypeStruct((16, 128), f32),
        ]
        scratch += [pltpu.VMEM((CHUNKS, CHUNK, PAIR), bf16)] * 3
        scratch += [pltpu.VMEM((6, CHUNK, PAIR), bf16)]
        scratch += [pltpu.VMEM((8, 16, 128), f32)] * 2 + [pltpu.VMEM((CHUNK, PAIR), f32)]
        sems += [dma((6,))] * 2 + [dma((CHUNKS,))] * 2 + [dma((6,))] * 2 + [dma((7,)), dma((8,))]
    else:
        out_specs += [full((16, D)), full((3, SIDE, PAIR)), full((3, SIDE, PAIR))]
        out_shape += [jax.ShapeDtypeStruct((16, D), f32)] + [jax.ShapeDtypeStruct((3, SIDE, PAIR), bf16)] * 2
    scratch_more = [pltpu.VMEM((2, half, ROWS, D), bf16), pltpu.VMEM((seq, D), bf16)]
    scratch_more += [pltpu.VMEM((seq, PAIR), bf16)] * 3
    scratch_more += [pltpu.VMEM((3, SIDE, PAIR), bf16)] * 2 + [dma((2, half))] * 3 + [dma((4,))]
    return pl.pallas_call(
        functools.partial(last_kernel, small),
        grid=(GRAD_STEPS + 2 * half + 2,),
        in_specs=[
            *[pl.BlockSpec(memory_space=pl.ANY)] * 4,
            full(cat.shape),
            pl.BlockSpec((ROWS, D), lambda i: (core() * half + own(i), 0)),
            pl.BlockSpec((1, ROWS), lambda i: (0, core() * half + own(i))),
            full((16, D)),
            mine,
            full((8, D)),
            mine,
            mine,
            mine,
            full(mid_near.shape),
            full(mid_keep.shape),
        ],
        out_specs=out_specs,
        out_shape=out_shape,
        scratch_shapes=scratch + sems + scratch_more,
        compiler_params=params(collective_id=2, has_side_effects=True),
        cost_estimate=cost(38),
        name="last",
    )(norm, dq, dk, dv, cat, tokens, passes, vec, grad_second, sums_two, second, chip, far, mid_near, mid_keep)


def precondition(grad, weight, left, right, left_root, right_root):
    high = lax.Precision.HIGHEST
    left_new = decay * left + (1.0 - decay) * jnp.einsum(
        "...ij,...kj->...ik", grad, grad, precision=high
    )
    right_new = decay * right + (1.0 - decay) * jnp.einsum(
        "...ji,...jk->...ik", grad, grad, precision=high
    )
    half = jnp.einsum("...ij,...jk->...ik", left_root, grad, precision=high)
    step = jnp.einsum("...ij,...jk->...ik", half, right_root, precision=high)
    return (left_new, right_new, step, weight - rate_matrix * step)


def two_part(value):
    high = value.astype(bf16)
    return high, (value - high.astype(f32)).astype(bf16)


def dot_three(dot, a, b):
    return dot(a[0], b[0]) + (dot(a[0], b[1]) + dot(a[1], b[0]))


def renew_kernel(
    late, own, one, two, three, weight, left, right, left_root, right_root, output, input_grad,
    left_new, right_new, step, new, output_new, input_grad_new,
):
    output_new[...] = output[...]
    input_grad_new[...] = input_grad[...]

    @pl.when(pl.program_id(0) < 3)
    def _():
        early = own[0].astype(f32) + one[0].astype(f32) + two[0].astype(f32) + three[0].astype(f32)
        z = lax.axis_index("dp") // 2
        both = late[0] + jnp.where(z > 1, early, 0.0)
        for n in range(2):
            grad = both[:, n * SIDE : (n + 1) * SIDE]
            grad = two_part(jnp.where(z == 0, grad.T, grad))
            left_new[0, n] = decay * left[0, n] + (1.0 - decay) * dot_three(nt, grad, grad)
            right_new[0, n] = decay * right[0, n] + (1.0 - decay) * dot_three(tn, grad, grad)
            half = dot_three(nn, two_part(left_root[0, n]), grad)
            value = dot_three(nn, two_part(half), two_part(right_root[0, n]))
            step[0, n] = value
            new[0, n] = weight[0, n] - rate_matrix * value


def renew(late, own, far, weight, left, right, left_root, right_root, output, input_grad):
    pair = pl.BlockSpec((1, SIDE, PAIR), lambda i: (jnp.minimum(i, 2), 0, 0))
    slot = pl.BlockSpec((1, 2, SIDE, SIDE), lambda i: (0, jnp.minimum(i, 2), 0, 0))
    rows = pl.BlockSpec((output.shape[0] // 4, D), lambda i: (i, 0))
    return pl.pallas_call(
        renew_kernel,
        grid=(4,),
        in_specs=[pair] * 5 + [slot] * 5 + [rows] * 2,
        out_specs=[slot] * 4 + [rows] * 2,
        out_shape=[jax.ShapeDtypeStruct(weight.shape, f32)] * 4
        + [jax.ShapeDtypeStruct(value.shape, value.dtype) for value in (output, input_grad)],
        compiler_params=params(),
        cost_estimate=cost(8),
        name="renew",
    )(late, own, *far, weight, left, right, left_root, right_root, output, input_grad)


def to_pairs(blocks):
    n = blocks.shape[0] // 2
    return blocks.reshape(n, 2, SIDE, SIDE).transpose(0, 2, 1, 3).reshape(n, SIDE, PAIR)


def from_pairs(pairs):
    n = pairs.shape[0]
    return pairs.reshape(n, SIDE, 2, SIDE).transpose(0, 2, 1, 3).reshape(2 * n, SIDE, SIDE)


def swap(value, bit):
    return lax.ppermute(value, "tensor", [(t, t ^ bit) for t in range(NT)])


def hop_x(value):
    return lax.ppermute(value, "dp", [(d, d ^ 1) for d in range(8)])


def hop_z(value, turn, ends):
    pairs = [(d, (d + 2 * turn) % 8) for d in range(8) if (d // 2 + turn) % 4 in ends]
    return lax.ppermute(value, "dp", pairs)


def tie(*values):
    return lax.optimization_barrier(values)


def on_device(
    tokens,
    pass_ids,
    doc_lengths,
    cotangent,
    block_weights,
    vector_params,
    vector_moment,
    block_left,
    block_right,
    block_left_root,
    block_right_root,
):
    t, dp = lax.axis_index("tensor"), lax.axis_index("dp")
    core, side = t % 2, t // 2
    n_dp = lax.axis_size("dp")
    small = n_dp == 8
    z, column = (dp // 2, dp % 2) if small else (0, 0)
    lens = doc_lengths[0]
    seq = tokens.shape[0]
    passes = pass_ids.reshape(1, seq)
    total_blocks = (D // SIDE) * (4 + 2 * (FF // D))
    slots = block_weights.shape[1] * n_dp

    if small:
        pairs, wo_other, vec, norm, q, k, v, cat = gather(block_weights, vector_params, tokens, passes)
    else:
        every = lax.all_gather(block_weights.astype(bf16), "dp", axis=1, tiled=True)[0]
        near = to_pairs(every[:total_blocks])
        far = swap(near, 2)
        pairs = jnp.where(side == 0, jnp.stack([near, far]), jnp.stack([far, near]))
        vec = lax.all_gather(vector_params, "dp", axis=1, tiled=True)
        vec = jnp.pad(vec, ((0, 16 - vec.shape[0]), (0, 0)))
        wo_other = swap(pairs[:, 6:8], 1)
        norm, q, k, v, cat = project(tokens, passes, vec, pairs)
    mine, lse = attend(lens, q, k, v)
    out_chip, second, grad_second, grad_mixed, sums_two, mid_send, mid_keep, *ends = feed(
        small, tokens, passes, vec, mine, cotangent, pairs, wo_other
    )
    out_far = swap(out_chip, 2)
    if small:
        far = [hop_z(ends[turn], turn, (2, 3)) for turn in (1, 2, 3)]
        mid_send = hop_x(mid_send)
    dq, dk, dv = attend_back(lens, q, k, v, mine, lse, grad_mixed)
    if small:
        *far, out_far, mid_send, dq = tie(*far, out_far, mid_send, dq)
    output, input_grad, *sums = last(
        small, norm, dq, dk, dv, cat, tokens, passes, vec, grad_second, sums_two, second, out_chip, out_far,
        mid_send, mid_keep,
    )
    if small:
        late, vector_sum = sums
        left_new, right_new, step, weight_new, output, input_grad = renew(
            late, ends[0], far, block_weights, block_left, block_right, block_left_root, block_right_root,
            output, input_grad,
        )
        vector_grad = vector_sum[: PASSES + 4, : vector_params.shape[1]]
    else:
        vector_part, g_send, g_keep = sums[0][: PASSES + 4], *sums[1:]
        send, keep = ends
        rest = jnp.stack(
            [
                jnp.concatenate([mid_keep, keep]).reshape(3, 3, SIDE, PAIR),
                jnp.concatenate([mid_send, send]).reshape(3, 3, SIDE, PAIR),
            ],
            axis=1,
        )
        grad_qkv = from_pairs(jnp.concatenate([g_keep, g_send], axis=0)).swapaxes(1, 2)
        grad_rest = from_pairs(rest.reshape(18, SIDE, PAIR))
        spare = jnp.zeros((slots - total_blocks, SIDE, SIDE), bf16)
        grad_blocks = jnp.concatenate([grad_qkv, grad_rest, spare], axis=0)[None].astype(f32)
        owned = lax.psum_scatter(grad_blocks, "dp", scatter_dimension=1, tiled=True)
        vector_grad = lax.psum_scatter(vector_part, "dp", scatter_dimension=1, tiled=True)
        left_new, right_new, step, weight_new = precondition(
            owned, block_weights, block_left, block_right, block_left_root, block_right_root
        )
    moment_new = decay * vector_moment + (1.0 - decay) * vector_grad * vector_grad
    vector_new = vector_params - rate_vector * vector_grad / (jnp.sqrt(moment_new) + moment_eps)
    return (
        output,
        input_grad,
        left_new,
        right_new,
        step,
        weight_new,
        vector_grad,
        moment_new,
        vector_new,
    )


def solution(mesh):
    rows, line = P("dp", None), P(None, "dp")
    block = P("tensor", "dp", None, None)
    return jax.shard_map(
        on_device,
        mesh=mesh,
        in_specs=(rows, P("dp"), rows, rows, block, line, line, block, block, block, block),
        out_specs=(rows, rows, block, block, block, block, line, line, line),
        check_vma=False,
    )
```

```python
import functools

import jax
import jax.numpy as jnp
from jax import lax
from jax.experimental import pallas as pl
from jax.experimental.pallas import tpu as pltpu
from jax.sharding import PartitionSpec as P

D = 768
HD = 64
FF = 3072
PASSES = 5
SIDE = 192
PAIR = 2 * SIDE
ROWS = 256
WIDE = 512
DOCS = 8
NT = 4

norm_eps = 1e-05
moment_eps = 1e-08
rate_matrix = 0.03
rate_vector = 0.2
decay = 0.5
gelu_coef = 0.7978845608028654
masked_score = -1e30
f32 = jnp.float32
bf16 = jnp.bfloat16
MESH = pl.DeviceIdType.MESH


def nn(a, b):
    return lax.dot_general(a, b, (((1,), (0,)), ((), ())), preferred_element_type=f32)


def nt(a, b):
    return lax.dot_general(a, b, (((1,), (1,)), ((), ())), preferred_element_type=f32)


def tn(a, b):
    return lax.dot_general(a, b, (((0,), (0,)), ((), ())), preferred_element_type=f32)


def split_three(value):
    high = value.astype(bf16)
    rest = value - high.astype(f32)
    mid = rest.astype(bf16)
    return high, mid, (rest - mid.astype(f32)).astype(bf16)


def one_hot(pass_row):
    kinds = lax.broadcasted_iota(jnp.int32, (16, pass_row.shape[1]), 0)
    return (kinds == pass_row).astype(f32).astype(bf16)


def embedded(tokens, pass_row, vec):
    chosen = jnp.concatenate([one_hot(pass_row)] * 3, axis=0)
    return tokens.astype(f32) + tn(chosen, jnp.concatenate(split_three(vec), axis=0))


def hat_of(hidden):
    mean = jnp.mean(hidden, axis=-1, keepdims=True)
    center = hidden - mean
    spread = jnp.mean(center * center, axis=-1, keepdims=True)
    root = lax.rsqrt(spread + norm_eps)
    return center * root, root


def norm_back(hat, root, grad, gain):
    scaled = grad * gain
    first = jnp.mean(scaled, axis=-1, keepdims=True)
    second = jnp.mean(scaled * hat, axis=-1, keepdims=True)
    return root * (scaled - first - hat * second)


def params(mebibytes=56, **kw):
    return pltpu.CompilerParams(vmem_limit_bytes=mebibytes * 1024 * 1024, **kw)


def cost(micros):
    return pl.CostEstimate(flops=int(micros * 1.1e9), bytes_accessed=int(micros * 1e6), transcendentals=0)


def full(shape):
    return pl.BlockSpec(shape, lambda *_: (0,) * len(shape))


def gather_kernel(
    own, vec_own, tokens, passes,
    all_pairs, wo_other, vec_out, norm, q, k_out, v, cat,
    pack, vec_pack, vec_land, wq, tok, norm_s, qkv_s, cat_s, *sems,
):
    (
        s_z1, r_z1, s_x1, r_x1, s_y1, r_y1, s_d1, r_d1, s_l, r_l, s_r, r_r, s_x2, r_x2, s_y2, r_y2, s_v, r_v, s_c, r_c,
        s_out, s_cat, s_tok, loc,
    ) = sems
    dp, t = lax.axis_index("dp"), lax.axis_index("tensor")
    z, x = dp // 2, dp % 2
    y, core = t // 2, t % 2
    far_x, far_y, near = z * 2 + (1 - x), (1 - y) * 2 + core, y * 2 + (1 - core)

    barrier = pltpu.get_barrier_semaphore()
    peers = [lax.rem(dp + n, 8) for n in range(1, 8)]
    for peer in peers:
        pl.semaphore_signal(barrier, inc=1, device_id={"dp": peer}, device_id_type=MESH)
    for to in (far_y, near):
        pl.semaphore_signal(barrier, inc=1, device_id={"tensor": to}, device_id_type=MESH)

    tok_copy = pltpu.make_async_copy(tokens, tok, s_tok)
    tok_copy.start()
    for m in range(3):
        pair = jnp.concatenate([own[0, 2 * m], own[0, 2 * m + 1]], axis=1).astype(bf16)
        pack[m] = pair

        @pl.when(z == 0)
        def _():
            wq[y, 3 * x + m] = pair

    vec_pack[...] = jnp.zeros_like(vec_pack)
    vec_pack[0 : PASSES + 4, 0 : D // 8] = vec_own[...]
    pl.semaphore_wait(barrier, 9)

    started = []

    def send(src, dst, s_sem, r_sem, to, cond=None):
        copy = pltpu.make_async_remote_copy(
            src_ref=src, dst_ref=dst, send_sem=s_sem, recv_sem=r_sem, device_id=to, device_id_type=MESH
        )
        started.append((cond, copy))
        if cond is None:
            copy.start()
        else:
            pl.when(cond)(copy.start)

    def arrived(dst, r_sem, cond=None):
        copy = pltpu.make_async_remote_copy(
            src_ref=dst, dst_ref=dst, send_sem=loc, recv_sem=r_sem, device_id={"dp": far_x}, device_id_type=MESH
        )
        if cond is None:
            copy.wait_recv()
        else:
            pl.when(cond)(copy.wait_recv)

    to_x, to_y, to_left, to_right = {"dp": far_x}, {"tensor": far_y}, {"dp": dp - 2}, {"dp": dp + 2}
    half = SIDE // 2

    def piece(side, column, k):
        return wq.at[side, 3 * column + k // 2, pl.ds((k % 2) * half, half)]

    def at_z(d, m):
        return all_pairs.at[y, 3 * dp + 6 * d + m]

    own_copy = pltpu.make_async_copy(pack, all_pairs.at[y, pl.ds(3 * dp, 3)], loc)
    pl.when(z > 0)(own_copy.start)

    for m in range(3):
        send(pack.at[m], at_z(0, m), s_l.at[0, m], r_l.at[0, m], to_left, z > 0)
    for n, peer in enumerate(peers):
        send(vec_pack, vec_land.at[dp], s_v.at[n], r_v.at[dp], {"dp": peer})
    send(pack.at[0], at_z(0, 0), s_r.at[0, 0], r_r.at[0, 0], to_right, z == 2)
    for m in range(3):
        send(pack.at[m], at_z(0, m), s_x2.at[z, m], r_x2.at[z, m], to_x, z > m)

    def diagonal(k):
        arrived(piece(y, 1 - x, k), r_x1.at[k])
        send(piece(y, 1 - x, k), piece(y, 1 - x, k), s_d1.at[k], r_d1.at[k], to_y)

    def from_right(d, m):
        arrived(at_z(d, m), r_l.at[d - 1, m], z + d < 4)
        if d < 3:
            send(at_z(d, m), at_z(d, m), s_l.at[d, m], r_l.at[d, m], to_left, (z + d < 4) & (z > 0))

    def from_left(d, m, cond):
        arrived(at_z(-d, m), r_r.at[d - 1, m], cond)
        if d == 1:
            send(at_z(-d, m), at_z(-d, m), s_r.at[1, m], r_r.at[1, m], to_right, cond & (z < 3))
        along_x(-d, m, cond)

    def along_x(d, m, cond):
        send(at_z(d, m), at_z(d, m), s_x2.at[z + d, m], r_x2.at[z + d, m], to_x, cond)

    for k in range(6):
        arrived(piece(y, x, k), r_z1.at[k], z > 0)
        send(piece(y, x, k), piece(y, x, k), s_z1.at[k], r_z1.at[k], to_right, z < 3)
        send(piece(y, x, k), piece(y, x, k), s_x1.at[k], r_x1.at[k], to_x)
        send(piece(y, x, k), piece(y, x, k), s_y1.at[k], r_y1.at[k], to_y)
        if k == 5:
            for m in range(3):
                send(pack.at[m], at_z(0, m), s_r.at[0, m], r_r.at[0, m], to_right, (z == 1) | ((z == 2) & (m > 0)))
                send(pack.at[m], at_z(0, m), s_x2.at[z, m], r_x2.at[z, m], to_x, (z > 0) & (z <= m))
        if k >= 1:
            diagonal(k - 1)
        if k % 2 == 1:
            from_right(1, k // 2)
    diagonal(5)
    pl.when(z > 0)(own_copy.wait)
    for m in range(3):
        along_x(1, m, z + 1 < 4)
    for m in range(3):
        from_left(1, m, z > 1)
        from_right(2, m)
        along_x(2, m, z + 2 < 4)
    for k in range(6):
        arrived(piece(1 - y, x, k), r_y1.at[k])
        arrived(piece(1 - y, 1 - x, k), r_d1.at[k])
    for peer in peers:
        arrived(vec_land.at[peer], r_v.at[peer])
    vec_land[dp] = vec_pack[...]
    vec = jnp.concatenate([vec_land[d][:, : D // 8] for d in range(8)], axis=1)
    vec_out[...] = vec
    for n in range(3):
        for i in range(4):
            at = (i % 2) * SIDE
            parts = [wq[h, 2 * n + i // 2][:, at : at + SIDE] for h in range(2)]
            cat_s[n, i * SIDE : (i + 1) * SIDE, :] = jnp.concatenate(parts, axis=1)
    writes = [pltpu.make_async_copy(cat_s, cat, s_cat)]
    writes[0].start()
    tok_copy.wait()

    def rows_of(b):
        rows = slice(b * WIDE, (b + 1) * WIDE)
        hat, _ = hat_of(embedded(tok[rows, :], passes[:, rows], vec))
        low = (hat * vec[PASSES : PASSES + 1] + vec[PASSES + 1 : PASSES + 2]).astype(bf16)
        norm_s[rows, :] = low
        writes.append(pltpu.make_async_copy(norm_s.at[rows, :], norm.at[rows, :], s_out.at[b, 3]))
        writes[-1].start()
        for n, out in enumerate((q, k_out, v)):
            qkv_s[n, rows, :] = nn(low, cat_s[n]).astype(bf16)
            writes.append(pltpu.make_async_copy(qkv_s.at[n, rows, :], out.at[rows, :], s_out.at[b, n]))
            writes[-1].start()

    count = tok.shape[0] // WIDE
    for b in range(count):
        rows_of(b)
        if b == 0:
            for m in range(3):
                from_right(3, m)
                along_x(3, m, z + 3 < 4)
        if b == 1:
            for m in range(3):
                from_left(2, m, z == 3)
        if b == 2:
            for m in range(2):
                ref = all_pairs.at[y, 6 + m]
                arrived(ref, r_x2.at[1, m], x == 1)
                send(ref, ref, s_y2.at[m], r_y2.at[m], to_y)
                send(ref, wo_other.at[y, m], s_c.at[0, m], r_c.at[y, m], {"tensor": near})
    for m in range(2):
        ref = all_pairs.at[1 - y, 6 + m]
        arrived(ref, r_y2.at[m])
        send(ref, wo_other.at[1 - y, m], s_c.at[1, m], r_c.at[1 - y, m], {"tensor": near})
    for w in range(1, 4):
        for m in range(3):
            ref = all_pairs.at[y, 6 * w + 3 * (1 - x) + m]
            if w == 1 and m < 2:
                arrived(ref, r_x2.at[w, m], x == 0)
            else:
                arrived(ref, r_x2.at[w, m])
    for h in range(2):
        for m in range(2):
            arrived(wo_other.at[h, m], r_c.at[h, m])
    for copy in writes:
        copy.wait()
    for cond, copy in started:
        if cond is None:
            copy.wait_send()
        else:
            pl.when(cond)(copy.wait_send)


def gather(block_weights, vector_params, tokens, passes):
    seq = tokens.shape[0]
    dma = pltpu.SemaphoreType.DMA
    sizes = [(6,)] * 8 + [(3, 3)] * 2 + [(2, 3)] * 2 + [(4, 3)] * 2 + [(2,)] * 2 + [(7,), (8,)] + [(2, 2)] * 2
    sizes += [(seq // WIDE, 4)]
    vmem, far = pl.BlockSpec(memory_space=pltpu.VMEM), pl.BlockSpec(memory_space=pl.ANY)
    wide = jax.ShapeDtypeStruct((seq, PAIR), bf16)
    return pl.pallas_call(
        gather_kernel,
        in_specs=[vmem, vmem, far, vmem],
        out_specs=[far, far, vmem, far, far, far, far, far],
        out_shape=[
            jax.ShapeDtypeStruct((2, 24, SIDE, PAIR), bf16),
            jax.ShapeDtypeStruct((2, 2, SIDE, PAIR), bf16),
            jax.ShapeDtypeStruct((16, D), f32),
            jax.ShapeDtypeStruct((seq, D), bf16),
            wide,
            wide,
            wide,
            jax.ShapeDtypeStruct((3, D, PAIR), bf16),
        ],
        scratch_shapes=[
            pltpu.VMEM((3, SIDE, PAIR), bf16),
            pltpu.VMEM((16, 128), f32),
            pltpu.VMEM((8, 16, 128), f32),
            pltpu.VMEM((2, 6, SIDE, PAIR), bf16),
            pltpu.VMEM((seq, D), bf16),
            pltpu.VMEM((seq, D), bf16),
            pltpu.VMEM((3, seq, PAIR), bf16),
            pltpu.VMEM((3, D, PAIR), bf16),
        ]
        + [dma(size) for size in sizes]
        + [dma] * 3,
        compiler_params=params(collective_id=0, has_side_effects=True),
        cost_estimate=cost(60),
        name="gather",
    )(block_weights, vector_params, tokens, passes)


def project_kernel(tok, pas, vec, wq, norm, q, k, v, cat):
    @pl.when(pl.program_id(0) == 0)
    def _():
        for x in range(3):
            for i in range(4):
                at = (i % 2) * SIDE
                parts = [wq[h, 2 * x + i // 2][:, at : at + SIDE] for h in range(2)]
                cat[x, i * SIDE : (i + 1) * SIDE, :] = jnp.concatenate(parts, axis=1)

    first = embedded(tok[...], pas[...], vec[...])
    hat, _ = hat_of(first)
    low = (hat * vec[PASSES : PASSES + 1] + vec[PASSES + 1 : PASSES + 2]).astype(bf16)
    norm[...] = low
    for x, out in enumerate((q, k, v)):
        out[...] = nn(low, cat[x]).astype(bf16)


def project(tokens, passes, vec, wq):
    seq = tokens.shape[0]
    row = lambda n: pl.BlockSpec((WIDE, n), lambda i: (i, 0))
    wide = jax.ShapeDtypeStruct((seq, PAIR), bf16)
    return pl.pallas_call(
        project_kernel,
        grid=(seq // WIDE,),
        in_specs=[
            row(D),
            pl.BlockSpec((1, WIDE), lambda i: (0, i)),
            full((16, D)),
            full((2, 6, SIDE, PAIR)),
        ],
        out_specs=[row(D), row(PAIR), row(PAIR), row(PAIR), full((3, D, PAIR))],
        out_shape=[
            jax.ShapeDtypeStruct((seq, D), bf16),
            wide,
            wide,
            wide,
            jax.ShapeDtypeStruct((3, D, PAIR), bf16),
        ],
        compiler_params=params(),
        cost_estimate=cost(16),
        name="project",
    )(tokens, passes, vec, wq)


def doc_state(lens, base):
    rows = base + lax.broadcasted_iota(jnp.int32, (1, ROWS), 1)
    rows = jnp.concatenate([rows, rows], axis=1)
    begin = jnp.int32(0)
    first = jnp.int32(0)
    starts = jnp.zeros((1, 2 * ROWS), jnp.int32)
    for c in range(DOCS):
        starts = jnp.where(rows >= begin, begin, starts)
        first = jnp.where(base >= begin, begin, first)
        begin = begin + lens[c]
    return rows, starts, first


def two_heads(block):
    left = lax.broadcasted_iota(jnp.int32, block.shape, 1) < HD
    none = jnp.zeros_like(block)
    return jnp.concatenate([jnp.where(left, block, none), jnp.where(left, none, block)], axis=0)


def one_above(both):
    return jnp.concatenate([both[:HD, :ROWS], both[HD:, ROWS:]], axis=0).T


def attend_kernel(lens, q, k, v, out, lse, acc):
    i = pl.program_id(0)
    base = i * ROWS
    rows, starts, first = doc_state(lens, base)
    pairs = [two_heads(q[:, p * 128 : (p + 1) * 128] * bf16(0.125)) for p in range(3)]
    for p in range(3):
        acc[p] = jnp.zeros((128, 2 * ROWS), f32)

    def step(j, carry):
        at = pl.multiple_of(j * ROWS, ROWS)
        keys = at + lax.broadcasted_iota(jnp.int32, (ROWS, 2 * ROWS), 0)
        seen = (keys >= starts) & (keys <= rows)
        here = pl.ds(at, ROWS)
        head = lambda p: slice(p * 128, (p + 1) * 128)
        scores = [jnp.where(seen, nt(k[here, head(p)], pairs[p]), masked_score) for p in range(3)]
        state = []
        for p in range(3):
            before, total = carry[2 * p], carry[2 * p + 1]
            now = jnp.maximum(before, jnp.max(scores[p], axis=0, keepdims=True))
            probs = jnp.exp(scores[p] - now)
            fade = jnp.exp(before - now)
            state += [now, total * fade + jnp.sum(probs, axis=0, keepdims=True)]
            acc[p] = acc[p] * fade + tn(v[here, head(p)], probs.astype(bf16))
        return tuple(state)

    zero = jnp.zeros((1, 2 * ROWS), f32)
    state = lax.fori_loop(first // ROWS, i + 1, step, (zero + masked_score, zero) * 3)
    lines = []
    for p in range(3):
        top, total = state[2 * p], state[2 * p + 1]
        out[:, p * 128 : (p + 1) * 128] = one_above(acc[p] / total).astype(bf16)
        line = top + jnp.log(total)
        lines += [line[:, :ROWS], line[:, ROWS:]]
    lse[...] = jnp.concatenate(lines + lines[:2], axis=0)


def attend(lens, q, k, v):
    seq = q.shape[0]
    row = pl.BlockSpec((ROWS, PAIR), lambda i, s: (i, 0))
    return pl.pallas_call(
        attend_kernel,
        grid_spec=pltpu.PrefetchScalarGridSpec(
            num_scalar_prefetch=1,
            grid=(seq // ROWS,),
            in_specs=[row, full((seq, PAIR)), full((seq, PAIR))],
            out_specs=[row, pl.BlockSpec((8, ROWS), lambda i, s: (0, i))],
            scratch_shapes=[
                pltpu.VMEM((3, 128, 2 * ROWS), f32),
            ],
        ),
        out_shape=[
            jax.ShapeDtypeStruct((seq, PAIR), bf16),
            jax.ShapeDtypeStruct((8, seq), f32),
        ],
        compiler_params=params(),
        cost_estimate=cost(30),
        name="attend",
    )(lens, q, k, v)


def attend_back_kernel(
    lens, q, k, v, mixed, lse, grad_mixed, dq, dk, dv, dk_acc, dv_acc, dq_acc
):
    i = pl.program_id(0)
    count = pl.num_programs(0)
    base = i * ROWS

    @pl.when(i == 0)
    def _():
        dk_acc[...] = jnp.zeros_like(dk_acc)
        dv_acc[...] = jnp.zeros_like(dv_acc)

    rows, starts, first = doc_state(lens, base)
    heads = lax.broadcasted_iota(jnp.int32, (8, 128), 0)
    lanes = lax.broadcasted_iota(jnp.int32, (8, 128), 1)
    pick = (lanes // HD == heads).astype(f32).astype(bf16)
    queries, grads, inner, lines = [], [], [], []
    for p in range(3):
        cols = slice(p * 128, (p + 1) * 128)
        queries.append(two_heads(q[:, cols] * bf16(0.125)))
        grads.append(two_heads(grad_mixed[:, cols]))
        product = grad_mixed[:, cols].astype(f32) * mixed[:, cols].astype(f32)
        high, low, _ = split_three(product)
        sums = nt(pick, high) + nt(pick, low)
        inner.append(jnp.concatenate([sums[0:1], sums[1:2]], axis=1))
        lines.append(jnp.concatenate([lse[2 * p : 2 * p + 1], lse[2 * p + 1 : 2 * p + 2]], axis=1))
        dq_acc[p] = jnp.zeros((128, 2 * ROWS), f32)

    def step(j, carry):
        at = pl.multiple_of(j * ROWS, ROWS)
        keys = at + lax.broadcasted_iota(jnp.int32, (ROWS, 2 * ROWS), 0)
        seen = (keys >= starts) & (keys <= rows)
        here = pl.ds(at, ROWS)
        for p in range(3):
            cols = slice(p * 128, (p + 1) * 128)
            kb = k[here, cols]
            scores = jnp.where(seen, nt(kb, queries[p]) - lines[p], masked_score)
            probs = jnp.exp(scores)
            grad_probs = nt(v[here, cols], grads[p])
            grad_scores = (probs * (grad_probs - inner[p])).astype(bf16)
            dv_acc[here, cols] += nn(probs.astype(bf16), grads[p])
            dk_acc[here, cols] += nn(grad_scores, queries[p])
            dq_acc[p] += tn(kb, grad_scores)
        return carry

    lax.fori_loop(first // ROWS, i + 1, step, 0)
    for p in range(3):
        dq[:, p * 128 : (p + 1) * 128] = (one_above(dq_acc[p]) * 0.125).astype(bf16)

    @pl.when(i == count - 1)
    def _():
        dk[...] = dk_acc[...].astype(bf16)
        dv[...] = dv_acc[...].astype(bf16)


def attend_back(lens, q, k, v, mixed, lse, grad_mixed):
    seq = q.shape[0]
    count = seq // ROWS
    row = pl.BlockSpec((ROWS, PAIR), lambda i, s: (i, 0))
    wide = jax.ShapeDtypeStruct((seq, PAIR), bf16)
    return pl.pallas_call(
        attend_back_kernel,
        grid_spec=pltpu.PrefetchScalarGridSpec(
            num_scalar_prefetch=1,
            grid=(count,),
            in_specs=[
                row,
                full((seq, PAIR)),
                full((seq, PAIR)),
                row,
                pl.BlockSpec((8, ROWS), lambda i, s: (0, i)),
                row,
            ],
            out_specs=[row, full((seq, PAIR)), full((seq, PAIR))],
            scratch_shapes=[
                pltpu.VMEM((seq, PAIR), f32),
                pltpu.VMEM((seq, PAIR), f32),
                pltpu.VMEM((3, 128, 2 * ROWS), f32),
            ],
        ),
        out_shape=[wide, wide, wide],
        compiler_params=params(),
        cost_estimate=cost(40),
        name="attend_back",
    )(lens, q, k, v, mixed, lse, grad_mixed)


def feed_kernel(
    small, tok, pas, vec, mine, cot, wo_mine, wo_other, w1, w2,
    out_chip, second_keep, grad_second, grad_mixed, sums, mid_send, mid_keep, *rest,
):
    results, rest = (rest[:4], rest[4:]) if small else (rest[:2], rest[2:])
    (
        wo, other, up, down, gup, gdown, go, core_out, core_in, far_out, far_in, ga_out, ga_in, oc_out, oc_in,
        g_send, g_keep, g_in, s_core, r_core, s_far, r_far, s_ga, r_ga, s_oc, r_oc, s_x, r_x, s_m, r_m,
    ) = rest
    step = pl.program_id(0)
    half = core_out.shape[0]
    t, dp = lax.axis_index("tensor"), lax.axis_index("dp")
    core, side = t % 2, t // 2
    near, far = side * 2 + (1 - core), (1 - side) * 2 + core
    z, column = (dp // 2, dp % 2) if small else (0, 0)
    far_x = z * 2 + 1 - column

    def copy(src, dst, s_sem, r_sem, j, to):
        return pltpu.make_async_remote_copy(
            src_ref=src.at[j],
            dst_ref=dst.at[j],
            send_sem=s_sem.at[j],
            recv_sem=r_sem.at[j],
            device_id={"tensor": to},
            device_id_type=MESH,
        )

    core_copy = lambda j: copy(core_out, core_in, s_core, r_core, j, near)
    far_copy = lambda j: copy(far_out, far_in, s_far, r_far, j, far)
    ga_copy = lambda j: copy(ga_out, ga_in, s_ga, r_ga, j, near)
    oc_copy = lambda j: copy(oc_out, oc_in, s_oc, r_oc, j, near)

    def x_copy(slot):
        return pltpu.make_async_remote_copy(
            src_ref=g_send.at[slot],
            dst_ref=g_in.at[slot],
            send_sem=s_x.at[slot],
            recv_sem=r_x.at[slot],
            device_id={"dp": far_x},
            device_id_type=MESH,
        )

    def mixed_copy(block):
        rows = pl.ds(pl.multiple_of(block * ROWS, ROWS), ROWS)
        return pltpu.make_async_remote_copy(
            src_ref=mine.at[rows],
            dst_ref=other.at[rows],
            send_sem=s_m.at[block],
            recv_sem=r_m.at[block],
            device_id={"tensor": near},
            device_id_type=MESH,
        )

    barrier = pltpu.get_barrier_semaphore()

    @pl.when(step == 0)
    def _():
        for to in (near, far):
            pl.semaphore_signal(barrier, inc=1, device_id={"tensor": to}, device_id_type=MESH)
        if small:
            pl.semaphore_signal(barrier, inc=1, device_id={"dp": far_x}, device_id_type=MESH)
        for h in range(2):
            for m in range(2):
                rows, cols = slice(h * SIDE, (h + 1) * SIDE), slice(m * PAIR, (m + 1) * PAIR)
                wo[rows, cols] = wo_mine[h, m]
                wo[PAIR + h * SIDE : PAIR + (h + 1) * SIDE, cols] = wo_other[h, m]
        for r in range(4):
            for m in range(2):
                rows, cols = slice(r * SIDE, (r + 1) * SIDE), slice(m * PAIR, (m + 1) * PAIR)
                up[rows, cols] = w1[0, 2 * r + m]
                down[rows, cols] = w2[0, 2 * r + m]
        pl.semaphore_wait(barrier, 3 if small else 2)
        for j in range(half):
            mixed_copy(core * half + j).start()
            mixed_copy((1 - core) * half + j).start()
        gup[...] = jnp.zeros_like(gup)
        gdown[...] = jnp.zeros_like(gdown)
        go[...] = jnp.zeros_like(go)
        sums[...] = jnp.zeros_like(sums)

    @pl.when(step < 2 * half)
    def _():
        j = step // 2
        owner = jnp.where(step % 2 == 0, 1 - core, core)
        here = pl.ds(pl.multiple_of((owner * half + j) * ROWS, ROWS), ROWS)
        first = embedded(tok[...], pas[...], vec[...])
        mixed_copy(owner * half + j).wait_recv()
        second = first + nn(jnp.concatenate([mine[here, :], other[here, :]], axis=1), wo[...])
        hat, _ = hat_of(second)
        low = (hat * vec[PASSES + 2 : PASSES + 3] + vec[PASSES + 3 : PASSES + 4]).astype(bf16)
        upper = nn(low, up[...])
        square = upper * upper
        bent = jnp.tanh(gelu_coef * upper * (1.0 + 0.044715 * square))
        act = (0.5 * upper * (1.0 + bent)).astype(bf16)
        slope = 0.5 * (1.0 + bent) + (0.5 * gelu_coef) * upper * (1.0 - bent * bent) * (
            1.0 + (3 * 0.044715) * square
        )
        grad_act = nt(cot[...], down[...])
        grad_upper = (grad_act * slope).astype(bf16)
        part = nt(grad_upper, up[...])

        @pl.when(step % 2 == 0)
        def _():
            core_out[j] = part.astype(bf16)
            core_copy(j).start()

        @pl.when(step % 2 == 1)
        def _():
            core_copy(j).wait_recv()
            far_out[j] = (part + core_in[j].astype(f32)).astype(bf16)
            far_copy(j).start()
            second_keep[pl.ds(pl.multiple_of(j * ROWS, ROWS), ROWS), :] = second

        gup[...] += tn(low, grad_upper)
        gdown[...] += tn(act, cot[...])
        out_part = nn(act, down[...])

        @pl.when(step % 2 == 0)
        def _():
            oc_out[j] = out_part.astype(bf16)
            oc_copy(j).start()

        @pl.when(step % 2 == 1)
        def _():
            oc_copy(j).wait_recv()
            out_chip[...] = (out_part + oc_in[j].astype(f32)).astype(bf16)

    @pl.when(step == 2 * half - 1)
    def _():
        for r in range(4):
            for m in range(2):
                rows, cols = slice(r * SIDE, (r + 1) * SIDE), slice(m * PAIR, (m + 1) * PAIR)
                for at, total in ((8, gup), (16, gdown)):
                    pair = at + 2 * r + m
                    slot, place = (pair // 6 - 1) * 3 + pair % 3, pair // 3 % 2
                    value = total[rows, cols].astype(bf16)
                    kept, sent, n = (mid_keep, mid_send, slot) if slot < 6 else (g_keep, g_send, slot - 6)

                    @pl.when(column == place)
                    def _():
                        kept[n] = value

                    @pl.when(column != place)
                    def _():
                        sent[n] = value
        if small:
            for n in range(3):
                x_copy(n).start()

    def through_out(grad, block):
        here = pl.ds(pl.multiple_of(block * ROWS, ROWS), ROWS)
        grad_mixed[here, :] = nt(grad, wo[:PAIR, :]).astype(bf16)
        go[...] += tn(mine[here, :], grad)

    @pl.when((step >= 2 * half) & (step < 3 * half))
    def _():
        j = step - 2 * half
        hat, root = hat_of(second_keep[pl.ds(pl.multiple_of(j * ROWS, ROWS), ROWS), :])
        far_copy(j).wait_recv()
        grad = far_out[j].astype(f32) + far_in[j].astype(f32)
        result = cot[...].astype(f32) + norm_back(hat, root, grad, vec[PASSES + 2 : PASSES + 3])
        low = result.astype(bf16)
        ga_out[j] = low
        ga_copy(j).start()
        grad_second[...] = result
        sums[0:1] += jnp.sum(grad * hat, axis=0, keepdims=True)
        sums[1:2] += jnp.sum(grad, axis=0, keepdims=True)
        through_out(low, core * half + j)

    @pl.when(step > 2 * half)
    def _():
        j = step - 2 * half - 1
        ga_copy(j).wait_recv()
        through_out(ga_in[j], (1 - core) * half + j)

    @pl.when(step == 3 * half)
    def _():
        at = pl.multiple_of(side * SIDE, SIDE)
        for m in range(2):
            value = go[pl.ds(at, SIDE), m * PAIR : (m + 1) * PAIR].astype(bf16)

            @pl.when(column == 0)
            def _():
                mid_keep[m] = value

            @pl.when(column != 0)
            def _():
                mid_send[m] = value

        for j in range(half):
            core_copy(j).wait_send()
            oc_copy(j).wait_send()
            mixed_copy(j).wait_send()
            mixed_copy(half + j).wait_send()
            far_copy(j).wait_send()
            ga_copy(j).wait_send()
        if small:
            for n in range(3):
                x_copy(n).wait_send()
                x_copy(n).wait_recv()
                value = (g_keep[n].astype(f32) + g_in[n].astype(f32)).astype(bf16)
                for turn in range(4):

                    @pl.when(z + turn == 3)
                    def _():
                        results[turn][n] = value
        else:
            results[0][...] = g_send[...]
            results[1][...] = g_keep[...]


def feed(small, tokens, passes, vec, mine, cotangent, pairs, wo_other):
    seq = tokens.shape[0]
    half = seq // ROWS // 2

    def block(i):
        core = lax.axis_index("tensor") % 2
        work = jnp.minimum(i, 2 * half - 1)
        owner = jnp.where(work % 2 == 0, 1 - core, core)
        return owner * half + work // 2

    def cot_block(i):
        core = lax.axis_index("tensor") % 2
        return jnp.where(i < 2 * half, block(i), core * half + jnp.minimum(i - 2 * half, half - 1))

    side = lambda: lax.axis_index("tensor") // 2
    row = lambda n: pl.BlockSpec((ROWS, n), lambda i: (block(i), 0))
    keep = pl.BlockSpec((ROWS, D), lambda i: (jnp.minimum(i // 2, half - 1), 0))
    last = pl.BlockSpec((ROWS, D), lambda i: (jnp.clip(i - 2 * half, 0, half - 1), 0))
    rows = lambda kind: jax.ShapeDtypeStruct((seq // 2, D), kind)
    gr = lambda n: jax.ShapeDtypeStruct((n, SIDE, PAIR), bf16)
    ends = [(3, SIDE, PAIR)] * (4 if small else 2)
    buffer = pltpu.VMEM((half, ROWS, D), bf16)
    dma = pltpu.SemaphoreType.DMA((half,))
    return pl.pallas_call(
        functools.partial(feed_kernel, small),
        grid=(3 * half + 1,),
        in_specs=[
            row(D),
            pl.BlockSpec((1, ROWS), lambda i: (0, block(i))),
            full((16, D)),
            full((seq, PAIR)),
            pl.BlockSpec((ROWS, D), lambda i: (cot_block(i), 0)),
            pl.BlockSpec((2, 2, SIDE, PAIR), lambda i: (0, 3, 0, 0)),
            full(wo_other.shape),
            pl.BlockSpec((1, 8, SIDE, PAIR), lambda i: (side(), 1, 0, 0)),
            pl.BlockSpec((1, 8, SIDE, PAIR), lambda i: (side(), 2, 0, 0)),
        ],
        out_specs=[
            keep,
            full((seq // 2, D)),
            last,
            full((seq, PAIR)),
            full((8, D)),
            full((6, SIDE, PAIR)),
            full((6, SIDE, PAIR)),
        ]
        + [full(shape) for shape in ends],
        scratch_shapes=[
            pltpu.VMEM((D, D), bf16),
            pltpu.VMEM((seq, PAIR), bf16),
            pltpu.VMEM((D, D), bf16),
            pltpu.VMEM((D, D), bf16),
            pltpu.VMEM((D, D), f32),
            pltpu.VMEM((D, D), f32),
            pltpu.VMEM((PAIR, D), f32),
        ]
        + [buffer] * 8
        + [pltpu.VMEM((3, SIDE, PAIR), bf16)] * 3
        + [dma] * 8
        + [pltpu.SemaphoreType.DMA((3,))] * 2
        + [pltpu.SemaphoreType.DMA((2 * half,))] * 2,
        out_shape=[
            rows(bf16),
            rows(f32),
            rows(f32),
            jax.ShapeDtypeStruct((seq, PAIR), bf16),
            jax.ShapeDtypeStruct((8, D), f32),
            gr(6),
            gr(6),
        ]
        + [jax.ShapeDtypeStruct(shape, bf16) for shape in ends],
        compiler_params=params(collective_id=1, has_side_effects=True),
        cost_estimate=cost(50),
        name="feed_forward",
    )(tokens, passes, vec, mine, cotangent, pairs, wo_other, pairs, pairs)


CHUNK = SIDE // 2
CHUNKS = 18
TAKEN = (
    ((8, 3), (10, 4), (12, 12)),
    ((5, 1), (7, 3), (8, 4), (9, 6), (10, 7), (11, 8), (12, 12)),
    ((2, 2), (4, 3), (5, 4), (7, 6), (8, 8), (9, 9), (10, 11), (12, 12)),
    ((0, 3), (2, 5), (4, 6), (5, 7), (6, 8), (7, 12)),
)
GRAD_STEPS = 3


def last_kernel(
    small, norm_all, dq_all, dk_all, dv_all, cat, tok, pas, vec, grad_second, sums_two, second, chip, far,
    mid_near, mid_keep, output, input_grad, *rest,
):
    if small:
        late, vec_sum = rest[:2]
        rest = rest[2:]
        (
            core_out, core_in, sums, core_sums, x_in, z_in, z_out, up_in, v_out, v_in, total,
            s_core, r_core, s_sum, r_sum, s_x, r_x, s_z, r_z, s_up, r_up, s_v, r_v, ready, norm, dq, dk, dv, g_send, g_keep,
            s_own, s_res, r_res, s_in,
        ) = rest
    else:
        (
            vec_sum, send_out, keep_out, core_out, core_in, sums, core_sums, s_core, r_core, s_sum, r_sum, ready,
            norm, dq, dk, dv, g_send, g_keep, s_own, s_res, r_res, s_in,
        ) = rest
    step = pl.program_id(0)
    i = step - GRAD_STEPS
    half = core_out.shape[0]
    t, dp = lax.axis_index("tensor"), lax.axis_index("dp")
    core, side = t % 2, t // 2
    near = side * 2 + (1 - core)
    z, column = (dp // 2, dp % 2) if small else (0, 0)
    far_x = z * 2 + 1 - column
    peers = [lax.rem(dp + k, 8) for k in range(1, 8)]

    def copy(src, dst, s_sem, r_sem, to):
        return pltpu.make_async_remote_copy(
            src_ref=src, dst_ref=dst, send_sem=s_sem, recv_sem=r_sem, device_id=to, device_id_type=MESH
        )

    core_copy = lambda j: copy(core_out.at[j], core_in.at[j], s_core.at[j], r_core.at[j], {"tensor": near})
    sum_copy = lambda: copy(sums, core_sums, s_sum, r_sum, {"tensor": near})

    def rows_at(n, j, owner):
        rows = pl.ds(pl.multiple_of((owner * half + j) * ROWS, ROWS), ROWS)
        return (output, input_grad)[n].at[rows]

    own_result = lambda n, j: pltpu.make_async_copy(ready.at[n, j], rows_at(n, j, core), s_own.at[n, j])
    near_result = lambda n, j, owner: copy(
        ready.at[n, j], rows_at(n, j, owner), s_res.at[n, j], r_res.at[n, j], {"tensor": near}
    )

    def part_of(ref, k):
        return ref.at[k // 2, pl.ds((k % 2) * CHUNK, CHUNK)]

    x_copy = lambda k: copy(part_of(g_send, k), x_in.at[k], s_x.at[k], r_x.at[k], {"dp": far_x})
    z_copy = lambda k: copy(z_out.at[k], z_in.at[k], s_z.at[k], r_z.at[k], {"dp": dp - 2})
    up_copy = lambda k: copy(z_out.at[k], up_in.at[k - 6], s_up.at[k - 6], r_up.at[k - 6], {"dp": dp + 2})
    v_copy = lambda n: copy(v_out.at[peers[n]], v_in.at[dp], s_v.at[n], r_v.at[dp], {"dp": peers[n]})
    barrier = pltpu.get_barrier_semaphore()

    loads = [
        pltpu.make_async_copy(src, dst, s_in.at[n])
        for n, (src, dst) in enumerate(((norm_all, norm), (dq_all, dq), (dv_all, dv), (dk_all, dk)))
    ]

    @pl.when(step == 0)
    def _():
        for load in loads:
            load.start()
        pl.semaphore_signal(barrier, inc=1, device_id={"tensor": near}, device_id_type=MESH)
        if small:
            for peer in peers:
                pl.semaphore_signal(barrier, inc=1, device_id={"dp": peer}, device_id_type=MESH)
            late[...] = jnp.zeros_like(late)
        sums[...] = jnp.zeros_like(sums)
        sums[PASSES + 2 : PASSES + 4] = sums_two[0:2]
        pl.semaphore_wait(barrier, 8 if small else 1)

    def mine_of(grad):
        return jnp.where(side == 0, grad[:, :SIDE], grad[:, SIDE:])

    def pairs_of(grad):
        value = tn(grad, norm[...]).astype(bf16)
        return value[:, :PAIR], value[:, PAIR:]

    second_two = jnp.where(jnp.asarray(column) == 0, 1, 0)

    @pl.when(step == 0)
    def _():
        for load in loads[:3]:
            load.wait()
        both = pairs_of(jnp.where(jnp.asarray(column) == 0, mine_of(dv), mine_of(dq)))
        for m in range(2):
            g_send[second_two + m] = both[m]
        if small:
            for m in range(4):
                x_copy(2 * second_two + m).start()

    @pl.when(step == 1)
    def _():
        loads[3].wait()
        both = pairs_of(mine_of(dk))
        for place, (kept, sent) in enumerate(((0, 1), (1, 0))):

            @pl.when(jnp.asarray(column) == place)
            def _():
                g_keep[2 - 2 * place] = both[kept]
                g_send[2 * place] = both[sent]

        if small:
            for m in range(2):
                x_copy(4 * column + m).start()

    @pl.when(step == 2)
    def _():
        both = pairs_of(jnp.where(jnp.asarray(column) == 0, mine_of(dq), mine_of(dv)))
        for m in range(2):
            g_keep[1 - second_two + m] = both[m]
        if not small:
            send_out[...] = g_send[...]
            keep_out[...] = g_keep[...]

    @pl.when((i >= 0) & (i < 2 * half))
    def _():
        block = lax.rem(i + (1 - core) * half, 2 * half)
        rows = pl.ds(pl.multiple_of(block * ROWS, ROWS), ROWS)
        part = nt(dq[rows, :], cat[0]) + nt(dk[rows, :], cat[1]) + nt(dv[rows, :], cat[2])

        @pl.when(i < half)
        def _():
            core_out[i] = part.astype(bf16)
            core_copy(i).start()

        @pl.when(i >= half)
        def _():
            j = i - half
            hat, root = hat_of(embedded(tok[...], pas[...], vec[...]))
            core_copy(j).wait_recv()
            grad = part + core_in[j].astype(f32)
            result = grad_second[...] + norm_back(hat, root, grad, vec[PASSES : PASSES + 1])
            ready[0, j] = (second[...] + (chip[...].astype(f32) + far[...].astype(f32))).astype(bf16)
            ready[1, j] = result.astype(bf16)
            for n in range(2):
                own_result(n, j).start()
                near_result(n, j, core).start()
            chosen = one_hot(pas[...])
            high, mid, _ = split_three(result)
            sums[...] += nn(chosen, high) + nn(chosen, mid)
            sums[PASSES : PASSES + 1] += jnp.sum(grad * hat, axis=0, keepdims=True)
            sums[PASSES + 1 : PASSES + 2] += jnp.sum(grad, axis=0, keepdims=True)

    @pl.when(i == 2 * half - 1)
    def _():
        sum_copy().start()

    if small:

        def term_of(k):
            rows = pl.ds(pl.multiple_of((k % 2) * CHUNK, 16), CHUNK)

            @pl.when(jnp.asarray(k) < 6)
            def _():
                x_copy(k).wait_recv()
                total[...] = g_keep[k // 2, rows, :].astype(f32) + x_in[k].astype(f32)

            @pl.when(jnp.asarray(k) >= 6)
            def _():
                total[...] = mid_keep[k // 2 - 3, rows, :].astype(f32) + mid_near[k // 2 - 3, rows, :].astype(f32)

            return total[...]

        def keep_late(k, pair, total):
            late[pair, pl.ds(pl.multiple_of((k % 2) * CHUNK, 16), CHUNK), :] = total

        def pass_on(k):
            term = term_of(k)

            @pl.when(z < 3)
            def _():
                z_copy(k).wait_recv()

            below = jnp.where(z < 3, z_in[k].astype(f32), 0.0)
            passed = term + below

            @pl.when((z > 1) | ((z == 1) & (k < 6)))
            def _():
                z_out[k] = passed.astype(bf16)
                z_copy(k).start()

            @pl.when(z == 0)
            def _():
                keep_late(k, k // 2, passed)

            @pl.when((z == 1) & (k >= 6))
            def _():
                up_copy(k).wait_recv()
                keep_late(k, k // 2 - 3, passed + up_in[k - 6].astype(f32))

        def at_position(p, carry):
            k = jnp.where(p < 3, p + 6, jnp.where(p < 9, lax.rem(p + 3 + 2 * column, 6), p))

            @pl.when((z > 0) | (k < 6))
            def _():
                pass_on(k)

            return carry

        begin, end = jnp.int32(0), jnp.int32(0)
        for place, line in enumerate(TAKEN):
            for at, upto in line:
                begin = jnp.where((z == place) & (step > at), upto, begin)
                end = jnp.where((z == place) & (step >= at), upto, end)
        lax.fori_loop(begin, end, at_position, 0)

        @pl.when((step == 0) & (z == 0))
        def _():
            for k in range(6, CHUNKS):
                z_out[k] = term_of(k).astype(bf16)
                up_copy(k).start()

        for at, first_chunk, upto in ((0, 12, 14), (7, 14, 18)):

            @pl.when((step == at) & (z == 3))
            def _(first_chunk=first_chunk, upto=upto):
                for k in range(first_chunk, upto):
                    z_out[k] = term_of(k).astype(bf16)
                    z_copy(k).start()

        for at, first_chunk, upto in ((10, 12, 16), (11, 16, 18)):

            @pl.when((step == at) & (z == 1))
            def _(first_chunk=first_chunk, upto=upto):
                for k in range(first_chunk, upto):
                    up_copy(k).wait_recv()
                    z_out[k] = (term_of(k) + up_in[k - 6].astype(f32)).astype(bf16)
                    up_copy(k).start()

        @pl.when((step == pl.num_programs(0) - 1) & (z == 2))
        def _():
            for k in range(12, CHUNKS):
                z_copy(k).wait_recv()
                up_copy(k).wait_recv()
                keep_late(k, k // 2 - 6, term_of(k) + z_in[k].astype(f32) + up_in[k - 6].astype(f32))

    @pl.when(i == 2 * half)
    def _():
        sum_copy().wait_recv()
        total = sums[...] + core_sums[...]
        if small:
            wide = D // 8
            for d in range(8):
                v_out[d, :, 0:wide] = total[:, d * wide : (d + 1) * wide]
                v_out[d, :, wide:] = jnp.zeros((16, 128 - wide), f32)
            for n in range(7):
                v_copy(n).start()
        else:
            vec_sum[...] = total

    @pl.when(step == pl.num_programs(0) - 1)
    def _():
        for j in range(half):
            core_copy(j).wait_send()
            for n in range(2):
                own_result(n, j).wait()
                near_result(n, j, core).wait_send()
                near_result(n, j, 1 - core).wait_recv()
        sum_copy().wait_send()
        if small:
            for peer in peers:
                copy(v_out.at[0], v_in.at[peer], s_v.at[0], r_v.at[peer], {"dp": far_x}).wait_recv()
            v_in[dp] = v_out[dp]
            total = v_in[0]
            for d in range(1, 8):
                total = total + v_in[d]
            vec_sum[...] = total
            for n in range(7):
                v_copy(n).wait_send()
            for k in range(CHUNKS):
                if k < 6:
                    x_copy(k).wait_send()
                    pl.when(z > 0)(z_copy(k).wait_send)
                elif k < 12:
                    pl.when(z > 1)(z_copy(k).wait_send)
                    pl.when(z == 0)(up_copy(k).wait_send)
                else:
                    pl.when(z == 3)(z_copy(k).wait_send)
                    pl.when(z < 2)(up_copy(k).wait_send)


def last(
    small, norm, dq, dk, dv, cat, tokens, passes, vec, grad_second, sums_two, second, chip, far, mid_near, mid_keep
):
    seq = dq.shape[0]
    half = seq // ROWS // 2
    core = lambda: lax.axis_index("tensor") % 2

    own = lambda i: jnp.clip(i - GRAD_STEPS - half, 0, half - 1)
    mine = pl.BlockSpec((ROWS, D), lambda i: (own(i), 0))
    dma = pltpu.SemaphoreType.DMA
    out_specs = [pl.BlockSpec(memory_space=pl.ANY)] * 2
    out_shape = [jax.ShapeDtypeStruct((seq, D), bf16)] * 2
    scratch = [
        pltpu.VMEM((half, ROWS, D), bf16),
        pltpu.VMEM((half, ROWS, D), bf16),
        pltpu.VMEM((16, D), f32),
        pltpu.VMEM((16, D), f32),
    ]
    sems = [dma((half,)), dma((half,)), dma, dma]
    if small:
        out_specs += [full((3, SIDE, PAIR)), full((16, 128))]
        out_shape += [
            jax.ShapeDtypeStruct((3, SIDE, PAIR), f32),
            jax.ShapeDtypeStruct((16, 128), f32),
        ]
        scratch += [pltpu.VMEM((CHUNKS, CHUNK, PAIR), bf16)] * 3
        scratch += [pltpu.VMEM((12, CHUNK, PAIR), bf16)]
        scratch += [pltpu.VMEM((8, 16, 128), f32)] * 2 + [pltpu.VMEM((CHUNK, PAIR), f32)]
        sems += [dma((6,))] * 2 + [dma((CHUNKS,))] * 2 + [dma((12,))] * 2 + [dma((7,)), dma((8,))]
    else:
        out_specs += [full((16, D)), full((3, SIDE, PAIR)), full((3, SIDE, PAIR))]
        out_shape += [jax.ShapeDtypeStruct((16, D), f32)] + [jax.ShapeDtypeStruct((3, SIDE, PAIR), bf16)] * 2
    scratch_more = [pltpu.VMEM((2, half, ROWS, D), bf16), pltpu.VMEM((seq, D), bf16)]
    scratch_more += [pltpu.VMEM((seq, PAIR), bf16)] * 3
    scratch_more += [pltpu.VMEM((3, SIDE, PAIR), bf16)] * 2 + [dma((2, half))] * 3 + [dma((4,))]
    return pl.pallas_call(
        functools.partial(last_kernel, small),
        grid=(GRAD_STEPS + 2 * half + 2,),
        in_specs=[
            *[pl.BlockSpec(memory_space=pl.ANY)] * 4,
            full(cat.shape),
            pl.BlockSpec((ROWS, D), lambda i: (core() * half + own(i), 0)),
            pl.BlockSpec((1, ROWS), lambda i: (0, core() * half + own(i))),
            full((16, D)),
            mine,
            full((8, D)),
            mine,
            mine,
            mine,
            full(mid_near.shape),
            full(mid_keep.shape),
        ],
        out_specs=out_specs,
        out_shape=out_shape,
        scratch_shapes=scratch + sems + scratch_more,
        compiler_params=params(collective_id=2, has_side_effects=True),
        cost_estimate=cost(38),
        name="last",
    )(norm, dq, dk, dv, cat, tokens, passes, vec, grad_second, sums_two, second, chip, far, mid_near, mid_keep)


def precondition(grad, weight, left, right, left_root, right_root):
    high = lax.Precision.HIGHEST
    left_new = decay * left + (1.0 - decay) * jnp.einsum(
        "...ij,...kj->...ik", grad, grad, precision=high
    )
    right_new = decay * right + (1.0 - decay) * jnp.einsum(
        "...ji,...jk->...ik", grad, grad, precision=high
    )
    half = jnp.einsum("...ij,...jk->...ik", left_root, grad, precision=high)
    step = jnp.einsum("...ij,...jk->...ik", half, right_root, precision=high)
    return (left_new, right_new, step, weight - rate_matrix * step)


def two_part(value):
    high = value.astype(bf16)
    return high, (value - high.astype(f32)).astype(bf16)


def dot_three(dot, a, b):
    return dot(a[0], b[0]) + (dot(a[0], b[1]) + dot(a[1], b[0]))


def renew_kernel(
    late, own, one, two, three, weight, left, right, left_root, right_root, output, input_grad,
    left_new, right_new, step, new, output_new, input_grad_new,
):
    output_new[...] = output[...]
    input_grad_new[...] = input_grad[...]

    @pl.when(pl.program_id(0) < 3)
    def _():
        early = own[0].astype(f32) + one[0].astype(f32) + two[0].astype(f32) + three[0].astype(f32)
        z = lax.axis_index("dp") // 2
        both = late[0] + jnp.where(z > 2, early, 0.0)
        for n in range(2):
            grad = both[:, n * SIDE : (n + 1) * SIDE]
            grad = two_part(jnp.where(z == 0, grad.T, grad))
            left_new[0, n] = decay * left[0, n] + (1.0 - decay) * dot_three(nt, grad, grad)
            right_new[0, n] = decay * right[0, n] + (1.0 - decay) * dot_three(tn, grad, grad)
            half = dot_three(nn, two_part(left_root[0, n]), grad)
            value = dot_three(nn, two_part(half), two_part(right_root[0, n]))
            step[0, n] = value
            new[0, n] = weight[0, n] - rate_matrix * value


def renew(late, own, far, weight, left, right, left_root, right_root, output, input_grad):
    pair = pl.BlockSpec((1, SIDE, PAIR), lambda i: (jnp.minimum(i, 2), 0, 0))
    slot = pl.BlockSpec((1, 2, SIDE, SIDE), lambda i: (0, jnp.minimum(i, 2), 0, 0))
    rows = pl.BlockSpec((output.shape[0] // 4, D), lambda i: (i, 0))
    return pl.pallas_call(
        renew_kernel,
        grid=(4,),
        in_specs=[pair] * 5 + [slot] * 5 + [rows] * 2,
        out_specs=[slot] * 4 + [rows] * 2,
        out_shape=[jax.ShapeDtypeStruct(weight.shape, f32)] * 4
        + [jax.ShapeDtypeStruct(value.shape, value.dtype) for value in (output, input_grad)],
        compiler_params=params(46),
        cost_estimate=cost(8),
        name="renew",
    )(late, own, *far, weight, left, right, left_root, right_root, output, input_grad)


def to_pairs(blocks):
    n = blocks.shape[0] // 2
    return blocks.reshape(n, 2, SIDE, SIDE).transpose(0, 2, 1, 3).reshape(n, SIDE, PAIR)


def from_pairs(pairs):
    n = pairs.shape[0]
    return pairs.reshape(n, SIDE, 2, SIDE).transpose(0, 2, 1, 3).reshape(2 * n, SIDE, SIDE)


def swap(value, bit):
    return lax.ppermute(value, "tensor", [(t, t ^ bit) for t in range(NT)])


def hop_x(value):
    return lax.ppermute(value, "dp", [(d, d ^ 1) for d in range(8)])


def hop_z(value, turn, ends):
    pairs = [(d, (d + 2 * turn) % 8) for d in range(8) if (d // 2 + turn) % 4 in ends]
    return lax.ppermute(value, "dp", pairs)


def tie(*values):
    return lax.optimization_barrier(values)


def on_device(
    tokens,
    pass_ids,
    doc_lengths,
    cotangent,
    block_weights,
    vector_params,
    vector_moment,
    block_left,
    block_right,
    block_left_root,
    block_right_root,
):
    t, dp = lax.axis_index("tensor"), lax.axis_index("dp")
    core, side = t % 2, t // 2
    n_dp = lax.axis_size("dp")
    small = n_dp == 8
    z, column = (dp // 2, dp % 2) if small else (0, 0)
    lens = doc_lengths[0]
    seq = tokens.shape[0]
    passes = pass_ids.reshape(1, seq)
    total_blocks = (D // SIDE) * (4 + 2 * (FF // D))
    slots = block_weights.shape[1] * n_dp

    if small:
        pairs, wo_other, vec, norm, q, k, v, cat = gather(block_weights, vector_params, tokens, passes)
    else:
        every = lax.all_gather(block_weights.astype(bf16), "dp", axis=1, tiled=True)[0]
        near = to_pairs(every[:total_blocks])
        far = swap(near, 2)
        pairs = jnp.where(side == 0, jnp.stack([near, far]), jnp.stack([far, near]))
        vec = lax.all_gather(vector_params, "dp", axis=1, tiled=True)
        vec = jnp.pad(vec, ((0, 16 - vec.shape[0]), (0, 0)))
        wo_other = swap(pairs[:, 6:8], 1)
        norm, q, k, v, cat = project(tokens, passes, vec, pairs)
    mine, lse = attend(lens, q, k, v)
    out_chip, second, grad_second, grad_mixed, sums_two, mid_send, mid_keep, *ends = feed(
        small, tokens, passes, vec, mine, cotangent, pairs, wo_other
    )
    out_far = swap(out_chip, 2)
    if small:
        far = [hop_z(ends[turn], turn, (3,)) for turn in (1, 2, 3)]
        mid_send = hop_x(mid_send)
    dq, dk, dv = attend_back(lens, q, k, v, mine, lse, grad_mixed)
    if small:
        *far, out_far, mid_send, dq = tie(*far, out_far, mid_send, dq)
    output, input_grad, *sums = last(
        small, norm, dq, dk, dv, cat, tokens, passes, vec, grad_second, sums_two, second, out_chip, out_far,
        mid_send, mid_keep,
    )
    if small:
        late, vector_sum = sums
        left_new, right_new, step, weight_new, output, input_grad = renew(
            late, ends[0], far, block_weights, block_left, block_right, block_left_root, block_right_root,
            output, input_grad,
        )
        vector_grad = vector_sum[: PASSES + 4, : vector_params.shape[1]]
    else:
        vector_part, g_send, g_keep = sums[0][: PASSES + 4], *sums[1:]
        send, keep = ends
        rest = jnp.stack(
            [
                jnp.concatenate([mid_keep, keep]).reshape(3, 3, SIDE, PAIR),
                jnp.concatenate([mid_send, send]).reshape(3, 3, SIDE, PAIR),
            ],
            axis=1,
        )
        grad_qkv = from_pairs(jnp.concatenate([g_keep, g_send], axis=0)).swapaxes(1, 2)
        grad_rest = from_pairs(rest.reshape(18, SIDE, PAIR))
        spare = jnp.zeros((slots - total_blocks, SIDE, SIDE), bf16)
        grad_blocks = jnp.concatenate([grad_qkv, grad_rest, spare], axis=0)[None].astype(f32)
        owned = lax.psum_scatter(grad_blocks, "dp", scatter_dimension=1, tiled=True)
        vector_grad = lax.psum_scatter(vector_part, "dp", scatter_dimension=1, tiled=True)
        left_new, right_new, step, weight_new = precondition(
            owned, block_weights, block_left, block_right, block_left_root, block_right_root
        )
    moment_new = decay * vector_moment + (1.0 - decay) * vector_grad * vector_grad
    vector_new = vector_params - rate_vector * vector_grad / (jnp.sqrt(moment_new) + moment_eps)
    return (
        output,
        input_grad,
        left_new,
        right_new,
        step,
        weight_new,
        vector_grad,
        moment_new,
        vector_new,
    )


def solution(mesh):
    rows, line = P("dp", None), P(None, "dp")
    block = P("tensor", "dp", None, None)
    return jax.shard_map(
        on_device,
        mesh=mesh,
        in_specs=(rows, P("dp"), rows, rows, block, line, line, block, block, block, block),
        out_specs=(rows, rows, block, block, block, block, line, line, line),
        check_vma=False,
    )
```

```python
import functools

import jax
import jax.numpy as jnp
from jax import lax
from jax.experimental import pallas as pl
from jax.experimental.pallas import tpu as pltpu
from jax.sharding import PartitionSpec as P

D = 768
HD = 64
FF = 3072
PASSES = 5
SIDE = 192
PAIR = 2 * SIDE
ROWS = 256
WIDE = 512
DOCS = 8
NT = 4

norm_eps = 1e-05
moment_eps = 1e-08
rate_matrix = 0.03
rate_vector = 0.2
decay = 0.5
gelu_coef = 0.7978845608028654
masked_score = -1e30
f32 = jnp.float32
bf16 = jnp.bfloat16
MESH = pl.DeviceIdType.MESH


def nn(a, b):
    return lax.dot_general(a, b, (((1,), (0,)), ((), ())), preferred_element_type=f32)


def nt(a, b):
    return lax.dot_general(a, b, (((1,), (1,)), ((), ())), preferred_element_type=f32)


def tn(a, b):
    return lax.dot_general(a, b, (((0,), (0,)), ((), ())), preferred_element_type=f32)


def split_three(value):
    high = value.astype(bf16)
    rest = value - high.astype(f32)
    mid = rest.astype(bf16)
    return high, mid, (rest - mid.astype(f32)).astype(bf16)


def one_hot(pass_row):
    kinds = lax.broadcasted_iota(jnp.int32, (16, pass_row.shape[1]), 0)
    return (kinds == pass_row).astype(f32).astype(bf16)


def embedded(tokens, pass_row, vec):
    chosen = jnp.concatenate([one_hot(pass_row)] * 3, axis=0)
    return tokens.astype(f32) + tn(chosen, jnp.concatenate(split_three(vec), axis=0))


def hat_of(hidden):
    mean = jnp.mean(hidden, axis=-1, keepdims=True)
    center = hidden - mean
    spread = jnp.mean(center * center, axis=-1, keepdims=True)
    root = lax.rsqrt(spread + norm_eps)
    return center * root, root


def norm_back(hat, root, grad, gain):
    scaled = grad * gain
    first = jnp.mean(scaled, axis=-1, keepdims=True)
    second = jnp.mean(scaled * hat, axis=-1, keepdims=True)
    return root * (scaled - first - hat * second)


def params(mebibytes=56, **kw):
    return pltpu.CompilerParams(vmem_limit_bytes=mebibytes * 1024 * 1024, **kw)


def cost(micros):
    return pl.CostEstimate(flops=int(micros * 1.1e9), bytes_accessed=int(micros * 1e6), transcendentals=0)


def full(shape):
    return pl.BlockSpec(shape, lambda *_: (0,) * len(shape))


def gather_kernel(
    own, vec_own, tokens, passes,
    all_pairs, columns, wo_other, vec_out, norm, q, k_out, v, cat,
    pack, vec_pack, vec_land, wq, tok, norm_s, qkv_s, cat_s, *sems,
):
    (
        s_z1, r_z1, s_x1, r_x1, s_y1, r_y1, s_d1, r_d1, s_l, r_l, s_r, r_r, s_x2, r_x2, s_y2, r_y2, s_v, r_v, s_c, r_c,
        s_out, s_cat, s_tok, loc,
    ) = sems
    dp, t = lax.axis_index("dp"), lax.axis_index("tensor")
    z, x = dp // 2, dp % 2
    y, core = t // 2, t % 2
    far_x, far_y, near = z * 2 + (1 - x), (1 - y) * 2 + core, y * 2 + (1 - core)

    barrier = pltpu.get_barrier_semaphore()
    peers = [lax.rem(dp + n, 8) for n in range(1, 8)]
    for peer in peers:
        pl.semaphore_signal(barrier, inc=1, device_id={"dp": peer}, device_id_type=MESH)
    for to in (far_y, near):
        pl.semaphore_signal(barrier, inc=1, device_id={"tensor": to}, device_id_type=MESH)

    tok_copy = pltpu.make_async_copy(tokens, tok, s_tok)
    tok_copy.start()
    for m in range(3):
        pair = jnp.concatenate([own[0, 2 * m], own[0, 2 * m + 1]], axis=1).astype(bf16)
        pack[m] = pair

        @pl.when(z == 0)
        def _():
            wq[y, 3 * x + m] = pair

    vec_pack[...] = jnp.zeros_like(vec_pack)
    vec_pack[0 : PASSES + 4, 0 : D // 8] = vec_own[...]
    pl.semaphore_wait(barrier, 9)

    started = []

    def send(src, dst, s_sem, r_sem, to, cond=None):
        copy = pltpu.make_async_remote_copy(
            src_ref=src, dst_ref=dst, send_sem=s_sem, recv_sem=r_sem, device_id=to, device_id_type=MESH
        )
        started.append((cond, copy))
        if cond is None:
            copy.start()
        else:
            pl.when(cond)(copy.start)

    def arrived(dst, r_sem, cond=None):
        copy = pltpu.make_async_remote_copy(
            src_ref=dst, dst_ref=dst, send_sem=loc, recv_sem=r_sem, device_id={"dp": far_x}, device_id_type=MESH
        )
        if cond is None:
            copy.wait_recv()
        else:
            pl.when(cond)(copy.wait_recv)

    to_x, to_y, to_left, to_right = {"dp": far_x}, {"tensor": far_y}, {"dp": dp - 2}, {"dp": dp + 2}
    half = SIDE // 2

    def piece(side, column, k):
        return wq.at[side, 3 * column + k // 2, pl.ds((k % 2) * half, half)]

    def at_one(m):
        return all_pairs.at[y, 6 + 3 * x + m]

    def at_z(d, m):
        return columns.at[3 * (z + d - 2) + m]

    own_one = pltpu.make_async_copy(pack, all_pairs.at[y, pl.ds(6 + 3 * x, 3)], loc)
    own_more = pltpu.make_async_copy(pack, columns.at[pl.ds(3 * (z - 2), 3)], loc)
    pl.when(z == 1)(own_one.start)
    pl.when(z > 1)(own_more.start)

    for m in range(3):
        send(pack.at[m], at_one(m), s_l.at[0, m], r_l.at[0, m], to_left, z == 1)
        send(pack.at[m], at_z(0, m), s_l.at[0, m], r_l.at[0, m], to_left, z > 1)
    for n, peer in enumerate(peers):
        send(vec_pack, vec_land.at[dp], s_v.at[n], r_v.at[dp], {"dp": peer})
    send(pack.at[0], at_z(0, 0), s_r.at[0, 0], r_r.at[0, 0], to_right, z == 2)
    send(pack.at[0], at_one(0), s_x2.at[0], r_x2.at[0], to_x, z == 1)

    def diagonal(k):
        if k % 2 == 0:
            arrived(piece(y, 1 - x, k), r_x1.at[k])
            send(piece(y, 1 - x, k), piece(y, 1 - x, k), s_d1.at[k], r_d1.at[k], to_y)
        else:
            arrived(piece(1 - y, x, k), r_y1.at[k])
            send(piece(1 - y, x, k), piece(1 - y, x, k), s_d1.at[k], r_d1.at[k], to_x)

    def from_right(d, m):
        arrived(columns.at[m], r_l.at[d - 1, m], z + d < 4)
        if d < 3:
            send(at_z(d, m), at_z(d, m), s_l.at[d, m], r_l.at[d, m], to_left, (z + d < 4) & (z > 0))

    def along_x(m, cond):
        send(at_one(m), at_one(m), s_x2.at[m], r_x2.at[m], to_x, cond)

    def from_left(d, m):
        arrived(columns.at[m], r_r.at[d - 1, m], z > d)
        if d == 1:
            send(at_one(m), at_one(m), s_r.at[1, m], r_r.at[1, m], to_right, z == 2)
        along_x(m, z == d + 1)

    for k in range(6):
        arrived(piece(y, x, k), r_z1.at[k], z > 0)
        send(piece(y, x, k), piece(y, x, k), s_z1.at[k], r_z1.at[k], to_right, z < 3)
        send(piece(y, x, k), piece(y, x, k), s_x1.at[k], r_x1.at[k], to_x)
        send(piece(y, x, k), piece(y, x, k), s_y1.at[k], r_y1.at[k], to_y)
        if k == 5:
            for m in range(3):
                send(pack.at[m], at_one(m), s_r.at[0, m], r_r.at[0, m], to_right, z == 1)
                if m > 0:
                    send(pack.at[m], at_z(0, m), s_r.at[0, m], r_r.at[0, m], to_right, z == 2)
                    send(pack.at[m], at_one(m), s_x2.at[m], r_x2.at[m], to_x, z == 1)
        if k >= 1:
            diagonal(k - 1)
        if k % 2 == 1:
            from_right(1, k // 2)
    diagonal(5)
    pl.when(z == 1)(own_one.wait)
    pl.when(z > 1)(own_more.wait)
    for m in range(3):
        along_x(m, z == 0)
    for m in range(3):
        from_left(1, m)
        from_right(2, m)
    for k in range(6):
        if k % 2 == 0:
            arrived(piece(1 - y, x, k), r_y1.at[k])
        else:
            arrived(piece(y, 1 - x, k), r_x1.at[k])
        arrived(piece(1 - y, 1 - x, k), r_d1.at[k])
    for peer in peers:
        arrived(vec_land.at[peer], r_v.at[peer])
    vec_land[dp] = vec_pack[...]
    vec = jnp.concatenate([vec_land[d][:, : D // 8] for d in range(8)], axis=1)
    vec_out[...] = vec
    for n in range(3):
        for i in range(4):
            at = (i % 2) * SIDE
            parts = [wq[h, 2 * n + i // 2][:, at : at + SIDE] for h in range(2)]
            cat_s[n, i * SIDE : (i + 1) * SIDE, :] = jnp.concatenate(parts, axis=1)
    writes = [pltpu.make_async_copy(cat_s, cat, s_cat)]
    writes[0].start()
    tok_copy.wait()

    def rows_of(b):
        rows = slice(b * WIDE, (b + 1) * WIDE)
        hat, _ = hat_of(embedded(tok[rows, :], passes[:, rows], vec))
        low = (hat * vec[PASSES : PASSES + 1] + vec[PASSES + 1 : PASSES + 2]).astype(bf16)
        norm_s[rows, :] = low
        writes.append(pltpu.make_async_copy(norm_s.at[rows, :], norm.at[rows, :], s_out.at[b, 3]))
        writes[-1].start()
        for n, out in enumerate((q, k_out, v)):
            qkv_s[n, rows, :] = nn(low, cat_s[n]).astype(bf16)
            writes.append(pltpu.make_async_copy(qkv_s.at[n, rows, :], out.at[rows, :], s_out.at[b, n]))
            writes[-1].start()

    count = tok.shape[0] // WIDE
    for b in range(count):
        rows_of(b)
        if b == 0:
            for m in range(3):
                from_left(2, m)
                from_right(3, m)
        if b == 1:
            for m in range(2):
                ref = all_pairs.at[y, 6 + m]
                arrived(ref, r_x2.at[m], x == 1)
                send(ref, ref, s_y2.at[m], r_y2.at[m], to_y)
                send(ref, wo_other.at[y, m], s_c.at[0, m], r_c.at[y, m], {"tensor": near})
    for m in range(2):
        ref = all_pairs.at[1 - y, 6 + m]
        arrived(ref, r_y2.at[m])
        send(ref, wo_other.at[1 - y, m], s_c.at[1, m], r_c.at[1 - y, m], {"tensor": near})
    for m in range(3):
        arrived(all_pairs.at[y, 6 + 3 * (1 - x) + m], r_x2.at[m], None if m == 2 else x == 0)
    for h in range(2):
        for m in range(2):
            arrived(wo_other.at[h, m], r_c.at[h, m])
    for copy in writes:
        copy.wait()
    for cond, copy in started:
        if cond is None:
            copy.wait_send()
        else:
            pl.when(cond)(copy.wait_send)


def gather(block_weights, vector_params, tokens, passes):
    seq = tokens.shape[0]
    dma = pltpu.SemaphoreType.DMA
    sizes = [(6,)] * 8 + [(3, 3)] * 2 + [(2, 3)] * 2 + [(3,)] * 2 + [(2,)] * 2 + [(7,), (8,)] + [(2, 2)] * 2
    sizes += [(seq // WIDE, 4)]
    vmem, far = pl.BlockSpec(memory_space=pltpu.VMEM), pl.BlockSpec(memory_space=pl.ANY)
    wide = jax.ShapeDtypeStruct((seq, PAIR), bf16)
    return pl.pallas_call(
        gather_kernel,
        in_specs=[vmem, vmem, far, vmem],
        out_specs=[far, far, far, vmem, far, far, far, far, far],
        out_shape=[
            jax.ShapeDtypeStruct((2, 24, SIDE, PAIR), bf16),
            jax.ShapeDtypeStruct((6, SIDE, PAIR), bf16),
            jax.ShapeDtypeStruct((2, 2, SIDE, PAIR), bf16),
            jax.ShapeDtypeStruct((16, D), f32),
            jax.ShapeDtypeStruct((seq, D), bf16),
            wide,
            wide,
            wide,
            jax.ShapeDtypeStruct((3, D, PAIR), bf16),
        ],
        scratch_shapes=[
            pltpu.VMEM((3, SIDE, PAIR), bf16),
            pltpu.VMEM((16, 128), f32),
            pltpu.VMEM((8, 16, 128), f32),
            pltpu.VMEM((2, 6, SIDE, PAIR), bf16),
            pltpu.VMEM((seq, D), bf16),
            pltpu.VMEM((seq, D), bf16),
            pltpu.VMEM((3, seq, PAIR), bf16),
            pltpu.VMEM((3, D, PAIR), bf16),
        ]
        + [dma(size) for size in sizes]
        + [dma] * 3,
        compiler_params=params(collective_id=0, has_side_effects=True),
        cost_estimate=cost(60),
        name="gather",
    )(block_weights, vector_params, tokens, passes)


def project_kernel(tok, pas, vec, wq, norm, q, k, v, cat):
    @pl.when(pl.program_id(0) == 0)
    def _():
        for x in range(3):
            for i in range(4):
                at = (i % 2) * SIDE
                parts = [wq[h, 2 * x + i // 2][:, at : at + SIDE] for h in range(2)]
                cat[x, i * SIDE : (i + 1) * SIDE, :] = jnp.concatenate(parts, axis=1)

    first = embedded(tok[...], pas[...], vec[...])
    hat, _ = hat_of(first)
    low = (hat * vec[PASSES : PASSES + 1] + vec[PASSES + 1 : PASSES + 2]).astype(bf16)
    norm[...] = low
    for x, out in enumerate((q, k, v)):
        out[...] = nn(low, cat[x]).astype(bf16)


def project(tokens, passes, vec, wq):
    seq = tokens.shape[0]
    row = lambda n: pl.BlockSpec((WIDE, n), lambda i: (i, 0))
    wide = jax.ShapeDtypeStruct((seq, PAIR), bf16)
    return pl.pallas_call(
        project_kernel,
        grid=(seq // WIDE,),
        in_specs=[
            row(D),
            pl.BlockSpec((1, WIDE), lambda i: (0, i)),
            full((16, D)),
            full((2, 6, SIDE, PAIR)),
        ],
        out_specs=[row(D), row(PAIR), row(PAIR), row(PAIR), full((3, D, PAIR))],
        out_shape=[
            jax.ShapeDtypeStruct((seq, D), bf16),
            wide,
            wide,
            wide,
            jax.ShapeDtypeStruct((3, D, PAIR), bf16),
        ],
        compiler_params=params(),
        cost_estimate=cost(16),
        name="project",
    )(tokens, passes, vec, wq)


def doc_state(lens, base):
    rows = base + lax.broadcasted_iota(jnp.int32, (1, ROWS), 1)
    rows = jnp.concatenate([rows, rows], axis=1)
    begin = jnp.int32(0)
    first = jnp.int32(0)
    starts = jnp.zeros((1, 2 * ROWS), jnp.int32)
    for c in range(DOCS):
        starts = jnp.where(rows >= begin, begin, starts)
        first = jnp.where(base >= begin, begin, first)
        begin = begin + lens[c]
    return rows, starts, first


def two_heads(block):
    left = lax.broadcasted_iota(jnp.int32, block.shape, 1) < HD
    none = jnp.zeros_like(block)
    return jnp.concatenate([jnp.where(left, block, none), jnp.where(left, none, block)], axis=0)


def one_above(both):
    return jnp.concatenate([both[:HD, :ROWS], both[HD:, ROWS:]], axis=0).T


def attend_kernel(lens, q, k, v, out, lse, acc):
    i = pl.program_id(0)
    base = i * ROWS
    rows, starts, first = doc_state(lens, base)
    pairs = [two_heads(q[:, p * 128 : (p + 1) * 128] * bf16(0.125)) for p in range(3)]
    for p in range(3):
        acc[p] = jnp.zeros((128, 2 * ROWS), f32)

    def step(j, carry):
        at = pl.multiple_of(j * ROWS, ROWS)
        keys = at + lax.broadcasted_iota(jnp.int32, (ROWS, 2 * ROWS), 0)
        seen = (keys >= starts) & (keys <= rows)
        here = pl.ds(at, ROWS)
        head = lambda p: slice(p * 128, (p + 1) * 128)
        scores = [jnp.where(seen, nt(k[here, head(p)], pairs[p]), masked_score) for p in range(3)]
        state = []
        for p in range(3):
            before, total = carry[2 * p], carry[2 * p + 1]
            now = jnp.maximum(before, jnp.max(scores[p], axis=0, keepdims=True))
            probs = jnp.exp(scores[p] - now)
            fade = jnp.exp(before - now)
            state += [now, total * fade + jnp.sum(probs, axis=0, keepdims=True)]
            acc[p] = acc[p] * fade + tn(v[here, head(p)], probs.astype(bf16))
        return tuple(state)

    zero = jnp.zeros((1, 2 * ROWS), f32)
    state = lax.fori_loop(first // ROWS, i + 1, step, (zero + masked_score, zero) * 3)
    lines = []
    for p in range(3):
        top, total = state[2 * p], state[2 * p + 1]
        out[:, p * 128 : (p + 1) * 128] = one_above(acc[p] / total).astype(bf16)
        line = top + jnp.log(total)
        lines += [line[:, :ROWS], line[:, ROWS:]]
    lse[...] = jnp.concatenate(lines + lines[:2], axis=0)


def attend(lens, q, k, v):
    seq = q.shape[0]
    row = pl.BlockSpec((ROWS, PAIR), lambda i, s: (i, 0))
    return pl.pallas_call(
        attend_kernel,
        grid_spec=pltpu.PrefetchScalarGridSpec(
            num_scalar_prefetch=1,
            grid=(seq // ROWS,),
            in_specs=[row, full((seq, PAIR)), full((seq, PAIR))],
            out_specs=[row, pl.BlockSpec((8, ROWS), lambda i, s: (0, i))],
            scratch_shapes=[
                pltpu.VMEM((3, 128, 2 * ROWS), f32),
            ],
        ),
        out_shape=[
            jax.ShapeDtypeStruct((seq, PAIR), bf16),
            jax.ShapeDtypeStruct((8, seq), f32),
        ],
        compiler_params=params(),
        cost_estimate=cost(30),
        name="attend",
    )(lens, q, k, v)


def attend_back_kernel(
    lens, q, k, v, mixed, lse, grad_mixed, dq, dk, dv, dk_acc, dv_acc, dq_acc
):
    i = pl.program_id(0)
    count = pl.num_programs(0)
    base = i * ROWS

    @pl.when(i == 0)
    def _():
        dk_acc[...] = jnp.zeros_like(dk_acc)
        dv_acc[...] = jnp.zeros_like(dv_acc)

    rows, starts, first = doc_state(lens, base)
    heads = lax.broadcasted_iota(jnp.int32, (8, 128), 0)
    lanes = lax.broadcasted_iota(jnp.int32, (8, 128), 1)
    pick = (lanes // HD == heads).astype(f32).astype(bf16)
    queries, grads, inner, lines = [], [], [], []
    for p in range(3):
        cols = slice(p * 128, (p + 1) * 128)
        queries.append(two_heads(q[:, cols] * bf16(0.125)))
        grads.append(two_heads(grad_mixed[:, cols]))
        product = grad_mixed[:, cols].astype(f32) * mixed[:, cols].astype(f32)
        high, low, _ = split_three(product)
        sums = nt(pick, high) + nt(pick, low)
        inner.append(jnp.concatenate([sums[0:1], sums[1:2]], axis=1))
        lines.append(jnp.concatenate([lse[2 * p : 2 * p + 1], lse[2 * p + 1 : 2 * p + 2]], axis=1))
        dq_acc[p] = jnp.zeros((128, 2 * ROWS), f32)

    def step(j, carry):
        at = pl.multiple_of(j * ROWS, ROWS)
        keys = at + lax.broadcasted_iota(jnp.int32, (ROWS, 2 * ROWS), 0)
        seen = (keys >= starts) & (keys <= rows)
        here = pl.ds(at, ROWS)
        for p in range(3):
            cols = slice(p * 128, (p + 1) * 128)
            kb = k[here, cols]
            scores = jnp.where(seen, nt(kb, queries[p]) - lines[p], masked_score)
            probs = jnp.exp(scores)
            grad_probs = nt(v[here, cols], grads[p])
            grad_scores = (probs * (grad_probs - inner[p])).astype(bf16)
            dv_acc[here, cols] += nn(probs.astype(bf16), grads[p])
            dk_acc[here, cols] += nn(grad_scores, queries[p])
            dq_acc[p] += tn(kb, grad_scores)
        return carry

    lax.fori_loop(first // ROWS, i + 1, step, 0)
    for p in range(3):
        dq[:, p * 128 : (p + 1) * 128] = (one_above(dq_acc[p]) * 0.125).astype(bf16)

    @pl.when(i == count - 1)
    def _():
        dk[...] = dk_acc[...].astype(bf16)
        dv[...] = dv_acc[...].astype(bf16)


def attend_back(lens, q, k, v, mixed, lse, grad_mixed):
    seq = q.shape[0]
    count = seq // ROWS
    row = pl.BlockSpec((ROWS, PAIR), lambda i, s: (i, 0))
    wide = jax.ShapeDtypeStruct((seq, PAIR), bf16)
    return pl.pallas_call(
        attend_back_kernel,
        grid_spec=pltpu.PrefetchScalarGridSpec(
            num_scalar_prefetch=1,
            grid=(count,),
            in_specs=[
                row,
                full((seq, PAIR)),
                full((seq, PAIR)),
                row,
                pl.BlockSpec((8, ROWS), lambda i, s: (0, i)),
                row,
            ],
            out_specs=[row, full((seq, PAIR)), full((seq, PAIR))],
            scratch_shapes=[
                pltpu.VMEM((seq, PAIR), f32),
                pltpu.VMEM((seq, PAIR), f32),
                pltpu.VMEM((3, 128, 2 * ROWS), f32),
            ],
        ),
        out_shape=[wide, wide, wide],
        compiler_params=params(),
        cost_estimate=cost(40),
        name="attend_back",
    )(lens, q, k, v, mixed, lse, grad_mixed)


def feed_kernel(
    small, tok, pas, vec, mine, cot, wo_mine, wo_other, four, columns, columns_x,
    out_chip, second_keep, grad_second, grad_mixed, sums, mid_send, mid_keep, *rest,
):
    results, rest = (rest[:4], rest[4:]) if small else (rest[:2], rest[2:])
    (
        wo, other, up, down, gup, gdown, go, core_out, core_in, far_out, far_in, ga_out, ga_in, oc_out, oc_in,
        g_send, g_keep, g_in, s_core, r_core, s_far, r_far, s_ga, r_ga, s_oc, r_oc, s_x, r_x, s_m, r_m,
    ) = rest
    step = pl.program_id(0)
    half = core_out.shape[0]
    t, dp = lax.axis_index("tensor"), lax.axis_index("dp")
    core, side = t % 2, t // 2
    near, far = side * 2 + (1 - core), (1 - side) * 2 + core
    z, column = (dp // 2, dp % 2) if small else (0, 0)
    far_x = z * 2 + 1 - column

    def copy(src, dst, s_sem, r_sem, j, to):
        return pltpu.make_async_remote_copy(
            src_ref=src.at[j],
            dst_ref=dst.at[j],
            send_sem=s_sem.at[j],
            recv_sem=r_sem.at[j],
            device_id={"tensor": to},
            device_id_type=MESH,
        )

    core_copy = lambda j: copy(core_out, core_in, s_core, r_core, j, near)
    far_copy = lambda j: copy(far_out, far_in, s_far, r_far, j, far)
    ga_copy = lambda j: copy(ga_out, ga_in, s_ga, r_ga, j, near)
    oc_copy = lambda j: copy(oc_out, oc_in, s_oc, r_oc, j, near)

    def x_copy(slot):
        return pltpu.make_async_remote_copy(
            src_ref=g_send.at[slot],
            dst_ref=g_in.at[slot],
            send_sem=s_x.at[slot],
            recv_sem=r_x.at[slot],
            device_id={"dp": far_x},
            device_id_type=MESH,
        )

    def mixed_copy(block):
        rows = pl.ds(pl.multiple_of(block * ROWS, ROWS), ROWS)
        return pltpu.make_async_remote_copy(
            src_ref=mine.at[rows],
            dst_ref=other.at[rows],
            send_sem=s_m.at[block],
            recv_sem=r_m.at[block],
            device_id={"tensor": near},
            device_id_type=MESH,
        )

    barrier = pltpu.get_barrier_semaphore()

    @pl.when(step == 0)
    def _():
        for to in (near, far):
            pl.semaphore_signal(barrier, inc=1, device_id={"tensor": to}, device_id_type=MESH)
        if small:
            pl.semaphore_signal(barrier, inc=1, device_id={"dp": far_x}, device_id_type=MESH)
        for h in range(2):
            for m in range(2):
                rows, cols = slice(h * SIDE, (h + 1) * SIDE), slice(m * PAIR, (m + 1) * PAIR)
                wo[rows, cols] = wo_mine[h, m]
                wo[PAIR + h * SIDE : PAIR + (h + 1) * SIDE, cols] = wo_other[h, m]
        for r in range(4):
            for m in range(2):
                rows, cols = slice(r * SIDE, (r + 1) * SIDE), slice(m * PAIR, (m + 1) * PAIR)
                for at, weight in ((8, up), (16, down)):
                    pair = at + 2 * r + m
                    if pair < 12:
                        weight[rows, cols] = four[0, pair - 8]
                        continue
                    n = (pair // 6 - 2) * 3 + pair % 3
                    for source, here in ((columns, pair // 3 % 2), (columns_x, 1 - pair // 3 % 2)):

                        @pl.when(column == here)
                        def _():
                            weight[rows, cols] = source[n]

        pl.semaphore_wait(barrier, 3 if small else 2)
        for j in range(half):
            mixed_copy(core * half + j).start()
            mixed_copy((1 - core) * half + j).start()
        gup[...] = jnp.zeros_like(gup)
        gdown[...] = jnp.zeros_like(gdown)
        go[...] = jnp.zeros_like(go)
        sums[...] = jnp.zeros_like(sums)

    @pl.when(step < 2 * half)
    def _():
        j = step // 2
        owner = jnp.where(step % 2 == 0, 1 - core, core)
        here = pl.ds(pl.multiple_of((owner * half + j) * ROWS, ROWS), ROWS)
        first = embedded(tok[...], pas[...], vec[...])
        mixed_copy(owner * half + j).wait_recv()
        second = first + nn(jnp.concatenate([mine[here, :], other[here, :]], axis=1), wo[...])
        hat, _ = hat_of(second)
        low = (hat * vec[PASSES + 2 : PASSES + 3] + vec[PASSES + 3 : PASSES + 4]).astype(bf16)
        upper = nn(low, up[...])
        square = upper * upper
        bent = jnp.tanh(gelu_coef * upper * (1.0 + 0.044715 * square))
        act = (0.5 * upper * (1.0 + bent)).astype(bf16)
        slope = 0.5 * (1.0 + bent) + (0.5 * gelu_coef) * upper * (1.0 - bent * bent) * (
            1.0 + (3 * 0.044715) * square
        )
        grad_act = nt(cot[...], down[...])
        grad_upper = (grad_act * slope).astype(bf16)
        part = nt(grad_upper, up[...])

        @pl.when(step % 2 == 0)
        def _():
            core_out[j] = part.astype(bf16)
            core_copy(j).start()

        @pl.when(step % 2 == 1)
        def _():
            core_copy(j).wait_recv()
            far_out[j] = (part + core_in[j].astype(f32)).astype(bf16)
            far_copy(j).start()
            second_keep[pl.ds(pl.multiple_of(j * ROWS, ROWS), ROWS), :] = second

        gup[...] += tn(low, grad_upper)
        gdown[...] += tn(act, cot[...])
        out_part = nn(act, down[...])

        @pl.when(step % 2 == 0)
        def _():
            oc_out[j] = out_part.astype(bf16)
            oc_copy(j).start()

        @pl.when(step % 2 == 1)
        def _():
            oc_copy(j).wait_recv()
            out_chip[...] = (out_part + oc_in[j].astype(f32)).astype(bf16)

    @pl.when(step == 2 * half - 1)
    def _():
        for r in range(4):
            for m in range(2):
                rows, cols = slice(r * SIDE, (r + 1) * SIDE), slice(m * PAIR, (m + 1) * PAIR)
                for at, total in ((8, gup), (16, gdown)):
                    pair = at + 2 * r + m
                    slot, place = (pair // 6 - 1) * 3 + pair % 3, pair // 3 % 2
                    value = total[rows, cols].astype(bf16)
                    kept, sent, n = (mid_keep, mid_send, slot) if slot < 6 else (g_keep, g_send, slot - 6)

                    @pl.when(column == place)
                    def _():
                        kept[n] = value

                    @pl.when(column != place)
                    def _():
                        sent[n] = value
        if small:
            for n in range(3):
                x_copy(n).start()

    def through_out(grad, block):
        here = pl.ds(pl.multiple_of(block * ROWS, ROWS), ROWS)
        grad_mixed[here, :] = nt(grad, wo[:PAIR, :]).astype(bf16)
        go[...] += tn(mine[here, :], grad)

    @pl.when((step >= 2 * half) & (step < 3 * half))
    def _():
        j = step - 2 * half
        hat, root = hat_of(second_keep[pl.ds(pl.multiple_of(j * ROWS, ROWS), ROWS), :])
        far_copy(j).wait_recv()
        grad = far_out[j].astype(f32) + far_in[j].astype(f32)
        result = cot[...].astype(f32) + norm_back(hat, root, grad, vec[PASSES + 2 : PASSES + 3])
        low = result.astype(bf16)
        ga_out[j] = low
        ga_copy(j).start()
        grad_second[...] = result
        sums[0:1] += jnp.sum(grad * hat, axis=0, keepdims=True)
        sums[1:2] += jnp.sum(grad, axis=0, keepdims=True)
        through_out(low, core * half + j)

    @pl.when(step > 2 * half)
    def _():
        j = step - 2 * half - 1
        ga_copy(j).wait_recv()
        through_out(ga_in[j], (1 - core) * half + j)

    @pl.when(step == 3 * half)
    def _():
        at = pl.multiple_of(side * SIDE, SIDE)
        for m in range(2):
            value = go[pl.ds(at, SIDE), m * PAIR : (m + 1) * PAIR].astype(bf16)

            @pl.when(column == 0)
            def _():
                mid_keep[m] = value

            @pl.when(column != 0)
            def _():
                mid_send[m] = value

        for j in range(half):
            core_copy(j).wait_send()
            oc_copy(j).wait_send()
            mixed_copy(j).wait_send()
            mixed_copy(half + j).wait_send()
            far_copy(j).wait_send()
            ga_copy(j).wait_send()
        if small:
            for n in range(3):
                x_copy(n).wait_send()
                x_copy(n).wait_recv()
                value = (g_keep[n].astype(f32) + g_in[n].astype(f32)).astype(bf16)
                for turn in range(4):

                    @pl.when(z + turn == 3)
                    def _():
                        results[turn][n] = value
        else:
            results[0][...] = g_send[...]
            results[1][...] = g_keep[...]


def feed(small, tokens, passes, vec, mine, cotangent, pairs, wo_other, columns, columns_x):
    seq = tokens.shape[0]
    half = seq // ROWS // 2

    def block(i):
        core = lax.axis_index("tensor") % 2
        work = jnp.minimum(i, 2 * half - 1)
        owner = jnp.where(work % 2 == 0, 1 - core, core)
        return owner * half + work // 2

    def cot_block(i):
        core = lax.axis_index("tensor") % 2
        return jnp.where(i < 2 * half, block(i), core * half + jnp.minimum(i - 2 * half, half - 1))

    side = lambda: lax.axis_index("tensor") // 2
    row = lambda n: pl.BlockSpec((ROWS, n), lambda i: (block(i), 0))
    keep = pl.BlockSpec((ROWS, D), lambda i: (jnp.minimum(i // 2, half - 1), 0))
    last = pl.BlockSpec((ROWS, D), lambda i: (jnp.clip(i - 2 * half, 0, half - 1), 0))
    rows = lambda kind: jax.ShapeDtypeStruct((seq // 2, D), kind)
    gr = lambda n: jax.ShapeDtypeStruct((n, SIDE, PAIR), bf16)
    ends = [(3, SIDE, PAIR)] * (4 if small else 2)
    buffer = pltpu.VMEM((half, ROWS, D), bf16)
    dma = pltpu.SemaphoreType.DMA((half,))
    return pl.pallas_call(
        functools.partial(feed_kernel, small),
        grid=(3 * half + 1,),
        in_specs=[
            row(D),
            pl.BlockSpec((1, ROWS), lambda i: (0, block(i))),
            full((16, D)),
            full((seq, PAIR)),
            pl.BlockSpec((ROWS, D), lambda i: (cot_block(i), 0)),
            pl.BlockSpec((2, 2, SIDE, PAIR), lambda i: (0, 3, 0, 0)),
            full(wo_other.shape),
            pl.BlockSpec((1, 4, SIDE, PAIR), lambda i: (side(), 2, 0, 0)),
            full(columns.shape),
            full(columns.shape),
        ],
        out_specs=[
            keep,
            full((seq // 2, D)),
            last,
            full((seq, PAIR)),
            full((8, D)),
            full((6, SIDE, PAIR)),
            full((6, SIDE, PAIR)),
        ]
        + [full(shape) for shape in ends],
        scratch_shapes=[
            pltpu.VMEM((D, D), bf16),
            pltpu.VMEM((seq, PAIR), bf16),
            pltpu.VMEM((D, D), bf16),
            pltpu.VMEM((D, D), bf16),
            pltpu.VMEM((D, D), f32),
            pltpu.VMEM((D, D), f32),
            pltpu.VMEM((PAIR, D), f32),
        ]
        + [buffer] * 8
        + [pltpu.VMEM((3, SIDE, PAIR), bf16)] * 3
        + [dma] * 8
        + [pltpu.SemaphoreType.DMA((3,))] * 2
        + [pltpu.SemaphoreType.DMA((2 * half,))] * 2,
        out_shape=[
            rows(bf16),
            rows(f32),
            rows(f32),
            jax.ShapeDtypeStruct((seq, PAIR), bf16),
            jax.ShapeDtypeStruct((8, D), f32),
            gr(6),
            gr(6),
        ]
        + [jax.ShapeDtypeStruct(shape, bf16) for shape in ends],
        compiler_params=params(collective_id=1, has_side_effects=True),
        cost_estimate=cost(50),
        name="feed_forward",
    )(tokens, passes, vec, mine, cotangent, pairs, wo_other, pairs, columns, columns_x)


CHUNK = SIDE // 2
CHUNKS = 18
TAKEN = (
    ((8, 3), (10, 4), (12, 12)),
    ((5, 1), (7, 3), (8, 4), (9, 6), (10, 7), (11, 8), (12, 12)),
    ((2, 2), (4, 3), (5, 4), (7, 6), (8, 8), (9, 9), (10, 11), (12, 12)),
    ((0, 3), (2, 5), (4, 6), (5, 7), (6, 8), (7, 12)),
)
GRAD_STEPS = 3


def last_kernel(
    small, norm_all, dq_all, dk_all, dv_all, cat, tok, pas, vec, grad_second, sums_two, second, chip, far,
    mid_near, mid_keep, output, input_grad, *rest,
):
    if small:
        late, vec_sum = rest[:2]
        rest = rest[2:]
        (
            core_out, core_in, sums, core_sums, x_in, z_in, z_out, up_in, v_out, v_in, total,
            s_core, r_core, s_sum, r_sum, s_x, r_x, s_z, r_z, s_up, r_up, s_v, r_v, ready, norm, dq, dk, dv, g_send, g_keep,
            s_own, s_res, r_res, s_in,
        ) = rest
    else:
        (
            vec_sum, send_out, keep_out, core_out, core_in, sums, core_sums, s_core, r_core, s_sum, r_sum, ready,
            norm, dq, dk, dv, g_send, g_keep, s_own, s_res, r_res, s_in,
        ) = rest
    step = pl.program_id(0)
    i = step - GRAD_STEPS
    half = core_out.shape[0]
    t, dp = lax.axis_index("tensor"), lax.axis_index("dp")
    core, side = t % 2, t // 2
    near = side * 2 + (1 - core)
    z, column = (dp // 2, dp % 2) if small else (0, 0)
    far_x = z * 2 + 1 - column
    peers = [lax.rem(dp + k, 8) for k in range(1, 8)]

    def copy(src, dst, s_sem, r_sem, to):
        return pltpu.make_async_remote_copy(
            src_ref=src, dst_ref=dst, send_sem=s_sem, recv_sem=r_sem, device_id=to, device_id_type=MESH
        )

    core_copy = lambda j: copy(core_out.at[j], core_in.at[j], s_core.at[j], r_core.at[j], {"tensor": near})
    sum_copy = lambda: copy(sums, core_sums, s_sum, r_sum, {"tensor": near})

    def rows_at(n, j, owner):
        rows = pl.ds(pl.multiple_of((owner * half + j) * ROWS, ROWS), ROWS)
        return (output, input_grad)[n].at[rows]

    own_result = lambda n, j: pltpu.make_async_copy(ready.at[n, j], rows_at(n, j, core), s_own.at[n, j])
    near_result = lambda n, j, owner: copy(
        ready.at[n, j], rows_at(n, j, owner), s_res.at[n, j], r_res.at[n, j], {"tensor": near}
    )

    def part_of(ref, k):
        return ref.at[k // 2, pl.ds((k % 2) * CHUNK, CHUNK)]

    x_copy = lambda k: copy(part_of(g_send, k), x_in.at[k], s_x.at[k], r_x.at[k], {"dp": far_x})
    z_copy = lambda k: copy(z_out.at[k], z_in.at[k], s_z.at[k], r_z.at[k], {"dp": dp - 2})
    up_copy = lambda k: copy(z_out.at[k], up_in.at[k - 6], s_up.at[k - 6], r_up.at[k - 6], {"dp": dp + 2})
    v_copy = lambda n: copy(v_out.at[peers[n]], v_in.at[dp], s_v.at[n], r_v.at[dp], {"dp": peers[n]})
    barrier = pltpu.get_barrier_semaphore()

    loads = [
        pltpu.make_async_copy(src, dst, s_in.at[n])
        for n, (src, dst) in enumerate(((norm_all, norm), (dq_all, dq), (dv_all, dv), (dk_all, dk)))
    ]

    @pl.when(step == 0)
    def _():
        for load in loads:
            load.start()
        pl.semaphore_signal(barrier, inc=1, device_id={"tensor": near}, device_id_type=MESH)
        if small:
            for peer in peers:
                pl.semaphore_signal(barrier, inc=1, device_id={"dp": peer}, device_id_type=MESH)
            late[...] = jnp.zeros_like(late)
        sums[...] = jnp.zeros_like(sums)
        sums[PASSES + 2 : PASSES + 4] = sums_two[0:2]
        pl.semaphore_wait(barrier, 8 if small else 1)

    def mine_of(grad):
        return jnp.where(side == 0, grad[:, :SIDE], grad[:, SIDE:])

    def pairs_of(grad):
        value = tn(grad, norm[...]).astype(bf16)
        return value[:, :PAIR], value[:, PAIR:]

    second_two = jnp.where(jnp.asarray(column) == 0, 1, 0)

    @pl.when(step == 0)
    def _():
        for load in loads[:3]:
            load.wait()
        both = pairs_of(jnp.where(jnp.asarray(column) == 0, mine_of(dv), mine_of(dq)))
        for m in range(2):
            g_send[second_two + m] = both[m]
        if small:
            for m in range(4):
                x_copy(2 * second_two + m).start()

    @pl.when(step == 1)
    def _():
        loads[3].wait()
        both = pairs_of(mine_of(dk))
        for place, (kept, sent) in enumerate(((0, 1), (1, 0))):

            @pl.when(jnp.asarray(column) == place)
            def _():
                g_keep[2 - 2 * place] = both[kept]
                g_send[2 * place] = both[sent]

        if small:
            for m in range(2):
                x_copy(4 * column + m).start()

    @pl.when(step == 2)
    def _():
        both = pairs_of(jnp.where(jnp.asarray(column) == 0, mine_of(dq), mine_of(dv)))
        for m in range(2):
            g_keep[1 - second_two + m] = both[m]
        if not small:
            send_out[...] = g_send[...]
            keep_out[...] = g_keep[...]

    @pl.when((i >= 0) & (i < 2 * half))
    def _():
        block = lax.rem(i + (1 - core) * half, 2 * half)
        rows = pl.ds(pl.multiple_of(block * ROWS, ROWS), ROWS)
        part = nt(dq[rows, :], cat[0]) + nt(dk[rows, :], cat[1]) + nt(dv[rows, :], cat[2])

        @pl.when(i < half)
        def _():
            core_out[i] = part.astype(bf16)
            core_copy(i).start()

        @pl.when(i >= half)
        def _():
            j = i - half
            hat, root = hat_of(embedded(tok[...], pas[...], vec[...]))
            core_copy(j).wait_recv()
            grad = part + core_in[j].astype(f32)
            result = grad_second[...] + norm_back(hat, root, grad, vec[PASSES : PASSES + 1])
            ready[0, j] = (second[...] + (chip[...].astype(f32) + far[...].astype(f32))).astype(bf16)
            ready[1, j] = result.astype(bf16)
            for n in range(2):
                own_result(n, j).start()
                near_result(n, j, core).start()
            chosen = one_hot(pas[...])
            high, mid, _ = split_three(result)
            sums[...] += nn(chosen, high) + nn(chosen, mid)
            sums[PASSES : PASSES + 1] += jnp.sum(grad * hat, axis=0, keepdims=True)
            sums[PASSES + 1 : PASSES + 2] += jnp.sum(grad, axis=0, keepdims=True)

    @pl.when(i == 2 * half - 1)
    def _():
        sum_copy().start()

    if small:

        def term_of(k):
            rows = pl.ds(pl.multiple_of((k % 2) * CHUNK, 16), CHUNK)

            @pl.when(jnp.asarray(k) < 6)
            def _():
                x_copy(k).wait_recv()
                total[...] = g_keep[k // 2, rows, :].astype(f32) + x_in[k].astype(f32)

            @pl.when(jnp.asarray(k) >= 6)
            def _():
                total[...] = mid_keep[k // 2 - 3, rows, :].astype(f32) + mid_near[k // 2 - 3, rows, :].astype(f32)

            return total[...]

        def keep_late(k, pair, total):
            late[pair, pl.ds(pl.multiple_of((k % 2) * CHUNK, 16), CHUNK), :] = total

        def pass_on(k):
            term = term_of(k)

            @pl.when(z < 3)
            def _():
                z_copy(k).wait_recv()

            below = jnp.where(z < 3, z_in[k].astype(f32), 0.0)
            passed = term + below

            @pl.when((z > 1) | ((z == 1) & (k < 6)))
            def _():
                z_out[k] = passed.astype(bf16)
                z_copy(k).start()

            @pl.when(z == 0)
            def _():
                keep_late(k, k // 2, passed)

            @pl.when((z == 1) & (k >= 6))
            def _():
                up_copy(k).wait_recv()
                keep_late(k, k // 2 - 3, passed + up_in[k - 6].astype(f32))

        def at_position(p, carry):
            k = jnp.where(p < 3, p + 6, jnp.where(p < 9, lax.rem(p + 3 + 2 * column, 6), p))

            @pl.when((z > 0) | (k < 6))
            def _():
                pass_on(k)

            return carry

        begin, end = jnp.int32(0), jnp.int32(0)
        for place, line in enumerate(TAKEN):
            for at, upto in line:
                begin = jnp.where((z == place) & (step > at), upto, begin)
                end = jnp.where((z == place) & (step >= at), upto, end)
        lax.fori_loop(begin, end, at_position, 0)

        @pl.when((step == 0) & (z == 0))
        def _():
            for k in range(6, CHUNKS):
                z_out[k] = term_of(k).astype(bf16)
                up_copy(k).start()

        for at, first_chunk, upto in ((0, 12, 14), (7, 14, 18)):

            @pl.when((step == at) & (z == 3))
            def _(first_chunk=first_chunk, upto=upto):
                for k in range(first_chunk, upto):
                    z_out[k] = term_of(k).astype(bf16)
                    z_copy(k).start()

        for at, first_chunk, upto in ((10, 12, 16), (11, 16, 18)):

            @pl.when((step == at) & (z == 1))
            def _(first_chunk=first_chunk, upto=upto):
                for k in range(first_chunk, upto):
                    up_copy(k).wait_recv()
                    z_out[k] = (term_of(k) + up_in[k - 6].astype(f32)).astype(bf16)
                    up_copy(k).start()

        @pl.when((step == pl.num_programs(0) - 1) & (z == 2))
        def _():
            for k in range(12, CHUNKS):
                z_copy(k).wait_recv()
                up_copy(k).wait_recv()
                keep_late(k, k // 2 - 6, term_of(k) + z_in[k].astype(f32) + up_in[k - 6].astype(f32))

    @pl.when(i == 2 * half)
    def _():
        sum_copy().wait_recv()
        total = sums[...] + core_sums[...]
        if small:
            wide = D // 8
            for d in range(8):
                v_out[d, :, 0:wide] = total[:, d * wide : (d + 1) * wide]
                v_out[d, :, wide:] = jnp.zeros((16, 128 - wide), f32)
            for n in range(7):
                v_copy(n).start()
        else:
            vec_sum[...] = total

    @pl.when(step == pl.num_programs(0) - 1)
    def _():
        for j in range(half):
            core_copy(j).wait_send()
            for n in range(2):
                own_result(n, j).wait()
                near_result(n, j, core).wait_send()
                near_result(n, j, 1 - core).wait_recv()
        sum_copy().wait_send()
        if small:
            for peer in peers:
                copy(v_out.at[0], v_in.at[peer], s_v.at[0], r_v.at[peer], {"dp": far_x}).wait_recv()
            v_in[dp] = v_out[dp]
            total = v_in[0]
            for d in range(1, 8):
                total = total + v_in[d]
            vec_sum[...] = total
            for n in range(7):
                v_copy(n).wait_send()
            for k in range(CHUNKS):
                if k < 6:
                    x_copy(k).wait_send()
                    pl.when(z > 0)(z_copy(k).wait_send)
                elif k < 12:
                    pl.when(z > 1)(z_copy(k).wait_send)
                    pl.when(z == 0)(up_copy(k).wait_send)
                else:
                    pl.when(z == 3)(z_copy(k).wait_send)
                    pl.when(z < 2)(up_copy(k).wait_send)


def last(
    small, norm, dq, dk, dv, cat, tokens, passes, vec, grad_second, sums_two, second, chip, far, mid_near, mid_keep
):
    seq = dq.shape[0]
    half = seq // ROWS // 2
    core = lambda: lax.axis_index("tensor") % 2

    own = lambda i: jnp.clip(i - GRAD_STEPS - half, 0, half - 1)
    mine = pl.BlockSpec((ROWS, D), lambda i: (own(i), 0))
    dma = pltpu.SemaphoreType.DMA
    out_specs = [pl.BlockSpec(memory_space=pl.ANY)] * 2
    out_shape = [jax.ShapeDtypeStruct((seq, D), bf16)] * 2
    scratch = [
        pltpu.VMEM((half, ROWS, D), bf16),
        pltpu.VMEM((half, ROWS, D), bf16),
        pltpu.VMEM((16, D), f32),
        pltpu.VMEM((16, D), f32),
    ]
    sems = [dma((half,)), dma((half,)), dma, dma]
    if small:
        out_specs += [full((3, SIDE, PAIR)), full((16, 128))]
        out_shape += [
            jax.ShapeDtypeStruct((3, SIDE, PAIR), f32),
            jax.ShapeDtypeStruct((16, 128), f32),
        ]
        scratch += [pltpu.VMEM((CHUNKS, CHUNK, PAIR), bf16)] * 3
        scratch += [pltpu.VMEM((12, CHUNK, PAIR), bf16)]
        scratch += [pltpu.VMEM((8, 16, 128), f32)] * 2 + [pltpu.VMEM((CHUNK, PAIR), f32)]
        sems += [dma((6,))] * 2 + [dma((CHUNKS,))] * 2 + [dma((12,))] * 2 + [dma((7,)), dma((8,))]
    else:
        out_specs += [full((16, D)), full((3, SIDE, PAIR)), full((3, SIDE, PAIR))]
        out_shape += [jax.ShapeDtypeStruct((16, D), f32)] + [jax.ShapeDtypeStruct((3, SIDE, PAIR), bf16)] * 2
    scratch_more = [pltpu.VMEM((2, half, ROWS, D), bf16), pltpu.VMEM((seq, D), bf16)]
    scratch_more += [pltpu.VMEM((seq, PAIR), bf16)] * 3
    scratch_more += [pltpu.VMEM((3, SIDE, PAIR), bf16)] * 2 + [dma((2, half))] * 3 + [dma((4,))]
    return pl.pallas_call(
        functools.partial(last_kernel, small),
        grid=(GRAD_STEPS + 2 * half + 2,),
        in_specs=[
            *[pl.BlockSpec(memory_space=pl.ANY)] * 4,
            full(cat.shape),
            pl.BlockSpec((ROWS, D), lambda i: (core() * half + own(i), 0)),
            pl.BlockSpec((1, ROWS), lambda i: (0, core() * half + own(i))),
            full((16, D)),
            mine,
            full((8, D)),
            mine,
            mine,
            mine,
            full(mid_near.shape),
            full(mid_keep.shape),
        ],
        out_specs=out_specs,
        out_shape=out_shape,
        scratch_shapes=scratch + sems + scratch_more,
        compiler_params=params(collective_id=2, has_side_effects=True),
        cost_estimate=cost(38),
        name="last",
    )(norm, dq, dk, dv, cat, tokens, passes, vec, grad_second, sums_two, second, chip, far, mid_near, mid_keep)


def precondition(grad, weight, left, right, left_root, right_root):
    high = lax.Precision.HIGHEST
    left_new = decay * left + (1.0 - decay) * jnp.einsum(
        "...ij,...kj->...ik", grad, grad, precision=high
    )
    right_new = decay * right + (1.0 - decay) * jnp.einsum(
        "...ji,...jk->...ik", grad, grad, precision=high
    )
    half = jnp.einsum("...ij,...jk->...ik", left_root, grad, precision=high)
    step = jnp.einsum("...ij,...jk->...ik", half, right_root, precision=high)
    return (left_new, right_new, step, weight - rate_matrix * step)


def two_part(value):
    high = value.astype(bf16)
    return high, (value - high.astype(f32)).astype(bf16)


def dot_three(dot, a, b):
    return dot(a[0], b[0]) + (dot(a[0], b[1]) + dot(a[1], b[0]))


def renew_kernel(
    late, own, one, two, three, weight, left, right, left_root, right_root, output, input_grad,
    left_new, right_new, step, new, output_new, input_grad_new,
):
    output_new[...] = output[...]
    input_grad_new[...] = input_grad[...]

    @pl.when(pl.program_id(0) < 3)
    def _():
        early = own[0].astype(f32) + one[0].astype(f32) + two[0].astype(f32) + three[0].astype(f32)
        z = lax.axis_index("dp") // 2
        both = late[0] + jnp.where(z > 2, early, 0.0)
        for n in range(2):
            grad = both[:, n * SIDE : (n + 1) * SIDE]
            grad = two_part(jnp.where(z == 0, grad.T, grad))
            left_new[0, n] = decay * left[0, n] + (1.0 - decay) * dot_three(nt, grad, grad)
            right_new[0, n] = decay * right[0, n] + (1.0 - decay) * dot_three(tn, grad, grad)
            half = dot_three(nn, two_part(left_root[0, n]), grad)
            value = dot_three(nn, two_part(half), two_part(right_root[0, n]))
            step[0, n] = value
            new[0, n] = weight[0, n] - rate_matrix * value


def renew(late, own, far, weight, left, right, left_root, right_root, output, input_grad):
    pair = pl.BlockSpec((1, SIDE, PAIR), lambda i: (jnp.minimum(i, 2), 0, 0))
    slot = pl.BlockSpec((1, 2, SIDE, SIDE), lambda i: (0, jnp.minimum(i, 2), 0, 0))
    rows = pl.BlockSpec((output.shape[0] // 4, D), lambda i: (i, 0))
    return pl.pallas_call(
        renew_kernel,
        grid=(4,),
        in_specs=[pair] * 5 + [slot] * 5 + [rows] * 2,
        out_specs=[slot] * 4 + [rows] * 2,
        out_shape=[jax.ShapeDtypeStruct(weight.shape, f32)] * 4
        + [jax.ShapeDtypeStruct(value.shape, value.dtype) for value in (output, input_grad)],
        compiler_params=params(46),
        cost_estimate=cost(8),
        name="renew",
    )(late, own, *far, weight, left, right, left_root, right_root, output, input_grad)


def to_pairs(blocks):
    n = blocks.shape[0] // 2
    return blocks.reshape(n, 2, SIDE, SIDE).transpose(0, 2, 1, 3).reshape(n, SIDE, PAIR)


def from_pairs(pairs):
    n = pairs.shape[0]
    return pairs.reshape(n, SIDE, 2, SIDE).transpose(0, 2, 1, 3).reshape(2 * n, SIDE, SIDE)


def swap(value, bit):
    return lax.ppermute(value, "tensor", [(t, t ^ bit) for t in range(NT)])


def hop_x(value):
    return lax.ppermute(value, "dp", [(d, d ^ 1) for d in range(8)])


def hop_z(value, turn, ends):
    pairs = [(d, (d + 2 * turn) % 8) for d in range(8) if (d // 2 + turn) % 4 in ends]
    return lax.ppermute(value, "dp", pairs)


def tie(*values):
    return lax.optimization_barrier(values)


def on_device(
    tokens,
    pass_ids,
    doc_lengths,
    cotangent,
    block_weights,
    vector_params,
    vector_moment,
    block_left,
    block_right,
    block_left_root,
    block_right_root,
):
    t, dp = lax.axis_index("tensor"), lax.axis_index("dp")
    core, side = t % 2, t // 2
    n_dp = lax.axis_size("dp")
    small = n_dp == 8
    z, column = (dp // 2, dp % 2) if small else (0, 0)
    lens = doc_lengths[0]
    seq = tokens.shape[0]
    passes = pass_ids.reshape(1, seq)
    total_blocks = (D // SIDE) * (4 + 2 * (FF // D))
    slots = block_weights.shape[1] * n_dp

    if small:
        pairs, columns, wo_other, vec, norm, q, k, v, cat = gather(
            block_weights, vector_params, tokens, passes
        )
        columns_x = hop_x(columns)
    else:
        every = lax.all_gather(block_weights.astype(bf16), "dp", axis=1, tiled=True)[0]
        near = to_pairs(every[:total_blocks])
        far = swap(near, 2)
        pairs = jnp.where(side == 0, jnp.stack([near, far]), jnp.stack([far, near]))
        vec = lax.all_gather(vector_params, "dp", axis=1, tiled=True)
        vec = jnp.pad(vec, ((0, 16 - vec.shape[0]), (0, 0)))
        wo_other = swap(pairs[:, 6:8], 1)
        columns = jnp.concatenate([near[12:15], near[18:21]], axis=0)
        columns_x = jnp.concatenate([near[15:18], near[21:24]], axis=0)
        norm, q, k, v, cat = project(tokens, passes, vec, pairs)
    mine, lse = attend(lens, q, k, v)
    out_chip, second, grad_second, grad_mixed, sums_two, mid_send, mid_keep, *ends = feed(
        small, tokens, passes, vec, mine, cotangent, pairs, wo_other, columns, columns_x
    )
    out_far = swap(out_chip, 2)
    if small:
        far = [hop_z(ends[turn], turn, (3,)) for turn in (1, 2, 3)]
        mid_send = hop_x(mid_send)
    dq, dk, dv = attend_back(lens, q, k, v, mine, lse, grad_mixed)
    if small:
        *far, out_far, mid_send, dq = tie(*far, out_far, mid_send, dq)
    output, input_grad, *sums = last(
        small, norm, dq, dk, dv, cat, tokens, passes, vec, grad_second, sums_two, second, out_chip, out_far,
        mid_send, mid_keep,
    )
    if small:
        late, vector_sum = sums
        left_new, right_new, step, weight_new, output, input_grad = renew(
            late, ends[0], far, block_weights, block_left, block_right, block_left_root, block_right_root,
            output, input_grad,
        )
        vector_grad = vector_sum[: PASSES + 4, : vector_params.shape[1]]
    else:
        vector_part, g_send, g_keep = sums[0][: PASSES + 4], *sums[1:]
        send, keep = ends
        rest = jnp.stack(
            [
                jnp.concatenate([mid_keep, keep]).reshape(3, 3, SIDE, PAIR),
                jnp.concatenate([mid_send, send]).reshape(3, 3, SIDE, PAIR),
            ],
            axis=1,
        )
        grad_qkv = from_pairs(jnp.concatenate([g_keep, g_send], axis=0)).swapaxes(1, 2)
        grad_rest = from_pairs(rest.reshape(18, SIDE, PAIR))
        spare = jnp.zeros((slots - total_blocks, SIDE, SIDE), bf16)
        grad_blocks = jnp.concatenate([grad_qkv, grad_rest, spare], axis=0)[None].astype(f32)
        owned = lax.psum_scatter(grad_blocks, "dp", scatter_dimension=1, tiled=True)
        vector_grad = lax.psum_scatter(vector_part, "dp", scatter_dimension=1, tiled=True)
        left_new, right_new, step, weight_new = precondition(
            owned, block_weights, block_left, block_right, block_left_root, block_right_root
        )
    moment_new = decay * vector_moment + (1.0 - decay) * vector_grad * vector_grad
    vector_new = vector_params - rate_vector * vector_grad / (jnp.sqrt(moment_new) + moment_eps)
    return (
        output,
        input_grad,
        left_new,
        right_new,
        step,
        weight_new,
        vector_grad,
        moment_new,
        vector_new,
    )


def solution(mesh):
    rows, line = P("dp", None), P(None, "dp")
    block = P("tensor", "dp", None, None)
    return jax.shard_map(
        on_device,
        mesh=mesh,
        in_specs=(rows, P("dp"), rows, rows, block, line, line, block, block, block, block),
        out_specs=(rows, rows, block, block, block, block, line, line, line),
        check_vma=False,
    )
```

```python
import functools

import jax
import jax.numpy as jnp
from jax import lax
from jax.experimental import pallas as pl
from jax.experimental.pallas import tpu as pltpu
from jax.sharding import PartitionSpec as P

D = 768
HD = 64
FF = 3072
PASSES = 5
SIDE = 192
PAIR = 2 * SIDE
ROWS = 256
WIDE = 512
DOCS = 8
NT = 4

norm_eps = 1e-05
moment_eps = 1e-08
rate_matrix = 0.03
rate_vector = 0.2
decay = 0.5
gelu_coef = 0.7978845608028654
masked_score = -1e30
f32 = jnp.float32
bf16 = jnp.bfloat16
MESH = pl.DeviceIdType.MESH


def nn(a, b):
    return lax.dot_general(a, b, (((1,), (0,)), ((), ())), preferred_element_type=f32)


def nt(a, b):
    return lax.dot_general(a, b, (((1,), (1,)), ((), ())), preferred_element_type=f32)


def tn(a, b):
    return lax.dot_general(a, b, (((0,), (0,)), ((), ())), preferred_element_type=f32)


def split_three(value):
    high = value.astype(bf16)
    rest = value - high.astype(f32)
    mid = rest.astype(bf16)
    return high, mid, (rest - mid.astype(f32)).astype(bf16)


def one_hot(pass_row):
    kinds = lax.broadcasted_iota(jnp.int32, (16, pass_row.shape[1]), 0)
    return (kinds == pass_row).astype(f32).astype(bf16)


def embedded(tokens, pass_row, vec):
    chosen = jnp.concatenate([one_hot(pass_row)] * 3, axis=0)
    return tokens.astype(f32) + tn(chosen, jnp.concatenate(split_three(vec), axis=0))


def hat_of(hidden):
    mean = jnp.mean(hidden, axis=-1, keepdims=True)
    center = hidden - mean
    spread = jnp.mean(center * center, axis=-1, keepdims=True)
    root = lax.rsqrt(spread + norm_eps)
    return center * root, root


def norm_back(hat, root, grad, gain):
    scaled = grad * gain
    first = jnp.mean(scaled, axis=-1, keepdims=True)
    second = jnp.mean(scaled * hat, axis=-1, keepdims=True)
    return root * (scaled - first - hat * second)


def params(mebibytes=56, **kw):
    return pltpu.CompilerParams(vmem_limit_bytes=mebibytes * 1024 * 1024, **kw)


def cost(micros):
    return pl.CostEstimate(flops=int(micros * 1.1e9), bytes_accessed=int(micros * 1e6), transcendentals=0)


def full(shape):
    return pl.BlockSpec(shape, lambda *_: (0,) * len(shape))


def gather_kernel(
    own, vec_own, tokens, passes,
    all_pairs, columns, wo_other, vec_out, norm, q, k_out, v, cat,
    pack, vec_pack, vec_land, wq, tok, norm_s, qkv_s, cat_s, *sems,
):
    (
        s_z1, r_z1, s_x1, r_x1, s_y1, r_y1, s_d1, r_d1, s_l, r_l, s_r, r_r, s_x2, r_x2, s_y2, r_y2, s_v, r_v, s_c, r_c,
        s_out, s_cat, s_tok, loc,
    ) = sems
    dp, t = lax.axis_index("dp"), lax.axis_index("tensor")
    z, x = dp // 2, dp % 2
    y, core = t // 2, t % 2
    far_x, far_y, near = z * 2 + (1 - x), (1 - y) * 2 + core, y * 2 + (1 - core)

    barrier = pltpu.get_barrier_semaphore()
    peers = [lax.rem(dp + n, 8) for n in range(1, 8)]
    for peer in peers:
        pl.semaphore_signal(barrier, inc=1, device_id={"dp": peer}, device_id_type=MESH)
    for to in (far_y, near):
        pl.semaphore_signal(barrier, inc=1, device_id={"tensor": to}, device_id_type=MESH)

    tok_copy = pltpu.make_async_copy(tokens, tok, s_tok)
    tok_copy.start()
    for m in range(3):
        pair = jnp.concatenate([own[0, 2 * m], own[0, 2 * m + 1]], axis=1).astype(bf16)
        pack[m] = pair

        @pl.when(z == 0)
        def _():
            wq[y, 3 * x + m] = pair

    vec_pack[...] = jnp.zeros_like(vec_pack)
    vec_pack[0 : PASSES + 4, 0 : D // 8] = vec_own[...]
    pl.semaphore_wait(barrier, 9)

    started = []

    def send(src, dst, s_sem, r_sem, to, cond=None):
        copy = pltpu.make_async_remote_copy(
            src_ref=src, dst_ref=dst, send_sem=s_sem, recv_sem=r_sem, device_id=to, device_id_type=MESH
        )
        started.append((cond, copy))
        if cond is None:
            copy.start()
        else:
            pl.when(cond)(copy.start)

    def arrived(dst, r_sem, cond=None):
        copy = pltpu.make_async_remote_copy(
            src_ref=dst, dst_ref=dst, send_sem=loc, recv_sem=r_sem, device_id={"dp": far_x}, device_id_type=MESH
        )
        if cond is None:
            copy.wait_recv()
        else:
            pl.when(cond)(copy.wait_recv)

    to_x, to_y, to_left, to_right = {"dp": far_x}, {"tensor": far_y}, {"dp": dp - 2}, {"dp": dp + 2}
    half = SIDE // 2

    def piece(side, column, k):
        return wq.at[side, 3 * column + k // 2, pl.ds((k % 2) * half, half)]

    def at_one(m):
        return all_pairs.at[y, 6 + 3 * x + m]

    def at_z(d, m):
        return columns.at[3 * (z + d - 2) + m]

    own_one = pltpu.make_async_copy(pack, all_pairs.at[y, pl.ds(6 + 3 * x, 3)], loc)
    own_more = pltpu.make_async_copy(pack, columns.at[pl.ds(3 * (z - 2), 3)], loc)
    pl.when(z == 1)(own_one.start)
    pl.when(z > 1)(own_more.start)

    for m in range(3):
        send(pack.at[m], at_one(m), s_l.at[0, m], r_l.at[0, m], to_left, z == 1)
        send(pack.at[m], at_z(0, m), s_l.at[0, m], r_l.at[0, m], to_left, z > 1)
    for n, peer in enumerate(peers):
        send(vec_pack, vec_land.at[dp], s_v.at[n], r_v.at[dp], {"dp": peer})
    send(pack.at[0], at_z(0, 0), s_r.at[0, 0], r_r.at[0, 0], to_right, z == 2)
    send(pack.at[0], at_one(0), s_x2.at[0], r_x2.at[0], to_x, z == 1)

    def diagonal(k):
        if k % 2 == 0:
            arrived(piece(y, 1 - x, k), r_x1.at[k])
            send(piece(y, 1 - x, k), piece(y, 1 - x, k), s_d1.at[k], r_d1.at[k], to_y)
        else:
            arrived(piece(1 - y, x, k), r_y1.at[k])
            send(piece(1 - y, x, k), piece(1 - y, x, k), s_d1.at[k], r_d1.at[k], to_x)

    def from_right(d, m):
        arrived(columns.at[m], r_l.at[d - 1, m], z + d < 4)
        if d < 3:
            send(at_z(d, m), at_z(d, m), s_l.at[d, m], r_l.at[d, m], to_left, (z + d < 4) & (z > 0))

    def along_x(m, cond):
        send(at_one(m), at_one(m), s_x2.at[m], r_x2.at[m], to_x, cond)

    def from_left(d, m):
        arrived(columns.at[m], r_r.at[d - 1, m], z > d)
        if d == 1:
            send(at_one(m), at_one(m), s_r.at[1, m], r_r.at[1, m], to_right, z == 2)
        along_x(m, z == d + 1)

    for k in range(6):
        arrived(piece(y, x, k), r_z1.at[k], z > 0)
        send(piece(y, x, k), piece(y, x, k), s_z1.at[k], r_z1.at[k], to_right, z < 3)
        send(piece(y, x, k), piece(y, x, k), s_x1.at[k], r_x1.at[k], to_x)
        send(piece(y, x, k), piece(y, x, k), s_y1.at[k], r_y1.at[k], to_y)
        if k == 5:
            for m in range(3):
                send(pack.at[m], at_one(m), s_r.at[0, m], r_r.at[0, m], to_right, z == 1)
                if m > 0:
                    send(pack.at[m], at_z(0, m), s_r.at[0, m], r_r.at[0, m], to_right, z == 2)
                    send(pack.at[m], at_one(m), s_x2.at[m], r_x2.at[m], to_x, z == 1)
        if k >= 1:
            diagonal(k - 1)
        if k % 2 == 1:
            from_right(1, k // 2)
    diagonal(5)
    pl.when(z == 1)(own_one.wait)
    pl.when(z > 1)(own_more.wait)
    for m in range(3):
        along_x(m, z == 0)
    for m in range(3):
        from_left(1, m)
        from_right(2, m)
    for k in range(6):
        if k % 2 == 0:
            arrived(piece(1 - y, x, k), r_y1.at[k])
        else:
            arrived(piece(y, 1 - x, k), r_x1.at[k])
        arrived(piece(1 - y, 1 - x, k), r_d1.at[k])
    for peer in peers:
        arrived(vec_land.at[peer], r_v.at[peer])
    vec_land[dp] = vec_pack[...]
    vec = jnp.concatenate([vec_land[d][:, : D // 8] for d in range(8)], axis=1)
    vec_out[...] = vec
    for n in range(3):
        for i in range(4):
            at = (i % 2) * SIDE
            parts = [wq[h, 2 * n + i // 2][:, at : at + SIDE] for h in range(2)]
            cat_s[n, i * SIDE : (i + 1) * SIDE, :] = jnp.concatenate(parts, axis=1)
    writes = [pltpu.make_async_copy(cat_s, cat, s_cat)]
    writes[0].start()
    tok_copy.wait()

    def rows_of(b):
        rows = slice(b * WIDE, (b + 1) * WIDE)
        hat, _ = hat_of(embedded(tok[rows, :], passes[:, rows], vec))
        low = (hat * vec[PASSES : PASSES + 1] + vec[PASSES + 1 : PASSES + 2]).astype(bf16)
        norm_s[rows, :] = low
        writes.append(pltpu.make_async_copy(norm_s.at[rows, :], norm.at[rows, :], s_out.at[b, 3]))
        writes[-1].start()
        for n, out in enumerate((q, k_out, v)):
            qkv_s[n, rows, :] = nn(low, cat_s[n]).astype(bf16)
            writes.append(pltpu.make_async_copy(qkv_s.at[n, rows, :], out.at[rows, :], s_out.at[b, n]))
            writes[-1].start()

    count = tok.shape[0] // WIDE
    for b in range(count):
        rows_of(b)
        if b == 0:
            for m in range(3):
                from_left(2, m)
                from_right(3, m)
        if b == 1:
            for m in range(2):
                ref = all_pairs.at[y, 6 + m]
                arrived(ref, r_x2.at[m], x == 1)
                send(ref, ref, s_y2.at[m], r_y2.at[m], to_y)
                send(ref, wo_other.at[y, m], s_c.at[0, m], r_c.at[y, m], {"tensor": near})
    for m in range(2):
        ref = all_pairs.at[1 - y, 6 + m]
        arrived(ref, r_y2.at[m])
        send(ref, wo_other.at[1 - y, m], s_c.at[1, m], r_c.at[1 - y, m], {"tensor": near})
    for m in range(3):
        arrived(all_pairs.at[y, 6 + 3 * (1 - x) + m], r_x2.at[m], None if m == 2 else x == 0)
    for h in range(2):
        for m in range(2):
            arrived(wo_other.at[h, m], r_c.at[h, m])
    for copy in writes:
        copy.wait()
    for cond, copy in started:
        if cond is None:
            copy.wait_send()
        else:
            pl.when(cond)(copy.wait_send)


def gather(block_weights, vector_params, tokens, passes):
    seq = tokens.shape[0]
    dma = pltpu.SemaphoreType.DMA
    sizes = [(6,)] * 8 + [(3, 3)] * 2 + [(2, 3)] * 2 + [(3,)] * 2 + [(2,)] * 2 + [(7,), (8,)] + [(2, 2)] * 2
    sizes += [(seq // WIDE, 4)]
    vmem, far = pl.BlockSpec(memory_space=pltpu.VMEM), pl.BlockSpec(memory_space=pl.ANY)
    wide = jax.ShapeDtypeStruct((seq, PAIR), bf16)
    return pl.pallas_call(
        gather_kernel,
        in_specs=[vmem, vmem, far, vmem],
        out_specs=[far, far, far, vmem, far, far, far, far, far],
        out_shape=[
            jax.ShapeDtypeStruct((2, 24, SIDE, PAIR), bf16),
            jax.ShapeDtypeStruct((6, SIDE, PAIR), bf16),
            jax.ShapeDtypeStruct((2, 2, SIDE, PAIR), bf16),
            jax.ShapeDtypeStruct((16, D), f32),
            jax.ShapeDtypeStruct((seq, D), bf16),
            wide,
            wide,
            wide,
            jax.ShapeDtypeStruct((3, D, PAIR), bf16),
        ],
        scratch_shapes=[
            pltpu.VMEM((3, SIDE, PAIR), bf16),
            pltpu.VMEM((16, 128), f32),
            pltpu.VMEM((8, 16, 128), f32),
            pltpu.VMEM((2, 6, SIDE, PAIR), bf16),
            pltpu.VMEM((seq, D), bf16),
            pltpu.VMEM((seq, D), bf16),
            pltpu.VMEM((3, seq, PAIR), bf16),
            pltpu.VMEM((3, D, PAIR), bf16),
        ]
        + [dma(size) for size in sizes]
        + [dma] * 3,
        compiler_params=params(collective_id=0, has_side_effects=True),
        cost_estimate=cost(60),
        name="gather",
    )(block_weights, vector_params, tokens, passes)


def project_kernel(tok, pas, vec, wq, norm, q, k, v, cat):
    @pl.when(pl.program_id(0) == 0)
    def _():
        for x in range(3):
            for i in range(4):
                at = (i % 2) * SIDE
                parts = [wq[h, 2 * x + i // 2][:, at : at + SIDE] for h in range(2)]
                cat[x, i * SIDE : (i + 1) * SIDE, :] = jnp.concatenate(parts, axis=1)

    first = embedded(tok[...], pas[...], vec[...])
    hat, _ = hat_of(first)
    low = (hat * vec[PASSES : PASSES + 1] + vec[PASSES + 1 : PASSES + 2]).astype(bf16)
    norm[...] = low
    for x, out in enumerate((q, k, v)):
        out[...] = nn(low, cat[x]).astype(bf16)


def project(tokens, passes, vec, wq):
    seq = tokens.shape[0]
    row = lambda n: pl.BlockSpec((WIDE, n), lambda i: (i, 0))
    wide = jax.ShapeDtypeStruct((seq, PAIR), bf16)
    return pl.pallas_call(
        project_kernel,
        grid=(seq // WIDE,),
        in_specs=[
            row(D),
            pl.BlockSpec((1, WIDE), lambda i: (0, i)),
            full((16, D)),
            full((2, 6, SIDE, PAIR)),
        ],
        out_specs=[row(D), row(PAIR), row(PAIR), row(PAIR), full((3, D, PAIR))],
        out_shape=[
            jax.ShapeDtypeStruct((seq, D), bf16),
            wide,
            wide,
            wide,
            jax.ShapeDtypeStruct((3, D, PAIR), bf16),
        ],
        compiler_params=params(),
        cost_estimate=cost(16),
        name="project",
    )(tokens, passes, vec, wq)


def doc_state(lens, base):
    rows = base + lax.broadcasted_iota(jnp.int32, (1, ROWS), 1)
    rows = jnp.concatenate([rows, rows], axis=1)
    begin = jnp.int32(0)
    first = jnp.int32(0)
    starts = jnp.zeros((1, 2 * ROWS), jnp.int32)
    for c in range(DOCS):
        starts = jnp.where(rows >= begin, begin, starts)
        first = jnp.where(base >= begin, begin, first)
        begin = begin + lens[c]
    return rows, starts, first


def two_heads(block):
    left = lax.broadcasted_iota(jnp.int32, block.shape, 1) < HD
    none = jnp.zeros_like(block)
    return jnp.concatenate([jnp.where(left, block, none), jnp.where(left, none, block)], axis=0)


def one_above(both):
    return jnp.concatenate([both[:HD, :ROWS], both[HD:, ROWS:]], axis=0).T


def attend_kernel(lens, q, k, v, out, lse, acc):
    i = pl.program_id(0)
    base = i * ROWS
    rows, starts, first = doc_state(lens, base)
    pairs = [two_heads(q[:, p * 128 : (p + 1) * 128] * bf16(0.125)) for p in range(3)]
    for p in range(3):
        acc[p] = jnp.zeros((128, 2 * ROWS), f32)

    def step(j, carry):
        at = pl.multiple_of(j * ROWS, ROWS)
        keys = at + lax.broadcasted_iota(jnp.int32, (ROWS, 2 * ROWS), 0)
        seen = (keys >= starts) & (keys <= rows)
        here = pl.ds(at, ROWS)
        head = lambda p: slice(p * 128, (p + 1) * 128)
        scores = [jnp.where(seen, nt(k[here, head(p)], pairs[p]), masked_score) for p in range(3)]
        state = []
        for p in range(3):
            before, total = carry[2 * p], carry[2 * p + 1]
            now = jnp.maximum(before, jnp.max(scores[p], axis=0, keepdims=True))
            probs = jnp.exp(scores[p] - now)
            fade = jnp.exp(before - now)
            state += [now, total * fade + jnp.sum(probs, axis=0, keepdims=True)]
            acc[p] = acc[p] * fade + tn(v[here, head(p)], probs.astype(bf16))
        return tuple(state)

    zero = jnp.zeros((1, 2 * ROWS), f32)
    state = lax.fori_loop(first // ROWS, i + 1, step, (zero + masked_score, zero) * 3)
    lines = []
    for p in range(3):
        top, total = state[2 * p], state[2 * p + 1]
        out[:, p * 128 : (p + 1) * 128] = one_above(acc[p] / total).astype(bf16)
        line = top + jnp.log(total)
        lines += [line[:, :ROWS], line[:, ROWS:]]
    lse[...] = jnp.concatenate(lines + lines[:2], axis=0)


def attend(lens, q, k, v):
    seq = q.shape[0]
    row = pl.BlockSpec((ROWS, PAIR), lambda i, s: (i, 0))
    return pl.pallas_call(
        attend_kernel,
        grid_spec=pltpu.PrefetchScalarGridSpec(
            num_scalar_prefetch=1,
            grid=(seq // ROWS,),
            in_specs=[row, full((seq, PAIR)), full((seq, PAIR))],
            out_specs=[row, pl.BlockSpec((8, ROWS), lambda i, s: (0, i))],
            scratch_shapes=[
                pltpu.VMEM((3, 128, 2 * ROWS), f32),
            ],
        ),
        out_shape=[
            jax.ShapeDtypeStruct((seq, PAIR), bf16),
            jax.ShapeDtypeStruct((8, seq), f32),
        ],
        compiler_params=params(),
        cost_estimate=cost(30),
        name="attend",
    )(lens, q, k, v)


def attend_back_kernel(
    lens, q, k, v, mixed, lse, grad_mixed, dq, dk, dv, dk_acc, dv_acc, dq_acc
):
    i = pl.program_id(0)
    count = pl.num_programs(0)
    base = i * ROWS

    @pl.when(i == 0)
    def _():
        dk_acc[...] = jnp.zeros_like(dk_acc)
        dv_acc[...] = jnp.zeros_like(dv_acc)

    rows, starts, first = doc_state(lens, base)
    heads = lax.broadcasted_iota(jnp.int32, (8, 128), 0)
    lanes = lax.broadcasted_iota(jnp.int32, (8, 128), 1)
    pick = (lanes // HD == heads).astype(f32).astype(bf16)
    queries, grads, inner, lines = [], [], [], []
    for p in range(3):
        cols = slice(p * 128, (p + 1) * 128)
        queries.append(two_heads(q[:, cols] * bf16(0.125)))
        grads.append(two_heads(grad_mixed[:, cols]))
        product = grad_mixed[:, cols].astype(f32) * mixed[:, cols].astype(f32)
        high, low, _ = split_three(product)
        sums = nt(pick, high) + nt(pick, low)
        inner.append(jnp.concatenate([sums[0:1], sums[1:2]], axis=1))
        lines.append(jnp.concatenate([lse[2 * p : 2 * p + 1], lse[2 * p + 1 : 2 * p + 2]], axis=1))
        dq_acc[p] = jnp.zeros((128, 2 * ROWS), f32)

    def step(j, carry):
        at = pl.multiple_of(j * ROWS, ROWS)
        keys = at + lax.broadcasted_iota(jnp.int32, (ROWS, 2 * ROWS), 0)
        seen = (keys >= starts) & (keys <= rows)
        here = pl.ds(at, ROWS)
        for p in range(3):
            cols = slice(p * 128, (p + 1) * 128)
            kb = k[here, cols]
            scores = jnp.where(seen, nt(kb, queries[p]) - lines[p], masked_score)
            probs = jnp.exp(scores)
            grad_probs = nt(v[here, cols], grads[p])
            grad_scores = (probs * (grad_probs - inner[p])).astype(bf16)
            dv_acc[here, cols] += nn(probs.astype(bf16), grads[p])
            dk_acc[here, cols] += nn(grad_scores, queries[p])
            dq_acc[p] += tn(kb, grad_scores)
        return carry

    lax.fori_loop(first // ROWS, i + 1, step, 0)
    for p in range(3):
        dq[:, p * 128 : (p + 1) * 128] = (one_above(dq_acc[p]) * 0.125).astype(bf16)

    @pl.when(i == count - 1)
    def _():
        dk[...] = dk_acc[...].astype(bf16)
        dv[...] = dv_acc[...].astype(bf16)


def attend_back(lens, q, k, v, mixed, lse, grad_mixed):
    seq = q.shape[0]
    count = seq // ROWS
    row = pl.BlockSpec((ROWS, PAIR), lambda i, s: (i, 0))
    wide = jax.ShapeDtypeStruct((seq, PAIR), bf16)
    return pl.pallas_call(
        attend_back_kernel,
        grid_spec=pltpu.PrefetchScalarGridSpec(
            num_scalar_prefetch=1,
            grid=(count,),
            in_specs=[
                row,
                full((seq, PAIR)),
                full((seq, PAIR)),
                row,
                pl.BlockSpec((8, ROWS), lambda i, s: (0, i)),
                row,
            ],
            out_specs=[row, full((seq, PAIR)), full((seq, PAIR))],
            scratch_shapes=[
                pltpu.VMEM((seq, PAIR), f32),
                pltpu.VMEM((seq, PAIR), f32),
                pltpu.VMEM((3, 128, 2 * ROWS), f32),
            ],
        ),
        out_shape=[wide, wide, wide],
        compiler_params=params(),
        cost_estimate=cost(40),
        name="attend_back",
    )(lens, q, k, v, mixed, lse, grad_mixed)


def feed_kernel(
    small, tok, pas, vec, mine, cot, wo_mine, wo_other, four, columns, columns_x,
    out_chip, second_keep, grad_second, grad_mixed, sums, mid_send, mid_keep, *rest,
):
    results, rest = (rest[:4], rest[4:]) if small else (rest[:2], rest[2:])
    (
        wo, other, up, down, gup, gdown, go, core_out, core_in, far_out, far_in, ga_out, ga_in, oc_out, oc_in,
        g_send, g_keep, g_in, s_core, r_core, s_far, r_far, s_ga, r_ga, s_oc, r_oc, s_x, r_x, s_m, r_m,
    ) = rest
    step = pl.program_id(0)
    half = core_out.shape[0]
    t, dp = lax.axis_index("tensor"), lax.axis_index("dp")
    core, side = t % 2, t // 2
    near, far = side * 2 + (1 - core), (1 - side) * 2 + core
    z, column = (dp // 2, dp % 2) if small else (0, 0)
    far_x = z * 2 + 1 - column

    def copy(src, dst, s_sem, r_sem, j, to):
        return pltpu.make_async_remote_copy(
            src_ref=src.at[j],
            dst_ref=dst.at[j],
            send_sem=s_sem.at[j],
            recv_sem=r_sem.at[j],
            device_id={"tensor": to},
            device_id_type=MESH,
        )

    core_copy = lambda j: copy(core_out, core_in, s_core, r_core, j, near)
    far_copy = lambda j: copy(far_out, far_in, s_far, r_far, j, far)
    ga_copy = lambda j: copy(ga_out, ga_in, s_ga, r_ga, j, near)
    oc_copy = lambda j: copy(oc_out, oc_in, s_oc, r_oc, j, near)

    def x_copy(slot):
        return pltpu.make_async_remote_copy(
            src_ref=g_send.at[slot],
            dst_ref=g_in.at[slot],
            send_sem=s_x.at[slot],
            recv_sem=r_x.at[slot],
            device_id={"dp": far_x},
            device_id_type=MESH,
        )

    def mixed_copy(block):
        rows = pl.ds(pl.multiple_of(block * ROWS, ROWS), ROWS)
        return pltpu.make_async_remote_copy(
            src_ref=mine.at[rows],
            dst_ref=other.at[rows],
            send_sem=s_m.at[block],
            recv_sem=r_m.at[block],
            device_id={"tensor": near},
            device_id_type=MESH,
        )

    barrier = pltpu.get_barrier_semaphore()

    @pl.when(step == 0)
    def _():
        for to in (near, far):
            pl.semaphore_signal(barrier, inc=1, device_id={"tensor": to}, device_id_type=MESH)
        if small:
            pl.semaphore_signal(barrier, inc=1, device_id={"dp": far_x}, device_id_type=MESH)
        for h in range(2):
            for m in range(2):
                rows, cols = slice(h * SIDE, (h + 1) * SIDE), slice(m * PAIR, (m + 1) * PAIR)
                wo[rows, cols] = wo_mine[h, m]
                wo[PAIR + h * SIDE : PAIR + (h + 1) * SIDE, cols] = wo_other[h, m]
        for r in range(4):
            for m in range(2):
                rows, cols = slice(r * SIDE, (r + 1) * SIDE), slice(m * PAIR, (m + 1) * PAIR)
                for at, weight in ((8, up), (16, down)):
                    pair = at + 2 * r + m
                    if pair < 12:
                        weight[rows, cols] = four[0, pair - 8]
                        continue
                    n = (pair // 6 - 2) * 3 + pair % 3
                    for source, here in ((columns, pair // 3 % 2), (columns_x, 1 - pair // 3 % 2)):

                        @pl.when(column == here)
                        def _():
                            weight[rows, cols] = source[n]

        pl.semaphore_wait(barrier, 3 if small else 2)
        for j in range(half):
            mixed_copy(core * half + j).start()
            mixed_copy((1 - core) * half + j).start()
        gup[...] = jnp.zeros_like(gup)
        gdown[...] = jnp.zeros_like(gdown)
        go[...] = jnp.zeros_like(go)
        sums[...] = jnp.zeros_like(sums)

    @pl.when(step < 2 * half)
    def _():
        j = step // 2
        owner = jnp.where(step % 2 == 0, 1 - core, core)
        here = pl.ds(pl.multiple_of((owner * half + j) * ROWS, ROWS), ROWS)
        first = embedded(tok[...], pas[...], vec[...])
        mixed_copy(owner * half + j).wait_recv()
        second = first + nn(jnp.concatenate([mine[here, :], other[here, :]], axis=1), wo[...])
        hat, _ = hat_of(second)
        low = (hat * vec[PASSES + 2 : PASSES + 3] + vec[PASSES + 3 : PASSES + 4]).astype(bf16)
        upper = nn(low, up[...])
        square = upper * upper
        bent = jnp.tanh(gelu_coef * upper * (1.0 + 0.044715 * square))
        act = (0.5 * upper * (1.0 + bent)).astype(bf16)
        slope = 0.5 * (1.0 + bent) + (0.5 * gelu_coef) * upper * (1.0 - bent * bent) * (
            1.0 + (3 * 0.044715) * square
        )
        grad_act = nt(cot[...], down[...])
        grad_upper = (grad_act * slope).astype(bf16)
        part = nt(grad_upper, up[...])

        @pl.when(step % 2 == 0)
        def _():
            core_out[j] = part.astype(bf16)
            core_copy(j).start()

        @pl.when(step % 2 == 1)
        def _():
            core_copy(j).wait_recv()
            far_out[j] = (part + core_in[j].astype(f32)).astype(bf16)
            far_copy(j).start()
            second_keep[pl.ds(pl.multiple_of(j * ROWS, ROWS), ROWS), :] = second

        gup[...] += tn(low, grad_upper)
        gdown[...] += tn(act, cot[...])
        out_part = nn(act, down[...])

        @pl.when(step % 2 == 0)
        def _():
            oc_out[j] = out_part.astype(bf16)
            oc_copy(j).start()

        @pl.when(step % 2 == 1)
        def _():
            oc_copy(j).wait_recv()
            out_chip[...] = (out_part + oc_in[j].astype(f32)).astype(bf16)

    @pl.when(step == 2 * half - 1)
    def _():
        for r in range(4):
            for m in range(2):
                rows, cols = slice(r * SIDE, (r + 1) * SIDE), slice(m * PAIR, (m + 1) * PAIR)
                for at, total in ((8, gup), (16, gdown)):
                    pair = at + 2 * r + m
                    slot, place = (pair // 6 - 1) * 3 + pair % 3, pair // 3 % 2
                    value = total[rows, cols].astype(bf16)
                    kept, sent, n = (mid_keep, mid_send, slot) if slot < 6 else (g_keep, g_send, slot - 6)

                    @pl.when(column == place)
                    def _():
                        kept[n] = value

                    @pl.when(column != place)
                    def _():
                        sent[n] = value
        if small:
            for n in range(3):
                x_copy(n).start()

    def through_out(grad, block):
        here = pl.ds(pl.multiple_of(block * ROWS, ROWS), ROWS)
        grad_mixed[here, :] = nt(grad, wo[:PAIR, :]).astype(bf16)
        go[...] += tn(mine[here, :], grad)

    @pl.when((step >= 2 * half) & (step < 3 * half))
    def _():
        j = step - 2 * half
        hat, root = hat_of(second_keep[pl.ds(pl.multiple_of(j * ROWS, ROWS), ROWS), :])
        far_copy(j).wait_recv()
        grad = far_out[j].astype(f32) + far_in[j].astype(f32)
        result = cot[...].astype(f32) + norm_back(hat, root, grad, vec[PASSES + 2 : PASSES + 3])
        low = result.astype(bf16)
        ga_out[j] = low
        ga_copy(j).start()
        grad_second[...] = result
        sums[0:1] += jnp.sum(grad * hat, axis=0, keepdims=True)
        sums[1:2] += jnp.sum(grad, axis=0, keepdims=True)
        through_out(low, core * half + j)

    @pl.when(step > 2 * half)
    def _():
        j = step - 2 * half - 1
        ga_copy(j).wait_recv()
        through_out(ga_in[j], (1 - core) * half + j)

    @pl.when(step == 3 * half)
    def _():
        at = pl.multiple_of(side * SIDE, SIDE)
        for m in range(2):
            value = go[pl.ds(at, SIDE), m * PAIR : (m + 1) * PAIR].astype(bf16)

            @pl.when(column == 0)
            def _():
                mid_keep[m] = value

            @pl.when(column != 0)
            def _():
                mid_send[m] = value

        for j in range(half):
            core_copy(j).wait_send()
            oc_copy(j).wait_send()
            mixed_copy(j).wait_send()
            mixed_copy(half + j).wait_send()
            far_copy(j).wait_send()
            ga_copy(j).wait_send()
        if small:
            for n in range(3):
                x_copy(n).wait_send()
                x_copy(n).wait_recv()
                value = (g_keep[n].astype(f32) + g_in[n].astype(f32)).astype(bf16)
                for turn in range(4):

                    @pl.when(z + turn == 3)
                    def _():
                        results[turn][n] = value
        else:
            results[0][...] = g_send[...]
            results[1][...] = g_keep[...]


def feed(small, tokens, passes, vec, mine, cotangent, pairs, wo_other, columns, columns_x):
    seq = tokens.shape[0]
    half = seq // ROWS // 2

    def block(i):
        core = lax.axis_index("tensor") % 2
        work = jnp.minimum(i, 2 * half - 1)
        owner = jnp.where(work % 2 == 0, 1 - core, core)
        return owner * half + work // 2

    def cot_block(i):
        core = lax.axis_index("tensor") % 2
        return jnp.where(i < 2 * half, block(i), core * half + jnp.minimum(i - 2 * half, half - 1))

    side = lambda: lax.axis_index("tensor") // 2
    row = lambda n: pl.BlockSpec((ROWS, n), lambda i: (block(i), 0))
    keep = pl.BlockSpec((ROWS, D), lambda i: (jnp.minimum(i // 2, half - 1), 0))
    last = pl.BlockSpec((ROWS, D), lambda i: (jnp.clip(i - 2 * half, 0, half - 1), 0))
    rows = lambda kind: jax.ShapeDtypeStruct((seq // 2, D), kind)
    gr = lambda n: jax.ShapeDtypeStruct((n, SIDE, PAIR), bf16)
    ends = [(3, SIDE, PAIR)] * (4 if small else 2)
    buffer = pltpu.VMEM((half, ROWS, D), bf16)
    dma = pltpu.SemaphoreType.DMA((half,))
    return pl.pallas_call(
        functools.partial(feed_kernel, small),
        grid=(3 * half + 1,),
        in_specs=[
            row(D),
            pl.BlockSpec((1, ROWS), lambda i: (0, block(i))),
            full((16, D)),
            full((seq, PAIR)),
            pl.BlockSpec((ROWS, D), lambda i: (cot_block(i), 0)),
            pl.BlockSpec((2, 2, SIDE, PAIR), lambda i: (0, 3, 0, 0)),
            full(wo_other.shape),
            pl.BlockSpec((1, 4, SIDE, PAIR), lambda i: (side(), 2, 0, 0)),
            full(columns.shape),
            full(columns.shape),
        ],
        out_specs=[
            keep,
            full((seq // 2, D)),
            last,
            full((seq, PAIR)),
            full((8, D)),
            full((6, SIDE, PAIR)),
            full((6, SIDE, PAIR)),
        ]
        + [full(shape) for shape in ends],
        scratch_shapes=[
            pltpu.VMEM((D, D), bf16),
            pltpu.VMEM((seq, PAIR), bf16),
            pltpu.VMEM((D, D), bf16),
            pltpu.VMEM((D, D), bf16),
            pltpu.VMEM((D, D), f32),
            pltpu.VMEM((D, D), f32),
            pltpu.VMEM((PAIR, D), f32),
        ]
        + [buffer] * 8
        + [pltpu.VMEM((3, SIDE, PAIR), bf16)] * 3
        + [dma] * 8
        + [pltpu.SemaphoreType.DMA((3,))] * 2
        + [pltpu.SemaphoreType.DMA((2 * half,))] * 2,
        out_shape=[
            rows(bf16),
            rows(f32),
            rows(f32),
            jax.ShapeDtypeStruct((seq, PAIR), bf16),
            jax.ShapeDtypeStruct((8, D), f32),
            gr(6),
            gr(6),
        ]
        + [jax.ShapeDtypeStruct(shape, bf16) for shape in ends],
        compiler_params=params(collective_id=1, has_side_effects=True),
        cost_estimate=cost(50),
        name="feed_forward",
    )(tokens, passes, vec, mine, cotangent, pairs, wo_other, pairs, columns, columns_x)


CHUNK = SIDE // 2
CHUNKS = 18
TAKEN = (
    ((8, 3), (10, 4), (12, 12)),
    ((3, 1), (5, 2), (7, 3), (8, 4), (9, 6), (10, 7), (11, 8), (12, 12)),
    ((1, 2), (2, 3), (5, 4), (6, 5), (7, 6), (8, 8), (9, 9), (10, 11), (12, 12)),
    ((-1, 3), (2, 5), (4, 6), (5, 7), (6, 8), (7, 12)),
)
GRAD_STEPS = 3


def last_kernel(
    small, norm_all, dq_all, dk_all, dv_all, cat, tok, pas, vec, grad_second, sums_two, second, chip, far,
    mid_near, mid_keep, output, input_grad, *rest,
):
    if small:
        late, vec_sum = rest[:2]
        rest = rest[2:]
        (
            core_out, core_in, sums, core_sums, x_in, z_in, z_out, up_in, v_out, v_in, total,
            s_core, r_core, s_sum, r_sum, s_x, r_x, s_z, r_z, s_up, r_up, s_v, r_v, ready, norm, dq, dk, dv, g_send, g_keep,
            s_own, s_res, r_res, s_in,
        ) = rest
    else:
        (
            vec_sum, send_out, keep_out, core_out, core_in, sums, core_sums, s_core, r_core, s_sum, r_sum, ready,
            norm, dq, dk, dv, g_send, g_keep, s_own, s_res, r_res, s_in,
        ) = rest
    step = pl.program_id(0)
    i = step - GRAD_STEPS
    half = core_out.shape[0]
    t, dp = lax.axis_index("tensor"), lax.axis_index("dp")
    core, side = t % 2, t // 2
    near = side * 2 + (1 - core)
    z, column = (dp // 2, dp % 2) if small else (0, 0)
    far_x = z * 2 + 1 - column
    peers = [lax.rem(dp + k, 8) for k in range(1, 8)]

    def copy(src, dst, s_sem, r_sem, to):
        return pltpu.make_async_remote_copy(
            src_ref=src, dst_ref=dst, send_sem=s_sem, recv_sem=r_sem, device_id=to, device_id_type=MESH
        )

    core_copy = lambda j: copy(core_out.at[j], core_in.at[j], s_core.at[j], r_core.at[j], {"tensor": near})
    sum_copy = lambda: copy(sums, core_sums, s_sum, r_sum, {"tensor": near})

    def rows_at(n, j, owner):
        rows = pl.ds(pl.multiple_of((owner * half + j) * ROWS, ROWS), ROWS)
        return (output, input_grad)[n].at[rows]

    own_result = lambda n, j: pltpu.make_async_copy(ready.at[n, j], rows_at(n, j, core), s_own.at[n, j])
    near_result = lambda n, j, owner: copy(
        ready.at[n, j], rows_at(n, j, owner), s_res.at[n, j], r_res.at[n, j], {"tensor": near}
    )

    def part_of(ref, k):
        return ref.at[k // 2, pl.ds((k % 2) * CHUNK, CHUNK)]

    x_copy = lambda k: copy(part_of(g_send, k), x_in.at[k], s_x.at[k], r_x.at[k], {"dp": far_x})
    z_copy = lambda k: copy(z_out.at[k], z_in.at[k], s_z.at[k], r_z.at[k], {"dp": dp - 2})
    up_copy = lambda k: copy(z_out.at[k], up_in.at[k - 6], s_up.at[k - 6], r_up.at[k - 6], {"dp": dp + 2})
    v_copy = lambda n: copy(v_out.at[peers[n]], v_in.at[dp], s_v.at[n], r_v.at[dp], {"dp": peers[n]})
    barrier = pltpu.get_barrier_semaphore()

    loads = [
        pltpu.make_async_copy(src, dst, s_in.at[n])
        for n, (src, dst) in enumerate(((norm_all, norm), (dq_all, dq), (dv_all, dv), (dk_all, dk)))
    ]

    @pl.when(step == 0)
    def _():
        for load in loads:
            load.start()
        pl.semaphore_signal(barrier, inc=1, device_id={"tensor": near}, device_id_type=MESH)
        if small:
            for peer in peers:
                pl.semaphore_signal(barrier, inc=1, device_id={"dp": peer}, device_id_type=MESH)
            late[...] = jnp.zeros_like(late)
        sums[...] = jnp.zeros_like(sums)
        sums[PASSES + 2 : PASSES + 4] = sums_two[0:2]
        pl.semaphore_wait(barrier, 8 if small else 1)

    if small:

        def term_of(k):
            rows = pl.ds(pl.multiple_of((k % 2) * CHUNK, 16), CHUNK)

            @pl.when(jnp.asarray(k) < 6)
            def _():
                x_copy(k).wait_recv()
                total[...] = g_keep[k // 2, rows, :].astype(f32) + x_in[k].astype(f32)

            @pl.when(jnp.asarray(k) >= 6)
            def _():
                total[...] = mid_keep[k // 2 - 3, rows, :].astype(f32) + mid_near[k // 2 - 3, rows, :].astype(f32)

            return total[...]

        @pl.when((step == 0) & (z == 3))
        def _():
            for k in (6, 7, 8, 12, 13):
                z_out[k] = term_of(k).astype(bf16)
                z_copy(k).start()

    def mine_of(grad):
        return jnp.where(side == 0, grad[:, :SIDE], grad[:, SIDE:])

    def pairs_of(grad):
        value = tn(grad, norm[...]).astype(bf16)
        return value[:, :PAIR], value[:, PAIR:]

    second_two = jnp.where(jnp.asarray(column) == 0, 1, 0)

    @pl.when(step == 0)
    def _():
        for load in loads[:3]:
            load.wait()
        both = pairs_of(jnp.where(jnp.asarray(column) == 0, mine_of(dv), mine_of(dq)))
        for m in range(2):
            g_send[second_two + m] = both[m]
        if small:
            for m in range(4):
                x_copy(2 * second_two + m).start()

    @pl.when(step == 1)
    def _():
        loads[3].wait()
        both = pairs_of(mine_of(dk))
        for place, (kept, sent) in enumerate(((0, 1), (1, 0))):

            @pl.when(jnp.asarray(column) == place)
            def _():
                g_keep[2 - 2 * place] = both[kept]
                g_send[2 * place] = both[sent]

        if small:
            for m in range(2):
                x_copy(4 * column + m).start()

    @pl.when(step == 2)
    def _():
        both = pairs_of(jnp.where(jnp.asarray(column) == 0, mine_of(dq), mine_of(dv)))
        for m in range(2):
            g_keep[1 - second_two + m] = both[m]
        if not small:
            send_out[...] = g_send[...]
            keep_out[...] = g_keep[...]

    @pl.when((i >= 0) & (i < 2 * half))
    def _():
        block = lax.rem(i + (1 - core) * half, 2 * half)
        rows = pl.ds(pl.multiple_of(block * ROWS, ROWS), ROWS)
        part = nt(dq[rows, :], cat[0]) + nt(dk[rows, :], cat[1]) + nt(dv[rows, :], cat[2])

        @pl.when(i < half)
        def _():
            core_out[i] = part.astype(bf16)
            core_copy(i).start()

        @pl.when(i >= half)
        def _():
            j = i - half
            hat, root = hat_of(embedded(tok[...], pas[...], vec[...]))
            core_copy(j).wait_recv()
            grad = part + core_in[j].astype(f32)
            result = grad_second[...] + norm_back(hat, root, grad, vec[PASSES : PASSES + 1])
            ready[0, j] = (second[...] + (chip[...].astype(f32) + far[...].astype(f32))).astype(bf16)
            ready[1, j] = result.astype(bf16)
            for n in range(2):
                own_result(n, j).start()
                near_result(n, j, core).start()
            chosen = one_hot(pas[...])
            high, mid, _ = split_three(result)
            sums[...] += nn(chosen, high) + nn(chosen, mid)
            sums[PASSES : PASSES + 1] += jnp.sum(grad * hat, axis=0, keepdims=True)
            sums[PASSES + 1 : PASSES + 2] += jnp.sum(grad, axis=0, keepdims=True)

    @pl.when(i == 2 * half - 1)
    def _():
        sum_copy().start()

    if small:

        def keep_late(k, pair, total):
            late[pair, pl.ds(pl.multiple_of((k % 2) * CHUNK, 16), CHUNK), :] = total

        def pass_on(k):
            term = term_of(k)

            @pl.when(z < 3)
            def _():
                z_copy(k).wait_recv()

            below = jnp.where(z < 3, z_in[k].astype(f32), 0.0)
            passed = term + below

            @pl.when((z > 1) | ((z == 1) & (k < 6)))
            def _():
                z_out[k] = passed.astype(bf16)
                z_copy(k).start()

            @pl.when(z == 0)
            def _():
                keep_late(k, k // 2, passed)

            @pl.when((z == 1) & (k >= 6))
            def _():
                up_copy(k).wait_recv()
                keep_late(k, k // 2 - 3, passed + up_in[k - 6].astype(f32))

        def at_position(p, carry):
            k = jnp.where(p < 3, p + 6, jnp.where(p < 9, lax.rem(p + 3 + 2 * column, 6), p))

            @pl.when((z > 0) | (k < 6))
            def _():
                pass_on(k)

            return carry

        begin, end = jnp.int32(0), jnp.int32(0)
        for place, line in enumerate(TAKEN):
            for at, upto in line:
                begin = jnp.where((z == place) & (step > at), upto, begin)
                end = jnp.where((z == place) & (step >= at), upto, end)
        lax.fori_loop(begin, end, at_position, 0)

        @pl.when((step == 0) & (z == 0))
        def _():
            for k in range(6, CHUNKS):
                z_out[k] = term_of(k).astype(bf16)
                up_copy(k).start()

        @pl.when((step == 7) & (z == 3))
        def _():
            for k in range(14, CHUNKS):
                z_out[k] = term_of(k).astype(bf16)
                z_copy(k).start()

        for at, first_chunk, upto in ((10, 12, 16), (11, 16, 18)):

            @pl.when((step == at) & (z == 1))
            def _(first_chunk=first_chunk, upto=upto):
                for k in range(first_chunk, upto):
                    up_copy(k).wait_recv()
                    z_out[k] = (term_of(k) + up_in[k - 6].astype(f32)).astype(bf16)
                    up_copy(k).start()

        @pl.when((step == pl.num_programs(0) - 1) & (z == 2))
        def _():
            for k in range(12, CHUNKS):
                z_copy(k).wait_recv()
                up_copy(k).wait_recv()
                keep_late(k, k // 2 - 6, term_of(k) + z_in[k].astype(f32) + up_in[k - 6].astype(f32))

    @pl.when(i == 2 * half)
    def _():
        sum_copy().wait_recv()
        total = sums[...] + core_sums[...]
        if small:
            wide = D // 8
            for d in range(8):
                v_out[d, :, 0:wide] = total[:, d * wide : (d + 1) * wide]
                v_out[d, :, wide:] = jnp.zeros((16, 128 - wide), f32)
            for n in range(7):
                v_copy(n).start()
        else:
            vec_sum[...] = total

    @pl.when(step == pl.num_programs(0) - 1)
    def _():
        for j in range(half):
            core_copy(j).wait_send()
            for n in range(2):
                own_result(n, j).wait()
                near_result(n, j, core).wait_send()
                near_result(n, j, 1 - core).wait_recv()
        sum_copy().wait_send()
        if small:
            for peer in peers:
                copy(v_out.at[0], v_in.at[peer], s_v.at[0], r_v.at[peer], {"dp": far_x}).wait_recv()
            v_in[dp] = v_out[dp]
            total = v_in[0]
            for d in range(1, 8):
                total = total + v_in[d]
            vec_sum[...] = total
            for n in range(7):
                v_copy(n).wait_send()
            for k in range(CHUNKS):
                if k < 6:
                    x_copy(k).wait_send()
                    pl.when(z > 0)(z_copy(k).wait_send)
                elif k < 12:
                    pl.when(z > 1)(z_copy(k).wait_send)
                    pl.when(z == 0)(up_copy(k).wait_send)
                else:
                    pl.when(z == 3)(z_copy(k).wait_send)
                    pl.when(z < 2)(up_copy(k).wait_send)


def last(
    small, norm, dq, dk, dv, cat, tokens, passes, vec, grad_second, sums_two, second, chip, far, mid_near, mid_keep
):
    seq = dq.shape[0]
    half = seq // ROWS // 2
    core = lambda: lax.axis_index("tensor") % 2

    own = lambda i: jnp.clip(i - GRAD_STEPS - half, 0, half - 1)
    mine = pl.BlockSpec((ROWS, D), lambda i: (own(i), 0))
    dma = pltpu.SemaphoreType.DMA
    out_specs = [pl.BlockSpec(memory_space=pl.ANY)] * 2
    out_shape = [jax.ShapeDtypeStruct((seq, D), bf16)] * 2
    scratch = [
        pltpu.VMEM((half, ROWS, D), bf16),
        pltpu.VMEM((half, ROWS, D), bf16),
        pltpu.VMEM((16, D), f32),
        pltpu.VMEM((16, D), f32),
    ]
    sems = [dma((half,)), dma((half,)), dma, dma]
    if small:
        out_specs += [full((3, SIDE, PAIR)), full((16, 128))]
        out_shape += [
            jax.ShapeDtypeStruct((3, SIDE, PAIR), f32),
            jax.ShapeDtypeStruct((16, 128), f32),
        ]
        scratch += [pltpu.VMEM((CHUNKS, CHUNK, PAIR), bf16)] * 3
        scratch += [pltpu.VMEM((12, CHUNK, PAIR), bf16)]
        scratch += [pltpu.VMEM((8, 16, 128), f32)] * 2 + [pltpu.VMEM((CHUNK, PAIR), f32)]
        sems += [dma((6,))] * 2 + [dma((CHUNKS,))] * 2 + [dma((12,))] * 2 + [dma((7,)), dma((8,))]
    else:
        out_specs += [full((16, D)), full((3, SIDE, PAIR)), full((3, SIDE, PAIR))]
        out_shape += [jax.ShapeDtypeStruct((16, D), f32)] + [jax.ShapeDtypeStruct((3, SIDE, PAIR), bf16)] * 2
    scratch_more = [pltpu.VMEM((2, half, ROWS, D), bf16), pltpu.VMEM((seq, D), bf16)]
    scratch_more += [pltpu.VMEM((seq, PAIR), bf16)] * 3
    scratch_more += [pltpu.VMEM((3, SIDE, PAIR), bf16)] * 2 + [dma((2, half))] * 3 + [dma((4,))]
    return pl.pallas_call(
        functools.partial(last_kernel, small),
        grid=(GRAD_STEPS + 2 * half + 2,),
        in_specs=[
            *[pl.BlockSpec(memory_space=pl.ANY)] * 4,
            full(cat.shape),
            pl.BlockSpec((ROWS, D), lambda i: (core() * half + own(i), 0)),
            pl.BlockSpec((1, ROWS), lambda i: (0, core() * half + own(i))),
            full((16, D)),
            mine,
            full((8, D)),
            mine,
            mine,
            mine,
            full(mid_near.shape),
            full(mid_keep.shape),
        ],
        out_specs=out_specs,
        out_shape=out_shape,
        scratch_shapes=scratch + sems + scratch_more,
        compiler_params=params(collective_id=2, has_side_effects=True),
        cost_estimate=cost(38),
        name="last",
    )(norm, dq, dk, dv, cat, tokens, passes, vec, grad_second, sums_two, second, chip, far, mid_near, mid_keep)


def precondition(grad, weight, left, right, left_root, right_root):
    high = lax.Precision.HIGHEST
    left_new = decay * left + (1.0 - decay) * jnp.einsum(
        "...ij,...kj->...ik", grad, grad, precision=high
    )
    right_new = decay * right + (1.0 - decay) * jnp.einsum(
        "...ji,...jk->...ik", grad, grad, precision=high
    )
    half = jnp.einsum("...ij,...jk->...ik", left_root, grad, precision=high)
    step = jnp.einsum("...ij,...jk->...ik", half, right_root, precision=high)
    return (left_new, right_new, step, weight - rate_matrix * step)


def two_part(value):
    high = value.astype(bf16)
    return high, (value - high.astype(f32)).astype(bf16)


def dot_three(dot, a, b):
    return dot(a[0], b[0]) + (dot(a[0], b[1]) + dot(a[1], b[0]))


def renew_kernel(
    late, own, one, two, three, weight, left, right, left_root, right_root, output, input_grad, vec_sum, vec, moment,
    left_new, right_new, step, new, output_new, input_grad_new, vec_grad, moment_new, vec_new,
):
    @pl.when(pl.program_id(0) == 0)
    def _():
        rows, wide = vec.shape
        grad = vec_sum[:rows, :wide]
        square = decay * moment[...] + (1.0 - decay) * grad * grad
        vec_grad[...] = grad
        moment_new[...] = square
        vec_new[...] = vec[...] - rate_vector * grad / (jnp.sqrt(square) + moment_eps)

    output_new[...] = output[...]
    input_grad_new[...] = input_grad[...]

    @pl.when(pl.program_id(0) < 3)
    def _():
        early = own[0].astype(f32) + one[0].astype(f32) + two[0].astype(f32) + three[0].astype(f32)
        z = lax.axis_index("dp") // 2
        both = late[0] + jnp.where(z > 2, early, 0.0)
        for n in range(2):
            grad = both[:, n * SIDE : (n + 1) * SIDE]
            grad = two_part(jnp.where(z == 0, grad.T, grad))
            left_new[0, n] = decay * left[0, n] + (1.0 - decay) * dot_three(nt, grad, grad)
            right_new[0, n] = decay * right[0, n] + (1.0 - decay) * dot_three(tn, grad, grad)
            half = dot_three(nn, two_part(left_root[0, n]), grad)
            value = dot_three(nn, two_part(half), two_part(right_root[0, n]))
            step[0, n] = value
            new[0, n] = weight[0, n] - rate_matrix * value


def renew(late, own, far, weight, left, right, left_root, right_root, output, input_grad, vec_sum, vec, moment):
    pair = pl.BlockSpec((1, SIDE, PAIR), lambda i: (jnp.minimum(i, 2), 0, 0))
    slot = pl.BlockSpec((1, 2, SIDE, SIDE), lambda i: (0, jnp.minimum(i, 2), 0, 0))
    rows = pl.BlockSpec((output.shape[0] // 4, D), lambda i: (i, 0))
    return pl.pallas_call(
        renew_kernel,
        grid=(4,),
        in_specs=[pair] * 5 + [slot] * 5 + [rows] * 2 + [full(vec_sum.shape)] + [full(vec.shape)] * 2,
        out_specs=[slot] * 4 + [rows] * 2 + [full(vec.shape)] * 3,
        out_shape=[jax.ShapeDtypeStruct(weight.shape, f32)] * 4
        + [jax.ShapeDtypeStruct(value.shape, value.dtype) for value in (output, input_grad, vec, vec, vec)],
        compiler_params=params(46),
        cost_estimate=cost(8),
        name="renew",
    )(late, own, *far, weight, left, right, left_root, right_root, output, input_grad, vec_sum, vec, moment)


def to_pairs(blocks):
    n = blocks.shape[0] // 2
    return blocks.reshape(n, 2, SIDE, SIDE).transpose(0, 2, 1, 3).reshape(n, SIDE, PAIR)


def from_pairs(pairs):
    n = pairs.shape[0]
    return pairs.reshape(n, SIDE, 2, SIDE).transpose(0, 2, 1, 3).reshape(2 * n, SIDE, SIDE)


def swap(value, bit):
    return lax.ppermute(value, "tensor", [(t, t ^ bit) for t in range(NT)])


def hop_x(value):
    return lax.ppermute(value, "dp", [(d, d ^ 1) for d in range(8)])


def hop_z(value, turn, ends):
    pairs = [(d, (d + 2 * turn) % 8) for d in range(8) if (d // 2 + turn) % 4 in ends]
    return lax.ppermute(value, "dp", pairs)


def tie(*values):
    return lax.optimization_barrier(values)


def on_device(
    tokens,
    pass_ids,
    doc_lengths,
    cotangent,
    block_weights,
    vector_params,
    vector_moment,
    block_left,
    block_right,
    block_left_root,
    block_right_root,
):
    t, dp = lax.axis_index("tensor"), lax.axis_index("dp")
    core, side = t % 2, t // 2
    n_dp = lax.axis_size("dp")
    small = n_dp == 8
    z, column = (dp // 2, dp % 2) if small else (0, 0)
    lens = doc_lengths[0]
    seq = tokens.shape[0]
    passes = pass_ids.reshape(1, seq)
    total_blocks = (D // SIDE) * (4 + 2 * (FF // D))
    slots = block_weights.shape[1] * n_dp

    if small:
        pairs, columns, wo_other, vec, norm, q, k, v, cat = gather(
            block_weights, vector_params, tokens, passes
        )
        columns_x = hop_x(columns)
    else:
        every = lax.all_gather(block_weights.astype(bf16), "dp", axis=1, tiled=True)[0]
        near = to_pairs(every[:total_blocks])
        far = swap(near, 2)
        pairs = jnp.where(side == 0, jnp.stack([near, far]), jnp.stack([far, near]))
        vec = lax.all_gather(vector_params, "dp", axis=1, tiled=True)
        vec = jnp.pad(vec, ((0, 16 - vec.shape[0]), (0, 0)))
        wo_other = swap(pairs[:, 6:8], 1)
        columns = jnp.concatenate([near[12:15], near[18:21]], axis=0)
        columns_x = jnp.concatenate([near[15:18], near[21:24]], axis=0)
        norm, q, k, v, cat = project(tokens, passes, vec, pairs)
    mine, lse = attend(lens, q, k, v)
    out_chip, second, grad_second, grad_mixed, sums_two, mid_send, mid_keep, *ends = feed(
        small, tokens, passes, vec, mine, cotangent, pairs, wo_other, columns, columns_x
    )
    out_far = swap(out_chip, 2)
    if small:
        far = [hop_z(ends[turn], turn, (3,)) for turn in (1, 2, 3)]
        mid_send = hop_x(mid_send)
    dq, dk, dv = attend_back(lens, q, k, v, mine, lse, grad_mixed)
    if small:
        *far, out_far, mid_send, dq = tie(*far, out_far, mid_send, dq)
    output, input_grad, *sums = last(
        small, norm, dq, dk, dv, cat, tokens, passes, vec, grad_second, sums_two, second, out_chip, out_far,
        mid_send, mid_keep,
    )
    if small:
        late, vector_sum = sums
        return_blocks = renew(
            late, ends[0], far, block_weights, block_left, block_right, block_left_root, block_right_root,
            output, input_grad, vector_sum, vector_params, vector_moment,
        )
        left_new, right_new, step, weight_new, output, input_grad, vector_grad, moment_new, vector_new = return_blocks
    else:
        vector_part, g_send, g_keep = sums[0][: PASSES + 4], *sums[1:]
        send, keep = ends
        rest = jnp.stack(
            [
                jnp.concatenate([mid_keep, keep]).reshape(3, 3, SIDE, PAIR),
                jnp.concatenate([mid_send, send]).reshape(3, 3, SIDE, PAIR),
            ],
            axis=1,
        )
        grad_qkv = from_pairs(jnp.concatenate([g_keep, g_send], axis=0)).swapaxes(1, 2)
        grad_rest = from_pairs(rest.reshape(18, SIDE, PAIR))
        spare = jnp.zeros((slots - total_blocks, SIDE, SIDE), bf16)
        grad_blocks = jnp.concatenate([grad_qkv, grad_rest, spare], axis=0)[None].astype(f32)
        owned = lax.psum_scatter(grad_blocks, "dp", scatter_dimension=1, tiled=True)
        vector_grad = lax.psum_scatter(vector_part, "dp", scatter_dimension=1, tiled=True)
        left_new, right_new, step, weight_new = precondition(
            owned, block_weights, block_left, block_right, block_left_root, block_right_root
        )
        moment_new = decay * vector_moment + (1.0 - decay) * vector_grad * vector_grad
        vector_new = vector_params - rate_vector * vector_grad / (jnp.sqrt(moment_new) + moment_eps)
    return (
        output,
        input_grad,
        left_new,
        right_new,
        step,
        weight_new,
        vector_grad,
        moment_new,
        vector_new,
    )


def solution(mesh):
    rows, line = P("dp", None), P(None, "dp")
    block = P("tensor", "dp", None, None)
    return jax.shard_map(
        on_device,
        mesh=mesh,
        in_specs=(rows, P("dp"), rows, rows, block, line, line, block, block, block, block),
        out_specs=(rows, rows, block, block, block, block, line, line, line),
        check_vma=False,
    )
```

```python
import functools

import jax
import jax.numpy as jnp
from jax import lax
from jax.experimental import pallas as pl
from jax.experimental.pallas import tpu as pltpu
from jax.sharding import PartitionSpec as P

D = 768
HD = 64
FF = 3072
PASSES = 5
SIDE = 192
PAIR = 2 * SIDE
ROWS = 256
WIDE = 512
DOCS = 8
NT = 4

norm_eps = 1e-05
moment_eps = 1e-08
rate_matrix = 0.03
rate_vector = 0.2
decay = 0.5
gelu_coef = 0.7978845608028654
masked_score = -1e30
f32 = jnp.float32
bf16 = jnp.bfloat16
MESH = pl.DeviceIdType.MESH


def nn(a, b):
    return lax.dot_general(a, b, (((1,), (0,)), ((), ())), preferred_element_type=f32)


def nt(a, b):
    return lax.dot_general(a, b, (((1,), (1,)), ((), ())), preferred_element_type=f32)


def tn(a, b):
    return lax.dot_general(a, b, (((0,), (0,)), ((), ())), preferred_element_type=f32)


def split_three(value):
    high = value.astype(bf16)
    rest = value - high.astype(f32)
    mid = rest.astype(bf16)
    return high, mid, (rest - mid.astype(f32)).astype(bf16)


def one_hot(pass_row):
    kinds = lax.broadcasted_iota(jnp.int32, (16, pass_row.shape[1]), 0)
    return (kinds == pass_row).astype(f32).astype(bf16)


def embedded(tokens, pass_row, vec):
    chosen = jnp.concatenate([one_hot(pass_row)] * 3, axis=0)
    return tokens.astype(f32) + tn(chosen, jnp.concatenate(split_three(vec), axis=0))


def hat_of(hidden):
    mean = jnp.mean(hidden, axis=-1, keepdims=True)
    center = hidden - mean
    spread = jnp.mean(center * center, axis=-1, keepdims=True)
    root = lax.rsqrt(spread + norm_eps)
    return center * root, root


def norm_back(hat, root, grad, gain):
    scaled = grad * gain
    first = jnp.mean(scaled, axis=-1, keepdims=True)
    second = jnp.mean(scaled * hat, axis=-1, keepdims=True)
    return root * (scaled - first - hat * second)


def params(mebibytes=56, **kw):
    return pltpu.CompilerParams(vmem_limit_bytes=mebibytes * 1024 * 1024, **kw)


def cost(micros):
    return pl.CostEstimate(flops=int(micros * 1.1e9), bytes_accessed=int(micros * 1e6), transcendentals=0)


def full(shape):
    return pl.BlockSpec(shape, lambda *_: (0,) * len(shape))


def gather_kernel(
    own, vec_own, tokens, passes,
    all_pairs, columns, wo_other, vec_out, norm, q, k_out, v, cat,
    pack, vec_pack, vec_land, wq, tok, norm_s, qkv_s, cat_s, *sems,
):
    (
        s_z1, r_z1, s_x1, r_x1, s_y1, r_y1, s_d1, r_d1, s_l, r_l, s_r, r_r, s_x2, r_x2, s_y2, r_y2, s_v, r_v, s_c, r_c,
        s_out, s_cat, s_tok, loc,
    ) = sems
    dp, t = lax.axis_index("dp"), lax.axis_index("tensor")
    z, x = dp // 2, dp % 2
    y, core = t // 2, t % 2
    far_x, far_y, near = z * 2 + (1 - x), (1 - y) * 2 + core, y * 2 + (1 - core)

    barrier = pltpu.get_barrier_semaphore()
    peers = [lax.rem(dp + n, 8) for n in range(1, 8)]
    for peer in peers:
        pl.semaphore_signal(barrier, inc=1, device_id={"dp": peer}, device_id_type=MESH)
    for to in (far_y, near):
        pl.semaphore_signal(barrier, inc=1, device_id={"tensor": to}, device_id_type=MESH)

    tok_copy = pltpu.make_async_copy(tokens, tok, s_tok)
    tok_copy.start()
    for m in range(3):
        pair = jnp.concatenate([own[0, 2 * m], own[0, 2 * m + 1]], axis=1).astype(bf16)
        pack[m] = pair

        @pl.when(z == 0)
        def _():
            wq[y, 3 * x + m] = pair

    vec_pack[...] = jnp.zeros_like(vec_pack)
    vec_pack[0 : PASSES + 4, 0 : D // 8] = vec_own[...]
    pl.semaphore_wait(barrier, 9)

    started = []

    def send(src, dst, s_sem, r_sem, to, cond=None):
        copy = pltpu.make_async_remote_copy(
            src_ref=src, dst_ref=dst, send_sem=s_sem, recv_sem=r_sem, device_id=to, device_id_type=MESH
        )
        started.append((cond, copy))
        if cond is None:
            copy.start()
        else:
            pl.when(cond)(copy.start)

    def arrived(dst, r_sem, cond=None):
        copy = pltpu.make_async_remote_copy(
            src_ref=dst, dst_ref=dst, send_sem=loc, recv_sem=r_sem, device_id={"dp": far_x}, device_id_type=MESH
        )
        if cond is None:
            copy.wait_recv()
        else:
            pl.when(cond)(copy.wait_recv)

    to_x, to_y, to_left, to_right = {"dp": far_x}, {"tensor": far_y}, {"dp": dp - 2}, {"dp": dp + 2}
    half = SIDE // 2

    def piece(side, column, k):
        return wq.at[side, 3 * column + k // 2, pl.ds((k % 2) * half, half)]

    def at_one(m):
        return all_pairs.at[y, 6 + 3 * x + m]

    def at_z(d, m):
        return columns.at[3 * (z + d - 2) + m]

    own_one = pltpu.make_async_copy(pack, all_pairs.at[y, pl.ds(6 + 3 * x, 3)], loc)
    own_more = pltpu.make_async_copy(pack, columns.at[pl.ds(3 * (z - 2), 3)], loc)
    pl.when(z == 1)(own_one.start)
    pl.when(z > 1)(own_more.start)

    for m in range(3):
        send(pack.at[m], at_one(m), s_l.at[0, m], r_l.at[0, m], to_left, z == 1)
        send(pack.at[m], at_z(0, m), s_l.at[0, m], r_l.at[0, m], to_left, z > 1)
    for n, peer in enumerate(peers):
        send(vec_pack, vec_land.at[dp], s_v.at[n], r_v.at[dp], {"dp": peer})
    send(pack.at[0], at_z(0, 0), s_r.at[0, 0], r_r.at[0, 0], to_right, z == 2)
    send(pack.at[0], at_one(0), s_x2.at[0], r_x2.at[0], to_x, z == 1)

    def diagonal(k):
        if k % 2 == 0:
            arrived(piece(y, 1 - x, k), r_x1.at[k])
            send(piece(y, 1 - x, k), piece(y, 1 - x, k), s_d1.at[k], r_d1.at[k], to_y)
        else:
            arrived(piece(1 - y, x, k), r_y1.at[k])
            send(piece(1 - y, x, k), piece(1 - y, x, k), s_d1.at[k], r_d1.at[k], to_x)

    def from_right(d, m):
        arrived(columns.at[m], r_l.at[d - 1, m], z + d < 4)
        if d < 3:
            send(at_z(d, m), at_z(d, m), s_l.at[d, m], r_l.at[d, m], to_left, (z + d < 4) & (z > 0))

    def along_x(m, cond):
        send(at_one(m), at_one(m), s_x2.at[m], r_x2.at[m], to_x, cond)

    def from_left(d, m):
        arrived(columns.at[m], r_r.at[d - 1, m], z > d)
        if d == 1:
            send(at_one(m), at_one(m), s_r.at[1, m], r_r.at[1, m], to_right, z == 2)
        along_x(m, z == d + 1)

    for k in range(6):
        arrived(piece(y, x, k), r_z1.at[k], z > 0)
        send(piece(y, x, k), piece(y, x, k), s_z1.at[k], r_z1.at[k], to_right, z < 3)
        send(piece(y, x, k), piece(y, x, k), s_x1.at[k], r_x1.at[k], to_x)
        send(piece(y, x, k), piece(y, x, k), s_y1.at[k], r_y1.at[k], to_y)
        if k == 5:
            for m in range(3):
                send(pack.at[m], at_one(m), s_r.at[0, m], r_r.at[0, m], to_right, z == 1)
                if m > 0:
                    send(pack.at[m], at_z(0, m), s_r.at[0, m], r_r.at[0, m], to_right, z == 2)
                    send(pack.at[m], at_one(m), s_x2.at[m], r_x2.at[m], to_x, z == 1)
        if k >= 1:
            diagonal(k - 1)
        if k % 2 == 1:
            from_right(1, k // 2)
    diagonal(5)
    pl.when(z == 1)(own_one.wait)
    pl.when(z > 1)(own_more.wait)
    for m in range(3):
        along_x(m, z == 0)
    for m in range(3):
        from_left(1, m)
        from_right(2, m)
    for k in range(6):
        if k % 2 == 0:
            arrived(piece(1 - y, x, k), r_y1.at[k])
        else:
            arrived(piece(y, 1 - x, k), r_x1.at[k])
        arrived(piece(1 - y, 1 - x, k), r_d1.at[k])
    for peer in peers:
        arrived(vec_land.at[peer], r_v.at[peer])
    vec_land[dp] = vec_pack[...]
    vec = jnp.concatenate([vec_land[d][:, : D // 8] for d in range(8)], axis=1)
    vec_out[...] = vec
    for n in range(3):
        for i in range(4):
            at = (i % 2) * SIDE
            parts = [wq[h, 2 * n + i // 2][:, at : at + SIDE] for h in range(2)]
            cat_s[n, i * SIDE : (i + 1) * SIDE, :] = jnp.concatenate(parts, axis=1)
    writes = [pltpu.make_async_copy(cat_s, cat, s_cat)]
    writes[0].start()
    tok_copy.wait()

    def rows_of(b):
        rows = slice(b * WIDE, (b + 1) * WIDE)
        hat, _ = hat_of(embedded(tok[rows, :], passes[:, rows], vec))
        low = (hat * vec[PASSES : PASSES + 1] + vec[PASSES + 1 : PASSES + 2]).astype(bf16)
        norm_s[rows, :] = low
        writes.append(pltpu.make_async_copy(norm_s.at[rows, :], norm.at[rows, :], s_out.at[b, 3]))
        writes[-1].start()
        for n, out in enumerate((q, k_out, v)):
            qkv_s[n, rows, :] = nn(low, cat_s[n]).astype(bf16)
            writes.append(pltpu.make_async_copy(qkv_s.at[n, rows, :], out.at[rows, :], s_out.at[b, n]))
            writes[-1].start()

    count = tok.shape[0] // WIDE
    for b in range(count):
        rows_of(b)
        if b == 0:
            for m in range(3):
                from_left(2, m)
                from_right(3, m)
        if b == 1:
            for m in range(2):
                ref = all_pairs.at[y, 6 + m]
                arrived(ref, r_x2.at[m], x == 1)
                send(ref, ref, s_y2.at[m], r_y2.at[m], to_y)
                send(ref, wo_other.at[y, m], s_c.at[0, m], r_c.at[y, m], {"tensor": near})
    for m in range(2):
        ref = all_pairs.at[1 - y, 6 + m]
        arrived(ref, r_y2.at[m])
        send(ref, wo_other.at[1 - y, m], s_c.at[1, m], r_c.at[1 - y, m], {"tensor": near})
    for m in range(3):
        arrived(all_pairs.at[y, 6 + 3 * (1 - x) + m], r_x2.at[m], None if m == 2 else x == 0)
    for h in range(2):
        for m in range(2):
            arrived(wo_other.at[h, m], r_c.at[h, m])
    for copy in writes:
        copy.wait()
    for cond, copy in started:
        if cond is None:
            copy.wait_send()
        else:
            pl.when(cond)(copy.wait_send)


def gather(block_weights, vector_params, tokens, passes):
    seq = tokens.shape[0]
    dma = pltpu.SemaphoreType.DMA
    sizes = [(6,)] * 8 + [(3, 3)] * 2 + [(2, 3)] * 2 + [(3,)] * 2 + [(2,)] * 2 + [(7,), (8,)] + [(2, 2)] * 2
    sizes += [(seq // WIDE, 4)]
    vmem, far = pl.BlockSpec(memory_space=pltpu.VMEM), pl.BlockSpec(memory_space=pl.ANY)
    wide = jax.ShapeDtypeStruct((seq, PAIR), bf16)
    return pl.pallas_call(
        gather_kernel,
        in_specs=[vmem, vmem, far, vmem],
        out_specs=[far, far, far, vmem, far, far, far, far, far],
        out_shape=[
            jax.ShapeDtypeStruct((2, 24, SIDE, PAIR), bf16),
            jax.ShapeDtypeStruct((6, SIDE, PAIR), bf16),
            jax.ShapeDtypeStruct((2, 2, SIDE, PAIR), bf16),
            jax.ShapeDtypeStruct((16, D), f32),
            jax.ShapeDtypeStruct((seq, D), bf16),
            wide,
            wide,
            wide,
            jax.ShapeDtypeStruct((3, D, PAIR), bf16),
        ],
        scratch_shapes=[
            pltpu.VMEM((3, SIDE, PAIR), bf16),
            pltpu.VMEM((16, 128), f32),
            pltpu.VMEM((8, 16, 128), f32),
            pltpu.VMEM((2, 6, SIDE, PAIR), bf16),
            pltpu.VMEM((seq, D), bf16),
            pltpu.VMEM((seq, D), bf16),
            pltpu.VMEM((3, seq, PAIR), bf16),
            pltpu.VMEM((3, D, PAIR), bf16),
        ]
        + [dma(size) for size in sizes]
        + [dma] * 3,
        compiler_params=params(collective_id=0, has_side_effects=True),
        cost_estimate=cost(60),
        name="gather",
    )(block_weights, vector_params, tokens, passes)


def project_kernel(tok, pas, vec, wq, norm, q, k, v, cat):
    @pl.when(pl.program_id(0) == 0)
    def _():
        for x in range(3):
            for i in range(4):
                at = (i % 2) * SIDE
                parts = [wq[h, 2 * x + i // 2][:, at : at + SIDE] for h in range(2)]
                cat[x, i * SIDE : (i + 1) * SIDE, :] = jnp.concatenate(parts, axis=1)

    first = embedded(tok[...], pas[...], vec[...])
    hat, _ = hat_of(first)
    low = (hat * vec[PASSES : PASSES + 1] + vec[PASSES + 1 : PASSES + 2]).astype(bf16)
    norm[...] = low
    for x, out in enumerate((q, k, v)):
        out[...] = nn(low, cat[x]).astype(bf16)


def project(tokens, passes, vec, wq):
    seq = tokens.shape[0]
    row = lambda n: pl.BlockSpec((WIDE, n), lambda i: (i, 0))
    wide = jax.ShapeDtypeStruct((seq, PAIR), bf16)
    return pl.pallas_call(
        project_kernel,
        grid=(seq // WIDE,),
        in_specs=[
            row(D),
            pl.BlockSpec((1, WIDE), lambda i: (0, i)),
            full((16, D)),
            full((2, 6, SIDE, PAIR)),
        ],
        out_specs=[row(D), row(PAIR), row(PAIR), row(PAIR), full((3, D, PAIR))],
        out_shape=[
            jax.ShapeDtypeStruct((seq, D), bf16),
            wide,
            wide,
            wide,
            jax.ShapeDtypeStruct((3, D, PAIR), bf16),
        ],
        compiler_params=params(),
        cost_estimate=cost(16),
        name="project",
    )(tokens, passes, vec, wq)


def doc_state(lens, base):
    rows = base + lax.broadcasted_iota(jnp.int32, (1, ROWS), 1)
    rows = jnp.concatenate([rows, rows], axis=1)
    begin = jnp.int32(0)
    first = jnp.int32(0)
    starts = jnp.zeros((1, 2 * ROWS), jnp.int32)
    for c in range(DOCS):
        starts = jnp.where(rows >= begin, begin, starts)
        first = jnp.where(base >= begin, begin, first)
        begin = begin + lens[c]
    return rows, starts, first


def two_heads(block):
    left = lax.broadcasted_iota(jnp.int32, block.shape, 1) < HD
    none = jnp.zeros_like(block)
    return jnp.concatenate([jnp.where(left, block, none), jnp.where(left, none, block)], axis=0)


def one_above(both):
    return jnp.concatenate([both[:HD, :ROWS], both[HD:, ROWS:]], axis=0).T


def attend_kernel(lens, q, k, v, out, lse, acc):
    i = pl.program_id(0)
    base = i * ROWS
    rows, starts, first = doc_state(lens, base)
    pairs = [two_heads(q[:, p * 128 : (p + 1) * 128] * bf16(0.125)) for p in range(3)]
    for p in range(3):
        acc[p] = jnp.zeros((128, 2 * ROWS), f32)

    def step(j, carry):
        at = pl.multiple_of(j * ROWS, ROWS)
        keys = at + lax.broadcasted_iota(jnp.int32, (ROWS, 2 * ROWS), 0)
        seen = (keys >= starts) & (keys <= rows)
        here = pl.ds(at, ROWS)
        head = lambda p: slice(p * 128, (p + 1) * 128)
        scores = [jnp.where(seen, nt(k[here, head(p)], pairs[p]), masked_score) for p in range(3)]
        state = []
        for p in range(3):
            before, total = carry[2 * p], carry[2 * p + 1]
            now = jnp.maximum(before, jnp.max(scores[p], axis=0, keepdims=True))
            probs = jnp.exp(scores[p] - now)
            fade = jnp.exp(before - now)
            state += [now, total * fade + jnp.sum(probs, axis=0, keepdims=True)]
            acc[p] = acc[p] * fade + tn(v[here, head(p)], probs.astype(bf16))
        return tuple(state)

    zero = jnp.zeros((1, 2 * ROWS), f32)
    state = lax.fori_loop(first // ROWS, i + 1, step, (zero + masked_score, zero) * 3)
    lines = []
    for p in range(3):
        top, total = state[2 * p], state[2 * p + 1]
        out[:, p * 128 : (p + 1) * 128] = one_above(acc[p] / total).astype(bf16)
        line = top + jnp.log(total)
        lines += [line[:, :ROWS], line[:, ROWS:]]
    lse[...] = jnp.concatenate(lines + lines[:2], axis=0)


def attend(lens, q, k, v):
    seq = q.shape[0]
    row = pl.BlockSpec((ROWS, PAIR), lambda i, s: (i, 0))
    return pl.pallas_call(
        attend_kernel,
        grid_spec=pltpu.PrefetchScalarGridSpec(
            num_scalar_prefetch=1,
            grid=(seq // ROWS,),
            in_specs=[row, full((seq, PAIR)), full((seq, PAIR))],
            out_specs=[row, pl.BlockSpec((8, ROWS), lambda i, s: (0, i))],
            scratch_shapes=[
                pltpu.VMEM((3, 128, 2 * ROWS), f32),
            ],
        ),
        out_shape=[
            jax.ShapeDtypeStruct((seq, PAIR), bf16),
            jax.ShapeDtypeStruct((8, seq), f32),
        ],
        compiler_params=params(),
        cost_estimate=cost(30),
        name="attend",
    )(lens, q, k, v)


def attend_back_kernel(
    lens, q, k, v, mixed, lse, grad_mixed, dq, dk, dv, dk_acc, dv_acc, dq_acc
):
    i = pl.program_id(0)
    count = pl.num_programs(0)
    base = i * ROWS

    @pl.when(i == 0)
    def _():
        dk_acc[...] = jnp.zeros_like(dk_acc)
        dv_acc[...] = jnp.zeros_like(dv_acc)

    rows, starts, first = doc_state(lens, base)
    heads = lax.broadcasted_iota(jnp.int32, (8, 128), 0)
    lanes = lax.broadcasted_iota(jnp.int32, (8, 128), 1)
    pick = (lanes // HD == heads).astype(f32).astype(bf16)
    queries, grads, inner, lines = [], [], [], []
    for p in range(3):
        cols = slice(p * 128, (p + 1) * 128)
        queries.append(two_heads(q[:, cols] * bf16(0.125)))
        grads.append(two_heads(grad_mixed[:, cols]))
        product = grad_mixed[:, cols].astype(f32) * mixed[:, cols].astype(f32)
        high, low, _ = split_three(product)
        sums = nt(pick, high) + nt(pick, low)
        inner.append(jnp.concatenate([sums[0:1], sums[1:2]], axis=1))
        lines.append(jnp.concatenate([lse[2 * p : 2 * p + 1], lse[2 * p + 1 : 2 * p + 2]], axis=1))
        dq_acc[p] = jnp.zeros((128, 2 * ROWS), f32)

    def step(j, carry):
        at = pl.multiple_of(j * ROWS, ROWS)
        keys = at + lax.broadcasted_iota(jnp.int32, (ROWS, 2 * ROWS), 0)
        seen = (keys >= starts) & (keys <= rows)
        here = pl.ds(at, ROWS)
        for p in range(3):
            cols = slice(p * 128, (p + 1) * 128)
            kb = k[here, cols]
            scores = jnp.where(seen, nt(kb, queries[p]) - lines[p], masked_score)
            probs = jnp.exp(scores)
            grad_probs = nt(v[here, cols], grads[p])
            grad_scores = (probs * (grad_probs - inner[p])).astype(bf16)
            dv_acc[here, cols] += nn(probs.astype(bf16), grads[p])
            dk_acc[here, cols] += nn(grad_scores, queries[p])
            dq_acc[p] += tn(kb, grad_scores)
        return carry

    lax.fori_loop(first // ROWS, i + 1, step, 0)
    for p in range(3):
        dq[:, p * 128 : (p + 1) * 128] = (one_above(dq_acc[p]) * 0.125).astype(bf16)

    @pl.when(i == count - 1)
    def _():
        dk[...] = dk_acc[...].astype(bf16)
        dv[...] = dv_acc[...].astype(bf16)


def attend_back(lens, q, k, v, mixed, lse, grad_mixed):
    seq = q.shape[0]
    count = seq // ROWS
    row = pl.BlockSpec((ROWS, PAIR), lambda i, s: (i, 0))
    wide = jax.ShapeDtypeStruct((seq, PAIR), bf16)
    return pl.pallas_call(
        attend_back_kernel,
        grid_spec=pltpu.PrefetchScalarGridSpec(
            num_scalar_prefetch=1,
            grid=(count,),
            in_specs=[
                row,
                full((seq, PAIR)),
                full((seq, PAIR)),
                row,
                pl.BlockSpec((8, ROWS), lambda i, s: (0, i)),
                row,
            ],
            out_specs=[row, full((seq, PAIR)), full((seq, PAIR))],
            scratch_shapes=[
                pltpu.VMEM((seq, PAIR), f32),
                pltpu.VMEM((seq, PAIR), f32),
                pltpu.VMEM((3, 128, 2 * ROWS), f32),
            ],
        ),
        out_shape=[wide, wide, wide],
        compiler_params=params(),
        cost_estimate=cost(40),
        name="attend_back",
    )(lens, q, k, v, mixed, lse, grad_mixed)


def feed_kernel(
    small, tok, pas, vec, mine, cot, wo_mine, wo_other, four, columns, columns_x,
    out_chip, second_keep, grad_second, grad_mixed, sums, mid_send, mid_keep, *rest,
):
    results, rest = (rest[:4], rest[4:]) if small else (rest[:2], rest[2:])
    (
        wo, other, up, down, gup, gdown, go, core_out, core_in, far_out, far_in, ga_out, ga_in, oc_out, oc_in,
        g_send, g_keep, g_in, s_core, r_core, s_far, r_far, s_ga, r_ga, s_oc, r_oc, s_x, r_x, s_m, r_m,
    ) = rest
    step = pl.program_id(0)
    half = core_out.shape[0]
    t, dp = lax.axis_index("tensor"), lax.axis_index("dp")
    core, side = t % 2, t // 2
    near, far = side * 2 + (1 - core), (1 - side) * 2 + core
    z, column = (dp // 2, dp % 2) if small else (0, 0)
    far_x = z * 2 + 1 - column

    def copy(src, dst, s_sem, r_sem, j, to):
        return pltpu.make_async_remote_copy(
            src_ref=src.at[j],
            dst_ref=dst.at[j],
            send_sem=s_sem.at[j],
            recv_sem=r_sem.at[j],
            device_id={"tensor": to},
            device_id_type=MESH,
        )

    core_copy = lambda j: copy(core_out, core_in, s_core, r_core, j, near)
    far_copy = lambda j: copy(far_out, far_in, s_far, r_far, j, far)
    ga_copy = lambda j: copy(ga_out, ga_in, s_ga, r_ga, j, near)
    oc_copy = lambda j: copy(oc_out, oc_in, s_oc, r_oc, j, near)

    def x_copy(slot):
        return pltpu.make_async_remote_copy(
            src_ref=g_send.at[slot],
            dst_ref=g_in.at[slot],
            send_sem=s_x.at[slot],
            recv_sem=r_x.at[slot],
            device_id={"dp": far_x},
            device_id_type=MESH,
        )

    def mixed_copy(block):
        rows = pl.ds(pl.multiple_of(block * ROWS, ROWS), ROWS)
        return pltpu.make_async_remote_copy(
            src_ref=mine.at[rows],
            dst_ref=other.at[rows],
            send_sem=s_m.at[block],
            recv_sem=r_m.at[block],
            device_id={"tensor": near},
            device_id_type=MESH,
        )

    barrier = pltpu.get_barrier_semaphore()

    @pl.when(step == 0)
    def _():
        for to in (near, far):
            pl.semaphore_signal(barrier, inc=1, device_id={"tensor": to}, device_id_type=MESH)
        if small:
            pl.semaphore_signal(barrier, inc=1, device_id={"dp": far_x}, device_id_type=MESH)
        for h in range(2):
            for m in range(2):
                rows, cols = slice(h * SIDE, (h + 1) * SIDE), slice(m * PAIR, (m + 1) * PAIR)
                wo[rows, cols] = wo_mine[h, m]
                wo[PAIR + h * SIDE : PAIR + (h + 1) * SIDE, cols] = wo_other[h, m]
        for r in range(4):
            for m in range(2):
                rows, cols = slice(r * SIDE, (r + 1) * SIDE), slice(m * PAIR, (m + 1) * PAIR)
                for at, weight in ((8, up), (16, down)):
                    pair = at + 2 * r + m
                    if pair < 12:
                        weight[rows, cols] = four[0, pair - 8]
                        continue
                    n = (pair // 6 - 2) * 3 + pair % 3
                    for source, here in ((columns, pair // 3 % 2), (columns_x, 1 - pair // 3 % 2)):

                        @pl.when(column == here)
                        def _():
                            weight[rows, cols] = source[n]

        pl.semaphore_wait(barrier, 3 if small else 2)
        for j in range(half):
            mixed_copy(core * half + j).start()
            mixed_copy((1 - core) * half + j).start()
        gup[...] = jnp.zeros_like(gup)
        gdown[...] = jnp.zeros_like(gdown)
        go[...] = jnp.zeros_like(go)
        sums[...] = jnp.zeros_like(sums)

    @pl.when(step < 2 * half)
    def _():
        j = step // 2
        owner = jnp.where(step % 2 == 0, 1 - core, core)
        here = pl.ds(pl.multiple_of((owner * half + j) * ROWS, ROWS), ROWS)
        first = embedded(tok[...], pas[...], vec[...])
        mixed_copy(owner * half + j).wait_recv()
        second = first + nn(jnp.concatenate([mine[here, :], other[here, :]], axis=1), wo[...])
        hat, _ = hat_of(second)
        low = (hat * vec[PASSES + 2 : PASSES + 3] + vec[PASSES + 3 : PASSES + 4]).astype(bf16)
        upper = nn(low, up[...])
        square = upper * upper
        bent = jnp.tanh(gelu_coef * upper * (1.0 + 0.044715 * square))
        act = (0.5 * upper * (1.0 + bent)).astype(bf16)
        slope = 0.5 * (1.0 + bent) + (0.5 * gelu_coef) * upper * (1.0 - bent * bent) * (
            1.0 + (3 * 0.044715) * square
        )
        grad_act = nt(cot[...], down[...])
        grad_upper = (grad_act * slope).astype(bf16)
        part = nt(grad_upper, up[...])

        @pl.when(step % 2 == 0)
        def _():
            core_out[j] = part.astype(bf16)
            core_copy(j).start()

        @pl.when(step % 2 == 1)
        def _():
            core_copy(j).wait_recv()
            far_out[j] = (part + core_in[j].astype(f32)).astype(bf16)
            far_copy(j).start()
            second_keep[pl.ds(pl.multiple_of(j * ROWS, ROWS), ROWS), :] = second

        gup[...] += tn(low, grad_upper)
        gdown[...] += tn(act, cot[...])
        out_part = nn(act, down[...])

        @pl.when(step % 2 == 0)
        def _():
            oc_out[j] = out_part.astype(bf16)
            oc_copy(j).start()

        @pl.when(step % 2 == 1)
        def _():
            oc_copy(j).wait_recv()
            out_chip[...] = (out_part + oc_in[j].astype(f32)).astype(bf16)

    @pl.when(step == 2 * half - 1)
    def _():
        for r in range(4):
            for m in range(2):
                rows, cols = slice(r * SIDE, (r + 1) * SIDE), slice(m * PAIR, (m + 1) * PAIR)
                for at, total in ((8, gup), (16, gdown)):
                    pair = at + 2 * r + m
                    slot, place = (pair // 6 - 1) * 3 + pair % 3, pair // 3 % 2
                    value = total[rows, cols].astype(bf16)
                    kept, sent, n = (mid_keep, mid_send, slot) if slot < 6 else (g_keep, g_send, slot - 6)

                    @pl.when(column == place)
                    def _():
                        kept[n] = value

                    @pl.when(column != place)
                    def _():
                        sent[n] = value
        if small:
            for n in range(3):
                x_copy(n).start()

    def through_out(grad, block):
        here = pl.ds(pl.multiple_of(block * ROWS, ROWS), ROWS)
        grad_mixed[here, :] = nt(grad, wo[:PAIR, :]).astype(bf16)
        go[...] += tn(mine[here, :], grad)

    @pl.when((step >= 2 * half) & (step < 3 * half))
    def _():
        j = step - 2 * half
        hat, root = hat_of(second_keep[pl.ds(pl.multiple_of(j * ROWS, ROWS), ROWS), :])
        far_copy(j).wait_recv()
        grad = far_out[j].astype(f32) + far_in[j].astype(f32)
        result = cot[...].astype(f32) + norm_back(hat, root, grad, vec[PASSES + 2 : PASSES + 3])
        low = result.astype(bf16)
        ga_out[j] = low
        ga_copy(j).start()
        grad_second[...] = result
        sums[0:1] += jnp.sum(grad * hat, axis=0, keepdims=True)
        sums[1:2] += jnp.sum(grad, axis=0, keepdims=True)
        through_out(low, core * half + j)

    @pl.when(step > 2 * half)
    def _():
        j = step - 2 * half - 1
        ga_copy(j).wait_recv()
        through_out(ga_in[j], (1 - core) * half + j)

    @pl.when(step == 3 * half)
    def _():
        at = pl.multiple_of(side * SIDE, SIDE)
        for m in range(2):
            value = go[pl.ds(at, SIDE), m * PAIR : (m + 1) * PAIR].astype(bf16)

            @pl.when(column == 0)
            def _():
                mid_keep[m] = value

            @pl.when(column != 0)
            def _():
                mid_send[m] = value

        for j in range(half):
            core_copy(j).wait_send()
            oc_copy(j).wait_send()
            mixed_copy(j).wait_send()
            mixed_copy(half + j).wait_send()
            far_copy(j).wait_send()
            ga_copy(j).wait_send()
        if small:
            for n in range(3):
                x_copy(n).wait_send()
                x_copy(n).wait_recv()
                value = (g_keep[n].astype(f32) + g_in[n].astype(f32)).astype(bf16)
                for turn in range(4):

                    @pl.when(z + turn == 3)
                    def _():
                        results[turn][n] = value
        else:
            results[0][...] = g_send[...]
            results[1][...] = g_keep[...]


def feed(small, tokens, passes, vec, mine, cotangent, pairs, wo_other, columns, columns_x):
    seq = tokens.shape[0]
    half = seq // ROWS // 2

    def block(i):
        core = lax.axis_index("tensor") % 2
        work = jnp.minimum(i, 2 * half - 1)
        owner = jnp.where(work % 2 == 0, 1 - core, core)
        return owner * half + work // 2

    def cot_block(i):
        core = lax.axis_index("tensor") % 2
        return jnp.where(i < 2 * half, block(i), core * half + jnp.minimum(i - 2 * half, half - 1))

    side = lambda: lax.axis_index("tensor") // 2
    row = lambda n: pl.BlockSpec((ROWS, n), lambda i: (block(i), 0))
    keep = pl.BlockSpec((ROWS, D), lambda i: (jnp.minimum(i // 2, half - 1), 0))
    last = pl.BlockSpec((ROWS, D), lambda i: (jnp.clip(i - 2 * half, 0, half - 1), 0))
    rows = lambda kind: jax.ShapeDtypeStruct((seq // 2, D), kind)
    gr = lambda n: jax.ShapeDtypeStruct((n, SIDE, PAIR), bf16)
    ends = [(3, SIDE, PAIR)] * (4 if small else 2)
    buffer = pltpu.VMEM((half, ROWS, D), bf16)
    dma = pltpu.SemaphoreType.DMA((half,))
    return pl.pallas_call(
        functools.partial(feed_kernel, small),
        grid=(3 * half + 1,),
        in_specs=[
            row(D),
            pl.BlockSpec((1, ROWS), lambda i: (0, block(i))),
            full((16, D)),
            full((seq, PAIR)),
            pl.BlockSpec((ROWS, D), lambda i: (cot_block(i), 0)),
            pl.BlockSpec((2, 2, SIDE, PAIR), lambda i: (0, 3, 0, 0)),
            full(wo_other.shape),
            pl.BlockSpec((1, 4, SIDE, PAIR), lambda i: (side(), 2, 0, 0)),
            full(columns.shape),
            full(columns.shape),
        ],
        out_specs=[
            keep,
            full((seq // 2, D)),
            last,
            full((seq, PAIR)),
            full((8, D)),
            full((6, SIDE, PAIR)),
            full((6, SIDE, PAIR)),
        ]
        + [full(shape) for shape in ends],
        scratch_shapes=[
            pltpu.VMEM((D, D), bf16),
            pltpu.VMEM((seq, PAIR), bf16),
            pltpu.VMEM((D, D), bf16),
            pltpu.VMEM((D, D), bf16),
            pltpu.VMEM((D, D), f32),
            pltpu.VMEM((D, D), f32),
            pltpu.VMEM((PAIR, D), f32),
        ]
        + [buffer] * 8
        + [pltpu.VMEM((3, SIDE, PAIR), bf16)] * 3
        + [dma] * 8
        + [pltpu.SemaphoreType.DMA((3,))] * 2
        + [pltpu.SemaphoreType.DMA((2 * half,))] * 2,
        out_shape=[
            rows(bf16),
            rows(f32),
            rows(f32),
            jax.ShapeDtypeStruct((seq, PAIR), bf16),
            jax.ShapeDtypeStruct((8, D), f32),
            gr(6),
            gr(6),
        ]
        + [jax.ShapeDtypeStruct(shape, bf16) for shape in ends],
        compiler_params=params(collective_id=1, has_side_effects=True),
        cost_estimate=cost(50),
        name="feed_forward",
    )(tokens, passes, vec, mine, cotangent, pairs, wo_other, pairs, columns, columns_x)


CHUNK = SIDE // 2
CHUNKS = 18
TAKEN = (
    ((8, 3), (10, 4), (12, 12)),
    ((3, 1), (5, 2), (7, 3), (8, 4), (9, 6), (10, 7), (11, 8), (12, 12)),
    ((1, 2), (2, 3), (5, 4), (6, 5), (7, 6), (8, 8), (9, 9), (10, 11), (12, 12)),
    ((-1, 3), (2, 5), (4, 6), (5, 7), (6, 8), (7, 12)),
)
GRAD_STEPS = 3


def last_kernel(
    small, norm_all, dq_all, dk_all, dv_all, cat, tok, pas, vec, grad_second, sums_two, second, chip, far,
    mid_near, mid_keep, output, input_grad, *rest,
):
    if small:
        late, vec_sum = rest[:2]
        rest = rest[2:]
        (
            core_out, core_in, sums, core_sums, x_in, z_in, z_out, up_in, v_out, v_in, total,
            s_core, r_core, s_sum, r_sum, s_x, r_x, s_z, r_z, s_up, r_up, s_v, r_v, ready, norm, dq, dk, dv, g_send, g_keep,
            s_own, s_res, r_res, s_in,
        ) = rest
    else:
        (
            vec_sum, send_out, keep_out, core_out, core_in, sums, core_sums, s_core, r_core, s_sum, r_sum, ready,
            norm, dq, dk, dv, g_send, g_keep, s_own, s_res, r_res, s_in,
        ) = rest
    step = pl.program_id(0)
    i = step - GRAD_STEPS
    half = core_out.shape[0]
    t, dp = lax.axis_index("tensor"), lax.axis_index("dp")
    core, side = t % 2, t // 2
    near = side * 2 + (1 - core)
    z, column = (dp // 2, dp % 2) if small else (0, 0)
    far_x = z * 2 + 1 - column
    peers = [lax.rem(dp + k, 8) for k in range(1, 8)]

    def copy(src, dst, s_sem, r_sem, to):
        return pltpu.make_async_remote_copy(
            src_ref=src, dst_ref=dst, send_sem=s_sem, recv_sem=r_sem, device_id=to, device_id_type=MESH
        )

    core_copy = lambda j: copy(core_out.at[j], core_in.at[j], s_core.at[j], r_core.at[j], {"tensor": near})
    sum_copy = lambda: copy(sums, core_sums, s_sum, r_sum, {"tensor": near})

    def rows_at(n, j, owner):
        rows = pl.ds(pl.multiple_of((owner * half + j) * ROWS, ROWS), ROWS)
        return (output, input_grad)[n].at[rows]

    own_result = lambda n, j: pltpu.make_async_copy(ready.at[n, j], rows_at(n, j, core), s_own.at[n, j])
    near_result = lambda n, j, owner: copy(
        ready.at[n, j], rows_at(n, j, owner), s_res.at[n, j], r_res.at[n, j], {"tensor": near}
    )

    def part_of(ref, k):
        return ref.at[k // 2, pl.ds((k % 2) * CHUNK, CHUNK)]

    x_copy = lambda k: copy(part_of(g_send, k), x_in.at[k], s_x.at[k], r_x.at[k], {"dp": far_x})
    z_copy = lambda k: copy(z_out.at[k], z_in.at[k], s_z.at[k], r_z.at[k], {"dp": dp - 2})
    up_copy = lambda k: copy(z_out.at[k], up_in.at[k - 6], s_up.at[k - 6], r_up.at[k - 6], {"dp": dp + 2})
    v_copy = lambda n: copy(v_out.at[peers[n]], v_in.at[dp], s_v.at[n], r_v.at[dp], {"dp": peers[n]})
    barrier = pltpu.get_barrier_semaphore()

    loads = [
        pltpu.make_async_copy(src, dst, s_in.at[n])
        for n, (src, dst) in enumerate(((norm_all, norm), (dq_all, dq), (dv_all, dv), (dk_all, dk)))
    ]

    @pl.when(step == 0)
    def _():
        for load in loads:
            load.start()
        pl.semaphore_signal(barrier, inc=1, device_id={"tensor": near}, device_id_type=MESH)
        if small:
            for peer in peers:
                pl.semaphore_signal(barrier, inc=1, device_id={"dp": peer}, device_id_type=MESH)
            late[...] = jnp.zeros_like(late)
        sums[...] = jnp.zeros_like(sums)
        sums[PASSES + 2 : PASSES + 4] = sums_two[0:2]
        pl.semaphore_wait(barrier, 8 if small else 1)

    if small:

        def term_of(k):
            rows = pl.ds(pl.multiple_of((k % 2) * CHUNK, 16), CHUNK)

            @pl.when(jnp.asarray(k) < 6)
            def _():
                x_copy(k).wait_recv()
                total[...] = g_keep[k // 2, rows, :].astype(f32) + x_in[k].astype(f32)

            @pl.when(jnp.asarray(k) >= 6)
            def _():
                total[...] = mid_keep[k // 2 - 3, rows, :].astype(f32) + mid_near[k // 2 - 3, rows, :].astype(f32)

            return total[...]

        @pl.when((step == 0) & (z == 0))
        def _():
            for k in range(6, CHUNKS):
                z_out[k] = term_of(k).astype(bf16)
                up_copy(k).start()

        @pl.when((step == 0) & (z == 3))
        def _():
            for k in (6, 7, 8, 12, 13):
                z_out[k] = term_of(k).astype(bf16)
                z_copy(k).start()

    def mine_of(grad):
        return jnp.where(side == 0, grad[:, :SIDE], grad[:, SIDE:])

    def pairs_of(grad):
        value = tn(grad, norm[...]).astype(bf16)
        return value[:, :PAIR], value[:, PAIR:]

    second_two = jnp.where(jnp.asarray(column) == 0, 1, 0)

    @pl.when(step == 0)
    def _():
        for load in loads[:3]:
            load.wait()
        both = pairs_of(jnp.where(jnp.asarray(column) == 0, mine_of(dv), mine_of(dq)))
        for m in range(2):
            g_send[second_two + m] = both[m]
        if small:
            for m in range(4):
                x_copy(2 * second_two + m).start()

    @pl.when(step == 1)
    def _():
        loads[3].wait()
        both = pairs_of(mine_of(dk))
        for place, (kept, sent) in enumerate(((0, 1), (1, 0))):

            @pl.when(jnp.asarray(column) == place)
            def _():
                g_keep[2 - 2 * place] = both[kept]
                g_send[2 * place] = both[sent]

        if small:
            for m in range(2):
                x_copy(4 * column + m).start()

    @pl.when(step == 2)
    def _():
        both = pairs_of(jnp.where(jnp.asarray(column) == 0, mine_of(dq), mine_of(dv)))
        for m in range(2):
            g_keep[1 - second_two + m] = both[m]
        if not small:
            send_out[...] = g_send[...]
            keep_out[...] = g_keep[...]

    @pl.when((i >= 0) & (i < 2 * half))
    def _():
        block = lax.rem(i + (1 - core) * half, 2 * half)
        rows = pl.ds(pl.multiple_of(block * ROWS, ROWS), ROWS)
        part = nt(dq[rows, :], cat[0]) + nt(dk[rows, :], cat[1]) + nt(dv[rows, :], cat[2])

        @pl.when(i < half)
        def _():
            core_out[i] = part.astype(bf16)
            core_copy(i).start()

        @pl.when(i >= half)
        def _():
            j = i - half
            hat, root = hat_of(embedded(tok[...], pas[...], vec[...]))
            core_copy(j).wait_recv()
            grad = part + core_in[j].astype(f32)
            result = grad_second[...] + norm_back(hat, root, grad, vec[PASSES : PASSES + 1])
            ready[0, j] = (second[...] + (chip[...].astype(f32) + far[...].astype(f32))).astype(bf16)
            ready[1, j] = result.astype(bf16)
            for n in range(2):
                own_result(n, j).start()
                near_result(n, j, core).start()
            chosen = one_hot(pas[...])
            high, mid, _ = split_three(result)
            sums[...] += nn(chosen, high) + nn(chosen, mid)
            sums[PASSES : PASSES + 1] += jnp.sum(grad * hat, axis=0, keepdims=True)
            sums[PASSES + 1 : PASSES + 2] += jnp.sum(grad, axis=0, keepdims=True)

    @pl.when(i == 2 * half - 1)
    def _():
        sum_copy().start()

    if small:

        def keep_late(k, pair, total):
            late[pair, pl.ds(pl.multiple_of((k % 2) * CHUNK, 16), CHUNK), :] = total

        def pass_on(k):
            term = term_of(k)

            @pl.when(z < 3)
            def _():
                z_copy(k).wait_recv()

            below = jnp.where(z < 3, z_in[k].astype(f32), 0.0)
            passed = term + below

            @pl.when((z > 1) | ((z == 1) & (k < 6)))
            def _():
                z_out[k] = passed.astype(bf16)
                z_copy(k).start()

            @pl.when(z == 0)
            def _():
                keep_late(k, k // 2, passed)

            @pl.when((z == 1) & (k >= 6))
            def _():
                up_copy(k).wait_recv()
                keep_late(k, k // 2 - 3, passed + up_in[k - 6].astype(f32))

        def at_position(p, carry):
            k = jnp.where(p < 3, p + 6, jnp.where(p < 9, lax.rem(p + 3 + 2 * column, 6), p))

            @pl.when((z > 0) | (k < 6))
            def _():
                pass_on(k)

            return carry

        begin, end = jnp.int32(0), jnp.int32(0)
        for place, line in enumerate(TAKEN):
            for at, upto in line:
                begin = jnp.where((z == place) & (step > at), upto, begin)
                end = jnp.where((z == place) & (step >= at), upto, end)
        lax.fori_loop(begin, end, at_position, 0)

        @pl.when((step == 7) & (z == 3))
        def _():
            for k in range(14, CHUNKS):
                z_out[k] = term_of(k).astype(bf16)
                z_copy(k).start()

        for at, first_chunk, upto in ((9, 12, 15), (10, 15, 18)):

            @pl.when((step == at) & (z == 1))
            def _(first_chunk=first_chunk, upto=upto):
                for k in range(first_chunk, upto):
                    up_copy(k).wait_recv()
                    z_out[k] = (term_of(k) + up_in[k - 6].astype(f32)).astype(bf16)
                    up_copy(k).start()

        @pl.when((step == pl.num_programs(0) - 1) & (z == 2))
        def _():
            for k in range(12, CHUNKS):
                z_copy(k).wait_recv()
                up_copy(k).wait_recv()
                keep_late(k, k // 2 - 6, term_of(k) + z_in[k].astype(f32) + up_in[k - 6].astype(f32))

    @pl.when(i == 2 * half)
    def _():
        sum_copy().wait_recv()
        total = sums[...] + core_sums[...]
        if small:
            wide = D // 8
            for d in range(8):
                v_out[d, :, 0:wide] = total[:, d * wide : (d + 1) * wide]
                v_out[d, :, wide:] = jnp.zeros((16, 128 - wide), f32)
            for n in range(7):
                v_copy(n).start()
        else:
            vec_sum[...] = total

    @pl.when(step == pl.num_programs(0) - 1)
    def _():
        for j in range(half):
            core_copy(j).wait_send()
            for n in range(2):
                own_result(n, j).wait()
                near_result(n, j, core).wait_send()
                near_result(n, j, 1 - core).wait_recv()
        sum_copy().wait_send()
        if small:
            for peer in peers:
                copy(v_out.at[0], v_in.at[peer], s_v.at[0], r_v.at[peer], {"dp": far_x}).wait_recv()
            v_in[dp] = v_out[dp]
            total = v_in[0]
            for d in range(1, 8):
                total = total + v_in[d]
            vec_sum[...] = total
            for n in range(7):
                v_copy(n).wait_send()
            for k in range(CHUNKS):
                if k < 6:
                    x_copy(k).wait_send()
                    pl.when(z > 0)(z_copy(k).wait_send)
                elif k < 12:
                    pl.when(z > 1)(z_copy(k).wait_send)
                    pl.when(z == 0)(up_copy(k).wait_send)
                else:
                    pl.when(z == 3)(z_copy(k).wait_send)
                    pl.when(z < 2)(up_copy(k).wait_send)


def last(
    small, norm, dq, dk, dv, cat, tokens, passes, vec, grad_second, sums_two, second, chip, far, mid_near, mid_keep
):
    seq = dq.shape[0]
    half = seq // ROWS // 2
    core = lambda: lax.axis_index("tensor") % 2

    own = lambda i: jnp.clip(i - GRAD_STEPS - half, 0, half - 1)
    mine = pl.BlockSpec((ROWS, D), lambda i: (own(i), 0))
    dma = pltpu.SemaphoreType.DMA
    out_specs = [pl.BlockSpec(memory_space=pl.ANY)] * 2
    out_shape = [jax.ShapeDtypeStruct((seq, D), bf16)] * 2
    scratch = [
        pltpu.VMEM((half, ROWS, D), bf16),
        pltpu.VMEM((half, ROWS, D), bf16),
        pltpu.VMEM((16, D), f32),
        pltpu.VMEM((16, D), f32),
    ]
    sems = [dma((half,)), dma((half,)), dma, dma]
    if small:
        out_specs += [full((3, SIDE, PAIR)), full((16, 128))]
        out_shape += [
            jax.ShapeDtypeStruct((3, SIDE, PAIR), f32),
            jax.ShapeDtypeStruct((16, 128), f32),
        ]
        scratch += [pltpu.VMEM((CHUNKS, CHUNK, PAIR), bf16)] * 3
        scratch += [pltpu.VMEM((12, CHUNK, PAIR), bf16)]
        scratch += [pltpu.VMEM((8, 16, 128), f32)] * 2 + [pltpu.VMEM((CHUNK, PAIR), f32)]
        sems += [dma((6,))] * 2 + [dma((CHUNKS,))] * 2 + [dma((12,))] * 2 + [dma((7,)), dma((8,))]
    else:
        out_specs += [full((16, D)), full((3, SIDE, PAIR)), full((3, SIDE, PAIR))]
        out_shape += [jax.ShapeDtypeStruct((16, D), f32)] + [jax.ShapeDtypeStruct((3, SIDE, PAIR), bf16)] * 2
    scratch_more = [pltpu.VMEM((2, half, ROWS, D), bf16), pltpu.VMEM((seq, D), bf16)]
    scratch_more += [pltpu.VMEM((seq, PAIR), bf16)] * 3
    scratch_more += [pltpu.VMEM((3, SIDE, PAIR), bf16)] * 2 + [dma((2, half))] * 3 + [dma((4,))]
    return pl.pallas_call(
        functools.partial(last_kernel, small),
        grid=(GRAD_STEPS + 2 * half + 2,),
        in_specs=[
            *[pl.BlockSpec(memory_space=pl.ANY)] * 4,
            full(cat.shape),
            pl.BlockSpec((ROWS, D), lambda i: (core() * half + own(i), 0)),
            pl.BlockSpec((1, ROWS), lambda i: (0, core() * half + own(i))),
            full((16, D)),
            mine,
            full((8, D)),
            mine,
            mine,
            mine,
            full(mid_near.shape),
            full(mid_keep.shape),
        ],
        out_specs=out_specs,
        out_shape=out_shape,
        scratch_shapes=scratch + sems + scratch_more,
        compiler_params=params(collective_id=2, has_side_effects=True),
        cost_estimate=cost(38),
        name="last",
    )(norm, dq, dk, dv, cat, tokens, passes, vec, grad_second, sums_two, second, chip, far, mid_near, mid_keep)


def precondition(grad, weight, left, right, left_root, right_root):
    high = lax.Precision.HIGHEST
    left_new = decay * left + (1.0 - decay) * jnp.einsum(
        "...ij,...kj->...ik", grad, grad, precision=high
    )
    right_new = decay * right + (1.0 - decay) * jnp.einsum(
        "...ji,...jk->...ik", grad, grad, precision=high
    )
    half = jnp.einsum("...ij,...jk->...ik", left_root, grad, precision=high)
    step = jnp.einsum("...ij,...jk->...ik", half, right_root, precision=high)
    return (left_new, right_new, step, weight - rate_matrix * step)


def two_part(value):
    high = value.astype(bf16)
    return high, (value - high.astype(f32)).astype(bf16)


def dot_three(dot, a, b):
    return dot(a[0], b[0]) + (dot(a[0], b[1]) + dot(a[1], b[0]))


def renew_kernel(
    late, own, one, two, three, weight, left, right, left_root, right_root, output, input_grad, vec_sum, vec, moment,
    left_new, right_new, step, new, output_new, input_grad_new, vec_grad, moment_new, vec_new,
):
    @pl.when(pl.program_id(0) == 0)
    def _():
        rows, wide = vec.shape
        grad = vec_sum[:rows, :wide]
        square = decay * moment[...] + (1.0 - decay) * grad * grad
        vec_grad[...] = grad
        moment_new[...] = square
        vec_new[...] = vec[...] - rate_vector * grad / (jnp.sqrt(square) + moment_eps)

    output_new[...] = output[...]
    input_grad_new[...] = input_grad[...]

    @pl.when(pl.program_id(0) < 3)
    def _():
        early = own[0].astype(f32) + one[0].astype(f32) + two[0].astype(f32) + three[0].astype(f32)
        z = lax.axis_index("dp") // 2
        both = late[0] + jnp.where(z > 2, early, 0.0)
        for n in range(2):
            grad = both[:, n * SIDE : (n + 1) * SIDE]
            grad = two_part(jnp.where(z == 0, grad.T, grad))
            left_new[0, n] = decay * left[0, n] + (1.0 - decay) * dot_three(nt, grad, grad)
            right_new[0, n] = decay * right[0, n] + (1.0 - decay) * dot_three(tn, grad, grad)
            half = dot_three(nn, two_part(left_root[0, n]), grad)
            value = dot_three(nn, two_part(half), two_part(right_root[0, n]))
            step[0, n] = value
            new[0, n] = weight[0, n] - rate_matrix * value


def renew(late, own, far, weight, left, right, left_root, right_root, output, input_grad, vec_sum, vec, moment):
    pair = pl.BlockSpec((1, SIDE, PAIR), lambda i: (jnp.minimum(i, 2), 0, 0))
    slot = pl.BlockSpec((1, 2, SIDE, SIDE), lambda i: (0, jnp.minimum(i, 2), 0, 0))
    rows = pl.BlockSpec((output.shape[0] // 4, D), lambda i: (i, 0))
    return pl.pallas_call(
        renew_kernel,
        grid=(4,),
        in_specs=[pair] * 5 + [slot] * 5 + [rows] * 2 + [full(vec_sum.shape)] + [full(vec.shape)] * 2,
        out_specs=[slot] * 4 + [rows] * 2 + [full(vec.shape)] * 3,
        out_shape=[jax.ShapeDtypeStruct(weight.shape, f32)] * 4
        + [jax.ShapeDtypeStruct(value.shape, value.dtype) for value in (output, input_grad, vec, vec, vec)],
        compiler_params=params(46),
        cost_estimate=cost(8),
        name="renew",
    )(late, own, *far, weight, left, right, left_root, right_root, output, input_grad, vec_sum, vec, moment)


def to_pairs(blocks):
    n = blocks.shape[0] // 2
    return blocks.reshape(n, 2, SIDE, SIDE).transpose(0, 2, 1, 3).reshape(n, SIDE, PAIR)


def from_pairs(pairs):
    n = pairs.shape[0]
    return pairs.reshape(n, SIDE, 2, SIDE).transpose(0, 2, 1, 3).reshape(2 * n, SIDE, SIDE)


def swap(value, bit):
    return lax.ppermute(value, "tensor", [(t, t ^ bit) for t in range(NT)])


def hop_x(value):
    return lax.ppermute(value, "dp", [(d, d ^ 1) for d in range(8)])


def hop_z(value, turn, ends):
    pairs = [(d, (d + 2 * turn) % 8) for d in range(8) if (d // 2 + turn) % 4 in ends]
    return lax.ppermute(value, "dp", pairs)


def tie(*values):
    return lax.optimization_barrier(values)


def on_device(
    tokens,
    pass_ids,
    doc_lengths,
    cotangent,
    block_weights,
    vector_params,
    vector_moment,
    block_left,
    block_right,
    block_left_root,
    block_right_root,
):
    t, dp = lax.axis_index("tensor"), lax.axis_index("dp")
    core, side = t % 2, t // 2
    n_dp = lax.axis_size("dp")
    small = n_dp == 8
    z, column = (dp // 2, dp % 2) if small else (0, 0)
    lens = doc_lengths[0]
    seq = tokens.shape[0]
    passes = pass_ids.reshape(1, seq)
    total_blocks = (D // SIDE) * (4 + 2 * (FF // D))
    slots = block_weights.shape[1] * n_dp

    if small:
        pairs, columns, wo_other, vec, norm, q, k, v, cat = gather(
            block_weights, vector_params, tokens, passes
        )
        columns_x = hop_x(columns)
    else:
        every = lax.all_gather(block_weights.astype(bf16), "dp", axis=1, tiled=True)[0]
        near = to_pairs(every[:total_blocks])
        far = swap(near, 2)
        pairs = jnp.where(side == 0, jnp.stack([near, far]), jnp.stack([far, near]))
        vec = lax.all_gather(vector_params, "dp", axis=1, tiled=True)
        vec = jnp.pad(vec, ((0, 16 - vec.shape[0]), (0, 0)))
        wo_other = swap(pairs[:, 6:8], 1)
        columns = jnp.concatenate([near[12:15], near[18:21]], axis=0)
        columns_x = jnp.concatenate([near[15:18], near[21:24]], axis=0)
        norm, q, k, v, cat = project(tokens, passes, vec, pairs)
    mine, lse = attend(lens, q, k, v)
    out_chip, second, grad_second, grad_mixed, sums_two, mid_send, mid_keep, *ends = feed(
        small, tokens, passes, vec, mine, cotangent, pairs, wo_other, columns, columns_x
    )
    out_far = swap(out_chip, 2)
    if small:
        far = [hop_z(ends[turn], turn, (3,)) for turn in (1, 2, 3)]
        mid_send = hop_x(mid_send)
    dq, dk, dv = attend_back(lens, q, k, v, mine, lse, grad_mixed)
    if small:
        *far, out_far, mid_send, dq = tie(*far, out_far, mid_send, dq)
    output, input_grad, *sums = last(
        small, norm, dq, dk, dv, cat, tokens, passes, vec, grad_second, sums_two, second, out_chip, out_far,
        mid_send, mid_keep,
    )
    if small:
        late, vector_sum = sums
        return_blocks = renew(
            late, ends[0], far, block_weights, block_left, block_right, block_left_root, block_right_root,
            output, input_grad, vector_sum, vector_params, vector_moment,
        )
        left_new, right_new, step, weight_new, output, input_grad, vector_grad, moment_new, vector_new = return_blocks
    else:
        vector_part, g_send, g_keep = sums[0][: PASSES + 4], *sums[1:]
        send, keep = ends
        rest = jnp.stack(
            [
                jnp.concatenate([mid_keep, keep]).reshape(3, 3, SIDE, PAIR),
                jnp.concatenate([mid_send, send]).reshape(3, 3, SIDE, PAIR),
            ],
            axis=1,
        )
        grad_qkv = from_pairs(jnp.concatenate([g_keep, g_send], axis=0)).swapaxes(1, 2)
        grad_rest = from_pairs(rest.reshape(18, SIDE, PAIR))
        spare = jnp.zeros((slots - total_blocks, SIDE, SIDE), bf16)
        grad_blocks = jnp.concatenate([grad_qkv, grad_rest, spare], axis=0)[None].astype(f32)
        owned = lax.psum_scatter(grad_blocks, "dp", scatter_dimension=1, tiled=True)
        vector_grad = lax.psum_scatter(vector_part, "dp", scatter_dimension=1, tiled=True)
        left_new, right_new, step, weight_new = precondition(
            owned, block_weights, block_left, block_right, block_left_root, block_right_root
        )
        moment_new = decay * vector_moment + (1.0 - decay) * vector_grad * vector_grad
        vector_new = vector_params - rate_vector * vector_grad / (jnp.sqrt(moment_new) + moment_eps)
    return (
        output,
        input_grad,
        left_new,
        right_new,
        step,
        weight_new,
        vector_grad,
        moment_new,
        vector_new,
    )


def solution(mesh):
    rows, line = P("dp", None), P(None, "dp")
    block = P("tensor", "dp", None, None)
    return jax.shard_map(
        on_device,
        mesh=mesh,
        in_specs=(rows, P("dp"), rows, rows, block, line, line, block, block, block, block),
        out_specs=(rows, rows, block, block, block, block, line, line, line),
        check_vma=False,
    )
```

```python
import functools

import jax
import jax.numpy as jnp
from jax import lax
from jax.experimental import pallas as pl
from jax.experimental.pallas import tpu as pltpu
from jax.sharding import PartitionSpec as P

D = 768
HD = 64
FF = 3072
PASSES = 5
SIDE = 192
PAIR = 2 * SIDE
ROWS = 256
WIDE = 512
DOCS = 8
NT = 4

norm_eps = 1e-05
moment_eps = 1e-08
rate_matrix = 0.03
rate_vector = 0.2
decay = 0.5
gelu_coef = 0.7978845608028654
masked_score = -1e30
f32 = jnp.float32
bf16 = jnp.bfloat16
MESH = pl.DeviceIdType.MESH


def nn(a, b):
    return lax.dot_general(a, b, (((1,), (0,)), ((), ())), preferred_element_type=f32)


def nt(a, b):
    return lax.dot_general(a, b, (((1,), (1,)), ((), ())), preferred_element_type=f32)


def tn(a, b):
    return lax.dot_general(a, b, (((0,), (0,)), ((), ())), preferred_element_type=f32)


def split_three(value):
    high = value.astype(bf16)
    rest = value - high.astype(f32)
    mid = rest.astype(bf16)
    return high, mid, (rest - mid.astype(f32)).astype(bf16)


def one_hot(pass_row):
    kinds = lax.broadcasted_iota(jnp.int32, (16, pass_row.shape[1]), 0)
    return (kinds == pass_row).astype(f32).astype(bf16)


def embedded(tokens, pass_row, vec):
    chosen = jnp.concatenate([one_hot(pass_row)] * 3, axis=0)
    return tokens.astype(f32) + tn(chosen, jnp.concatenate(split_three(vec), axis=0))


def hat_of(hidden):
    mean = jnp.mean(hidden, axis=-1, keepdims=True)
    center = hidden - mean
    spread = jnp.mean(center * center, axis=-1, keepdims=True)
    root = lax.rsqrt(spread + norm_eps)
    return center * root, root


def norm_back(hat, root, grad, gain):
    scaled = grad * gain
    first = jnp.mean(scaled, axis=-1, keepdims=True)
    second = jnp.mean(scaled * hat, axis=-1, keepdims=True)
    return root * (scaled - first - hat * second)


def params(mebibytes=56, **kw):
    return pltpu.CompilerParams(vmem_limit_bytes=mebibytes * 1024 * 1024, **kw)


def cost(micros):
    return pl.CostEstimate(flops=int(micros * 1.1e9), bytes_accessed=int(micros * 1e6), transcendentals=0)


def full(shape):
    return pl.BlockSpec(shape, lambda *_: (0,) * len(shape))


def gather_kernel(
    own, vec_own, tokens, passes,
    all_pairs, columns, wo_other, vec_out, norm, q, k_out, v, cat,
    pack, vec_pack, vec_land, wq, tok, norm_s, qkv_s, cat_s, *sems,
):
    (
        s_z1, r_z1, s_x1, r_x1, s_y1, r_y1, s_d1, r_d1, s_l, r_l, s_r, r_r, s_x2, r_x2, s_y2, r_y2, s_v, r_v, s_c, r_c,
        s_out, s_cat, s_tok, loc,
    ) = sems
    dp, t = lax.axis_index("dp"), lax.axis_index("tensor")
    z, x = dp // 2, dp % 2
    y, core = t // 2, t % 2
    far_x, far_y, near = z * 2 + (1 - x), (1 - y) * 2 + core, y * 2 + (1 - core)

    barrier = pltpu.get_barrier_semaphore()
    peers = [lax.rem(dp + n, 8) for n in range(1, 8)]
    for peer in peers:
        pl.semaphore_signal(barrier, inc=1, device_id={"dp": peer}, device_id_type=MESH)
    for to in (far_y, near):
        pl.semaphore_signal(barrier, inc=1, device_id={"tensor": to}, device_id_type=MESH)

    tok_copy = pltpu.make_async_copy(tokens, tok, s_tok)
    tok_copy.start()
    for m in range(3):
        pair = jnp.concatenate([own[0, 2 * m], own[0, 2 * m + 1]], axis=1).astype(bf16)
        pack[m] = pair

        @pl.when(z == 0)
        def _():
            wq[y, 3 * x + m] = pair

    vec_pack[...] = jnp.zeros_like(vec_pack)
    vec_pack[0 : PASSES + 4, 0 : D // 8] = vec_own[...]
    pl.semaphore_wait(barrier, 9)

    started = []

    def send(src, dst, s_sem, r_sem, to, cond=None):
        copy = pltpu.make_async_remote_copy(
            src_ref=src, dst_ref=dst, send_sem=s_sem, recv_sem=r_sem, device_id=to, device_id_type=MESH
        )
        started.append((cond, copy))
        if cond is None:
            copy.start()
        else:
            pl.when(cond)(copy.start)

    def arrived(dst, r_sem, cond=None):
        copy = pltpu.make_async_remote_copy(
            src_ref=dst, dst_ref=dst, send_sem=loc, recv_sem=r_sem, device_id={"dp": far_x}, device_id_type=MESH
        )
        if cond is None:
            copy.wait_recv()
        else:
            pl.when(cond)(copy.wait_recv)

    to_x, to_y, to_left, to_right = {"dp": far_x}, {"tensor": far_y}, {"dp": dp - 2}, {"dp": dp + 2}
    half = SIDE // 2

    def piece(side, column, k):
        return wq.at[side, 3 * column + k // 2, pl.ds((k % 2) * half, half)]

    def at_one(m):
        return all_pairs.at[y, 6 + 3 * x + m]

    def at_z(d, m):
        return columns.at[3 * (z + d - 2) + m]

    own_one = pltpu.make_async_copy(pack, all_pairs.at[y, pl.ds(6 + 3 * x, 3)], loc)
    own_more = pltpu.make_async_copy(pack, columns.at[pl.ds(3 * (z - 2), 3)], loc)
    pl.when(z == 1)(own_one.start)
    pl.when(z > 1)(own_more.start)

    for m in range(3):
        send(pack.at[m], at_one(m), s_l.at[0, m], r_l.at[0, m], to_left, z == 1)
        send(pack.at[m], at_z(0, m), s_l.at[0, m], r_l.at[0, m], to_left, z > 1)
    for n, peer in enumerate(peers):
        send(vec_pack, vec_land.at[dp], s_v.at[n], r_v.at[dp], {"dp": peer})
    send(pack.at[0], at_z(0, 0), s_r.at[0, 0], r_r.at[0, 0], to_right, z == 2)
    send(pack.at[0], at_one(0), s_x2.at[0], r_x2.at[0], to_x, z == 1)

    def diagonal(k):
        if k % 2 == 0:
            arrived(piece(y, 1 - x, k), r_x1.at[k])
            send(piece(y, 1 - x, k), piece(y, 1 - x, k), s_d1.at[k], r_d1.at[k], to_y)
        else:
            arrived(piece(1 - y, x, k), r_y1.at[k])
            send(piece(1 - y, x, k), piece(1 - y, x, k), s_d1.at[k], r_d1.at[k], to_x)

    def from_right(d, m):
        arrived(columns.at[m], r_l.at[d - 1, m], z + d < 4)
        if d < 3:
            send(at_z(d, m), at_z(d, m), s_l.at[d, m], r_l.at[d, m], to_left, (z + d < 4) & (z > 0))

    def along_x(m, cond):
        send(at_one(m), at_one(m), s_x2.at[m], r_x2.at[m], to_x, cond)

    def from_left(d, m):
        arrived(columns.at[m], r_r.at[d - 1, m], z > d)
        if d == 1:
            send(at_one(m), at_one(m), s_r.at[1, m], r_r.at[1, m], to_right, z == 2)
        along_x(m, z == d + 1)

    for k in range(6):
        arrived(piece(y, x, k), r_z1.at[k], z > 0)
        send(piece(y, x, k), piece(y, x, k), s_z1.at[k], r_z1.at[k], to_right, z < 3)
        send(piece(y, x, k), piece(y, x, k), s_x1.at[k], r_x1.at[k], to_x)
        send(piece(y, x, k), piece(y, x, k), s_y1.at[k], r_y1.at[k], to_y)
        if k == 5:
            for m in range(3):
                send(pack.at[m], at_one(m), s_r.at[0, m], r_r.at[0, m], to_right, z == 1)
                if m > 0:
                    send(pack.at[m], at_z(0, m), s_r.at[0, m], r_r.at[0, m], to_right, z == 2)
                    send(pack.at[m], at_one(m), s_x2.at[m], r_x2.at[m], to_x, z == 1)
        if k >= 1:
            diagonal(k - 1)
        if k % 2 == 1:
            from_right(1, k // 2)
    diagonal(5)
    pl.when(z == 1)(own_one.wait)
    pl.when(z > 1)(own_more.wait)
    for m in range(3):
        along_x(m, z == 0)
    for m in range(3):
        from_left(1, m)
        from_right(2, m)
    for k in range(6):
        if k % 2 == 0:
            arrived(piece(1 - y, x, k), r_y1.at[k])
        else:
            arrived(piece(y, 1 - x, k), r_x1.at[k])
        arrived(piece(1 - y, 1 - x, k), r_d1.at[k])
    for peer in peers:
        arrived(vec_land.at[peer], r_v.at[peer])
    vec_land[dp] = vec_pack[...]
    vec = jnp.concatenate([vec_land[d][:, : D // 8] for d in range(8)], axis=1)
    vec_out[...] = vec
    for n in range(3):
        for i in range(4):
            at = (i % 2) * SIDE
            parts = [wq[h, 2 * n + i // 2][:, at : at + SIDE] for h in range(2)]
            cat_s[n, i * SIDE : (i + 1) * SIDE, :] = jnp.concatenate(parts, axis=1)
    writes = [pltpu.make_async_copy(cat_s, cat, s_cat)]
    writes[0].start()
    tok_copy.wait()

    def rows_of(b):
        rows = slice(b * WIDE, (b + 1) * WIDE)
        hat, _ = hat_of(embedded(tok[rows, :], passes[:, rows], vec))
        low = (hat * vec[PASSES : PASSES + 1] + vec[PASSES + 1 : PASSES + 2]).astype(bf16)
        norm_s[rows, :] = low
        writes.append(pltpu.make_async_copy(norm_s.at[rows, :], norm.at[rows, :], s_out.at[b, 3]))
        writes[-1].start()
        for n, out in enumerate((q, k_out, v)):
            qkv_s[n, rows, :] = nn(low, cat_s[n]).astype(bf16)
            writes.append(pltpu.make_async_copy(qkv_s.at[n, rows, :], out.at[rows, :], s_out.at[b, n]))
            writes[-1].start()

    count = tok.shape[0] // WIDE
    for b in range(count):
        rows_of(b)
        if b == 0:
            for m in range(3):
                from_left(2, m)
                from_right(3, m)
        if b == 1:
            for m in range(2):
                ref = all_pairs.at[y, 6 + m]
                arrived(ref, r_x2.at[m], x == 1)
                send(ref, ref, s_y2.at[m], r_y2.at[m], to_y)
                send(ref, wo_other.at[y, m], s_c.at[0, m], r_c.at[y, m], {"tensor": near})
    for m in range(2):
        ref = all_pairs.at[1 - y, 6 + m]
        arrived(ref, r_y2.at[m])
        send(ref, wo_other.at[1 - y, m], s_c.at[1, m], r_c.at[1 - y, m], {"tensor": near})
    for m in range(3):
        arrived(all_pairs.at[y, 6 + 3 * (1 - x) + m], r_x2.at[m], None if m == 2 else x == 0)
    for h in range(2):
        for m in range(2):
            arrived(wo_other.at[h, m], r_c.at[h, m])
    for copy in writes:
        copy.wait()
    for cond, copy in started:
        if cond is None:
            copy.wait_send()
        else:
            pl.when(cond)(copy.wait_send)


def gather(block_weights, vector_params, tokens, passes):
    seq = tokens.shape[0]
    dma = pltpu.SemaphoreType.DMA
    sizes = [(6,)] * 8 + [(3, 3)] * 2 + [(2, 3)] * 2 + [(3,)] * 2 + [(2,)] * 2 + [(7,), (8,)] + [(2, 2)] * 2
    sizes += [(seq // WIDE, 4)]
    vmem, far = pl.BlockSpec(memory_space=pltpu.VMEM), pl.BlockSpec(memory_space=pl.ANY)
    wide = jax.ShapeDtypeStruct((seq, PAIR), bf16)
    return pl.pallas_call(
        gather_kernel,
        in_specs=[vmem, vmem, far, vmem],
        out_specs=[far, far, far, vmem, far, far, far, far, far],
        out_shape=[
            jax.ShapeDtypeStruct((2, 24, SIDE, PAIR), bf16),
            jax.ShapeDtypeStruct((6, SIDE, PAIR), bf16),
            jax.ShapeDtypeStruct((2, 2, SIDE, PAIR), bf16),
            jax.ShapeDtypeStruct((16, D), f32),
            jax.ShapeDtypeStruct((seq, D), bf16),
            wide,
            wide,
            wide,
            jax.ShapeDtypeStruct((3, D, PAIR), bf16),
        ],
        scratch_shapes=[
            pltpu.VMEM((3, SIDE, PAIR), bf16),
            pltpu.VMEM((16, 128), f32),
            pltpu.VMEM((8, 16, 128), f32),
            pltpu.VMEM((2, 6, SIDE, PAIR), bf16),
            pltpu.VMEM((seq, D), bf16),
            pltpu.VMEM((seq, D), bf16),
            pltpu.VMEM((3, seq, PAIR), bf16),
            pltpu.VMEM((3, D, PAIR), bf16),
        ]
        + [dma(size) for size in sizes]
        + [dma] * 3,
        compiler_params=params(collective_id=0, has_side_effects=True),
        cost_estimate=cost(60),
        name="gather",
    )(block_weights, vector_params, tokens, passes)


def project_kernel(tok, pas, vec, wq, norm, q, k, v, cat):
    @pl.when(pl.program_id(0) == 0)
    def _():
        for x in range(3):
            for i in range(4):
                at = (i % 2) * SIDE
                parts = [wq[h, 2 * x + i // 2][:, at : at + SIDE] for h in range(2)]
                cat[x, i * SIDE : (i + 1) * SIDE, :] = jnp.concatenate(parts, axis=1)

    first = embedded(tok[...], pas[...], vec[...])
    hat, _ = hat_of(first)
    low = (hat * vec[PASSES : PASSES + 1] + vec[PASSES + 1 : PASSES + 2]).astype(bf16)
    norm[...] = low
    for x, out in enumerate((q, k, v)):
        out[...] = nn(low, cat[x]).astype(bf16)


def project(tokens, passes, vec, wq):
    seq = tokens.shape[0]
    row = lambda n: pl.BlockSpec((WIDE, n), lambda i: (i, 0))
    wide = jax.ShapeDtypeStruct((seq, PAIR), bf16)
    return pl.pallas_call(
        project_kernel,
        grid=(seq // WIDE,),
        in_specs=[
            row(D),
            pl.BlockSpec((1, WIDE), lambda i: (0, i)),
            full((16, D)),
            full((2, 6, SIDE, PAIR)),
        ],
        out_specs=[row(D), row(PAIR), row(PAIR), row(PAIR), full((3, D, PAIR))],
        out_shape=[
            jax.ShapeDtypeStruct((seq, D), bf16),
            wide,
            wide,
            wide,
            jax.ShapeDtypeStruct((3, D, PAIR), bf16),
        ],
        compiler_params=params(),
        cost_estimate=cost(16),
        name="project",
    )(tokens, passes, vec, wq)


def doc_state(lens, base):
    rows = base + lax.broadcasted_iota(jnp.int32, (1, ROWS), 1)
    rows = jnp.concatenate([rows, rows], axis=1)
    begin = jnp.int32(0)
    first = jnp.int32(0)
    starts = jnp.zeros((1, 2 * ROWS), jnp.int32)
    for c in range(DOCS):
        starts = jnp.where(rows >= begin, begin, starts)
        first = jnp.where(base >= begin, begin, first)
        begin = begin + lens[c]
    return rows, starts, first


def two_heads(block):
    left = lax.broadcasted_iota(jnp.int32, block.shape, 1) < HD
    none = jnp.zeros_like(block)
    return jnp.concatenate([jnp.where(left, block, none), jnp.where(left, none, block)], axis=0)


def one_above(both):
    return jnp.concatenate([both[:HD, :ROWS], both[HD:, ROWS:]], axis=0).T


def attend_kernel(lens, q, k, v, out, lse, acc):
    i = pl.program_id(0)
    base = i * ROWS
    rows, starts, first = doc_state(lens, base)
    pairs = [two_heads(q[:, p * 128 : (p + 1) * 128] * bf16(0.125)) for p in range(3)]
    for p in range(3):
        acc[p] = jnp.zeros((128, 2 * ROWS), f32)

    def step(j, carry):
        at = pl.multiple_of(j * ROWS, ROWS)
        keys = at + lax.broadcasted_iota(jnp.int32, (ROWS, 2 * ROWS), 0)
        seen = (keys >= starts) & (keys <= rows)
        here = pl.ds(at, ROWS)
        head = lambda p: slice(p * 128, (p + 1) * 128)
        scores = [jnp.where(seen, nt(k[here, head(p)], pairs[p]), masked_score) for p in range(3)]
        state = []
        for p in range(3):
            before, total = carry[2 * p], carry[2 * p + 1]
            now = jnp.maximum(before, jnp.max(scores[p], axis=0, keepdims=True))
            probs = jnp.exp(scores[p] - now)
            fade = jnp.exp(before - now)
            state += [now, total * fade + jnp.sum(probs, axis=0, keepdims=True)]
            acc[p] = acc[p] * fade + tn(v[here, head(p)], probs.astype(bf16))
        return tuple(state)

    zero = jnp.zeros((1, 2 * ROWS), f32)
    state = lax.fori_loop(first // ROWS, i + 1, step, (zero + masked_score, zero) * 3)
    lines = []
    for p in range(3):
        top, total = state[2 * p], state[2 * p + 1]
        out[:, p * 128 : (p + 1) * 128] = one_above(acc[p] / total).astype(bf16)
        line = top + jnp.log(total)
        lines += [line[:, :ROWS], line[:, ROWS:]]
    lse[...] = jnp.concatenate(lines + lines[:2], axis=0)


def attend(lens, q, k, v):
    seq = q.shape[0]
    row = pl.BlockSpec((ROWS, PAIR), lambda i, s: (i, 0))
    return pl.pallas_call(
        attend_kernel,
        grid_spec=pltpu.PrefetchScalarGridSpec(
            num_scalar_prefetch=1,
            grid=(seq // ROWS,),
            in_specs=[row, full((seq, PAIR)), full((seq, PAIR))],
            out_specs=[row, pl.BlockSpec((8, ROWS), lambda i, s: (0, i))],
            scratch_shapes=[
                pltpu.VMEM((3, 128, 2 * ROWS), f32),
            ],
        ),
        out_shape=[
            jax.ShapeDtypeStruct((seq, PAIR), bf16),
            jax.ShapeDtypeStruct((8, seq), f32),
        ],
        compiler_params=params(),
        cost_estimate=cost(30),
        name="attend",
    )(lens, q, k, v)


def attend_back_kernel(
    lens, q, k, v, mixed, lse, grad_mixed, dq, dk, dv, dk_acc, dv_acc, dq_acc
):
    i = pl.program_id(0)
    count = pl.num_programs(0)
    base = i * ROWS

    @pl.when(i == 0)
    def _():
        dk_acc[...] = jnp.zeros_like(dk_acc)
        dv_acc[...] = jnp.zeros_like(dv_acc)

    rows, starts, first = doc_state(lens, base)
    heads = lax.broadcasted_iota(jnp.int32, (8, 128), 0)
    lanes = lax.broadcasted_iota(jnp.int32, (8, 128), 1)
    pick = (lanes // HD == heads).astype(f32).astype(bf16)
    queries, grads, inner, lines = [], [], [], []
    for p in range(3):
        cols = slice(p * 128, (p + 1) * 128)
        queries.append(two_heads(q[:, cols] * bf16(0.125)))
        grads.append(two_heads(grad_mixed[:, cols]))
        product = grad_mixed[:, cols].astype(f32) * mixed[:, cols].astype(f32)
        high, low, _ = split_three(product)
        sums = nt(pick, high) + nt(pick, low)
        inner.append(jnp.concatenate([sums[0:1], sums[1:2]], axis=1))
        lines.append(jnp.concatenate([lse[2 * p : 2 * p + 1], lse[2 * p + 1 : 2 * p + 2]], axis=1))
        dq_acc[p] = jnp.zeros((128, 2 * ROWS), f32)

    def step(j, carry):
        at = pl.multiple_of(j * ROWS, ROWS)
        keys = at + lax.broadcasted_iota(jnp.int32, (ROWS, 2 * ROWS), 0)
        seen = (keys >= starts) & (keys <= rows)
        here = pl.ds(at, ROWS)
        for p in range(3):
            cols = slice(p * 128, (p + 1) * 128)
            kb = k[here, cols]
            scores = jnp.where(seen, nt(kb, queries[p]) - lines[p], masked_score)
            probs = jnp.exp(scores)
            grad_probs = nt(v[here, cols], grads[p])
            grad_scores = (probs * (grad_probs - inner[p])).astype(bf16)
            dv_acc[here, cols] += nn(probs.astype(bf16), grads[p])
            dk_acc[here, cols] += nn(grad_scores, queries[p])
            dq_acc[p] += tn(kb, grad_scores)
        return carry

    lax.fori_loop(first // ROWS, i + 1, step, 0)
    for p in range(3):
        dq[:, p * 128 : (p + 1) * 128] = (one_above(dq_acc[p]) * 0.125).astype(bf16)

    @pl.when(i == count - 1)
    def _():
        dk[...] = dk_acc[...].astype(bf16)
        dv[...] = dv_acc[...].astype(bf16)


def attend_back(lens, q, k, v, mixed, lse, grad_mixed):
    seq = q.shape[0]
    count = seq // ROWS
    row = pl.BlockSpec((ROWS, PAIR), lambda i, s: (i, 0))
    wide = jax.ShapeDtypeStruct((seq, PAIR), bf16)
    return pl.pallas_call(
        attend_back_kernel,
        grid_spec=pltpu.PrefetchScalarGridSpec(
            num_scalar_prefetch=1,
            grid=(count,),
            in_specs=[
                row,
                full((seq, PAIR)),
                full((seq, PAIR)),
                row,
                pl.BlockSpec((8, ROWS), lambda i, s: (0, i)),
                row,
            ],
            out_specs=[row, full((seq, PAIR)), full((seq, PAIR))],
            scratch_shapes=[
                pltpu.VMEM((seq, PAIR), f32),
                pltpu.VMEM((seq, PAIR), f32),
                pltpu.VMEM((3, 128, 2 * ROWS), f32),
            ],
        ),
        out_shape=[wide, wide, wide],
        compiler_params=params(),
        cost_estimate=cost(40),
        name="attend_back",
    )(lens, q, k, v, mixed, lse, grad_mixed)


def feed_kernel(
    small, tok, pas, vec, mine, cot, wo_mine, wo_other, four, columns, columns_x,
    out_chip, second_keep, grad_second, grad_mixed, sums, mid_send, mid_keep, *rest,
):
    results, rest = (rest[:4], rest[4:]) if small else (rest[:2], rest[2:])
    (
        wo, other, up, down, gup, gdown, go, core_out, core_in, far_out, far_in, ga_out, ga_in, oc_out, oc_in,
        g_send, g_keep, g_in, s_core, r_core, s_far, r_far, s_ga, r_ga, s_oc, r_oc, s_x, r_x, s_m, r_m,
    ) = rest
    step = pl.program_id(0)
    half = core_out.shape[0]
    t, dp = lax.axis_index("tensor"), lax.axis_index("dp")
    core, side = t % 2, t // 2
    near, far = side * 2 + (1 - core), (1 - side) * 2 + core
    z, column = (dp // 2, dp % 2) if small else (0, 0)
    far_x = z * 2 + 1 - column

    def copy(src, dst, s_sem, r_sem, j, to):
        return pltpu.make_async_remote_copy(
            src_ref=src.at[j],
            dst_ref=dst.at[j],
            send_sem=s_sem.at[j],
            recv_sem=r_sem.at[j],
            device_id={"tensor": to},
            device_id_type=MESH,
        )

    core_copy = lambda j: copy(core_out, core_in, s_core, r_core, j, near)
    far_copy = lambda j: copy(far_out, far_in, s_far, r_far, j, far)
    ga_copy = lambda j: copy(ga_out, ga_in, s_ga, r_ga, j, near)
    oc_copy = lambda j: copy(oc_out, oc_in, s_oc, r_oc, j, near)

    def x_copy(slot):
        return pltpu.make_async_remote_copy(
            src_ref=g_send.at[slot],
            dst_ref=g_in.at[slot],
            send_sem=s_x.at[slot],
            recv_sem=r_x.at[slot],
            device_id={"dp": far_x},
            device_id_type=MESH,
        )

    def mixed_copy(block):
        rows = pl.ds(pl.multiple_of(block * ROWS, ROWS), ROWS)
        return pltpu.make_async_remote_copy(
            src_ref=mine.at[rows],
            dst_ref=other.at[rows],
            send_sem=s_m.at[block],
            recv_sem=r_m.at[block],
            device_id={"tensor": near},
            device_id_type=MESH,
        )

    barrier = pltpu.get_barrier_semaphore()

    @pl.when(step == 0)
    def _():
        for to in (near, far):
            pl.semaphore_signal(barrier, inc=1, device_id={"tensor": to}, device_id_type=MESH)
        if small:
            pl.semaphore_signal(barrier, inc=1, device_id={"dp": far_x}, device_id_type=MESH)
        for h in range(2):
            for m in range(2):
                rows, cols = slice(h * SIDE, (h + 1) * SIDE), slice(m * PAIR, (m + 1) * PAIR)
                wo[rows, cols] = wo_mine[h, m]
                wo[PAIR + h * SIDE : PAIR + (h + 1) * SIDE, cols] = wo_other[h, m]
        for r in range(4):
            for m in range(2):
                rows, cols = slice(r * SIDE, (r + 1) * SIDE), slice(m * PAIR, (m + 1) * PAIR)
                for at, weight in ((8, up), (16, down)):
                    pair = at + 2 * r + m
                    if pair < 12:
                        weight[rows, cols] = four[0, pair - 8]
                        continue
                    n = (pair // 6 - 2) * 3 + pair % 3
                    for source, here in ((columns, pair // 3 % 2), (columns_x, 1 - pair // 3 % 2)):

                        @pl.when(column == here)
                        def _():
                            weight[rows, cols] = source[n]

        pl.semaphore_wait(barrier, 3 if small else 2)
        for j in range(half):
            mixed_copy(core * half + j).start()
            mixed_copy((1 - core) * half + j).start()
        gup[...] = jnp.zeros_like(gup)
        gdown[...] = jnp.zeros_like(gdown)
        go[...] = jnp.zeros_like(go)
        sums[...] = jnp.zeros_like(sums)

    @pl.when(step < 2 * half)
    def _():
        j = step // 2
        owner = jnp.where(step % 2 == 0, 1 - core, core)
        here = pl.ds(pl.multiple_of((owner * half + j) * ROWS, ROWS), ROWS)
        first = embedded(tok[...], pas[...], vec[...])
        mixed_copy(owner * half + j).wait_recv()
        second = first + nn(jnp.concatenate([mine[here, :], other[here, :]], axis=1), wo[...])
        hat, _ = hat_of(second)
        low = (hat * vec[PASSES + 2 : PASSES + 3] + vec[PASSES + 3 : PASSES + 4]).astype(bf16)
        upper = nn(low, up[...])
        square = upper * upper
        bent = jnp.tanh(gelu_coef * upper * (1.0 + 0.044715 * square))
        act = (0.5 * upper * (1.0 + bent)).astype(bf16)
        slope = 0.5 * (1.0 + bent) + (0.5 * gelu_coef) * upper * (1.0 - bent * bent) * (
            1.0 + (3 * 0.044715) * square
        )
        grad_act = nt(cot[...], down[...])
        grad_upper = (grad_act * slope).astype(bf16)
        part = nt(grad_upper, up[...])

        @pl.when(step % 2 == 0)
        def _():
            core_out[j] = part.astype(bf16)
            core_copy(j).start()

        @pl.when(step % 2 == 1)
        def _():
            core_copy(j).wait_recv()
            far_out[j] = (part + core_in[j].astype(f32)).astype(bf16)
            far_copy(j).start()
            second_keep[pl.ds(pl.multiple_of(j * ROWS, ROWS), ROWS), :] = second

        gup[...] += tn(low, grad_upper)
        gdown[...] += tn(act, cot[...])
        out_part = nn(act, down[...])

        @pl.when(step % 2 == 0)
        def _():
            oc_out[j] = out_part.astype(bf16)
            oc_copy(j).start()

        @pl.when(step % 2 == 1)
        def _():
            oc_copy(j).wait_recv()
            out_chip[...] = (out_part + oc_in[j].astype(f32)).astype(bf16)

    @pl.when(step == 2 * half - 1)
    def _():
        for r in range(4):
            for m in range(2):
                rows, cols = slice(r * SIDE, (r + 1) * SIDE), slice(m * PAIR, (m + 1) * PAIR)
                for at, total in ((8, gup), (16, gdown)):
                    pair = at + 2 * r + m
                    slot, place = (pair // 6 - 1) * 3 + pair % 3, pair // 3 % 2
                    value = total[rows, cols].astype(bf16)
                    kept, sent, n = (mid_keep, mid_send, slot) if slot < 6 else (g_keep, g_send, slot - 6)

                    @pl.when(column == place)
                    def _():
                        kept[n] = value

                    @pl.when(column != place)
                    def _():
                        sent[n] = value
        if small:
            for n in range(3):
                x_copy(n).start()

    def through_out(grad, block):
        here = pl.ds(pl.multiple_of(block * ROWS, ROWS), ROWS)
        grad_mixed[here, :] = nt(grad, wo[:PAIR, :]).astype(bf16)
        go[...] += tn(mine[here, :], grad)

    @pl.when((step >= 2 * half) & (step < 3 * half))
    def _():
        j = step - 2 * half
        hat, root = hat_of(second_keep[pl.ds(pl.multiple_of(j * ROWS, ROWS), ROWS), :])
        far_copy(j).wait_recv()
        grad = far_out[j].astype(f32) + far_in[j].astype(f32)
        result = cot[...].astype(f32) + norm_back(hat, root, grad, vec[PASSES + 2 : PASSES + 3])
        low = result.astype(bf16)
        ga_out[j] = low
        ga_copy(j).start()
        grad_second[...] = result
        sums[0:1] += jnp.sum(grad * hat, axis=0, keepdims=True)
        sums[1:2] += jnp.sum(grad, axis=0, keepdims=True)
        through_out(low, core * half + j)

    @pl.when(step > 2 * half)
    def _():
        j = step - 2 * half - 1
        ga_copy(j).wait_recv()
        through_out(ga_in[j], (1 - core) * half + j)

    @pl.when(step == 3 * half)
    def _():
        at = pl.multiple_of(side * SIDE, SIDE)
        for m in range(2):
            value = go[pl.ds(at, SIDE), m * PAIR : (m + 1) * PAIR].astype(bf16)

            @pl.when(column == 0)
            def _():
                mid_keep[m] = value

            @pl.when(column != 0)
            def _():
                mid_send[m] = value

        for j in range(half):
            core_copy(j).wait_send()
            oc_copy(j).wait_send()
            mixed_copy(j).wait_send()
            mixed_copy(half + j).wait_send()
            far_copy(j).wait_send()
            ga_copy(j).wait_send()
        if small:
            for n in range(3):
                x_copy(n).wait_send()
                x_copy(n).wait_recv()
                value = (g_keep[n].astype(f32) + g_in[n].astype(f32)).astype(bf16)
                for turn in range(4):

                    @pl.when(z + turn == 3)
                    def _():
                        results[turn][n] = value
        else:
            results[0][...] = g_send[...]
            results[1][...] = g_keep[...]


def feed(small, tokens, passes, vec, mine, cotangent, pairs, wo_other, columns, columns_x):
    seq = tokens.shape[0]
    half = seq // ROWS // 2

    def block(i):
        core = lax.axis_index("tensor") % 2
        work = jnp.minimum(i, 2 * half - 1)
        owner = jnp.where(work % 2 == 0, 1 - core, core)
        return owner * half + work // 2

    def cot_block(i):
        core = lax.axis_index("tensor") % 2
        return jnp.where(i < 2 * half, block(i), core * half + jnp.minimum(i - 2 * half, half - 1))

    side = lambda: lax.axis_index("tensor") // 2
    row = lambda n: pl.BlockSpec((ROWS, n), lambda i: (block(i), 0))
    keep = pl.BlockSpec((ROWS, D), lambda i: (jnp.minimum(i // 2, half - 1), 0))
    last = pl.BlockSpec((ROWS, D), lambda i: (jnp.clip(i - 2 * half, 0, half - 1), 0))
    rows = lambda kind: jax.ShapeDtypeStruct((seq // 2, D), kind)
    gr = lambda n: jax.ShapeDtypeStruct((n, SIDE, PAIR), bf16)
    ends = [(3, SIDE, PAIR)] * (4 if small else 2)
    buffer = pltpu.VMEM((half, ROWS, D), bf16)
    dma = pltpu.SemaphoreType.DMA((half,))
    return pl.pallas_call(
        functools.partial(feed_kernel, small),
        grid=(3 * half + 1,),
        in_specs=[
            row(D),
            pl.BlockSpec((1, ROWS), lambda i: (0, block(i))),
            full((16, D)),
            full((seq, PAIR)),
            pl.BlockSpec((ROWS, D), lambda i: (cot_block(i), 0)),
            pl.BlockSpec((2, 2, SIDE, PAIR), lambda i: (0, 3, 0, 0)),
            full(wo_other.shape),
            pl.BlockSpec((1, 4, SIDE, PAIR), lambda i: (side(), 2, 0, 0)),
            full(columns.shape),
            full(columns.shape),
        ],
        out_specs=[
            keep,
            full((seq // 2, D)),
            last,
            full((seq, PAIR)),
            full((8, D)),
            full((6, SIDE, PAIR)),
            full((6, SIDE, PAIR)),
        ]
        + [full(shape) for shape in ends],
        scratch_shapes=[
            pltpu.VMEM((D, D), bf16),
            pltpu.VMEM((seq, PAIR), bf16),
            pltpu.VMEM((D, D), bf16),
            pltpu.VMEM((D, D), bf16),
            pltpu.VMEM((D, D), f32),
            pltpu.VMEM((D, D), f32),
            pltpu.VMEM((PAIR, D), f32),
        ]
        + [buffer] * 8
        + [pltpu.VMEM((3, SIDE, PAIR), bf16)] * 3
        + [dma] * 8
        + [pltpu.SemaphoreType.DMA((3,))] * 2
        + [pltpu.SemaphoreType.DMA((2 * half,))] * 2,
        out_shape=[
            rows(bf16),
            rows(f32),
            rows(f32),
            jax.ShapeDtypeStruct((seq, PAIR), bf16),
            jax.ShapeDtypeStruct((8, D), f32),
            gr(6),
            gr(6),
        ]
        + [jax.ShapeDtypeStruct(shape, bf16) for shape in ends],
        compiler_params=params(collective_id=1, has_side_effects=True),
        cost_estimate=cost(50),
        name="feed_forward",
    )(tokens, passes, vec, mine, cotangent, pairs, wo_other, pairs, columns, columns_x)


CHUNK = SIDE // 2
CHUNKS = 18
TAKEN = (
    ((8, 3), (10, 4), (12, 12)),
    ((3, 1), (5, 2), (7, 3), (8, 4), (9, 6), (10, 7), (11, 8), (12, 12)),
    ((1, 2), (2, 3), (5, 4), (6, 5), (7, 6), (8, 8), (9, 9), (10, 11), (12, 12)),
    ((-1, 3), (2, 5), (4, 6), (5, 7), (6, 8), (7, 12)),
)
GRAD_STEPS = 3


def last_kernel(
    small, norm_all, dq_all, dk_all, dv_all, cat, tok, pas, vec, grad_second, sums_two, second, chip, far,
    mid_near, mid_keep, output, input_grad, *rest,
):
    if small:
        late, vec_sum = rest[:2]
        rest = rest[2:]
        (
            core_out, core_in, sums, core_sums, x_in, z_in, z_out, up_in, v_out, v_in, total,
            s_core, r_core, s_sum, r_sum, s_x, r_x, s_z, r_z, s_up, r_up, s_v, r_v, ready, norm, dq, dk, dv, g_send, g_keep,
            s_own, s_res, r_res, s_in,
        ) = rest
    else:
        (
            vec_sum, send_out, keep_out, core_out, core_in, sums, core_sums, s_core, r_core, s_sum, r_sum, ready,
            norm, dq, dk, dv, g_send, g_keep, s_own, s_res, r_res, s_in,
        ) = rest
    step = pl.program_id(0)
    i = step - GRAD_STEPS
    half = core_out.shape[0]
    t, dp = lax.axis_index("tensor"), lax.axis_index("dp")
    core, side = t % 2, t // 2
    near = side * 2 + (1 - core)
    z, column = (dp // 2, dp % 2) if small else (0, 0)
    far_x = z * 2 + 1 - column
    peers = [lax.rem(dp + k, 8) for k in range(1, 8)]

    def copy(src, dst, s_sem, r_sem, to):
        return pltpu.make_async_remote_copy(
            src_ref=src, dst_ref=dst, send_sem=s_sem, recv_sem=r_sem, device_id=to, device_id_type=MESH
        )

    core_copy = lambda j: copy(core_out.at[j], core_in.at[j], s_core.at[j], r_core.at[j], {"tensor": near})
    sum_copy = lambda: copy(sums, core_sums, s_sum, r_sum, {"tensor": near})

    def rows_at(n, j, owner):
        rows = pl.ds(pl.multiple_of((owner * half + j) * ROWS, ROWS), ROWS)
        return (output, input_grad)[n].at[rows]

    own_result = lambda n, j: pltpu.make_async_copy(ready.at[n, j], rows_at(n, j, core), s_own.at[n, j])
    near_result = lambda n, j, owner: copy(
        ready.at[n, j], rows_at(n, j, owner), s_res.at[n, j], r_res.at[n, j], {"tensor": near}
    )

    def part_of(ref, k):
        return ref.at[k // 2, pl.ds((k % 2) * CHUNK, CHUNK)]

    x_copy = lambda k: copy(part_of(g_send, k), x_in.at[k], s_x.at[k], r_x.at[k], {"dp": far_x})
    z_copy = lambda k: copy(z_out.at[k], z_in.at[k], s_z.at[k], r_z.at[k], {"dp": dp - 2})
    up_copy = lambda k: copy(z_out.at[k], up_in.at[k - 6], s_up.at[k - 6], r_up.at[k - 6], {"dp": dp + 2})
    v_copy = lambda n: copy(v_out.at[peers[n]], v_in.at[dp], s_v.at[n], r_v.at[dp], {"dp": peers[n]})
    barrier = pltpu.get_barrier_semaphore()

    loads = [
        pltpu.make_async_copy(src, dst, s_in.at[n])
        for n, (src, dst) in enumerate(((norm_all, norm), (dq_all, dq), (dv_all, dv), (dk_all, dk)))
    ]

    @pl.when(step == 0)
    def _():
        for load in loads:
            load.start()
        pl.semaphore_signal(barrier, inc=1, device_id={"tensor": near}, device_id_type=MESH)
        if small:
            for peer in peers:
                pl.semaphore_signal(barrier, inc=1, device_id={"dp": peer}, device_id_type=MESH)
            late[...] = jnp.zeros_like(late)
        sums[...] = jnp.zeros_like(sums)
        sums[PASSES + 2 : PASSES + 4] = sums_two[0:2]
        pl.semaphore_wait(barrier, 8 if small else 1)

    if small:

        def term_of(k):
            rows = pl.ds(pl.multiple_of((k % 2) * CHUNK, 16), CHUNK)

            @pl.when(jnp.asarray(k) < 6)
            def _():
                x_copy(k).wait_recv()
                total[...] = g_keep[k // 2, rows, :].astype(f32) + x_in[k].astype(f32)

            @pl.when(jnp.asarray(k) >= 6)
            def _():
                total[...] = mid_keep[k // 2 - 3, rows, :].astype(f32) + mid_near[k // 2 - 3, rows, :].astype(f32)

            return total[...]

        @pl.when((step == 0) & (z == 0))
        def _():
            for k in range(6, CHUNKS):
                z_out[k] = term_of(k).astype(bf16)
                up_copy(k).start()

        @pl.when((step == 0) & (z == 3))
        def _():
            for k in (6, 7, 8, 12, 13):
                z_out[k] = term_of(k).astype(bf16)
                z_copy(k).start()

    def mine_of(grad):
        return jnp.where(side == 0, grad[:, :SIDE], grad[:, SIDE:])

    def pairs_of(grad):
        value = tn(grad, norm[...]).astype(bf16)
        return value[:, :PAIR], value[:, PAIR:]

    second_two = jnp.where(jnp.asarray(column) == 0, 1, 0)

    @pl.when(step == 0)
    def _():
        for load in loads[:3]:
            load.wait()
        both = pairs_of(jnp.where(jnp.asarray(column) == 0, mine_of(dv), mine_of(dq)))
        for m in range(2):
            g_send[second_two + m] = both[m]
        if small:
            for m in range(4):
                x_copy(2 * second_two + m).start()

    @pl.when(step == 1)
    def _():
        loads[3].wait()
        both = pairs_of(mine_of(dk))
        for place, (kept, sent) in enumerate(((0, 1), (1, 0))):

            @pl.when(jnp.asarray(column) == place)
            def _():
                g_keep[2 - 2 * place] = both[kept]
                g_send[2 * place] = both[sent]

        if small:
            for m in range(2):
                x_copy(4 * column + m).start()

    @pl.when(step == 2)
    def _():
        both = pairs_of(jnp.where(jnp.asarray(column) == 0, mine_of(dq), mine_of(dv)))
        for m in range(2):
            g_keep[1 - second_two + m] = both[m]
        if not small:
            send_out[...] = g_send[...]
            keep_out[...] = g_keep[...]

    @pl.when((i >= 0) & (i < 2 * half))
    def _():
        block = lax.rem(i + (1 - core) * half, 2 * half)
        rows = pl.ds(pl.multiple_of(block * ROWS, ROWS), ROWS)
        part = nt(dq[rows, :], cat[0]) + nt(dk[rows, :], cat[1]) + nt(dv[rows, :], cat[2])

        @pl.when(i < half)
        def _():
            core_out[i] = part.astype(bf16)
            core_copy(i).start()

        @pl.when(i >= half)
        def _():
            j = i - half
            hat, root = hat_of(embedded(tok[...], pas[...], vec[...]))
            core_copy(j).wait_recv()
            grad = part + core_in[j].astype(f32)
            result = grad_second[...] + norm_back(hat, root, grad, vec[PASSES : PASSES + 1])
            ready[0, j] = (second[...] + (chip[...].astype(f32) + far[...].astype(f32))).astype(bf16)
            ready[1, j] = result.astype(bf16)
            for n in range(2):
                own_result(n, j).start()
                near_result(n, j, core).start()
            chosen = one_hot(pas[...])
            high, mid, _ = split_three(result)
            sums[...] += nn(chosen, high) + nn(chosen, mid)
            sums[PASSES : PASSES + 1] += jnp.sum(grad * hat, axis=0, keepdims=True)
            sums[PASSES + 1 : PASSES + 2] += jnp.sum(grad, axis=0, keepdims=True)

    @pl.when(i == 2 * half - 1)
    def _():
        sum_copy().start()

    if small:

        def keep_late(k, pair, total):
            late[pair, pl.ds(pl.multiple_of((k % 2) * CHUNK, 16), CHUNK), :] = total

        def pass_on(k):
            term = term_of(k)

            @pl.when(z < 3)
            def _():
                z_copy(k).wait_recv()

            below = jnp.where(z < 3, z_in[k].astype(f32), 0.0)
            passed = term + below

            @pl.when((z > 1) | ((z == 1) & (k < 6)))
            def _():
                z_out[k] = passed.astype(bf16)
                z_copy(k).start()

            @pl.when(z == 0)
            def _():
                keep_late(k, k // 2, passed)

            @pl.when((z == 1) & (k >= 6))
            def _():
                up_copy(k).wait_recv()
                keep_late(k, k // 2 - 3, passed + up_in[k - 6].astype(f32))

        def at_position(p, carry):
            k = jnp.where(p < 3, p + 6, jnp.where(p < 9, lax.rem(p + 3 + 2 * column, 6), p))

            @pl.when((z > 0) | (k < 6))
            def _():
                pass_on(k)

            return carry

        begin, end = jnp.int32(0), jnp.int32(0)
        for place, line in enumerate(TAKEN):
            for at, upto in line:
                begin = jnp.where((z == place) & (step > at), upto, begin)
                end = jnp.where((z == place) & (step >= at), upto, end)
        lax.fori_loop(begin, end, at_position, 0)

        @pl.when((step == 7) & (z == 3))
        def _():
            for k in range(14, CHUNKS):
                z_out[k] = term_of(k).astype(bf16)
                z_copy(k).start()

        for at, first_chunk, upto in ((9, 12, 15), (10, 15, 18)):

            @pl.when((step == at) & (z == 1))
            def _(first_chunk=first_chunk, upto=upto):
                for k in range(first_chunk, upto):
                    up_copy(k).wait_recv()
                    z_out[k] = (term_of(k) + up_in[k - 6].astype(f32)).astype(bf16)
                    up_copy(k).start()

        @pl.when((step == pl.num_programs(0) - 1) & (z == 2))
        def _():
            for k in range(12, CHUNKS):
                z_copy(k).wait_recv()
                up_copy(k).wait_recv()
                keep_late(k, k // 2 - 6, term_of(k) + z_in[k].astype(f32) + up_in[k - 6].astype(f32))

    @pl.when(i == 2 * half)
    def _():
        sum_copy().wait_recv()
        total = sums[...] + core_sums[...]
        if small:
            wide = D // 8
            for d in range(8):
                v_out[d, :, 0:wide] = total[:, d * wide : (d + 1) * wide]
                v_out[d, :, wide:] = jnp.zeros((16, 128 - wide), f32)
            for n in range(7):
                v_copy(n).start()
        else:
            vec_sum[...] = total

    @pl.when(step == pl.num_programs(0) - 1)
    def _():
        for j in range(half):
            core_copy(j).wait_send()
            for n in range(2):
                own_result(n, j).wait()
                near_result(n, j, core).wait_send()
                near_result(n, j, 1 - core).wait_recv()
        sum_copy().wait_send()
        if small:
            for peer in peers:
                copy(v_out.at[0], v_in.at[peer], s_v.at[0], r_v.at[peer], {"dp": far_x}).wait_recv()
            v_in[dp] = v_out[dp]
            total = v_in[0]
            for d in range(1, 8):
                total = total + v_in[d]
            vec_sum[...] = total
            for n in range(7):
                v_copy(n).wait_send()
            for k in range(CHUNKS):
                if k < 6:
                    x_copy(k).wait_send()
                    pl.when(z > 0)(z_copy(k).wait_send)
                elif k < 12:
                    pl.when(z > 1)(z_copy(k).wait_send)
                    pl.when(z == 0)(up_copy(k).wait_send)
                else:
                    pl.when(z == 3)(z_copy(k).wait_send)
                    pl.when(z < 2)(up_copy(k).wait_send)


def last(
    small, norm, dq, dk, dv, cat, tokens, passes, vec, grad_second, sums_two, second, chip, far, mid_near, mid_keep
):
    seq = dq.shape[0]
    half = seq // ROWS // 2
    core = lambda: lax.axis_index("tensor") % 2

    own = lambda i: jnp.clip(i - GRAD_STEPS - half, 0, half - 1)
    mine = pl.BlockSpec((ROWS, D), lambda i: (own(i), 0))
    dma = pltpu.SemaphoreType.DMA
    out_specs = [pl.BlockSpec(memory_space=pl.ANY)] * 2
    out_shape = [jax.ShapeDtypeStruct((seq, D), bf16)] * 2
    scratch = [
        pltpu.VMEM((half, ROWS, D), bf16),
        pltpu.VMEM((half, ROWS, D), bf16),
        pltpu.VMEM((16, D), f32),
        pltpu.VMEM((16, D), f32),
    ]
    sems = [dma((half,)), dma((half,)), dma, dma]
    if small:
        out_specs += [full((3, SIDE, PAIR)), full((16, 128))]
        out_shape += [
            jax.ShapeDtypeStruct((3, SIDE, PAIR), f32),
            jax.ShapeDtypeStruct((16, 128), f32),
        ]
        scratch += [pltpu.VMEM((CHUNKS, CHUNK, PAIR), bf16)] * 3
        scratch += [pltpu.VMEM((12, CHUNK, PAIR), bf16)]
        scratch += [pltpu.VMEM((8, 16, 128), f32)] * 2 + [pltpu.VMEM((CHUNK, PAIR), f32)]
        sems += [dma((6,))] * 2 + [dma((CHUNKS,))] * 2 + [dma((12,))] * 2 + [dma((7,)), dma((8,))]
    else:
        out_specs += [full((16, D)), full((3, SIDE, PAIR)), full((3, SIDE, PAIR))]
        out_shape += [jax.ShapeDtypeStruct((16, D), f32)] + [jax.ShapeDtypeStruct((3, SIDE, PAIR), bf16)] * 2
    scratch_more = [pltpu.VMEM((2, half, ROWS, D), bf16), pltpu.VMEM((seq, D), bf16)]
    scratch_more += [pltpu.VMEM((seq, PAIR), bf16)] * 3
    scratch_more += [pltpu.VMEM((3, SIDE, PAIR), bf16)] * 2 + [dma((2, half))] * 3 + [dma((4,))]
    return pl.pallas_call(
        functools.partial(last_kernel, small),
        grid=(GRAD_STEPS + 2 * half + 2,),
        in_specs=[
            *[pl.BlockSpec(memory_space=pl.ANY)] * 4,
            full(cat.shape),
            pl.BlockSpec((ROWS, D), lambda i: (core() * half + own(i), 0)),
            pl.BlockSpec((1, ROWS), lambda i: (0, core() * half + own(i))),
            full((16, D)),
            mine,
            full((8, D)),
            mine,
            mine,
            mine,
            full(mid_near.shape),
            full(mid_keep.shape),
        ],
        out_specs=out_specs,
        out_shape=out_shape,
        scratch_shapes=scratch + sems + scratch_more,
        compiler_params=params(collective_id=2, has_side_effects=True),
        cost_estimate=cost(38),
        name="last",
    )(norm, dq, dk, dv, cat, tokens, passes, vec, grad_second, sums_two, second, chip, far, mid_near, mid_keep)


def precondition(grad, weight, left, right, left_root, right_root):
    high = lax.Precision.HIGHEST
    left_new = decay * left + (1.0 - decay) * jnp.einsum(
        "...ij,...kj->...ik", grad, grad, precision=high
    )
    right_new = decay * right + (1.0 - decay) * jnp.einsum(
        "...ji,...jk->...ik", grad, grad, precision=high
    )
    half = jnp.einsum("...ij,...jk->...ik", left_root, grad, precision=high)
    step = jnp.einsum("...ij,...jk->...ik", half, right_root, precision=high)
    return (left_new, right_new, step, weight - rate_matrix * step)


def two_part(value):
    high = value.astype(bf16)
    return high, (value - high.astype(f32)).astype(bf16)


def dot_three(dot, a, b):
    return dot(a[0], b[0]) + (dot(a[0], b[1]) + dot(a[1], b[0]))


def renew_kernel(
    late, own, one, two, three, weight, left, right, left_root, right_root, output, input_grad, vec_sum, vec, moment,
    left_new, right_new, step, new, output_new, input_grad_new, vec_grad, moment_new, vec_new,
):
    @pl.when(pl.program_id(0) == 0)
    def _():
        rows, wide = vec.shape
        grad = vec_sum[:rows, :wide]
        square = decay * moment[...] + (1.0 - decay) * grad * grad
        vec_grad[...] = grad
        moment_new[...] = square
        vec_new[...] = vec[...] - rate_vector * grad / (jnp.sqrt(square) + moment_eps)

    output_new[...] = output[...]
    input_grad_new[...] = input_grad[...]

    @pl.when(pl.program_id(0) < 3)
    def _():
        early = own[0].astype(f32) + one[0].astype(f32) + two[0].astype(f32) + three[0].astype(f32)
        z = lax.axis_index("dp") // 2
        both = late[0] + jnp.where(z > 2, early, 0.0)
        for n in range(2):
            grad = both[:, n * SIDE : (n + 1) * SIDE]
            grad = two_part(jnp.where(z == 0, grad.T, grad))
            left_new[0, n] = decay * left[0, n] + (1.0 - decay) * dot_three(nt, grad, grad)
            right_new[0, n] = decay * right[0, n] + (1.0 - decay) * dot_three(tn, grad, grad)
            half = dot_three(nn, two_part(left_root[0, n]), grad)
            value = dot_three(nn, two_part(half), two_part(right_root[0, n]))
            step[0, n] = value
            new[0, n] = weight[0, n] - rate_matrix * value


def renew(late, own, far, weight, left, right, left_root, right_root, output, input_grad, vec_sum, vec, moment):
    pair = pl.BlockSpec((1, SIDE, PAIR), lambda i: (jnp.minimum(i, 2), 0, 0))
    slot = pl.BlockSpec((1, 2, SIDE, SIDE), lambda i: (0, jnp.minimum(i, 2), 0, 0))
    rows = pl.BlockSpec((output.shape[0] // 4, D), lambda i: (i, 0))
    return pl.pallas_call(
        renew_kernel,
        grid=(4,),
        in_specs=[pair] * 5 + [slot] * 5 + [rows] * 2 + [full(vec_sum.shape)] + [full(vec.shape)] * 2,
        out_specs=[slot] * 4 + [rows] * 2 + [full(vec.shape)] * 3,
        out_shape=[jax.ShapeDtypeStruct(weight.shape, f32)] * 4
        + [jax.ShapeDtypeStruct(value.shape, value.dtype) for value in (output, input_grad, vec, vec, vec)],
        compiler_params=params(46),
        cost_estimate=cost(8),
        name="renew",
    )(late, own, *far, weight, left, right, left_root, right_root, output, input_grad, vec_sum, vec, moment)


def to_pairs(blocks):
    n = blocks.shape[0] // 2
    return blocks.reshape(n, 2, SIDE, SIDE).transpose(0, 2, 1, 3).reshape(n, SIDE, PAIR)


def from_pairs(pairs):
    n = pairs.shape[0]
    return pairs.reshape(n, SIDE, 2, SIDE).transpose(0, 2, 1, 3).reshape(2 * n, SIDE, SIDE)


def swap(value, bit):
    return lax.ppermute(value, "tensor", [(t, t ^ bit) for t in range(NT)])


def hop_x(value):
    return lax.ppermute(value, "dp", [(d, d ^ 1) for d in range(8)])


def hop_z(value, turn, ends):
    pairs = [(d, (d + 2 * turn) % 8) for d in range(8) if (d // 2 + turn) % 4 in ends]
    return lax.ppermute(value, "dp", pairs)


def tie(*values):
    return lax.optimization_barrier(values)


def on_device(
    tokens,
    pass_ids,
    doc_lengths,
    cotangent,
    block_weights,
    vector_params,
    vector_moment,
    block_left,
    block_right,
    block_left_root,
    block_right_root,
):
    t, dp = lax.axis_index("tensor"), lax.axis_index("dp")
    core, side = t % 2, t // 2
    n_dp = lax.axis_size("dp")
    small = n_dp == 8
    z, column = (dp // 2, dp % 2) if small else (0, 0)
    lens = doc_lengths[0]
    seq = tokens.shape[0]
    passes = pass_ids.reshape(1, seq)
    total_blocks = (D // SIDE) * (4 + 2 * (FF // D))
    slots = block_weights.shape[1] * n_dp

    if small:
        pairs, columns, wo_other, vec, norm, q, k, v, cat = gather(
            block_weights, vector_params, tokens, passes
        )
        columns_x = hop_x(columns)
    else:
        every = lax.all_gather(block_weights.astype(bf16), "dp", axis=1, tiled=True)[0]
        near = to_pairs(every[:total_blocks])
        far = swap(near, 2)
        pairs = jnp.where(side == 0, jnp.stack([near, far]), jnp.stack([far, near]))
        vec = lax.all_gather(vector_params, "dp", axis=1, tiled=True)
        vec = jnp.pad(vec, ((0, 16 - vec.shape[0]), (0, 0)))
        wo_other = swap(pairs[:, 6:8], 1)
        columns = jnp.concatenate([near[12:15], near[18:21]], axis=0)
        columns_x = jnp.concatenate([near[15:18], near[21:24]], axis=0)
        norm, q, k, v, cat = project(tokens, passes, vec, pairs)
    mine, lse = attend(lens, q, k, v)
    out_chip, second, grad_second, grad_mixed, sums_two, mid_send, mid_keep, *ends = feed(
        small, tokens, passes, vec, mine, cotangent, pairs, wo_other, columns, columns_x
    )
    out_far = swap(out_chip, 2)
    if small:
        far = [hop_z(ends[turn], turn, (3,)) for turn in (1, 2, 3)]
        mid_send = hop_x(mid_send)
    dq, dk, dv = attend_back(lens, q, k, v, mine, lse, grad_mixed)
    if small:
        out_far, mid_send, dq = tie(out_far, mid_send, dq)
    output, input_grad, *sums = last(
        small, norm, dq, dk, dv, cat, tokens, passes, vec, grad_second, sums_two, second, out_chip, out_far,
        mid_send, mid_keep,
    )
    if small:
        late, vector_sum = sums
        return_blocks = renew(
            late, ends[0], far, block_weights, block_left, block_right, block_left_root, block_right_root,
            output, input_grad, vector_sum, vector_params, vector_moment,
        )
        left_new, right_new, step, weight_new, output, input_grad, vector_grad, moment_new, vector_new = return_blocks
    else:
        vector_part, g_send, g_keep = sums[0][: PASSES + 4], *sums[1:]
        send, keep = ends
        rest = jnp.stack(
            [
                jnp.concatenate([mid_keep, keep]).reshape(3, 3, SIDE, PAIR),
                jnp.concatenate([mid_send, send]).reshape(3, 3, SIDE, PAIR),
            ],
            axis=1,
        )
        grad_qkv = from_pairs(jnp.concatenate([g_keep, g_send], axis=0)).swapaxes(1, 2)
        grad_rest = from_pairs(rest.reshape(18, SIDE, PAIR))
        spare = jnp.zeros((slots - total_blocks, SIDE, SIDE), bf16)
        grad_blocks = jnp.concatenate([grad_qkv, grad_rest, spare], axis=0)[None].astype(f32)
        owned = lax.psum_scatter(grad_blocks, "dp", scatter_dimension=1, tiled=True)
        vector_grad = lax.psum_scatter(vector_part, "dp", scatter_dimension=1, tiled=True)
        left_new, right_new, step, weight_new = precondition(
            owned, block_weights, block_left, block_right, block_left_root, block_right_root
        )
        moment_new = decay * vector_moment + (1.0 - decay) * vector_grad * vector_grad
        vector_new = vector_params - rate_vector * vector_grad / (jnp.sqrt(moment_new) + moment_eps)
    return (
        output,
        input_grad,
        left_new,
        right_new,
        step,
        weight_new,
        vector_grad,
        moment_new,
        vector_new,
    )


def solution(mesh):
    rows, line = P("dp", None), P(None, "dp")
    block = P("tensor", "dp", None, None)
    return jax.shard_map(
        on_device,
        mesh=mesh,
        in_specs=(rows, P("dp"), rows, rows, block, line, line, block, block, block, block),
        out_specs=(rows, rows, block, block, block, block, line, line, line),
        check_vma=False,
    )
```

```python
import functools

import jax
import jax.numpy as jnp
from jax import lax
from jax.experimental import pallas as pl
from jax.experimental.pallas import tpu as pltpu
from jax.sharding import PartitionSpec as P

D = 768
HD = 64
FF = 3072
PASSES = 5
SIDE = 192
PAIR = 2 * SIDE
ROWS = 256
WIDE = 512
DOCS = 8
NT = 4

norm_eps = 1e-05
moment_eps = 1e-08
rate_matrix = 0.03
rate_vector = 0.2
decay = 0.5
gelu_coef = 0.7978845608028654
masked_score = -1e30
f32 = jnp.float32
bf16 = jnp.bfloat16
MESH = pl.DeviceIdType.MESH


def nn(a, b):
    return lax.dot_general(a, b, (((1,), (0,)), ((), ())), preferred_element_type=f32)


def nt(a, b):
    return lax.dot_general(a, b, (((1,), (1,)), ((), ())), preferred_element_type=f32)


def tn(a, b):
    return lax.dot_general(a, b, (((0,), (0,)), ((), ())), preferred_element_type=f32)


def split_three(value):
    high = value.astype(bf16)
    rest = value - high.astype(f32)
    mid = rest.astype(bf16)
    return high, mid, (rest - mid.astype(f32)).astype(bf16)


def one_hot(pass_row):
    kinds = lax.broadcasted_iota(jnp.int32, (16, pass_row.shape[1]), 0)
    return (kinds == pass_row).astype(f32).astype(bf16)


def embedded(tokens, pass_row, vec):
    chosen = jnp.concatenate([one_hot(pass_row)] * 3, axis=0)
    return tokens.astype(f32) + tn(chosen, jnp.concatenate(split_three(vec), axis=0))


def hat_of(hidden):
    mean = jnp.mean(hidden, axis=-1, keepdims=True)
    center = hidden - mean
    spread = jnp.mean(center * center, axis=-1, keepdims=True)
    root = lax.rsqrt(spread + norm_eps)
    return center * root, root


def norm_back(hat, root, grad, gain):
    scaled = grad * gain
    first = jnp.mean(scaled, axis=-1, keepdims=True)
    second = jnp.mean(scaled * hat, axis=-1, keepdims=True)
    return root * (scaled - first - hat * second)


def params(mebibytes=56, **kw):
    return pltpu.CompilerParams(vmem_limit_bytes=mebibytes * 1024 * 1024, **kw)


def cost(micros):
    return pl.CostEstimate(flops=int(micros * 1.1e9), bytes_accessed=int(micros * 1e6), transcendentals=0)


def full(shape):
    return pl.BlockSpec(shape, lambda *_: (0,) * len(shape))


def gather_kernel(
    own, vec_own, tokens, passes,
    all_pairs, columns, wo_other, vec_out, norm, q, k_out, v, cat,
    pack, vec_pack, vec_land, wq, tok, norm_s, qkv_s, cat_s, *sems,
):
    (
        s_z1, r_z1, s_x1, r_x1, s_y1, r_y1, s_d1, r_d1, s_l, r_l, s_r, r_r, s_x2, r_x2, s_y2, r_y2, s_v, r_v, s_c, r_c,
        s_out, s_cat, s_tok, loc,
    ) = sems
    dp, t = lax.axis_index("dp"), lax.axis_index("tensor")
    z, x = dp // 2, dp % 2
    y, core = t // 2, t % 2
    far_x, far_y, near = z * 2 + (1 - x), (1 - y) * 2 + core, y * 2 + (1 - core)

    barrier = pltpu.get_barrier_semaphore()
    peers = [lax.rem(dp + n, 8) for n in range(1, 8)]
    for peer in peers:
        pl.semaphore_signal(barrier, inc=1, device_id={"dp": peer}, device_id_type=MESH)
    for to in (far_y, near):
        pl.semaphore_signal(barrier, inc=1, device_id={"tensor": to}, device_id_type=MESH)

    tok_copy = pltpu.make_async_copy(tokens, tok, s_tok)
    tok_copy.start()
    for m in range(3):
        pair = jnp.concatenate([own[0, 2 * m], own[0, 2 * m + 1]], axis=1).astype(bf16)
        pack[m] = pair

        @pl.when(z == 0)
        def _():
            wq[y, 3 * x + m] = pair

    vec_pack[...] = jnp.zeros_like(vec_pack)
    vec_pack[0 : PASSES + 4, 0 : D // 8] = vec_own[...]
    pl.semaphore_wait(barrier, 9)

    started = []

    def send(src, dst, s_sem, r_sem, to, cond=None):
        copy = pltpu.make_async_remote_copy(
            src_ref=src, dst_ref=dst, send_sem=s_sem, recv_sem=r_sem, device_id=to, device_id_type=MESH
        )
        started.append((cond, copy))
        if cond is None:
            copy.start()
        else:
            pl.when(cond)(copy.start)

    def arrived(dst, r_sem, cond=None):
        copy = pltpu.make_async_remote_copy(
            src_ref=dst, dst_ref=dst, send_sem=loc, recv_sem=r_sem, device_id={"dp": far_x}, device_id_type=MESH
        )
        if cond is None:
            copy.wait_recv()
        else:
            pl.when(cond)(copy.wait_recv)

    to_x, to_y, to_left, to_right = {"dp": far_x}, {"tensor": far_y}, {"dp": dp - 2}, {"dp": dp + 2}
    half = SIDE // 2

    def piece(side, column, k):
        return wq.at[side, 3 * column + k // 2, pl.ds((k % 2) * half, half)]

    def at_one(m):
        return all_pairs.at[y, 6 + 3 * x + m]

    def at_z(d, m):
        return columns.at[3 * (z + d - 2) + m]

    own_one = pltpu.make_async_copy(pack, all_pairs.at[y, pl.ds(6 + 3 * x, 3)], loc)
    own_more = pltpu.make_async_copy(pack, columns.at[pl.ds(3 * (z - 2), 3)], loc)
    pl.when(z == 1)(own_one.start)
    pl.when(z > 1)(own_more.start)

    for m in range(3):
        send(pack.at[m], at_one(m), s_l.at[0, m], r_l.at[0, m], to_left, z == 1)
        send(pack.at[m], at_z(0, m), s_l.at[0, m], r_l.at[0, m], to_left, z > 1)
    for n, peer in enumerate(peers):
        send(vec_pack, vec_land.at[dp], s_v.at[n], r_v.at[dp], {"dp": peer})
    send(pack.at[0], at_z(0, 0), s_r.at[0, 0], r_r.at[0, 0], to_right, z == 2)
    send(pack.at[0], at_one(0), s_x2.at[0], r_x2.at[0], to_x, z == 1)

    def diagonal(k):
        if k % 2 == 0:
            arrived(piece(y, 1 - x, k), r_x1.at[k])
            send(piece(y, 1 - x, k), piece(y, 1 - x, k), s_d1.at[k], r_d1.at[k], to_y)
        else:
            arrived(piece(1 - y, x, k), r_y1.at[k])
            send(piece(1 - y, x, k), piece(1 - y, x, k), s_d1.at[k], r_d1.at[k], to_x)

    def from_right(d, m, cond=True):
        arrived(columns.at[m], r_l.at[d - 1, m], (z + d < 4) & cond)
        if d < 3:
            send(at_z(d, m), at_z(d, m), s_l.at[d, m], r_l.at[d, m], to_left, (z + d < 4) & (z > 0))

    def along_x(m, cond):
        send(at_one(m), at_one(m), s_x2.at[m], r_x2.at[m], to_x, cond)

    def from_left(d, m):
        arrived(columns.at[m], r_r.at[d - 1, m], z > d)
        if d == 1:
            send(at_one(m), at_one(m), s_r.at[1, m], r_r.at[1, m], to_right, z == 2)
        along_x(m, z == d + 1)

    for k in range(6):
        arrived(piece(y, x, k), r_z1.at[k], z > 0)
        send(piece(y, x, k), piece(y, x, k), s_z1.at[k], r_z1.at[k], to_right, z < 3)
        send(piece(y, x, k), piece(y, x, k), s_x1.at[k], r_x1.at[k], to_x)
        send(piece(y, x, k), piece(y, x, k), s_y1.at[k], r_y1.at[k], to_y)
        if k == 5:
            for m in range(3):
                send(pack.at[m], at_one(m), s_r.at[0, m], r_r.at[0, m], to_right, z == 1)
                if m > 0:
                    send(pack.at[m], at_z(0, m), s_r.at[0, m], r_r.at[0, m], to_right, z == 2)
                    send(pack.at[m], at_one(m), s_x2.at[m], r_x2.at[m], to_x, z == 1)
        if k >= 1:
            diagonal(k - 1)
        if k % 2 == 1:
            from_right(1, k // 2, z > 0)
    diagonal(5)
    pl.when(z == 1)(own_one.wait)
    pl.when(z > 1)(own_more.wait)
    for m in range(3):
        arrived(columns.at[m], r_l.at[0, m], z == 0)
        along_x(m, z == 0)
    for m in range(3):
        from_left(1, m)
        from_right(2, m)
    for k in range(6):
        if k % 2 == 0:
            arrived(piece(1 - y, x, k), r_y1.at[k])
        else:
            arrived(piece(y, 1 - x, k), r_x1.at[k])
        arrived(piece(1 - y, 1 - x, k), r_d1.at[k])
    for peer in peers:
        arrived(vec_land.at[peer], r_v.at[peer])
    vec_land[dp] = vec_pack[...]
    vec = jnp.concatenate([vec_land[d][:, : D // 8] for d in range(8)], axis=1)
    vec_out[...] = vec
    for n in range(3):
        for i in range(4):
            at = (i % 2) * SIDE
            parts = [wq[h, 2 * n + i // 2][:, at : at + SIDE] for h in range(2)]
            cat_s[n, i * SIDE : (i + 1) * SIDE, :] = jnp.concatenate(parts, axis=1)
    writes = [pltpu.make_async_copy(cat_s, cat, s_cat)]
    writes[0].start()
    tok_copy.wait()

    def rows_of(b):
        rows = slice(b * WIDE, (b + 1) * WIDE)
        hat, _ = hat_of(embedded(tok[rows, :], passes[:, rows], vec))
        low = (hat * vec[PASSES : PASSES + 1] + vec[PASSES + 1 : PASSES + 2]).astype(bf16)
        norm_s[rows, :] = low
        writes.append(pltpu.make_async_copy(norm_s.at[rows, :], norm.at[rows, :], s_out.at[b, 3]))
        writes[-1].start()
        for n, out in enumerate((q, k_out, v)):
            qkv_s[n, rows, :] = nn(low, cat_s[n]).astype(bf16)
            writes.append(pltpu.make_async_copy(qkv_s.at[n, rows, :], out.at[rows, :], s_out.at[b, n]))
            writes[-1].start()

    count = tok.shape[0] // WIDE
    for b in range(count):
        rows_of(b)
        if b == 0:
            for m in range(3):
                from_left(2, m)
                from_right(3, m)
        if b == 1:
            for m in range(2):
                ref = all_pairs.at[y, 6 + m]
                arrived(ref, r_x2.at[m], x == 1)
                send(ref, ref, s_y2.at[m], r_y2.at[m], to_y)
                send(ref, wo_other.at[y, m], s_c.at[0, m], r_c.at[y, m], {"tensor": near})
    for m in range(2):
        ref = all_pairs.at[1 - y, 6 + m]
        arrived(ref, r_y2.at[m])
        send(ref, wo_other.at[1 - y, m], s_c.at[1, m], r_c.at[1 - y, m], {"tensor": near})
    for m in range(3):
        arrived(all_pairs.at[y, 6 + 3 * (1 - x) + m], r_x2.at[m], None if m == 2 else x == 0)
    for h in range(2):
        for m in range(2):
            arrived(wo_other.at[h, m], r_c.at[h, m])
    for copy in writes:
        copy.wait()
    for cond, copy in started:
        if cond is None:
            copy.wait_send()
        else:
            pl.when(cond)(copy.wait_send)


def gather(block_weights, vector_params, tokens, passes):
    seq = tokens.shape[0]
    dma = pltpu.SemaphoreType.DMA
    sizes = [(6,)] * 8 + [(3, 3)] * 2 + [(2, 3)] * 2 + [(3,)] * 2 + [(2,)] * 2 + [(7,), (8,)] + [(2, 2)] * 2
    sizes += [(seq // WIDE, 4)]
    vmem, far = pl.BlockSpec(memory_space=pltpu.VMEM), pl.BlockSpec(memory_space=pl.ANY)
    wide = jax.ShapeDtypeStruct((seq, PAIR), bf16)
    return pl.pallas_call(
        gather_kernel,
        in_specs=[vmem, vmem, far, vmem],
        out_specs=[far, far, far, vmem, far, far, far, far, far],
        out_shape=[
            jax.ShapeDtypeStruct((2, 24, SIDE, PAIR), bf16),
            jax.ShapeDtypeStruct((6, SIDE, PAIR), bf16),
            jax.ShapeDtypeStruct((2, 2, SIDE, PAIR), bf16),
            jax.ShapeDtypeStruct((16, D), f32),
            jax.ShapeDtypeStruct((seq, D), bf16),
            wide,
            wide,
            wide,
            jax.ShapeDtypeStruct((3, D, PAIR), bf16),
        ],
        scratch_shapes=[
            pltpu.VMEM((3, SIDE, PAIR), bf16),
            pltpu.VMEM((16, 128), f32),
            pltpu.VMEM((8, 16, 128), f32),
            pltpu.VMEM((2, 6, SIDE, PAIR), bf16),
            pltpu.VMEM((seq, D), bf16),
            pltpu.VMEM((seq, D), bf16),
            pltpu.VMEM((3, seq, PAIR), bf16),
            pltpu.VMEM((3, D, PAIR), bf16),
        ]
        + [dma(size) for size in sizes]
        + [dma] * 3,
        compiler_params=params(collective_id=0, has_side_effects=True),
        cost_estimate=cost(60),
        name="gather",
    )(block_weights, vector_params, tokens, passes)


def project_kernel(tok, pas, vec, wq, norm, q, k, v, cat):
    @pl.when(pl.program_id(0) == 0)
    def _():
        for x in range(3):
            for i in range(4):
                at = (i % 2) * SIDE
                parts = [wq[h, 2 * x + i // 2][:, at : at + SIDE] for h in range(2)]
                cat[x, i * SIDE : (i + 1) * SIDE, :] = jnp.concatenate(parts, axis=1)

    first = embedded(tok[...], pas[...], vec[...])
    hat, _ = hat_of(first)
    low = (hat * vec[PASSES : PASSES + 1] + vec[PASSES + 1 : PASSES + 2]).astype(bf16)
    norm[...] = low
    for x, out in enumerate((q, k, v)):
        out[...] = nn(low, cat[x]).astype(bf16)


def project(tokens, passes, vec, wq):
    seq = tokens.shape[0]
    row = lambda n: pl.BlockSpec((WIDE, n), lambda i: (i, 0))
    wide = jax.ShapeDtypeStruct((seq, PAIR), bf16)
    return pl.pallas_call(
        project_kernel,
        grid=(seq // WIDE,),
        in_specs=[
            row(D),
            pl.BlockSpec((1, WIDE), lambda i: (0, i)),
            full((16, D)),
            full((2, 6, SIDE, PAIR)),
        ],
        out_specs=[row(D), row(PAIR), row(PAIR), row(PAIR), full((3, D, PAIR))],
        out_shape=[
            jax.ShapeDtypeStruct((seq, D), bf16),
            wide,
            wide,
            wide,
            jax.ShapeDtypeStruct((3, D, PAIR), bf16),
        ],
        compiler_params=params(),
        cost_estimate=cost(16),
        name="project",
    )(tokens, passes, vec, wq)


def doc_state(lens, base):
    rows = base + lax.broadcasted_iota(jnp.int32, (1, ROWS), 1)
    rows = jnp.concatenate([rows, rows], axis=1)
    begin = jnp.int32(0)
    first = jnp.int32(0)
    starts = jnp.zeros((1, 2 * ROWS), jnp.int32)
    for c in range(DOCS):
        starts = jnp.where(rows >= begin, begin, starts)
        first = jnp.where(base >= begin, begin, first)
        begin = begin + lens[c]
    return rows, starts, first


def two_heads(block):
    left = lax.broadcasted_iota(jnp.int32, block.shape, 1) < HD
    none = jnp.zeros_like(block)
    return jnp.concatenate([jnp.where(left, block, none), jnp.where(left, none, block)], axis=0)


def one_above(both):
    return jnp.concatenate([both[:HD, :ROWS], both[HD:, ROWS:]], axis=0).T


def attend_kernel(lens, q, k, v, out, lse, acc):
    i = pl.program_id(0)
    base = i * ROWS
    rows, starts, first = doc_state(lens, base)
    pairs = [two_heads(q[:, p * 128 : (p + 1) * 128] * bf16(0.125)) for p in range(3)]
    for p in range(3):
        acc[p] = jnp.zeros((128, 2 * ROWS), f32)

    def step(j, carry):
        at = pl.multiple_of(j * ROWS, ROWS)
        keys = at + lax.broadcasted_iota(jnp.int32, (ROWS, 2 * ROWS), 0)
        seen = (keys >= starts) & (keys <= rows)
        here = pl.ds(at, ROWS)
        head = lambda p: slice(p * 128, (p + 1) * 128)
        scores = [jnp.where(seen, nt(k[here, head(p)], pairs[p]), masked_score) for p in range(3)]
        state = []
        for p in range(3):
            before, total = carry[2 * p], carry[2 * p + 1]
            now = jnp.maximum(before, jnp.max(scores[p], axis=0, keepdims=True))
            probs = jnp.exp(scores[p] - now)
            fade = jnp.exp(before - now)
            state += [now, total * fade + jnp.sum(probs, axis=0, keepdims=True)]
            acc[p] = acc[p] * fade + tn(v[here, head(p)], probs.astype(bf16))
        return tuple(state)

    zero = jnp.zeros((1, 2 * ROWS), f32)
    state = lax.fori_loop(first // ROWS, i + 1, step, (zero + masked_score, zero) * 3)
    lines = []
    for p in range(3):
        top, total = state[2 * p], state[2 * p + 1]
        out[:, p * 128 : (p + 1) * 128] = one_above(acc[p] / total).astype(bf16)
        line = top + jnp.log(total)
        lines += [line[:, :ROWS], line[:, ROWS:]]
    lse[...] = jnp.concatenate(lines + lines[:2], axis=0)


def attend(lens, q, k, v):
    seq = q.shape[0]
    row = pl.BlockSpec((ROWS, PAIR), lambda i, s: (i, 0))
    return pl.pallas_call(
        attend_kernel,
        grid_spec=pltpu.PrefetchScalarGridSpec(
            num_scalar_prefetch=1,
            grid=(seq // ROWS,),
            in_specs=[row, full((seq, PAIR)), full((seq, PAIR))],
            out_specs=[row, pl.BlockSpec((8, ROWS), lambda i, s: (0, i))],
            scratch_shapes=[
                pltpu.VMEM((3, 128, 2 * ROWS), f32),
            ],
        ),
        out_shape=[
            jax.ShapeDtypeStruct((seq, PAIR), bf16),
            jax.ShapeDtypeStruct((8, seq), f32),
        ],
        compiler_params=params(),
        cost_estimate=cost(30),
        name="attend",
    )(lens, q, k, v)


def attend_back_kernel(
    lens, q, k, v, mixed, lse, grad_mixed, dq, dk, dv, dk_acc, dv_acc, dq_acc
):
    i = pl.program_id(0)
    count = pl.num_programs(0)
    base = i * ROWS

    @pl.when(i == 0)
    def _():
        dk_acc[...] = jnp.zeros_like(dk_acc)
        dv_acc[...] = jnp.zeros_like(dv_acc)

    rows, starts, first = doc_state(lens, base)
    heads = lax.broadcasted_iota(jnp.int32, (8, 128), 0)
    lanes = lax.broadcasted_iota(jnp.int32, (8, 128), 1)
    pick = (lanes // HD == heads).astype(f32).astype(bf16)
    queries, grads, inner, lines = [], [], [], []
    for p in range(3):
        cols = slice(p * 128, (p + 1) * 128)
        queries.append(two_heads(q[:, cols] * bf16(0.125)))
        grads.append(two_heads(grad_mixed[:, cols]))
        product = grad_mixed[:, cols].astype(f32) * mixed[:, cols].astype(f32)
        high, low, _ = split_three(product)
        sums = nt(pick, high) + nt(pick, low)
        inner.append(jnp.concatenate([sums[0:1], sums[1:2]], axis=1))
        lines.append(jnp.concatenate([lse[2 * p : 2 * p + 1], lse[2 * p + 1 : 2 * p + 2]], axis=1))
        dq_acc[p] = jnp.zeros((128, 2 * ROWS), f32)

    def step(j, carry):
        at = pl.multiple_of(j * ROWS, ROWS)
        keys = at + lax.broadcasted_iota(jnp.int32, (ROWS, 2 * ROWS), 0)
        seen = (keys >= starts) & (keys <= rows)
        here = pl.ds(at, ROWS)
        for p in range(3):
            cols = slice(p * 128, (p + 1) * 128)
            kb = k[here, cols]
            scores = jnp.where(seen, nt(kb, queries[p]) - lines[p], masked_score)
            probs = jnp.exp(scores)
            grad_probs = nt(v[here, cols], grads[p])
            grad_scores = (probs * (grad_probs - inner[p])).astype(bf16)
            dv_acc[here, cols] += nn(probs.astype(bf16), grads[p])
            dk_acc[here, cols] += nn(grad_scores, queries[p])
            dq_acc[p] += tn(kb, grad_scores)
        return carry

    lax.fori_loop(first // ROWS, i + 1, step, 0)
    for p in range(3):
        dq[:, p * 128 : (p + 1) * 128] = (one_above(dq_acc[p]) * 0.125).astype(bf16)

    @pl.when(i == count - 1)
    def _():
        dk[...] = dk_acc[...].astype(bf16)
        dv[...] = dv_acc[...].astype(bf16)


def attend_back(lens, q, k, v, mixed, lse, grad_mixed):
    seq = q.shape[0]
    count = seq // ROWS
    row = pl.BlockSpec((ROWS, PAIR), lambda i, s: (i, 0))
    wide = jax.ShapeDtypeStruct((seq, PAIR), bf16)
    return pl.pallas_call(
        attend_back_kernel,
        grid_spec=pltpu.PrefetchScalarGridSpec(
            num_scalar_prefetch=1,
            grid=(count,),
            in_specs=[
                row,
                full((seq, PAIR)),
                full((seq, PAIR)),
                row,
                pl.BlockSpec((8, ROWS), lambda i, s: (0, i)),
                row,
            ],
            out_specs=[row, full((seq, PAIR)), full((seq, PAIR))],
            scratch_shapes=[
                pltpu.VMEM((seq, PAIR), f32),
                pltpu.VMEM((seq, PAIR), f32),
                pltpu.VMEM((3, 128, 2 * ROWS), f32),
            ],
        ),
        out_shape=[wide, wide, wide],
        compiler_params=params(),
        cost_estimate=cost(40),
        name="attend_back",
    )(lens, q, k, v, mixed, lse, grad_mixed)


def feed_kernel(
    small, tok, pas, vec, mine, cot, wo_mine, wo_other, four, columns, columns_x,
    out_chip, second_keep, grad_second, grad_mixed, sums, mid_send, mid_keep, *rest,
):
    results, rest = (rest[:4], rest[4:]) if small else (rest[:2], rest[2:])
    (
        wo, other, up, down, gup, gdown, go, core_out, core_in, far_out, far_in, ga_out, ga_in, oc_out, oc_in,
        g_send, g_keep, g_in, s_core, r_core, s_far, r_far, s_ga, r_ga, s_oc, r_oc, s_x, r_x, s_m, r_m,
    ) = rest
    step = pl.program_id(0)
    half = core_out.shape[0]
    t, dp = lax.axis_index("tensor"), lax.axis_index("dp")
    core, side = t % 2, t // 2
    near, far = side * 2 + (1 - core), (1 - side) * 2 + core
    z, column = (dp // 2, dp % 2) if small else (0, 0)
    far_x = z * 2 + 1 - column

    def copy(src, dst, s_sem, r_sem, j, to):
        return pltpu.make_async_remote_copy(
            src_ref=src.at[j],
            dst_ref=dst.at[j],
            send_sem=s_sem.at[j],
            recv_sem=r_sem.at[j],
            device_id={"tensor": to},
            device_id_type=MESH,
        )

    core_copy = lambda j: copy(core_out, core_in, s_core, r_core, j, near)
    far_copy = lambda j: copy(far_out, far_in, s_far, r_far, j, far)
    ga_copy = lambda j: copy(ga_out, ga_in, s_ga, r_ga, j, near)
    oc_copy = lambda j: copy(oc_out, oc_in, s_oc, r_oc, j, near)

    def x_copy(slot):
        return pltpu.make_async_remote_copy(
            src_ref=g_send.at[slot],
            dst_ref=g_in.at[slot],
            send_sem=s_x.at[slot],
            recv_sem=r_x.at[slot],
            device_id={"dp": far_x},
            device_id_type=MESH,
        )

    def mixed_copy(block):
        rows = pl.ds(pl.multiple_of(block * ROWS, ROWS), ROWS)
        return pltpu.make_async_remote_copy(
            src_ref=mine.at[rows],
            dst_ref=other.at[rows],
            send_sem=s_m.at[block],
            recv_sem=r_m.at[block],
            device_id={"tensor": near},
            device_id_type=MESH,
        )

    barrier = pltpu.get_barrier_semaphore()

    @pl.when(step == 0)
    def _():
        for to in (near, far):
            pl.semaphore_signal(barrier, inc=1, device_id={"tensor": to}, device_id_type=MESH)
        if small:
            pl.semaphore_signal(barrier, inc=1, device_id={"dp": far_x}, device_id_type=MESH)
        for h in range(2):
            for m in range(2):
                rows, cols = slice(h * SIDE, (h + 1) * SIDE), slice(m * PAIR, (m + 1) * PAIR)
                wo[rows, cols] = wo_mine[h, m]
                wo[PAIR + h * SIDE : PAIR + (h + 1) * SIDE, cols] = wo_other[h, m]
        for r in range(4):
            for m in range(2):
                rows, cols = slice(r * SIDE, (r + 1) * SIDE), slice(m * PAIR, (m + 1) * PAIR)
                for at, weight in ((8, up), (16, down)):
                    pair = at + 2 * r + m
                    if pair < 12:
                        weight[rows, cols] = four[0, pair - 8]
                        continue
                    n = (pair // 6 - 2) * 3 + pair % 3
                    for source, here in ((columns, pair // 3 % 2), (columns_x, 1 - pair // 3 % 2)):

                        @pl.when(column == here)
                        def _():
                            weight[rows, cols] = source[n]

        pl.semaphore_wait(barrier, 3 if small else 2)
        for j in range(half):
            mixed_copy(core * half + j).start()
            mixed_copy((1 - core) * half + j).start()
        gup[...] = jnp.zeros_like(gup)
        gdown[...] = jnp.zeros_like(gdown)
        go[...] = jnp.zeros_like(go)
        sums[...] = jnp.zeros_like(sums)

    @pl.when(step < 2 * half)
    def _():
        j = step // 2
        owner = jnp.where(step % 2 == 0, 1 - core, core)
        here = pl.ds(pl.multiple_of((owner * half + j) * ROWS, ROWS), ROWS)
        first = embedded(tok[...], pas[...], vec[...])
        mixed_copy(owner * half + j).wait_recv()
        second = first + nn(jnp.concatenate([mine[here, :], other[here, :]], axis=1), wo[...])
        hat, _ = hat_of(second)
        low = (hat * vec[PASSES + 2 : PASSES + 3] + vec[PASSES + 3 : PASSES + 4]).astype(bf16)
        upper = nn(low, up[...])
        square = upper * upper
        bent = jnp.tanh(gelu_coef * upper * (1.0 + 0.044715 * square))
        act = (0.5 * upper * (1.0 + bent)).astype(bf16)
        slope = 0.5 * (1.0 + bent) + (0.5 * gelu_coef) * upper * (1.0 - bent * bent) * (
            1.0 + (3 * 0.044715) * square
        )
        grad_act = nt(cot[...], down[...])
        grad_upper = (grad_act * slope).astype(bf16)
        part = nt(grad_upper, up[...])

        @pl.when(step % 2 == 0)
        def _():
            core_out[j] = part.astype(bf16)
            core_copy(j).start()

        @pl.when(step % 2 == 1)
        def _():
            core_copy(j).wait_recv()
            far_out[j] = (part + core_in[j].astype(f32)).astype(bf16)
            far_copy(j).start()
            second_keep[pl.ds(pl.multiple_of(j * ROWS, ROWS), ROWS), :] = second

        gup[...] += tn(low, grad_upper)
        gdown[...] += tn(act, cot[...])
        out_part = nn(act, down[...])

        @pl.when(step % 2 == 0)
        def _():
            oc_out[j] = out_part.astype(bf16)
            oc_copy(j).start()

        @pl.when(step % 2 == 1)
        def _():
            oc_copy(j).wait_recv()
            out_chip[...] = (out_part + oc_in[j].astype(f32)).astype(bf16)

    @pl.when(step == 2 * half - 1)
    def _():
        for r in range(4):
            for m in range(2):
                rows, cols = slice(r * SIDE, (r + 1) * SIDE), slice(m * PAIR, (m + 1) * PAIR)
                for at, total in ((8, gup), (16, gdown)):
                    pair = at + 2 * r + m
                    slot, place = (pair // 6 - 1) * 3 + pair % 3, pair // 3 % 2
                    value = total[rows, cols].astype(bf16)
                    kept, sent, n = (mid_keep, mid_send, slot) if slot < 6 else (g_keep, g_send, slot - 6)

                    @pl.when(column == place)
                    def _():
                        kept[n] = value

                    @pl.when(column != place)
                    def _():
                        sent[n] = value
        if small:
            for n in range(3):
                x_copy(n).start()

    def through_out(grad, block):
        here = pl.ds(pl.multiple_of(block * ROWS, ROWS), ROWS)
        grad_mixed[here, :] = nt(grad, wo[:PAIR, :]).astype(bf16)
        go[...] += tn(mine[here, :], grad)

    @pl.when((step >= 2 * half) & (step < 3 * half))
    def _():
        j = step - 2 * half
        hat, root = hat_of(second_keep[pl.ds(pl.multiple_of(j * ROWS, ROWS), ROWS), :])
        far_copy(j).wait_recv()
        grad = far_out[j].astype(f32) + far_in[j].astype(f32)
        result = cot[...].astype(f32) + norm_back(hat, root, grad, vec[PASSES + 2 : PASSES + 3])
        low = result.astype(bf16)
        ga_out[j] = low
        ga_copy(j).start()
        grad_second[...] = result
        sums[0:1] += jnp.sum(grad * hat, axis=0, keepdims=True)
        sums[1:2] += jnp.sum(grad, axis=0, keepdims=True)
        through_out(low, core * half + j)

    @pl.when(step > 2 * half)
    def _():
        j = step - 2 * half - 1
        ga_copy(j).wait_recv()
        through_out(ga_in[j], (1 - core) * half + j)

    @pl.when(step == 3 * half)
    def _():
        at = pl.multiple_of(side * SIDE, SIDE)
        for m in range(2):
            value = go[pl.ds(at, SIDE), m * PAIR : (m + 1) * PAIR].astype(bf16)

            @pl.when(column == 0)
            def _():
                mid_keep[m] = value

            @pl.when(column != 0)
            def _():
                mid_send[m] = value

        for j in range(half):
            core_copy(j).wait_send()
            oc_copy(j).wait_send()
            mixed_copy(j).wait_send()
            mixed_copy(half + j).wait_send()
            far_copy(j).wait_send()
            ga_copy(j).wait_send()
        if small:
            for n in range(3):
                x_copy(n).wait_send()
                x_copy(n).wait_recv()
                value = (g_keep[n].astype(f32) + g_in[n].astype(f32)).astype(bf16)
                for turn in range(4):

                    @pl.when(z + turn == 3)
                    def _():
                        results[turn][n] = value
        else:
            results[0][...] = g_send[...]
            results[1][...] = g_keep[...]


def feed(small, tokens, passes, vec, mine, cotangent, pairs, wo_other, columns, columns_x):
    seq = tokens.shape[0]
    half = seq // ROWS // 2

    def block(i):
        core = lax.axis_index("tensor") % 2
        work = jnp.minimum(i, 2 * half - 1)
        owner = jnp.where(work % 2 == 0, 1 - core, core)
        return owner * half + work // 2

    def cot_block(i):
        core = lax.axis_index("tensor") % 2
        return jnp.where(i < 2 * half, block(i), core * half + jnp.minimum(i - 2 * half, half - 1))

    side = lambda: lax.axis_index("tensor") // 2
    row = lambda n: pl.BlockSpec((ROWS, n), lambda i: (block(i), 0))
    keep = pl.BlockSpec((ROWS, D), lambda i: (jnp.minimum(i // 2, half - 1), 0))
    last = pl.BlockSpec((ROWS, D), lambda i: (jnp.clip(i - 2 * half, 0, half - 1), 0))
    rows = lambda kind: jax.ShapeDtypeStruct((seq // 2, D), kind)
    gr = lambda n: jax.ShapeDtypeStruct((n, SIDE, PAIR), bf16)
    ends = [(3, SIDE, PAIR)] * (4 if small else 2)
    buffer = pltpu.VMEM((half, ROWS, D), bf16)
    dma = pltpu.SemaphoreType.DMA((half,))
    return pl.pallas_call(
        functools.partial(feed_kernel, small),
        grid=(3 * half + 1,),
        in_specs=[
            row(D),
            pl.BlockSpec((1, ROWS), lambda i: (0, block(i))),
            full((16, D)),
            full((seq, PAIR)),
            pl.BlockSpec((ROWS, D), lambda i: (cot_block(i), 0)),
            pl.BlockSpec((2, 2, SIDE, PAIR), lambda i: (0, 3, 0, 0)),
            full(wo_other.shape),
            pl.BlockSpec((1, 4, SIDE, PAIR), lambda i: (side(), 2, 0, 0)),
            full(columns.shape),
            full(columns.shape),
        ],
        out_specs=[
            keep,
            full((seq // 2, D)),
            last,
            full((seq, PAIR)),
            full((8, D)),
            full((6, SIDE, PAIR)),
            full((6, SIDE, PAIR)),
        ]
        + [full(shape) for shape in ends],
        scratch_shapes=[
            pltpu.VMEM((D, D), bf16),
            pltpu.VMEM((seq, PAIR), bf16),
            pltpu.VMEM((D, D), bf16),
            pltpu.VMEM((D, D), bf16),
            pltpu.VMEM((D, D), f32),
            pltpu.VMEM((D, D), f32),
            pltpu.VMEM((PAIR, D), f32),
        ]
        + [buffer] * 8
        + [pltpu.VMEM((3, SIDE, PAIR), bf16)] * 3
        + [dma] * 8
        + [pltpu.SemaphoreType.DMA((3,))] * 2
        + [pltpu.SemaphoreType.DMA((2 * half,))] * 2,
        out_shape=[
            rows(bf16),
            rows(f32),
            rows(f32),
            jax.ShapeDtypeStruct((seq, PAIR), bf16),
            jax.ShapeDtypeStruct((8, D), f32),
            gr(6),
            gr(6),
        ]
        + [jax.ShapeDtypeStruct(shape, bf16) for shape in ends],
        compiler_params=params(collective_id=1, has_side_effects=True),
        cost_estimate=cost(50),
        name="feed_forward",
    )(tokens, passes, vec, mine, cotangent, pairs, wo_other, pairs, columns, columns_x)


CHUNK = SIDE // 2
CHUNKS = 18
TAKEN = (
    ((8, 3), (10, 4), (12, 12)),
    ((3, 1), (5, 2), (7, 3), (8, 4), (9, 6), (10, 7), (11, 8), (12, 12)),
    ((1, 2), (2, 3), (5, 4), (6, 5), (7, 6), (8, 8), (9, 9), (10, 11), (12, 12)),
    ((-1, 3), (2, 5), (4, 6), (5, 7), (6, 8), (7, 12)),
)
GRAD_STEPS = 3


def last_kernel(
    small, norm_all, dq_all, dk_all, dv_all, cat, tok, pas, vec, grad_second, sums_two, second, chip, far,
    mid_near, mid_keep, output, input_grad, *rest,
):
    if small:
        late, vec_sum = rest[:2]
        rest = rest[2:]
        (
            core_out, core_in, sums, core_sums, x_in, z_in, z_out, up_in, v_out, v_in, total,
            s_core, r_core, s_sum, r_sum, s_x, r_x, s_z, r_z, s_up, r_up, s_v, r_v, ready, norm, dq, dk, dv, g_send, g_keep,
            s_own, s_res, r_res, s_in,
        ) = rest
    else:
        (
            vec_sum, send_out, keep_out, core_out, core_in, sums, core_sums, s_core, r_core, s_sum, r_sum, ready,
            norm, dq, dk, dv, g_send, g_keep, s_own, s_res, r_res, s_in,
        ) = rest
    step = pl.program_id(0)
    i = step - GRAD_STEPS
    half = core_out.shape[0]
    t, dp = lax.axis_index("tensor"), lax.axis_index("dp")
    core, side = t % 2, t // 2
    near = side * 2 + (1 - core)
    z, column = (dp // 2, dp % 2) if small else (0, 0)
    far_x = z * 2 + 1 - column
    peers = [lax.rem(dp + k, 8) for k in range(1, 8)]

    def copy(src, dst, s_sem, r_sem, to):
        return pltpu.make_async_remote_copy(
            src_ref=src, dst_ref=dst, send_sem=s_sem, recv_sem=r_sem, device_id=to, device_id_type=MESH
        )

    core_copy = lambda j: copy(core_out.at[j], core_in.at[j], s_core.at[j], r_core.at[j], {"tensor": near})
    sum_copy = lambda: copy(sums, core_sums, s_sum, r_sum, {"tensor": near})

    def rows_at(n, j, owner):
        rows = pl.ds(pl.multiple_of((owner * half + j) * ROWS, ROWS), ROWS)
        return (output, input_grad)[n].at[rows]

    own_result = lambda n, j: pltpu.make_async_copy(ready.at[n, j], rows_at(n, j, core), s_own.at[n, j])
    near_result = lambda n, j, owner: copy(
        ready.at[n, j], rows_at(n, j, owner), s_res.at[n, j], r_res.at[n, j], {"tensor": near}
    )

    def part_of(ref, k):
        return ref.at[k // 2, pl.ds((k % 2) * CHUNK, CHUNK)]

    x_copy = lambda k: copy(part_of(g_send, k), x_in.at[k], s_x.at[k], r_x.at[k], {"dp": far_x})
    z_copy = lambda k: copy(z_out.at[k], z_in.at[k], s_z.at[k], r_z.at[k], {"dp": dp - 2})
    up_copy = lambda k: copy(z_out.at[k], up_in.at[k - 6], s_up.at[k - 6], r_up.at[k - 6], {"dp": dp + 2})
    v_copy = lambda n: copy(v_out.at[peers[n]], v_in.at[dp], s_v.at[n], r_v.at[dp], {"dp": peers[n]})
    barrier = pltpu.get_barrier_semaphore()

    loads = [
        pltpu.make_async_copy(src, dst, s_in.at[n])
        for n, (src, dst) in enumerate(((norm_all, norm), (dq_all, dq), (dv_all, dv), (dk_all, dk)))
    ]

    @pl.when(step == 0)
    def _():
        for load in loads:
            load.start()
        pl.semaphore_signal(barrier, inc=1, device_id={"tensor": near}, device_id_type=MESH)
        if small:
            for peer in peers:
                pl.semaphore_signal(barrier, inc=1, device_id={"dp": peer}, device_id_type=MESH)
            late[...] = jnp.zeros_like(late)
        sums[...] = jnp.zeros_like(sums)
        sums[PASSES + 2 : PASSES + 4] = sums_two[0:2]
        pl.semaphore_wait(barrier, 8 if small else 1)

    if small:

        def term_of(k):
            rows = pl.ds(pl.multiple_of((k % 2) * CHUNK, 16), CHUNK)

            @pl.when(jnp.asarray(k) < 6)
            def _():
                x_copy(k).wait_recv()
                total[...] = g_keep[k // 2, rows, :].astype(f32) + x_in[k].astype(f32)

            @pl.when(jnp.asarray(k) >= 6)
            def _():
                total[...] = mid_keep[k // 2 - 3, rows, :].astype(f32) + mid_near[k // 2 - 3, rows, :].astype(f32)

            return total[...]

        @pl.when((step == 0) & (z == 0))
        def _():
            for k in range(6, CHUNKS):
                z_out[k] = term_of(k).astype(bf16)
                up_copy(k).start()

        @pl.when((step == 0) & (z == 3))
        def _():
            for k in (6, 7, 8, 12, 13):
                z_out[k] = term_of(k).astype(bf16)
                z_copy(k).start()

    def mine_of(grad):
        return jnp.where(side == 0, grad[:, :SIDE], grad[:, SIDE:])

    def pairs_of(grad):
        value = tn(grad, norm[...]).astype(bf16)
        return value[:, :PAIR], value[:, PAIR:]

    second_two = jnp.where(jnp.asarray(column) == 0, 1, 0)

    @pl.when(step == 0)
    def _():
        for load in loads[:3]:
            load.wait()
        both = pairs_of(jnp.where(jnp.asarray(column) == 0, mine_of(dv), mine_of(dq)))
        for m in range(2):
            g_send[second_two + m] = both[m]
        if small:
            for m in range(4):
                x_copy(2 * second_two + m).start()

    @pl.when(step == 1)
    def _():
        loads[3].wait()
        both = pairs_of(mine_of(dk))
        for place, (kept, sent) in enumerate(((0, 1), (1, 0))):

            @pl.when(jnp.asarray(column) == place)
            def _():
                g_keep[2 - 2 * place] = both[kept]
                g_send[2 * place] = both[sent]

        if small:
            for m in range(2):
                x_copy(4 * column + m).start()

    @pl.when(step == 2)
    def _():
        both = pairs_of(jnp.where(jnp.asarray(column) == 0, mine_of(dq), mine_of(dv)))
        for m in range(2):
            g_keep[1 - second_two + m] = both[m]
        if not small:
            send_out[...] = g_send[...]
            keep_out[...] = g_keep[...]

    @pl.when((i >= 0) & (i < 2 * half))
    def _():
        block = lax.rem(i + (1 - core) * half, 2 * half)
        rows = pl.ds(pl.multiple_of(block * ROWS, ROWS), ROWS)
        part = nt(dq[rows, :], cat[0]) + nt(dk[rows, :], cat[1]) + nt(dv[rows, :], cat[2])

        @pl.when(i < half)
        def _():
            core_out[i] = part.astype(bf16)
            core_copy(i).start()

        @pl.when(i >= half)
        def _():
            j = i - half
            hat, root = hat_of(embedded(tok[...], pas[...], vec[...]))
            core_copy(j).wait_recv()
            grad = part + core_in[j].astype(f32)
            result = grad_second[...] + norm_back(hat, root, grad, vec[PASSES : PASSES + 1])
            ready[0, j] = (second[...] + (chip[...].astype(f32) + far[...].astype(f32))).astype(bf16)
            ready[1, j] = result.astype(bf16)
            for n in range(2):
                own_result(n, j).start()
                near_result(n, j, core).start()
            chosen = one_hot(pas[...])
            high, mid, _ = split_three(result)
            sums[...] += nn(chosen, high) + nn(chosen, mid)
            sums[PASSES : PASSES + 1] += jnp.sum(grad * hat, axis=0, keepdims=True)
            sums[PASSES + 1 : PASSES + 2] += jnp.sum(grad, axis=0, keepdims=True)

    @pl.when(i == 2 * half - 1)
    def _():
        sum_copy().start()

    if small:

        def keep_late(k, pair, total):
            late[pair, pl.ds(pl.multiple_of((k % 2) * CHUNK, 16), CHUNK), :] = total

        def pass_on(k):
            term = term_of(k)

            @pl.when(z < 3)
            def _():
                z_copy(k).wait_recv()

            below = jnp.where(z < 3, z_in[k].astype(f32), 0.0)
            passed = term + below

            @pl.when((z > 1) | ((z == 1) & (k < 6)))
            def _():
                z_out[k] = passed.astype(bf16)
                z_copy(k).start()

            @pl.when(z == 0)
            def _():
                keep_late(k, k // 2, passed)

            @pl.when((z == 1) & (k >= 6))
            def _():
                up_copy(k).wait_recv()
                keep_late(k, k // 2 - 3, passed + up_in[k - 6].astype(f32))

        def at_position(p, carry):
            k = jnp.where(p < 3, p + 6, jnp.where(p < 9, lax.rem(p + 3 + 2 * column, 6), p))

            @pl.when((z > 0) | (k < 6))
            def _():
                pass_on(k)

            return carry

        begin, end = jnp.int32(0), jnp.int32(0)
        for place, line in enumerate(TAKEN):
            for at, upto in line:
                begin = jnp.where((z == place) & (step > at), upto, begin)
                end = jnp.where((z == place) & (step >= at), upto, end)
        lax.fori_loop(begin, end, at_position, 0)

        @pl.when((step == 7) & (z == 3))
        def _():
            for k in range(14, CHUNKS):
                z_out[k] = term_of(k).astype(bf16)
                z_copy(k).start()

        for at, first_chunk, upto in ((9, 12, 15), (10, 15, 18)):

            @pl.when((step == at) & (z == 1))
            def _(first_chunk=first_chunk, upto=upto):
                for k in range(first_chunk, upto):
                    up_copy(k).wait_recv()
                    z_out[k] = (term_of(k) + up_in[k - 6].astype(f32)).astype(bf16)
                    up_copy(k).start()

        @pl.when((step == pl.num_programs(0) - 1) & (z == 2))
        def _():
            for k in range(12, CHUNKS):
                z_copy(k).wait_recv()
                up_copy(k).wait_recv()
                keep_late(k, k // 2 - 6, term_of(k) + z_in[k].astype(f32) + up_in[k - 6].astype(f32))

    @pl.when(i == 2 * half)
    def _():
        sum_copy().wait_recv()
        total = sums[...] + core_sums[...]
        if small:
            wide = D // 8
            for d in range(8):
                v_out[d, :, 0:wide] = total[:, d * wide : (d + 1) * wide]
                v_out[d, :, wide:] = jnp.zeros((16, 128 - wide), f32)
            for n in range(7):
                v_copy(n).start()
        else:
            vec_sum[...] = total

    @pl.when(step == pl.num_programs(0) - 1)
    def _():
        for j in range(half):
            core_copy(j).wait_send()
            for n in range(2):
                own_result(n, j).wait()
                near_result(n, j, core).wait_send()
                near_result(n, j, 1 - core).wait_recv()
        sum_copy().wait_send()
        if small:
            for peer in peers:
                copy(v_out.at[0], v_in.at[peer], s_v.at[0], r_v.at[peer], {"dp": far_x}).wait_recv()
            v_in[dp] = v_out[dp]
            total = v_in[0]
            for d in range(1, 8):
                total = total + v_in[d]
            vec_sum[...] = total
            for n in range(7):
                v_copy(n).wait_send()
            for k in range(CHUNKS):
                if k < 6:
                    x_copy(k).wait_send()
                    pl.when(z > 0)(z_copy(k).wait_send)
                elif k < 12:
                    pl.when(z > 1)(z_copy(k).wait_send)
                    pl.when(z == 0)(up_copy(k).wait_send)
                else:
                    pl.when(z == 3)(z_copy(k).wait_send)
                    pl.when(z < 2)(up_copy(k).wait_send)


def last(
    small, norm, dq, dk, dv, cat, tokens, passes, vec, grad_second, sums_two, second, chip, far, mid_near, mid_keep
):
    seq = dq.shape[0]
    half = seq // ROWS // 2
    core = lambda: lax.axis_index("tensor") % 2

    own = lambda i: jnp.clip(i - GRAD_STEPS - half, 0, half - 1)
    mine = pl.BlockSpec((ROWS, D), lambda i: (own(i), 0))
    dma = pltpu.SemaphoreType.DMA
    out_specs = [pl.BlockSpec(memory_space=pl.ANY)] * 2
    out_shape = [jax.ShapeDtypeStruct((seq, D), bf16)] * 2
    scratch = [
        pltpu.VMEM((half, ROWS, D), bf16),
        pltpu.VMEM((half, ROWS, D), bf16),
        pltpu.VMEM((16, D), f32),
        pltpu.VMEM((16, D), f32),
    ]
    sems = [dma((half,)), dma((half,)), dma, dma]
    if small:
        out_specs += [full((3, SIDE, PAIR)), full((16, 128))]
        out_shape += [
            jax.ShapeDtypeStruct((3, SIDE, PAIR), f32),
            jax.ShapeDtypeStruct((16, 128), f32),
        ]
        scratch += [pltpu.VMEM((CHUNKS, CHUNK, PAIR), bf16)] * 3
        scratch += [pltpu.VMEM((12, CHUNK, PAIR), bf16)]
        scratch += [pltpu.VMEM((8, 16, 128), f32)] * 2 + [pltpu.VMEM((CHUNK, PAIR), f32)]
        sems += [dma((6,))] * 2 + [dma((CHUNKS,))] * 2 + [dma((12,))] * 2 + [dma((7,)), dma((8,))]
    else:
        out_specs += [full((16, D)), full((3, SIDE, PAIR)), full((3, SIDE, PAIR))]
        out_shape += [jax.ShapeDtypeStruct((16, D), f32)] + [jax.ShapeDtypeStruct((3, SIDE, PAIR), bf16)] * 2
    scratch_more = [pltpu.VMEM((2, half, ROWS, D), bf16), pltpu.VMEM((seq, D), bf16)]
    scratch_more += [pltpu.VMEM((seq, PAIR), bf16)] * 3
    scratch_more += [pltpu.VMEM((3, SIDE, PAIR), bf16)] * 2 + [dma((2, half))] * 3 + [dma((4,))]
    return pl.pallas_call(
        functools.partial(last_kernel, small),
        grid=(GRAD_STEPS + 2 * half + 2,),
        in_specs=[
            *[pl.BlockSpec(memory_space=pl.ANY)] * 4,
            full(cat.shape),
            pl.BlockSpec((ROWS, D), lambda i: (core() * half + own(i), 0)),
            pl.BlockSpec((1, ROWS), lambda i: (0, core() * half + own(i))),
            full((16, D)),
            mine,
            full((8, D)),
            mine,
            mine,
            mine,
            full(mid_near.shape),
            full(mid_keep.shape),
        ],
        out_specs=out_specs,
        out_shape=out_shape,
        scratch_shapes=scratch + sems + scratch_more,
        compiler_params=params(collective_id=2, has_side_effects=True),
        cost_estimate=cost(38),
        name="last",
    )(norm, dq, dk, dv, cat, tokens, passes, vec, grad_second, sums_two, second, chip, far, mid_near, mid_keep)


def precondition(grad, weight, left, right, left_root, right_root):
    high = lax.Precision.HIGHEST
    left_new = decay * left + (1.0 - decay) * jnp.einsum(
        "...ij,...kj->...ik", grad, grad, precision=high
    )
    right_new = decay * right + (1.0 - decay) * jnp.einsum(
        "...ji,...jk->...ik", grad, grad, precision=high
    )
    half = jnp.einsum("...ij,...jk->...ik", left_root, grad, precision=high)
    step = jnp.einsum("...ij,...jk->...ik", half, right_root, precision=high)
    return (left_new, right_new, step, weight - rate_matrix * step)


def two_part(value):
    high = value.astype(bf16)
    return high, (value - high.astype(f32)).astype(bf16)


def dot_three(dot, a, b):
    return dot(a[0], b[0]) + (dot(a[0], b[1]) + dot(a[1], b[0]))


def renew_kernel(
    late, own, one, two, three, weight, left, right, left_root, right_root, output, input_grad, vec_sum, vec, moment,
    left_new, right_new, step, new, output_new, input_grad_new, vec_grad, moment_new, vec_new,
):
    @pl.when(pl.program_id(0) == 0)
    def _():
        rows, wide = vec.shape
        grad = vec_sum[:rows, :wide]
        square = decay * moment[...] + (1.0 - decay) * grad * grad
        vec_grad[...] = grad
        moment_new[...] = square
        vec_new[...] = vec[...] - rate_vector * grad / (jnp.sqrt(square) + moment_eps)

    output_new[...] = output[...]
    input_grad_new[...] = input_grad[...]

    @pl.when(pl.program_id(0) < 3)
    def _():
        early = own[0].astype(f32) + one[0].astype(f32) + two[0].astype(f32) + three[0].astype(f32)
        z = lax.axis_index("dp") // 2
        both = late[0] + jnp.where(z > 2, early, 0.0)
        for n in range(2):
            grad = both[:, n * SIDE : (n + 1) * SIDE]
            grad = two_part(jnp.where(z == 0, grad.T, grad))
            left_new[0, n] = decay * left[0, n] + (1.0 - decay) * dot_three(nt, grad, grad)
            right_new[0, n] = decay * right[0, n] + (1.0 - decay) * dot_three(tn, grad, grad)
            half = dot_three(nn, two_part(left_root[0, n]), grad)
            value = dot_three(nn, two_part(half), two_part(right_root[0, n]))
            step[0, n] = value
            new[0, n] = weight[0, n] - rate_matrix * value


def renew(late, own, far, weight, left, right, left_root, right_root, output, input_grad, vec_sum, vec, moment):
    pair = pl.BlockSpec((1, SIDE, PAIR), lambda i: (jnp.minimum(i, 2), 0, 0))
    slot = pl.BlockSpec((1, 2, SIDE, SIDE), lambda i: (0, jnp.minimum(i, 2), 0, 0))
    rows = pl.BlockSpec((output.shape[0] // 4, D), lambda i: (i, 0))
    return pl.pallas_call(
        renew_kernel,
        grid=(4,),
        in_specs=[pair] * 5 + [slot] * 5 + [rows] * 2 + [full(vec_sum.shape)] + [full(vec.shape)] * 2,
        out_specs=[slot] * 4 + [rows] * 2 + [full(vec.shape)] * 3,
        out_shape=[jax.ShapeDtypeStruct(weight.shape, f32)] * 4
        + [jax.ShapeDtypeStruct(value.shape, value.dtype) for value in (output, input_grad, vec, vec, vec)],
        compiler_params=params(46),
        cost_estimate=cost(8),
        name="renew",
    )(late, own, *far, weight, left, right, left_root, right_root, output, input_grad, vec_sum, vec, moment)


def to_pairs(blocks):
    n = blocks.shape[0] // 2
    return blocks.reshape(n, 2, SIDE, SIDE).transpose(0, 2, 1, 3).reshape(n, SIDE, PAIR)


def from_pairs(pairs):
    n = pairs.shape[0]
    return pairs.reshape(n, SIDE, 2, SIDE).transpose(0, 2, 1, 3).reshape(2 * n, SIDE, SIDE)


def swap(value, bit):
    return lax.ppermute(value, "tensor", [(t, t ^ bit) for t in range(NT)])


def hop_x(value):
    return lax.ppermute(value, "dp", [(d, d ^ 1) for d in range(8)])


def hop_z(value, turn, ends):
    pairs = [(d, (d + 2 * turn) % 8) for d in range(8) if (d // 2 + turn) % 4 in ends]
    return lax.ppermute(value, "dp", pairs)


def tie(*values):
    return lax.optimization_barrier(values)


def on_device(
    tokens,
    pass_ids,
    doc_lengths,
    cotangent,
    block_weights,
    vector_params,
    vector_moment,
    block_left,
    block_right,
    block_left_root,
    block_right_root,
):
    t, dp = lax.axis_index("tensor"), lax.axis_index("dp")
    core, side = t % 2, t // 2
    n_dp = lax.axis_size("dp")
    small = n_dp == 8
    z, column = (dp // 2, dp % 2) if small else (0, 0)
    lens = doc_lengths[0]
    seq = tokens.shape[0]
    passes = pass_ids.reshape(1, seq)
    total_blocks = (D // SIDE) * (4 + 2 * (FF // D))
    slots = block_weights.shape[1] * n_dp

    if small:
        pairs, columns, wo_other, vec, norm, q, k, v, cat = gather(
            block_weights, vector_params, tokens, passes
        )
        columns_x = hop_x(columns)
    else:
        every = lax.all_gather(block_weights.astype(bf16), "dp", axis=1, tiled=True)[0]
        near = to_pairs(every[:total_blocks])
        far = swap(near, 2)
        pairs = jnp.where(side == 0, jnp.stack([near, far]), jnp.stack([far, near]))
        vec = lax.all_gather(vector_params, "dp", axis=1, tiled=True)
        vec = jnp.pad(vec, ((0, 16 - vec.shape[0]), (0, 0)))
        wo_other = swap(pairs[:, 6:8], 1)
        columns = jnp.concatenate([near[12:15], near[18:21]], axis=0)
        columns_x = jnp.concatenate([near[15:18], near[21:24]], axis=0)
        norm, q, k, v, cat = project(tokens, passes, vec, pairs)
    mine, lse = attend(lens, q, k, v)
    out_chip, second, grad_second, grad_mixed, sums_two, mid_send, mid_keep, *ends = feed(
        small, tokens, passes, vec, mine, cotangent, pairs, wo_other, columns, columns_x
    )
    out_far = swap(out_chip, 2)
    if small:
        far = [hop_z(ends[turn], turn, (3,)) for turn in (1, 2, 3)]
        mid_send = hop_x(mid_send)
    dq, dk, dv = attend_back(lens, q, k, v, mine, lse, grad_mixed)
    if small:
        *far, out_far, mid_send, dq = tie(*far, out_far, mid_send, dq)
    output, input_grad, *sums = last(
        small, norm, dq, dk, dv, cat, tokens, passes, vec, grad_second, sums_two, second, out_chip, out_far,
        mid_send, mid_keep,
    )
    if small:
        late, vector_sum = sums
        return_blocks = renew(
            late, ends[0], far, block_weights, block_left, block_right, block_left_root, block_right_root,
            output, input_grad, vector_sum, vector_params, vector_moment,
        )
        left_new, right_new, step, weight_new, output, input_grad, vector_grad, moment_new, vector_new = return_blocks
    else:
        vector_part, g_send, g_keep = sums[0][: PASSES + 4], *sums[1:]
        send, keep = ends
        rest = jnp.stack(
            [
                jnp.concatenate([mid_keep, keep]).reshape(3, 3, SIDE, PAIR),
                jnp.concatenate([mid_send, send]).reshape(3, 3, SIDE, PAIR),
            ],
            axis=1,
        )
        grad_qkv = from_pairs(jnp.concatenate([g_keep, g_send], axis=0)).swapaxes(1, 2)
        grad_rest = from_pairs(rest.reshape(18, SIDE, PAIR))
        spare = jnp.zeros((slots - total_blocks, SIDE, SIDE), bf16)
        grad_blocks = jnp.concatenate([grad_qkv, grad_rest, spare], axis=0)[None].astype(f32)
        owned = lax.psum_scatter(grad_blocks, "dp", scatter_dimension=1, tiled=True)
        vector_grad = lax.psum_scatter(vector_part, "dp", scatter_dimension=1, tiled=True)
        left_new, right_new, step, weight_new = precondition(
            owned, block_weights, block_left, block_right, block_left_root, block_right_root
        )
        moment_new = decay * vector_moment + (1.0 - decay) * vector_grad * vector_grad
        vector_new = vector_params - rate_vector * vector_grad / (jnp.sqrt(moment_new) + moment_eps)
    return (
        output,
        input_grad,
        left_new,
        right_new,
        step,
        weight_new,
        vector_grad,
        moment_new,
        vector_new,
    )


def solution(mesh):
    rows, line = P("dp", None), P(None, "dp")
    block = P("tensor", "dp", None, None)
    return jax.shard_map(
        on_device,
        mesh=mesh,
        in_specs=(rows, P("dp"), rows, rows, block, line, line, block, block, block, block),
        out_specs=(rows, rows, block, block, block, block, line, line, line),
        check_vma=False,
    )
```
